32 devices in a mesh: section: 2 (over x), ctx: 8 (over z, y), wsh: 2 (over core).
Axes of the slice: x: 2, y: 2, z: 4, core: 2. Of those that a mesh axis runs over, the one named last changes fastest.
Arguments:
- inputs: bfloat16 [2, 2, 1024, 1024], P(None, 'wsh', 'ctx'), may hold values from -6 to 6
- cotangent: bfloat16 [2, 2, 1024, 1024], P(None, 'wsh', 'ctx'), may hold values from -6 to 6
- block_pair: int32 [8], replicated, may hold values from 0 to 7, each once
- qkv_weight: bfloat16 [2, 1024, 3072], P('section', 'wsh'), may hold values from -0.1875 to 0.1875
- qkv_bias: bfloat16 [2, 3072], P('section', 'wsh'), may hold values from -1.75 to 1.75
- proj_weight: bfloat16 [2, 1024, 1024], P('section', 'wsh'), may hold values from -3 to 3
- proj_bias: bfloat16 [2, 1024], P('section', 'wsh'), may hold values from -1.75 to 1.75
- up_weight: bfloat16 [2, 1024, 4096], P('section', 'wsh'), may hold values from -0.1875 to 0.1875
- up_bias: bfloat16 [2, 4096], P('section', 'wsh'), may hold values from -1.75 to 1.75
- down_weight: bfloat16 [2, 4096, 1024], P('section', 'wsh'), may hold values from -0.09375 to 0.09375
- down_bias: bfloat16 [2, 1024], P('section', 'wsh'), may hold values from -1.75 to 1.75
- attn_gain: bfloat16 [2, 1024], P('section', 'wsh'), may hold values from 0.099609375 to 1.8984375
- attn_shift: bfloat16 [2, 1024], P('section', 'wsh'), may hold values from -1.75 to 1.75
- mlp_gain: bfloat16 [2, 1024], P('section', 'wsh'), may hold values from 0.099609375 to 1.8984375
- mlp_shift: bfloat16 [2, 1024], P('section', 'wsh'), may hold values from -1.75 to 1.75
Outputs:
- layer_out: bfloat16 [2, 2, 2, 1024, 1024], P('section', None, 'wsh', 'ctx')
- input_grad: bfloat16 [2, 2, 2, 1024, 1024], P('section', None, 'wsh', 'ctx')
- grad_qkv_weight: float32 [2, 1024, 3072], P('section', 'wsh')
- grad_qkv_bias: float32 [2, 3072], P('section', 'wsh')
- grad_proj_weight: float32 [2, 1024, 1024], P('section', 'wsh')
- grad_proj_bias: float32 [2, 1024], P('section', 'wsh')
- grad_up_weight: float32 [2, 1024, 4096], P('section', 'wsh')
- grad_up_bias: float32 [2, 4096], P('section', 'wsh')
- grad_down_weight: float32 [2, 4096, 1024], P('section', 'wsh')
- grad_down_bias: float32 [2, 1024], P('section', 'wsh')
- grad_attn_gain: float32 [2, 1024], P('section', 'wsh')
- grad_attn_shift: float32 [2, 1024], P('section', 'wsh')
- grad_mlp_gain: float32 [2, 1024], P('section', 'wsh')
- grad_mlp_shift: float32 [2, 1024], P('section', 'wsh')
The draws below stay inside these ranges and needn't reach their ends.
Inputs may be any that keep to these rules, and one draw needn't show every extreme that they name: The index d of ctx stores for every sequence the causal blocks block_pair[d] and 15 - block_pair[d], in that order; each value occurs once.
All inputs are finite; a program needn't handle non-finite values.
Results may differ from the reference program's by a relative error of at most 0.015.
Values may be sent and summed in bfloat16 or wider, within the bound.
No kernel may reach another device: no remote copies, remote signals or barrier semaphores. Data moves between devices by JAX's collectives and lax.ppermute only.
A program may use at most 320 MiB of HBM per device.

```python
import jax
import jax.numpy as jnp
from jax import lax

D = 1024
HEADS = 16
HEAD = 64
ROT = 16
FF = 4096
TOK_DEV = 128
MICRO = 2
SECTIONS = 2
BATCH = 2
SEQ = 1024
BLOCK = 64
BLOCKS = 16


def shard_levels(rng, dims, pieces, smallest, high):
    factor_of, own = 1.0, jax.random.fold_in(rng, 6)
    for axis_at, blocks in pieces:
        heights = jnp.exp(jax.random.uniform(jax.random.fold_in(own, axis_at), (blocks,), jnp.float32, smallest / len(pieces), high / len(pieces)))
        factor_of = factor_of * jnp.repeat(heights, dims[axis_at] // blocks).reshape([-1 if axis == axis_at else 1 for axis in range(len(dims))])
    return factor_of


def noise(rng, extent, width, reach, shards=(), kind=jnp.bfloat16):
    drawn = jax.random.normal(rng, extent, jnp.float32) * width
    if len(shards) > 0:
        drawn = shard_levels(rng, extent, shards, -0.22, 0.18) * drawn
    return jnp.clip(drawn, min=-reach, max=reach).astype(kind)


def setup_inputs(seed: int = 0) -> dict:
    streams_of = jax.random.split(jax.random.key(seed), 16)
    inputs = noise(streams_of[0], (MICRO, BATCH, SEQ, D), 1.0, 6.0, ((1, 2), (2, 8)))
    cotangent = noise(streams_of[1], (MICRO, BATCH, SEQ, D), 1.0, 6.0, ((1, 2), (2, 8)))
    block_pair = jax.random.permutation(streams_of[2], BLOCKS // 2).astype(jnp.int32)
    qkv_weight = noise(streams_of[3], (SECTIONS, D, 3 * D), D ** -0.5, 0.1875, ((0, 2), (1, 2)))
    qkv_bias = noise(streams_of[4], (SECTIONS, 3 * D), 0.3, 1.75, ((0, 2), (1, 2)))
    proj_weight = noise(streams_of[5], (SECTIONS, D, D), (max(1, 4 * D // SEQ)) ** -0.5, 3.0, ((0, 2), (1, 2)))
    proj_bias = noise(streams_of[6], (SECTIONS, D), 0.3, 1.75, ((0, 2), (1, 2)))
    up_weight = noise(streams_of[7], (SECTIONS, D, FF), D ** -0.5, 0.1875, ((0, 2), (1, 2)))
    up_bias = noise(streams_of[8], (SECTIONS, FF), 0.3, 1.75, ((0, 2), (1, 2)))
    down_weight = noise(streams_of[9], (SECTIONS, FF, D), FF ** -0.5, 0.09375, ((0, 2), (1, 2)))
    down_bias = noise(streams_of[10], (SECTIONS, D), 0.3, 1.75, ((0, 2), (1, 2)))
    attn_gain = jnp.clip(1.0 + 0.18 * jax.random.normal(streams_of[11], (SECTIONS, D), jnp.float32), 0.099609375, 1.8984375).astype(jnp.bfloat16)
    attn_shift = noise(streams_of[12], (SECTIONS, D), 0.3, 1.75, ((0, 2), (1, 2)))
    mlp_gain = jnp.clip(1.0 + 0.18 * jax.random.normal(streams_of[13], (SECTIONS, D), jnp.float32), 0.099609375, 1.8984375).astype(jnp.bfloat16)
    mlp_shift = noise(streams_of[14], (SECTIONS, D), 0.3, 1.75, ((0, 2), (1, 2)))
    return {"inputs": inputs, "cotangent": cotangent, "block_pair": block_pair, "qkv_weight": qkv_weight, "qkv_bias": qkv_bias, "proj_weight": proj_weight, "proj_bias": proj_bias, "up_weight": up_weight, "up_bias": up_bias, "down_weight": down_weight, "down_bias": down_bias, "attn_gain": attn_gain, "attn_shift": attn_shift, "mlp_gain": mlp_gain, "mlp_shift": mlp_shift}


@jax.custom_vjp
def low(v):
    return lax.optimization_barrier(v.astype(jnp.bfloat16)).astype(jnp.float32)

@jax.custom_vjp
def low_back(v):
    return v

def low_keep(v):
    return (low(v), None)

def low_pass(kept, grad):
    return (grad,)

def back_keep(v):
    return (v, None)

def back_low(kept, grad):
    return (low(grad),)
low.defvjp(low_keep, low_pass)
low_back.defvjp(back_keep, back_low)
NORM_EPS = 1e-05
ROPE_BASE = 10000.0
MASKED_SCORE = -1e+30
EXACT_PREC = lax.Precision.HIGHEST

def layer_norm(hidden_in, gain_vec, shift_vec):
    row_mean = lax.optimization_barrier(jnp.mean(hidden_in, axis=-1, keepdims=True))
    centered = hidden_in - row_mean
    spread = lax.optimization_barrier(jnp.mean(centered * centered, axis=-1, keepdims=True))
    return centered * lax.rsqrt(spread + NORM_EPS) * gain_vec + shift_vec

def rotate(head_vals, cosine, sine_tab):
    half_rot = cosine.shape[-1]
    lead_part = head_vals[..., :half_rot]
    second = head_vals[..., half_rot:2 * half_rot]
    tail_part = head_vals[..., 2 * half_rot:]
    cos_wide = cosine[:, None, :]
    sin_wide = sine_tab[:, None, :]
    return jnp.concatenate([lead_part * cos_wide - second * sin_wide, second * cos_wide + lead_part * sin_wide, tail_part], axis=-1)

def rotary_tables(positions):
    half_rot = ROT // 2
    inv_freq = ROPE_BASE ** (-(jnp.arange(half_rot, dtype=jnp.float32) * 2.0) / ROT)
    angles = positions.astype(jnp.float32)[:, None] * inv_freq[None, :]
    return (jnp.cos(angles), jnp.sin(angles))

def sequence_positions(block_pair):
    stored = jnp.arange(SEQ, dtype=jnp.int32)
    device = stored // TOK_DEV
    within = stored % TOK_DEV
    pair_block = block_pair[device]
    block_idx = jnp.where(within < BLOCK, pair_block, BLOCKS - 1 - pair_block)
    return (block_idx * BLOCK + within % BLOCK).astype(jnp.int32)

def attend_seq(queries, key_rows, value_rows, positions):
    query_rows = min(512, SEQ)
    num_blocks = SEQ // query_rows
    score_scale = HEAD ** (-0.5)
    query_split = queries.reshape(num_blocks, query_rows, HEADS, HEAD)
    pos_split = positions.reshape(num_blocks, query_rows)

    def one_block(block_in):
        query_block, pos_block = block_in
        raw_scores = low_back(jnp.einsum('qhd,khd->hqk', query_block, key_rows, precision=EXACT_PREC))
        allowed = (pos_block[:, None] >= positions[None, :])[None]
        scores = jnp.where(allowed, raw_scores * score_scale, MASKED_SCORE)
        attn_probs = low(jax.nn.softmax(scores, axis=-1))
        return jnp.einsum('hqk,khd->qhd', attn_probs, value_rows, precision=EXACT_PREC)
    merged = lax.map(jax.checkpoint(one_block), (query_split, pos_split))
    return merged.reshape(SEQ, HEADS, HEAD)

def layer_forward(hidden_in, params, positions, cosine, sine_tab):
    qkv_weight, qkv_bias, proj_weight, proj_bias, up_weight, up_bias, down_weight, down_bias, attn_gain, attn_shift, mlp_gain, mlp_shift = params
    normed = low(layer_norm(hidden_in, attn_gain, attn_shift))
    mixed_in = low(layer_norm(hidden_in, mlp_gain, mlp_shift))
    qkv = low_back(jnp.dot(normed, qkv_weight, precision=EXACT_PREC) + qkv_bias)
    queries = low(low_back(rotate(qkv[:, :D].reshape(SEQ, HEADS, HEAD), cosine, sine_tab)))
    key_rows = low(low_back(rotate(qkv[:, D:2 * D].reshape(SEQ, HEADS, HEAD), cosine, sine_tab)))
    value_rows = low(low_back(qkv[:, 2 * D:].reshape(SEQ, HEADS, HEAD)))
    attended = attend_seq(queries, key_rows, value_rows, positions).reshape(SEQ, D)
    attended = low(low_back(attended))
    attn_out = jnp.dot(attended, proj_weight, precision=EXACT_PREC) + proj_bias
    pre_act = low_back(jnp.dot(mixed_in, up_weight, precision=EXACT_PREC) + up_bias)
    active = low(jax.nn.gelu(pre_act, approximate=False))
    mlp_out = jnp.dot(active, down_weight, precision=EXACT_PREC) + down_bias
    return hidden_in + attn_out + mlp_out

def two_sections(hidden_in, extra_in, first_params, second_params, positions, cosine, sine_tab):
    first_out = layer_forward(hidden_in, first_params, positions, cosine, sine_tab)
    handed = low(low_back(first_out + extra_in))
    second_out = layer_forward(handed, second_params, positions, cosine, sine_tab)
    return (first_out, second_out)

def reference(inputs, cotangent, block_pair, qkv_weight, qkv_bias, proj_weight, proj_bias, up_weight, up_bias, down_weight, down_bias, attn_gain, attn_shift, mlp_gain, mlp_shift):
    weight_set = (qkv_weight, qkv_bias, proj_weight, proj_bias, up_weight, up_bias, down_weight, down_bias, attn_gain, attn_shift, mlp_gain, mlp_shift)
    params = tuple((member.astype(jnp.float32) for member in weight_set))
    first_params = tuple((member[0] for member in params))
    second_params = tuple((member[1] for member in params))
    positions = sequence_positions(block_pair)
    cosine, sine_tab = rotary_tables(positions)
    rows_all = inputs.astype(jnp.float32).reshape(MICRO * BATCH, SEQ, D)
    cot_all = cotangent.astype(jnp.float32).reshape(MICRO * BATCH, SEQ, D)

    def run_sections(hidden_in, extra_in, first_set, second_set):
        return two_sections(hidden_in, extra_in, first_set, second_set, positions, cosine, sine_tab)

    def one_sequence(totals, pair_in):
        hidden_in, cot_rows = pair_in
        section_outs, pull_back = jax.vjp(run_sections, hidden_in, jnp.zeros_like(hidden_in), first_params, second_params)
        grad_rows, grad_extra, grad_first, grad_second = pull_back((jnp.zeros_like(section_outs[0]), cot_rows))
        totals = jax.tree.map(jnp.add, totals, (grad_first, grad_second))
        return (totals, (section_outs[0].astype(jnp.bfloat16), section_outs[1].astype(jnp.bfloat16), grad_rows.astype(jnp.bfloat16), grad_extra.astype(jnp.bfloat16)))
    zero_totals = jax.tree.map(jnp.zeros_like, (first_params, second_params))
    totals, (out_first, out_second, grad_first_rows, grad_second_rows) = lax.scan(one_sequence, zero_totals, (rows_all, cot_all))
    out_shape = (MICRO, BATCH, SEQ, D)
    layer_out = jnp.stack([out_first.reshape(out_shape), out_second.reshape(out_shape)])
    input_grad = jnp.stack([grad_first_rows.reshape(out_shape), grad_second_rows.reshape(out_shape)])
    grad_set = [jnp.stack([totals[0][index], totals[1][index]]) for index in range(12)]
    return (layer_out, input_grad, grad_set[0], grad_set[1], grad_set[2], grad_set[3], grad_set[4], grad_set[5], grad_set[6], grad_set[7], grad_set[8], grad_set[9], grad_set[10], grad_set[11])
```

```python
import functools

import jax
import jax.numpy as jnp
from jax import lax
from jax.experimental import pallas as pl
from jax.experimental.pallas import tpu as pltpu
from jax.sharding import PartitionSpec as P

HEADS = 16
ROT = 16
NORM_EPS = 1e-05
ROPE_BASE = 10000.0
MASKED_SCORE = -1e30
LANES = 128
VMEM_LIMIT = 48 * 1024 * 1024
INV_SQRT2 = 0.7071067811865476
INV_SQRT_2PI = 0.3989422804014327

f32 = jnp.float32
bf16 = jnp.bfloat16


def dot_nn(left, right):
    return lax.dot_general(left, right, (((1,), (0,)), ((), ())), preferred_element_type=f32)


def dot_nt(left, right):
    return lax.dot_general(left, right, (((1,), (1,)), ((), ())), preferred_element_type=f32)


def params_of(flops, nbytes, **extra):
    return dict(
        compiler_params=pltpu.CompilerParams(vmem_limit_bytes=VMEM_LIMIT),
        cost_estimate=pl.CostEstimate(flops=flops, bytes_accessed=nbytes, transcendentals=0),
        **extra,
    )


def whole(shape):
    rank = len(shape)
    return pl.BlockSpec(shape, lambda *args: (0,) * rank)


def shape_of(shape, dtype):
    return jax.ShapeDtypeStruct(shape, dtype)


def rope(vals, tab_ref):
    return (
        vals * tab_ref[0]
        + pltpu.roll(vals, LANES - ROT // 2, 1) * tab_ref[1]
        + pltpu.roll(vals, ROT // 2, 1) * tab_ref[2]
    )


def unrope(vals, tab_ref):
    return (
        vals * tab_ref[0]
        - pltpu.roll(vals, LANES - ROT // 2, 1) * tab_ref[1]
        - pltpu.roll(vals, ROT // 2, 1) * tab_ref[2]
    )


def normalized(hidden):
    row_mean = jnp.mean(hidden, axis=-1, keepdims=True)
    centered = hidden - row_mean
    spread = jnp.mean(centered * centered, axis=-1, keepdims=True)
    scale = lax.rsqrt(spread + NORM_EPS)
    return centered * scale, scale


def qkv_kernel(half, wsh_ref, x_ref, vec_ref, bq, bk, bv, tab_ref, *rest):
    weights = rest[:6]
    out_ref, na_own, na_oth, nm_own, nm_oth = rest[6:11]
    wsh = wsh_ref[0]

    @pl.when(pl.program_id(0) == 0)
    def _():
        xhat, _ = normalized(x_ref[...].astype(f32))
        na = (xhat * vec_ref[0:1] + vec_ref[1:2]).astype(bf16)
        nm = (xhat * vec_ref[2:3] + vec_ref[3:4]).astype(bf16)
        first = wsh == 0
        na_own[...] = jnp.where(first, na[:, :half], na[:, half:])
        na_oth[...] = jnp.where(first, na[:, half:], na[:, :half])
        nm_own[...] = jnp.where(first, nm[:, :half], nm[:, half:])
        nm_oth[...] = jnp.where(first, nm[:, half:], nm[:, :half])

    for part, bias in enumerate((bq, bk, bv)):
        res = (
            dot_nn(na_own[...], weights[2 * part][...])
            + dot_nn(na_oth[...], weights[2 * part + 1][...])
            + bias[...]
        )
        for pair in range(res.shape[1] // LANES):
            vals = res[:, pair * LANES : (pair + 1) * LANES]
            if part < 2:
                vals = rope(vals, tab_ref)
            out_ref[pair, part] = vals.astype(bf16)


def qkv_call(x, vecs, qkv_b, tab, w_own, w_oth, wsh):
    rows, dim = x.shape
    half = w_own.shape[0]
    pairs = dim // LANES
    tile = 2 * LANES
    steps = dim // tile

    def col(part):
        return lambda j, s: (0, part * steps + j)

    wspecs = []
    for part in range(3):
        wspecs += [pl.BlockSpec((half, tile), col(part))] * 2
    return pl.pallas_call(
        functools.partial(qkv_kernel, half),
        grid_spec=pltpu.PrefetchScalarGridSpec(
            num_scalar_prefetch=1,
            grid=(steps,),
            in_specs=[
                whole((rows, dim)),
                whole(vecs.shape),
                pl.BlockSpec((1, tile), col(0)),
                pl.BlockSpec((1, tile), col(1)),
                pl.BlockSpec((1, tile), col(2)),
                whole(tab.shape),
            ]
            + wspecs,
            out_specs=[pl.BlockSpec((tile // LANES, 3, rows, LANES), lambda j, s: (j, 0, 0, 0))]
            + [whole((rows, half))] * 4,
        ),
        out_shape=[shape_of((pairs, 3, rows, LANES), bf16)] + [shape_of((rows, half), bf16)] * 4,
        name="qkv_proj",
        **params_of(6 * rows * dim * dim, 6 * dim * dim + 8 * rows * dim),
    )(wsh, x, vecs, qkv_b, qkv_b, qkv_b, tab, w_own, w_oth, w_own, w_oth, w_own, w_oth)


def gather_rows(dst, refs, dtype=None):
    rows = refs[0].shape[0]
    for i, ref in enumerate(refs):
        dst[i * rows : (i + 1) * rows] = ref[...]


def mlp_kernel(micros, tiles, save, wsh_ref, *refs):
    owns, oths = refs[:micros], refs[micros : 2 * micros]
    up_b, down_b, up_own, up_oth, dn_own, dn_oth = refs[2 * micros : 2 * micros + 6]
    outs = refs[2 * micros + 6 :]
    if save:
        out_ref, u_ref, g_own, g_oth, own_s, oth_s = outs
    else:
        out_ref, own_s, oth_s = outs
    step = pl.program_id(0)

    @pl.when(step == 0)
    def _():
        gather_rows(own_s, owns)
        gather_rows(oth_s, oths)
        out_ref[...] = jnp.broadcast_to(down_b[...], out_ref.shape)

    pre = dot_nn(own_s[...], up_own[...]) + dot_nn(oth_s[...], up_oth[...]) + up_b[...]
    act = (0.5 * pre * (1.0 + lax.erf(pre * INV_SQRT2))).astype(bf16)
    if save:
        u_ref[...] = pre

    @pl.when(step < tiles)
    def _():
        if save:
            g_own[...] = act
        out_ref[...] += dot_nn(act, dn_own[...])

    @pl.when(step >= tiles)
    def _():
        if save:
            g_oth[...] = act
        out_ref[...] += dot_nn(act, dn_oth[...])


def ff_maps(tiles):
    def ff_tile(j, s):
        return (s[0] * tiles + j) % (2 * tiles)

    own_tile = lambda j: jnp.minimum(j, tiles - 1)
    oth_tile = lambda j: jnp.maximum(j - tiles, 0)
    return ff_tile, own_tile, oth_tile


def mlp_call(nm_own, nm_oth, up_b, down_b, up_own, up_oth, dn_own, dn_oth, wsh, save):
    micros = len(nm_own)
    rows, half = nm_own[0].shape
    total = micros * rows
    dim = dn_own.shape[1]
    ff = up_own.shape[1]
    tile = 512
    tiles = ff // tile // 2
    ff_tile, own_tile, oth_tile = ff_maps(tiles)
    out_specs = [whole((total, dim))]
    out_shape = [shape_of((total, dim), f32)]
    if save:
        out_specs += [
            pl.BlockSpec((total, tile), lambda j, s: (0, ff_tile(j, s))),
            pl.BlockSpec((total, tile), lambda j, s: (0, own_tile(j))),
            pl.BlockSpec((total, tile), lambda j, s: (0, oth_tile(j))),
        ]
        out_shape += [
            shape_of((total, ff), f32),
            shape_of((total, ff // 2), bf16),
            shape_of((total, ff // 2), bf16),
        ]
    return pl.pallas_call(
        functools.partial(mlp_kernel, micros, tiles, save),
        grid_spec=pltpu.PrefetchScalarGridSpec(
            num_scalar_prefetch=1,
            grid=(2 * tiles,),
            in_specs=[whole((rows, half))] * (2 * micros)
            + [
                pl.BlockSpec((1, tile), lambda j, s: (0, ff_tile(j, s))),
                whole((1, dim)),
                pl.BlockSpec((half, tile), lambda j, s: (0, ff_tile(j, s))),
                pl.BlockSpec((half, tile), lambda j, s: (0, ff_tile(j, s))),
                pl.BlockSpec((tile, dim), lambda j, s: (own_tile(j), 0)),
                pl.BlockSpec((tile, dim), lambda j, s: (oth_tile(j), 0)),
            ],
            out_specs=out_specs,
            scratch_shapes=[pltpu.VMEM((total, half), bf16), pltpu.VMEM((total, half), bf16)],
        ),
        out_shape=out_shape,
        name="mlp_forward",
        **params_of(4 * total * dim * ff, 4 * dim * ff + 8 * total * ff),
    )(wsh, *nm_own, *nm_oth, up_b, down_b, up_own, up_oth, dn_own, dn_oth)


def mlp_back_kernel(micros, tiles, half, wsh_ref, *refs):
    dys = refs[:micros]
    u_ref, up_own, up_oth, dn_own, dn_oth = refs[micros : micros + 5]
    du_ref, dnm_ref, dy_s, acc_own, acc_oth = refs[micros + 5 :]
    step = pl.program_id(0)

    @pl.when(step == 0)
    def _():
        gather_rows(dy_s, dys)
        acc_own[...] = jnp.zeros(acc_own.shape, f32)
        acc_oth[...] = jnp.zeros(acc_oth.shape, f32)

    def finish(down):
        pre = u_ref[...]
        dact = dot_nt(dy_s[...], down)
        slope = 0.5 * (1.0 + lax.erf(pre * INV_SQRT2)) + pre * (
            INV_SQRT_2PI * jnp.exp(-0.5 * pre * pre)
        )
        du = (dact * slope).astype(bf16)
        du_ref[...] = du
        acc_own[...] += dot_nt(du, up_own[...])
        acc_oth[...] += dot_nt(du, up_oth[...])

    @pl.when(step < tiles)
    def _():
        finish(dn_own[...])

    @pl.when(step >= tiles)
    def _():
        finish(dn_oth[...])

    @pl.when(step == 2 * tiles - 1)
    def _():
        first = wsh_ref[0] == 0
        dnm_ref[:, :half] = jnp.where(first, acc_own[...], acc_oth[...])
        dnm_ref[:, half:] = jnp.where(first, acc_oth[...], acc_own[...])


def mlp_back_call(dys, pre, up_own, up_oth, dn_own, dn_oth, wsh):
    micros = len(dys)
    rows, dim = dys[0].shape
    half = up_own.shape[0]
    total = micros * rows
    ff = pre.shape[1]
    tile = 512
    tiles = ff // tile // 2
    ff_tile, own_tile, oth_tile = ff_maps(tiles)
    by_ff = lambda j, s: (0, ff_tile(j, s))
    return pl.pallas_call(
        functools.partial(mlp_back_kernel, micros, tiles, half),
        grid_spec=pltpu.PrefetchScalarGridSpec(
            num_scalar_prefetch=1,
            grid=(2 * tiles,),
            in_specs=[whole((rows, dim))] * micros
            + [
                pl.BlockSpec((total, tile), by_ff),
                pl.BlockSpec((half, tile), by_ff),
                pl.BlockSpec((half, tile), by_ff),
                pl.BlockSpec((tile, dim), lambda j, s: (own_tile(j), 0)),
                pl.BlockSpec((tile, dim), lambda j, s: (oth_tile(j), 0)),
            ],
            out_specs=[pl.BlockSpec((total, tile), by_ff), whole((total, dim))],
            scratch_shapes=[
                pltpu.VMEM((total, dim), bf16),
                pltpu.VMEM((total, half), f32),
                pltpu.VMEM((total, half), f32),
            ],
        ),
        out_shape=[shape_of((total, ff), bf16), shape_of((total, dim), f32)],
        name="mlp_backward",
        **params_of(4 * total * dim * ff, 4 * dim * ff + 8 * total * ff),
    )(wsh, *dys, pre, up_own, up_oth, dn_own, dn_oth)


def sort_in(loc_ref, ref, dst, half_rows, part=None):
    for block in range(dst.shape[0] // half_rows):
        place = loc_ref[block]
        rows = pl.ds(pl.multiple_of((place % 2) * half_rows, half_rows), half_rows)
        if part is None:
            vals = ref[place // 2, rows, :]
        else:
            vals = ref[place // 2, part, rows, :]
        dst[block * half_rows : (block + 1) * half_rows] = vals


def sort_out(loc_ref, vals, ref, half_rows, part=None):
    for block in range(vals.shape[0] // half_rows):
        place = loc_ref[block]
        rows = pl.ds(pl.multiple_of((place % 2) * half_rows, half_rows), half_rows)
        piece = vals[block * half_rows : (block + 1) * half_rows]
        if part is None:
            ref[place // 2, rows, :] = piece
        else:
            ref[place // 2, part, rows, :] = piece


def head_of(vals, head):
    lane = lax.broadcasted_iota(jnp.int32, vals.shape, 1)
    return jnp.where(lane // (LANES // 2) == head, vals, jnp.zeros_like(vals))


def scores_of(keys, queries, scale, diagonal):
    scores = dot_nt(keys, queries) * scale
    if diagonal:
        key_at = lax.broadcasted_iota(jnp.int32, scores.shape, 0)
        query_at = lax.broadcasted_iota(jnp.int32, scores.shape, 1)
        scores = jnp.where(key_at <= query_at, scores, MASKED_SCORE)
    return scores


def attend_kernel(tile, loc_ref, qkv_ref, o_ref, lse_ref, q_s, k_s, v_s, vt_s, o_s):
    half_rows = qkv_ref.shape[2] // 2
    seq = q_s.shape[0]
    head_size = LANES // 2
    scale = head_size**-0.5
    sort_in(loc_ref, qkv_ref, q_s, half_rows, 0)
    sort_in(loc_ref, qkv_ref, k_s, half_rows, 1)
    sort_in(loc_ref, qkv_ref, v_s, half_rows, 2)
    vt_s[...] = v_s[...].T
    for t in range(seq // tile):
        rows = slice(t * tile, (t + 1) * tile)
        queries = q_s[rows]
        outs = []
        for head in range(2):
            picked = head_of(queries, head)
            parts = [
                scores_of(k_s[i * tile : (i + 1) * tile], picked, scale, i == t)
                for i in range(t + 1)
            ]
            top = functools.reduce(
                jnp.maximum, [jnp.max(p, axis=0, keepdims=True) for p in parts]
            )
            parts = [jnp.exp(p - top) for p in parts]
            total = sum(jnp.sum(p, axis=0, keepdims=True) for p in parts)
            lse_ref[head : head + 1, rows] = top + jnp.log(total)
            inverse = 1.0 / total
            acc = None
            for i, p in enumerate(parts):
                term = dot_nn(
                    vt_s[head * head_size : (head + 1) * head_size, i * tile : (i + 1) * tile],
                    (p * inverse).astype(bf16),
                )
                acc = term if acc is None else acc + term
            outs.append(acc)
        o_s[rows] = jnp.concatenate(outs, axis=0).T.astype(bf16)
    sort_out(loc_ref, o_s, o_ref, half_rows)


def attend_call(qkv, loc):
    count, _, rows, _ = qkv.shape
    seq = count * rows
    return pl.pallas_call(
        functools.partial(attend_kernel, 256),
        grid_spec=pltpu.PrefetchScalarGridSpec(
            num_scalar_prefetch=1,
            grid=(1,),
            in_specs=[whole(qkv.shape)],
            out_specs=[whole((count, rows, LANES)), whole((2, seq))],
            scratch_shapes=[
                pltpu.VMEM((seq, LANES), bf16),
                pltpu.VMEM((seq, LANES), bf16),
                pltpu.VMEM((seq, LANES), bf16),
                pltpu.VMEM((LANES, seq), bf16),
                pltpu.VMEM((seq, LANES), bf16),
            ],
        ),
        out_shape=[shape_of((count, rows, LANES), bf16), shape_of((2, seq), f32)],
        name="attention",
        **params_of(8 * seq * seq * LANES, 8 * seq * LANES),
    )(loc, qkv)


def attend_back_kernel(
    tile, loc_ref, qkv_ref, da_ref, lse_ref, out_ref, q_s, k_s, v_s, da_s, kt_s, dq_s, dk_s, dv_s
):
    half_rows = qkv_ref.shape[2] // 2
    seq = q_s.shape[0]
    head_size = LANES // 2
    scale = head_size**-0.5
    sort_in(loc_ref, qkv_ref, q_s, half_rows, 0)
    sort_in(loc_ref, qkv_ref, k_s, half_rows, 1)
    sort_in(loc_ref, qkv_ref, v_s, half_rows, 2)
    sort_in(loc_ref, da_ref, da_s, half_rows)
    kt_s[...] = k_s[...].T
    dk_s[...] = jnp.zeros(dk_s.shape, f32)
    dv_s[...] = jnp.zeros(dv_s.shape, f32)
    for t in range(seq // tile):
        rows = slice(t * tile, (t + 1) * tile)
        outs = []
        for head in range(2):
            queries = head_of(q_s[rows], head)
            grads = head_of(da_s[rows], head)
            lse = lse_ref[head : head + 1, rows]
            probs, dprobs, row_dot = [], [], 0.0
            for i in range(t + 1):
                keys = slice(i * tile, (i + 1) * tile)
                p = jnp.exp(scores_of(k_s[keys], queries, scale, i == t) - lse)
                dp = dot_nt(v_s[keys], grads)
                row_dot = row_dot + jnp.sum(p * dp, axis=0, keepdims=True)
                dv_s[keys] += dot_nn(p.astype(bf16), grads)
                probs.append(p)
                dprobs.append(dp)
            acc = None
            for i in range(t + 1):
                keys = slice(i * tile, (i + 1) * tile)
                ds = (probs[i] * (dprobs[i] - row_dot) * scale).astype(bf16)
                dk_s[keys] += dot_nn(ds, queries)
                term = dot_nn(kt_s[head * head_size : (head + 1) * head_size, keys], ds)
                acc = term if acc is None else acc + term
            outs.append(acc)
        dq_s[rows] = jnp.concatenate(outs, axis=0).T.astype(bf16)
    sort_out(loc_ref, dq_s, out_ref, half_rows, 0)
    k_s[...] = dk_s[...].astype(bf16)
    v_s[...] = dv_s[...].astype(bf16)
    sort_out(loc_ref, k_s, out_ref, half_rows, 1)
    sort_out(loc_ref, v_s, out_ref, half_rows, 2)


def attend_back_call(qkv, da, lse, loc):
    count, _, rows, _ = qkv.shape
    seq = count * rows
    return pl.pallas_call(
        functools.partial(attend_back_kernel, 256),
        grid_spec=pltpu.PrefetchScalarGridSpec(
            num_scalar_prefetch=1,
            grid=(1,),
            in_specs=[whole(qkv.shape), whole(da.shape), whole(lse.shape)],
            out_specs=whole(qkv.shape),
            scratch_shapes=[
                pltpu.VMEM((seq, LANES), bf16),
                pltpu.VMEM((seq, LANES), bf16),
                pltpu.VMEM((seq, LANES), bf16),
                pltpu.VMEM((seq, LANES), bf16),
                pltpu.VMEM((LANES, seq), bf16),
                pltpu.VMEM((seq, LANES), bf16),
                pltpu.VMEM((seq, LANES), f32),
                pltpu.VMEM((seq, LANES), f32),
            ],
        ),
        out_shape=shape_of(qkv.shape, bf16),
        name="attention_backward",
        **params_of(20 * seq * seq * LANES, 14 * seq * LANES),
    )(loc, qkv, da, lse)


def by_head(parts):
    pairs, rows, lanes = parts.shape
    return jnp.transpose(parts, (1, 0, 2)).reshape(rows, HEADS, pairs * lanes // HEADS)


def by_pair(heads):
    rows = heads.shape[0]
    return jnp.transpose(heads.reshape(rows, -1, LANES), (1, 0, 2))


def wide_scores(queries, keys, query_pos, key_pos):
    raw = jnp.einsum("qhd,khd->hqk", queries, keys, preferred_element_type=f32)
    allowed = (query_pos[:, None] >= key_pos[None, :])[None]
    return jnp.where(allowed, raw * queries.shape[-1] ** (-0.5), MASKED_SCORE)


def key_blocks(arrays, rows):
    return tuple(a.reshape((a.shape[0] // rows, rows) + a.shape[1:]) for a in arrays)


def wide_attend(qkv, query_pos, key_pos):
    queries = by_head(qkv[:, 0])
    keys = lax.all_gather(by_head(qkv[:, 1]), "ctx", axis=0, tiled=True)
    values = lax.all_gather(by_head(qkv[:, 2]), "ctx", axis=0, tiled=True)
    block = min(512, keys.shape[0])
    split = key_blocks((keys, values, key_pos), block)
    rows, _, head_size = queries.shape

    def max_step(carry, block_in):
        top, total = carry
        scores = wide_scores(queries, block_in[0], query_pos, block_in[2])
        new_top = jnp.maximum(top, jnp.max(scores, axis=-1))
        part = jnp.sum(jnp.exp(scores - new_top[..., None]), axis=-1)
        return ((new_top, total * jnp.exp(top - new_top) + part), None)

    start = (jnp.full((HEADS, rows), MASKED_SCORE, f32), jnp.zeros((HEADS, rows), f32))
    (top, total), _ = lax.scan(max_step, start, split)
    lse = top + jnp.log(total)

    def value_step(running, block_in):
        scores = wide_scores(queries, block_in[0], query_pos, block_in[2])
        probs = jnp.exp(scores - lse[..., None]).astype(bf16)
        term = jnp.einsum("hqk,khd->qhd", probs, block_in[1], preferred_element_type=f32)
        return (running + term, None)

    attended, _ = lax.scan(value_step, jnp.zeros((rows, HEADS, head_size), f32), split)
    return by_pair(attended.astype(bf16)), (queries, keys, values, lse)


def wide_attend_back(kept, da, query_pos, key_pos):
    queries, keys, values, lse = kept
    grads = by_head(da)
    block = min(512, keys.shape[0])
    split = key_blocks((keys, values, key_pos), block)
    scale = queries.shape[-1] ** (-0.5)

    def pieces(block_in):
        scores = wide_scores(queries, block_in[0], query_pos, block_in[2])
        probs = jnp.exp(scores - lse[..., None])
        dprobs = jnp.einsum("qhd,khd->hqk", grads, block_in[1], preferred_element_type=f32)
        return probs, dprobs

    def dot_step(running, block_in):
        probs, dprobs = pieces(block_in)
        return (running + jnp.sum(probs * dprobs, axis=-1), None)

    row_dot, _ = lax.scan(dot_step, jnp.zeros(lse.shape, f32), split)

    def key_step(running, block_in):
        probs, dprobs = pieces(block_in)
        ds = (scale * probs * (dprobs - row_dot[..., None])).astype(bf16)
        running = running + jnp.einsum("hqk,khd->qhd", ds, block_in[0], preferred_element_type=f32)
        dk = jnp.einsum("hqk,qhd->khd", ds, queries, preferred_element_type=f32)
        dv = jnp.einsum("hqk,qhd->khd", probs.astype(bf16), grads, preferred_element_type=f32)
        return (running, (dk.astype(bf16), dv.astype(bf16)))

    dq, (dk, dv) = lax.scan(key_step, jnp.zeros(queries.shape, f32), split)
    dk, dv = (
        lax.psum_scatter(part.reshape(keys.shape), "ctx", scatter_dimension=0, tiled=True)
        for part in (dk, dv)
    )
    return jnp.stack([by_pair(dq.astype(bf16)), by_pair(dk), by_pair(dv)], axis=1)


def lanes_of(ref):
    return jnp.concatenate([ref[i] for i in range(ref.shape[0])], axis=1)


def proj_kernel(half, wsh_ref, a_ref, x_ref, mlp_ref, bias_ref, p_own, p_oth, y_ref, a_own, a_oth):
    first = wsh_ref[0] == 0
    a = lanes_of(a_ref)
    own = jnp.where(first, a[:, :half], a[:, half:])
    oth = jnp.where(first, a[:, half:], a[:, :half])
    a_own[...] = own
    a_oth[...] = oth
    attn = dot_nn(own, p_own[...]) + dot_nn(oth, p_oth[...]) + bias_ref[...]
    y_ref[...] = (x_ref[...].astype(f32) + attn + mlp_ref[...]).astype(bf16)


def proj_call(a, x, mlp, micro, bias, p_own, p_oth, wsh):
    rows, dim = x.shape
    half = p_own.shape[0]
    return pl.pallas_call(
        functools.partial(proj_kernel, half),
        grid_spec=pltpu.PrefetchScalarGridSpec(
            num_scalar_prefetch=1,
            grid=(1,),
            in_specs=[
                whole(a.shape),
                whole(x.shape),
                pl.BlockSpec((rows, dim), lambda j, s: (micro, 0)),
                whole(bias.shape),
                whole(p_own.shape),
                whole(p_oth.shape),
            ],
            out_specs=[whole((rows, dim)), whole((rows, half)), whole((rows, half))],
        ),
        out_shape=[shape_of((rows, dim), bf16)] + [shape_of((rows, half), bf16)] * 2,
        name="attn_out",
        **params_of(2 * rows * dim * dim, 2 * dim * dim + 10 * rows * dim),
    )(wsh, a, x, mlp, bias, p_own, p_oth)


def da_kernel(wsh_ref, dy_ref, p_own, p_oth, out_ref):
    dy = dy_ref[...]
    wsh = wsh_ref[0]
    count = out_ref.shape[0] // 2
    for place, weight in ((wsh * count, p_own), ((1 - wsh) * count, p_oth)):
        part = dot_nt(dy, weight[...]).astype(bf16)
        for i in range(count):
            out_ref[place + i] = part[:, i * LANES : (i + 1) * LANES]


def da_call(dy, p_own, p_oth, wsh):
    rows, dim = dy.shape
    pairs = dim // LANES
    return pl.pallas_call(
        da_kernel,
        grid_spec=pltpu.PrefetchScalarGridSpec(
            num_scalar_prefetch=1,
            grid=(1,),
            in_specs=[whole(dy.shape), whole(p_own.shape), whole(p_oth.shape)],
            out_specs=whole((pairs, rows, LANES)),
        ),
        out_shape=shape_of((pairs, rows, LANES), bf16),
        name="attn_out_backward",
        **params_of(2 * rows * dim * dim, 2 * dim * dim + 4 * rows * dim),
    )(wsh, dy, p_own, p_oth)


def dx_kernel(half, steps, wsh_ref, dqkv_ref, tab_ref, x_ref, dy_ref, dnm_ref, vec_ref, *rest):
    weights = rest[:6]
    back_ref, dx_ref, sums_ref, acc_own, acc_oth = rest[6:]
    step = pl.program_id(0)

    @pl.when(step == 0)
    def _():
        acc_own[...] = jnp.zeros(acc_own.shape, f32)
        acc_oth[...] = jnp.zeros(acc_oth.shape, f32)

    for part in range(3):
        cols = []
        for pair in range(dqkv_ref.shape[0]):
            vals = dqkv_ref[pair, part]
            if part < 2:
                vals = unrope(vals.astype(f32), tab_ref).astype(bf16)
            back_ref[pair, part] = vals
            cols.append(vals)
        grad = jnp.concatenate(cols, axis=1)
        acc_own[...] += dot_nt(grad, weights[2 * part][...])
        acc_oth[...] += dot_nt(grad, weights[2 * part + 1][...])

    @pl.when(step == steps - 1)
    def _():
        first = wsh_ref[0] == 0
        own, oth = acc_own[...], acc_oth[...]
        dna = jnp.concatenate(
            [jnp.where(first, own, oth), jnp.where(first, oth, own)], axis=1
        )
        dnm = dnm_ref[...]
        xhat, scale = normalized(x_ref[...].astype(f32))
        grad = dna * vec_ref[0:1] + dnm * vec_ref[2:3]
        inner = (
            grad
            - jnp.mean(grad, axis=-1, keepdims=True)
            - xhat * jnp.mean(grad * xhat, axis=-1, keepdims=True)
        )
        dx_ref[...] = (dy_ref[...].astype(f32) + scale * inner).astype(bf16)
        sums_ref[0:1] = jnp.sum(dna * xhat, axis=0, keepdims=True)
        sums_ref[1:2] = jnp.sum(dna, axis=0, keepdims=True)
        sums_ref[2:3] = jnp.sum(dnm * xhat, axis=0, keepdims=True)
        sums_ref[3:4] = jnp.sum(dnm, axis=0, keepdims=True)


def dx_call(dqkv, tab, x, dy, dnm, micro, vecs, w_own, w_oth, wsh):
    rows, dim = x.shape
    half = w_own.shape[0]
    tile = 2 * LANES
    steps = dim // tile
    block = (tile // LANES, 3, rows, LANES)

    def col(part):
        return lambda j, s: (0, part * steps + j)

    wspecs = []
    for part in range(3):
        wspecs += [pl.BlockSpec((half, tile), col(part))] * 2
    return pl.pallas_call(
        functools.partial(dx_kernel, half, steps),
        grid_spec=pltpu.PrefetchScalarGridSpec(
            num_scalar_prefetch=1,
            grid=(steps,),
            in_specs=[
                pl.BlockSpec(block, lambda j, s: (j, 0, 0, 0)),
                whole(tab.shape),
                whole(x.shape),
                whole(dy.shape),
                pl.BlockSpec((rows, dim), lambda j, s: (micro, 0)),
                whole(vecs.shape),
            ]
            + wspecs,
            out_specs=[
                pl.BlockSpec(block, lambda j, s: (j, 0, 0, 0)),
                whole((rows, dim)),
                whole((4, dim)),
            ],
            scratch_shapes=[pltpu.VMEM((rows, half), f32), pltpu.VMEM((rows, half), f32)],
        ),
        out_shape=[
            shape_of(dqkv.shape, bf16),
            shape_of((rows, dim), bf16),
            shape_of((4, dim), f32),
        ],
        name="section_input_grad",
        **params_of(6 * rows * dim * dim, 6 * dim * dim + 16 * rows * dim),
    )(wsh, dqkv, tab, x, dy, dnm, vecs, w_own, w_oth, w_own, w_oth, w_own, w_oth)


def stack_rows(refs, cols=slice(None)):
    return jnp.concatenate([ref[:, cols] for ref in refs], axis=0)


def row_grad_kernel(xs, dys, *refs):
    x_refs, dy_refs = refs[:xs], refs[xs : xs + dys]
    out_ref, sum_ref, dy_s = refs[xs + dys :]

    @pl.when(pl.program_id(0) == 0)
    def _():
        dy = stack_rows(dy_refs)
        dy_s[...] = dy
        sum_ref[...] = jnp.sum(dy.astype(f32), axis=0, keepdims=True)

    out_ref[...] = dot_nn(stack_rows(x_refs).T, dy_s[...]).astype(bf16)


def row_grad_call(x_list, dy_list, name):
    cols = x_list[0].shape[1]
    dim = dy_list[0].shape[1]
    total = sum(x.shape[0] for x in x_list)
    tile = 256
    return pl.pallas_call(
        functools.partial(row_grad_kernel, len(x_list), len(dy_list)),
        grid=(cols // tile,),
        in_specs=[pl.BlockSpec((x.shape[0], tile), lambda j: (0, j)) for x in x_list]
        + [whole(dy.shape) for dy in dy_list],
        out_specs=[pl.BlockSpec((tile, dim), lambda j: (j, 0)), whole((1, dim))],
        out_shape=[shape_of((cols, dim), bf16), shape_of((1, dim), f32)],
        scratch_shapes=[pltpu.VMEM((total, dim), bf16)],
        name=name,
        **params_of(2 * total * cols * dim, 2 * cols * dim + 2 * total * (cols + dim)),
    )(*x_list, *dy_list)


def col_grad_kernel(xs, dys, *refs):
    x_refs, dy_refs = refs[:xs], refs[xs : xs + dys]
    out_ref, sum_ref, xt_s = refs[xs + dys :]

    @pl.when(pl.program_id(0) == 0)
    def _():
        xt_s[...] = stack_rows(x_refs).T

    dy = stack_rows(dy_refs)
    sum_ref[...] = jnp.sum(dy.astype(f32), axis=0, keepdims=True)
    out_ref[...] = dot_nn(xt_s[...], dy).astype(bf16)


def up_grad_call(x_list, du_list):
    half = x_list[0].shape[1]
    ff = du_list[0].shape[1]
    total = sum(x.shape[0] for x in x_list)
    tile = 512
    return pl.pallas_call(
        functools.partial(col_grad_kernel, len(x_list), len(du_list)),
        grid=(ff // tile,),
        in_specs=[whole(x.shape) for x in x_list]
        + [pl.BlockSpec((d.shape[0], tile), lambda j: (0, j)) for d in du_list],
        out_specs=[
            pl.BlockSpec((half, tile), lambda j: (0, j)),
            pl.BlockSpec((1, tile), lambda j: (0, j)),
        ],
        out_shape=[shape_of((half, ff), bf16), shape_of((1, ff), f32)],
        scratch_shapes=[pltpu.VMEM((half, total), bf16)],
        name="up_grad",
        **params_of(2 * total * half * ff, 2 * half * ff + 2 * total * ff),
    )(*x_list, *du_list)


def qkv_grad_kernel(xs, *refs):
    x_refs, d_refs = refs[:xs], refs[xs : 2 * xs]
    out_ref, sum_ref, xt_s = refs[2 * xs :]

    @pl.when((pl.program_id(0) == 0) & (pl.program_id(1) == 0))
    def _():
        xt_s[...] = stack_rows(x_refs).T

    dy = jnp.concatenate([lanes_of(ref.at[:, 0]) for ref in d_refs], axis=0)
    sum_ref[...] = jnp.sum(dy.astype(f32), axis=0, keepdims=True)
    out_ref[...] = dot_nn(xt_s[...], dy).astype(bf16)


def qkv_grad_call(x_list, d_list):
    half = x_list[0].shape[1]
    pairs, _, rows, _ = d_list[0].shape
    dim = pairs * LANES
    total = sum(x.shape[0] for x in x_list)
    group = 4
    steps = pairs // group
    tile = group * LANES
    return pl.pallas_call(
        functools.partial(qkv_grad_kernel, len(x_list)),
        grid=(3, steps),
        in_specs=[whole(x.shape) for x in x_list]
        + [pl.BlockSpec((group, 1, rows, LANES), lambda i, j: (j, i, 0, 0)) for _ in d_list],
        out_specs=[
            pl.BlockSpec((half, tile), lambda i, j: (0, i * steps + j)),
            pl.BlockSpec((1, tile), lambda i, j: (0, i * steps + j)),
        ],
        out_shape=[shape_of((half, 3 * dim), bf16), shape_of((1, 3 * dim), f32)],
        scratch_shapes=[pltpu.VMEM((half, total), bf16)],
        name="qkv_grad",
        **params_of(6 * total * half * dim, 6 * half * dim + 6 * total * dim),
    )(*x_list, *d_list)


def ring_of(count):
    return list(range(0, count, 2)) + list(range(count - 1, 0, -2))


def ring_place(axis):
    count = lax.axis_size(axis)
    me = lax.axis_index(axis)
    return jnp.where(me % 2 == 0, me // 2, count - (me + 1) // 2)


def ring_shift(vals, axis, by):
    order = ring_of(lax.axis_size(axis))
    count = len(order)
    pairs = [(order[i], order[(i + by) % count]) for i in range(count)]
    return lax.ppermute(vals, axis, pairs)


def low_sum(*terms):
    total = terms[0].astype(f32)
    for term in terms[1:]:
        total = total + term.astype(f32)
    return total.astype(bf16)


def ring_sum(own, axis):
    count = lax.axis_size(axis)
    place = ring_place(axis)
    full_rows, cols = own.shape
    rows = full_rows // count
    own = own.reshape(count, rows, cols)
    half = count // 2
    cut = rows // 2

    def index(k):
        return (place + (k + count)) % count

    def take(k):
        return lax.dynamic_index_in_dim(own, index(k), 0, keepdims=False)

    far = take(half)
    ahead = ring_shift(far[:cut], axis, 1)
    behind = ring_shift(far[cut:], axis, -1)
    for k in range(half - 1, 0, -1):
        mine_a, mine_b = take(k), take(-k)
        if k == half - 1:
            ahead = jnp.concatenate([low_sum(mine_a[:cut], ahead), mine_a[cut:]], axis=0)
            behind = jnp.concatenate([mine_b[:cut], low_sum(mine_b[cut:], behind)], axis=0)
        else:
            ahead, behind = low_sum(mine_a, ahead), low_sum(mine_b, behind)
        ahead = ring_shift(ahead, axis, 1)
        behind = ring_shift(behind, axis, -1)
    mine = low_sum(take(0), ahead, behind)
    total = jnp.zeros((count, rows, cols), f32)

    def put(total, piece, k, at=0):
        return lax.dynamic_update_slice(total, piece.astype(f32)[None], (index(k), at, 0))

    total = put(total, mine, 0)
    ahead = ring_shift(mine, axis, 1)
    behind = ring_shift(mine, axis, -1)
    for k in range(1, half):
        last = k == half - 1
        next_ahead = ring_shift(ahead[:cut] if last else ahead, axis, 1)
        next_behind = ring_shift(behind[cut:] if last else behind, axis, -1)
        total = put(put(total, ahead, -k), behind, k)
        ahead, behind = next_ahead, next_behind
    total = put(put(total, ahead, -half), behind, half, cut)
    return total.reshape(full_rows, cols)


def swap(vals):
    return lax.ppermute(vals, "wsh", [(0, 1), (1, 0)])


def pass_on(vals, by):
    pairs = [(0, 1)] if by > 0 else [(1, 0)]
    return lax.ppermute(vals, "section", pairs)


def block_places(block_pair, count):
    want = jnp.arange(2 * count, dtype=jnp.int32)
    device = jnp.arange(count, dtype=jnp.int32)
    first = (block_pair[None, :] == want[:, None]).astype(jnp.int32)
    second = ((2 * count - 1 - block_pair)[None, :] == want[:, None]).astype(jnp.int32)
    return jnp.sum(first * (2 * device) + second * (2 * device + 1), axis=1)


def row_positions(block_pair, stored, tok_dev):
    count = block_pair.shape[0]
    device = stored // tok_dev
    within = stored % tok_dev
    half_rows = tok_dev // 2
    matches = device[:, None] == jnp.arange(count, dtype=jnp.int32)[None, :]
    pair_block = jnp.sum(jnp.where(matches, block_pair[None, :], 0), axis=1)
    block_idx = jnp.where(within < half_rows, pair_block, 2 * count - 1 - pair_block)
    return block_idx * half_rows + within % half_rows


def rotary_table(positions, head_size):
    half_rot = ROT // 2
    lane = jnp.arange(LANES, dtype=jnp.int32) % head_size
    inv_freq = ROPE_BASE ** (-((lane % half_rot).astype(f32) * 2.0) / ROT)
    angles = positions.astype(f32)[:, None] * inv_freq[None, :]
    cosine, sine = jnp.cos(angles), jnp.sin(angles)
    lead, second = (lane < half_rot)[None], ((lane >= half_rot) & (lane < ROT))[None]
    return jnp.stack(
        [
            jnp.where(lead | second, cosine, 1.0),
            jnp.where(lead, -sine, 0.0),
            jnp.where(second, sine, 0.0),
        ]
    )


def body(
    inputs,
    cotangent,
    block_pair,
    qkv_weight,
    qkv_bias,
    proj_weight,
    proj_bias,
    up_weight,
    up_bias,
    down_weight,
    down_bias,
    attn_gain,
    attn_shift,
    mlp_gain,
    mlp_shift,
):
    first_section = lax.axis_index("section") == 0
    count = lax.axis_size("ctx")
    micros, _, tok_dev, dim = inputs.shape
    head_size = dim // HEADS
    half = dim // 2
    my_half = lax.axis_index("wsh")
    wsh = my_half.astype(jnp.int32).reshape(1)
    one_pair_each = count == dim // LANES

    wq, wp, wu, wd = (w[0] for w in (qkv_weight, proj_weight, up_weight, down_weight))
    small = jnp.concatenate(
        [
            v[0].reshape(-1, half)
            for v in (
                attn_gain,
                attn_shift,
                mlp_gain,
                mlp_shift,
                proj_bias,
                down_bias,
                qkv_bias,
                up_bias,
            )
        ],
        axis=0,
    )
    small_oth = swap(small)
    wq_oth = swap(wq)
    wp_oth = swap(wp)
    wu_oth = swap(wu)
    wd_oth = swap(wd)
    low_part = jnp.where(my_half == 0, small, small_oth).astype(f32)
    high_part = jnp.where(my_half == 0, small_oth, small).astype(f32)
    vecs = jnp.concatenate([low_part[:6], high_part[:6]], axis=1)
    qkv_rows = 6 + qkv_bias.shape[1] // half
    proj_b, down_b = vecs[4:5], vecs[5:6]
    qkv_b = jnp.concatenate([low_part[6:qkv_rows], high_part[6:qkv_rows]], axis=0).reshape(1, -1)
    up_b = jnp.concatenate([low_part[qkv_rows:], high_part[qkv_rows:]], axis=0).reshape(1, -1)

    local_rows = lax.axis_index("ctx") * tok_dev + jnp.arange(tok_dev, dtype=jnp.int32)
    query_pos = row_positions(block_pair, local_rows, tok_dev)
    key_pos = row_positions(block_pair, jnp.arange(count * tok_dev, dtype=jnp.int32), tok_dev)
    tab = rotary_table(query_pos, head_size)
    loc = block_places(block_pair, count)

    def exchange(vals):
        return lax.all_to_all(vals, "ctx", split_axis=0, concat_axis=0, tiled=True)

    def attention(qkv_list):
        if one_pair_each:
            got = [exchange(qkv) for qkv in qkv_list]
            res = [attend_call(qkv, loc) for qkv in got]
            return [exchange(o) for o, _ in res], [
                (qkv, lse) for qkv, (_, lse) in zip(got, res)
            ]
        res = [wide_attend(qkv, query_pos, key_pos) for qkv in qkv_list]
        return [r[0] for r in res], [r[1] for r in res]

    def attention_back(kept, da_list):
        if one_pair_each:
            got = [exchange(da) for da in da_list]
            res = [attend_back_call(k[0], da, k[1], loc) for k, da in zip(kept, got)]
            return [exchange(d) for d in res]
        return [wide_attend_back(k, da, query_pos, key_pos) for k, da in zip(kept, da_list)]

    def forward(xs, save):
        made = [qkv_call(x, vecs, qkv_b, tab, wq, wq_oth, wsh) for x in xs]
        mlp = mlp_call(
            [m[3] for m in made], [m[4] for m in made],
            up_b, down_b, wu, wu_oth, wd, wd_oth, wsh, save,
        )
        attended, kept = attention([m[0] for m in made])
        outs = [
            proj_call(a, x, mlp[0], i, proj_b, wp, wp_oth, wsh)
            for i, (a, x) in enumerate(zip(attended, xs))
        ]
        return [o[0] for o in outs], (made, mlp, outs, kept)

    def backward(dys, xs, saved):
        made, mlp, outs, kept = saved
        da = [da_call(dy, wp, wp_oth, wsh) for dy in dys]
        du, dnm = mlp_back_call(dys, mlp[1], wu, wu_oth, wd, wd_oth, wsh)
        dqkv = attention_back(kept, da)
        return du, [
            dx_call(d, tab, x, dy, dnm, i, vecs, wq, wq_oth, wsh)
            for i, (d, x, dy) in enumerate(zip(dqkv, xs, dys))
        ]

    given = [inputs[i, 0] for i in range(micros)]
    asked = [cotangent[i, 0] for i in range(micros)]
    early, _ = forward(given, False)
    xs = [jnp.where(first_section, g, pass_on(y, 1)) for g, y in zip(given, early)]
    ys, saved = forward(xs, True)
    _, late = backward(asked, xs, saved)
    dys = [jnp.where(first_section, pass_on(d[1], -1), c) for d, c in zip(late, asked)]
    du, back = backward(dys, xs, saved)

    made, mlp, outs, _ = saved
    dy_list = dys + [swap(dy) for dy in dys]
    down_grad, dy_sum = row_grad_call([mlp[2], swap(mlp[3])], dy_list, "down_grad")
    proj_grad, _ = row_grad_call(
        [o[1] for o in outs] + [swap(o[2]) for o in outs], dy_list, "proj_grad"
    )
    up_grad, du_sum = up_grad_call(
        [m[3] for m in made] + [swap(m[4]) for m in made], [du, swap(du)]
    )
    qkv_grad, dqkv_sum = qkv_grad_call(
        [m[1] for m in made] + [swap(m[2]) for m in made],
        [b[0] for b in back] + [swap(b[0]) for b in back],
    )
    down_grad = ring_sum(down_grad, "ctx")
    proj_grad = ring_sum(proj_grad, "ctx")
    up_grad = ring_sum(up_grad, "ctx")
    qkv_grad = ring_sum(qkv_grad, "ctx")

    norm_sums = sum(b[2] for b in back)
    norm_own = lax.dynamic_slice_in_dim(norm_sums, my_half * half, half, 1)
    norm_oth = swap(lax.dynamic_slice_in_dim(norm_sums, (1 - my_half) * half, half, 1))

    def own_part(vec):
        size = vec.shape[1] // 2
        return lax.dynamic_slice_in_dim(vec, my_half * size, size, 1).reshape(-1, half)

    small_sums = jnp.concatenate(
        [norm_own + norm_oth, own_part(dy_sum), own_part(dqkv_sum), own_part(du_sum)], axis=0
    )
    small_sums = jnp.sum(lax.all_gather(small_sums, "ctx"), axis=0)
    qkv_end = 5 + dqkv_sum.shape[1] // 2 // half
    dy_total = small_sums[4:5]
    layer_out = jnp.stack(ys)[None, :, None]
    input_grad = jnp.stack([b[1] for b in back])[None, :, None]
    return (
        layer_out,
        input_grad,
        qkv_grad[None],
        small_sums[5:qkv_end].reshape(1, -1),
        proj_grad[None],
        dy_total,
        up_grad[None],
        small_sums[qkv_end:].reshape(1, -1),
        down_grad[None],
        dy_total,
        small_sums[0:1],
        small_sums[1:2],
        small_sums[2:3],
        small_sums[3:4],
    )


def solution(mesh):
    in_specs = (
        P(None, "wsh", "ctx", None),
        P(None, "wsh", "ctx", None),
        P(),
        P("section", "wsh", None),
        P("section", "wsh"),
        P("section", "wsh", None),
        P("section", "wsh"),
        P("section", "wsh", None),
        P("section", "wsh"),
        P("section", "wsh", None),
        P("section", "wsh"),
        P("section", "wsh"),
        P("section", "wsh"),
        P("section", "wsh"),
        P("section", "wsh"),
    )
    out_specs = (
        P("section", None, "wsh", "ctx", None),
        P("section", None, "wsh", "ctx", None),
        P("section", "wsh", None),
        P("section", "wsh"),
        P("section", "wsh", None),
        P("section", "wsh"),
        P("section", "wsh", None),
        P("section", "wsh"),
        P("section", "wsh", None),
        P("section", "wsh"),
        P("section", "wsh"),
        P("section", "wsh"),
        P("section", "wsh"),
        P("section", "wsh"),
    )
    return jax.shard_map(body, mesh=mesh, in_specs=in_specs, out_specs=out_specs, check_vma=False)
```

```python
import functools

import jax
import jax.numpy as jnp
from jax import lax
from jax.experimental import pallas as pl
from jax.experimental.pallas import tpu as pltpu
from jax.sharding import PartitionSpec as P

HEADS = 16
ROT = 16
NORM_EPS = 1e-05
ROPE_BASE = 10000.0
MASKED_SCORE = -1e30
LANES = 128
VMEM_LIMIT = 60 * 1024 * 1024
INV_SQRT2 = 0.7071067811865476
INV_SQRT_2PI = 0.3989422804014327

f32 = jnp.float32
bf16 = jnp.bfloat16


def dot_nn(left, right):
    return lax.dot_general(left, right, (((1,), (0,)), ((), ())), preferred_element_type=f32)


def dot_nt(left, right):
    return lax.dot_general(left, right, (((1,), (1,)), ((), ())), preferred_element_type=f32)


def params_of(flops, nbytes, **extra):
    return dict(
        compiler_params=pltpu.CompilerParams(vmem_limit_bytes=VMEM_LIMIT),
        cost_estimate=pl.CostEstimate(flops=flops, bytes_accessed=nbytes, transcendentals=0),
        **extra,
    )


def whole(shape):
    rank = len(shape)
    return pl.BlockSpec(shape, lambda *args: (0,) * rank)


def shape_of(shape, dtype):
    return jax.ShapeDtypeStruct(shape, dtype)


def rope(vals, tab_ref):
    return (
        vals * tab_ref[0]
        + pltpu.roll(vals, LANES - ROT // 2, 1) * tab_ref[1]
        + pltpu.roll(vals, ROT // 2, 1) * tab_ref[2]
    )


def unrope(vals, tab_ref):
    return (
        vals * tab_ref[0]
        - pltpu.roll(vals, LANES - ROT // 2, 1) * tab_ref[1]
        - pltpu.roll(vals, ROT // 2, 1) * tab_ref[2]
    )


def normalized(hidden):
    row_mean = jnp.mean(hidden, axis=-1, keepdims=True)
    centered = hidden - row_mean
    spread = jnp.mean(centered * centered, axis=-1, keepdims=True)
    scale = lax.rsqrt(spread + NORM_EPS)
    return centered * scale, scale


def qkv_kernel(half, wsh_ref, given_ref, got_ref, vec_ref, bq, bk, bv, tab_ref, *rest):
    weights = rest[:6]
    out_ref, x_ref, na_own, na_oth, nm_own, nm_oth = rest[6:12]
    wsh = wsh_ref[0]

    @pl.when(pl.program_id(0) == 0)
    def _():
        x = jnp.where(wsh_ref[1] == 1, given_ref[...], got_ref[...])
        x_ref[...] = x
        xhat, _ = normalized(x.astype(f32))
        na = (xhat * vec_ref[0:1] + vec_ref[1:2]).astype(bf16)
        nm = (xhat * vec_ref[2:3] + vec_ref[3:4]).astype(bf16)
        first = wsh == 0
        na_own[...] = jnp.where(first, na[:, :half], na[:, half:])
        na_oth[...] = jnp.where(first, na[:, half:], na[:, :half])
        nm_own[...] = jnp.where(first, nm[:, :half], nm[:, half:])
        nm_oth[...] = jnp.where(first, nm[:, half:], nm[:, :half])

    for part, bias in enumerate((bq, bk, bv)):
        res = (
            dot_nn(na_own[...], weights[2 * part][...])
            + dot_nn(na_oth[...], weights[2 * part + 1][...])
            + bias[...]
        )
        for pair in range(res.shape[1] // LANES):
            vals = res[:, pair * LANES : (pair + 1) * LANES]
            if part < 2:
                vals = rope(vals, tab_ref)
            out_ref[pair, part] = vals.astype(bf16)


def qkv_call(given, got, vecs, qkv_b, tab, w_own, w_oth, wsh):
    rows, dim = given.shape
    half = w_own.shape[0]
    pairs = dim // LANES
    tile = 2 * LANES
    steps = dim // tile

    def col(part):
        return lambda j, s: (0, part * steps + j)

    wspecs = []
    for part in range(3):
        wspecs += [pl.BlockSpec((half, tile), col(part))] * 2
    return pl.pallas_call(
        functools.partial(qkv_kernel, half),
        grid_spec=pltpu.PrefetchScalarGridSpec(
            num_scalar_prefetch=1,
            grid=(steps,),
            in_specs=[
                whole((rows, dim)),
                whole((rows, dim)),
                whole(vecs.shape),
                pl.BlockSpec((1, tile), col(0)),
                pl.BlockSpec((1, tile), col(1)),
                pl.BlockSpec((1, tile), col(2)),
                whole(tab.shape),
            ]
            + wspecs,
            out_specs=[pl.BlockSpec((tile // LANES, 3, rows, LANES), lambda j, s: (j, 0, 0, 0))]
            + [whole((rows, dim))]
            + [whole((rows, half))] * 4,
        ),
        out_shape=[shape_of((pairs, 3, rows, LANES), bf16), shape_of((rows, dim), bf16)]
        + [shape_of((rows, half), bf16)] * 4,
        name="qkv_proj",
        **params_of(6 * rows * dim * dim, 6 * dim * dim + 8 * rows * dim),
    )(wsh, given, got, vecs, qkv_b, qkv_b, qkv_b, tab, w_own, w_oth, w_own, w_oth, w_own, w_oth)


def gather_rows(dst, refs, dtype=None):
    rows = refs[0].shape[0]
    for i, ref in enumerate(refs):
        dst[i * rows : (i + 1) * rows] = ref[...]


def mlp_kernel(micros, tiles, save, wsh_ref, *refs):
    owns, oths = refs[:micros], refs[micros : 2 * micros]
    up_b, down_b, up_own, up_oth, dn_own, dn_oth = refs[2 * micros : 2 * micros + 6]
    outs = refs[2 * micros + 6 :]
    if save:
        out_ref, u_ref, g_own, g_oth, own_s, oth_s = outs
    else:
        out_ref, own_s, oth_s = outs
    step = pl.program_id(0)

    @pl.when(step == 0)
    def _():
        gather_rows(own_s, owns)
        gather_rows(oth_s, oths)
        out_ref[...] = jnp.broadcast_to(down_b[...], out_ref.shape)

    pre = dot_nn(own_s[...], up_own[...]) + dot_nn(oth_s[...], up_oth[...]) + up_b[...]
    act = (0.5 * pre * (1.0 + lax.erf(pre * INV_SQRT2))).astype(bf16)
    if save:
        u_ref[...] = pre

    @pl.when(step < tiles)
    def _():
        if save:
            g_own[...] = act
        out_ref[...] += dot_nn(act, dn_own[...])

    @pl.when(step >= tiles)
    def _():
        if save:
            g_oth[...] = act
        out_ref[...] += dot_nn(act, dn_oth[...])


def ff_maps(tiles):
    def ff_tile(j, s):
        return (s[0] * tiles + j) % (2 * tiles)

    own_tile = lambda j: jnp.minimum(j, tiles - 1)
    oth_tile = lambda j: jnp.maximum(j - tiles, 0)
    return ff_tile, own_tile, oth_tile


def mlp_call(nm_own, nm_oth, up_b, down_b, up_own, up_oth, dn_own, dn_oth, wsh, save):
    micros = len(nm_own)
    rows, half = nm_own[0].shape
    total = micros * rows
    dim = dn_own.shape[1]
    ff = up_own.shape[1]
    tile = 512
    tiles = ff // tile // 2
    ff_tile, own_tile, oth_tile = ff_maps(tiles)
    out_specs = [whole((total, dim))]
    out_shape = [shape_of((total, dim), f32)]
    if save:
        out_specs += [
            pl.BlockSpec((total, tile), lambda j, s: (0, ff_tile(j, s))),
            pl.BlockSpec((total, tile), lambda j, s: (0, own_tile(j))),
            pl.BlockSpec((total, tile), lambda j, s: (0, oth_tile(j))),
        ]
        out_shape += [
            shape_of((total, ff), f32),
            shape_of((total, ff // 2), bf16),
            shape_of((total, ff // 2), bf16),
        ]
    return pl.pallas_call(
        functools.partial(mlp_kernel, micros, tiles, save),
        grid_spec=pltpu.PrefetchScalarGridSpec(
            num_scalar_prefetch=1,
            grid=(2 * tiles,),
            in_specs=[whole((rows, half))] * (2 * micros)
            + [
                pl.BlockSpec((1, tile), lambda j, s: (0, ff_tile(j, s))),
                whole((1, dim)),
                pl.BlockSpec((half, tile), lambda j, s: (0, ff_tile(j, s))),
                pl.BlockSpec((half, tile), lambda j, s: (0, ff_tile(j, s))),
                pl.BlockSpec((tile, dim), lambda j, s: (own_tile(j), 0)),
                pl.BlockSpec((tile, dim), lambda j, s: (oth_tile(j), 0)),
            ],
            out_specs=out_specs,
            scratch_shapes=[pltpu.VMEM((total, half), bf16), pltpu.VMEM((total, half), bf16)],
        ),
        out_shape=out_shape,
        name="mlp_forward",
        **params_of(4 * total * dim * ff, 4 * dim * ff + 8 * total * ff),
    )(wsh, *nm_own, *nm_oth, up_b, down_b, up_own, up_oth, dn_own, dn_oth)


def mlp_back_kernel(micros, tiles, half, wsh_ref, *refs):
    dys = refs[:micros]
    u_ref, up_own, up_oth, dn_own, dn_oth = refs[micros : micros + 5]
    du_ref, dnm_ref, dy_s, acc_own, acc_oth = refs[micros + 5 :]
    step = pl.program_id(0)

    @pl.when(step == 0)
    def _():
        gather_rows(dy_s, dys)
        acc_own[...] = jnp.zeros(acc_own.shape, f32)
        acc_oth[...] = jnp.zeros(acc_oth.shape, f32)

    def finish(down):
        pre = u_ref[...]
        dact = dot_nt(dy_s[...], down)
        slope = 0.5 * (1.0 + lax.erf(pre * INV_SQRT2)) + pre * (
            INV_SQRT_2PI * jnp.exp(-0.5 * pre * pre)
        )
        du = (dact * slope).astype(bf16)
        du_ref[...] = du
        acc_own[...] += dot_nt(du, up_own[...])
        acc_oth[...] += dot_nt(du, up_oth[...])

    @pl.when(step < tiles)
    def _():
        finish(dn_own[...])

    @pl.when(step >= tiles)
    def _():
        finish(dn_oth[...])

    @pl.when(step == 2 * tiles - 1)
    def _():
        first = wsh_ref[0] == 0
        dnm_ref[:, :half] = jnp.where(first, acc_own[...], acc_oth[...])
        dnm_ref[:, half:] = jnp.where(first, acc_oth[...], acc_own[...])


def mlp_back_call(dys, pre, up_own, up_oth, dn_own, dn_oth, wsh):
    micros = len(dys)
    rows, dim = dys[0].shape
    half = up_own.shape[0]
    total = micros * rows
    ff = pre.shape[1]
    tile = 512
    tiles = ff // tile // 2
    ff_tile, own_tile, oth_tile = ff_maps(tiles)
    by_ff = lambda j, s: (0, ff_tile(j, s))
    return pl.pallas_call(
        functools.partial(mlp_back_kernel, micros, tiles, half),
        grid_spec=pltpu.PrefetchScalarGridSpec(
            num_scalar_prefetch=1,
            grid=(2 * tiles,),
            in_specs=[whole((rows, dim))] * micros
            + [
                pl.BlockSpec((total, tile), by_ff),
                pl.BlockSpec((half, tile), by_ff),
                pl.BlockSpec((half, tile), by_ff),
                pl.BlockSpec((tile, dim), lambda j, s: (own_tile(j), 0)),
                pl.BlockSpec((tile, dim), lambda j, s: (oth_tile(j), 0)),
            ],
            out_specs=[pl.BlockSpec((total, tile), by_ff), whole((total, dim))],
            scratch_shapes=[
                pltpu.VMEM((total, dim), bf16),
                pltpu.VMEM((total, half), f32),
                pltpu.VMEM((total, half), f32),
            ],
        ),
        out_shape=[shape_of((total, ff), bf16), shape_of((total, dim), f32)],
        name="mlp_backward",
        **params_of(4 * total * dim * ff, 4 * dim * ff + 8 * total * ff),
    )(wsh, *dys, pre, up_own, up_oth, dn_own, dn_oth)


def sort_in(loc_ref, ref, dst, half_rows, part=None):
    for block in range(dst.shape[0] // half_rows):
        place = loc_ref[block]
        rows = pl.ds(pl.multiple_of((place % 2) * half_rows, half_rows), half_rows)
        if part is None:
            vals = ref[place // 2, rows, :]
        else:
            vals = ref[place // 2, part, rows, :]
        dst[block * half_rows : (block + 1) * half_rows] = vals


def sort_out(loc_ref, vals, ref, half_rows, part=None):
    for block in range(vals.shape[0] // half_rows):
        place = loc_ref[block]
        rows = pl.ds(pl.multiple_of((place % 2) * half_rows, half_rows), half_rows)
        piece = vals[block * half_rows : (block + 1) * half_rows]
        if part is None:
            ref[place // 2, rows, :] = piece
        else:
            ref[place // 2, part, rows, :] = piece


def head_of(vals, head):
    lane = lax.broadcasted_iota(jnp.int32, vals.shape, 1)
    return jnp.where(lane // (LANES // 2) == head, vals, jnp.zeros_like(vals))


def scores_of(keys, queries, scale, diagonal):
    scores = dot_nt(keys, queries) * scale
    if diagonal:
        key_at = lax.broadcasted_iota(jnp.int32, scores.shape, 0)
        query_at = lax.broadcasted_iota(jnp.int32, scores.shape, 1)
        scores = jnp.where(key_at <= query_at, scores, MASKED_SCORE)
    return scores


def attend_kernel(tile, loc_ref, qkv_ref, o_ref, lse_ref, q_s, k_s, v_s, vt_s, o_s):
    half_rows = qkv_ref.shape[2] // 2
    seq = q_s.shape[0]
    head_size = LANES // 2
    scale = head_size**-0.5
    sort_in(loc_ref, qkv_ref, q_s, half_rows, 0)
    sort_in(loc_ref, qkv_ref, k_s, half_rows, 1)
    sort_in(loc_ref, qkv_ref, v_s, half_rows, 2)
    vt_s[...] = v_s[...].T
    for t in range(seq // tile):
        rows = slice(t * tile, (t + 1) * tile)
        queries = q_s[rows]
        outs = []
        for head in range(2):
            picked = head_of(queries, head)
            parts = [
                scores_of(k_s[i * tile : (i + 1) * tile], picked, scale, i == t)
                for i in range(t + 1)
            ]
            top = functools.reduce(
                jnp.maximum, [jnp.max(p, axis=0, keepdims=True) for p in parts]
            )
            parts = [jnp.exp(p - top) for p in parts]
            total = sum(jnp.sum(p, axis=0, keepdims=True) for p in parts)
            lse_ref[head : head + 1, rows] = top + jnp.log(total)
            inverse = 1.0 / total
            acc = None
            for i, p in enumerate(parts):
                term = dot_nn(
                    vt_s[head * head_size : (head + 1) * head_size, i * tile : (i + 1) * tile],
                    (p * inverse).astype(bf16),
                )
                acc = term if acc is None else acc + term
            outs.append(acc)
        o_s[rows] = jnp.concatenate(outs, axis=0).T.astype(bf16)
    sort_out(loc_ref, o_s, o_ref, half_rows)


def attend_call(qkv, loc):
    count, _, rows, _ = qkv.shape
    seq = count * rows
    return pl.pallas_call(
        functools.partial(attend_kernel, 256),
        grid_spec=pltpu.PrefetchScalarGridSpec(
            num_scalar_prefetch=1,
            grid=(1,),
            in_specs=[whole(qkv.shape)],
            out_specs=[whole((count, rows, LANES)), whole((2, seq))],
            scratch_shapes=[
                pltpu.VMEM((seq, LANES), bf16),
                pltpu.VMEM((seq, LANES), bf16),
                pltpu.VMEM((seq, LANES), bf16),
                pltpu.VMEM((LANES, seq), bf16),
                pltpu.VMEM((seq, LANES), bf16),
            ],
        ),
        out_shape=[shape_of((count, rows, LANES), bf16), shape_of((2, seq), f32)],
        name="attention",
        **params_of(8 * seq * seq * LANES, 8 * seq * LANES),
    )(loc, qkv)


def attend_back_kernel(
    tile, loc_ref, qkv_ref, da_ref, lse_ref, out_ref, q_s, k_s, v_s, da_s, kt_s, dq_s, dk_s, dv_s
):
    half_rows = qkv_ref.shape[2] // 2
    seq = q_s.shape[0]
    head_size = LANES // 2
    scale = head_size**-0.5
    sort_in(loc_ref, qkv_ref, q_s, half_rows, 0)
    sort_in(loc_ref, qkv_ref, k_s, half_rows, 1)
    sort_in(loc_ref, qkv_ref, v_s, half_rows, 2)
    sort_in(loc_ref, da_ref, da_s, half_rows)
    kt_s[...] = k_s[...].T
    dk_s[...] = jnp.zeros(dk_s.shape, f32)
    dv_s[...] = jnp.zeros(dv_s.shape, f32)
    for t in range(seq // tile):
        rows = slice(t * tile, (t + 1) * tile)
        outs = []
        for head in range(2):
            queries = head_of(q_s[rows], head)
            grads = head_of(da_s[rows], head)
            lse = lse_ref[head : head + 1, rows]
            probs, dprobs, row_dot = [], [], 0.0
            for i in range(t + 1):
                keys = slice(i * tile, (i + 1) * tile)
                p = jnp.exp(scores_of(k_s[keys], queries, scale, i == t) - lse)
                dp = dot_nt(v_s[keys], grads)
                row_dot = row_dot + jnp.sum(p * dp, axis=0, keepdims=True)
                dv_s[keys] += dot_nn(p.astype(bf16), grads)
                probs.append(p)
                dprobs.append(dp)
            acc = None
            for i in range(t + 1):
                keys = slice(i * tile, (i + 1) * tile)
                ds = (probs[i] * (dprobs[i] - row_dot) * scale).astype(bf16)
                dk_s[keys] += dot_nn(ds, queries)
                term = dot_nn(kt_s[head * head_size : (head + 1) * head_size, keys], ds)
                acc = term if acc is None else acc + term
            outs.append(acc)
        dq_s[rows] = jnp.concatenate(outs, axis=0).T.astype(bf16)
    sort_out(loc_ref, dq_s, out_ref, half_rows, 0)
    k_s[...] = dk_s[...].astype(bf16)
    v_s[...] = dv_s[...].astype(bf16)
    sort_out(loc_ref, k_s, out_ref, half_rows, 1)
    sort_out(loc_ref, v_s, out_ref, half_rows, 2)


def attend_back_call(qkv, da, lse, loc):
    count, _, rows, _ = qkv.shape
    seq = count * rows
    return pl.pallas_call(
        functools.partial(attend_back_kernel, 256),
        grid_spec=pltpu.PrefetchScalarGridSpec(
            num_scalar_prefetch=1,
            grid=(1,),
            in_specs=[whole(qkv.shape), whole(da.shape), whole(lse.shape)],
            out_specs=whole(qkv.shape),
            scratch_shapes=[
                pltpu.VMEM((seq, LANES), bf16),
                pltpu.VMEM((seq, LANES), bf16),
                pltpu.VMEM((seq, LANES), bf16),
                pltpu.VMEM((seq, LANES), bf16),
                pltpu.VMEM((LANES, seq), bf16),
                pltpu.VMEM((seq, LANES), bf16),
                pltpu.VMEM((seq, LANES), f32),
                pltpu.VMEM((seq, LANES), f32),
            ],
        ),
        out_shape=shape_of(qkv.shape, bf16),
        name="attention_backward",
        **params_of(20 * seq * seq * LANES, 14 * seq * LANES),
    )(loc, qkv, da, lse)


def by_head(parts):
    pairs, rows, lanes = parts.shape
    return jnp.transpose(parts, (1, 0, 2)).reshape(rows, HEADS, pairs * lanes // HEADS)


def by_pair(heads):
    rows = heads.shape[0]
    return jnp.transpose(heads.reshape(rows, -1, LANES), (1, 0, 2))


def wide_scores(queries, keys, query_pos, key_pos):
    raw = jnp.einsum("qhd,khd->hqk", queries, keys, preferred_element_type=f32)
    allowed = (query_pos[:, None] >= key_pos[None, :])[None]
    return jnp.where(allowed, raw * queries.shape[-1] ** (-0.5), MASKED_SCORE)


def key_blocks(arrays, rows):
    return tuple(a.reshape((a.shape[0] // rows, rows) + a.shape[1:]) for a in arrays)


def wide_attend(qkv, query_pos, key_pos):
    queries = by_head(qkv[:, 0])
    keys = lax.all_gather(by_head(qkv[:, 1]), "ctx", axis=0, tiled=True)
    values = lax.all_gather(by_head(qkv[:, 2]), "ctx", axis=0, tiled=True)
    block = min(512, keys.shape[0])
    split = key_blocks((keys, values, key_pos), block)
    rows, _, head_size = queries.shape

    def max_step(carry, block_in):
        top, total = carry
        scores = wide_scores(queries, block_in[0], query_pos, block_in[2])
        new_top = jnp.maximum(top, jnp.max(scores, axis=-1))
        part = jnp.sum(jnp.exp(scores - new_top[..., None]), axis=-1)
        return ((new_top, total * jnp.exp(top - new_top) + part), None)

    start = (jnp.full((HEADS, rows), MASKED_SCORE, f32), jnp.zeros((HEADS, rows), f32))
    (top, total), _ = lax.scan(max_step, start, split)
    lse = top + jnp.log(total)

    def value_step(running, block_in):
        scores = wide_scores(queries, block_in[0], query_pos, block_in[2])
        probs = jnp.exp(scores - lse[..., None]).astype(bf16)
        term = jnp.einsum("hqk,khd->qhd", probs, block_in[1], preferred_element_type=f32)
        return (running + term, None)

    attended, _ = lax.scan(value_step, jnp.zeros((rows, HEADS, head_size), f32), split)
    return by_pair(attended.astype(bf16)), (queries, keys, values, lse)


def wide_attend_back(kept, da, query_pos, key_pos):
    queries, keys, values, lse = kept
    grads = by_head(da)
    block = min(512, keys.shape[0])
    split = key_blocks((keys, values, key_pos), block)
    scale = queries.shape[-1] ** (-0.5)

    def pieces(block_in):
        scores = wide_scores(queries, block_in[0], query_pos, block_in[2])
        probs = jnp.exp(scores - lse[..., None])
        dprobs = jnp.einsum("qhd,khd->hqk", grads, block_in[1], preferred_element_type=f32)
        return probs, dprobs

    def dot_step(running, block_in):
        probs, dprobs = pieces(block_in)
        return (running + jnp.sum(probs * dprobs, axis=-1), None)

    row_dot, _ = lax.scan(dot_step, jnp.zeros(lse.shape, f32), split)

    def key_step(running, block_in):
        probs, dprobs = pieces(block_in)
        ds = (scale * probs * (dprobs - row_dot[..., None])).astype(bf16)
        running = running + jnp.einsum("hqk,khd->qhd", ds, block_in[0], preferred_element_type=f32)
        dk = jnp.einsum("hqk,qhd->khd", ds, queries, preferred_element_type=f32)
        dv = jnp.einsum("hqk,qhd->khd", probs.astype(bf16), grads, preferred_element_type=f32)
        return (running, (dk.astype(bf16), dv.astype(bf16)))

    dq, (dk, dv) = lax.scan(key_step, jnp.zeros(queries.shape, f32), split)
    dk, dv = (
        lax.psum_scatter(part.reshape(keys.shape), "ctx", scatter_dimension=0, tiled=True)
        for part in (dk, dv)
    )
    return jnp.stack([by_pair(dq.astype(bf16)), by_pair(dk), by_pair(dv)], axis=1)


def lanes_of(ref):
    return jnp.concatenate([ref[i] for i in range(ref.shape[0])], axis=1)


def proj_kernel(half, wsh_ref, a_ref, x_ref, mlp_ref, bias_ref, p_own, p_oth, y_ref, a_own, a_oth):
    first = wsh_ref[0] == 0
    a = lanes_of(a_ref)
    own = jnp.where(first, a[:, :half], a[:, half:])
    oth = jnp.where(first, a[:, half:], a[:, :half])
    a_own[...] = own
    a_oth[...] = oth
    attn = dot_nn(own, p_own[...]) + dot_nn(oth, p_oth[...]) + bias_ref[...]
    y_ref[...] = (x_ref[...].astype(f32) + attn + mlp_ref[...]).astype(bf16)


def proj_call(a, x, mlp, micro, bias, p_own, p_oth, wsh):
    rows, dim = x.shape
    half = p_own.shape[0]
    return pl.pallas_call(
        functools.partial(proj_kernel, half),
        grid_spec=pltpu.PrefetchScalarGridSpec(
            num_scalar_prefetch=1,
            grid=(1,),
            in_specs=[
                whole(a.shape),
                whole(x.shape),
                pl.BlockSpec((rows, dim), lambda j, s: (micro, 0)),
                whole(bias.shape),
                whole(p_own.shape),
                whole(p_oth.shape),
            ],
            out_specs=[whole((rows, dim)), whole((rows, half)), whole((rows, half))],
        ),
        out_shape=[shape_of((rows, dim), bf16)] + [shape_of((rows, half), bf16)] * 2,
        name="attn_out",
        **params_of(2 * rows * dim * dim, 2 * dim * dim + 10 * rows * dim),
    )(wsh, a, x, mlp, bias, p_own, p_oth)


def da_kernel(wsh_ref, given_ref, got_ref, p_own, p_oth, out_ref, dy_ref):
    dy = jnp.where(wsh_ref[1] == 1, got_ref[...], given_ref[...])
    dy_ref[...] = dy
    wsh = wsh_ref[0]
    count = out_ref.shape[0] // 2
    for place, weight in ((wsh * count, p_own), ((1 - wsh) * count, p_oth)):
        part = dot_nt(dy, weight[...]).astype(bf16)
        for i in range(count):
            out_ref[place + i] = part[:, i * LANES : (i + 1) * LANES]


def da_call(given, got, p_own, p_oth, wsh):
    rows, dim = given.shape
    pairs = dim // LANES
    return pl.pallas_call(
        da_kernel,
        grid_spec=pltpu.PrefetchScalarGridSpec(
            num_scalar_prefetch=1,
            grid=(1,),
            in_specs=[whole((rows, dim))] * 2 + [whole(p_own.shape), whole(p_oth.shape)],
            out_specs=[whole((pairs, rows, LANES)), whole((rows, dim))],
        ),
        out_shape=[shape_of((pairs, rows, LANES), bf16), shape_of((rows, dim), bf16)],
        name="attn_out_backward",
        **params_of(2 * rows * dim * dim, 2 * dim * dim + 4 * rows * dim),
    )(wsh, given, got, p_own, p_oth)


def dx_kernel(half, steps, wsh_ref, dqkv_ref, tab_ref, x_ref, dy_ref, dnm_ref, vec_ref, *rest):
    weights = rest[:6]
    back_ref, dx_ref, sums_ref, acc_own, acc_oth = rest[6:]
    step = pl.program_id(0)

    @pl.when(step == 0)
    def _():
        acc_own[...] = jnp.zeros(acc_own.shape, f32)
        acc_oth[...] = jnp.zeros(acc_oth.shape, f32)

    for part in range(3):
        cols = []
        for pair in range(dqkv_ref.shape[0]):
            vals = dqkv_ref[pair, part]
            if part < 2:
                vals = unrope(vals.astype(f32), tab_ref).astype(bf16)
            back_ref[pair, part] = vals
            cols.append(vals)
        grad = jnp.concatenate(cols, axis=1)
        acc_own[...] += dot_nt(grad, weights[2 * part][...])
        acc_oth[...] += dot_nt(grad, weights[2 * part + 1][...])

    @pl.when(step == steps - 1)
    def _():
        first = wsh_ref[0] == 0
        own, oth = acc_own[...], acc_oth[...]
        dna = jnp.concatenate(
            [jnp.where(first, own, oth), jnp.where(first, oth, own)], axis=1
        )
        dnm = dnm_ref[...]
        xhat, scale = normalized(x_ref[...].astype(f32))
        grad = dna * vec_ref[0:1] + dnm * vec_ref[2:3]
        inner = (
            grad
            - jnp.mean(grad, axis=-1, keepdims=True)
            - xhat * jnp.mean(grad * xhat, axis=-1, keepdims=True)
        )
        dx_ref[...] = (dy_ref[...].astype(f32) + scale * inner).astype(bf16)
        sums_ref[0:1] = jnp.sum(dna * xhat, axis=0, keepdims=True)
        sums_ref[1:2] = jnp.sum(dna, axis=0, keepdims=True)
        sums_ref[2:3] = jnp.sum(dnm * xhat, axis=0, keepdims=True)
        sums_ref[3:4] = jnp.sum(dnm, axis=0, keepdims=True)


def dx_call(dqkv, tab, x, dy, dnm, micro, vecs, w_own, w_oth, wsh):
    rows, dim = x.shape
    half = w_own.shape[0]
    tile = 2 * LANES
    steps = dim // tile
    block = (tile // LANES, 3, rows, LANES)

    def col(part):
        return lambda j, s: (0, part * steps + j)

    wspecs = []
    for part in range(3):
        wspecs += [pl.BlockSpec((half, tile), col(part))] * 2
    return pl.pallas_call(
        functools.partial(dx_kernel, half, steps),
        grid_spec=pltpu.PrefetchScalarGridSpec(
            num_scalar_prefetch=1,
            grid=(steps,),
            in_specs=[
                pl.BlockSpec(block, lambda j, s: (j, 0, 0, 0)),
                whole(tab.shape),
                whole(x.shape),
                whole(dy.shape),
                pl.BlockSpec((rows, dim), lambda j, s: (micro, 0)),
                whole(vecs.shape),
            ]
            + wspecs,
            out_specs=[
                pl.BlockSpec(block, lambda j, s: (j, 0, 0, 0)),
                whole((rows, dim)),
                whole((4, dim)),
            ],
            scratch_shapes=[pltpu.VMEM((rows, half), f32), pltpu.VMEM((rows, half), f32)],
        ),
        out_shape=[
            shape_of(dqkv.shape, bf16),
            shape_of((rows, dim), bf16),
            shape_of((4, dim), f32),
        ],
        name="section_input_grad",
        **params_of(6 * rows * dim * dim, 6 * dim * dim + 16 * rows * dim),
    )(wsh, dqkv, tab, x, dy, dnm, vecs, w_own, w_oth, w_own, w_oth, w_own, w_oth)


def stack_rows(refs, cols=slice(None)):
    return jnp.concatenate([ref[:, cols] for ref in refs], axis=0)


def row_grad_kernel(xs, dys, *refs):
    x_refs, dy_refs = refs[:xs], refs[xs : xs + dys]
    out_ref, sum_ref, dy_s = refs[xs + dys :]

    @pl.when(pl.program_id(0) == 0)
    def _():
        dy = stack_rows(dy_refs)
        dy_s[...] = dy
        sum_ref[...] = jnp.sum(dy.astype(f32), axis=0, keepdims=True)

    out_ref[...] = dot_nn(stack_rows(x_refs).T, dy_s[...]).astype(bf16)


def row_grad_call(x_list, dy_list, name):
    cols = x_list[0].shape[1]
    dim = dy_list[0].shape[1]
    total = sum(x.shape[0] for x in x_list)
    tile = 256
    return pl.pallas_call(
        functools.partial(row_grad_kernel, len(x_list), len(dy_list)),
        grid=(cols // tile,),
        in_specs=[pl.BlockSpec((x.shape[0], tile), lambda j: (0, j)) for x in x_list]
        + [whole(dy.shape) for dy in dy_list],
        out_specs=[pl.BlockSpec((tile, dim), lambda j: (j, 0)), whole((1, dim))],
        out_shape=[shape_of((cols, dim), bf16), shape_of((1, dim), f32)],
        scratch_shapes=[pltpu.VMEM((total, dim), bf16)],
        name=name,
        **params_of(2 * total * cols * dim, 2 * cols * dim + 2 * total * (cols + dim)),
    )(*x_list, *dy_list)


def col_grad_kernel(xs, dys, *refs):
    x_refs, dy_refs = refs[:xs], refs[xs : xs + dys]
    out_ref, sum_ref, xt_s = refs[xs + dys :]

    @pl.when(pl.program_id(0) == 0)
    def _():
        xt_s[...] = stack_rows(x_refs).T

    dy = stack_rows(dy_refs)
    sum_ref[...] = jnp.sum(dy.astype(f32), axis=0, keepdims=True)
    out_ref[...] = dot_nn(xt_s[...], dy).astype(bf16)


def up_grad_call(x_list, du_list):
    half = x_list[0].shape[1]
    ff = du_list[0].shape[1]
    total = sum(x.shape[0] for x in x_list)
    tile = 512
    return pl.pallas_call(
        functools.partial(col_grad_kernel, len(x_list), len(du_list)),
        grid=(ff // tile,),
        in_specs=[whole(x.shape) for x in x_list]
        + [pl.BlockSpec((d.shape[0], tile), lambda j: (0, j)) for d in du_list],
        out_specs=[
            pl.BlockSpec((half, tile), lambda j: (0, j)),
            pl.BlockSpec((1, tile), lambda j: (0, j)),
        ],
        out_shape=[shape_of((half, ff), bf16), shape_of((1, ff), f32)],
        scratch_shapes=[pltpu.VMEM((half, total), bf16)],
        name="up_grad",
        **params_of(2 * total * half * ff, 2 * half * ff + 2 * total * ff),
    )(*x_list, *du_list)


def qkv_grad_kernel(xs, *refs):
    x_refs, d_refs = refs[:xs], refs[xs : 2 * xs]
    out_ref, sum_ref, xt_s = refs[2 * xs :]

    @pl.when((pl.program_id(0) == 0) & (pl.program_id(1) == 0))
    def _():
        xt_s[...] = stack_rows(x_refs).T

    dy = jnp.concatenate([lanes_of(ref.at[:, 0]) for ref in d_refs], axis=0)
    sum_ref[...] = jnp.sum(dy.astype(f32), axis=0, keepdims=True)
    out_ref[...] = dot_nn(xt_s[...], dy).astype(bf16)


def qkv_grad_call(x_list, d_list):
    half = x_list[0].shape[1]
    pairs, _, rows, _ = d_list[0].shape
    dim = pairs * LANES
    total = sum(x.shape[0] for x in x_list)
    group = 4
    steps = pairs // group
    tile = group * LANES
    return pl.pallas_call(
        functools.partial(qkv_grad_kernel, len(x_list)),
        grid=(3, steps),
        in_specs=[whole(x.shape) for x in x_list]
        + [pl.BlockSpec((group, 1, rows, LANES), lambda i, j: (j, i, 0, 0)) for _ in d_list],
        out_specs=[
            pl.BlockSpec((half, tile), lambda i, j: (0, i * steps + j)),
            pl.BlockSpec((1, tile), lambda i, j: (0, i * steps + j)),
        ],
        out_shape=[shape_of((half, 3 * dim), bf16), shape_of((1, 3 * dim), f32)],
        scratch_shapes=[pltpu.VMEM((half, total), bf16)],
        name="qkv_grad",
        **params_of(6 * total * half * dim, 6 * half * dim + 6 * total * dim),
    )(*x_list, *d_list)


def ring_of(count):
    return list(range(0, count, 2)) + list(range(count - 1, 0, -2))


def ring_place(axis):
    count = lax.axis_size(axis)
    me = lax.axis_index(axis)
    return jnp.where(me % 2 == 0, me // 2, count - (me + 1) // 2)


def ring_shift(vals, axis, by):
    order = ring_of(lax.axis_size(axis))
    count = len(order)
    pairs = [(order[i], order[(i + by) % count]) for i in range(count)]
    return lax.ppermute(vals, axis, pairs)


def low_sum(*terms):
    total = terms[0].astype(f32)
    for term in terms[1:]:
        total = total + term.astype(f32)
    return total.astype(bf16)


def ring_sum(own, axis):
    count = lax.axis_size(axis)
    place = ring_place(axis)
    full_rows, cols = own.shape
    rows = full_rows // count
    own = own.reshape(count, rows, cols)
    half = count // 2
    cut = rows // 2

    def index(k):
        return (place + (k + count)) % count

    def take(k):
        return lax.dynamic_index_in_dim(own, index(k), 0, keepdims=False)

    far = take(half)
    ahead = ring_shift(far[:cut], axis, 1)
    behind = ring_shift(far[cut:], axis, -1)
    for k in range(half - 1, 0, -1):
        mine_a, mine_b = take(k), take(-k)
        if k == half - 1:
            ahead = jnp.concatenate([low_sum(mine_a[:cut], ahead), mine_a[cut:]], axis=0)
            behind = jnp.concatenate([mine_b[:cut], low_sum(mine_b[cut:], behind)], axis=0)
        else:
            ahead, behind = low_sum(mine_a, ahead), low_sum(mine_b, behind)
        ahead = ring_shift(ahead, axis, 1)
        behind = ring_shift(behind, axis, -1)
    mine = low_sum(take(0), ahead, behind)
    total = jnp.zeros((count, rows, cols), f32)

    def put(total, piece, k, at=0):
        return lax.dynamic_update_slice(total, piece.astype(f32)[None], (index(k), at, 0))

    total = put(total, mine, 0)
    ahead = ring_shift(mine, axis, 1)
    behind = ring_shift(mine, axis, -1)
    for k in range(1, half):
        last = k == half - 1
        next_ahead = ring_shift(ahead[:cut] if last else ahead, axis, 1)
        next_behind = ring_shift(behind[cut:] if last else behind, axis, -1)
        total = put(put(total, ahead, -k), behind, k)
        ahead, behind = next_ahead, next_behind
    total = put(put(total, ahead, -half), behind, half, cut)
    return total.reshape(full_rows, cols)


def butterfly_sum(vals, axis):
    count = lax.axis_size(axis)
    if count & (count - 1):
        return lax.psum(vals, axis)
    by = 1
    while by < count:
        vals = vals + lax.ppermute(vals, axis, [(i, i ^ by) for i in range(count)])
        by *= 2
    return vals


def swap(vals):
    return lax.ppermute(vals, "wsh", [(0, 1), (1, 0)])


def pass_on(vals, by):
    pairs = [(0, 1)] if by > 0 else [(1, 0)]
    return lax.ppermute(vals, "section", pairs)


def block_places(block_pair, count):
    want = jnp.arange(2 * count, dtype=jnp.int32)
    device = jnp.arange(count, dtype=jnp.int32)
    first = (block_pair[None, :] == want[:, None]).astype(jnp.int32)
    second = ((2 * count - 1 - block_pair)[None, :] == want[:, None]).astype(jnp.int32)
    return jnp.sum(first * (2 * device) + second * (2 * device + 1), axis=1)


def row_positions(block_pair, stored, tok_dev):
    count = block_pair.shape[0]
    device = stored // tok_dev
    within = stored % tok_dev
    half_rows = tok_dev // 2
    matches = device[:, None] == jnp.arange(count, dtype=jnp.int32)[None, :]
    pair_block = jnp.sum(jnp.where(matches, block_pair[None, :], 0), axis=1)
    block_idx = jnp.where(within < half_rows, pair_block, 2 * count - 1 - pair_block)
    return block_idx * half_rows + within % half_rows


def rotary_table(positions, head_size):
    half_rot = ROT // 2
    lane = jnp.arange(LANES, dtype=jnp.int32) % head_size
    inv_freq = ROPE_BASE ** (-((lane % half_rot).astype(f32) * 2.0) / ROT)
    angles = positions.astype(f32)[:, None] * inv_freq[None, :]
    cosine, sine = jnp.cos(angles), jnp.sin(angles)
    lead, second = (lane < half_rot)[None], ((lane >= half_rot) & (lane < ROT))[None]
    return jnp.stack(
        [
            jnp.where(lead | second, cosine, 1.0),
            jnp.where(lead, -sine, 0.0),
            jnp.where(second, sine, 0.0),
        ]
    )


def body(
    inputs,
    cotangent,
    block_pair,
    qkv_weight,
    qkv_bias,
    proj_weight,
    proj_bias,
    up_weight,
    up_bias,
    down_weight,
    down_bias,
    attn_gain,
    attn_shift,
    mlp_gain,
    mlp_shift,
):
    first_section = lax.axis_index("section") == 0
    count = lax.axis_size("ctx")
    micros, _, tok_dev, dim = inputs.shape
    head_size = dim // HEADS
    half = dim // 2
    my_half = lax.axis_index("wsh")
    wsh = jnp.stack([my_half.astype(jnp.int32), first_section.astype(jnp.int32)])
    one_pair_each = count == dim // LANES

    wq, wp, wu, wd = (w[0] for w in (qkv_weight, proj_weight, up_weight, down_weight))
    small = jnp.concatenate(
        [
            v[0].reshape(-1, half)
            for v in (
                attn_gain,
                attn_shift,
                mlp_gain,
                mlp_shift,
                proj_bias,
                down_bias,
                qkv_bias,
                up_bias,
            )
        ],
        axis=0,
    )
    small_oth = swap(small)
    wq_oth = swap(wq)
    wu_oth = swap(wu)
    wd_oth = swap(wd)
    wp_oth = swap(wp)
    low_part = jnp.where(my_half == 0, small, small_oth).astype(f32)
    high_part = jnp.where(my_half == 0, small_oth, small).astype(f32)
    vecs = jnp.concatenate([low_part[:6], high_part[:6]], axis=1)
    qkv_rows = 6 + qkv_bias.shape[1] // half
    proj_b, down_b = vecs[4:5], vecs[5:6]
    qkv_b = jnp.concatenate([low_part[6:qkv_rows], high_part[6:qkv_rows]], axis=0).reshape(1, -1)
    up_b = jnp.concatenate([low_part[qkv_rows:], high_part[qkv_rows:]], axis=0).reshape(1, -1)

    local_rows = lax.axis_index("ctx") * tok_dev + jnp.arange(tok_dev, dtype=jnp.int32)
    query_pos = row_positions(block_pair, local_rows, tok_dev)
    key_pos = row_positions(block_pair, jnp.arange(count * tok_dev, dtype=jnp.int32), tok_dev)
    tab = rotary_table(query_pos, head_size)
    loc = block_places(block_pair, count)

    def exchange(vals):
        return lax.all_to_all(vals, "ctx", split_axis=0, concat_axis=0, tiled=True)

    def forward(given, got, save):
        qkv, *made = qkv_call(given, got, vecs, qkv_b, tab, wq, wq_oth, wsh)
        mlp = mlp_call(
            [made[3]], [made[4]], up_b, down_b, wu, wu_oth, wd, wd_oth, wsh, save
        )
        if one_pair_each:
            qkv, mlp = lax.optimization_barrier((exchange(qkv), mlp))
            attended, lse = attend_call(qkv, loc)
            attended, kept = exchange(attended), (qkv, lse)
        else:
            attended, kept = wide_attend(qkv, query_pos, key_pos)
        y, a_own, a_oth = proj_call(attended, made[0], mlp[0], 0, proj_b, wp, wp_oth, wsh)
        return y, (made, mlp, (a_own, a_oth), kept)

    def backward_head(given, got, saved):
        _, mlp, _, _ = saved
        da, dy = da_call(given, got, wp, wp_oth, wsh)
        du, dnm = mlp_back_call([dy], mlp[1], wu, wu_oth, wd, wd_oth, wsh)
        return (exchange(da) if one_pair_each else da), dy, du, dnm

    def backward_rest(da, dy, dnm, saved):
        made, _, _, kept = saved
        if one_pair_each:
            dqkv = exchange(attend_back_call(kept[0], da, kept[1], loc))
        else:
            dqkv = wide_attend_back(kept, da, query_pos, key_pos)
        return dx_call(dqkv, tab, made[0], dy, dnm, 0, vecs, wq, wq_oth, wsh)

    given = [inputs[i, 0] for i in range(micros)]
    asked = [cotangent[i, 0] for i in range(micros)]
    y_a, _ = forward(given[0], given[0], False)
    y_b, saved_b = forward(given[1], pass_on(y_a, 1), True)
    y_c, saved_c = forward(given[0], pass_on(y_b, 1), True)
    da_a, dy_a, _, dnm_a = backward_head(asked[0], asked[0], saved_b)
    da_a, dnm_a = lax.optimization_barrier((da_a, dnm_a))
    _, dx_a, _ = backward_rest(da_a, dy_a, dnm_a, saved_b)
    da_b, dy_b, du_b, dnm_b = backward_head(asked[1], pass_on(dx_a, -1), saved_c)
    da_b, dnm_b = lax.optimization_barrier((da_b, dnm_b))
    back_b, dx_b, sums_b = backward_rest(da_b, dy_b, dnm_b, saved_c)
    da_c, dy_c, du_c, dnm_c = backward_head(asked[0], pass_on(dx_b, -1), saved_b)

    kept_pair = (saved_b, saved_c)
    dy_list = [dy_c, dy_b]
    dy_list = dy_list + [swap(dy) for dy in dy_list]
    down_grad, dy_sum = row_grad_call(
        [s[1][2] for s in kept_pair] + [swap(s[1][3]) for s in kept_pair], dy_list, "down_grad"
    )
    proj_grad, _ = row_grad_call(
        [s[2][0] for s in kept_pair] + [swap(s[2][1]) for s in kept_pair], dy_list, "proj_grad"
    )
    up_grad, du_sum = up_grad_call(
        [s[0][3] for s in kept_pair] + [swap(s[0][4]) for s in kept_pair],
        [du_c, du_b, swap(du_c), swap(du_b)],
    )
    da_c, dnm_c, down_grad, proj_grad, up_grad = lax.optimization_barrier(
        (da_c, dnm_c, down_grad, proj_grad, up_grad)
    )
    back_c, dx_c, sums_c = backward_rest(da_c, dy_c, dnm_c, saved_b)
    qkv_grad, dqkv_sum = qkv_grad_call(
        [s[0][1] for s in kept_pair] + [swap(s[0][2]) for s in kept_pair],
        [back_c, back_b, swap(back_c), swap(back_b)],
    )
    down_grad = ring_sum(down_grad, "ctx")
    up_grad = ring_sum(up_grad, "ctx")
    proj_grad = ring_sum(proj_grad, "ctx")
    qkv_grad = ring_sum(qkv_grad, "ctx")

    norm_sums = sums_b + sums_c
    norm_own = lax.dynamic_slice_in_dim(norm_sums, my_half * half, half, 1)
    norm_oth = swap(lax.dynamic_slice_in_dim(norm_sums, (1 - my_half) * half, half, 1))

    def own_part(vec):
        size = vec.shape[1] // 2
        return lax.dynamic_slice_in_dim(vec, my_half * size, size, 1).reshape(-1, half)

    small_sums = jnp.concatenate(
        [norm_own + norm_oth, own_part(dy_sum), own_part(dqkv_sum), own_part(du_sum)], axis=0
    )
    small_sums = butterfly_sum(small_sums, "ctx")
    qkv_end = 5 + dqkv_sum.shape[1] // 2 // half
    dy_total = small_sums[4:5]
    pick = lambda yes, no: jnp.where(first_section, yes, no)
    layer_out = jnp.stack([pick(y_c, y_b), pick(y_b, y_c)])[None, :, None]
    input_grad = jnp.stack([pick(dx_b, dx_c), pick(dx_c, dx_b)])[None, :, None]
    return (
        layer_out,
        input_grad,
        qkv_grad[None],
        small_sums[5:qkv_end].reshape(1, -1),
        proj_grad[None],
        dy_total,
        up_grad[None],
        small_sums[qkv_end:].reshape(1, -1),
        down_grad[None],
        dy_total,
        small_sums[0:1],
        small_sums[1:2],
        small_sums[2:3],
        small_sums[3:4],
    )


def solution(mesh):
    in_specs = (
        P(None, "wsh", "ctx", None),
        P(None, "wsh", "ctx", None),
        P(),
        P("section", "wsh", None),
        P("section", "wsh"),
        P("section", "wsh", None),
        P("section", "wsh"),
        P("section", "wsh", None),
        P("section", "wsh"),
        P("section", "wsh", None),
        P("section", "wsh"),
        P("section", "wsh"),
        P("section", "wsh"),
        P("section", "wsh"),
        P("section", "wsh"),
    )
    out_specs = (
        P("section", None, "wsh", "ctx", None),
        P("section", None, "wsh", "ctx", None),
        P("section", "wsh", None),
        P("section", "wsh"),
        P("section", "wsh", None),
        P("section", "wsh"),
        P("section", "wsh", None),
        P("section", "wsh"),
        P("section", "wsh", None),
        P("section", "wsh"),
        P("section", "wsh"),
        P("section", "wsh"),
        P("section", "wsh"),
        P("section", "wsh"),
    )
    return jax.shard_map(body, mesh=mesh, in_specs=in_specs, out_specs=out_specs, check_vma=False)
```

```python
import functools

import jax
import jax.numpy as jnp
from jax import lax
from jax.experimental import pallas as pl
from jax.experimental.pallas import tpu as pltpu
from jax.sharding import PartitionSpec as P

HEADS = 16
ROT = 16
NORM_EPS = 1e-05
ROPE_BASE = 10000.0
MASKED_SCORE = -1e30
LANES = 128
VMEM_LIMIT = 60 * 1024 * 1024
INV_SQRT2 = 0.7071067811865476
INV_SQRT_2PI = 0.3989422804014327

f32 = jnp.float32
bf16 = jnp.bfloat16


def dot_nn(left, right):
    return lax.dot_general(left, right, (((1,), (0,)), ((), ())), preferred_element_type=f32)


def dot_nt(left, right):
    return lax.dot_general(left, right, (((1,), (1,)), ((), ())), preferred_element_type=f32)


def params_of(flops, nbytes, **extra):
    return dict(
        compiler_params=pltpu.CompilerParams(vmem_limit_bytes=VMEM_LIMIT),
        cost_estimate=pl.CostEstimate(flops=flops, bytes_accessed=nbytes, transcendentals=0),
        **extra,
    )


def whole(shape):
    rank = len(shape)
    return pl.BlockSpec(shape, lambda *args: (0,) * rank)


def shape_of(shape, dtype):
    return jax.ShapeDtypeStruct(shape, dtype)


def rope(vals, tab_ref):
    return (
        vals * tab_ref[0]
        + pltpu.roll(vals, LANES - ROT // 2, 1) * tab_ref[1]
        + pltpu.roll(vals, ROT // 2, 1) * tab_ref[2]
    )


def unrope(vals, tab_ref):
    return (
        vals * tab_ref[0]
        - pltpu.roll(vals, LANES - ROT // 2, 1) * tab_ref[1]
        - pltpu.roll(vals, ROT // 2, 1) * tab_ref[2]
    )


def normalized(hidden):
    row_mean = jnp.mean(hidden, axis=-1, keepdims=True)
    centered = hidden - row_mean
    spread = jnp.mean(centered * centered, axis=-1, keepdims=True)
    scale = lax.rsqrt(spread + NORM_EPS)
    return centered * scale, scale


def start_all(tiles, steps):
    @pl.when(pl.program_id(0) == 0)
    def _():
        for t in range(steps):
            for copy in tiles(t):
                copy.start()


def column_tiles(wsh_ref, w_own, w_oth, buf, sems, dim):
    tile = buf.shape[-1]

    def tiles(t):
        copies = []
        for part in range(3):
            cols = pl.ds(pl.multiple_of(part * dim + t * tile, tile), tile)
            for side, weight in enumerate((w_own, w_oth)):
                copies.append(
                    pltpu.make_async_copy(
                        weight.at[:, cols], buf.at[t, part, side], sems.at[t, part, side]
                    )
                )
        return copies

    return tiles


def qkv_kernel(half, steps, wsh_ref, given_ref, got_ref, vec_ref, bq, bk, bv, tab_ref, *rest):
    w_own, w_oth, out_ref, x_ref, na_own, na_oth, nm_own, nm_oth, buf, sems = rest
    step = pl.program_id(0)
    tiles = column_tiles(wsh_ref, w_own, w_oth, buf, sems, 2 * half)
    start_all(tiles, steps)

    @pl.when(step == 0)
    def _():
        x = jnp.where(wsh_ref[1] == 1, given_ref[...], got_ref[...])
        x_ref[...] = x
        xhat, _ = normalized(x.astype(f32))
        na = (xhat * vec_ref[0:1] + vec_ref[1:2]).astype(bf16)
        nm = (xhat * vec_ref[2:3] + vec_ref[3:4]).astype(bf16)
        first = wsh_ref[0] == 0
        na_own[...] = jnp.where(first, na[:, :half], na[:, half:])
        na_oth[...] = jnp.where(first, na[:, half:], na[:, :half])
        nm_own[...] = jnp.where(first, nm[:, :half], nm[:, half:])
        nm_oth[...] = jnp.where(first, nm[:, half:], nm[:, :half])

    for copy in tiles(step):
        copy.wait()
    for part, bias in enumerate((bq, bk, bv)):
        res = (
            dot_nn(na_own[...], buf[step, part, 0])
            + dot_nn(na_oth[...], buf[step, part, 1])
            + bias[...]
        )
        for pair in range(res.shape[1] // LANES):
            vals = res[:, pair * LANES : (pair + 1) * LANES]
            if part < 2:
                vals = rope(vals, tab_ref)
            out_ref[pair, part] = vals.astype(bf16)


def layer_of(shape, index):
    return pl.BlockSpec((pl.squeezed,) + shape, lambda *args: (index, 0, 0))


ANYWHERE = pl.BlockSpec(memory_space=pl.ANY)


def qkv_call(given, index, got, vecs, qkv_b, tab, w_own, w_oth, wsh):
    rows, dim = given.shape[1:]
    half = w_own.shape[0]
    pairs = dim // LANES
    tile = 2 * LANES
    steps = dim // tile

    def bias(part):
        return pl.BlockSpec((1, tile), lambda j, s: (0, part * steps + j))

    got_spec = whole((rows, dim))
    if got is None:
        got, got_spec = given, layer_of((rows, dim), index)
    return pl.pallas_call(
        functools.partial(qkv_kernel, half, steps),
        grid_spec=pltpu.PrefetchScalarGridSpec(
            num_scalar_prefetch=1,
            grid=(steps,),
            in_specs=[
                layer_of((rows, dim), index),
                got_spec,
                whole(vecs.shape),
                bias(0),
                bias(1),
                bias(2),
                whole(tab.shape),
                ANYWHERE,
                ANYWHERE,
            ],
            out_specs=[pl.BlockSpec((tile // LANES, 3, rows, LANES), lambda j, s: (j, 0, 0, 0))]
            + [whole((rows, dim))]
            + [whole((rows, half))] * 4,
            scratch_shapes=[
                pltpu.VMEM((steps, 3, 2, half, tile), bf16),
                pltpu.SemaphoreType.DMA((steps, 3, 2)),
            ],
        ),
        out_shape=[shape_of((pairs, 3, rows, LANES), bf16), shape_of((rows, dim), bf16)]
        + [shape_of((rows, half), bf16)] * 4,
        name="qkv_proj",
        **params_of(6 * rows * dim * dim, 6 * dim * dim + 8 * rows * dim),
    )(wsh, given, got, vecs, qkv_b, qkv_b, qkv_b, tab, w_own, w_oth)


MLP_TILE = 1024
MLP_PIECE = 512


def ff_tiles(wsh_ref, up_own, up_oth, dn_own, dn_oth, up_buf, dn_buf, sems):
    tile = dn_buf.shape[1]
    own = dn_own.shape[0] // tile

    def tiles(t):
        cols = pl.ds(pl.multiple_of(((wsh_ref[0] * own + t) % (2 * own)) * tile, tile), tile)
        copies = [
            pltpu.make_async_copy(weight.at[:, cols], up_buf.at[t, side], sems.at[t, side])
            for side, weight in enumerate((up_own, up_oth))
        ]
        held = not isinstance(t, int) or t < own
        down = dn_own if held else dn_oth
        rows = pl.ds((t % own) * tile, tile)
        return copies + [pltpu.make_async_copy(down.at[rows], dn_buf.at[t], sems.at[t, 2])]

    return tiles


def mlp_kernel(own_tiles, save, wsh_ref, nm_own, nm_oth, up_b, down_b, *refs):
    weights, outs = refs[:4], refs[4:]
    if save:
        out_ref, slope_ref, gt_own, gt_oth, up_buf, dn_buf, sems = outs
    else:
        out_ref, up_buf, dn_buf, sems = outs
    step = pl.program_id(0)
    tiles = ff_tiles(wsh_ref, *weights, up_buf, dn_buf, sems)
    start_all(tiles, 2 * own_tiles)

    @pl.when(step == 0)
    def _():
        out_ref[...] = jnp.broadcast_to(down_b[...], out_ref.shape)

    for copy in tiles(step):
        copy.wait()
    for at in range(0, dn_buf.shape[1], MLP_PIECE):
        piece = pl.ds(at, MLP_PIECE)
        pre = (
            dot_nn(nm_own[...], up_buf[step, 0, :, piece])
            + dot_nn(nm_oth[...], up_buf[step, 1, :, piece])
            + up_b[:, piece]
        )
        gate = 0.5 + 0.5 * lax.erf(pre * INV_SQRT2)
        act = (pre * gate).astype(bf16)
        if save:
            slope_ref[:, piece] = (
                gate + pre * (INV_SQRT_2PI * jnp.exp(-0.5 * pre * pre))
            ).astype(bf16)
            turned = act.T

            @pl.when(step < own_tiles)
            def _():
                gt_own[piece] = turned

            @pl.when(step >= own_tiles)
            def _():
                gt_oth[piece] = turned

        out_ref[...] += dot_nn(act, dn_buf[step, piece])


def mlp_scratch(half, dim, steps):
    return [
        pltpu.VMEM((steps, 2, half, MLP_TILE), bf16),
        pltpu.VMEM((steps, MLP_TILE, dim), bf16),
        pltpu.SemaphoreType.DMA((steps, 3)),
    ]


def mlp_call(nm_own, nm_oth, up_b, down_b, up_own, up_oth, dn_own, dn_oth, wsh, save):
    rows, half = nm_own.shape
    dim = dn_own.shape[1]
    ff = up_own.shape[1]
    own = dn_own.shape[0] // MLP_TILE
    by_ff = lambda j, s: (0, (s[0] * own + j) % (2 * own))
    out_specs = [whole((rows, dim))]
    out_shape = [shape_of((rows, dim), f32)]
    if save:
        out_specs += [
            pl.BlockSpec((rows, MLP_TILE), by_ff),
            pl.BlockSpec((MLP_TILE, rows), lambda j, s: (jnp.minimum(j, own - 1), 0)),
            pl.BlockSpec((MLP_TILE, rows), lambda j, s: (jnp.maximum(j - own, 0), 0)),
        ]
        out_shape += [shape_of((rows, ff), bf16)] + [shape_of((ff // 2, rows), bf16)] * 2
    return pl.pallas_call(
        functools.partial(mlp_kernel, own, save),
        grid_spec=pltpu.PrefetchScalarGridSpec(
            num_scalar_prefetch=1,
            grid=(2 * own,),
            in_specs=[whole((rows, half))] * 2
            + [pl.BlockSpec((1, MLP_TILE), by_ff), whole((1, dim))]
            + [ANYWHERE] * 4,
            out_specs=out_specs,
            scratch_shapes=mlp_scratch(half, dim, 2 * own),
        ),
        out_shape=out_shape,
        name="mlp_forward",
        **params_of(4 * rows * dim * ff, 4 * dim * ff + 8 * rows * ff),
    )(wsh, nm_own, nm_oth, up_b, down_b, up_own, up_oth, dn_own, dn_oth)


def mlp_back_kernel(own_tiles, half, wsh_ref, dy_ref, slope_ref, *refs):
    weights = refs[:4]
    du_ref, dnm_ref, acc_own, acc_oth, up_buf, dn_buf, sems = refs[4:]
    step = pl.program_id(0)
    tiles = ff_tiles(wsh_ref, *weights, up_buf, dn_buf, sems)
    start_all(tiles, 2 * own_tiles)

    @pl.when(step == 0)
    def _():
        acc_own[...] = jnp.zeros(acc_own.shape, f32)
        acc_oth[...] = jnp.zeros(acc_oth.shape, f32)

    for copy in tiles(step):
        copy.wait()
    for at in range(0, dn_buf.shape[1], MLP_PIECE):
        piece = pl.ds(at, MLP_PIECE)
        dact = dot_nt(dy_ref[...], dn_buf[step, piece])
        du = (dact * slope_ref[:, piece].astype(f32)).astype(bf16)
        du_ref[:, piece] = du
        acc_own[...] += dot_nt(du, up_buf[step, 0, :, piece])
        acc_oth[...] += dot_nt(du, up_buf[step, 1, :, piece])

    @pl.when(step == 2 * own_tiles - 1)
    def _():
        first = wsh_ref[0] == 0
        dnm_ref[:, :half] = jnp.where(first, acc_own[...], acc_oth[...])
        dnm_ref[:, half:] = jnp.where(first, acc_oth[...], acc_own[...])


def mlp_back_call(dy, slope, up_own, up_oth, dn_own, dn_oth, wsh):
    rows, dim = dy.shape
    half = up_own.shape[0]
    ff = slope.shape[1]
    own = dn_own.shape[0] // MLP_TILE
    by_ff = lambda j, s: (0, (s[0] * own + j) % (2 * own))
    return pl.pallas_call(
        functools.partial(mlp_back_kernel, own, half),
        grid_spec=pltpu.PrefetchScalarGridSpec(
            num_scalar_prefetch=1,
            grid=(2 * own,),
            in_specs=[whole((rows, dim)), pl.BlockSpec((rows, MLP_TILE), by_ff)] + [ANYWHERE] * 4,
            out_specs=[pl.BlockSpec((rows, MLP_TILE), by_ff), whole((rows, dim))],
            scratch_shapes=[pltpu.VMEM((rows, half), f32), pltpu.VMEM((rows, half), f32)]
            + mlp_scratch(half, dim, 2 * own),
        ),
        out_shape=[shape_of((rows, ff), bf16), shape_of((rows, dim), f32)],
        name="mlp_backward",
        **params_of(4 * rows * dim * ff, 4 * dim * ff + 8 * rows * ff),
    )(wsh, dy, slope, up_own, up_oth, dn_own, dn_oth)


def sort_in(loc_ref, ref, dst, half_rows, part=None):
    for block in range(dst.shape[0] // half_rows):
        place = loc_ref[block]
        rows = pl.ds(pl.multiple_of((place % 2) * half_rows, half_rows), half_rows)
        if part is None:
            vals = ref[place // 2, rows, :]
        else:
            vals = ref[place // 2, part, rows, :]
        dst[block * half_rows : (block + 1) * half_rows] = vals


def sort_out(loc_ref, vals, ref, half_rows, part=None):
    for block in range(vals.shape[0] // half_rows):
        place = loc_ref[block]
        rows = pl.ds(pl.multiple_of((place % 2) * half_rows, half_rows), half_rows)
        piece = vals[block * half_rows : (block + 1) * half_rows]
        if part is None:
            ref[place // 2, rows, :] = piece
        else:
            ref[place // 2, part, rows, :] = piece


def head_of(vals, head):
    lane = lax.broadcasted_iota(jnp.int32, vals.shape, 1)
    return jnp.where(lane // (LANES // 2) == head, vals, jnp.zeros_like(vals))


def scores_of(keys, queries, scale, diagonal):
    scores = dot_nt(keys, queries) * scale
    if diagonal:
        key_at = lax.broadcasted_iota(jnp.int32, scores.shape, 0)
        query_at = lax.broadcasted_iota(jnp.int32, scores.shape, 1)
        scores = jnp.where(key_at <= query_at, scores, MASKED_SCORE)
    return scores


def attend_kernel(tile, loc_ref, qkv_ref, o_ref, lse_ref, q_s, k_s, v_s, vt_s, o_s):
    half_rows = qkv_ref.shape[2] // 2
    seq = q_s.shape[0]
    head_size = LANES // 2
    scale = head_size**-0.5
    sort_in(loc_ref, qkv_ref, q_s, half_rows, 0)
    sort_in(loc_ref, qkv_ref, k_s, half_rows, 1)
    sort_in(loc_ref, qkv_ref, v_s, half_rows, 2)
    vt_s[...] = v_s[...].T
    for t in range(seq // tile):
        rows = slice(t * tile, (t + 1) * tile)
        queries = q_s[rows]
        outs = []
        for head in range(2):
            picked = head_of(queries, head)
            parts = [
                scores_of(k_s[i * tile : (i + 1) * tile], picked, scale, i == t)
                for i in range(t + 1)
            ]
            top = functools.reduce(
                jnp.maximum, [jnp.max(p, axis=0, keepdims=True) for p in parts]
            )
            parts = [jnp.exp(p - top) for p in parts]
            total = sum(jnp.sum(p, axis=0, keepdims=True) for p in parts)
            lse_ref[head : head + 1, rows] = top + jnp.log(total)
            inverse = 1.0 / total
            acc = None
            for i, p in enumerate(parts):
                term = dot_nn(
                    vt_s[head * head_size : (head + 1) * head_size, i * tile : (i + 1) * tile],
                    (p * inverse).astype(bf16),
                )
                acc = term if acc is None else acc + term
            outs.append(acc)
        o_s[rows] = jnp.concatenate(outs, axis=0).T.astype(bf16)
    sort_out(loc_ref, o_s, o_ref, half_rows)


def attend_call(qkv, loc):
    count, _, rows, _ = qkv.shape
    seq = count * rows
    return pl.pallas_call(
        functools.partial(attend_kernel, 256),
        grid_spec=pltpu.PrefetchScalarGridSpec(
            num_scalar_prefetch=1,
            grid=(1,),
            in_specs=[whole(qkv.shape)],
            out_specs=[whole((count, rows, LANES)), whole((2, seq))],
            scratch_shapes=[
                pltpu.VMEM((seq, LANES), bf16),
                pltpu.VMEM((seq, LANES), bf16),
                pltpu.VMEM((seq, LANES), bf16),
                pltpu.VMEM((LANES, seq), bf16),
                pltpu.VMEM((seq, LANES), bf16),
            ],
        ),
        out_shape=[shape_of((count, rows, LANES), bf16), shape_of((2, seq), f32)],
        name="attention",
        **params_of(8 * seq * seq * LANES, 8 * seq * LANES),
    )(loc, qkv)


def attend_back_kernel(
    tile, loc_ref, qkv_ref, da_ref, lse_ref, out_ref, q_s, k_s, v_s, da_s, kt_s, dq_s, dk_s, dv_s
):
    half_rows = qkv_ref.shape[2] // 2
    seq = q_s.shape[0]
    head_size = LANES // 2
    scale = head_size**-0.5
    sort_in(loc_ref, qkv_ref, q_s, half_rows, 0)
    sort_in(loc_ref, qkv_ref, k_s, half_rows, 1)
    sort_in(loc_ref, qkv_ref, v_s, half_rows, 2)
    sort_in(loc_ref, da_ref, da_s, half_rows)
    kt_s[...] = k_s[...].T
    dk_s[...] = jnp.zeros(dk_s.shape, f32)
    dv_s[...] = jnp.zeros(dv_s.shape, f32)
    for t in range(seq // tile):
        rows = slice(t * tile, (t + 1) * tile)
        outs = []
        for head in range(2):
            queries = head_of(q_s[rows], head)
            grads = head_of(da_s[rows], head)
            lse = lse_ref[head : head + 1, rows]
            probs, dprobs, row_dot = [], [], 0.0
            for i in range(t + 1):
                keys = slice(i * tile, (i + 1) * tile)
                p = jnp.exp(scores_of(k_s[keys], queries, scale, i == t) - lse)
                dp = dot_nt(v_s[keys], grads)
                row_dot = row_dot + jnp.sum(p * dp, axis=0, keepdims=True)
                dv_s[keys] += dot_nn(p.astype(bf16), grads)
                probs.append(p)
                dprobs.append(dp)
            acc = None
            for i in range(t + 1):
                keys = slice(i * tile, (i + 1) * tile)
                ds = (probs[i] * (dprobs[i] - row_dot) * scale).astype(bf16)
                dk_s[keys] += dot_nn(ds, queries)
                term = dot_nn(kt_s[head * head_size : (head + 1) * head_size, keys], ds)
                acc = term if acc is None else acc + term
            outs.append(acc)
        dq_s[rows] = jnp.concatenate(outs, axis=0).T.astype(bf16)
    sort_out(loc_ref, dq_s, out_ref, half_rows, 0)
    k_s[...] = dk_s[...].astype(bf16)
    v_s[...] = dv_s[...].astype(bf16)
    sort_out(loc_ref, k_s, out_ref, half_rows, 1)
    sort_out(loc_ref, v_s, out_ref, half_rows, 2)


def attend_back_call(qkv, da, lse, loc):
    count, _, rows, _ = qkv.shape
    seq = count * rows
    return pl.pallas_call(
        functools.partial(attend_back_kernel, 256),
        grid_spec=pltpu.PrefetchScalarGridSpec(
            num_scalar_prefetch=1,
            grid=(1,),
            in_specs=[whole(qkv.shape), whole(da.shape), whole(lse.shape)],
            out_specs=whole(qkv.shape),
            scratch_shapes=[
                pltpu.VMEM((seq, LANES), bf16),
                pltpu.VMEM((seq, LANES), bf16),
                pltpu.VMEM((seq, LANES), bf16),
                pltpu.VMEM((seq, LANES), bf16),
                pltpu.VMEM((LANES, seq), bf16),
                pltpu.VMEM((seq, LANES), bf16),
                pltpu.VMEM((seq, LANES), f32),
                pltpu.VMEM((seq, LANES), f32),
            ],
        ),
        out_shape=shape_of(qkv.shape, bf16),
        name="attention_backward",
        **params_of(20 * seq * seq * LANES, 14 * seq * LANES),
    )(loc, qkv, da, lse)


def by_head(parts):
    pairs, rows, lanes = parts.shape
    return jnp.transpose(parts, (1, 0, 2)).reshape(rows, HEADS, pairs * lanes // HEADS)


def by_pair(heads):
    rows = heads.shape[0]
    return jnp.transpose(heads.reshape(rows, -1, LANES), (1, 0, 2))


def wide_scores(queries, keys, query_pos, key_pos):
    raw = jnp.einsum("qhd,khd->hqk", queries, keys, preferred_element_type=f32)
    allowed = (query_pos[:, None] >= key_pos[None, :])[None]
    return jnp.where(allowed, raw * queries.shape[-1] ** (-0.5), MASKED_SCORE)


def key_blocks(arrays, rows):
    return tuple(a.reshape((a.shape[0] // rows, rows) + a.shape[1:]) for a in arrays)


def wide_attend(qkv, query_pos, key_pos):
    queries = by_head(qkv[:, 0])
    keys = lax.all_gather(by_head(qkv[:, 1]), "ctx", axis=0, tiled=True)
    values = lax.all_gather(by_head(qkv[:, 2]), "ctx", axis=0, tiled=True)
    block = min(512, keys.shape[0])
    split = key_blocks((keys, values, key_pos), block)
    rows, _, head_size = queries.shape

    def max_step(carry, block_in):
        top, total = carry
        scores = wide_scores(queries, block_in[0], query_pos, block_in[2])
        new_top = jnp.maximum(top, jnp.max(scores, axis=-1))
        part = jnp.sum(jnp.exp(scores - new_top[..., None]), axis=-1)
        return ((new_top, total * jnp.exp(top - new_top) + part), None)

    start = (jnp.full((HEADS, rows), MASKED_SCORE, f32), jnp.zeros((HEADS, rows), f32))
    (top, total), _ = lax.scan(max_step, start, split)
    lse = top + jnp.log(total)

    def value_step(running, block_in):
        scores = wide_scores(queries, block_in[0], query_pos, block_in[2])
        probs = jnp.exp(scores - lse[..., None]).astype(bf16)
        term = jnp.einsum("hqk,khd->qhd", probs, block_in[1], preferred_element_type=f32)
        return (running + term, None)

    attended, _ = lax.scan(value_step, jnp.zeros((rows, HEADS, head_size), f32), split)
    return by_pair(attended.astype(bf16)), (queries, keys, values, lse)


def wide_attend_back(kept, da, query_pos, key_pos):
    queries, keys, values, lse = kept
    grads = by_head(da)
    block = min(512, keys.shape[0])
    split = key_blocks((keys, values, key_pos), block)
    scale = queries.shape[-1] ** (-0.5)

    def pieces(block_in):
        scores = wide_scores(queries, block_in[0], query_pos, block_in[2])
        probs = jnp.exp(scores - lse[..., None])
        dprobs = jnp.einsum("qhd,khd->hqk", grads, block_in[1], preferred_element_type=f32)
        return probs, dprobs

    def dot_step(running, block_in):
        probs, dprobs = pieces(block_in)
        return (running + jnp.sum(probs * dprobs, axis=-1), None)

    row_dot, _ = lax.scan(dot_step, jnp.zeros(lse.shape, f32), split)

    def key_step(running, block_in):
        probs, dprobs = pieces(block_in)
        ds = (scale * probs * (dprobs - row_dot[..., None])).astype(bf16)
        running = running + jnp.einsum("hqk,khd->qhd", ds, block_in[0], preferred_element_type=f32)
        dk = jnp.einsum("hqk,qhd->khd", ds, queries, preferred_element_type=f32)
        dv = jnp.einsum("hqk,qhd->khd", probs.astype(bf16), grads, preferred_element_type=f32)
        return (running, (dk.astype(bf16), dv.astype(bf16)))

    dq, (dk, dv) = lax.scan(key_step, jnp.zeros(queries.shape, f32), split)
    dk, dv = (
        lax.psum_scatter(part.reshape(keys.shape), "ctx", scatter_dimension=0, tiled=True)
        for part in (dk, dv)
    )
    return jnp.stack([by_pair(dq.astype(bf16)), by_pair(dk), by_pair(dv)], axis=1)


def lanes_of(ref):
    return jnp.concatenate([ref[i] for i in range(ref.shape[0])], axis=1)


def proj_kernel(half, wsh_ref, a_ref, x_ref, mlp_ref, bias_ref, p_own, p_oth, y_ref, a_own, a_oth):
    first = wsh_ref[0] == 0
    a = lanes_of(a_ref)
    own = jnp.where(first, a[:, :half], a[:, half:])
    oth = jnp.where(first, a[:, half:], a[:, :half])
    a_own[...] = own
    a_oth[...] = oth
    attn = dot_nn(own, p_own[...]) + dot_nn(oth, p_oth[...]) + bias_ref[...]
    y_ref[...] = (x_ref[...].astype(f32) + attn + mlp_ref[...]).astype(bf16)


def proj_call(a, x, mlp, bias, p_own, p_oth, wsh):
    rows, dim = x.shape
    half = p_own.shape[0]
    return pl.pallas_call(
        functools.partial(proj_kernel, half),
        grid_spec=pltpu.PrefetchScalarGridSpec(
            num_scalar_prefetch=1,
            grid=(1,),
            in_specs=[
                whole(a.shape),
                whole(x.shape),
                whole((rows, dim)),
                whole(bias.shape),
                whole(p_own.shape),
                whole(p_oth.shape),
            ],
            out_specs=[whole((rows, dim)), whole((rows, half)), whole((rows, half))],
        ),
        out_shape=[shape_of((rows, dim), bf16)] + [shape_of((rows, half), bf16)] * 2,
        name="attn_out",
        **params_of(2 * rows * dim * dim, 2 * dim * dim + 10 * rows * dim),
    )(wsh, a, x, mlp, bias, p_own, p_oth)


def da_kernel(wsh_ref, given_ref, got_ref, p_own, p_oth, out_ref, dy_ref):
    dy = jnp.where(wsh_ref[1] == 1, got_ref[...], given_ref[...])
    dy_ref[...] = dy
    wsh = wsh_ref[0]
    count = out_ref.shape[0] // 2
    for place, weight in ((wsh * count, p_own), ((1 - wsh) * count, p_oth)):
        part = dot_nt(dy, weight[...]).astype(bf16)
        for i in range(count):
            out_ref[place + i] = part[:, i * LANES : (i + 1) * LANES]


def da_call(given, index, got, p_own, p_oth, wsh):
    rows, dim = given.shape[1:]
    pairs = dim // LANES
    got_spec = whole((rows, dim))
    if got is None:
        got, got_spec = given, layer_of((rows, dim), index)
    return pl.pallas_call(
        da_kernel,
        grid_spec=pltpu.PrefetchScalarGridSpec(
            num_scalar_prefetch=1,
            grid=(1,),
            in_specs=[layer_of((rows, dim), index), got_spec]
            + [whole(p_own.shape), whole(p_oth.shape)],
            out_specs=[whole((pairs, rows, LANES)), whole((rows, dim))],
        ),
        out_shape=[shape_of((pairs, rows, LANES), bf16), shape_of((rows, dim), bf16)],
        name="attn_out_backward",
        **params_of(2 * rows * dim * dim, 2 * dim * dim + 4 * rows * dim),
    )(wsh, given, got, p_own, p_oth)


def dx_kernel(half, steps, wsh_ref, dqkv_ref, tab_ref, x_ref, dy_ref, dnm_ref, vec_ref, *rest):
    w_own, w_oth, back_ref, dx_ref, sums_ref, acc_own, acc_oth, buf, sems = rest
    step = pl.program_id(0)
    tiles = column_tiles(wsh_ref, w_own, w_oth, buf, sems, 2 * half)
    start_all(tiles, steps)

    @pl.when(step == 0)
    def _():
        acc_own[...] = jnp.zeros(acc_own.shape, f32)
        acc_oth[...] = jnp.zeros(acc_oth.shape, f32)

    for copy in tiles(step):
        copy.wait()
    for part in range(3):
        cols = []
        for pair in range(dqkv_ref.shape[0]):
            vals = dqkv_ref[pair, part]
            if part < 2:
                vals = unrope(vals.astype(f32), tab_ref).astype(bf16)
            back_ref[pair, part] = vals
            cols.append(vals)
        grad = jnp.concatenate(cols, axis=1)
        acc_own[...] += dot_nt(grad, buf[step, part, 0])
        acc_oth[...] += dot_nt(grad, buf[step, part, 1])

    @pl.when(step == steps - 1)
    def _():
        first = wsh_ref[0] == 0
        own, oth = acc_own[...], acc_oth[...]
        dna = jnp.concatenate(
            [jnp.where(first, own, oth), jnp.where(first, oth, own)], axis=1
        )
        dnm = dnm_ref[...]
        xhat, scale = normalized(x_ref[...].astype(f32))
        grad = dna * vec_ref[0:1] + dnm * vec_ref[2:3]
        inner = (
            grad
            - jnp.mean(grad, axis=-1, keepdims=True)
            - xhat * jnp.mean(grad * xhat, axis=-1, keepdims=True)
        )
        dx_ref[...] = (dy_ref[...].astype(f32) + scale * inner).astype(bf16)
        sums_ref[0:1] = jnp.sum(dna * xhat, axis=0, keepdims=True)
        sums_ref[1:2] = jnp.sum(dna, axis=0, keepdims=True)
        sums_ref[2:3] = jnp.sum(dnm * xhat, axis=0, keepdims=True)
        sums_ref[3:4] = jnp.sum(dnm, axis=0, keepdims=True)


def dx_call(dqkv, tab, x, dy, dnm, vecs, w_own, w_oth, wsh):
    rows, dim = x.shape
    half = w_own.shape[0]
    tile = 2 * LANES
    steps = dim // tile
    block = (tile // LANES, 3, rows, LANES)
    return pl.pallas_call(
        functools.partial(dx_kernel, half, steps),
        grid_spec=pltpu.PrefetchScalarGridSpec(
            num_scalar_prefetch=1,
            grid=(steps,),
            in_specs=[
                pl.BlockSpec(block, lambda j, s: (j, 0, 0, 0)),
                whole(tab.shape),
                whole(x.shape),
                whole(dy.shape),
                whole(dnm.shape),
                whole(vecs.shape),
                ANYWHERE,
                ANYWHERE,
            ],
            out_specs=[
                pl.BlockSpec(block, lambda j, s: (j, 0, 0, 0)),
                whole((rows, dim)),
                whole((4, dim)),
            ],
            scratch_shapes=[
                pltpu.VMEM((rows, half), f32),
                pltpu.VMEM((rows, half), f32),
                pltpu.VMEM((steps, 3, 2, half, tile), bf16),
                pltpu.SemaphoreType.DMA((steps, 3, 2)),
            ],
        ),
        out_shape=[
            shape_of(dqkv.shape, bf16),
            shape_of((rows, dim), bf16),
            shape_of((4, dim), f32),
        ],
        name="section_input_grad",
        **params_of(6 * rows * dim * dim, 6 * dim * dim + 16 * rows * dim),
    )(wsh, dqkv, tab, x, dy, dnm, vecs, w_own, w_oth)


def stack_rows(refs, cols=slice(None)):
    return jnp.concatenate([ref[:, cols] for ref in refs], axis=0)


def row_grad_kernel(xs, dys, turned, *refs):
    x_refs, dy_refs = refs[:xs], refs[xs : xs + dys]
    out_ref, sum_ref, dy_s = refs[xs + dys :]

    @pl.when(pl.program_id(0) == 0)
    def _():
        dy = stack_rows(dy_refs)
        dy_s[...] = dy
        sum_ref[...] = jnp.sum(dy.astype(f32), axis=0, keepdims=True)

    if turned:
        left = jnp.concatenate([ref[...] for ref in x_refs], axis=1)
    else:
        left = stack_rows(x_refs).T
    out_ref[...] = dot_nn(left, dy_s[...]).astype(bf16)


def row_grad_call(x_list, dy_list, turned, name):
    cols = x_list[0].shape[0 if turned else 1]
    dim = dy_list[0].shape[1]
    total = sum(dy.shape[0] for dy in dy_list)
    tile = 512 if turned else 256
    if turned:
        x_specs = [pl.BlockSpec((tile, x.shape[1]), lambda j: (j, 0)) for x in x_list]
    else:
        x_specs = [pl.BlockSpec((x.shape[0], tile), lambda j: (0, j)) for x in x_list]
    return pl.pallas_call(
        functools.partial(row_grad_kernel, len(x_list), len(dy_list), turned),
        grid=(cols // tile,),
        in_specs=x_specs + [whole(dy.shape) for dy in dy_list],
        out_specs=[pl.BlockSpec((tile, dim), lambda j: (j, 0)), whole((1, dim))],
        out_shape=[shape_of((cols, dim), bf16), shape_of((1, dim), f32)],
        scratch_shapes=[pltpu.VMEM((total, dim), bf16)],
        name=name,
        **params_of(2 * total * cols * dim, 2 * cols * dim + 2 * total * (cols + dim)),
    )(*x_list, *dy_list)


def col_grad_kernel(xs, dys, *refs):
    x_refs, dy_refs = refs[:xs], refs[xs : xs + dys]
    out_ref, sum_ref, xt_s = refs[xs + dys :]

    @pl.when(pl.program_id(0) == 0)
    def _():
        xt_s[...] = stack_rows(x_refs).T

    dy = stack_rows(dy_refs)
    sum_ref[...] = jnp.sum(dy.astype(f32), axis=0, keepdims=True)
    out_ref[...] = dot_nn(xt_s[...], dy).astype(bf16)


def up_grad_call(x_list, du_list):
    half = x_list[0].shape[1]
    ff = du_list[0].shape[1]
    total = sum(x.shape[0] for x in x_list)
    tile = 512
    return pl.pallas_call(
        functools.partial(col_grad_kernel, len(x_list), len(du_list)),
        grid=(ff // tile,),
        in_specs=[whole(x.shape) for x in x_list]
        + [pl.BlockSpec((d.shape[0], tile), lambda j: (0, j)) for d in du_list],
        out_specs=[
            pl.BlockSpec((half, tile), lambda j: (0, j)),
            pl.BlockSpec((1, tile), lambda j: (0, j)),
        ],
        out_shape=[shape_of((half, ff), bf16), shape_of((1, ff), f32)],
        scratch_shapes=[pltpu.VMEM((half, total), bf16)],
        name="up_grad",
        **params_of(2 * total * half * ff, 2 * half * ff + 2 * total * ff),
    )(*x_list, *du_list)


def qkv_grad_kernel(xs, *refs):
    x_refs, d_refs = refs[:xs], refs[xs : 2 * xs]
    out_ref, sum_ref, xt_s = refs[2 * xs :]

    @pl.when((pl.program_id(0) == 0) & (pl.program_id(1) == 0))
    def _():
        xt_s[...] = stack_rows(x_refs).T

    dy = jnp.concatenate([lanes_of(ref.at[:, 0]) for ref in d_refs], axis=0)
    sum_ref[...] = jnp.sum(dy.astype(f32), axis=0, keepdims=True)
    out_ref[...] = dot_nn(xt_s[...], dy).astype(bf16)


def qkv_grad_call(x_list, d_list):
    half = x_list[0].shape[1]
    pairs, _, rows, _ = d_list[0].shape
    dim = pairs * LANES
    total = sum(x.shape[0] for x in x_list)
    group = 4
    steps = pairs // group
    tile = group * LANES
    return pl.pallas_call(
        functools.partial(qkv_grad_kernel, len(x_list)),
        grid=(3, steps),
        in_specs=[whole(x.shape) for x in x_list]
        + [pl.BlockSpec((group, 1, rows, LANES), lambda i, j: (j, i, 0, 0)) for _ in d_list],
        out_specs=[
            pl.BlockSpec((half, tile), lambda i, j: (0, i * steps + j)),
            pl.BlockSpec((1, tile), lambda i, j: (0, i * steps + j)),
        ],
        out_shape=[shape_of((half, 3 * dim), bf16), shape_of((1, 3 * dim), f32)],
        scratch_shapes=[pltpu.VMEM((half, total), bf16)],
        name="qkv_grad",
        **params_of(6 * total * half * dim, 6 * half * dim + 6 * total * dim),
    )(*x_list, *d_list)


def ring_of(count):
    return list(range(0, count, 2)) + list(range(count - 1, 0, -2))


def ring_place(axis):
    count = lax.axis_size(axis)
    me = lax.axis_index(axis)
    return jnp.where(me % 2 == 0, me // 2, count - (me + 1) // 2)


def ring_shift(vals, axis, by):
    order = ring_of(lax.axis_size(axis))
    count = len(order)
    pairs = [(order[i], order[(i + by) % count]) for i in range(count)]
    return lax.ppermute(vals, axis, pairs)


def low_sum(*terms):
    total = terms[0].astype(f32)
    for term in terms[1:]:
        total = total + term.astype(f32)
    return total.astype(bf16)


def tied(token, *vals):
    return lax.optimization_barrier((token,) + vals)[1:]


def ring_sum(pieces, axis):
    count = lax.axis_size(axis)
    place = ring_place(axis)
    half = count // 2
    heights = [own.shape[0] // count for own in pieces]
    pieces = [own.reshape(count, -1, own.shape[1]) for own in pieces]
    cut = sum(heights) // 2

    def index(k):
        return (place + (k + count)) % count

    def take(k):
        parts = [lax.dynamic_index_in_dim(own, index(k), 0, keepdims=False) for own in pieces]
        return parts[0] if len(parts) == 1 else jnp.concatenate(parts, axis=0)

    def put(totals, piece, k, lo=0):
        hi, at = lo + piece.shape[0], 0
        for i, rows in enumerate(heights):
            first, last = max(lo, at), min(hi, at + rows)
            if first < last:
                totals[i] = lax.dynamic_update_slice(
                    totals[i],
                    piece[first - lo : last - lo].astype(f32)[None],
                    (index(k), first - at, 0),
                )
            at += rows

    token = yield None
    (far,) = tied(token, take(half))
    ahead = ring_shift(far[:cut], axis, 1)
    behind = ring_shift(far[cut:], axis, -1)
    token = yield far
    for k in range(half - 1, 0, -1):
        ahead, behind = tied(token, ahead, behind)
        mine_a, mine_b = take(k), take(-k)
        if k == half - 1:
            ahead = jnp.concatenate([low_sum(mine_a[:cut], ahead), mine_a[cut:]], axis=0)
            behind = jnp.concatenate([mine_b[:cut], low_sum(mine_b[cut:], behind)], axis=0)
        else:
            ahead, behind = low_sum(mine_a, ahead), low_sum(mine_b, behind)
        token = behind
        ahead = ring_shift(ahead, axis, 1)
        behind = ring_shift(behind, axis, -1)
        token = yield token
    ahead, behind = tied(token, ahead, behind)
    mine = low_sum(take(0), ahead, behind)
    totals = [jnp.zeros(own.shape, f32) for own in pieces]
    put(totals, mine, 0)
    ahead = ring_shift(mine, axis, 1)
    behind = ring_shift(mine, axis, -1)
    token = yield mine
    for k in range(1, half):
        ahead, behind = tied(token, ahead, behind)
        last = k == half - 1
        next_ahead = ring_shift(ahead[:cut] if last else ahead, axis, 1)
        next_behind = ring_shift(behind[cut:] if last else behind, axis, -1)
        put(totals, ahead, -k)
        put(totals, behind, k)
        token = behind
        ahead, behind = next_ahead, next_behind
        token = yield token
    ahead, behind = tied(token, ahead, behind)
    put(totals, ahead, -half)
    put(totals, behind, half, cut)
    yield [total.reshape(-1, total.shape[2]) for total in totals]


def butterfly_sum(vals, axis):
    count = lax.axis_size(axis)
    if count & (count - 1):
        return lax.psum(vals, axis)
    by = 1
    while by < count:
        vals = vals + lax.ppermute(vals, axis, [(i, i ^ by) for i in range(count)])
        by *= 2
    return vals


def swap(vals):
    return lax.ppermute(vals, "wsh", [(0, 1), (1, 0)])


def pass_on(vals, by):
    pairs = [(0, 1)] if by > 0 else [(1, 0)]
    return lax.ppermute(vals, "section", pairs)


def block_places(block_pair, count):
    want = jnp.arange(2 * count, dtype=jnp.int32)
    device = jnp.arange(count, dtype=jnp.int32)
    first = (block_pair[None, :] == want[:, None]).astype(jnp.int32)
    second = ((2 * count - 1 - block_pair)[None, :] == want[:, None]).astype(jnp.int32)
    return jnp.sum(first * (2 * device) + second * (2 * device + 1), axis=1)


def row_positions(block_pair, stored, tok_dev):
    count = block_pair.shape[0]
    device = stored // tok_dev
    within = stored % tok_dev
    half_rows = tok_dev // 2
    matches = device[:, None] == jnp.arange(count, dtype=jnp.int32)[None, :]
    pair_block = jnp.sum(jnp.where(matches, block_pair[None, :], 0), axis=1)
    block_idx = jnp.where(within < half_rows, pair_block, 2 * count - 1 - pair_block)
    return block_idx * half_rows + within % half_rows


def rotary_table(positions, head_size):
    half_rot = ROT // 2
    lane = jnp.arange(LANES, dtype=jnp.int32) % head_size
    inv_freq = ROPE_BASE ** (-((lane % half_rot).astype(f32) * 2.0) / ROT)
    angles = positions.astype(f32)[:, None] * inv_freq[None, :]
    cosine, sine = jnp.cos(angles), jnp.sin(angles)
    lead, second = (lane < half_rot)[None], ((lane >= half_rot) & (lane < ROT))[None]
    return jnp.stack(
        [
            jnp.where(lead | second, cosine, 1.0),
            jnp.where(lead, -sine, 0.0),
            jnp.where(second, sine, 0.0),
        ]
    )


def body(
    inputs,
    cotangent,
    block_pair,
    qkv_weight,
    qkv_bias,
    proj_weight,
    proj_bias,
    up_weight,
    up_bias,
    down_weight,
    down_bias,
    attn_gain,
    attn_shift,
    mlp_gain,
    mlp_shift,
):
    first_section = lax.axis_index("section") == 0
    count = lax.axis_size("ctx")
    micros, _, tok_dev, dim = inputs.shape
    head_size = dim // HEADS
    half = dim // 2
    my_half = lax.axis_index("wsh")
    wsh = jnp.stack([my_half.astype(jnp.int32), first_section.astype(jnp.int32)])
    one_pair_each = count == dim // LANES

    wq, wp, wu, wd = (w[0] for w in (qkv_weight, proj_weight, up_weight, down_weight))
    small = jnp.concatenate(
        [
            v[0].reshape(-1, half)
            for v in (
                attn_gain,
                attn_shift,
                mlp_gain,
                mlp_shift,
                proj_bias,
                down_bias,
                qkv_bias,
                up_bias,
            )
        ],
        axis=0,
    )
    small_oth = swap(small)
    wq_oth = swap(wq)
    wu_oth = swap(wu)
    wd_oth = swap(wd)
    wp_oth = swap(wp)
    low_part = jnp.where(my_half == 0, small, small_oth).astype(f32)
    high_part = jnp.where(my_half == 0, small_oth, small).astype(f32)
    vecs = jnp.concatenate([low_part[:6], high_part[:6]], axis=1)
    qkv_rows = 6 + qkv_bias.shape[1] // half
    proj_b, down_b = vecs[4:5], vecs[5:6]
    qkv_b = jnp.concatenate([low_part[6:qkv_rows], high_part[6:qkv_rows]], axis=0).reshape(1, -1)
    up_b = jnp.concatenate([low_part[qkv_rows:], high_part[qkv_rows:]], axis=0).reshape(1, -1)

    local_rows = lax.axis_index("ctx") * tok_dev + jnp.arange(tok_dev, dtype=jnp.int32)
    query_pos = row_positions(block_pair, local_rows, tok_dev)
    key_pos = row_positions(block_pair, jnp.arange(count * tok_dev, dtype=jnp.int32), tok_dev)
    tab = rotary_table(query_pos, head_size)
    loc = block_places(block_pair, count)

    def exchange(vals):
        return lax.all_to_all(vals, "ctx", split_axis=0, concat_axis=0, tiled=True)

    def forward(given, got, save):
        qkv, *made = qkv_call(rows_in, given, got, vecs, qkv_b, tab, wq, wq_oth, wsh)
        mlp = mlp_call(made[3], made[4], up_b, down_b, wu, wu_oth, wd, wd_oth, wsh, save)
        if one_pair_each:
            qkv, mlp = lax.optimization_barrier((exchange(qkv), mlp))
            attended, lse = attend_call(qkv, loc)
            attended, kept = exchange(attended), (qkv, lse)
        else:
            attended, kept = wide_attend(qkv, query_pos, key_pos)
        y, a_own, a_oth = proj_call(attended, made[0], mlp[0], proj_b, wp, wp_oth, wsh)
        return y, (made, mlp, (a_own, a_oth), kept)

    def backward_head(given, got, saved):
        _, mlp, _, _ = saved
        da, dy = da_call(cot_in, given, got, wp, wp_oth, wsh)
        du, dnm = mlp_back_call(dy, mlp[1], wu, wu_oth, wd, wd_oth, wsh)
        return (exchange(da) if one_pair_each else da), dy, du, dnm

    def backward_rest(da, dy, dnm, saved):
        made, _, _, kept = saved
        if one_pair_each:
            dqkv = exchange(attend_back_call(kept[0], da, kept[1], loc))
        else:
            dqkv = wide_attend_back(kept, da, query_pos, key_pos)
        return dx_call(dqkv, tab, made[0], dy, dnm, vecs, wq, wq_oth, wsh)

    rows_in, cot_in = inputs[:, 0], cotangent[:, 0]
    y_a, _ = forward(0, None, False)
    y_b, saved_b = forward(1, pass_on(y_a, 1), True)
    y_c, saved_c = forward(0, pass_on(y_b, 1), True)
    da_a, dy_a, _, dnm_a = backward_head(0, None, saved_b)
    da_a, dnm_a = lax.optimization_barrier((da_a, dnm_a))
    _, dx_a, _ = backward_rest(da_a, dy_a, dnm_a, saved_b)
    da_b, dy_b, du_b, dnm_b = backward_head(1, pass_on(dx_a, -1), saved_c)
    da_b, dnm_b = lax.optimization_barrier((da_b, dnm_b))
    back_b, dx_b, sums_b = backward_rest(da_b, dy_b, dnm_b, saved_c)
    da_c, dy_c, du_c, dnm_c = backward_head(0, pass_on(dx_b, -1), saved_b)

    kept_pair = (saved_b, saved_c)
    dy_list = [dy_c, dy_b]
    dy_list = dy_list + [swap(dy) for dy in dy_list]
    down_grad, dy_sum = row_grad_call(
        [s[1][2] for s in kept_pair] + [swap(s[1][3]) for s in kept_pair], dy_list, True, "down_grad"
    )
    proj_grad, _ = row_grad_call(
        [s[2][0] for s in kept_pair] + [swap(s[2][1]) for s in kept_pair], dy_list, False, "proj_grad"
    )
    up_grad, du_sum = up_grad_call(
        [s[0][3] for s in kept_pair] + [swap(s[0][4]) for s in kept_pair],
        [du_c, du_b, swap(du_c), swap(du_b)],
    )
    da_c, dnm_c, down_grad, proj_grad, up_grad = lax.optimization_barrier(
        (da_c, dnm_c, down_grad, proj_grad, up_grad)
    )
    back_c, dx_c, sums_c = backward_rest(da_c, dy_c, dnm_c, saved_b)
    qkv_grad, dqkv_sum = qkv_grad_call(
        [s[0][1] for s in kept_pair] + [swap(s[0][2]) for s in kept_pair],
        [back_c, back_b, swap(back_c), swap(back_b)],
    )

    rows_ring = ring_sum([down_grad, proj_grad], "ctx")
    cols_ring = ring_sum([up_grad], "ctx")
    qkv_ring = ring_sum([qkv_grad], "ctx")
    for ring in (rows_ring, cols_ring, qkv_ring):
        next(ring)
    steps = count + 1
    left = {rows_ring: steps, cols_ring: steps, qkv_ring: steps}
    order = [rows_ring, cols_ring] * 2
    late = [qkv_ring, rows_ring, qkv_ring, cols_ring]
    token = dy_c
    results = {}

    def turn(ring, token):
        left[ring] -= 1
        made = ring.send(token)
        if left[ring] == 0:
            results[ring] = made
            return token
        return made

    for ring in order:
        token = turn(ring, token)
    token = lax.optimization_barrier((token, dx_c))[0]
    for ring in (rows_ring, cols_ring):
        token = turn(ring, token)
    token = lax.optimization_barrier((token, dqkv_sum))[0]
    at = 0
    while any(left.values()):
        ring = late[at % len(late)]
        if left[ring]:
            token = turn(ring, token)
        at += 1
    down_grad, proj_grad = results[rows_ring]
    (up_grad,) = results[cols_ring]
    (qkv_grad,) = results[qkv_ring]

    norm_sums = sums_b + sums_c
    norm_own = lax.dynamic_slice_in_dim(norm_sums, my_half * half, half, 1)
    norm_oth = swap(lax.dynamic_slice_in_dim(norm_sums, (1 - my_half) * half, half, 1))

    def own_part(vec):
        size = vec.shape[1] // 2
        return lax.dynamic_slice_in_dim(vec, my_half * size, size, 1).reshape(-1, half)

    small_sums = jnp.concatenate(
        [norm_own + norm_oth, own_part(dy_sum), own_part(dqkv_sum), own_part(du_sum)], axis=0
    )
    small_sums = butterfly_sum(small_sums, "ctx")
    qkv_end = 5 + dqkv_sum.shape[1] // 2 // half
    dy_total = small_sums[4:5]
    pick = lambda yes, no: jnp.where(first_section, yes, no)
    layer_out = jnp.stack([pick(y_c, y_b), pick(y_b, y_c)])[None, :, None]
    input_grad = jnp.stack([pick(dx_b, dx_c), pick(dx_c, dx_b)])[None, :, None]
    return (
        layer_out,
        input_grad,
        qkv_grad[None],
        small_sums[5:qkv_end].reshape(1, -1),
        proj_grad[None],
        dy_total,
        up_grad[None],
        small_sums[qkv_end:].reshape(1, -1),
        down_grad[None],
        dy_total,
        small_sums[0:1],
        small_sums[1:2],
        small_sums[2:3],
        small_sums[3:4],
    )


def solution(mesh):
    in_specs = (
        P(None, "wsh", "ctx", None),
        P(None, "wsh", "ctx", None),
        P(),
        P("section", "wsh", None),
        P("section", "wsh"),
        P("section", "wsh", None),
        P("section", "wsh"),
        P("section", "wsh", None),
        P("section", "wsh"),
        P("section", "wsh", None),
        P("section", "wsh"),
        P("section", "wsh"),
        P("section", "wsh"),
        P("section", "wsh"),
        P("section", "wsh"),
    )
    out_specs = (
        P("section", None, "wsh", "ctx", None),
        P("section", None, "wsh", "ctx", None),
        P("section", "wsh", None),
        P("section", "wsh"),
        P("section", "wsh", None),
        P("section", "wsh"),
        P("section", "wsh", None),
        P("section", "wsh"),
        P("section", "wsh", None),
        P("section", "wsh"),
        P("section", "wsh"),
        P("section", "wsh"),
        P("section", "wsh"),
        P("section", "wsh"),
    )
    return jax.shard_map(body, mesh=mesh, in_specs=in_specs, out_specs=out_specs, check_vma=False)
```

```python
import functools

import jax
import jax.numpy as jnp
from jax import lax
from jax.experimental import pallas as pl
from jax.experimental.pallas import tpu as pltpu
from jax.sharding import PartitionSpec as P

HEADS = 16
ROT = 16
NORM_EPS = 1e-05
ROPE_BASE = 10000.0
MASKED_SCORE = -1e30
LANES = 128
VMEM_LIMIT = 60 * 1024 * 1024
INV_SQRT2 = 0.7071067811865476
INV_SQRT_2PI = 0.3989422804014327

f32 = jnp.float32
bf16 = jnp.bfloat16


def dot_nn(left, right):
    return lax.dot_general(left, right, (((1,), (0,)), ((), ())), preferred_element_type=f32)


def dot_nt(left, right):
    return lax.dot_general(left, right, (((1,), (1,)), ((), ())), preferred_element_type=f32)


def params_of(flops, nbytes, **extra):
    return dict(
        compiler_params=pltpu.CompilerParams(vmem_limit_bytes=VMEM_LIMIT),
        cost_estimate=pl.CostEstimate(flops=flops, bytes_accessed=nbytes, transcendentals=0),
        **extra,
    )


def whole(shape):
    rank = len(shape)
    return pl.BlockSpec(shape, lambda *args: (0,) * rank)


def shape_of(shape, dtype):
    return jax.ShapeDtypeStruct(shape, dtype)


def rope(vals, tab_ref):
    return (
        vals * tab_ref[0]
        + pltpu.roll(vals, LANES - ROT // 2, 1) * tab_ref[1]
        + pltpu.roll(vals, ROT // 2, 1) * tab_ref[2]
    )


def unrope(vals, tab_ref):
    return (
        vals * tab_ref[0]
        - pltpu.roll(vals, LANES - ROT // 2, 1) * tab_ref[1]
        - pltpu.roll(vals, ROT // 2, 1) * tab_ref[2]
    )


def normalized(hidden):
    row_mean = jnp.mean(hidden, axis=-1, keepdims=True)
    centered = hidden - row_mean
    spread = jnp.mean(centered * centered, axis=-1, keepdims=True)
    scale = lax.rsqrt(spread + NORM_EPS)
    return centered * scale, scale


def start_all(tiles, steps):
    @pl.when(pl.program_id(0) == 0)
    def _():
        for t in range(steps):
            for copy in tiles(t):
                copy.start()


def qkv_kernel(half, wsh_ref, given_ref, got_ref, vec_ref, bias_ref, tab_ref, *rest):
    w_own, w_oth, out_ref, x_ref, na_own, na_oth, nm_own, nm_oth, buf, sems = rest
    part = pl.program_id(0)
    dim = 2 * half

    def tiles(t):
        cols = pl.ds(pl.multiple_of(t * dim, dim), dim)
        return [
            pltpu.make_async_copy(weight.at[:, cols], buf.at[t, side], sems.at[t, side])
            for side, weight in enumerate((w_own, w_oth))
        ]

    start_all(tiles, 3)

    @pl.when(part == 0)
    def _():
        x = jnp.where(wsh_ref[1] == 1, given_ref[...], got_ref[...])
        x_ref[...] = x
        xhat, _ = normalized(x.astype(f32))
        na = (xhat * vec_ref[0:1] + vec_ref[1:2]).astype(bf16)
        nm = (xhat * vec_ref[2:3] + vec_ref[3:4]).astype(bf16)
        first = wsh_ref[0] == 0
        na_own[...] = jnp.where(first, na[:, :half], na[:, half:])
        na_oth[...] = jnp.where(first, na[:, half:], na[:, :half])
        nm_own[...] = jnp.where(first, nm[:, :half], nm[:, half:])
        nm_oth[...] = jnp.where(first, nm[:, half:], nm[:, :half])

    for copy in tiles(part):
        copy.wait()

    def finish(turn):
        for at in range(0, dim, 2 * LANES):
            cols = pl.ds(at, 2 * LANES)
            res = (
                dot_nn(na_own[...], buf[part, 0, :, cols])
                + dot_nn(na_oth[...], buf[part, 1, :, cols])
                + bias_ref[:, cols]
            )
            for pair in range(2):
                vals = res[:, pair * LANES : (pair + 1) * LANES]
                if turn:
                    vals = rope(vals, tab_ref)
                out_ref[at // LANES + pair] = vals.astype(bf16)

    @pl.when(part < 2)
    def _():
        finish(True)

    @pl.when(part == 2)
    def _():
        finish(False)


def layer_of(shape, index):
    return pl.BlockSpec((pl.squeezed,) + shape, lambda *args: (index, 0, 0))


ANYWHERE = pl.BlockSpec(memory_space=pl.ANY)


def qkv_call(given, index, got, vecs, qkv_b, tab, w_own, w_oth, wsh):
    rows, dim = given.shape[1:]
    half = w_own.shape[0]
    pairs = dim // LANES
    got_spec = whole((rows, dim))
    if got is None:
        got, got_spec = given, layer_of((rows, dim), index)
    return pl.pallas_call(
        functools.partial(qkv_kernel, half),
        grid_spec=pltpu.PrefetchScalarGridSpec(
            num_scalar_prefetch=1,
            grid=(3,),
            in_specs=[
                layer_of((rows, dim), index),
                got_spec,
                whole(vecs.shape),
                pl.BlockSpec((1, dim), lambda j, s: (0, j)),
                whole(tab.shape),
                ANYWHERE,
                ANYWHERE,
            ],
            out_specs=[
                pl.BlockSpec((pairs, pl.squeezed, rows, LANES), lambda j, s: (0, j, 0, 0)),
                whole((rows, dim)),
            ]
            + [whole((rows, half))] * 4,
            scratch_shapes=[
                pltpu.VMEM((3, 2, half, dim), bf16),
                pltpu.SemaphoreType.DMA((3, 2)),
            ],
        ),
        out_shape=[shape_of((pairs, 3, rows, LANES), bf16), shape_of((rows, dim), bf16)]
        + [shape_of((rows, half), bf16)] * 4,
        name="qkv_proj",
        **params_of(6 * rows * dim * dim, 6 * dim * dim + 8 * rows * dim),
    )(wsh, given, got, vecs, qkv_b, tab, w_own, w_oth)


MLP_TILE = 1024
MLP_PIECE = 512


def ff_tiles(wsh_ref, up_own, up_oth, dn_own, dn_oth, up_buf, dn_buf, sems):
    tile = dn_buf.shape[1]
    own = dn_own.shape[0] // tile

    def tiles(t):
        cols = pl.ds(pl.multiple_of(((wsh_ref[0] * own + t) % (2 * own)) * tile, tile), tile)
        copies = [
            pltpu.make_async_copy(weight.at[:, cols], up_buf.at[t, side], sems.at[t, side])
            for side, weight in enumerate((up_own, up_oth))
        ]
        held = not isinstance(t, int) or t < own
        down = dn_own if held else dn_oth
        rows = pl.ds((t % own) * tile, tile)
        return copies + [pltpu.make_async_copy(down.at[rows], dn_buf.at[t], sems.at[t, 2])]

    return tiles


def mlp_kernel(own_tiles, save, wsh_ref, nm_own, nm_oth, up_b, down_b, *refs):
    weights, outs = refs[:4], refs[4:]
    if save:
        out_ref, slope_ref, gt_own, gt_oth, up_buf, dn_buf, sems = outs
    else:
        out_ref, up_buf, dn_buf, sems = outs
    step = pl.program_id(0)
    tiles = ff_tiles(wsh_ref, *weights, up_buf, dn_buf, sems)
    start_all(tiles, 2 * own_tiles)

    @pl.when(step == 0)
    def _():
        out_ref[...] = jnp.broadcast_to(down_b[...], out_ref.shape)

    for copy in tiles(step):
        copy.wait()
    for at in range(0, dn_buf.shape[1], MLP_PIECE):
        piece = pl.ds(at, MLP_PIECE)
        pre = (
            dot_nn(nm_own[...], up_buf[step, 0, :, piece])
            + dot_nn(nm_oth[...], up_buf[step, 1, :, piece])
            + up_b[:, piece]
        )
        gate = 0.5 + 0.5 * lax.erf(pre * INV_SQRT2)
        act = (pre * gate).astype(bf16)
        if save:
            slope_ref[:, piece] = (
                gate + pre * (INV_SQRT_2PI * jnp.exp(-0.5 * pre * pre))
            ).astype(bf16)
            turned = act.T

            @pl.when(step < own_tiles)
            def _():
                gt_own[piece] = turned

            @pl.when(step >= own_tiles)
            def _():
                gt_oth[piece] = turned

        out_ref[...] += dot_nn(act, dn_buf[step, piece])


def mlp_scratch(half, dim, steps):
    return [
        pltpu.VMEM((steps, 2, half, MLP_TILE), bf16),
        pltpu.VMEM((steps, MLP_TILE, dim), bf16),
        pltpu.SemaphoreType.DMA((steps, 3)),
    ]


def mlp_call(nm_own, nm_oth, up_b, down_b, up_own, up_oth, dn_own, dn_oth, wsh, save):
    rows, half = nm_own.shape
    dim = dn_own.shape[1]
    ff = up_own.shape[1]
    own = dn_own.shape[0] // MLP_TILE
    by_ff = lambda j, s: (0, (s[0] * own + j) % (2 * own))
    out_specs = [whole((rows, dim))]
    out_shape = [shape_of((rows, dim), f32)]
    if save:
        out_specs += [
            pl.BlockSpec((rows, MLP_TILE), by_ff),
            pl.BlockSpec((MLP_TILE, rows), lambda j, s: (jnp.minimum(j, own - 1), 0)),
            pl.BlockSpec((MLP_TILE, rows), lambda j, s: (jnp.maximum(j - own, 0), 0)),
        ]
        out_shape += [shape_of((rows, ff), bf16)] + [shape_of((ff // 2, rows), bf16)] * 2
    return pl.pallas_call(
        functools.partial(mlp_kernel, own, save),
        grid_spec=pltpu.PrefetchScalarGridSpec(
            num_scalar_prefetch=1,
            grid=(2 * own,),
            in_specs=[whole((rows, half))] * 2
            + [pl.BlockSpec((1, MLP_TILE), by_ff), whole((1, dim))]
            + [ANYWHERE] * 4,
            out_specs=out_specs,
            scratch_shapes=mlp_scratch(half, dim, 2 * own),
        ),
        out_shape=out_shape,
        name="mlp_forward",
        **params_of(4 * rows * dim * ff, 4 * dim * ff + 8 * rows * ff),
    )(wsh, nm_own, nm_oth, up_b, down_b, up_own, up_oth, dn_own, dn_oth)


def mlp_back_kernel(own_tiles, half, wsh_ref, dy_ref, slope_ref, *refs):
    weights = refs[:4]
    du_ref, dnm_ref, acc_own, acc_oth, up_buf, dn_buf, sems = refs[4:]
    step = pl.program_id(0)
    tiles = ff_tiles(wsh_ref, *weights, up_buf, dn_buf, sems)
    start_all(tiles, 2 * own_tiles)

    @pl.when(step == 0)
    def _():
        acc_own[...] = jnp.zeros(acc_own.shape, f32)
        acc_oth[...] = jnp.zeros(acc_oth.shape, f32)

    for copy in tiles(step):
        copy.wait()
    for at in range(0, dn_buf.shape[1], MLP_PIECE):
        piece = pl.ds(at, MLP_PIECE)
        dact = dot_nt(dy_ref[...], dn_buf[step, piece])
        du = (dact * slope_ref[:, piece].astype(f32)).astype(bf16)
        du_ref[:, piece] = du
        acc_own[...] += dot_nt(du, up_buf[step, 0, :, piece])
        acc_oth[...] += dot_nt(du, up_buf[step, 1, :, piece])

    @pl.when(step == 2 * own_tiles - 1)
    def _():
        first = wsh_ref[0] == 0
        dnm_ref[:, :half] = jnp.where(first, acc_own[...], acc_oth[...])
        dnm_ref[:, half:] = jnp.where(first, acc_oth[...], acc_own[...])


def mlp_back_call(dy, slope, up_own, up_oth, dn_own, dn_oth, wsh):
    rows, dim = dy.shape
    half = up_own.shape[0]
    ff = slope.shape[1]
    own = dn_own.shape[0] // MLP_TILE
    by_ff = lambda j, s: (0, (s[0] * own + j) % (2 * own))
    return pl.pallas_call(
        functools.partial(mlp_back_kernel, own, half),
        grid_spec=pltpu.PrefetchScalarGridSpec(
            num_scalar_prefetch=1,
            grid=(2 * own,),
            in_specs=[whole((rows, dim)), pl.BlockSpec((rows, MLP_TILE), by_ff)] + [ANYWHERE] * 4,
            out_specs=[pl.BlockSpec((rows, MLP_TILE), by_ff), whole((rows, dim))],
            scratch_shapes=[pltpu.VMEM((rows, half), f32), pltpu.VMEM((rows, half), f32)]
            + mlp_scratch(half, dim, 2 * own),
        ),
        out_shape=[shape_of((rows, ff), bf16), shape_of((rows, dim), f32)],
        name="mlp_backward",
        **params_of(4 * rows * dim * ff, 4 * dim * ff + 8 * rows * ff),
    )(wsh, dy, slope, up_own, up_oth, dn_own, dn_oth)


def sort_in(loc_ref, ref, dst, half_rows, part=None):
    for block in range(dst.shape[0] // half_rows):
        place = loc_ref[block]
        rows = pl.ds(pl.multiple_of((place % 2) * half_rows, half_rows), half_rows)
        if part is None:
            vals = ref[place // 2, rows, :]
        else:
            vals = ref[place // 2, part, rows, :]
        dst[block * half_rows : (block + 1) * half_rows] = vals


def sort_out(loc_ref, vals, ref, half_rows, part=None):
    for block in range(vals.shape[0] // half_rows):
        place = loc_ref[block]
        rows = pl.ds(pl.multiple_of((place % 2) * half_rows, half_rows), half_rows)
        piece = vals[block * half_rows : (block + 1) * half_rows]
        if part is None:
            ref[place // 2, rows, :] = piece
        else:
            ref[place // 2, part, rows, :] = piece


def head_of(vals, head):
    lane = lax.broadcasted_iota(jnp.int32, vals.shape, 1)
    return jnp.where(lane // (LANES // 2) == head, vals, jnp.zeros_like(vals))


def scores_of(keys, queries, scale, diagonal):
    scores = dot_nt(keys, queries) * scale
    if diagonal:
        key_at = lax.broadcasted_iota(jnp.int32, scores.shape, 0)
        query_at = lax.broadcasted_iota(jnp.int32, scores.shape, 1)
        scores = jnp.where(key_at <= query_at, scores, MASKED_SCORE)
    return scores


def attend_kernel(tile, loc_ref, qkv_ref, o_ref, lse_ref, q_s, k_s, v_s, vt_s, o_s):
    half_rows = qkv_ref.shape[2] // 2
    seq = q_s.shape[0]
    head_size = LANES // 2
    scale = head_size**-0.5
    sort_in(loc_ref, qkv_ref, q_s, half_rows, 0)
    sort_in(loc_ref, qkv_ref, k_s, half_rows, 1)
    sort_in(loc_ref, qkv_ref, v_s, half_rows, 2)
    vt_s[...] = v_s[...].T
    for t in range(seq // tile):
        rows = slice(t * tile, (t + 1) * tile)
        queries = q_s[rows]
        outs = []
        for head in range(2):
            picked = head_of(queries, head)
            parts = [
                scores_of(k_s[i * tile : (i + 1) * tile], picked, scale, i == t)
                for i in range(t + 1)
            ]
            top = functools.reduce(
                jnp.maximum, [jnp.max(p, axis=0, keepdims=True) for p in parts]
            )
            parts = [jnp.exp(p - top) for p in parts]
            total = sum(jnp.sum(p, axis=0, keepdims=True) for p in parts)
            lse_ref[head : head + 1, rows] = top + jnp.log(total)
            inverse = 1.0 / total
            acc = None
            for i, p in enumerate(parts):
                term = dot_nn(
                    vt_s[head * head_size : (head + 1) * head_size, i * tile : (i + 1) * tile],
                    (p * inverse).astype(bf16),
                )
                acc = term if acc is None else acc + term
            outs.append(acc)
        o_s[rows] = jnp.concatenate(outs, axis=0).T.astype(bf16)
    sort_out(loc_ref, o_s, o_ref, half_rows)


def attend_call(qkv, loc):
    count, _, rows, _ = qkv.shape
    seq = count * rows
    return pl.pallas_call(
        functools.partial(attend_kernel, 256),
        grid_spec=pltpu.PrefetchScalarGridSpec(
            num_scalar_prefetch=1,
            grid=(1,),
            in_specs=[whole(qkv.shape)],
            out_specs=[whole((count, rows, LANES)), whole((2, seq))],
            scratch_shapes=[
                pltpu.VMEM((seq, LANES), bf16),
                pltpu.VMEM((seq, LANES), bf16),
                pltpu.VMEM((seq, LANES), bf16),
                pltpu.VMEM((LANES, seq), bf16),
                pltpu.VMEM((seq, LANES), bf16),
            ],
        ),
        out_shape=[shape_of((count, rows, LANES), bf16), shape_of((2, seq), f32)],
        name="attention",
        **params_of(8 * seq * seq * LANES, 8 * seq * LANES),
    )(loc, qkv)


def attend_back_kernel(
    tile, loc_ref, qkv_ref, da_ref, lse_ref, out_ref, q_s, k_s, v_s, da_s, kt_s, dq_s, dk_s, dv_s
):
    half_rows = qkv_ref.shape[2] // 2
    seq = q_s.shape[0]
    head_size = LANES // 2
    scale = head_size**-0.5
    sort_in(loc_ref, qkv_ref, q_s, half_rows, 0)
    sort_in(loc_ref, qkv_ref, k_s, half_rows, 1)
    sort_in(loc_ref, qkv_ref, v_s, half_rows, 2)
    sort_in(loc_ref, da_ref, da_s, half_rows)
    kt_s[...] = k_s[...].T
    dk_s[...] = jnp.zeros(dk_s.shape, f32)
    dv_s[...] = jnp.zeros(dv_s.shape, f32)
    for t in range(seq // tile):
        rows = slice(t * tile, (t + 1) * tile)
        outs = []
        for head in range(2):
            queries = head_of(q_s[rows], head)
            grads = head_of(da_s[rows], head)
            lse = lse_ref[head : head + 1, rows]
            probs, dprobs, row_dot = [], [], 0.0
            for i in range(t + 1):
                keys = slice(i * tile, (i + 1) * tile)
                p = jnp.exp(scores_of(k_s[keys], queries, scale, i == t) - lse)
                dp = dot_nt(v_s[keys], grads)
                row_dot = row_dot + jnp.sum(p * dp, axis=0, keepdims=True)
                dv_s[keys] += dot_nn(p.astype(bf16), grads)
                probs.append(p)
                dprobs.append(dp)
            acc = None
            for i in range(t + 1):
                keys = slice(i * tile, (i + 1) * tile)
                ds = (probs[i] * (dprobs[i] - row_dot) * scale).astype(bf16)
                dk_s[keys] += dot_nn(ds, queries)
                term = dot_nn(kt_s[head * head_size : (head + 1) * head_size, keys], ds)
                acc = term if acc is None else acc + term
            outs.append(acc)
        dq_s[rows] = jnp.concatenate(outs, axis=0).T.astype(bf16)
    sort_out(loc_ref, dq_s, out_ref, half_rows, 0)
    k_s[...] = dk_s[...].astype(bf16)
    v_s[...] = dv_s[...].astype(bf16)
    sort_out(loc_ref, k_s, out_ref, half_rows, 1)
    sort_out(loc_ref, v_s, out_ref, half_rows, 2)


def attend_back_call(qkv, da, lse, loc):
    count, _, rows, _ = qkv.shape
    seq = count * rows
    return pl.pallas_call(
        functools.partial(attend_back_kernel, 256),
        grid_spec=pltpu.PrefetchScalarGridSpec(
            num_scalar_prefetch=1,
            grid=(1,),
            in_specs=[whole(qkv.shape), whole(da.shape), whole(lse.shape)],
            out_specs=whole(qkv.shape),
            scratch_shapes=[
                pltpu.VMEM((seq, LANES), bf16),
                pltpu.VMEM((seq, LANES), bf16),
                pltpu.VMEM((seq, LANES), bf16),
                pltpu.VMEM((seq, LANES), bf16),
                pltpu.VMEM((LANES, seq), bf16),
                pltpu.VMEM((seq, LANES), bf16),
                pltpu.VMEM((seq, LANES), f32),
                pltpu.VMEM((seq, LANES), f32),
            ],
        ),
        out_shape=shape_of(qkv.shape, bf16),
        name="attention_backward",
        **params_of(20 * seq * seq * LANES, 14 * seq * LANES),
    )(loc, qkv, da, lse)


def by_head(parts):
    pairs, rows, lanes = parts.shape
    return jnp.transpose(parts, (1, 0, 2)).reshape(rows, HEADS, pairs * lanes // HEADS)


def by_pair(heads):
    rows = heads.shape[0]
    return jnp.transpose(heads.reshape(rows, -1, LANES), (1, 0, 2))


def wide_scores(queries, keys, query_pos, key_pos):
    raw = jnp.einsum("qhd,khd->hqk", queries, keys, preferred_element_type=f32)
    allowed = (query_pos[:, None] >= key_pos[None, :])[None]
    return jnp.where(allowed, raw * queries.shape[-1] ** (-0.5), MASKED_SCORE)


def key_blocks(arrays, rows):
    return tuple(a.reshape((a.shape[0] // rows, rows) + a.shape[1:]) for a in arrays)


def wide_attend(qkv, query_pos, key_pos):
    queries = by_head(qkv[:, 0])
    keys = lax.all_gather(by_head(qkv[:, 1]), "ctx", axis=0, tiled=True)
    values = lax.all_gather(by_head(qkv[:, 2]), "ctx", axis=0, tiled=True)
    block = min(512, keys.shape[0])
    split = key_blocks((keys, values, key_pos), block)
    rows, _, head_size = queries.shape

    def max_step(carry, block_in):
        top, total = carry
        scores = wide_scores(queries, block_in[0], query_pos, block_in[2])
        new_top = jnp.maximum(top, jnp.max(scores, axis=-1))
        part = jnp.sum(jnp.exp(scores - new_top[..., None]), axis=-1)
        return ((new_top, total * jnp.exp(top - new_top) + part), None)

    start = (jnp.full((HEADS, rows), MASKED_SCORE, f32), jnp.zeros((HEADS, rows), f32))
    (top, total), _ = lax.scan(max_step, start, split)
    lse = top + jnp.log(total)

    def value_step(running, block_in):
        scores = wide_scores(queries, block_in[0], query_pos, block_in[2])
        probs = jnp.exp(scores - lse[..., None]).astype(bf16)
        term = jnp.einsum("hqk,khd->qhd", probs, block_in[1], preferred_element_type=f32)
        return (running + term, None)

    attended, _ = lax.scan(value_step, jnp.zeros((rows, HEADS, head_size), f32), split)
    return by_pair(attended.astype(bf16)), (queries, keys, values, lse)


def wide_attend_back(kept, da, query_pos, key_pos):
    queries, keys, values, lse = kept
    grads = by_head(da)
    block = min(512, keys.shape[0])
    split = key_blocks((keys, values, key_pos), block)
    scale = queries.shape[-1] ** (-0.5)

    def pieces(block_in):
        scores = wide_scores(queries, block_in[0], query_pos, block_in[2])
        probs = jnp.exp(scores - lse[..., None])
        dprobs = jnp.einsum("qhd,khd->hqk", grads, block_in[1], preferred_element_type=f32)
        return probs, dprobs

    def dot_step(running, block_in):
        probs, dprobs = pieces(block_in)
        return (running + jnp.sum(probs * dprobs, axis=-1), None)

    row_dot, _ = lax.scan(dot_step, jnp.zeros(lse.shape, f32), split)

    def key_step(running, block_in):
        probs, dprobs = pieces(block_in)
        ds = (scale * probs * (dprobs - row_dot[..., None])).astype(bf16)
        running = running + jnp.einsum("hqk,khd->qhd", ds, block_in[0], preferred_element_type=f32)
        dk = jnp.einsum("hqk,qhd->khd", ds, queries, preferred_element_type=f32)
        dv = jnp.einsum("hqk,qhd->khd", probs.astype(bf16), grads, preferred_element_type=f32)
        return (running, (dk.astype(bf16), dv.astype(bf16)))

    dq, (dk, dv) = lax.scan(key_step, jnp.zeros(queries.shape, f32), split)
    dk, dv = (
        lax.psum_scatter(part.reshape(keys.shape), "ctx", scatter_dimension=0, tiled=True)
        for part in (dk, dv)
    )
    return jnp.stack([by_pair(dq.astype(bf16)), by_pair(dk), by_pair(dv)], axis=1)


def lanes_of(ref):
    return jnp.concatenate([ref[i] for i in range(ref.shape[0])], axis=1)


def proj_kernel(half, wsh_ref, a_ref, x_ref, mlp_ref, bias_ref, p_own, p_oth, y_ref, a_own, a_oth):
    first = wsh_ref[0] == 0
    a = lanes_of(a_ref)
    own = jnp.where(first, a[:, :half], a[:, half:])
    oth = jnp.where(first, a[:, half:], a[:, :half])
    a_own[...] = own
    a_oth[...] = oth
    attn = dot_nn(own, p_own[...]) + dot_nn(oth, p_oth[...]) + bias_ref[...]
    y_ref[...] = (x_ref[...].astype(f32) + attn + mlp_ref[...]).astype(bf16)


def proj_call(a, x, mlp, bias, p_own, p_oth, wsh):
    rows, dim = x.shape
    half = p_own.shape[0]
    return pl.pallas_call(
        functools.partial(proj_kernel, half),
        grid_spec=pltpu.PrefetchScalarGridSpec(
            num_scalar_prefetch=1,
            grid=(1,),
            in_specs=[
                whole(a.shape),
                whole(x.shape),
                whole((rows, dim)),
                whole(bias.shape),
                whole(p_own.shape),
                whole(p_oth.shape),
            ],
            out_specs=[whole((rows, dim)), whole((rows, half)), whole((rows, half))],
        ),
        out_shape=[shape_of((rows, dim), bf16)] + [shape_of((rows, half), bf16)] * 2,
        name="attn_out",
        **params_of(2 * rows * dim * dim, 2 * dim * dim + 10 * rows * dim),
    )(wsh, a, x, mlp, bias, p_own, p_oth)


def da_kernel(wsh_ref, given_ref, got_ref, p_own, p_oth, out_ref, dy_ref):
    dy = jnp.where(wsh_ref[1] == 1, got_ref[...], given_ref[...])
    dy_ref[...] = dy
    wsh = wsh_ref[0]
    count = out_ref.shape[0] // 2
    for place, weight in ((wsh * count, p_own), ((1 - wsh) * count, p_oth)):
        part = dot_nt(dy, weight[...]).astype(bf16)
        for i in range(count):
            out_ref[place + i] = part[:, i * LANES : (i + 1) * LANES]


def da_call(given, index, got, p_own, p_oth, wsh):
    rows, dim = given.shape[1:]
    pairs = dim // LANES
    got_spec = whole((rows, dim))
    if got is None:
        got, got_spec = given, layer_of((rows, dim), index)
    return pl.pallas_call(
        da_kernel,
        grid_spec=pltpu.PrefetchScalarGridSpec(
            num_scalar_prefetch=1,
            grid=(1,),
            in_specs=[layer_of((rows, dim), index), got_spec]
            + [whole(p_own.shape), whole(p_oth.shape)],
            out_specs=[whole((pairs, rows, LANES)), whole((rows, dim))],
        ),
        out_shape=[shape_of((pairs, rows, LANES), bf16), shape_of((rows, dim), bf16)],
        name="attn_out_backward",
        **params_of(2 * rows * dim * dim, 2 * dim * dim + 4 * rows * dim),
    )(wsh, given, got, p_own, p_oth)


DX_ROWS = 256


def dx_kernel(half, wsh_ref, dqkv_ref, tab_ref, x_ref, dy_ref, dnm_ref, vec_ref, *rest):
    w_own, w_oth, back_ref, dx_ref, sums_ref, grad_s, buf, sems = rest
    pairs = dqkv_ref.shape[0]
    copies = []
    for side, weight in enumerate((w_own, w_oth)):
        for t in range(half // DX_ROWS):
            copies.append(
                pltpu.make_async_copy(
                    weight.at[pl.ds(t * DX_ROWS, DX_ROWS)], buf.at[side, t], sems.at[side, t]
                )
            )
    for copy in copies:
        copy.start()
    for part in range(3):
        for pair in range(pairs):
            vals = dqkv_ref[pair, part]
            if part < 2:
                vals = unrope(vals.astype(f32), tab_ref).astype(bf16)
            back_ref[pair, part] = vals
            grad_s[:, pl.ds((part * pairs + pair) * LANES, LANES)] = vals
    halves = []
    for side in range(2):
        cols = []
        for t in range(half // DX_ROWS):
            copies[side * (half // DX_ROWS) + t].wait()
            cols.append(dot_nt(grad_s[...], buf[side, t]))
        halves.append(jnp.concatenate(cols, axis=1))
    first = wsh_ref[0] == 0
    own, oth = halves
    dna = jnp.concatenate([jnp.where(first, own, oth), jnp.where(first, oth, own)], axis=1)
    dnm = dnm_ref[...]
    xhat, scale = normalized(x_ref[...].astype(f32))
    grad = dna * vec_ref[0:1] + dnm * vec_ref[2:3]
    inner = (
        grad
        - jnp.mean(grad, axis=-1, keepdims=True)
        - xhat * jnp.mean(grad * xhat, axis=-1, keepdims=True)
    )
    dx_ref[...] = (dy_ref[...].astype(f32) + scale * inner).astype(bf16)
    sums_ref[0:1] = jnp.sum(dna * xhat, axis=0, keepdims=True)
    sums_ref[1:2] = jnp.sum(dna, axis=0, keepdims=True)
    sums_ref[2:3] = jnp.sum(dnm * xhat, axis=0, keepdims=True)
    sums_ref[3:4] = jnp.sum(dnm, axis=0, keepdims=True)


def dx_call(dqkv, tab, x, dy, dnm, vecs, w_own, w_oth, wsh):
    rows, dim = x.shape
    half = w_own.shape[0]
    return pl.pallas_call(
        functools.partial(dx_kernel, half),
        grid_spec=pltpu.PrefetchScalarGridSpec(
            num_scalar_prefetch=1,
            grid=(1,),
            in_specs=[
                whole(dqkv.shape),
                whole(tab.shape),
                whole(x.shape),
                whole(dy.shape),
                whole(dnm.shape),
                whole(vecs.shape),
                ANYWHERE,
                ANYWHERE,
            ],
            out_specs=[whole(dqkv.shape), whole((rows, dim)), whole((4, dim))],
            scratch_shapes=[
                pltpu.VMEM((rows, 3 * dim), bf16),
                pltpu.VMEM((2, half // DX_ROWS, DX_ROWS, 3 * dim), bf16),
                pltpu.SemaphoreType.DMA((2, half // DX_ROWS)),
            ],
        ),
        out_shape=[
            shape_of(dqkv.shape, bf16),
            shape_of((rows, dim), bf16),
            shape_of((4, dim), f32),
        ],
        name="section_input_grad",
        **params_of(6 * rows * dim * dim, 6 * dim * dim + 16 * rows * dim),
    )(wsh, dqkv, tab, x, dy, dnm, vecs, w_own, w_oth)


def stack_rows(refs, cols=slice(None)):
    return jnp.concatenate([ref[:, cols] for ref in refs], axis=0)


def row_grad_kernel(micros, *refs):
    gt_refs, a_refs, dy_refs = (refs[i * micros : (i + 1) * micros] for i in range(3))
    out_ref, sum_ref, dy_s = refs[3 * micros :]

    @pl.when(pl.program_id(0) == 0)
    def _():
        dy = stack_rows(dy_refs)
        dy_s[...] = dy
        sum_ref[...] = jnp.sum(dy.astype(f32), axis=0, keepdims=True)

    chunks = out_ref.shape[0]
    down = dot_nn(jnp.concatenate([ref[...] for ref in gt_refs], axis=1), dy_s[...])
    proj = dot_nn(stack_rows(a_refs).T, dy_s[...])
    down_rows, proj_rows = down.shape[0] // chunks, proj.shape[0] // chunks
    for c in range(chunks):
        out_ref[c, :down_rows] = down[c * down_rows : (c + 1) * down_rows].astype(bf16)
        out_ref[c, down_rows:] = proj[c * proj_rows : (c + 1) * proj_rows].astype(bf16)


def row_grad_call(gt_list, a_list, dy_list, count):
    down_rows, rows = gt_list[0].shape
    proj_rows = a_list[0].shape[1]
    dim = dy_list[0].shape[1]
    micros = len(dy_list)
    total = micros * rows
    steps = 4
    chunk = (down_rows + proj_rows) // count
    return pl.pallas_call(
        functools.partial(row_grad_kernel, micros),
        grid=(steps,),
        in_specs=[pl.BlockSpec((down_rows // steps, rows), lambda j: (j, 0))] * micros
        + [pl.BlockSpec((rows, proj_rows // steps), lambda j: (0, j))] * micros
        + [whole((rows, dim))] * micros,
        out_specs=[
            pl.BlockSpec((count // steps, chunk, dim), lambda j: (j, 0, 0)),
            whole((1, dim)),
        ],
        out_shape=[shape_of((count, chunk, dim), bf16), shape_of((1, dim), f32)],
        scratch_shapes=[pltpu.VMEM((total, dim), bf16)],
        name="down_proj_grad",
        **params_of(
            2 * total * (down_rows + proj_rows) * dim,
            2 * (down_rows + proj_rows) * (dim + total),
        ),
    )(*gt_list, *a_list, *dy_list)


def col_grad_kernel(xs, dys, *refs):
    x_refs, dy_refs = refs[:xs], refs[xs : xs + dys]
    out_ref, sum_ref, xt_s = refs[xs + dys :]

    @pl.when(pl.program_id(0) == 0)
    def _():
        xt_s[...] = stack_rows(x_refs).T

    dy = stack_rows(dy_refs)
    sum_ref[...] = jnp.sum(dy.astype(f32), axis=0, keepdims=True)
    out_ref[...] = dot_nn(xt_s[...], dy).astype(bf16)


def up_grad_call(x_list, du_list):
    half = x_list[0].shape[1]
    ff = du_list[0].shape[1]
    total = sum(x.shape[0] for x in x_list)
    tile = 512
    return pl.pallas_call(
        functools.partial(col_grad_kernel, len(x_list), len(du_list)),
        grid=(ff // tile,),
        in_specs=[whole(x.shape) for x in x_list]
        + [pl.BlockSpec((d.shape[0], tile), lambda j: (0, j)) for d in du_list],
        out_specs=[
            pl.BlockSpec((half, tile), lambda j: (0, j)),
            pl.BlockSpec((1, tile), lambda j: (0, j)),
        ],
        out_shape=[shape_of((half, ff), bf16), shape_of((1, ff), f32)],
        scratch_shapes=[pltpu.VMEM((half, total), bf16)],
        name="up_grad",
        **params_of(2 * total * half * ff, 2 * half * ff + 2 * total * ff),
    )(*x_list, *du_list)


def qkv_grad_kernel(xs, *refs):
    x_refs, d_refs = refs[:xs], refs[xs : 2 * xs]
    out_ref, sum_ref, xt_s = refs[2 * xs :]

    @pl.when((pl.program_id(0) == 0) & (pl.program_id(1) == 0))
    def _():
        xt_s[...] = stack_rows(x_refs).T

    dy = jnp.concatenate([lanes_of(ref.at[:, 0]) for ref in d_refs], axis=0)
    sum_ref[...] = jnp.sum(dy.astype(f32), axis=0, keepdims=True)
    out_ref[...] = dot_nn(xt_s[...], dy).astype(bf16)


def qkv_grad_call(x_list, d_list):
    half = x_list[0].shape[1]
    pairs, _, rows, _ = d_list[0].shape
    dim = pairs * LANES
    total = sum(x.shape[0] for x in x_list)
    group = 4
    steps = pairs // group
    tile = group * LANES
    return pl.pallas_call(
        functools.partial(qkv_grad_kernel, len(x_list)),
        grid=(3, steps),
        in_specs=[whole(x.shape) for x in x_list]
        + [pl.BlockSpec((group, 1, rows, LANES), lambda i, j: (j, i, 0, 0)) for _ in d_list],
        out_specs=[
            pl.BlockSpec((half, tile), lambda i, j: (0, i * steps + j)),
            pl.BlockSpec((1, tile), lambda i, j: (0, i * steps + j)),
        ],
        out_shape=[shape_of((half, 3 * dim), bf16), shape_of((1, 3 * dim), f32)],
        scratch_shapes=[pltpu.VMEM((half, total), bf16)],
        name="qkv_grad",
        **params_of(6 * total * half * dim, 6 * half * dim + 6 * total * dim),
    )(*x_list, *d_list)


def ring_of(count):
    return list(range(0, count, 2)) + list(range(count - 1, 0, -2))


def ring_place(axis):
    count = lax.axis_size(axis)
    me = lax.axis_index(axis)
    return jnp.where(me % 2 == 0, me // 2, count - (me + 1) // 2)


def ring_shift(vals, axis, by):
    order = ring_of(lax.axis_size(axis))
    count = len(order)
    pairs = [(order[i], order[(i + by) % count]) for i in range(count)]
    return lax.ppermute(vals, axis, pairs)


def low_sum(*terms):
    total = terms[0].astype(f32)
    for term in terms[1:]:
        total = total + term.astype(f32)
    return total.astype(bf16)


def tied(token, *vals):
    return lax.optimization_barrier((token,) + vals)[1:]


def ring_sum(own, heights, axis):
    count = lax.axis_size(axis)
    place = ring_place(axis)
    half = count // 2
    cut = sum(heights) // 2

    def index(k):
        return (place + (k + count)) % count

    def take(k):
        return lax.dynamic_index_in_dim(own, index(k), 0, keepdims=False)

    def put(totals, piece, k, lo=0):
        hi, at = lo + piece.shape[0], 0
        for i, rows in enumerate(heights):
            first, last = max(lo, at), min(hi, at + rows)
            if first < last:
                totals[i] = lax.dynamic_update_slice(
                    totals[i],
                    piece[first - lo : last - lo].astype(f32)[None],
                    (index(k), first - at, 0),
                )
            at += rows

    token = yield None
    (far,) = tied(token, take(half))
    ahead = ring_shift(far[:cut], axis, 1)
    behind = ring_shift(far[cut:], axis, -1)
    token = yield far
    for k in range(half - 1, 0, -1):
        ahead, behind = tied(token, ahead, behind)
        mine_a, mine_b = take(k), take(-k)
        if k == half - 1:
            ahead = jnp.concatenate([low_sum(mine_a[:cut], ahead), mine_a[cut:]], axis=0)
            behind = jnp.concatenate([mine_b[:cut], low_sum(mine_b[cut:], behind)], axis=0)
        else:
            ahead, behind = low_sum(mine_a, ahead), low_sum(mine_b, behind)
        token = behind
        ahead = ring_shift(ahead, axis, 1)
        behind = ring_shift(behind, axis, -1)
        token = yield token
    ahead, behind = tied(token, ahead, behind)
    mine = low_sum(take(0), ahead, behind)
    totals = [jnp.zeros((count, rows, own.shape[2]), f32) for rows in heights]
    put(totals, mine, 0)
    ahead = ring_shift(mine, axis, 1)
    behind = ring_shift(mine, axis, -1)
    token = yield mine
    for k in range(1, half):
        ahead, behind = tied(token, ahead, behind)
        last = k == half - 1
        next_ahead = ring_shift(ahead[:cut] if last else ahead, axis, 1)
        next_behind = ring_shift(behind[cut:] if last else behind, axis, -1)
        put(totals, ahead, -k)
        put(totals, behind, k)
        token = behind
        ahead, behind = next_ahead, next_behind
        token = yield token
    ahead, behind = tied(token, ahead, behind)
    put(totals, ahead, -half)
    put(totals, behind, half, cut)
    yield [total.reshape(-1, total.shape[2]) for total in totals]


def butterfly_sum(vals, axis):
    count = lax.axis_size(axis)
    if count & (count - 1):
        return lax.psum(vals, axis)
    by = 1
    while by < count:
        vals = vals + lax.ppermute(vals, axis, [(i, i ^ by) for i in range(count)])
        by *= 2
    return vals


def swap(vals):
    return lax.ppermute(vals, "wsh", [(0, 1), (1, 0)])


def pass_on(vals, by):
    pairs = [(0, 1)] if by > 0 else [(1, 0)]
    return lax.ppermute(vals, "section", pairs)


def block_places(block_pair, count):
    want = jnp.arange(2 * count, dtype=jnp.int32)
    device = jnp.arange(count, dtype=jnp.int32)
    first = (block_pair[None, :] == want[:, None]).astype(jnp.int32)
    second = ((2 * count - 1 - block_pair)[None, :] == want[:, None]).astype(jnp.int32)
    return jnp.sum(first * (2 * device) + second * (2 * device + 1), axis=1)


def row_positions(block_pair, stored, tok_dev):
    count = block_pair.shape[0]
    device = stored // tok_dev
    within = stored % tok_dev
    half_rows = tok_dev // 2
    matches = device[:, None] == jnp.arange(count, dtype=jnp.int32)[None, :]
    pair_block = jnp.sum(jnp.where(matches, block_pair[None, :], 0), axis=1)
    block_idx = jnp.where(within < half_rows, pair_block, 2 * count - 1 - pair_block)
    return block_idx * half_rows + within % half_rows


def rotary_table(positions, head_size):
    half_rot = ROT // 2
    lane = jnp.arange(LANES, dtype=jnp.int32) % head_size
    inv_freq = ROPE_BASE ** (-((lane % half_rot).astype(f32) * 2.0) / ROT)
    angles = positions.astype(f32)[:, None] * inv_freq[None, :]
    cosine, sine = jnp.cos(angles), jnp.sin(angles)
    lead, second = (lane < half_rot)[None], ((lane >= half_rot) & (lane < ROT))[None]
    return jnp.stack(
        [
            jnp.where(lead | second, cosine, 1.0),
            jnp.where(lead, -sine, 0.0),
            jnp.where(second, sine, 0.0),
        ]
    )


def body(
    inputs,
    cotangent,
    block_pair,
    qkv_weight,
    qkv_bias,
    proj_weight,
    proj_bias,
    up_weight,
    up_bias,
    down_weight,
    down_bias,
    attn_gain,
    attn_shift,
    mlp_gain,
    mlp_shift,
):
    first_section = lax.axis_index("section") == 0
    count = lax.axis_size("ctx")
    micros, _, tok_dev, dim = inputs.shape
    head_size = dim // HEADS
    half = dim // 2
    my_half = lax.axis_index("wsh")
    wsh = jnp.stack([my_half.astype(jnp.int32), first_section.astype(jnp.int32)])
    one_pair_each = count == dim // LANES

    wq, wp, wu, wd = (w[0] for w in (qkv_weight, proj_weight, up_weight, down_weight))
    small = jnp.concatenate(
        [
            v[0].reshape(-1, half)
            for v in (
                attn_gain,
                attn_shift,
                mlp_gain,
                mlp_shift,
                proj_bias,
                down_bias,
                qkv_bias,
                up_bias,
            )
        ],
        axis=0,
    )
    small_oth = swap(small)
    wq_oth = swap(wq)
    wu_oth = swap(wu)
    wd_oth = swap(wd)
    wp_oth = swap(wp)
    low_part = jnp.where(my_half == 0, small, small_oth).astype(f32)
    high_part = jnp.where(my_half == 0, small_oth, small).astype(f32)
    vecs = jnp.concatenate([low_part[:6], high_part[:6]], axis=1)
    qkv_rows = 6 + qkv_bias.shape[1] // half
    proj_b, down_b = vecs[4:5], vecs[5:6]
    qkv_b = jnp.concatenate([low_part[6:qkv_rows], high_part[6:qkv_rows]], axis=0).reshape(1, -1)
    up_b = jnp.concatenate([low_part[qkv_rows:], high_part[qkv_rows:]], axis=0).reshape(1, -1)

    local_rows = lax.axis_index("ctx") * tok_dev + jnp.arange(tok_dev, dtype=jnp.int32)
    query_pos = row_positions(block_pair, local_rows, tok_dev)
    key_pos = row_positions(block_pair, jnp.arange(count * tok_dev, dtype=jnp.int32), tok_dev)
    tab = rotary_table(query_pos, head_size)
    loc = block_places(block_pair, count)

    def exchange(vals):
        return lax.all_to_all(vals, "ctx", split_axis=0, concat_axis=0, tiled=True)

    def norm_qkv(index, got):
        return qkv_call(rows_in, index, got, vecs, qkv_b, tab, wq, wq_oth, wsh)

    def mlp(made, save):
        return mlp_call(made[4], made[5], up_b, down_b, wu, wu_oth, wd, wd_oth, wsh, save)

    def mlp_back(dy, mlp_kept):
        return mlp_back_call(dy, mlp_kept[1], wu, wu_oth, wd, wd_oth, wsh)

    def out_back(index, got):
        return da_call(cot_in, index, got, wp, wp_oth, wsh)

    def to_heads(vals):
        return exchange(vals) if one_pair_each else vals

    def to_rows(vals):
        return exchange(vals) if one_pair_each else vals

    def attend(qkv):
        if one_pair_each:
            attended, lse = attend_call(qkv, loc)
            return attended, (qkv, lse)
        return wide_attend(qkv, query_pos, key_pos)

    def attend_back(kept, da):
        if one_pair_each:
            return attend_back_call(kept[0], da, kept[1], loc)
        return wide_attend_back(kept, da, query_pos, key_pos)

    def project(attended, made, mlp_out):
        return proj_call(attended, made[1], mlp_out[0], proj_b, wp, wp_oth, wsh)

    def input_grad_of(dqkv, made, dy, dnm):
        return dx_call(dqkv, tab, made[1], dy, dnm, vecs, wq, wq_oth, wsh)

    rows_in, cot_in = inputs[:, 0], cotangent[:, 0]
    da_a, dy_a = out_back(0, None)
    (rows_in,) = tied(dy_a, rows_in)
    da_a = to_heads(da_a)

    made_a = norm_qkv(0, None)
    qkv_a = to_heads(made_a[0])
    mlp_a = mlp(made_a, False)
    (qkv_a,) = tied(mlp_a[0], qkv_a)
    att_a, _ = attend(qkv_a)
    y_a = project(to_rows(att_a), made_a, mlp_a)[0]

    made_b = norm_qkv(1, pass_on(y_a, 1))
    qkv_b_ = to_heads(made_b[0])
    mlp_b = mlp(made_b, True)
    _, dnm_a = mlp_back(dy_a, mlp_b)
    (qkv_b_,) = tied(dnm_a, qkv_b_)
    att_b, kept_b = attend(qkv_b_)
    att_b = to_rows(att_b)
    (da_a,) = tied(att_b if not one_pair_each else kept_b[1], da_a)
    dqkv_a = attend_back(kept_b, da_a)
    (att_b,) = tied(dqkv_a, att_b)
    dqkv_a = to_rows(dqkv_a)
    y_b, *a_b = project(att_b, made_b, mlp_b)

    made_c = norm_qkv(0, pass_on(y_b, 1))
    (dqkv_a,) = tied(made_c[1], dqkv_a)
    qkv_c = to_heads(made_c[0])
    _, dx_a, _ = input_grad_of(dqkv_a, made_b, dy_a, dnm_a)
    got_a = pass_on(dx_a, -1)
    nm_c = tied(dx_a, made_c[4], made_c[5])
    made_c = list(made_c[:4]) + list(nm_c)
    mlp_c = mlp(made_c, True)
    (got_a,) = tied(mlp_c[0], got_a)
    da_b, dy_b = out_back(1, got_a)
    (qkv_c,) = tied(dy_b, qkv_c)
    da_b = to_heads(da_b)
    att_c, kept_c = attend(qkv_c)
    (dy_b2,) = tied(att_c, dy_b)
    du_b, dnm_b = mlp_back(dy_b2, mlp_c)
    (da_b,) = tied(dnm_b, da_b)
    dqkv_b = attend_back(kept_c, da_b)
    (att_c,) = tied(dqkv_b, att_c)
    dqkv_b = to_rows(dqkv_b)
    back_b, dx_b, sums_b = input_grad_of(dqkv_b, made_c, dy_b, dnm_b)
    (att_c,) = tied(dx_b, att_c)
    att_c = to_rows(att_c)

    da_c, dy_c = out_back(0, pass_on(dx_b, -1))
    (att_c,) = tied(dy_c, att_c)
    y_c, *a_c = project(att_c, made_c, mlp_c)
    da_c = to_heads(da_c)
    dy_list = [dy_c, dy_b, swap(dy_c), swap(dy_b)]
    row_grad, dy_sum = row_grad_call(
        [mlp_b[2], mlp_c[2], swap(mlp_b[3]), swap(mlp_c[3])],
        [a_b[0], a_c[0], swap(a_b[1]), swap(a_c[1])],
        dy_list,
        count,
    )
    rows_ring = ring_sum(row_grad, (wd.shape[0] // count, wp.shape[0] // count), "ctx")
    next(rows_ring)
    token = rows_ring.send(dy_sum)
    (dy_c2,) = tied(token, dy_c)
    du_c, dnm_c = mlp_back(dy_c2, mlp_b)
    (da_c,) = tied(dnm_c, da_c)
    dqkv_c = attend_back(kept_b, da_c)
    (nm_c,) = tied(dqkv_c, made_b[4])
    dqkv_c = to_rows(dqkv_c)
    up_grad, du_sum = up_grad_call(
        [nm_c, made_c[4], swap(made_b[5]), swap(made_c[5])], [du_c, du_b, swap(du_c), swap(du_b)]
    )
    cols_ring = ring_sum(up_grad.reshape(count, -1, up_grad.shape[1]), (half // count,), "ctx")
    next(cols_ring)
    token = cols_ring.send(du_sum)
    token = rows_ring.send(token)
    (dqkv_c,) = tied(token, dqkv_c)
    back_c, dx_c, sums_c = input_grad_of(dqkv_c, made_b, dy_c, dnm_c)
    token = cols_ring.send(dx_c)
    (back_c2,) = tied(token, back_c)
    qkv_grad, dqkv_sum = qkv_grad_call(
        [made_b[2], made_c[2], swap(made_b[3]), swap(made_c[3])],
        [back_c2, back_b, swap(back_c), swap(back_b)],
    )
    qkv_ring = ring_sum(qkv_grad.reshape(count, -1, qkv_grad.shape[1]), (half // count,), "ctx")
    next(qkv_ring)
    token = dqkv_sum
    steps = count + 1
    left = {rows_ring: steps - 2, cols_ring: steps - 2, qkv_ring: steps}
    late = [qkv_ring, rows_ring, qkv_ring, cols_ring]
    results = {}

    def turn(ring, token):
        left[ring] -= 1
        made = ring.send(token)
        if left[ring] == 0:
            results[ring] = made
            return token
        return made

    at = 0
    while any(left.values()):
        ring = late[at % len(late)]
        if left[ring]:
            token = turn(ring, token)
        at += 1
    down_grad, proj_grad = results[rows_ring]
    (up_grad,) = results[cols_ring]
    (qkv_grad,) = results[qkv_ring]

    norm_sums = sums_b + sums_c
    norm_own = lax.dynamic_slice_in_dim(norm_sums, my_half * half, half, 1)
    norm_oth = swap(lax.dynamic_slice_in_dim(norm_sums, (1 - my_half) * half, half, 1))

    def own_part(vec):
        size = vec.shape[1] // 2
        return lax.dynamic_slice_in_dim(vec, my_half * size, size, 1).reshape(-1, half)

    small_sums = jnp.concatenate(
        [norm_own + norm_oth, own_part(dy_sum), own_part(dqkv_sum), own_part(du_sum)], axis=0
    )
    small_sums = butterfly_sum(small_sums, "ctx")
    qkv_end = 5 + dqkv_sum.shape[1] // 2 // half
    dy_total = small_sums[4:5]
    pick = lambda yes, no: jnp.where(first_section, yes, no)
    layer_out = jnp.stack([pick(y_c, y_b), pick(y_b, y_c)])[None, :, None]
    input_grad = jnp.stack([pick(dx_b, dx_c), pick(dx_c, dx_b)])[None, :, None]
    return (
        layer_out,
        input_grad,
        qkv_grad[None],
        small_sums[5:qkv_end].reshape(1, -1),
        proj_grad[None],
        dy_total,
        up_grad[None],
        small_sums[qkv_end:].reshape(1, -1),
        down_grad[None],
        dy_total,
        small_sums[0:1],
        small_sums[1:2],
        small_sums[2:3],
        small_sums[3:4],
    )


def solution(mesh):
    in_specs = (
        P(None, "wsh", "ctx", None),
        P(None, "wsh", "ctx", None),
        P(),
        P("section", "wsh", None),
        P("section", "wsh"),
        P("section", "wsh", None),
        P("section", "wsh"),
        P("section", "wsh", None),
        P("section", "wsh"),
        P("section", "wsh", None),
        P("section", "wsh"),
        P("section", "wsh"),
        P("section", "wsh"),
        P("section", "wsh"),
        P("section", "wsh"),
    )
    out_specs = (
        P("section", None, "wsh", "ctx", None),
        P("section", None, "wsh", "ctx", None),
        P("section", "wsh", None),
        P("section", "wsh"),
        P("section", "wsh", None),
        P("section", "wsh"),
        P("section", "wsh", None),
        P("section", "wsh"),
        P("section", "wsh", None),
        P("section", "wsh"),
        P("section", "wsh"),
        P("section", "wsh"),
        P("section", "wsh"),
        P("section", "wsh"),
    )
    return jax.shard_map(body, mesh=mesh, in_specs=in_specs, out_specs=out_specs, check_vma=False)
```

```python
import functools

import jax
import jax.numpy as jnp
from jax import lax
from jax.experimental import pallas as pl
from jax.experimental.pallas import tpu as pltpu
from jax.sharding import PartitionSpec as P

HEADS = 16
ROT = 16
NORM_EPS = 1e-05
ROPE_BASE = 10000.0
MASKED_SCORE = -1e30
LANES = 128
VMEM_LIMIT = 60 * 1024 * 1024
INV_SQRT2 = 0.7071067811865476
INV_SQRT_2PI = 0.3989422804014327

f32 = jnp.float32
bf16 = jnp.bfloat16


def dot_nn(left, right):
    return lax.dot_general(left, right, (((1,), (0,)), ((), ())), preferred_element_type=f32)


def dot_nt(left, right):
    return lax.dot_general(left, right, (((1,), (1,)), ((), ())), preferred_element_type=f32)


def params_of(**extra):
    return dict(
        compiler_params=pltpu.CompilerParams(vmem_limit_bytes=VMEM_LIMIT),
        cost_estimate=pl.CostEstimate(flops=1, bytes_accessed=1, transcendentals=0),
        **extra,
    )


def whole(shape):
    rank = len(shape)
    return pl.BlockSpec(shape, lambda *args: (0,) * rank)


def shape_of(shape, dtype):
    return jax.ShapeDtypeStruct(shape, dtype)


def rope(vals, tab_ref):
    return (
        vals * tab_ref[0]
        + pltpu.roll(vals, LANES - ROT // 2, 1) * tab_ref[1]
        + pltpu.roll(vals, ROT // 2, 1) * tab_ref[2]
    )


def unrope(vals, tab_ref):
    return (
        vals * tab_ref[0]
        - pltpu.roll(vals, LANES - ROT // 2, 1) * tab_ref[1]
        - pltpu.roll(vals, ROT // 2, 1) * tab_ref[2]
    )


def normalized(hidden):
    row_mean = jnp.mean(hidden, axis=-1, keepdims=True)
    centered = hidden - row_mean
    spread = jnp.mean(centered * centered, axis=-1, keepdims=True)
    scale = lax.rsqrt(spread + NORM_EPS)
    return centered * scale, scale


def start_all(tiles, steps):
    @pl.when(pl.program_id(0) == 0)
    def _():
        for t in range(steps):
            for copy in tiles(t):
                copy.start()


def qkv_kernel(half, wsh_ref, given_ref, got_ref, vec_ref, bias_ref, tab_ref, *rest):
    w_own, w_oth, out_ref, x_ref, na_own, na_oth, nm_own, nm_oth, buf, sems = rest
    part = pl.program_id(0)
    dim = 2 * half

    def tiles(t):
        cols = pl.ds(pl.multiple_of(t * dim, dim), dim)
        return [
            pltpu.make_async_copy(weight.at[:, cols], buf.at[t, side], sems.at[t, side])
            for side, weight in enumerate((w_own, w_oth))
        ]

    start_all(tiles, 3)

    @pl.when(part == 0)
    def _():
        x = jnp.where(wsh_ref[1] == 1, given_ref[...], got_ref[...])
        x_ref[...] = x
        xhat, _ = normalized(x.astype(f32))
        na = (xhat * vec_ref[0:1] + vec_ref[1:2]).astype(bf16)
        nm = (xhat * vec_ref[2:3] + vec_ref[3:4]).astype(bf16)
        first = wsh_ref[0] == 0
        na_own[...] = jnp.where(first, na[:, :half], na[:, half:])
        na_oth[...] = jnp.where(first, na[:, half:], na[:, :half])
        nm_own[...] = jnp.where(first, nm[:, :half], nm[:, half:])
        nm_oth[...] = jnp.where(first, nm[:, half:], nm[:, :half])

    for copy in tiles(part):
        copy.wait()

    def finish(turn):
        for at in range(0, dim, 2 * LANES):
            cols = pl.ds(at, 2 * LANES)
            res = (
                dot_nn(na_own[...], buf[part, 0, :, cols])
                + dot_nn(na_oth[...], buf[part, 1, :, cols])
                + bias_ref[:, cols]
            )
            for pair in range(2):
                vals = res[:, pair * LANES : (pair + 1) * LANES]
                if turn:
                    vals = rope(vals, tab_ref)
                out_ref[at // LANES + pair] = vals.astype(bf16)

    @pl.when(part < 2)
    def _():
        finish(True)

    @pl.when(part == 2)
    def _():
        finish(False)


def layer_of(shape, index):
    return pl.BlockSpec((pl.squeezed,) + shape, lambda *args: (index, 0, 0))


ANYWHERE = pl.BlockSpec(memory_space=pl.ANY)


def qkv_call(given, index, got, vecs, qkv_b, tab, w_own, w_oth, wsh):
    rows, dim = given.shape[1:]
    half = w_own.shape[0]
    pairs = dim // LANES
    got_spec = whole((rows, dim))
    if got is None:
        got, got_spec = given, layer_of((rows, dim), index)
    return pl.pallas_call(
        functools.partial(qkv_kernel, half),
        grid_spec=pltpu.PrefetchScalarGridSpec(
            num_scalar_prefetch=1,
            grid=(3,),
            in_specs=[
                layer_of((rows, dim), index),
                got_spec,
                whole(vecs.shape),
                pl.BlockSpec((1, dim), lambda j, s: (0, j)),
                whole(tab.shape),
                ANYWHERE,
                ANYWHERE,
            ],
            out_specs=[
                pl.BlockSpec((pairs, pl.squeezed, rows, LANES), lambda j, s: (0, j, 0, 0)),
                whole((rows, dim)),
            ]
            + [whole((rows, half))] * 4,
            scratch_shapes=[
                pltpu.VMEM((3, 2, half, dim), bf16),
                pltpu.SemaphoreType.DMA((3, 2)),
            ],
        ),
        out_shape=[shape_of((pairs, 3, rows, LANES), bf16), shape_of((rows, dim), bf16)]
        + [shape_of((rows, half), bf16)] * 4,
        name="qkv_proj",
        **params_of(),
    )(wsh, given, got, vecs, qkv_b, tab, w_own, w_oth)


MLP_TILE = 1024
MLP_PIECE = 512


def ff_tiles(wsh_ref, up_own, up_oth, dn_own, dn_oth, up_buf, dn_buf, sems):
    tile = dn_buf.shape[1]
    own = dn_own.shape[0] // tile

    def tiles(t):
        cols = pl.ds(pl.multiple_of(((wsh_ref[0] * own + t) % (2 * own)) * tile, tile), tile)
        copies = [
            pltpu.make_async_copy(weight.at[:, cols], up_buf.at[t, side], sems.at[t, side])
            for side, weight in enumerate((up_own, up_oth))
        ]
        held = not isinstance(t, int) or t < own
        down = dn_own if held else dn_oth
        rows = pl.ds((t % own) * tile, tile)
        return copies + [pltpu.make_async_copy(down.at[rows], dn_buf.at[t], sems.at[t, 2])]

    return tiles


def mlp_kernel(own_tiles, save, wsh_ref, nm_own, nm_oth, up_b, down_b, *refs):
    weights, outs = refs[:4], refs[4:]
    if save:
        out_ref, slope_ref, gt_own, gt_oth, up_buf, dn_buf, sems = outs
    else:
        out_ref, up_buf, dn_buf, sems = outs
    step = pl.program_id(0)
    tiles = ff_tiles(wsh_ref, *weights, up_buf, dn_buf, sems)
    start_all(tiles, 2 * own_tiles)

    @pl.when(step == 0)
    def _():
        out_ref[...] = jnp.broadcast_to(down_b[...], out_ref.shape)

    for copy in tiles(step):
        copy.wait()
    for at in range(0, dn_buf.shape[1], MLP_PIECE):
        piece = pl.ds(at, MLP_PIECE)
        pre = (
            dot_nn(nm_own[...], up_buf[step, 0, :, piece])
            + dot_nn(nm_oth[...], up_buf[step, 1, :, piece])
            + up_b[:, piece]
        )
        gate = 0.5 + 0.5 * lax.erf(pre * INV_SQRT2)
        act = (pre * gate).astype(bf16)
        if save:
            slope_ref[:, piece] = (
                gate + pre * (INV_SQRT_2PI * jnp.exp(-0.5 * pre * pre))
            ).astype(bf16)
            turned = act.T

            @pl.when(step < own_tiles)
            def _():
                gt_own[piece] = turned

            @pl.when(step >= own_tiles)
            def _():
                gt_oth[piece] = turned

        out_ref[...] += dot_nn(act, dn_buf[step, piece])


def mlp_scratch(half, dim, steps):
    return [
        pltpu.VMEM((steps, 2, half, MLP_TILE), bf16),
        pltpu.VMEM((steps, MLP_TILE, dim), bf16),
        pltpu.SemaphoreType.DMA((steps, 3)),
    ]


def mlp_call(nm_own, nm_oth, up_b, down_b, up_own, up_oth, dn_own, dn_oth, wsh, save):
    rows, half = nm_own.shape
    dim = dn_own.shape[1]
    ff = up_own.shape[1]
    own = dn_own.shape[0] // MLP_TILE
    by_ff = lambda j, s: (0, (s[0] * own + j) % (2 * own))
    out_specs = [whole((rows, dim))]
    out_shape = [shape_of((rows, dim), f32)]
    if save:
        out_specs += [
            pl.BlockSpec((rows, MLP_TILE), by_ff),
            pl.BlockSpec((MLP_TILE, rows), lambda j, s: (jnp.minimum(j, own - 1), 0)),
            pl.BlockSpec((MLP_TILE, rows), lambda j, s: (jnp.maximum(j - own, 0), 0)),
        ]
        out_shape += [shape_of((rows, ff), bf16)] + [shape_of((ff // 2, rows), bf16)] * 2
    return pl.pallas_call(
        functools.partial(mlp_kernel, own, save),
        grid_spec=pltpu.PrefetchScalarGridSpec(
            num_scalar_prefetch=1,
            grid=(2 * own,),
            in_specs=[whole((rows, half))] * 2
            + [pl.BlockSpec((1, MLP_TILE), by_ff), whole((1, dim))]
            + [ANYWHERE] * 4,
            out_specs=out_specs,
            scratch_shapes=mlp_scratch(half, dim, 2 * own),
        ),
        out_shape=out_shape,
        name="mlp_forward",
        **params_of(),
    )(wsh, nm_own, nm_oth, up_b, down_b, up_own, up_oth, dn_own, dn_oth)


def mlp_back_kernel(own_tiles, half, wsh_ref, dy_ref, slope_ref, *refs):
    weights = refs[:4]
    du_ref, dnm_ref, acc_own, acc_oth, up_buf, dn_buf, sems = refs[4:]
    step = pl.program_id(0)
    tiles = ff_tiles(wsh_ref, *weights, up_buf, dn_buf, sems)
    start_all(tiles, 2 * own_tiles)

    @pl.when(step == 0)
    def _():
        acc_own[...] = jnp.zeros(acc_own.shape, f32)
        acc_oth[...] = jnp.zeros(acc_oth.shape, f32)

    for copy in tiles(step):
        copy.wait()
    for at in range(0, dn_buf.shape[1], MLP_PIECE):
        piece = pl.ds(at, MLP_PIECE)
        dact = dot_nt(dy_ref[...], dn_buf[step, piece])
        du = (dact * slope_ref[:, piece].astype(f32)).astype(bf16)
        du_ref[:, piece] = du
        acc_own[...] += dot_nt(du, up_buf[step, 0, :, piece])
        acc_oth[...] += dot_nt(du, up_buf[step, 1, :, piece])

    @pl.when(step == 2 * own_tiles - 1)
    def _():
        first = wsh_ref[0] == 0
        dnm_ref[:, :half] = jnp.where(first, acc_own[...], acc_oth[...])
        dnm_ref[:, half:] = jnp.where(first, acc_oth[...], acc_own[...])


def mlp_back_call(dy, slope, up_own, up_oth, dn_own, dn_oth, wsh):
    rows, dim = dy.shape
    half = up_own.shape[0]
    ff = slope.shape[1]
    own = dn_own.shape[0] // MLP_TILE
    by_ff = lambda j, s: (0, (s[0] * own + j) % (2 * own))
    return pl.pallas_call(
        functools.partial(mlp_back_kernel, own, half),
        grid_spec=pltpu.PrefetchScalarGridSpec(
            num_scalar_prefetch=1,
            grid=(2 * own,),
            in_specs=[whole((rows, dim)), pl.BlockSpec((rows, MLP_TILE), by_ff)] + [ANYWHERE] * 4,
            out_specs=[pl.BlockSpec((rows, MLP_TILE), by_ff), whole((rows, dim))],
            scratch_shapes=[pltpu.VMEM((rows, half), f32), pltpu.VMEM((rows, half), f32)]
            + mlp_scratch(half, dim, 2 * own),
        ),
        out_shape=[shape_of((rows, ff), bf16), shape_of((rows, dim), f32)],
        name="mlp_backward",
        **params_of(),
    )(wsh, dy, slope, up_own, up_oth, dn_own, dn_oth)


def sort_in(loc_ref, ref, dst, half_rows, part=None):
    for block in range(dst.shape[0] // half_rows):
        place = loc_ref[block]
        rows = pl.ds(pl.multiple_of((place % 2) * half_rows, half_rows), half_rows)
        if part is None:
            vals = ref[place // 2, rows, :]
        else:
            vals = ref[place // 2, part, rows, :]
        dst[block * half_rows : (block + 1) * half_rows] = vals


def sort_out(loc_ref, vals, ref, half_rows, part=None):
    for block in range(vals.shape[0] // half_rows):
        place = loc_ref[block]
        rows = pl.ds(pl.multiple_of((place % 2) * half_rows, half_rows), half_rows)
        piece = vals[block * half_rows : (block + 1) * half_rows]
        if part is None:
            ref[place // 2, rows, :] = piece
        else:
            ref[place // 2, part, rows, :] = piece


def head_of(vals, head):
    lane = lax.broadcasted_iota(jnp.int32, vals.shape, 1)
    return jnp.where(lane // (LANES // 2) == head, vals, jnp.zeros_like(vals))


def scores_of(keys, queries, scale, diagonal):
    scores = dot_nt(keys, queries) * scale
    if diagonal:
        key_at = lax.broadcasted_iota(jnp.int32, scores.shape, 0)
        query_at = lax.broadcasted_iota(jnp.int32, scores.shape, 1)
        scores = jnp.where(key_at <= query_at, scores, MASKED_SCORE)
    return scores


def attend_kernel(tile, loc_ref, qkv_ref, o_ref, lse_ref, q_s, k_s, v_s, vt_s, o_s):
    half_rows = qkv_ref.shape[2] // 2
    seq = q_s.shape[0]
    head_size = LANES // 2
    scale = head_size**-0.5
    sort_in(loc_ref, qkv_ref, q_s, half_rows, 0)
    sort_in(loc_ref, qkv_ref, k_s, half_rows, 1)
    sort_in(loc_ref, qkv_ref, v_s, half_rows, 2)
    vt_s[...] = v_s[...].T
    for t in range(seq // tile):
        rows = slice(t * tile, (t + 1) * tile)
        queries = q_s[rows]
        outs = []
        for head in range(2):
            picked = head_of(queries, head)
            parts = [
                scores_of(k_s[i * tile : (i + 1) * tile], picked, scale, i == t)
                for i in range(t + 1)
            ]
            top = functools.reduce(
                jnp.maximum, [jnp.max(p, axis=0, keepdims=True) for p in parts]
            )
            parts = [jnp.exp(p - top) for p in parts]
            total = sum(jnp.sum(p, axis=0, keepdims=True) for p in parts)
            lse_ref[head : head + 1, rows] = top + jnp.log(total)
            inverse = 1.0 / total
            acc = None
            for i, p in enumerate(parts):
                term = dot_nn(
                    vt_s[head * head_size : (head + 1) * head_size, i * tile : (i + 1) * tile],
                    (p * inverse).astype(bf16),
                )
                acc = term if acc is None else acc + term
            outs.append(acc)
        o_s[rows] = jnp.concatenate(outs, axis=0).T.astype(bf16)
    sort_out(loc_ref, o_s, o_ref, half_rows)


def attend_call(qkv, loc):
    count, _, rows, _ = qkv.shape
    seq = count * rows
    return pl.pallas_call(
        functools.partial(attend_kernel, 256),
        grid_spec=pltpu.PrefetchScalarGridSpec(
            num_scalar_prefetch=1,
            grid=(1,),
            in_specs=[whole(qkv.shape)],
            out_specs=[whole((count, rows, LANES)), whole((2, seq))],
            scratch_shapes=[
                pltpu.VMEM((seq, LANES), bf16),
                pltpu.VMEM((seq, LANES), bf16),
                pltpu.VMEM((seq, LANES), bf16),
                pltpu.VMEM((LANES, seq), bf16),
                pltpu.VMEM((seq, LANES), bf16),
            ],
        ),
        out_shape=[shape_of((count, rows, LANES), bf16), shape_of((2, seq), f32)],
        name="attention",
        **params_of(),
    )(loc, qkv)


def attend_back_kernel(
    tile, loc_ref, qkv_ref, da_ref, lse_ref, out_ref, q_s, k_s, v_s, da_s, kt_s, dq_s, dk_s, dv_s
):
    half_rows = qkv_ref.shape[2] // 2
    seq = q_s.shape[0]
    head_size = LANES // 2
    scale = head_size**-0.5
    sort_in(loc_ref, qkv_ref, q_s, half_rows, 0)
    sort_in(loc_ref, qkv_ref, k_s, half_rows, 1)
    sort_in(loc_ref, qkv_ref, v_s, half_rows, 2)
    sort_in(loc_ref, da_ref, da_s, half_rows)
    kt_s[...] = k_s[...].T
    dk_s[...] = jnp.zeros(dk_s.shape, f32)
    dv_s[...] = jnp.zeros(dv_s.shape, f32)
    for t in range(seq // tile):
        rows = slice(t * tile, (t + 1) * tile)
        outs = []
        for head in range(2):
            queries = head_of(q_s[rows], head)
            grads = head_of(da_s[rows], head)
            lse = lse_ref[head : head + 1, rows]
            probs, dprobs, row_dot = [], [], 0.0
            for i in range(t + 1):
                keys = slice(i * tile, (i + 1) * tile)
                p = jnp.exp(scores_of(k_s[keys], queries, scale, i == t) - lse)
                dp = dot_nt(v_s[keys], grads)
                row_dot = row_dot + jnp.sum(p * dp, axis=0, keepdims=True)
                dv_s[keys] += dot_nn(p.astype(bf16), grads)
                probs.append(p)
                dprobs.append(dp)
            acc = None
            for i in range(t + 1):
                keys = slice(i * tile, (i + 1) * tile)
                ds = (probs[i] * (dprobs[i] - row_dot) * scale).astype(bf16)
                dk_s[keys] += dot_nn(ds, queries)
                term = dot_nn(kt_s[head * head_size : (head + 1) * head_size, keys], ds)
                acc = term if acc is None else acc + term
            outs.append(acc)
        dq_s[rows] = jnp.concatenate(outs, axis=0).T.astype(bf16)
    sort_out(loc_ref, dq_s, out_ref, half_rows, 0)
    k_s[...] = dk_s[...].astype(bf16)
    v_s[...] = dv_s[...].astype(bf16)
    sort_out(loc_ref, k_s, out_ref, half_rows, 1)
    sort_out(loc_ref, v_s, out_ref, half_rows, 2)


def attend_back_call(qkv, da, lse, loc):
    count, _, rows, _ = qkv.shape
    seq = count * rows
    return pl.pallas_call(
        functools.partial(attend_back_kernel, 256),
        grid_spec=pltpu.PrefetchScalarGridSpec(
            num_scalar_prefetch=1,
            grid=(1,),
            in_specs=[whole(qkv.shape), whole(da.shape), whole(lse.shape)],
            out_specs=whole(qkv.shape),
            scratch_shapes=[
                pltpu.VMEM((seq, LANES), bf16),
                pltpu.VMEM((seq, LANES), bf16),
                pltpu.VMEM((seq, LANES), bf16),
                pltpu.VMEM((seq, LANES), bf16),
                pltpu.VMEM((LANES, seq), bf16),
                pltpu.VMEM((seq, LANES), bf16),
                pltpu.VMEM((seq, LANES), f32),
                pltpu.VMEM((seq, LANES), f32),
            ],
        ),
        out_shape=shape_of(qkv.shape, bf16),
        name="attention_backward",
        **params_of(),
    )(loc, qkv, da, lse)


def by_head(parts):
    pairs, rows, lanes = parts.shape
    return jnp.transpose(parts, (1, 0, 2)).reshape(rows, HEADS, pairs * lanes // HEADS)


def by_pair(heads):
    rows = heads.shape[0]
    return jnp.transpose(heads.reshape(rows, -1, LANES), (1, 0, 2))


def wide_scores(queries, keys, query_pos, key_pos):
    raw = jnp.einsum("qhd,khd->hqk", queries, keys, preferred_element_type=f32)
    allowed = (query_pos[:, None] >= key_pos[None, :])[None]
    return jnp.where(allowed, raw * queries.shape[-1] ** (-0.5), MASKED_SCORE)


def key_blocks(arrays, rows):
    return tuple(a.reshape((a.shape[0] // rows, rows) + a.shape[1:]) for a in arrays)


def wide_attend(qkv, query_pos, key_pos):
    queries = by_head(qkv[:, 0])
    keys = lax.all_gather(by_head(qkv[:, 1]), "ctx", axis=0, tiled=True)
    values = lax.all_gather(by_head(qkv[:, 2]), "ctx", axis=0, tiled=True)
    block = min(512, keys.shape[0])
    split = key_blocks((keys, values, key_pos), block)
    rows, _, head_size = queries.shape

    def max_step(carry, block_in):
        top, total = carry
        scores = wide_scores(queries, block_in[0], query_pos, block_in[2])
        new_top = jnp.maximum(top, jnp.max(scores, axis=-1))
        part = jnp.sum(jnp.exp(scores - new_top[..., None]), axis=-1)
        return ((new_top, total * jnp.exp(top - new_top) + part), None)

    start = (jnp.full((HEADS, rows), MASKED_SCORE, f32), jnp.zeros((HEADS, rows), f32))
    (top, total), _ = lax.scan(max_step, start, split)
    lse = top + jnp.log(total)

    def value_step(running, block_in):
        scores = wide_scores(queries, block_in[0], query_pos, block_in[2])
        probs = jnp.exp(scores - lse[..., None]).astype(bf16)
        term = jnp.einsum("hqk,khd->qhd", probs, block_in[1], preferred_element_type=f32)
        return (running + term, None)

    attended, _ = lax.scan(value_step, jnp.zeros((rows, HEADS, head_size), f32), split)
    return by_pair(attended.astype(bf16)), (queries, keys, values, lse)


def wide_attend_back(kept, da, query_pos, key_pos):
    queries, keys, values, lse = kept
    grads = by_head(da)
    block = min(512, keys.shape[0])
    split = key_blocks((keys, values, key_pos), block)
    scale = queries.shape[-1] ** (-0.5)

    def pieces(block_in):
        scores = wide_scores(queries, block_in[0], query_pos, block_in[2])
        probs = jnp.exp(scores - lse[..., None])
        dprobs = jnp.einsum("qhd,khd->hqk", grads, block_in[1], preferred_element_type=f32)
        return probs, dprobs

    def dot_step(running, block_in):
        probs, dprobs = pieces(block_in)
        return (running + jnp.sum(probs * dprobs, axis=-1), None)

    row_dot, _ = lax.scan(dot_step, jnp.zeros(lse.shape, f32), split)

    def key_step(running, block_in):
        probs, dprobs = pieces(block_in)
        ds = (scale * probs * (dprobs - row_dot[..., None])).astype(bf16)
        running = running + jnp.einsum("hqk,khd->qhd", ds, block_in[0], preferred_element_type=f32)
        dk = jnp.einsum("hqk,qhd->khd", ds, queries, preferred_element_type=f32)
        dv = jnp.einsum("hqk,qhd->khd", probs.astype(bf16), grads, preferred_element_type=f32)
        return (running, (dk.astype(bf16), dv.astype(bf16)))

    dq, (dk, dv) = lax.scan(key_step, jnp.zeros(queries.shape, f32), split)
    dk, dv = (
        lax.psum_scatter(part.reshape(keys.shape), "ctx", scatter_dimension=0, tiled=True)
        for part in (dk, dv)
    )
    return jnp.stack([by_pair(dq.astype(bf16)), by_pair(dk), by_pair(dv)], axis=1)


def lanes_of(ref):
    return jnp.concatenate([ref[i] for i in range(ref.shape[0])], axis=1)


def proj_kernel(half, wsh_ref, a_ref, x_ref, mlp_ref, bias_ref, p_own, p_oth, y_ref, a_own, a_oth):
    first = wsh_ref[0] == 0
    a = lanes_of(a_ref)
    own = jnp.where(first, a[:, :half], a[:, half:])
    oth = jnp.where(first, a[:, half:], a[:, :half])
    a_own[...] = own
    a_oth[...] = oth
    attn = dot_nn(own, p_own[...]) + dot_nn(oth, p_oth[...]) + bias_ref[...]
    y_ref[...] = (x_ref[...].astype(f32) + attn + mlp_ref[...]).astype(bf16)


def proj_call(a, x, mlp, bias, p_own, p_oth, wsh):
    rows, dim = x.shape
    half = p_own.shape[0]
    return pl.pallas_call(
        functools.partial(proj_kernel, half),
        grid_spec=pltpu.PrefetchScalarGridSpec(
            num_scalar_prefetch=1,
            grid=(1,),
            in_specs=[
                whole(a.shape),
                whole(x.shape),
                whole((rows, dim)),
                whole(bias.shape),
                whole(p_own.shape),
                whole(p_oth.shape),
            ],
            out_specs=[whole((rows, dim)), whole((rows, half)), whole((rows, half))],
        ),
        out_shape=[shape_of((rows, dim), bf16)] + [shape_of((rows, half), bf16)] * 2,
        name="attn_out",
        **params_of(),
    )(wsh, a, x, mlp, bias, p_own, p_oth)


def da_kernel(wsh_ref, given_ref, got_ref, p_own, p_oth, out_ref, dy_ref):
    dy = jnp.where(wsh_ref[1] == 1, got_ref[...], given_ref[...])
    dy_ref[...] = dy
    wsh = wsh_ref[0]
    count = out_ref.shape[0] // 2
    for place, weight in ((wsh * count, p_own), ((1 - wsh) * count, p_oth)):
        part = dot_nt(dy, weight[...]).astype(bf16)
        for i in range(count):
            out_ref[place + i] = part[:, i * LANES : (i + 1) * LANES]


def da_call(given, index, got, p_own, p_oth, wsh):
    rows, dim = given.shape[1:]
    pairs = dim // LANES
    got_spec = whole((rows, dim))
    if got is None:
        got, got_spec = given, layer_of((rows, dim), index)
    return pl.pallas_call(
        da_kernel,
        grid_spec=pltpu.PrefetchScalarGridSpec(
            num_scalar_prefetch=1,
            grid=(1,),
            in_specs=[layer_of((rows, dim), index), got_spec]
            + [whole(p_own.shape), whole(p_oth.shape)],
            out_specs=[whole((pairs, rows, LANES)), whole((rows, dim))],
        ),
        out_shape=[shape_of((pairs, rows, LANES), bf16), shape_of((rows, dim), bf16)],
        name="attn_out_backward",
        **params_of(),
    )(wsh, given, got, p_own, p_oth)


DX_ROWS = 256


def dx_kernel(half, wsh_ref, dqkv_ref, tab_ref, x_ref, dy_ref, dnm_ref, vec_ref, *rest):
    w_own, w_oth, back_ref, dx_ref, sums_ref, grad_s, buf, sems = rest
    pairs = dqkv_ref.shape[0]
    copies = []
    for side, weight in enumerate((w_own, w_oth)):
        for t in range(half // DX_ROWS):
            copies.append(
                pltpu.make_async_copy(
                    weight.at[pl.ds(t * DX_ROWS, DX_ROWS)], buf.at[side, t], sems.at[side, t]
                )
            )
    for copy in copies:
        copy.start()
    for part in range(3):
        for pair in range(pairs):
            vals = dqkv_ref[pair, part]
            if part < 2:
                vals = unrope(vals.astype(f32), tab_ref).astype(bf16)
            back_ref[pair, part] = vals
            grad_s[:, pl.ds((part * pairs + pair) * LANES, LANES)] = vals
    halves = []
    for side in range(2):
        cols = []
        for t in range(half // DX_ROWS):
            copies[side * (half // DX_ROWS) + t].wait()
            cols.append(dot_nt(grad_s[...], buf[side, t]))
        halves.append(jnp.concatenate(cols, axis=1))
    first = wsh_ref[0] == 0
    own, oth = halves
    dna = jnp.concatenate([jnp.where(first, own, oth), jnp.where(first, oth, own)], axis=1)
    dnm = dnm_ref[...]
    xhat, scale = normalized(x_ref[...].astype(f32))
    grad = dna * vec_ref[0:1] + dnm * vec_ref[2:3]
    inner = (
        grad
        - jnp.mean(grad, axis=-1, keepdims=True)
        - xhat * jnp.mean(grad * xhat, axis=-1, keepdims=True)
    )
    dx_ref[...] = (dy_ref[...].astype(f32) + scale * inner).astype(bf16)
    sums_ref[0:1] = jnp.sum(dna * xhat, axis=0, keepdims=True)
    sums_ref[1:2] = jnp.sum(dna, axis=0, keepdims=True)
    sums_ref[2:3] = jnp.sum(dnm * xhat, axis=0, keepdims=True)
    sums_ref[3:4] = jnp.sum(dnm, axis=0, keepdims=True)


def dx_call(dqkv, tab, x, dy, dnm, vecs, w_own, w_oth, wsh):
    rows, dim = x.shape
    half = w_own.shape[0]
    return pl.pallas_call(
        functools.partial(dx_kernel, half),
        grid_spec=pltpu.PrefetchScalarGridSpec(
            num_scalar_prefetch=1,
            grid=(1,),
            in_specs=[
                whole(dqkv.shape),
                whole(tab.shape),
                whole(x.shape),
                whole(dy.shape),
                whole(dnm.shape),
                whole(vecs.shape),
                ANYWHERE,
                ANYWHERE,
            ],
            out_specs=[whole(dqkv.shape), whole((rows, dim)), whole((4, dim))],
            scratch_shapes=[
                pltpu.VMEM((rows, 3 * dim), bf16),
                pltpu.VMEM((2, half // DX_ROWS, DX_ROWS, 3 * dim), bf16),
                pltpu.SemaphoreType.DMA((2, half // DX_ROWS)),
            ],
        ),
        out_shape=[
            shape_of(dqkv.shape, bf16),
            shape_of((rows, dim), bf16),
            shape_of((4, dim), f32),
        ],
        name="section_input_grad",
        **params_of(),
    )(wsh, dqkv, tab, x, dy, dnm, vecs, w_own, w_oth)


def stack_rows(refs, cols=slice(None)):
    return jnp.concatenate([ref[:, cols] for ref in refs], axis=0)


def down_grad_kernel(micros, *refs):
    gt_refs, dy_refs = refs[:micros], refs[micros : 2 * micros]
    out_ref, sum_ref, dy_s = refs[2 * micros :]

    @pl.when(pl.program_id(0) == 0)
    def _():
        dy = stack_rows(dy_refs)
        dy_s[...] = dy
        sum_ref[...] = jnp.sum(dy.astype(f32), axis=0, keepdims=True)

    left = jnp.concatenate([ref[...] for ref in gt_refs], axis=1)
    out_ref[...] = dot_nn(left, dy_s[...]).astype(bf16)


def down_grad_call(gt_list, dy_list):
    ff_rows, rows = gt_list[0].shape
    dim = dy_list[0].shape[1]
    micros = len(dy_list)
    tile = 512
    return pl.pallas_call(
        functools.partial(down_grad_kernel, micros),
        grid=(ff_rows // tile,),
        in_specs=[pl.BlockSpec((tile, rows), lambda j: (j, 0))] * micros
        + [whole((rows, dim))] * micros,
        out_specs=[pl.BlockSpec((tile, dim), lambda j: (j, 0)), whole((1, dim))],
        out_shape=[shape_of((ff_rows, dim), bf16), shape_of((1, dim), f32)],
        scratch_shapes=[pltpu.VMEM((micros * rows, dim), bf16)],
        name="down_grad",
        **params_of(),
    )(*gt_list, *dy_list)


def up_grad_kernel(micros, *refs):
    x_refs, du_refs = refs[:micros], refs[micros : 2 * micros]
    out_ref, sum_ref, xt_s = refs[2 * micros :]

    @pl.when(pl.program_id(0) == 0)
    def _():
        xt_s[...] = stack_rows(x_refs).T

    du = stack_rows(du_refs)
    sum_ref[...] = jnp.sum(du.astype(f32), axis=0, keepdims=True)
    out_ref[...] = dot_nn(xt_s[...], du).astype(bf16)


def up_grad_call(x_list, du_list):
    rows, half = x_list[0].shape
    ff = du_list[0].shape[1]
    micros = len(x_list)
    tile = 1024
    return pl.pallas_call(
        functools.partial(up_grad_kernel, micros),
        grid=(ff // tile,),
        in_specs=[whole((rows, half))] * micros
        + [pl.BlockSpec((rows, tile), lambda j: (0, j))] * micros,
        out_specs=[
            pl.BlockSpec((half, tile), lambda j: (0, j)),
            pl.BlockSpec((1, tile), lambda j: (0, j)),
        ],
        out_shape=[shape_of((half, ff), bf16), shape_of((1, ff), f32)],
        scratch_shapes=[pltpu.VMEM((half, micros * rows), bf16)],
        name="up_grad",
        **params_of(),
    )(*x_list, *du_list)


def attn_grad_kernel(micros, *refs):
    x_refs, a_refs, d_refs, dy_refs = (refs[i * micros : (i + 1) * micros] for i in range(4))
    out_ref, sum_ref, xt_s = refs[4 * micros :]
    part = pl.program_id(0)

    def finish(dy):
        sum_ref[...] = jnp.sum(dy.astype(f32), axis=0, keepdims=True)
        out_ref[...] = dot_nn(xt_s[...], dy).astype(bf16)

    @pl.when(part == 0)
    def _():
        xt_s[...] = stack_rows(x_refs).T

    @pl.when(part < 3)
    def _():
        finish(jnp.concatenate([lanes_of(ref) for ref in d_refs], axis=0))

    @pl.when(part == 3)
    def _():
        xt_s[...] = stack_rows(a_refs).T
        finish(stack_rows(dy_refs))


def attn_grad_call(x_list, a_list, d_list, dy_list):
    rows, half = x_list[0].shape
    pairs = d_list[0].shape[0]
    dim = pairs * LANES
    micros = len(x_list)
    d_spec = pl.BlockSpec(
        (pairs, pl.squeezed, rows, LANES), lambda j: (0, jnp.minimum(j, 2), 0, 0)
    )
    return pl.pallas_call(
        functools.partial(attn_grad_kernel, micros),
        grid=(4,),
        in_specs=[whole((rows, half))] * (2 * micros)
        + [d_spec] * micros
        + [whole((rows, dim))] * micros,
        out_specs=[
            pl.BlockSpec((half, dim), lambda j: (0, j)),
            pl.BlockSpec((1, dim), lambda j: (0, j)),
        ],
        out_shape=[shape_of((half, 4 * dim), bf16), shape_of((1, 4 * dim), f32)],
        scratch_shapes=[pltpu.VMEM((half, micros * rows), bf16)],
        name="attn_grad",
        **params_of(),
    )(*x_list, *a_list, *d_list, *dy_list)


def ring_of(count):
    return list(range(0, count, 2)) + list(range(count - 1, 0, -2))


def ring_place(axis):
    count = lax.axis_size(axis)
    me = lax.axis_index(axis)
    return jnp.where(me % 2 == 0, me // 2, count - (me + 1) // 2)


def ring_shift(vals, axis, by):
    order = ring_of(lax.axis_size(axis))
    count = len(order)
    pairs = [(order[i], order[(i + by) % count]) for i in range(count)]
    return lax.ppermute(vals, axis, pairs)


def low_sum(*terms):
    total = terms[0].astype(f32)
    for term in terms[1:]:
        total = total + term.astype(f32)
    return total.astype(bf16)


def tied(token, *vals):
    return lax.optimization_barrier((token,) + vals)[1:]


def ring_sum(own, widths, axis):
    count = lax.axis_size(axis)
    place = ring_place(axis)
    half = count // 2
    full_rows, cols = own.shape
    rows = full_rows // count
    own = own.reshape(count, rows, cols)
    cut = rows // 2
    starts = [sum(widths[:i]) for i in range(len(widths))]

    def index(k):
        return (place + (k + count)) % count

    def take(k):
        return lax.dynamic_index_in_dim(own, index(k), 0, keepdims=False)

    def put(totals, piece, k, lo=0):
        for i, (start, width) in enumerate(zip(starts, widths)):
            part = piece[:, start : start + width].astype(f32)[None]
            totals[i] = lax.dynamic_update_slice(totals[i], part, (index(k), lo, 0))

    token = yield None
    (far,) = tied(token, take(half))
    ahead = ring_shift(far[:cut], axis, 1)
    behind = ring_shift(far[cut:], axis, -1)
    token = yield far
    for k in range(half - 1, 0, -1):
        ahead, behind = tied(token, ahead, behind)
        mine_a, mine_b = take(k), take(-k)
        if k == half - 1:
            ahead = jnp.concatenate([low_sum(mine_a[:cut], ahead), mine_a[cut:]], axis=0)
            behind = jnp.concatenate([mine_b[:cut], low_sum(mine_b[cut:], behind)], axis=0)
        else:
            ahead, behind = low_sum(mine_a, ahead), low_sum(mine_b, behind)
        token = behind
        ahead = ring_shift(ahead, axis, 1)
        behind = ring_shift(behind, axis, -1)
        token = yield token
    ahead, behind = tied(token, ahead, behind)
    mine = low_sum(take(0), ahead, behind)
    totals = [jnp.zeros((count, rows, width), f32) for width in widths]
    put(totals, mine, 0)
    ahead = ring_shift(mine, axis, 1)
    behind = ring_shift(mine, axis, -1)
    token = yield mine
    for k in range(1, half):
        ahead, behind = tied(token, ahead, behind)
        last = k == half - 1
        next_ahead = ring_shift(ahead[:cut] if last else ahead, axis, 1)
        next_behind = ring_shift(behind[cut:] if last else behind, axis, -1)
        put(totals, ahead, -k)
        put(totals, behind, k)
        token = behind
        ahead, behind = next_ahead, next_behind
        token = yield token
    ahead, behind = tied(token, ahead, behind)
    put(totals, ahead, -half)
    put(totals, behind, half, cut)
    yield [total.reshape(full_rows, -1) for total in totals]


def butterfly_sum(vals, axis):
    count = lax.axis_size(axis)
    if count & (count - 1):
        return lax.psum(vals, axis)
    by = 1
    while by < count:
        vals = vals + lax.ppermute(vals, axis, [(i, i ^ by) for i in range(count)])
        by *= 2
    return vals


def swap(vals):
    return lax.ppermute(vals, "wsh", [(0, 1), (1, 0)])


def pass_on(vals, by):
    pairs = [(0, 1)] if by > 0 else [(1, 0)]
    return lax.ppermute(vals, "section", pairs)


def block_places(block_pair, count):
    want = jnp.arange(2 * count, dtype=jnp.int32)
    device = jnp.arange(count, dtype=jnp.int32)
    first = (block_pair[None, :] == want[:, None]).astype(jnp.int32)
    second = ((2 * count - 1 - block_pair)[None, :] == want[:, None]).astype(jnp.int32)
    return jnp.sum(first * (2 * device) + second * (2 * device + 1), axis=1)


def row_positions(block_pair, stored, tok_dev):
    count = block_pair.shape[0]
    device = stored // tok_dev
    within = stored % tok_dev
    half_rows = tok_dev // 2
    matches = device[:, None] == jnp.arange(count, dtype=jnp.int32)[None, :]
    pair_block = jnp.sum(jnp.where(matches, block_pair[None, :], 0), axis=1)
    block_idx = jnp.where(within < half_rows, pair_block, 2 * count - 1 - pair_block)
    return block_idx * half_rows + within % half_rows


def rotary_table(positions, head_size):
    half_rot = ROT // 2
    lane = jnp.arange(LANES, dtype=jnp.int32) % head_size
    inv_freq = ROPE_BASE ** (-((lane % half_rot).astype(f32) * 2.0) / ROT)
    angles = positions.astype(f32)[:, None] * inv_freq[None, :]
    cosine, sine = jnp.cos(angles), jnp.sin(angles)
    lead, second = (lane < half_rot)[None], ((lane >= half_rot) & (lane < ROT))[None]
    return jnp.stack(
        [
            jnp.where(lead | second, cosine, 1.0),
            jnp.where(lead, -sine, 0.0),
            jnp.where(second, sine, 0.0),
        ]
    )


def body(
    inputs,
    cotangent,
    block_pair,
    qkv_weight,
    qkv_bias,
    proj_weight,
    proj_bias,
    up_weight,
    up_bias,
    down_weight,
    down_bias,
    attn_gain,
    attn_shift,
    mlp_gain,
    mlp_shift,
):
    first_section = lax.axis_index("section") == 0
    count = lax.axis_size("ctx")
    micros, _, tok_dev, dim = inputs.shape
    head_size = dim // HEADS
    half = dim // 2
    my_half = lax.axis_index("wsh")
    wsh = jnp.stack([my_half.astype(jnp.int32), first_section.astype(jnp.int32)])
    one_pair_each = count == dim // LANES

    wq, wp, wu, wd = (w[0] for w in (qkv_weight, proj_weight, up_weight, down_weight))
    small = jnp.concatenate(
        [
            v[0].reshape(-1, half)
            for v in (
                attn_gain,
                attn_shift,
                mlp_gain,
                mlp_shift,
                proj_bias,
                down_bias,
                qkv_bias,
                up_bias,
            )
        ],
        axis=0,
    )
    small_oth = swap(small)
    wq_oth = swap(wq)
    first_here = lax.optimization_barrier((wq_oth, small_oth))
    wq_oth, small_oth = first_here
    wu_oth = swap(tied(wq_oth, wu)[0])
    wd_oth = swap(tied(wq_oth, wd)[0])
    wp_oth = swap(tied(wu_oth, wp)[0])
    low_part = jnp.where(my_half == 0, small, small_oth).astype(f32)
    high_part = jnp.where(my_half == 0, small_oth, small).astype(f32)
    vecs = jnp.concatenate([low_part[:6], high_part[:6]], axis=1)
    qkv_rows = 6 + qkv_bias.shape[1] // half
    proj_b, down_b = vecs[4:5], vecs[5:6]
    qkv_b = jnp.concatenate([low_part[6:qkv_rows], high_part[6:qkv_rows]], axis=0).reshape(1, -1)
    up_b = jnp.concatenate([low_part[qkv_rows:], high_part[qkv_rows:]], axis=0).reshape(1, -1)

    local_rows = lax.axis_index("ctx") * tok_dev + jnp.arange(tok_dev, dtype=jnp.int32)
    query_pos = row_positions(block_pair, local_rows, tok_dev)
    key_pos = row_positions(block_pair, jnp.arange(count * tok_dev, dtype=jnp.int32), tok_dev)
    tab = rotary_table(query_pos, head_size)
    loc = block_places(block_pair, count)

    def exchange(vals):
        return lax.all_to_all(vals, "ctx", split_axis=0, concat_axis=0, tiled=True)

    def norm_qkv(index, got):
        return qkv_call(rows_in, index, got, vecs, qkv_b, tab, wq, wq_oth, wsh)

    def mlp(made, save):
        return mlp_call(made[4], made[5], up_b, down_b, wu, wu_oth, wd, wd_oth, wsh, save)

    def mlp_back(dy, mlp_kept):
        return mlp_back_call(dy, mlp_kept[1], wu, wu_oth, wd, wd_oth, wsh)

    def out_back(index, got):
        return da_call(cot_in, index, got, wp, wp_oth, wsh)

    def to_heads(vals):
        return exchange(vals) if one_pair_each else vals

    def to_rows(vals):
        return exchange(vals) if one_pair_each else vals

    def attend(qkv):
        if one_pair_each:
            attended, lse = attend_call(qkv, loc)
            return attended, (qkv, lse)
        return wide_attend(qkv, query_pos, key_pos)

    def attend_back(kept, da):
        if one_pair_each:
            return attend_back_call(kept[0], da, kept[1], loc)
        return wide_attend_back(kept, da, query_pos, key_pos)

    def project(attended, made, mlp_out):
        return proj_call(attended, made[1], mlp_out[0], proj_b, wp, wp_oth, wsh)

    def input_grad_of(dqkv, made, dy, dnm):
        return dx_call(dqkv, tab, made[1], dy, dnm, vecs, wq, wq_oth, wsh)

    rows_in, cot_in = inputs[:, 0], cotangent[:, 0]
    made_a = norm_qkv(0, None)
    qkv_a = to_heads(made_a[0])
    mlp_a = mlp(made_a, False)
    (qkv_a,) = tied(mlp_a[0], qkv_a)
    att_a, _ = attend(qkv_a)
    att_a = to_rows(att_a)
    da_a, dy_a = out_back(0, None)
    (att_a,) = tied(dy_a, att_a)
    y_a = project(att_a, made_a, mlp_a)[0]
    da_a = to_heads(tied(y_a, da_a)[0])

    made_b = norm_qkv(1, pass_on(y_a, 1))
    qkv_b_ = to_heads(tied(da_a, made_b[0])[0])
    mlp_b = mlp(made_b, True)
    _, dnm_a = mlp_back(dy_a, mlp_b)
    (qkv_b_,) = tied(dnm_a, qkv_b_)
    att_b, kept_b = attend(qkv_b_)
    att_b = to_rows(att_b)
    (da_a,) = tied(att_b if not one_pair_each else kept_b[1], da_a)
    dqkv_a = attend_back(kept_b, da_a)
    (att_b,) = tied(dqkv_a, att_b)
    dqkv_a = to_rows(dqkv_a)
    y_b, *a_b = project(att_b, made_b, mlp_b)

    made_c = norm_qkv(0, pass_on(y_b, 1))
    (dqkv_a,) = tied(made_c[1], dqkv_a)
    qkv_c = to_heads(made_c[0])
    _, dx_a, _ = input_grad_of(dqkv_a, made_b, dy_a, dnm_a)
    got_a = pass_on(dx_a, -1)
    nm_c = tied(dx_a, made_c[4], made_c[5])
    made_c = list(made_c[:4]) + list(nm_c)
    mlp_c = mlp(made_c, True)
    (got_a,) = tied(mlp_c[0], got_a)
    da_b, dy_b = out_back(1, got_a)
    (qkv_c,) = tied(dy_b, qkv_c)
    da_b = to_heads(da_b)
    att_c, kept_c = attend(qkv_c)
    (dy_b2,) = tied(att_c, dy_b)
    du_b, dnm_b = mlp_back(dy_b2, mlp_c)
    (da_b,) = tied(dnm_b, da_b)
    dqkv_b = attend_back(kept_c, da_b)
    (att_c,) = tied(dqkv_b, att_c)
    dqkv_b = to_rows(dqkv_b)
    back_b, dx_b, sums_b = input_grad_of(dqkv_b, made_c, dy_b, dnm_b)

    da_c, dy_c = out_back(0, pass_on(dx_b, -1))
    att_c = to_rows(tied(dy_c, att_c)[0])
    dy_list = [dy_c, dy_b, swap(dy_c), swap(dy_b)]
    down_grad, dy_sum = down_grad_call(
        [mlp_b[2], mlp_c[2], swap(mlp_b[3]), swap(mlp_c[3])], dy_list
    )
    down_ring = ring_sum(down_grad, (dim,), "ctx")
    next(down_ring)
    token = down_ring.send(dy_sum)
    da_c = to_heads(tied(att_c, da_c)[0])
    (dy_c2,) = tied(token, dy_c)
    du_c, dnm_c = mlp_back(dy_c2, mlp_b)
    token = down_ring.send(dnm_c)
    (da_c,) = tied(token, da_c)
    dqkv_c = attend_back(kept_b, da_c)
    (nm_c,) = tied(dqkv_c, made_b[4])
    dqkv_c = to_rows(dqkv_c)
    up_grad, du_sum = up_grad_call(
        [nm_c, made_c[4], swap(made_b[5]), swap(made_c[5])], [du_c, du_b, swap(du_c), swap(du_b)]
    )
    up_ring = ring_sum(up_grad, (up_grad.shape[1],), "ctx")
    next(up_ring)
    token = up_ring.send(du_sum)
    token = down_ring.send(token)
    (att_c,) = tied(token, att_c)
    y_c, *a_c = project(att_c, made_c, mlp_c)
    (dqkv_c,) = tied(y_c, dqkv_c)
    back_c, dx_c, sums_c = input_grad_of(dqkv_c, made_b, dy_c, dnm_c)
    token = up_ring.send(dx_c)
    token = down_ring.send(token)
    (back_c2,) = tied(token, back_c)
    attn_grad, attn_sum = attn_grad_call(
        [made_b[2], made_c[2], swap(made_b[3]), swap(made_c[3])],
        [a_b[0], a_c[0], swap(a_b[1]), swap(a_c[1])],
        [back_c2, back_b, swap(back_c), swap(back_b)],
        dy_list,
    )
    dqkv_sum = attn_sum[:, : 3 * dim]
    attn_ring = ring_sum(attn_grad, (3 * dim, dim), "ctx")
    next(attn_ring)
    token = dqkv_sum
    steps = count + 1
    left = {down_ring: steps - 4, up_ring: steps - 2, attn_ring: steps}
    late = [attn_ring, up_ring, attn_ring, down_ring]
    results = {}

    def turn(ring, token):
        left[ring] -= 1
        made = ring.send(token)
        if left[ring] == 0:
            results[ring] = made
            return token
        return made

    at = 0
    while any(left.values()):
        ring = late[at % len(late)]
        if left[ring]:
            token = turn(ring, token)
        at += 1
    (down_grad,) = results[down_ring]
    (up_grad,) = results[up_ring]
    qkv_grad, proj_grad = results[attn_ring]

    norm_sums = sums_b + sums_c
    norm_own = lax.dynamic_slice_in_dim(norm_sums, my_half * half, half, 1)
    norm_oth = swap(lax.dynamic_slice_in_dim(norm_sums, (1 - my_half) * half, half, 1))

    def own_part(vec):
        size = vec.shape[1] // 2
        return lax.dynamic_slice_in_dim(vec, my_half * size, size, 1).reshape(-1, half)

    small_sums = jnp.concatenate(
        [norm_own + norm_oth, own_part(dy_sum), own_part(dqkv_sum), own_part(du_sum)], axis=0
    )
    small_sums = butterfly_sum(small_sums, "ctx")
    qkv_end = 5 + dqkv_sum.shape[1] // 2 // half
    dy_total = small_sums[4:5]
    pick = lambda yes, no: jnp.where(first_section, yes, no)
    layer_out = jnp.stack([pick(y_c, y_b), pick(y_b, y_c)])[None, :, None]
    input_grad = jnp.stack([pick(dx_b, dx_c), pick(dx_c, dx_b)])[None, :, None]
    return (
        layer_out,
        input_grad,
        qkv_grad[None],
        small_sums[5:qkv_end].reshape(1, -1),
        proj_grad[None],
        dy_total,
        up_grad[None],
        small_sums[qkv_end:].reshape(1, -1),
        down_grad[None],
        dy_total,
        small_sums[0:1],
        small_sums[1:2],
        small_sums[2:3],
        small_sums[3:4],
    )


def solution(mesh):
    in_specs = (
        P(None, "wsh", "ctx", None),
        P(None, "wsh", "ctx", None),
        P(),
        P("section", "wsh", None),
        P("section", "wsh"),
        P("section", "wsh", None),
        P("section", "wsh"),
        P("section", "wsh", None),
        P("section", "wsh"),
        P("section", "wsh", None),
        P("section", "wsh"),
        P("section", "wsh"),
        P("section", "wsh"),
        P("section", "wsh"),
        P("section", "wsh"),
    )
    out_specs = (
        P("section", None, "wsh", "ctx", None),
        P("section", None, "wsh", "ctx", None),
        P("section", "wsh", None),
        P("section", "wsh"),
        P("section", "wsh", None),
        P("section", "wsh"),
        P("section", "wsh", None),
        P("section", "wsh"),
        P("section", "wsh", None),
        P("section", "wsh"),
        P("section", "wsh"),
        P("section", "wsh"),
        P("section", "wsh"),
        P("section", "wsh"),
    )
    return jax.shard_map(body, mesh=mesh, in_specs=in_specs, out_specs=out_specs, check_vma=False)
```

```python
import functools

import jax
import jax.numpy as jnp
from jax import lax
from jax.experimental import pallas as pl
from jax.experimental.pallas import tpu as pltpu
from jax.sharding import PartitionSpec as P

HEADS = 16
ROT = 16
NORM_EPS = 1e-05
ROPE_BASE = 10000.0
MASKED_SCORE = -1e30
LANES = 128
VMEM_LIMIT = 60 * 1024 * 1024
INV_SQRT2 = 0.7071067811865476
INV_SQRT_2PI = 0.3989422804014327

f32 = jnp.float32
bf16 = jnp.bfloat16


def dot_nn(left, right):
    return lax.dot_general(left, right, (((1,), (0,)), ((), ())), preferred_element_type=f32)


def dot_nt(left, right):
    return lax.dot_general(left, right, (((1,), (1,)), ((), ())), preferred_element_type=f32)


def params_of(**extra):
    return dict(
        compiler_params=pltpu.CompilerParams(vmem_limit_bytes=VMEM_LIMIT),
        cost_estimate=pl.CostEstimate(flops=1, bytes_accessed=1, transcendentals=0),
        **extra,
    )


def whole(shape):
    rank = len(shape)
    return pl.BlockSpec(shape, lambda *args: (0,) * rank)


def shape_of(shape, dtype):
    return jax.ShapeDtypeStruct(shape, dtype)


def rope(vals, tab_ref):
    return (
        vals * tab_ref[0]
        + pltpu.roll(vals, LANES - ROT // 2, 1) * tab_ref[1]
        + pltpu.roll(vals, ROT // 2, 1) * tab_ref[2]
    )


def unrope(vals, tab_ref):
    return (
        vals * tab_ref[0]
        - pltpu.roll(vals, LANES - ROT // 2, 1) * tab_ref[1]
        - pltpu.roll(vals, ROT // 2, 1) * tab_ref[2]
    )


def normalized(hidden):
    row_mean = jnp.mean(hidden, axis=-1, keepdims=True)
    centered = hidden - row_mean
    spread = jnp.mean(centered * centered, axis=-1, keepdims=True)
    scale = lax.rsqrt(spread + NORM_EPS)
    return centered * scale, scale


def start_all(tiles, steps):
    @pl.when(pl.program_id(0) == 0)
    def _():
        for t in range(steps):
            for copy in tiles(t):
                copy.start()


def qkv_kernel(half, wsh_ref, given_ref, got_ref, vec_ref, bias_ref, tab_ref, *rest):
    w_own, w_oth, out_ref, x_ref, own_ref, oth_ref, buf, sems = rest
    part = pl.program_id(0)
    dim = 2 * half

    def tiles(t):
        cols = pl.ds(pl.multiple_of(t * dim, dim), dim)
        return [
            pltpu.make_async_copy(weight.at[:, cols], buf.at[t, side], sems.at[t, side])
            for side, weight in enumerate((w_own, w_oth))
        ]

    start_all(tiles, 3)

    @pl.when(part == 0)
    def _():
        x = jnp.where(wsh_ref[1] == 1, given_ref[...], got_ref[...])
        x_ref[...] = x
        xhat, _ = normalized(x.astype(f32))
        na = (xhat * vec_ref[0:1] + vec_ref[1:2]).astype(bf16)
        nm = (xhat * vec_ref[2:3] + vec_ref[3:4]).astype(bf16)
        first = wsh_ref[0] == 0
        for i, rows in enumerate((na, nm)):
            own_ref[i] = jnp.where(first, rows[:, :half], rows[:, half:])
            oth_ref[i] = jnp.where(first, rows[:, half:], rows[:, :half])

    for copy in tiles(part):
        copy.wait()

    def finish(turn):
        for at in range(0, dim, 2 * LANES):
            cols = pl.ds(at, 2 * LANES)
            res = (
                dot_nn(own_ref[0], buf[part, 0, :, cols])
                + dot_nn(oth_ref[0], buf[part, 1, :, cols])
                + bias_ref[:, cols]
            )
            for pair in range(2):
                vals = res[:, pair * LANES : (pair + 1) * LANES]
                if turn:
                    vals = rope(vals, tab_ref)
                out_ref[at // LANES + pair] = vals.astype(bf16)

    @pl.when(part < 2)
    def _():
        finish(True)

    @pl.when(part == 2)
    def _():
        finish(False)


def layer_of(shape, index):
    return pl.BlockSpec((pl.squeezed,) + shape, lambda *args: (index, 0, 0))


ANYWHERE = pl.BlockSpec(memory_space=pl.ANY)


def qkv_call(given, index, got, vecs, qkv_b, tab, w_own, w_oth, wsh):
    rows, dim = given.shape[1:]
    half = w_own.shape[0]
    pairs = dim // LANES
    got_spec = whole((rows, dim))
    if got is None:
        got, got_spec = given, layer_of((rows, dim), index)
    return pl.pallas_call(
        functools.partial(qkv_kernel, half),
        grid_spec=pltpu.PrefetchScalarGridSpec(
            num_scalar_prefetch=1,
            grid=(3,),
            in_specs=[
                layer_of((rows, dim), index),
                got_spec,
                whole(vecs.shape),
                pl.BlockSpec((1, dim), lambda j, s: (0, j)),
                whole(tab.shape),
                ANYWHERE,
                ANYWHERE,
            ],
            out_specs=[
                pl.BlockSpec((pairs, pl.squeezed, rows, LANES), lambda j, s: (0, j, 0, 0)),
                whole((rows, dim)),
            ]
            + [whole((2, rows, half))] * 2,
            scratch_shapes=[
                pltpu.VMEM((3, 2, half, dim), bf16),
                pltpu.SemaphoreType.DMA((3, 2)),
            ],
        ),
        out_shape=[shape_of((pairs, 3, rows, LANES), bf16), shape_of((rows, dim), bf16)]
        + [shape_of((2, rows, half), bf16)] * 2,
        name="qkv_proj",
        **params_of(),
    )(wsh, given, got, vecs, qkv_b, tab, w_own, w_oth)


MLP_TILE = 1024
MLP_PIECE = 512


def ff_tiles(wsh_ref, up_own, up_oth, dn_own, dn_oth, up_buf, dn_buf, sems):
    tile = dn_buf.shape[1]
    own = dn_own.shape[0] // tile

    def tiles(t):
        cols = pl.ds(pl.multiple_of(((wsh_ref[0] * own + t) % (2 * own)) * tile, tile), tile)
        copies = [
            pltpu.make_async_copy(weight.at[:, cols], up_buf.at[t, side], sems.at[t, side])
            for side, weight in enumerate((up_own, up_oth))
        ]
        held = not isinstance(t, int) or t < own
        down = dn_own if held else dn_oth
        rows = pl.ds((t % own) * tile, tile)
        return copies + [pltpu.make_async_copy(down.at[rows], dn_buf.at[t], sems.at[t, 2])]

    return tiles


def mlp_kernel(own_tiles, save, wsh_ref, nm_own, nm_oth, up_b, down_b, *refs):
    weights, outs = refs[:4], refs[4:]
    if save:
        out_ref, slope_ref, gt_own, gt_oth, up_buf, dn_buf, sems = outs
    else:
        out_ref, up_buf, dn_buf, sems = outs
    step = pl.program_id(0)
    tiles = ff_tiles(wsh_ref, *weights, up_buf, dn_buf, sems)
    start_all(tiles, 2 * own_tiles)

    @pl.when(step == 0)
    def _():
        out_ref[...] = jnp.broadcast_to(down_b[...], out_ref.shape)

    for copy in tiles(step):
        copy.wait()
    for at in range(0, dn_buf.shape[1], MLP_PIECE):
        piece = pl.ds(at, MLP_PIECE)
        pre = (
            dot_nn(nm_own[...], up_buf[step, 0, :, piece])
            + dot_nn(nm_oth[...], up_buf[step, 1, :, piece])
            + up_b[:, piece]
        )
        gate = 0.5 + 0.5 * lax.erf(pre * INV_SQRT2)
        act = (pre * gate).astype(bf16)
        if save:
            slope = gate + pre * (INV_SQRT_2PI * jnp.exp(-0.5 * pre * pre))
            slope_ref[piece] = slope.astype(bf16).T
            turned = act.T

            @pl.when(step < own_tiles)
            def _():
                gt_own[piece] = turned

            @pl.when(step >= own_tiles)
            def _():
                gt_oth[piece] = turned

        out_ref[...] += dot_nn(act, dn_buf[step, piece])


def mlp_scratch(half, dim, steps):
    return [
        pltpu.VMEM((steps, 2, half, MLP_TILE), bf16),
        pltpu.VMEM((steps, MLP_TILE, dim), bf16),
        pltpu.SemaphoreType.DMA((steps, 3)),
    ]


def mlp_call(nm_own, nm_oth, up_b, down_b, up_own, up_oth, dn_own, dn_oth, wsh, save):
    rows, half = nm_own.shape[1:]
    dim = dn_own.shape[1]
    ff = up_own.shape[1]
    own = dn_own.shape[0] // MLP_TILE
    by_ff = lambda j, s: (0, (s[0] * own + j) % (2 * own))
    out_specs = [whole((rows, dim))]
    out_shape = [shape_of((rows, dim), f32)]
    if save:
        out_specs += [
            pl.BlockSpec((MLP_TILE, rows), lambda j, s: by_ff(j, s)[::-1]),
            pl.BlockSpec((MLP_TILE, rows), lambda j, s: (jnp.minimum(j, own - 1), 0)),
            pl.BlockSpec((MLP_TILE, rows), lambda j, s: (jnp.maximum(j - own, 0), 0)),
        ]
        out_shape += [shape_of((ff, rows), bf16)] + [shape_of((ff // 2, rows), bf16)] * 2
    return pl.pallas_call(
        functools.partial(mlp_kernel, own, save),
        grid_spec=pltpu.PrefetchScalarGridSpec(
            num_scalar_prefetch=1,
            grid=(2 * own,),
            in_specs=[layer_of((rows, half), 1)] * 2
            + [pl.BlockSpec((1, MLP_TILE), by_ff), whole((1, dim))]
            + [ANYWHERE] * 4,
            out_specs=out_specs,
            scratch_shapes=mlp_scratch(half, dim, 2 * own),
        ),
        out_shape=out_shape,
        name="mlp_forward",
        **params_of(),
    )(wsh, nm_own, nm_oth, up_b, down_b, up_own, up_oth, dn_own, dn_oth)


def mlp_back_kernel(own_tiles, half, wsh_ref, dy_ref, slope_ref, *refs):
    weights = refs[:4]
    du_ref, dnm_ref, acc_own, acc_oth, up_buf, dn_buf, sems = refs[4:]
    step = pl.program_id(0)
    tiles = ff_tiles(wsh_ref, *weights, up_buf, dn_buf, sems)
    start_all(tiles, 2 * own_tiles)

    @pl.when(step == 0)
    def _():
        acc_own[...] = jnp.zeros(acc_own.shape, f32)
        acc_oth[...] = jnp.zeros(acc_oth.shape, f32)

    for copy in tiles(step):
        copy.wait()
    for at in range(0, dn_buf.shape[1], MLP_PIECE):
        piece = pl.ds(at, MLP_PIECE)
        dact = dot_nt(dn_buf[step, piece], dy_ref[...])
        du = (dact * slope_ref[piece].astype(f32)).astype(bf16)
        du_ref[piece] = du
        acc_own[...] += dot_nn(up_buf[step, 0, :, piece], du)
        acc_oth[...] += dot_nn(up_buf[step, 1, :, piece], du)

    @pl.when(step == 2 * own_tiles - 1)
    def _():
        first = wsh_ref[0] == 0
        dnm_ref[:, :half] = jnp.where(first, acc_own[...], acc_oth[...]).T
        dnm_ref[:, half:] = jnp.where(first, acc_oth[...], acc_own[...]).T


def mlp_back_call(dy, slope, up_own, up_oth, dn_own, dn_oth, wsh):
    rows, dim = dy.shape
    half = up_own.shape[0]
    ff = slope.shape[0]
    own = dn_own.shape[0] // MLP_TILE
    by_ff = lambda j, s: ((s[0] * own + j) % (2 * own), 0)
    return pl.pallas_call(
        functools.partial(mlp_back_kernel, own, half),
        grid_spec=pltpu.PrefetchScalarGridSpec(
            num_scalar_prefetch=1,
            grid=(2 * own,),
            in_specs=[whole((rows, dim)), pl.BlockSpec((MLP_TILE, rows), by_ff)] + [ANYWHERE] * 4,
            out_specs=[pl.BlockSpec((MLP_TILE, rows), by_ff), whole((rows, dim))],
            scratch_shapes=[pltpu.VMEM((half, rows), f32), pltpu.VMEM((half, rows), f32)]
            + mlp_scratch(half, dim, 2 * own),
        ),
        out_shape=[shape_of((ff, rows), bf16), shape_of((rows, dim), f32)],
        name="mlp_backward",
        **params_of(),
    )(wsh, dy, slope, up_own, up_oth, dn_own, dn_oth)


def sort_in(loc_ref, ref, dst, half_rows, part=None):
    for block in range(dst.shape[0] // half_rows):
        place = loc_ref[block]
        rows = pl.ds(pl.multiple_of((place % 2) * half_rows, half_rows), half_rows)
        if part is None:
            vals = ref[place // 2, rows, :]
        else:
            vals = ref[place // 2, part, rows, :]
        dst[block * half_rows : (block + 1) * half_rows] = vals


def sort_out(loc_ref, vals, ref, half_rows, part=None):
    for block in range(vals.shape[0] // half_rows):
        place = loc_ref[block]
        rows = pl.ds(pl.multiple_of((place % 2) * half_rows, half_rows), half_rows)
        piece = vals[block * half_rows : (block + 1) * half_rows]
        if part is None:
            ref[place // 2, rows, :] = piece
        else:
            ref[place // 2, part, rows, :] = piece


def head_of(vals, head):
    lane = lax.broadcasted_iota(jnp.int32, vals.shape, 1)
    return jnp.where(lane // (LANES // 2) == head, vals, jnp.zeros_like(vals))


def scores_of(keys, queries, scale, diagonal):
    scores = dot_nt(keys, queries) * scale
    if diagonal:
        key_at = lax.broadcasted_iota(jnp.int32, scores.shape, 0)
        query_at = lax.broadcasted_iota(jnp.int32, scores.shape, 1)
        scores = jnp.where(key_at <= query_at, scores, MASKED_SCORE)
    return scores


def attend_kernel(tile, loc_ref, qkv_ref, o_ref, lse_ref, q_s, k_s, v_s, vt_s, o_s):
    half_rows = qkv_ref.shape[2] // 2
    seq = q_s.shape[0]
    head_size = LANES // 2
    scale = head_size**-0.5
    sort_in(loc_ref, qkv_ref, q_s, half_rows, 0)
    sort_in(loc_ref, qkv_ref, k_s, half_rows, 1)
    sort_in(loc_ref, qkv_ref, v_s, half_rows, 2)
    vt_s[...] = v_s[...].T
    for t in range(seq // tile):
        rows = slice(t * tile, (t + 1) * tile)
        queries = q_s[rows]
        outs = []
        for head in range(2):
            picked = head_of(queries, head)
            parts = [
                scores_of(k_s[i * tile : (i + 1) * tile], picked, scale, i == t)
                for i in range(t + 1)
            ]
            top = functools.reduce(
                jnp.maximum, [jnp.max(p, axis=0, keepdims=True) for p in parts]
            )
            parts = [jnp.exp(p - top) for p in parts]
            total = sum(jnp.sum(p, axis=0, keepdims=True) for p in parts)
            lse_ref[head : head + 1, rows] = top + jnp.log(total)
            inverse = 1.0 / total
            acc = None
            for i, p in enumerate(parts):
                term = dot_nn(
                    vt_s[head * head_size : (head + 1) * head_size, i * tile : (i + 1) * tile],
                    (p * inverse).astype(bf16),
                )
                acc = term if acc is None else acc + term
            outs.append(acc)
        o_s[rows] = jnp.concatenate(outs, axis=0).T.astype(bf16)
    sort_out(loc_ref, o_s, o_ref, half_rows)


def attend_call(qkv, loc):
    count, _, rows, _ = qkv.shape
    seq = count * rows
    return pl.pallas_call(
        functools.partial(attend_kernel, 256),
        grid_spec=pltpu.PrefetchScalarGridSpec(
            num_scalar_prefetch=1,
            grid=(1,),
            in_specs=[whole(qkv.shape)],
            out_specs=[whole((count, rows, LANES)), whole((2, seq))],
            scratch_shapes=[
                pltpu.VMEM((seq, LANES), bf16),
                pltpu.VMEM((seq, LANES), bf16),
                pltpu.VMEM((seq, LANES), bf16),
                pltpu.VMEM((LANES, seq), bf16),
                pltpu.VMEM((seq, LANES), bf16),
            ],
        ),
        out_shape=[shape_of((count, rows, LANES), bf16), shape_of((2, seq), f32)],
        name="attention",
        **params_of(),
    )(loc, qkv)


def attend_back_kernel(
    tile, loc_ref, qkv_ref, da_ref, lse_ref, out_ref, q_s, k_s, v_s, da_s, kt_s, dq_s, dk_s, dv_s
):
    half_rows = qkv_ref.shape[2] // 2
    seq = q_s.shape[0]
    head_size = LANES // 2
    scale = head_size**-0.5
    sort_in(loc_ref, qkv_ref, q_s, half_rows, 0)
    sort_in(loc_ref, qkv_ref, k_s, half_rows, 1)
    sort_in(loc_ref, qkv_ref, v_s, half_rows, 2)
    sort_in(loc_ref, da_ref, da_s, half_rows)
    kt_s[...] = k_s[...].T
    dk_s[...] = jnp.zeros(dk_s.shape, f32)
    dv_s[...] = jnp.zeros(dv_s.shape, f32)
    for t in range(seq // tile):
        rows = slice(t * tile, (t + 1) * tile)
        outs = []
        for head in range(2):
            queries = head_of(q_s[rows], head)
            grads = head_of(da_s[rows], head)
            lse = lse_ref[head : head + 1, rows]
            probs, dprobs, row_dot = [], [], 0.0
            for i in range(t + 1):
                keys = slice(i * tile, (i + 1) * tile)
                p = jnp.exp(scores_of(k_s[keys], queries, scale, i == t) - lse)
                dp = dot_nt(v_s[keys], grads)
                row_dot = row_dot + jnp.sum(p * dp, axis=0, keepdims=True)
                dv_s[keys] += dot_nn(p.astype(bf16), grads)
                probs.append(p)
                dprobs.append(dp)
            acc = None
            for i in range(t + 1):
                keys = slice(i * tile, (i + 1) * tile)
                ds = (probs[i] * (dprobs[i] - row_dot) * scale).astype(bf16)
                dk_s[keys] += dot_nn(ds, queries)
                term = dot_nn(kt_s[head * head_size : (head + 1) * head_size, keys], ds)
                acc = term if acc is None else acc + term
            outs.append(acc)
        dq_s[rows] = jnp.concatenate(outs, axis=0).T.astype(bf16)
    sort_out(loc_ref, dq_s, out_ref, half_rows, 0)
    k_s[...] = dk_s[...].astype(bf16)
    v_s[...] = dv_s[...].astype(bf16)
    sort_out(loc_ref, k_s, out_ref, half_rows, 1)
    sort_out(loc_ref, v_s, out_ref, half_rows, 2)


def attend_back_call(qkv, da, lse, loc):
    count, _, rows, _ = qkv.shape
    seq = count * rows
    return pl.pallas_call(
        functools.partial(attend_back_kernel, 256),
        grid_spec=pltpu.PrefetchScalarGridSpec(
            num_scalar_prefetch=1,
            grid=(1,),
            in_specs=[whole(qkv.shape), whole(da.shape), whole(lse.shape)],
            out_specs=whole(qkv.shape),
            scratch_shapes=[
                pltpu.VMEM((seq, LANES), bf16),
                pltpu.VMEM((seq, LANES), bf16),
                pltpu.VMEM((seq, LANES), bf16),
                pltpu.VMEM((seq, LANES), bf16),
                pltpu.VMEM((LANES, seq), bf16),
                pltpu.VMEM((seq, LANES), bf16),
                pltpu.VMEM((seq, LANES), f32),
                pltpu.VMEM((seq, LANES), f32),
            ],
        ),
        out_shape=shape_of(qkv.shape, bf16),
        name="attention_backward",
        **params_of(),
    )(loc, qkv, da, lse)


def by_head(parts):
    pairs, rows, lanes = parts.shape
    return jnp.transpose(parts, (1, 0, 2)).reshape(rows, HEADS, pairs * lanes // HEADS)


def by_pair(heads):
    rows = heads.shape[0]
    return jnp.transpose(heads.reshape(rows, -1, LANES), (1, 0, 2))


def wide_scores(queries, keys, query_pos, key_pos):
    raw = jnp.einsum("qhd,khd->hqk", queries, keys, preferred_element_type=f32)
    allowed = (query_pos[:, None] >= key_pos[None, :])[None]
    return jnp.where(allowed, raw * queries.shape[-1] ** (-0.5), MASKED_SCORE)


def key_blocks(arrays, rows):
    return tuple(a.reshape((a.shape[0] // rows, rows) + a.shape[1:]) for a in arrays)


def wide_attend(qkv, query_pos, key_pos):
    queries = by_head(qkv[:, 0])
    keys = lax.all_gather(by_head(qkv[:, 1]), "ctx", axis=0, tiled=True)
    values = lax.all_gather(by_head(qkv[:, 2]), "ctx", axis=0, tiled=True)
    block = min(512, keys.shape[0])
    split = key_blocks((keys, values, key_pos), block)
    rows, _, head_size = queries.shape

    def max_step(carry, block_in):
        top, total = carry
        scores = wide_scores(queries, block_in[0], query_pos, block_in[2])
        new_top = jnp.maximum(top, jnp.max(scores, axis=-1))
        part = jnp.sum(jnp.exp(scores - new_top[..., None]), axis=-1)
        return ((new_top, total * jnp.exp(top - new_top) + part), None)

    start = (jnp.full((HEADS, rows), MASKED_SCORE, f32), jnp.zeros((HEADS, rows), f32))
    (top, total), _ = lax.scan(max_step, start, split)
    lse = top + jnp.log(total)

    def value_step(running, block_in):
        scores = wide_scores(queries, block_in[0], query_pos, block_in[2])
        probs = jnp.exp(scores - lse[..., None]).astype(bf16)
        term = jnp.einsum("hqk,khd->qhd", probs, block_in[1], preferred_element_type=f32)
        return (running + term, None)

    attended, _ = lax.scan(value_step, jnp.zeros((rows, HEADS, head_size), f32), split)
    return by_pair(attended.astype(bf16)), (queries, keys, values, lse)


def wide_attend_back(kept, da, query_pos, key_pos):
    queries, keys, values, lse = kept
    grads = by_head(da)
    block = min(512, keys.shape[0])
    split = key_blocks((keys, values, key_pos), block)
    scale = queries.shape[-1] ** (-0.5)

    def pieces(block_in):
        scores = wide_scores(queries, block_in[0], query_pos, block_in[2])
        probs = jnp.exp(scores - lse[..., None])
        dprobs = jnp.einsum("qhd,khd->hqk", grads, block_in[1], preferred_element_type=f32)
        return probs, dprobs

    def dot_step(running, block_in):
        probs, dprobs = pieces(block_in)
        return (running + jnp.sum(probs * dprobs, axis=-1), None)

    row_dot, _ = lax.scan(dot_step, jnp.zeros(lse.shape, f32), split)

    def key_step(running, block_in):
        probs, dprobs = pieces(block_in)
        ds = (scale * probs * (dprobs - row_dot[..., None])).astype(bf16)
        running = running + jnp.einsum("hqk,khd->qhd", ds, block_in[0], preferred_element_type=f32)
        dk = jnp.einsum("hqk,qhd->khd", ds, queries, preferred_element_type=f32)
        dv = jnp.einsum("hqk,qhd->khd", probs.astype(bf16), grads, preferred_element_type=f32)
        return (running, (dk.astype(bf16), dv.astype(bf16)))

    dq, (dk, dv) = lax.scan(key_step, jnp.zeros(queries.shape, f32), split)
    dk, dv = (
        lax.psum_scatter(part.reshape(keys.shape), "ctx", scatter_dimension=0, tiled=True)
        for part in (dk, dv)
    )
    return jnp.stack([by_pair(dq.astype(bf16)), by_pair(dk), by_pair(dv)], axis=1)


def lanes_of(ref):
    return jnp.concatenate([ref[i] for i in range(ref.shape[0])], axis=1)


def proj_kernel(half, wsh_ref, a_ref, x_ref, mlp_ref, bias_ref, p_own, p_oth, y_ref, a_own, a_oth):
    first = wsh_ref[0] == 0
    a = lanes_of(a_ref)
    own = jnp.where(first, a[:, :half], a[:, half:])
    oth = jnp.where(first, a[:, half:], a[:, :half])
    a_own[...] = own
    a_oth[...] = oth
    attn = dot_nn(own, p_own[...]) + dot_nn(oth, p_oth[...]) + bias_ref[...]
    y_ref[...] = (x_ref[...].astype(f32) + attn + mlp_ref[...]).astype(bf16)


def proj_call(a, x, mlp, bias, p_own, p_oth, wsh):
    rows, dim = x.shape
    half = p_own.shape[0]
    return pl.pallas_call(
        functools.partial(proj_kernel, half),
        grid_spec=pltpu.PrefetchScalarGridSpec(
            num_scalar_prefetch=1,
            grid=(1,),
            in_specs=[
                whole(a.shape),
                whole(x.shape),
                whole((rows, dim)),
                whole(bias.shape),
                whole(p_own.shape),
                whole(p_oth.shape),
            ],
            out_specs=[whole((rows, dim)), whole((rows, half)), whole((rows, half))],
        ),
        out_shape=[shape_of((rows, dim), bf16)] + [shape_of((rows, half), bf16)] * 2,
        name="attn_out",
        **params_of(),
    )(wsh, a, x, mlp, bias, p_own, p_oth)


def da_kernel(wsh_ref, given_ref, got_ref, p_own, p_oth, out_ref, dy_ref):
    dy = jnp.where(wsh_ref[1] == 1, got_ref[...], given_ref[...])
    dy_ref[...] = dy
    wsh = wsh_ref[0]
    count = out_ref.shape[0] // 2
    for place, weight in ((wsh * count, p_own), ((1 - wsh) * count, p_oth)):
        part = dot_nt(weight[...], dy).T.astype(bf16)
        for i in range(count):
            out_ref[place + i] = part[:, i * LANES : (i + 1) * LANES]


def da_call(given, index, got, p_own, p_oth, wsh):
    rows, dim = given.shape[1:]
    pairs = dim // LANES
    got_spec = whole((rows, dim))
    if got is None:
        got, got_spec = given, layer_of((rows, dim), index)
    return pl.pallas_call(
        da_kernel,
        grid_spec=pltpu.PrefetchScalarGridSpec(
            num_scalar_prefetch=1,
            grid=(1,),
            in_specs=[layer_of((rows, dim), index), got_spec]
            + [whole(p_own.shape), whole(p_oth.shape)],
            out_specs=[whole((pairs, rows, LANES)), whole((rows, dim))],
        ),
        out_shape=[shape_of((pairs, rows, LANES), bf16), shape_of((rows, dim), bf16)],
        name="attn_out_backward",
        **params_of(),
    )(wsh, given, got, p_own, p_oth)


DX_ROWS = 256


def dx_kernel(half, wsh_ref, dqkv_ref, tab_ref, x_ref, dy_ref, dnm_ref, vec_ref, *rest):
    w_own, w_oth, back_ref, dx_ref, sums_ref, grad_s, buf, sems = rest
    pairs = dqkv_ref.shape[0]
    copies = []
    for side, weight in enumerate((w_own, w_oth)):
        for t in range(half // DX_ROWS):
            copies.append(
                pltpu.make_async_copy(
                    weight.at[pl.ds(t * DX_ROWS, DX_ROWS)], buf.at[side, t], sems.at[side, t]
                )
            )
    for copy in copies:
        copy.start()
    for part in range(3):
        for pair in range(pairs):
            vals = dqkv_ref[pair, part]
            if part < 2:
                vals = unrope(vals.astype(f32), tab_ref).astype(bf16)
            back_ref[pair, part] = vals
            grad_s[:, pl.ds((part * pairs + pair) * LANES, LANES)] = vals
    halves = []
    for side in range(2):
        cols = []
        for t in range(half // DX_ROWS):
            copies[side * (half // DX_ROWS) + t].wait()
            cols.append(dot_nt(buf[side, t], grad_s[...]).T)
        halves.append(jnp.concatenate(cols, axis=1))
    first = wsh_ref[0] == 0
    own, oth = halves
    dna = jnp.concatenate([jnp.where(first, own, oth), jnp.where(first, oth, own)], axis=1)
    dnm = dnm_ref[...]
    xhat, scale = normalized(x_ref[...].astype(f32))
    grad = dna * vec_ref[0:1] + dnm * vec_ref[2:3]
    inner = (
        grad
        - jnp.mean(grad, axis=-1, keepdims=True)
        - xhat * jnp.mean(grad * xhat, axis=-1, keepdims=True)
    )
    dx_ref[...] = (dy_ref[...].astype(f32) + scale * inner).astype(bf16)
    sums_ref[0:1] = jnp.sum(dna * xhat, axis=0, keepdims=True)
    sums_ref[1:2] = jnp.sum(dna, axis=0, keepdims=True)
    sums_ref[2:3] = jnp.sum(dnm * xhat, axis=0, keepdims=True)
    sums_ref[3:4] = jnp.sum(dnm, axis=0, keepdims=True)


def dx_call(dqkv, tab, x, dy, dnm, vecs, w_own, w_oth, wsh):
    rows, dim = x.shape
    half = w_own.shape[0]
    return pl.pallas_call(
        functools.partial(dx_kernel, half),
        grid_spec=pltpu.PrefetchScalarGridSpec(
            num_scalar_prefetch=1,
            grid=(1,),
            in_specs=[
                whole(dqkv.shape),
                whole(tab.shape),
                whole(x.shape),
                whole(dy.shape),
                whole(dnm.shape),
                whole(vecs.shape),
                ANYWHERE,
                ANYWHERE,
            ],
            out_specs=[whole(dqkv.shape), whole((rows, dim)), whole((4, dim))],
            scratch_shapes=[
                pltpu.VMEM((rows, 3 * dim), bf16),
                pltpu.VMEM((2, half // DX_ROWS, DX_ROWS, 3 * dim), bf16),
                pltpu.SemaphoreType.DMA((2, half // DX_ROWS)),
            ],
        ),
        out_shape=[
            shape_of(dqkv.shape, bf16),
            shape_of((rows, dim), bf16),
            shape_of((4, dim), f32),
        ],
        name="section_input_grad",
        **params_of(),
    )(wsh, dqkv, tab, x, dy, dnm, vecs, w_own, w_oth)


def stack_rows(refs, cols=slice(None)):
    return jnp.concatenate([ref[:, cols] for ref in refs], axis=0)


def down_grad_kernel(micros, *refs):
    gt_refs, dy_refs = refs[:micros], refs[micros : 2 * micros]
    out_ref, sum_ref, dy_s = refs[2 * micros :]

    @pl.when(pl.program_id(0) == 0)
    def _():
        dy = stack_rows(dy_refs)
        dy_s[...] = dy
        sum_ref[...] = jnp.sum(dy.astype(f32), axis=0, keepdims=True)

    left = jnp.concatenate([ref[...] for ref in gt_refs], axis=1)
    out_ref[...] = dot_nn(left, dy_s[...]).astype(bf16)


def down_grad_call(gt_list, dy_list):
    ff_rows, rows = gt_list[0].shape
    dim = dy_list[0].shape[1]
    micros = len(dy_list)
    tile = 512
    return pl.pallas_call(
        functools.partial(down_grad_kernel, micros),
        grid=(ff_rows // tile,),
        in_specs=[pl.BlockSpec((tile, rows), lambda j: (j, 0))] * micros
        + [whole((rows, dim))] * micros,
        out_specs=[pl.BlockSpec((tile, dim), lambda j: (j, 0)), whole((1, dim))],
        out_shape=[shape_of((ff_rows, dim), bf16), shape_of((1, dim), f32)],
        scratch_shapes=[pltpu.VMEM((micros * rows, dim), bf16)],
        name="down_grad",
        **params_of(),
    )(*gt_list, *dy_list)


def up_grad_kernel(micros, *refs):
    x_refs, du_refs = refs[:micros], refs[micros : 2 * micros]
    out_ref, sum_ref, xt_s = refs[2 * micros :]

    @pl.when(pl.program_id(0) == 0)
    def _():
        xt_s[...] = stack_rows(x_refs).T

    du = jnp.concatenate([ref[...] for ref in du_refs], axis=1)
    sum_ref[...] = dot_nt(jnp.ones((8, du.shape[1]), bf16), du)[:1]
    out_ref[...] = dot_nt(xt_s[...], du).astype(bf16)


def up_grad_call(x_list, du_list):
    rows, half = x_list[0].shape[1:]
    ff = du_list[0].shape[0]
    micros = len(x_list)
    tile = 1024
    return pl.pallas_call(
        functools.partial(up_grad_kernel, micros),
        grid=(ff // tile,),
        in_specs=[layer_of((rows, half), 1)] * micros
        + [pl.BlockSpec((tile, rows), lambda j: (j, 0))] * micros,
        out_specs=[
            pl.BlockSpec((half, tile), lambda j: (0, j)),
            pl.BlockSpec((1, tile), lambda j: (0, j)),
        ],
        out_shape=[shape_of((half, ff), bf16), shape_of((1, ff), f32)],
        scratch_shapes=[pltpu.VMEM((half, micros * rows), bf16)],
        name="up_grad",
        **params_of(),
    )(*x_list, *du_list)


def attn_grad_kernel(micros, *refs):
    x_refs, a_refs, d_refs, dy_refs = (refs[i * micros : (i + 1) * micros] for i in range(4))
    out_ref, sum_ref, xt_s = refs[4 * micros :]
    part = pl.program_id(0)

    def finish(dy):
        sum_ref[...] = jnp.sum(dy.astype(f32), axis=0, keepdims=True)
        out_ref[...] = dot_nn(xt_s[...], dy).astype(bf16)

    @pl.when(part == 0)
    def _():
        xt_s[...] = stack_rows(x_refs).T

    @pl.when(part < 3)
    def _():
        finish(jnp.concatenate([lanes_of(ref) for ref in d_refs], axis=0))

    @pl.when(part == 3)
    def _():
        xt_s[...] = stack_rows(a_refs).T
        finish(stack_rows(dy_refs))


def attn_grad_call(x_list, a_list, d_list, dy_list):
    rows, half = x_list[0].shape[1:]
    pairs = d_list[0].shape[0]
    dim = pairs * LANES
    micros = len(x_list)
    d_spec = pl.BlockSpec(
        (pairs, pl.squeezed, rows, LANES), lambda j: (0, jnp.minimum(j, 2), 0, 0)
    )
    return pl.pallas_call(
        functools.partial(attn_grad_kernel, micros),
        grid=(4,),
        in_specs=[layer_of((rows, half), 0)] * micros
        + [whole((rows, half))] * micros
        + [d_spec] * micros
        + [whole((rows, dim))] * micros,
        out_specs=[
            pl.BlockSpec((half, dim), lambda j: (0, j)),
            pl.BlockSpec((1, dim), lambda j: (0, j)),
        ],
        out_shape=[shape_of((half, 4 * dim), bf16), shape_of((1, 4 * dim), f32)],
        scratch_shapes=[pltpu.VMEM((half, micros * rows), bf16)],
        name="attn_grad",
        **params_of(),
    )(*x_list, *a_list, *d_list, *dy_list)


def ring_of(count):
    return list(range(0, count, 2)) + list(range(count - 1, 0, -2))


def ring_place(axis):
    count = lax.axis_size(axis)
    me = lax.axis_index(axis)
    return jnp.where(me % 2 == 0, me // 2, count - (me + 1) // 2)


def ring_shift(vals, axis, by):
    order = ring_of(lax.axis_size(axis))
    count = len(order)
    pairs = [(order[i], order[(i + by) % count]) for i in range(count)]
    return lax.ppermute(vals, axis, pairs)


def low_sum(*terms):
    total = terms[0].astype(f32)
    for term in terms[1:]:
        total = total + term.astype(f32)
    return total.astype(bf16)


def tied(token, *vals):
    return lax.optimization_barrier((token, vals))[1]


def ring_sum(own, widths, axis):
    count = lax.axis_size(axis)
    place = ring_place(axis)
    half = count // 2
    full_rows, cols = own.shape
    rows = full_rows // count
    own = own.reshape(count, rows, cols)
    cut = rows // 2
    starts = [sum(widths[:i]) for i in range(len(widths))]

    def index(k):
        return (place + (k + count)) % count

    def take(k):
        return lax.dynamic_index_in_dim(own, index(k), 0, keepdims=False)

    def put(totals, piece, k, lo=0):
        for i, (start, width) in enumerate(zip(starts, widths)):
            part = piece[:, start : start + width].astype(f32)[None]
            totals[i] = lax.dynamic_update_slice(totals[i], part, (index(k), lo, 0))

    token = yield None
    (far,) = tied(token, take(half))
    ahead = ring_shift(far[:cut], axis, 1)
    behind = ring_shift(far[cut:], axis, -1)
    token = yield far
    for k in range(half - 1, 0, -1):
        ahead, behind = tied(token, ahead, behind)
        mine_a, mine_b = take(k), take(-k)
        if k == half - 1:
            ahead = jnp.concatenate([low_sum(mine_a[:cut], ahead), mine_a[cut:]], axis=0)
            behind = jnp.concatenate([mine_b[:cut], low_sum(mine_b[cut:], behind)], axis=0)
        else:
            ahead, behind = low_sum(mine_a, ahead), low_sum(mine_b, behind)
        token = behind
        ahead = ring_shift(ahead, axis, 1)
        behind = ring_shift(behind, axis, -1)
        token = yield token
    ahead, behind = tied(token, ahead, behind)
    mine = low_sum(take(0), ahead, behind)
    totals = [jnp.zeros((count, rows, width), f32) for width in widths]
    put(totals, mine, 0)
    ahead = ring_shift(mine, axis, 1)
    behind = ring_shift(mine, axis, -1)
    token = yield mine
    for k in range(1, half):
        ahead, behind = tied(token, ahead, behind)
        last = k == half - 1
        next_ahead = ring_shift(ahead[:cut] if last else ahead, axis, 1)
        next_behind = ring_shift(behind[cut:] if last else behind, axis, -1)
        put(totals, ahead, -k)
        put(totals, behind, k)
        token = behind
        ahead, behind = next_ahead, next_behind
        token = yield token
    ahead, behind = tied(token, ahead, behind)
    put(totals, ahead, -half)
    put(totals, behind, half, cut)
    yield [total.reshape(full_rows, -1) for total in totals]


def butterfly_sum(vals, axis):
    count = lax.axis_size(axis)
    if count & (count - 1):
        return lax.psum(vals, axis)
    by = 1
    while by < count:
        vals = vals + lax.ppermute(vals, axis, [(i, i ^ by) for i in range(count)])
        by *= 2
    return vals


def swap(vals):
    return lax.ppermute(vals, "wsh", [(0, 1), (1, 0)])


def pass_on(vals, by):
    pairs = [(0, 1)] if by > 0 else [(1, 0)]
    return lax.ppermute(vals, "section", pairs)


def block_places(block_pair, count):
    want = jnp.arange(2 * count, dtype=jnp.int32)
    device = jnp.arange(count, dtype=jnp.int32)
    first = (block_pair[None, :] == want[:, None]).astype(jnp.int32)
    second = ((2 * count - 1 - block_pair)[None, :] == want[:, None]).astype(jnp.int32)
    return jnp.sum(first * (2 * device) + second * (2 * device + 1), axis=1)


def row_positions(block_pair, stored, tok_dev):
    count = block_pair.shape[0]
    device = stored // tok_dev
    within = stored % tok_dev
    half_rows = tok_dev // 2
    matches = device[:, None] == jnp.arange(count, dtype=jnp.int32)[None, :]
    pair_block = jnp.sum(jnp.where(matches, block_pair[None, :], 0), axis=1)
    block_idx = jnp.where(within < half_rows, pair_block, 2 * count - 1 - pair_block)
    return block_idx * half_rows + within % half_rows


def rotary_table(positions, head_size):
    half_rot = ROT // 2
    lane = jnp.arange(LANES, dtype=jnp.int32) % head_size
    inv_freq = ROPE_BASE ** (-((lane % half_rot).astype(f32) * 2.0) / ROT)
    angles = positions.astype(f32)[:, None] * inv_freq[None, :]
    cosine, sine = jnp.cos(angles), jnp.sin(angles)
    lead, second = (lane < half_rot)[None], ((lane >= half_rot) & (lane < ROT))[None]
    return jnp.stack(
        [
            jnp.where(lead | second, cosine, 1.0),
            jnp.where(lead, -sine, 0.0),
            jnp.where(second, sine, 0.0),
        ]
    )


def body(
    inputs,
    cotangent,
    block_pair,
    qkv_weight,
    qkv_bias,
    proj_weight,
    proj_bias,
    up_weight,
    up_bias,
    down_weight,
    down_bias,
    attn_gain,
    attn_shift,
    mlp_gain,
    mlp_shift,
):
    first_section = lax.axis_index("section") == 0
    count = lax.axis_size("ctx")
    micros, _, tok_dev, dim = inputs.shape
    head_size = dim // HEADS
    half = dim // 2
    my_half = lax.axis_index("wsh")
    wsh = jnp.stack([my_half.astype(jnp.int32), first_section.astype(jnp.int32)])
    one_pair_each = count == dim // LANES

    wq, wp, wu, wd = (w[0] for w in (qkv_weight, proj_weight, up_weight, down_weight))
    small = jnp.concatenate(
        [
            v[0].reshape(-1, half)
            for v in (
                attn_gain,
                attn_shift,
                mlp_gain,
                mlp_shift,
                proj_bias,
                down_bias,
                qkv_bias,
                up_bias,
            )
        ],
        axis=0,
    )
    small_oth = swap(small)
    wq_oth = swap(wq)
    first_here = lax.optimization_barrier((wq_oth, small_oth))
    wq_oth, small_oth = first_here
    wu_oth = swap(tied(wq_oth, wu)[0])
    wd_oth = swap(tied(wq_oth, wd)[0])
    wp_oth = swap(tied(wu_oth, wp)[0])
    low_part = jnp.where(my_half == 0, small, small_oth).astype(f32)
    high_part = jnp.where(my_half == 0, small_oth, small).astype(f32)
    vecs = jnp.concatenate([low_part[:6], high_part[:6]], axis=1)
    qkv_rows = 6 + qkv_bias.shape[1] // half
    proj_b, down_b = vecs[4:5], vecs[5:6]
    qkv_b = jnp.concatenate([low_part[6:qkv_rows], high_part[6:qkv_rows]], axis=0).reshape(1, -1)
    up_b = jnp.concatenate([low_part[qkv_rows:], high_part[qkv_rows:]], axis=0).reshape(1, -1)

    local_rows = lax.axis_index("ctx") * tok_dev + jnp.arange(tok_dev, dtype=jnp.int32)
    query_pos = row_positions(block_pair, local_rows, tok_dev)
    key_pos = row_positions(block_pair, jnp.arange(count * tok_dev, dtype=jnp.int32), tok_dev)
    tab = rotary_table(query_pos, head_size)
    loc = block_places(block_pair, count)

    def exchange(vals):
        return lax.all_to_all(vals, "ctx", split_axis=0, concat_axis=0, tiled=True)

    def norm_qkv(index, got):
        return qkv_call(rows_in, index, got, vecs, qkv_b, tab, wq, wq_oth, wsh)

    def mlp(made, save):
        return mlp_call(made[2], made[3], up_b, down_b, wu, wu_oth, wd, wd_oth, wsh, save)

    def mlp_back(dy, mlp_kept):
        return mlp_back_call(dy, mlp_kept[1], wu, wu_oth, wd, wd_oth, wsh)

    def out_back(index, got):
        return da_call(cot_in, index, got, wp, wp_oth, wsh)

    def to_heads(vals):
        return exchange(vals) if one_pair_each else vals

    def to_rows(vals):
        return exchange(vals) if one_pair_each else vals

    def attend(qkv):
        if one_pair_each:
            attended, lse = attend_call(qkv, loc)
            return attended, (qkv, lse)
        return wide_attend(qkv, query_pos, key_pos)

    def attend_back(kept, da):
        if one_pair_each:
            return attend_back_call(kept[0], da, kept[1], loc)
        return wide_attend_back(kept, da, query_pos, key_pos)

    def project(attended, made, mlp_out):
        return proj_call(attended, made[1], mlp_out[0], proj_b, wp, wp_oth, wsh)

    def input_grad_of(dqkv, made, dy, dnm):
        return dx_call(dqkv, tab, made[1], dy, dnm, vecs, wq, wq_oth, wsh)

    rows_in, cot_in = inputs[:, 0], cotangent[:, 0]
    made_a = norm_qkv(0, None)
    qkv_a = to_heads(made_a[0])
    mlp_a = mlp(made_a, False)
    (qkv_a,) = tied(mlp_a[0], qkv_a)
    att_a, _ = attend(qkv_a)
    att_a = to_rows(att_a)
    da_a, dy_a = out_back(0, None)
    (att_a,) = tied(dy_a, att_a)
    y_a = project(att_a, made_a, mlp_a)[0]
    da_a = to_heads(tied(y_a, da_a)[0])

    made_b = norm_qkv(1, pass_on(y_a, 1))
    qkv_b_ = to_heads(tied(da_a, made_b[0])[0])
    norms_b = swap(made_b[3])
    mlp_b = mlp(made_b, True)
    (qkv_b_,) = tied((mlp_b[0], norms_b), qkv_b_)
    att_b, kept_b = attend(qkv_b_)
    att_b = to_rows(att_b)
    gt_b = swap(mlp_b[3])
    (da_a,) = tied((gt_b, kept_b[1]), da_a)
    dqkv_a = attend_back(kept_b, da_a)
    (att_b,) = tied(dqkv_a, att_b)
    dqkv_a = to_rows(dqkv_a)
    y_b, *a_b = project(att_b, made_b, mlp_b)

    made_c = norm_qkv(0, pass_on(y_b, 1))
    (dy_a2,) = tied(made_c[1], dy_a)
    _, dnm_a = mlp_back(dy_a2, mlp_b)
    qkv_c = to_heads(made_c[0])
    norms_c = swap(made_c[3])
    a_b_oth = swap(a_b[1])
    (dqkv_a,) = tied((dnm_a, norms_c, a_b_oth), dqkv_a)
    _, dx_a, _ = input_grad_of(dqkv_a, made_b, dy_a, dnm_a)
    got_a = pass_on(dx_a, -1)
    made_c = list(made_c[:2]) + list(tied(dx_a, made_c[2], made_c[3]))
    mlp_c = mlp(made_c, True)
    (got_a,) = tied(mlp_c[0], got_a)
    da_b, dy_b = out_back(1, got_a)
    (qkv_c,) = tied(dy_b, qkv_c)
    da_b = to_heads(da_b)
    att_c, kept_c = attend(qkv_c)
    dy_b_oth, gt_c = swap(dy_b), swap(mlp_c[3])
    (da_b,) = tied((dy_b_oth, gt_c), da_b)
    dqkv_b = attend_back(kept_c, da_b)
    (dy_b2,) = tied(dqkv_b, dy_b)
    dqkv_b = to_rows(dqkv_b)
    du_b, dnm_b = mlp_back(dy_b2, mlp_c)
    du_b_oth = swap(du_b)
    (dqkv_b,) = tied((dnm_b, du_b_oth), dqkv_b)
    back_b, dx_b, sums_b = input_grad_of(dqkv_b, made_c, dy_b, dnm_b)
    got_b = pass_on(dx_b, -1)
    back_b_oth = swap(back_b)
    (got_b,) = tied(back_b_oth, got_b)

    da_c, dy_c = out_back(0, got_b)
    dy_list = [dy_c, dy_b, swap(dy_c), dy_b_oth]
    da_c = to_heads(da_c)
    down_grad, dy_sum = down_grad_call([mlp_b[2], mlp_c[2], gt_b, gt_c], dy_list)
    down_ring = ring_sum(down_grad, (dim,), "ctx")
    next(down_ring)
    token = down_ring.send(dy_sum)
    token = down_ring.send(token)
    (dy_c2,) = tied(token, dy_c)
    du_c, dnm_c = mlp_back(dy_c2, mlp_b)
    token = down_ring.send(dnm_c)
    du_c_oth = swap(du_c)
    (da_c,) = tied((token, du_c_oth), da_c)
    dqkv_c = attend_back(kept_b, da_c)
    token = down_ring.send(dqkv_c)
    dqkv_c = to_rows(dqkv_c)
    (du_c2,) = tied(token, du_c)
    up_grad, du_sum = up_grad_call(
        [made_b[2], made_c[2], norms_b, norms_c], [du_c2, du_b, du_c_oth, du_b_oth]
    )
    up_ring = ring_sum(up_grad, (up_grad.shape[1],), "ctx")
    next(up_ring)
    token = up_ring.send(du_sum)
    token = down_ring.send(token)
    token = up_ring.send(token)
    (dqkv_c,) = tied(token, dqkv_c)
    att_c = to_rows(tied(dqkv_c, att_c)[0])
    back_c, dx_c, sums_c = input_grad_of(dqkv_c, made_b, dy_c, dnm_c)
    back_c_oth = swap(back_c)
    token = down_ring.send(dx_c)
    (att_c,) = tied(token, att_c)
    y_c, *a_c = project(att_c, made_c, mlp_c)
    a_c_oth = swap(a_c[1])
    token = up_ring.send(y_c)
    (back_c2,) = tied(token, back_c)
    attn_grad, attn_sum = attn_grad_call(
        [made_b[2], made_c[2], norms_b, norms_c],
        [a_b[0], a_c[0], a_b_oth, a_c_oth],
        [back_c2, back_b, back_c_oth, back_b_oth],
        dy_list,
    )
    dqkv_sum = attn_sum[:, : 3 * dim]
    attn_ring = ring_sum(attn_grad, (3 * dim, dim), "ctx")
    next(attn_ring)
    token = dqkv_sum
    steps = count + 1
    left = {down_ring: steps - 6, up_ring: steps - 3, attn_ring: steps}
    late = [attn_ring, up_ring, attn_ring, down_ring]
    results = {}

    def turn(ring, token):
        left[ring] -= 1
        made = ring.send(token)
        if left[ring] == 0:
            results[ring] = made
            return token
        return made

    at = 0
    while any(left.values()):
        ring = late[at % len(late)]
        if left[ring]:
            token = turn(ring, token)
        at += 1
        if at == 6:
            middle = token
    (down_grad,) = results[down_ring]
    (up_grad,) = results[up_ring]
    qkv_grad, proj_grad = results[attn_ring]

    norm_sums = tied(middle, sums_b + sums_c)[0]
    norm_own = lax.dynamic_slice_in_dim(norm_sums, my_half * half, half, 1)
    norm_oth = swap(lax.dynamic_slice_in_dim(norm_sums, (1 - my_half) * half, half, 1))

    def own_part(vec):
        size = vec.shape[1] // 2
        return lax.dynamic_slice_in_dim(vec, my_half * size, size, 1).reshape(-1, half)

    small_sums = jnp.concatenate(
        [norm_own + norm_oth, own_part(dy_sum), own_part(dqkv_sum), own_part(du_sum)], axis=0
    )
    small_sums = butterfly_sum(tied(middle, small_sums)[0], "ctx")
    qkv_end = 5 + dqkv_sum.shape[1] // 2 // half
    dy_total = small_sums[4:5]
    pick = lambda yes, no: jnp.where(first_section, yes, no)
    layer_out = jnp.stack([pick(y_c, y_b), pick(y_b, y_c)])[None, :, None]
    input_grad = jnp.stack([pick(dx_b, dx_c), pick(dx_c, dx_b)])[None, :, None]
    return (
        layer_out,
        input_grad,
        qkv_grad[None],
        small_sums[5:qkv_end].reshape(1, -1),
        proj_grad[None],
        dy_total,
        up_grad[None],
        small_sums[qkv_end:].reshape(1, -1),
        down_grad[None],
        dy_total,
        small_sums[0:1],
        small_sums[1:2],
        small_sums[2:3],
        small_sums[3:4],
    )


def solution(mesh):
    in_specs = (
        P(None, "wsh", "ctx", None),
        P(None, "wsh", "ctx", None),
        P(),
        P("section", "wsh", None),
        P("section", "wsh"),
        P("section", "wsh", None),
        P("section", "wsh"),
        P("section", "wsh", None),
        P("section", "wsh"),
        P("section", "wsh", None),
        P("section", "wsh"),
        P("section", "wsh"),
        P("section", "wsh"),
        P("section", "wsh"),
        P("section", "wsh"),
    )
    out_specs = (
        P("section", None, "wsh", "ctx", None),
        P("section", None, "wsh", "ctx", None),
        P("section", "wsh", None),
        P("section", "wsh"),
        P("section", "wsh", None),
        P("section", "wsh"),
        P("section", "wsh", None),
        P("section", "wsh"),
        P("section", "wsh", None),
        P("section", "wsh"),
        P("section", "wsh"),
        P("section", "wsh"),
        P("section", "wsh"),
        P("section", "wsh"),
    )
    return jax.shard_map(body, mesh=mesh, in_specs=in_specs, out_specs=out_specs, check_vma=False)
```

```python
import functools

import jax
import jax.numpy as jnp
from jax import lax
from jax.experimental import pallas as pl
from jax.experimental.pallas import tpu as pltpu
from jax.sharding import PartitionSpec as P

HEADS = 16
ROT = 16
NORM_EPS = 1e-05
ROPE_BASE = 10000.0
MASKED_SCORE = -1e30
LANES = 128
VMEM_LIMIT = 18 * 1024 * 1024
INV_SQRT2 = 0.7071067811865476
INV_SQRT_2PI = 0.3989422804014327

f32 = jnp.float32
bf16 = jnp.bfloat16


def dot_nn(left, right):
    return lax.dot_general(left, right, (((1,), (0,)), ((), ())), preferred_element_type=f32)


def dot_nt(left, right):
    return lax.dot_general(left, right, (((1,), (1,)), ((), ())), preferred_element_type=f32)


def params_of(**extra):
    return dict(
        compiler_params=pltpu.CompilerParams(vmem_limit_bytes=VMEM_LIMIT),
        cost_estimate=pl.CostEstimate(flops=1, bytes_accessed=1, transcendentals=0),
        **extra,
    )


def whole(shape):
    rank = len(shape)
    return pl.BlockSpec(shape, lambda *args: (0,) * rank)


def shape_of(shape, dtype):
    return jax.ShapeDtypeStruct(shape, dtype)


def rope(vals, tab_ref):
    return (
        vals * tab_ref[0]
        + pltpu.roll(vals, LANES - ROT // 2, 1) * tab_ref[1]
        + pltpu.roll(vals, ROT // 2, 1) * tab_ref[2]
    )


def unrope(vals, tab_ref):
    return (
        vals * tab_ref[0]
        - pltpu.roll(vals, LANES - ROT // 2, 1) * tab_ref[1]
        - pltpu.roll(vals, ROT // 2, 1) * tab_ref[2]
    )


def normalized(hidden):
    row_mean = jnp.mean(hidden, axis=-1, keepdims=True)
    centered = hidden - row_mean
    spread = jnp.mean(centered * centered, axis=-1, keepdims=True)
    scale = lax.rsqrt(spread + NORM_EPS)
    return centered * scale, scale


def qkv_kernel(index, own_given, wsh_ref, given_ref, got_ref, vec_ref, bias_ref, tab_ref, *rest):
    w_own, w_oth, out_ref, x_ref, own_ref, oth_ref = rest
    half, width = w_own.shape
    x = given_ref[index]
    if not own_given:
        x = jnp.where(wsh_ref[1] == 1, x, got_ref[...])
    x_ref[...] = x
    xhat, _ = normalized(x.astype(f32))
    na = (xhat * vec_ref[0:1] + vec_ref[1:2]).astype(bf16)
    nm = (xhat * vec_ref[2:3] + vec_ref[3:4]).astype(bf16)
    first = wsh_ref[0] == 0
    for i, rows in enumerate((na, nm)):
        own_ref[i] = jnp.where(first, rows[:, :half], rows[:, half:])
        oth_ref[i] = jnp.where(first, rows[:, half:], rows[:, :half])
    pairs = out_ref.shape[0]
    for at in range(0, width, 2 * LANES):
        cols = slice(at, at + 2 * LANES)
        res = (
            dot_nn(own_ref[0], w_own[:, cols])
            + dot_nn(oth_ref[0], w_oth[:, cols])
            + bias_ref[:, cols]
        )
        for i in range(2):
            part, pair = divmod(at // LANES + i, pairs)
            vals = res[:, i * LANES : (i + 1) * LANES]
            if part < 2:
                vals = rope(vals, tab_ref)
            out_ref[pair, part] = vals.astype(bf16)


def layer_of(shape, index):
    return pl.BlockSpec((pl.squeezed,) + shape, lambda *args: (index, 0, 0))


HERE = pl.BlockSpec(memory_space=pltpu.VMEM)
SCALARS = pl.BlockSpec(memory_space=pltpu.SMEM)
ANYWHERE = pl.BlockSpec(memory_space=pl.ANY)


def local_call(kernel, name, scalars, arrays, out_shape, scratch=()):
    multiple = isinstance(out_shape, (list, tuple))
    return pl.pallas_call(
        kernel,
        in_specs=[SCALARS] * len(scalars) + [HERE] * len(arrays),
        out_specs=[HERE] * len(out_shape) if multiple else HERE,
        out_shape=out_shape,
        scratch_shapes=scratch,
        name=name,
        **params_of(),
    )(*scalars, *arrays)


def qkv_call(given, index, got, vecs, qkv_b, tab, w_own, w_oth, wsh):
    rows, dim = given.shape[1:]
    half = w_own.shape[0]
    pairs = dim // LANES
    return local_call(
        functools.partial(qkv_kernel, index, got is None),
        "qkv_proj",
        [wsh],
        [given, given if got is None else got, vecs, qkv_b, tab, w_own, w_oth],
        [shape_of((pairs, 3, rows, LANES), bf16), shape_of((rows, dim), bf16)]
        + [shape_of((2, rows, half), bf16)] * 2,
    )


FF_TILE = 512


def ff_tiles(wsh_ref, dn_own, dn_oth):
    own = dn_own.shape[0] // FF_TILE
    for t in range(2 * own):
        start = pl.multiple_of(((wsh_ref[0] * own + t) % (2 * own)) * FF_TILE, FF_TILE)
        rows = slice((t % own) * FF_TILE, (t % own + 1) * FF_TILE)
        yield pl.ds(start, FF_TILE), t < own, rows


def mlp_kernel(save, wsh_ref, own_ref, oth_ref, up_b, down_b, up_own, up_oth, dn_own, dn_oth, *outs):
    out_ref = outs[0]
    nm_own, nm_oth = own_ref[1], oth_ref[1]
    out_ref[...] = jnp.broadcast_to(down_b[...], out_ref.shape)
    for place, held, rows in ff_tiles(wsh_ref, dn_own, dn_oth):
        pre = dot_nn(nm_own, up_own[:, place]) + dot_nn(nm_oth, up_oth[:, place]) + up_b[:, place]
        gate = 0.5 + 0.5 * lax.erf(pre * INV_SQRT2)
        act = (pre * gate).astype(bf16)
        if save:
            slope_ref, gt_own, gt_oth = outs[1:]
            slope = gate + pre * (INV_SQRT_2PI * jnp.exp(-0.5 * pre * pre))
            slope_ref[place] = slope.astype(bf16).T
            (gt_own if held else gt_oth)[rows] = act.T
        out_ref[...] += dot_nn(act, (dn_own if held else dn_oth)[rows])


def mlp_call(own, oth, up_b, down_b, up_own, up_oth, dn_own, dn_oth, wsh, save):
    rows = own.shape[1]
    dim = dn_own.shape[1]
    ff = up_own.shape[1]
    out_shape = [shape_of((rows, dim), f32)]
    if save:
        out_shape += [shape_of((ff, rows), bf16)] + [shape_of((ff // 2, rows), bf16)] * 2
    return local_call(
        functools.partial(mlp_kernel, save),
        "mlp_forward",
        [wsh],
        [own, oth, up_b, down_b, up_own, up_oth, dn_own, dn_oth],
        out_shape,
    )


def mlp_back_kernel(wsh_ref, dy_ref, slope_ref, up_own, up_oth, dn_own, dn_oth, du_ref, dnm_ref, *accs):
    half = up_own.shape[0]
    acc_own, acc_oth = accs
    acc_own[...] = jnp.zeros(acc_own.shape, f32)
    acc_oth[...] = jnp.zeros(acc_oth.shape, f32)
    for place, held, rows in ff_tiles(wsh_ref, dn_own, dn_oth):
        dact = dot_nt((dn_own if held else dn_oth)[rows], dy_ref[...])
        du = (dact * slope_ref[place].astype(f32)).astype(bf16)
        du_ref[place] = du
        acc_own[...] += dot_nn(up_own[:, place], du)
        acc_oth[...] += dot_nn(up_oth[:, place], du)
    first = wsh_ref[0] == 0
    dnm_ref[:, :half] = jnp.where(first, acc_own[...], acc_oth[...]).T
    dnm_ref[:, half:] = jnp.where(first, acc_oth[...], acc_own[...]).T


def mlp_back_call(dy, slope, up_own, up_oth, dn_own, dn_oth, wsh):
    rows, dim = dy.shape
    half = up_own.shape[0]
    return local_call(
        mlp_back_kernel,
        "mlp_backward",
        [wsh],
        [dy, slope, up_own, up_oth, dn_own, dn_oth],
        [shape_of(slope.shape, bf16), shape_of((rows, dim), f32)],
        [pltpu.VMEM((half, rows), f32), pltpu.VMEM((half, rows), f32)],
    )


def sort_in(loc_ref, ref, dst, half_rows, part=None):
    for block in range(dst.shape[0] // half_rows):
        place = loc_ref[block]
        rows = pl.ds(pl.multiple_of((place % 2) * half_rows, half_rows), half_rows)
        if part is None:
            vals = ref[place // 2, rows, :]
        else:
            vals = ref[place // 2, part, rows, :]
        dst[block * half_rows : (block + 1) * half_rows] = vals


def sort_out(loc_ref, vals, ref, half_rows, part=None):
    for block in range(vals.shape[0] // half_rows):
        place = loc_ref[block]
        rows = pl.ds(pl.multiple_of((place % 2) * half_rows, half_rows), half_rows)
        piece = vals[block * half_rows : (block + 1) * half_rows]
        if part is None:
            ref[place // 2, rows, :] = piece
        else:
            ref[place // 2, part, rows, :] = piece


def head_of(vals, head):
    lane = lax.broadcasted_iota(jnp.int32, vals.shape, 1)
    return jnp.where(lane // (LANES // 2) == head, vals, jnp.zeros_like(vals))


def scores_of(keys, queries, scale, diagonal):
    scores = dot_nt(keys, queries) * scale
    if diagonal:
        key_at = lax.broadcasted_iota(jnp.int32, scores.shape, 0)
        query_at = lax.broadcasted_iota(jnp.int32, scores.shape, 1)
        scores = jnp.where(key_at <= query_at, scores, MASKED_SCORE)
    return scores


def attend_kernel(tile, loc_ref, qkv_ref, o_ref, lse_ref, q_s, k_s, v_s, vt_s, o_s):
    half_rows = qkv_ref.shape[2] // 2
    seq = q_s.shape[0]
    head_size = LANES // 2
    scale = head_size**-0.5
    sort_in(loc_ref, qkv_ref, q_s, half_rows, 0)
    sort_in(loc_ref, qkv_ref, k_s, half_rows, 1)
    sort_in(loc_ref, qkv_ref, v_s, half_rows, 2)
    vt_s[...] = v_s[...].T
    for t in range(seq // tile):
        rows = slice(t * tile, (t + 1) * tile)
        queries = q_s[rows]
        outs = []
        for head in range(2):
            picked = head_of(queries, head)
            parts = [
                scores_of(k_s[i * tile : (i + 1) * tile], picked, scale, i == t)
                for i in range(t + 1)
            ]
            top = functools.reduce(
                jnp.maximum, [jnp.max(p, axis=0, keepdims=True) for p in parts]
            )
            parts = [jnp.exp(p - top) for p in parts]
            total = sum(jnp.sum(p, axis=0, keepdims=True) for p in parts)
            lse_ref[head : head + 1, rows] = top + jnp.log(total)
            inverse = 1.0 / total
            acc = None
            for i, p in enumerate(parts):
                term = dot_nn(
                    vt_s[head * head_size : (head + 1) * head_size, i * tile : (i + 1) * tile],
                    (p * inverse).astype(bf16),
                )
                acc = term if acc is None else acc + term
            outs.append(acc)
        o_s[rows] = jnp.concatenate(outs, axis=0).T.astype(bf16)
    sort_out(loc_ref, o_s, o_ref, half_rows)


def attend_call(qkv, loc):
    count, _, rows, _ = qkv.shape
    seq = count * rows
    return local_call(
        functools.partial(attend_kernel, 256),
        "attention",
        [loc],
        [qkv],
        [shape_of((count, rows, LANES), bf16), shape_of((2, seq), f32)],
        [
            pltpu.VMEM((seq, LANES), bf16),
            pltpu.VMEM((seq, LANES), bf16),
            pltpu.VMEM((seq, LANES), bf16),
            pltpu.VMEM((LANES, seq), bf16),
            pltpu.VMEM((seq, LANES), bf16),
        ],
    )


def attend_back_kernel(
    tile, loc_ref, qkv_ref, da_ref, lse_ref, out_ref, q_s, k_s, v_s, da_s, kt_s, dq_s, dk_s, dv_s
):
    half_rows = qkv_ref.shape[2] // 2
    seq = q_s.shape[0]
    head_size = LANES // 2
    scale = head_size**-0.5
    sort_in(loc_ref, qkv_ref, q_s, half_rows, 0)
    sort_in(loc_ref, qkv_ref, k_s, half_rows, 1)
    sort_in(loc_ref, qkv_ref, v_s, half_rows, 2)
    sort_in(loc_ref, da_ref, da_s, half_rows)
    kt_s[...] = k_s[...].T
    dk_s[...] = jnp.zeros(dk_s.shape, f32)
    dv_s[...] = jnp.zeros(dv_s.shape, f32)
    for t in range(seq // tile):
        rows = slice(t * tile, (t + 1) * tile)
        outs = []
        for head in range(2):
            queries = head_of(q_s[rows], head)
            grads = head_of(da_s[rows], head)
            lse = lse_ref[head : head + 1, rows]
            probs, dprobs, row_dot = [], [], 0.0
            for i in range(t + 1):
                keys = slice(i * tile, (i + 1) * tile)
                p = jnp.exp(scores_of(k_s[keys], queries, scale, i == t) - lse)
                dp = dot_nt(v_s[keys], grads)
                row_dot = row_dot + jnp.sum(p * dp, axis=0, keepdims=True)
                dv_s[keys] += dot_nn(p.astype(bf16), grads)
                probs.append(p)
                dprobs.append(dp)
            acc = None
            for i in range(t + 1):
                keys = slice(i * tile, (i + 1) * tile)
                ds = (probs[i] * (dprobs[i] - row_dot) * scale).astype(bf16)
                dk_s[keys] += dot_nn(ds, queries)
                term = dot_nn(kt_s[head * head_size : (head + 1) * head_size, keys], ds)
                acc = term if acc is None else acc + term
            outs.append(acc)
        dq_s[rows] = jnp.concatenate(outs, axis=0).T.astype(bf16)
    sort_out(loc_ref, dq_s, out_ref, half_rows, 0)
    k_s[...] = dk_s[...].astype(bf16)
    v_s[...] = dv_s[...].astype(bf16)
    sort_out(loc_ref, k_s, out_ref, half_rows, 1)
    sort_out(loc_ref, v_s, out_ref, half_rows, 2)


def attend_back_call(qkv, da, lse, loc):
    count, _, rows, _ = qkv.shape
    seq = count * rows
    return local_call(
        functools.partial(attend_back_kernel, 256),
        "attention_backward",
        [loc],
        [qkv, da, lse],
        shape_of(qkv.shape, bf16),
        [pltpu.VMEM((seq, LANES), bf16)] * 4
        + [pltpu.VMEM((LANES, seq), bf16), pltpu.VMEM((seq, LANES), bf16)]
        + [pltpu.VMEM((seq, LANES), f32)] * 2,
    )


def by_head(parts):
    pairs, rows, lanes = parts.shape
    return jnp.transpose(parts, (1, 0, 2)).reshape(rows, HEADS, pairs * lanes // HEADS)


def by_pair(heads):
    rows = heads.shape[0]
    return jnp.transpose(heads.reshape(rows, -1, LANES), (1, 0, 2))


def wide_scores(queries, keys, query_pos, key_pos):
    raw = jnp.einsum("qhd,khd->hqk", queries, keys, preferred_element_type=f32)
    allowed = (query_pos[:, None] >= key_pos[None, :])[None]
    return jnp.where(allowed, raw * queries.shape[-1] ** (-0.5), MASKED_SCORE)


def key_blocks(arrays, rows):
    return tuple(a.reshape((a.shape[0] // rows, rows) + a.shape[1:]) for a in arrays)


def wide_attend(qkv, query_pos, key_pos):
    queries = by_head(qkv[:, 0])
    keys = lax.all_gather(by_head(qkv[:, 1]), "ctx", axis=0, tiled=True)
    values = lax.all_gather(by_head(qkv[:, 2]), "ctx", axis=0, tiled=True)
    block = min(512, keys.shape[0])
    split = key_blocks((keys, values, key_pos), block)
    rows, _, head_size = queries.shape

    def max_step(carry, block_in):
        top, total = carry
        scores = wide_scores(queries, block_in[0], query_pos, block_in[2])
        new_top = jnp.maximum(top, jnp.max(scores, axis=-1))
        part = jnp.sum(jnp.exp(scores - new_top[..., None]), axis=-1)
        return ((new_top, total * jnp.exp(top - new_top) + part), None)

    start = (jnp.full((HEADS, rows), MASKED_SCORE, f32), jnp.zeros((HEADS, rows), f32))
    (top, total), _ = lax.scan(max_step, start, split)
    lse = top + jnp.log(total)

    def value_step(running, block_in):
        scores = wide_scores(queries, block_in[0], query_pos, block_in[2])
        probs = jnp.exp(scores - lse[..., None]).astype(bf16)
        term = jnp.einsum("hqk,khd->qhd", probs, block_in[1], preferred_element_type=f32)
        return (running + term, None)

    attended, _ = lax.scan(value_step, jnp.zeros((rows, HEADS, head_size), f32), split)
    return by_pair(attended.astype(bf16)), (queries, keys, values, lse)


def wide_attend_back(kept, da, query_pos, key_pos):
    queries, keys, values, lse = kept
    grads = by_head(da)
    block = min(512, keys.shape[0])
    split = key_blocks((keys, values, key_pos), block)
    scale = queries.shape[-1] ** (-0.5)

    def pieces(block_in):
        scores = wide_scores(queries, block_in[0], query_pos, block_in[2])
        probs = jnp.exp(scores - lse[..., None])
        dprobs = jnp.einsum("qhd,khd->hqk", grads, block_in[1], preferred_element_type=f32)
        return probs, dprobs

    def dot_step(running, block_in):
        probs, dprobs = pieces(block_in)
        return (running + jnp.sum(probs * dprobs, axis=-1), None)

    row_dot, _ = lax.scan(dot_step, jnp.zeros(lse.shape, f32), split)

    def key_step(running, block_in):
        probs, dprobs = pieces(block_in)
        ds = (scale * probs * (dprobs - row_dot[..., None])).astype(bf16)
        running = running + jnp.einsum("hqk,khd->qhd", ds, block_in[0], preferred_element_type=f32)
        dk = jnp.einsum("hqk,qhd->khd", ds, queries, preferred_element_type=f32)
        dv = jnp.einsum("hqk,qhd->khd", probs.astype(bf16), grads, preferred_element_type=f32)
        return (running, (dk.astype(bf16), dv.astype(bf16)))

    dq, (dk, dv) = lax.scan(key_step, jnp.zeros(queries.shape, f32), split)
    dk, dv = (
        lax.psum_scatter(part.reshape(keys.shape), "ctx", scatter_dimension=0, tiled=True)
        for part in (dk, dv)
    )
    return jnp.stack([by_pair(dq.astype(bf16)), by_pair(dk), by_pair(dv)], axis=1)


def lanes_of(ref):
    return jnp.concatenate([ref[i] for i in range(ref.shape[0])], axis=1)


def proj_kernel(half, wsh_ref, a_ref, x_ref, mlp_ref, bias_ref, p_own, p_oth, y_ref, a_own, a_oth):
    first = wsh_ref[0] == 0
    a = lanes_of(a_ref)
    own = jnp.where(first, a[:, :half], a[:, half:])
    oth = jnp.where(first, a[:, half:], a[:, :half])
    a_own[...] = own
    a_oth[...] = oth
    attn = dot_nn(own, p_own[...]) + dot_nn(oth, p_oth[...]) + bias_ref[...]
    y_ref[...] = (x_ref[...].astype(f32) + attn + mlp_ref[...]).astype(bf16)


def proj_call(a, x, mlp, bias, p_own, p_oth, wsh):
    rows, dim = x.shape
    half = p_own.shape[0]
    return local_call(
        functools.partial(proj_kernel, half),
        "attn_out",
        [wsh],
        [a, x, mlp, bias, p_own, p_oth],
        [shape_of((rows, dim), bf16)] + [shape_of((rows, half), bf16)] * 2,
    )


def da_kernel(index, own_given, wsh_ref, given_ref, got_ref, p_own, p_oth, out_ref, dy_ref):
    dy = given_ref[index]
    if not own_given:
        dy = jnp.where(wsh_ref[1] == 1, got_ref[...], dy)
    dy_ref[...] = dy
    wsh = wsh_ref[0]
    count = out_ref.shape[0] // 2
    for place, weight in ((wsh * count, p_own), ((1 - wsh) * count, p_oth)):
        part = dot_nt(dy, weight[...]).astype(bf16)
        for i in range(count):
            out_ref[place + i] = part[:, i * LANES : (i + 1) * LANES]


def da_call(given, index, got, p_own, p_oth, wsh):
    rows, dim = given.shape[1:]
    return local_call(
        functools.partial(da_kernel, index, got is None),
        "attn_out_backward",
        [wsh],
        [given, given if got is None else got, p_own, p_oth],
        [shape_of((dim // LANES, rows, LANES), bf16), shape_of((rows, dim), bf16)],
    )


def dx_kernel(wsh_ref, dqkv_ref, tab_ref, x_ref, dy_ref, dnm_ref, vec_ref, *rest):
    w_own, w_oth, back_ref, dx_ref, sums_ref, grad_s = rest
    pairs = dqkv_ref.shape[0]
    for part in range(3):
        for pair in range(pairs):
            vals = dqkv_ref[pair, part]
            if part < 2:
                vals = unrope(vals.astype(f32), tab_ref).astype(bf16)
            back_ref[pair, part] = vals
            grad_s[:, pl.ds((part * pairs + pair) * LANES, LANES)] = vals
    first = wsh_ref[0] == 0
    own, oth = dot_nt(grad_s[...], w_own[...]), dot_nt(grad_s[...], w_oth[...])
    dna = jnp.concatenate([jnp.where(first, own, oth), jnp.where(first, oth, own)], axis=1)
    dnm = dnm_ref[...]
    xhat, scale = normalized(x_ref[...].astype(f32))
    grad = dna * vec_ref[0:1] + dnm * vec_ref[2:3]
    inner = (
        grad
        - jnp.mean(grad, axis=-1, keepdims=True)
        - xhat * jnp.mean(grad * xhat, axis=-1, keepdims=True)
    )
    dx_ref[...] = (dy_ref[...].astype(f32) + scale * inner).astype(bf16)
    sums_ref[0:1] = jnp.sum(dna * xhat, axis=0, keepdims=True)
    sums_ref[1:2] = jnp.sum(dna, axis=0, keepdims=True)
    sums_ref[2:3] = jnp.sum(dnm * xhat, axis=0, keepdims=True)
    sums_ref[3:4] = jnp.sum(dnm, axis=0, keepdims=True)


def dx_call(dqkv, tab, x, dy, dnm, vecs, w_own, w_oth, wsh):
    rows, dim = x.shape
    return local_call(
        dx_kernel,
        "section_input_grad",
        [wsh],
        [dqkv, tab, x, dy, dnm, vecs, w_own, w_oth],
        [shape_of(dqkv.shape, bf16), shape_of((rows, dim), bf16), shape_of((4, dim), f32)],
        [pltpu.VMEM((rows, 3 * dim), bf16)],
    )


def stack_rows(refs, cols=slice(None)):
    return jnp.concatenate([ref[:, cols] for ref in refs], axis=0)


def down_grad_kernel(micros, *refs):
    gt_refs, dy_refs = refs[:micros], refs[micros : 2 * micros]
    out_ref, sum_ref, dy_s = refs[2 * micros :]

    @pl.when(pl.program_id(0) == 0)
    def _():
        dy = stack_rows(dy_refs)
        dy_s[...] = dy
        sum_ref[...] = jnp.sum(dy.astype(f32), axis=0, keepdims=True)

    left = jnp.concatenate([ref[...] for ref in gt_refs], axis=1)
    out_ref[...] = dot_nn(left, dy_s[...]).astype(bf16)


def down_grad_call(gt_list, dy_list):
    ff_rows, rows = gt_list[0].shape
    dim = dy_list[0].shape[1]
    micros = len(dy_list)
    tile = 512
    return pl.pallas_call(
        functools.partial(down_grad_kernel, micros),
        grid=(ff_rows // tile,),
        in_specs=[pl.BlockSpec((tile, rows), lambda j: (j, 0))] * micros
        + [whole((rows, dim))] * micros,
        out_specs=[pl.BlockSpec((tile, dim), lambda j: (j, 0)), whole((1, dim))],
        out_shape=[shape_of((ff_rows, dim), bf16), shape_of((1, dim), f32)],
        scratch_shapes=[pltpu.VMEM((micros * rows, dim), bf16)],
        name="down_grad",
        **params_of(),
    )(*gt_list, *dy_list)


def up_grad_kernel(micros, *refs):
    x_refs, du_refs = refs[:micros], refs[micros : 2 * micros]
    out_ref, sum_ref, xt_s = refs[2 * micros :]

    @pl.when(pl.program_id(0) == 0)
    def _():
        xt_s[...] = stack_rows(x_refs).T

    du = jnp.concatenate([ref[...] for ref in du_refs], axis=1)
    sum_ref[...] = dot_nt(jnp.ones((8, du.shape[1]), bf16), du)[:1]
    out_ref[...] = dot_nt(xt_s[...], du).astype(bf16)


def up_grad_call(x_list, du_list):
    rows, half = x_list[0].shape[1:]
    ff = du_list[0].shape[0]
    micros = len(x_list)
    tile = 1024
    return pl.pallas_call(
        functools.partial(up_grad_kernel, micros),
        grid=(ff // tile,),
        in_specs=[layer_of((rows, half), 1)] * micros
        + [pl.BlockSpec((tile, rows), lambda j: (j, 0))] * micros,
        out_specs=[
            pl.BlockSpec((half, tile), lambda j: (0, j)),
            pl.BlockSpec((1, tile), lambda j: (0, j)),
        ],
        out_shape=[shape_of((half, ff), bf16), shape_of((1, ff), f32)],
        scratch_shapes=[pltpu.VMEM((half, micros * rows), bf16)],
        name="up_grad",
        **params_of(),
    )(*x_list, *du_list)


def attn_grad_kernel(micros, *refs):
    x_refs, a_refs, d_refs, dy_refs = (refs[i * micros : (i + 1) * micros] for i in range(4))
    out_ref, sum_ref, xt_s = refs[4 * micros :]
    part = pl.program_id(0)

    def finish(dy):
        sum_ref[...] = jnp.sum(dy.astype(f32), axis=0, keepdims=True)
        out_ref[...] = dot_nn(xt_s[...], dy).astype(bf16)

    @pl.when(part == 0)
    def _():
        xt_s[...] = stack_rows(x_refs).T

    @pl.when(part < 3)
    def _():
        finish(jnp.concatenate([lanes_of(ref) for ref in d_refs], axis=0))

    @pl.when(part == 3)
    def _():
        xt_s[...] = stack_rows(a_refs).T
        finish(stack_rows(dy_refs))


def attn_grad_call(x_list, a_list, d_list, dy_list):
    rows, half = x_list[0].shape[1:]
    pairs = d_list[0].shape[0]
    dim = pairs * LANES
    micros = len(x_list)
    d_spec = pl.BlockSpec(
        (pairs, pl.squeezed, rows, LANES), lambda j: (0, jnp.minimum(j, 2), 0, 0)
    )
    return pl.pallas_call(
        functools.partial(attn_grad_kernel, micros),
        grid=(4,),
        in_specs=[layer_of((rows, half), 0)] * micros
        + [whole((rows, half))] * micros
        + [d_spec] * micros
        + [whole((rows, dim))] * micros,
        out_specs=[
            pl.BlockSpec((half, dim), lambda j: (0, j)),
            pl.BlockSpec((1, dim), lambda j: (0, j)),
        ],
        out_shape=[shape_of((half, 4 * dim), bf16), shape_of((1, 4 * dim), f32)],
        scratch_shapes=[pltpu.VMEM((half, micros * rows), bf16)],
        name="attn_grad",
        **params_of(),
    )(*x_list, *a_list, *d_list, *dy_list)


def ring_of(count):
    return list(range(0, count, 2)) + list(range(count - 1, 0, -2))


def ring_place(axis):
    count = lax.axis_size(axis)
    me = lax.axis_index(axis)
    return jnp.where(me % 2 == 0, me // 2, count - (me + 1) // 2)


def ring_shift(vals, axis, by):
    order = ring_of(lax.axis_size(axis))
    count = len(order)
    pairs = [(order[i], order[(i + by) % count]) for i in range(count)]
    return lax.ppermute(vals, axis, pairs)


def tied(token, *vals):
    return lax.optimization_barrier((token, vals))[1]


def ring_split_kernel(idx_ref, far_ref, ahead_ref, behind_ref):
    cut = ahead_ref.shape[1]
    ahead_ref[...] = far_ref[:, :cut]
    behind_ref[...] = far_ref[:, cut:]


def ring_add_kernel(partial, idx_ref, mine_a, mine_b, ahead_ref, behind_ref, out_a, out_b):
    def total(left, right):
        return (left.astype(f32) + right.astype(f32)).astype(bf16)

    if partial:
        cut = ahead_ref.shape[1]
        out_a[:, :cut] = total(mine_a[:, :cut], ahead_ref[...])
        out_a[:, cut:] = mine_a[:, cut:]
        out_b[:, :cut] = mine_b[:, :cut]
        out_b[:, cut:] = total(mine_b[:, cut:], behind_ref[...])
    else:
        out_a[...] = total(mine_a[...], ahead_ref[...])
        out_b[...] = total(mine_b[...], behind_ref[...])


def put_copies(chunk, cols, buf, totals, starts, sem):
    lo, hi = cols, cols + buf.shape[1]
    copies = []
    for i, (total, start) in enumerate(zip(totals, starts)):
        first, last = max(lo, start), min(hi, start + total.shape[2])
        if first < last:
            copies.append(
                pltpu.make_async_copy(
                    buf.at[:, pl.ds(first - lo, last - first)],
                    total.at[chunk, :, pl.ds(first - start, last - first)],
                    sem.at[i],
                )
            )
    return copies


def ring_own_kernel(starts, idx_ref, mine_ref, ahead_ref, behind_ref, out_ref, *rest):
    totals, (buf, sems) = rest[:-2], rest[-2:]
    mine = (
        mine_ref[...].astype(f32) + ahead_ref[...].astype(f32) + behind_ref[...].astype(f32)
    ).astype(bf16)
    out_ref[...] = mine
    buf[...] = mine.astype(f32)
    copies = put_copies(idx_ref[0], 0, buf, totals, starts, sems)
    for copy in copies:
        copy.start()
    for copy in copies:
        copy.wait()


def ring_put_kernel(starts, slots, cols, idx_ref, ahead_ref, behind_ref, *rest):
    totals, bufs, sems = rest[len(starts) : 2 * len(starts)], rest[-3:-1], rest[-1]
    copies = []
    for side, ref in enumerate((ahead_ref, behind_ref)):
        bufs[side][...] = ref[...].astype(f32)
        made = put_copies(
            idx_ref[slots[side]], cols[side], bufs[side], totals, starts, sems.at[side]
        )
        for copy in made:
            copy.start()
        copies += made
    for copy in copies:
        copy.wait()


def ring_sum(own, widths, axis):
    count = lax.axis_size(axis)
    half = count // 2
    full_rows, cols = own.shape
    rows = full_rows // count
    own = own.reshape(count, rows, cols)
    cut = cols // 2
    starts = [sum(widths[:i]) for i in range(len(widths))]
    idx = (ring_place(axis) + jnp.arange(count, dtype=jnp.int32)) % count
    chunk, piece = shape_of((rows, cols), bf16), shape_of((rows, cut), bf16)
    sums = [shape_of((count, rows, width), f32) for width in widths]

    def taking(k):
        return pl.BlockSpec((pl.squeezed, rows, cols), lambda j, s: (s[k % count], 0, 0))

    def call(kernel, name, in_specs, out_specs, out_shape, scratch, aliases, *arrays):
        return pl.pallas_call(
            kernel,
            grid_spec=pltpu.PrefetchScalarGridSpec(
                num_scalar_prefetch=1,
                grid=(1,),
                in_specs=in_specs,
                out_specs=out_specs,
                scratch_shapes=scratch,
            ),
            out_shape=out_shape,
            input_output_aliases=aliases,
            name=name,
            **params_of(),
        )(idx, *arrays)

    def put(totals, ahead, behind, k):
        width = ahead.shape[1]
        part_cols = (0, 0) if width == cols else (0, cut)
        return call(
            functools.partial(ring_put_kernel, starts, ((-k) % count, k % count), part_cols),
            "ring_put",
            [HERE, HERE] + [ANYWHERE] * len(sums),
            [ANYWHERE] * len(sums),
            sums,
            [pltpu.VMEM((rows, width), f32)] * 2 + [pltpu.SemaphoreType.DMA((2, len(sums)))],
            {3 + i: i for i in range(len(sums))},
            ahead,
            behind,
            *totals,
        )

    token = yield None
    (own,) = tied(token, own)
    ahead, behind = call(
        ring_split_kernel, "ring_split", [taking(half)], [HERE, HERE], [piece, piece], [], {}, own
    )
    token = behind
    ahead, behind = ring_shift(ahead, axis, 1), ring_shift(behind, axis, -1)
    token = yield token
    for k in range(half - 1, 0, -1):
        ahead, behind = tied(token, ahead, behind)
        ahead, behind = call(
            functools.partial(ring_add_kernel, k == half - 1),
            "ring_add",
            [taking(k), taking(-k), HERE, HERE],
            [HERE, HERE],
            [chunk, chunk],
            [],
            {},
            own,
            own,
            ahead,
            behind,
        )
        token = behind
        ahead, behind = ring_shift(ahead, axis, 1), ring_shift(behind, axis, -1)
        token = yield token
    ahead, behind = tied(token, ahead, behind)
    mine, *totals = call(
        functools.partial(ring_own_kernel, starts),
        "ring_own",
        [taking(0), HERE, HERE],
        [HERE] + [ANYWHERE] * len(sums),
        [chunk] + sums,
        [pltpu.VMEM((rows, cols), f32), pltpu.SemaphoreType.DMA((len(sums),))],
        {},
        own,
        ahead,
        behind,
    )
    token = mine
    ahead, behind = ring_shift(mine, axis, 1), ring_shift(mine, axis, -1)
    token = yield token
    for k in range(1, half):
        ahead, behind = tied(token, ahead, behind)
        last = k == half - 1
        next_ahead = ring_shift(ahead[:, :cut] if last else ahead, axis, 1)
        next_behind = ring_shift(behind[:, cut:] if last else behind, axis, -1)
        totals = put(totals, ahead, behind, k)
        token = behind
        ahead, behind = next_ahead, next_behind
        token = yield token
    ahead, behind = tied(token, ahead, behind)
    totals = put(totals, ahead, behind, half)
    yield [total.reshape(full_rows, -1) for total in totals]


def butterfly_sum(vals, axis):
    count = lax.axis_size(axis)
    if count & (count - 1):
        return lax.psum(vals, axis)
    by = 1
    while by < count:
        vals = vals + lax.ppermute(vals, axis, [(i, i ^ by) for i in range(count)])
        by *= 2
    return vals


def swap(vals):
    return lax.ppermute(vals, "wsh", [(0, 1), (1, 0)])


def pass_on(vals, by):
    pairs = [(0, 1)] if by > 0 else [(1, 0)]
    return lax.ppermute(vals, "section", pairs)


def block_places(block_pair, count):
    want = jnp.arange(2 * count, dtype=jnp.int32)
    device = jnp.arange(count, dtype=jnp.int32)
    first = (block_pair[None, :] == want[:, None]).astype(jnp.int32)
    second = ((2 * count - 1 - block_pair)[None, :] == want[:, None]).astype(jnp.int32)
    return jnp.sum(first * (2 * device) + second * (2 * device + 1), axis=1)


def row_positions(block_pair, stored, tok_dev):
    count = block_pair.shape[0]
    device = stored // tok_dev
    within = stored % tok_dev
    half_rows = tok_dev // 2
    matches = device[:, None] == jnp.arange(count, dtype=jnp.int32)[None, :]
    pair_block = jnp.sum(jnp.where(matches, block_pair[None, :], 0), axis=1)
    block_idx = jnp.where(within < half_rows, pair_block, 2 * count - 1 - pair_block)
    return block_idx * half_rows + within % half_rows


def rotary_table(positions, head_size):
    half_rot = ROT // 2
    lane = jnp.arange(LANES, dtype=jnp.int32) % head_size
    inv_freq = ROPE_BASE ** (-((lane % half_rot).astype(f32) * 2.0) / ROT)
    angles = positions.astype(f32)[:, None] * inv_freq[None, :]
    cosine, sine = jnp.cos(angles), jnp.sin(angles)
    lead, second = (lane < half_rot)[None], ((lane >= half_rot) & (lane < ROT))[None]
    return jnp.stack(
        [
            jnp.where(lead | second, cosine, 1.0),
            jnp.where(lead, -sine, 0.0),
            jnp.where(second, sine, 0.0),
        ]
    )


def body(
    inputs,
    cotangent,
    block_pair,
    qkv_weight,
    qkv_bias,
    proj_weight,
    proj_bias,
    up_weight,
    up_bias,
    down_weight,
    down_bias,
    attn_gain,
    attn_shift,
    mlp_gain,
    mlp_shift,
):
    first_section = lax.axis_index("section") == 0
    count = lax.axis_size("ctx")
    micros, _, tok_dev, dim = inputs.shape
    head_size = dim // HEADS
    half = dim // 2
    my_half = lax.axis_index("wsh")
    wsh = jnp.stack([my_half.astype(jnp.int32), first_section.astype(jnp.int32)])
    one_pair_each = count == dim // LANES

    wq, wp, wu, wd = (w[0] for w in (qkv_weight, proj_weight, up_weight, down_weight))
    small = jnp.concatenate(
        [
            v[0].reshape(-1, half)
            for v in (
                attn_gain,
                attn_shift,
                mlp_gain,
                mlp_shift,
                proj_bias,
                down_bias,
                qkv_bias,
                up_bias,
            )
        ],
        axis=0,
    )
    small_oth = swap(small)
    wq_oth = swap(wq)
    first_here = lax.optimization_barrier((wq_oth, small_oth))
    wq_oth, small_oth = first_here
    wu_oth = swap(tied(wq_oth, wu)[0])
    wd_oth = swap(tied(wq_oth, wd)[0])
    wp_oth = swap(tied(wu_oth, wp)[0])
    low_part = jnp.where(my_half == 0, small, small_oth).astype(f32)
    high_part = jnp.where(my_half == 0, small_oth, small).astype(f32)
    vecs = jnp.concatenate([low_part[:6], high_part[:6]], axis=1)
    qkv_rows = 6 + qkv_bias.shape[1] // half
    proj_b, down_b = vecs[4:5], vecs[5:6]
    qkv_b = jnp.concatenate([low_part[6:qkv_rows], high_part[6:qkv_rows]], axis=0).reshape(1, -1)
    up_b = jnp.concatenate([low_part[qkv_rows:], high_part[qkv_rows:]], axis=0).reshape(1, -1)

    local_rows = lax.axis_index("ctx") * tok_dev + jnp.arange(tok_dev, dtype=jnp.int32)
    query_pos = row_positions(block_pair, local_rows, tok_dev)
    key_pos = row_positions(block_pair, jnp.arange(count * tok_dev, dtype=jnp.int32), tok_dev)
    tab = rotary_table(query_pos, head_size)
    loc = block_places(block_pair, count)

    def exchange(vals):
        return lax.all_to_all(vals, "ctx", split_axis=0, concat_axis=0, tiled=True)

    def norm_qkv(index, got):
        return qkv_call(rows_in, index, got, vecs, qkv_b, tab, wq, wq_oth, wsh)

    def mlp(made, save):
        return mlp_call(made[2], made[3], up_b, down_b, wu, wu_oth, wd, wd_oth, wsh, save)

    def mlp_back(dy, mlp_kept):
        return mlp_back_call(dy, mlp_kept[1], wu, wu_oth, wd, wd_oth, wsh)

    def out_back(index, got):
        return da_call(cot_in, index, got, wp, wp_oth, wsh)

    def to_heads(vals):
        return exchange(vals) if one_pair_each else vals

    def to_rows(vals):
        return exchange(vals) if one_pair_each else vals

    def attend(qkv):
        if one_pair_each:
            attended, lse = attend_call(qkv, loc)
            return attended, (qkv, lse)
        return wide_attend(qkv, query_pos, key_pos)

    def attend_back(kept, da):
        if one_pair_each:
            return attend_back_call(kept[0], da, kept[1], loc)
        return wide_attend_back(kept, da, query_pos, key_pos)

    def project(attended, made, mlp_out):
        return proj_call(attended, made[1], mlp_out[0], proj_b, wp, wp_oth, wsh)

    def input_grad_of(dqkv, made, dy, dnm):
        return dx_call(dqkv, tab, made[1], dy, dnm, vecs, wq, wq_oth, wsh)

    rows_in, cot_in = inputs[:, 0], cotangent[:, 0]
    made_a = norm_qkv(0, None)
    qkv_a = to_heads(made_a[0])
    mlp_a = mlp(made_a, False)
    (qkv_a,) = tied(mlp_a[0], qkv_a)
    att_a, _ = attend(qkv_a)
    att_a = to_rows(att_a)
    da_a, dy_a = out_back(0, None)
    (att_a,) = tied(dy_a, att_a)
    y_a = project(att_a, made_a, mlp_a)[0]
    da_a = to_heads(tied(y_a, da_a)[0])

    made_b = norm_qkv(1, pass_on(y_a, 1))
    qkv_b_ = to_heads(tied(da_a, made_b[0])[0])
    norms_b = swap(made_b[3])
    mlp_b = mlp(made_b, True)
    (qkv_b_,) = tied((mlp_b[0], norms_b), qkv_b_)
    att_b, kept_b = attend(qkv_b_)
    att_b = to_rows(att_b)
    gt_b = swap(mlp_b[3])
    (da_a,) = tied((gt_b, kept_b[1]), da_a)
    dqkv_a = attend_back(kept_b, da_a)
    (att_b,) = tied(dqkv_a, att_b)
    dqkv_a = to_rows(dqkv_a)
    y_b, *a_b = project(att_b, made_b, mlp_b)

    made_c = norm_qkv(0, pass_on(y_b, 1))
    (dy_a2,) = tied(made_c[1], dy_a)
    _, dnm_a = mlp_back(dy_a2, mlp_b)
    qkv_c = to_heads(made_c[0])
    norms_c = swap(made_c[3])
    a_b_oth = swap(a_b[1])
    (dqkv_a,) = tied((dnm_a, norms_c, a_b_oth), dqkv_a)
    _, dx_a, _ = input_grad_of(dqkv_a, made_b, dy_a, dnm_a)
    got_a = pass_on(dx_a, -1)
    made_c = list(made_c[:2]) + list(tied(dx_a, made_c[2], made_c[3]))
    mlp_c = mlp(made_c, True)
    (got_a,) = tied(mlp_c[0], got_a)
    da_b, dy_b = out_back(1, got_a)
    (qkv_c,) = tied(dy_b, qkv_c)
    da_b = to_heads(tied(qkv_c, da_b)[0])
    att_c, kept_c = attend(qkv_c)
    dy_b_oth, gt_c = swap(dy_b), swap(mlp_c[3])
    (da_b,) = tied((dy_b_oth, gt_c), da_b)
    dqkv_b = attend_back(kept_c, da_b)
    (dy_b2,) = tied(dqkv_b, dy_b)
    dqkv_b = to_rows(dqkv_b)
    du_b, dnm_b = mlp_back(dy_b2, mlp_c)
    du_b_oth = swap(du_b)
    (dqkv_b,) = tied((dnm_b, du_b_oth), dqkv_b)
    back_b, dx_b, sums_b = input_grad_of(dqkv_b, made_c, dy_b, dnm_b)
    got_b = pass_on(dx_b, -1)
    back_b_oth = swap(back_b)
    (got_b,) = tied(back_b_oth, got_b)

    da_c, dy_c = out_back(0, got_b)
    dy_list = [dy_c, dy_b, swap(dy_c), dy_b_oth]
    da_c = to_heads(da_c)
    down_grad, dy_sum = down_grad_call([mlp_b[2], mlp_c[2], gt_b, gt_c], dy_list)
    down_ring = ring_sum(down_grad, (dim,), "ctx")
    next(down_ring)
    token = down_ring.send(dy_sum)
    token = down_ring.send(token)
    (dy_c2,) = tied(token, dy_c)
    du_c, dnm_c = mlp_back(dy_c2, mlp_b)
    token = down_ring.send(dnm_c)
    du_c_oth = swap(du_c)
    (da_c,) = tied((token, du_c_oth), da_c)
    dqkv_c = attend_back(kept_b, da_c)
    token = down_ring.send(dqkv_c)
    dqkv_c = to_rows(dqkv_c)
    (du_c2,) = tied(token, du_c)
    up_grad, du_sum = up_grad_call(
        [made_b[2], made_c[2], norms_b, norms_c], [du_c2, du_b, du_c_oth, du_b_oth]
    )
    up_ring = ring_sum(up_grad, (up_grad.shape[1],), "ctx")
    next(up_ring)
    token = up_ring.send(du_sum)
    token = down_ring.send(token)
    token = up_ring.send(token)
    (dqkv_c,) = tied(token, dqkv_c)
    att_c = to_rows(tied(dqkv_c, att_c)[0])
    back_c, dx_c, sums_c = input_grad_of(dqkv_c, made_b, dy_c, dnm_c)
    back_c_oth = swap(back_c)
    token = down_ring.send(dx_c)
    (att_c,) = tied(token, att_c)
    y_c, *a_c = project(att_c, made_c, mlp_c)
    a_c_oth = swap(a_c[1])
    token = up_ring.send(y_c)
    (back_c2,) = tied(token, back_c)
    attn_grad, attn_sum = attn_grad_call(
        [made_b[2], made_c[2], norms_b, norms_c],
        [a_b[0], a_c[0], a_b_oth, a_c_oth],
        [back_c2, back_b, back_c_oth, back_b_oth],
        dy_list,
    )
    dqkv_sum = attn_sum[:, : 3 * dim]
    attn_ring = ring_sum(attn_grad, (3 * dim, dim), "ctx")
    next(attn_ring)
    token = dqkv_sum
    steps = count + 1
    left = {down_ring: steps - 6, up_ring: steps - 3, attn_ring: steps}
    late = [attn_ring, up_ring, attn_ring, down_ring]
    results = {}

    def turn(ring, token):
        left[ring] -= 1
        made = ring.send(token)
        if left[ring] == 0:
            results[ring] = made
            return token
        return made

    at = 0
    while any(left.values()):
        ring = late[at % len(late)]
        if left[ring]:
            token = turn(ring, token)
        at += 1
        if at == 6:
            middle = token
    (down_grad,) = results[down_ring]
    (up_grad,) = results[up_ring]
    qkv_grad, proj_grad = results[attn_ring]

    norm_sums = tied(middle, sums_b + sums_c)[0]
    norm_own = lax.dynamic_slice_in_dim(norm_sums, my_half * half, half, 1)
    norm_oth = swap(lax.dynamic_slice_in_dim(norm_sums, (1 - my_half) * half, half, 1))

    def own_part(vec):
        size = vec.shape[1] // 2
        return lax.dynamic_slice_in_dim(vec, my_half * size, size, 1).reshape(-1, half)

    small_sums = jnp.concatenate(
        [norm_own + norm_oth, own_part(dy_sum), own_part(dqkv_sum), own_part(du_sum)], axis=0
    )
    small_sums = butterfly_sum(tied(middle, small_sums)[0], "ctx")
    qkv_end = 5 + dqkv_sum.shape[1] // 2 // half
    dy_total = small_sums[4:5]
    pick = lambda yes, no: jnp.where(first_section, yes, no)
    layer_out = jnp.stack([pick(y_c, y_b), pick(y_b, y_c)])[None, :, None]
    input_grad = jnp.stack([pick(dx_b, dx_c), pick(dx_c, dx_b)])[None, :, None]
    return (
        layer_out,
        input_grad,
        qkv_grad[None],
        small_sums[5:qkv_end].reshape(1, -1),
        proj_grad[None],
        dy_total,
        up_grad[None],
        small_sums[qkv_end:].reshape(1, -1),
        down_grad[None],
        dy_total,
        small_sums[0:1],
        small_sums[1:2],
        small_sums[2:3],
        small_sums[3:4],
    )


def solution(mesh):
    in_specs = (
        P(None, "wsh", "ctx", None),
        P(None, "wsh", "ctx", None),
        P(),
        P("section", "wsh", None),
        P("section", "wsh"),
        P("section", "wsh", None),
        P("section", "wsh"),
        P("section", "wsh", None),
        P("section", "wsh"),
        P("section", "wsh", None),
        P("section", "wsh"),
        P("section", "wsh"),
        P("section", "wsh"),
        P("section", "wsh"),
        P("section", "wsh"),
    )
    out_specs = (
        P("section", None, "wsh", "ctx", None),
        P("section", None, "wsh", "ctx", None),
        P("section", "wsh", None),
        P("section", "wsh"),
        P("section", "wsh", None),
        P("section", "wsh"),
        P("section", "wsh", None),
        P("section", "wsh"),
        P("section", "wsh", None),
        P("section", "wsh"),
        P("section", "wsh"),
        P("section", "wsh"),
        P("section", "wsh"),
        P("section", "wsh"),
    )
    return jax.shard_map(body, mesh=mesh, in_specs=in_specs, out_specs=out_specs, check_vma=False)
```

```python
import functools

import jax
import jax.numpy as jnp
from jax import lax
from jax.experimental import pallas as pl
from jax.experimental.pallas import tpu as pltpu
from jax.sharding import PartitionSpec as P

HEADS = 16
ROT = 16
NORM_EPS = 1e-05
ROPE_BASE = 10000.0
MASKED_SCORE = -1e30
LANES = 128
VMEM_LIMIT = 26 * 1024 * 1024
INV_SQRT2 = 0.7071067811865476
INV_SQRT_2PI = 0.3989422804014327

f32 = jnp.float32
bf16 = jnp.bfloat16


def dot_nn(left, right):
    return lax.dot_general(left, right, (((1,), (0,)), ((), ())), preferred_element_type=f32)


def dot_nt(left, right):
    return lax.dot_general(left, right, (((1,), (1,)), ((), ())), preferred_element_type=f32)


def params_of(**extra):
    return dict(
        compiler_params=pltpu.CompilerParams(vmem_limit_bytes=VMEM_LIMIT),
        cost_estimate=pl.CostEstimate(flops=1, bytes_accessed=1, transcendentals=0),
        **extra,
    )


def whole(shape):
    rank = len(shape)
    return pl.BlockSpec(shape, lambda *args: (0,) * rank)


def shape_of(shape, dtype):
    return jax.ShapeDtypeStruct(shape, dtype)


def rope(vals, tab_ref):
    return (
        vals * tab_ref[0]
        + pltpu.roll(vals, LANES - ROT // 2, 1) * tab_ref[1]
        + pltpu.roll(vals, ROT // 2, 1) * tab_ref[2]
    )


def unrope(vals, tab_ref):
    return (
        vals * tab_ref[0]
        - pltpu.roll(vals, LANES - ROT // 2, 1) * tab_ref[1]
        - pltpu.roll(vals, ROT // 2, 1) * tab_ref[2]
    )


def normalized(hidden):
    row_mean = jnp.mean(hidden, axis=-1, keepdims=True)
    centered = hidden - row_mean
    spread = jnp.mean(centered * centered, axis=-1, keepdims=True)
    scale = lax.rsqrt(spread + NORM_EPS)
    return centered * scale, scale


def start_all(copies):
    for copy in copies:
        copy.start()
    return copies


def wait_all(copies):
    for copy in copies:
        copy.wait()


def qkv_kernel(index, own_given, wsh_ref, given_ref, got_ref, vec_ref, bias_ref, tab_ref, *rest):
    w_own, w_oth, out_ref, x_ref, own_ref, oth_ref, buf, sems = rest
    half, dim = buf.shape[2:]
    copies = start_all(
        [
            pltpu.make_async_copy(
                weight.at[:, pl.ds(part * dim, dim)], buf.at[part, side], sems.at[part, side]
            )
            for part in range(3)
            for side, weight in enumerate((w_own, w_oth))
        ]
    )
    x = given_ref[index]
    if not own_given:
        x = jnp.where(wsh_ref[1] == 1, x, got_ref[...])
    x_ref[...] = x
    xhat, _ = normalized(x.astype(f32))
    na = (xhat * vec_ref[0:1] + vec_ref[1:2]).astype(bf16)
    nm = (xhat * vec_ref[2:3] + vec_ref[3:4]).astype(bf16)
    first = wsh_ref[0] == 0
    for i, rows in enumerate((na, nm)):
        own_ref[i] = jnp.where(first, rows[:, :half], rows[:, half:])
        oth_ref[i] = jnp.where(first, rows[:, half:], rows[:, :half])
    for part in range(3):
        wait_all(copies[2 * part : 2 * part + 2])
        for at in range(0, dim, 2 * LANES):
            cols = slice(at, at + 2 * LANES)
            res = (
                dot_nn(own_ref[0], buf[part, 0, :, cols])
                + dot_nn(oth_ref[0], buf[part, 1, :, cols])
                + bias_ref[:, part * dim + at : part * dim + at + 2 * LANES]
            )
            for i in range(2):
                vals = res[:, i * LANES : (i + 1) * LANES]
                if part < 2:
                    vals = rope(vals, tab_ref)
                out_ref[at // LANES + i, part] = vals.astype(bf16)


def layer_of(shape, index):
    return pl.BlockSpec((pl.squeezed,) + shape, lambda *args: (index, 0, 0))


HERE = pl.BlockSpec(memory_space=pltpu.VMEM)
SCALARS = pl.BlockSpec(memory_space=pltpu.SMEM)
ANYWHERE = pl.BlockSpec(memory_space=pl.ANY)


def local_call(kernel, name, scalars, arrays, weights, out_shape, scratch=()):
    multiple = isinstance(out_shape, (list, tuple))
    return pl.pallas_call(
        kernel,
        in_specs=[SCALARS] * len(scalars) + [HERE] * len(arrays) + [ANYWHERE] * len(weights),
        out_specs=[HERE] * len(out_shape) if multiple else HERE,
        out_shape=out_shape,
        scratch_shapes=scratch,
        name=name,
        **params_of(),
    )(*scalars, *arrays, *weights)


def qkv_call(given, index, got, vecs, qkv_b, tab, w_own, w_oth, wsh):
    rows, dim = given.shape[1:]
    half = w_own.shape[0]
    pairs = dim // LANES
    return local_call(
        functools.partial(qkv_kernel, index, got is None),
        "qkv_proj",
        [wsh],
        [given, given if got is None else got, vecs, qkv_b, tab],
        [w_own, w_oth],
        [shape_of((pairs, 3, rows, LANES), bf16), shape_of((rows, dim), bf16)]
        + [shape_of((2, rows, half), bf16)] * 2,
        [pltpu.VMEM((3, 2, half, dim), bf16), pltpu.SemaphoreType.DMA((3, 2))],
    )


FF_TILE = 512


def ff_tiles(wsh_ref, up_own, up_oth, dn_own, dn_oth, up_buf, dn_buf, sems):
    own = dn_own.shape[0] // FF_TILE
    tiles = []
    for t in range(2 * own):
        start = pl.multiple_of(((wsh_ref[0] * own + t) % (2 * own)) * FF_TILE, FF_TILE)
        place = pl.ds(start, FF_TILE)
        down = (dn_own if t < own else dn_oth).at[pl.ds((t % own) * FF_TILE, FF_TILE)]
        copies = [
            pltpu.make_async_copy(up_own.at[:, place], up_buf.at[t, 0], sems.at[t, 0]),
            pltpu.make_async_copy(up_oth.at[:, place], up_buf.at[t, 1], sems.at[t, 1]),
            pltpu.make_async_copy(down, dn_buf.at[t], sems.at[t, 2]),
        ]
        start_all(copies)
        tiles.append((t, place, t < own, slice((t % own) * FF_TILE, (t % own + 1) * FF_TILE), copies))
    for t, place, held, rows, copies in tiles:
        wait_all(copies)
        yield t, place, held, rows


def ff_scratch(half, ff, dim):
    tiles = ff // FF_TILE
    return [
        pltpu.VMEM((tiles, 2, half, FF_TILE), bf16),
        pltpu.VMEM((tiles, FF_TILE, dim), bf16),
        pltpu.SemaphoreType.DMA((tiles, 3)),
    ]


def mlp_kernel(save, wsh_ref, own_ref, oth_ref, up_b, down_b, *rest):
    weights, outs, (up_buf, dn_buf, sems) = rest[:4], rest[4:-3], rest[-3:]
    out_ref = outs[0]
    out_ref[...] = jnp.broadcast_to(down_b[...], out_ref.shape)
    for t, place, held, rows in ff_tiles(wsh_ref, *weights, up_buf, dn_buf, sems):
        pre = dot_nn(own_ref[1], up_buf[t, 0]) + dot_nn(oth_ref[1], up_buf[t, 1]) + up_b[:, place]
        gate = 0.5 + 0.5 * lax.erf(pre * INV_SQRT2)
        act = (pre * gate).astype(bf16)
        if save:
            slope_ref, gt_own, gt_oth = outs[1:]
            slope = gate + pre * (INV_SQRT_2PI * jnp.exp(-0.5 * pre * pre))
            slope_ref[place] = slope.astype(bf16).T
            (gt_own if held else gt_oth)[rows] = act.T
        out_ref[...] += dot_nn(act, dn_buf[t])


def mlp_call(own, oth, up_b, down_b, up_own, up_oth, dn_own, dn_oth, wsh, save):
    rows, half = own.shape[1:]
    dim = dn_own.shape[1]
    ff = up_own.shape[1]
    out_shape = [shape_of((rows, dim), f32)]
    if save:
        out_shape += [shape_of((ff, rows), bf16)] + [shape_of((ff // 2, rows), bf16)] * 2
    return local_call(
        functools.partial(mlp_kernel, save),
        "mlp_forward",
        [wsh],
        [own, oth, up_b, down_b],
        [up_own, up_oth, dn_own, dn_oth],
        out_shape,
        ff_scratch(half, ff, dim),
    )


def mlp_back_kernel(wsh_ref, dy_ref, slope_ref, *rest):
    weights, (du_ref, dnm_ref, acc_own, acc_oth, up_buf, dn_buf, sems) = rest[:4], rest[4:]
    half = acc_own.shape[0]
    acc_own[...] = jnp.zeros(acc_own.shape, f32)
    acc_oth[...] = jnp.zeros(acc_oth.shape, f32)
    for t, place, _, _ in ff_tiles(wsh_ref, *weights, up_buf, dn_buf, sems):
        dact = dot_nt(dn_buf[t], dy_ref[...])
        du = (dact * slope_ref[place].astype(f32)).astype(bf16)
        du_ref[place] = du
        acc_own[...] += dot_nn(up_buf[t, 0], du)
        acc_oth[...] += dot_nn(up_buf[t, 1], du)
    first = wsh_ref[0] == 0
    dnm_ref[:, :half] = jnp.where(first, acc_own[...], acc_oth[...]).T
    dnm_ref[:, half:] = jnp.where(first, acc_oth[...], acc_own[...]).T


def mlp_back_call(dy, slope, up_own, up_oth, dn_own, dn_oth, wsh):
    rows, dim = dy.shape
    half, ff = up_own.shape
    return local_call(
        mlp_back_kernel,
        "mlp_backward",
        [wsh],
        [dy, slope],
        [up_own, up_oth, dn_own, dn_oth],
        [shape_of(slope.shape, bf16), shape_of((rows, dim), f32)],
        [pltpu.VMEM((half, rows), f32), pltpu.VMEM((half, rows), f32)] + ff_scratch(half, ff, dim),
    )


def sort_in(loc_ref, ref, dst, half_rows, part=None):
    for block in range(dst.shape[0] // half_rows):
        place = loc_ref[block]
        rows = pl.ds(pl.multiple_of((place % 2) * half_rows, half_rows), half_rows)
        if part is None:
            vals = ref[place // 2, rows, :]
        else:
            vals = ref[place // 2, part, rows, :]
        dst[block * half_rows : (block + 1) * half_rows] = vals


def sort_out(loc_ref, vals, ref, half_rows, part=None):
    for block in range(vals.shape[0] // half_rows):
        place = loc_ref[block]
        rows = pl.ds(pl.multiple_of((place % 2) * half_rows, half_rows), half_rows)
        piece = vals[block * half_rows : (block + 1) * half_rows]
        if part is None:
            ref[place // 2, rows, :] = piece
        else:
            ref[place // 2, part, rows, :] = piece


def head_of(vals, head):
    lane = lax.broadcasted_iota(jnp.int32, vals.shape, 1)
    return jnp.where(lane // (LANES // 2) == head, vals, jnp.zeros_like(vals))


def scores_of(keys, queries, scale, diagonal):
    scores = dot_nt(keys, queries) * scale
    if diagonal:
        key_at = lax.broadcasted_iota(jnp.int32, scores.shape, 0)
        query_at = lax.broadcasted_iota(jnp.int32, scores.shape, 1)
        scores = jnp.where(key_at <= query_at, scores, MASKED_SCORE)
    return scores


def attend_kernel(tile, loc_ref, qkv_ref, o_ref, lse_ref, q_s, k_s, v_s, vt_s, o_s):
    half_rows = qkv_ref.shape[2] // 2
    seq = q_s.shape[0]
    head_size = LANES // 2
    scale = head_size**-0.5
    sort_in(loc_ref, qkv_ref, q_s, half_rows, 0)
    sort_in(loc_ref, qkv_ref, k_s, half_rows, 1)
    sort_in(loc_ref, qkv_ref, v_s, half_rows, 2)
    vt_s[...] = v_s[...].T
    for t in range(seq // tile):
        rows = slice(t * tile, (t + 1) * tile)
        queries = q_s[rows]
        outs = []
        for head in range(2):
            picked = head_of(queries, head)
            parts = [
                scores_of(k_s[i * tile : (i + 1) * tile], picked, scale, i == t)
                for i in range(t + 1)
            ]
            top = functools.reduce(
                jnp.maximum, [jnp.max(p, axis=0, keepdims=True) for p in parts]
            )
            parts = [jnp.exp(p - top) for p in parts]
            total = sum(jnp.sum(p, axis=0, keepdims=True) for p in parts)
            lse_ref[head : head + 1, rows] = top + jnp.log(total)
            inverse = 1.0 / total
            acc = None
            for i, p in enumerate(parts):
                term = dot_nn(
                    vt_s[head * head_size : (head + 1) * head_size, i * tile : (i + 1) * tile],
                    (p * inverse).astype(bf16),
                )
                acc = term if acc is None else acc + term
            outs.append(acc)
        o_s[rows] = jnp.concatenate(outs, axis=0).T.astype(bf16)
    sort_out(loc_ref, o_s, o_ref, half_rows)


def attend_call(qkv, loc):
    count, _, rows, _ = qkv.shape
    seq = count * rows
    return local_call(
        functools.partial(attend_kernel, 256),
        "attention",
        [loc],
        [qkv],
        [],
        [shape_of((count, rows, LANES), bf16), shape_of((2, seq), f32)],
        [
            pltpu.VMEM((seq, LANES), bf16),
            pltpu.VMEM((seq, LANES), bf16),
            pltpu.VMEM((seq, LANES), bf16),
            pltpu.VMEM((LANES, seq), bf16),
            pltpu.VMEM((seq, LANES), bf16),
        ],
    )


def attend_back_kernel(
    tile, loc_ref, qkv_ref, da_ref, lse_ref, out_ref, q_s, k_s, v_s, da_s, kt_s, dq_s, dk_s, dv_s
):
    half_rows = qkv_ref.shape[2] // 2
    seq = q_s.shape[0]
    head_size = LANES // 2
    scale = head_size**-0.5
    sort_in(loc_ref, qkv_ref, q_s, half_rows, 0)
    sort_in(loc_ref, qkv_ref, k_s, half_rows, 1)
    sort_in(loc_ref, qkv_ref, v_s, half_rows, 2)
    sort_in(loc_ref, da_ref, da_s, half_rows)
    kt_s[...] = k_s[...].T
    dk_s[...] = jnp.zeros(dk_s.shape, f32)
    dv_s[...] = jnp.zeros(dv_s.shape, f32)
    for t in range(seq // tile):
        rows = slice(t * tile, (t + 1) * tile)
        outs = []
        for head in range(2):
            queries = head_of(q_s[rows], head)
            grads = head_of(da_s[rows], head)
            lse = lse_ref[head : head + 1, rows]
            probs, dprobs, row_dot = [], [], 0.0
            for i in range(t + 1):
                keys = slice(i * tile, (i + 1) * tile)
                p = jnp.exp(scores_of(k_s[keys], queries, scale, i == t) - lse)
                dp = dot_nt(v_s[keys], grads)
                row_dot = row_dot + jnp.sum(p * dp, axis=0, keepdims=True)
                dv_s[keys] += dot_nn(p.astype(bf16), grads)
                probs.append(p)
                dprobs.append(dp)
            acc = None
            for i in range(t + 1):
                keys = slice(i * tile, (i + 1) * tile)
                ds = (probs[i] * (dprobs[i] - row_dot) * scale).astype(bf16)
                dk_s[keys] += dot_nn(ds, queries)
                term = dot_nn(kt_s[head * head_size : (head + 1) * head_size, keys], ds)
                acc = term if acc is None else acc + term
            outs.append(acc)
        dq_s[rows] = jnp.concatenate(outs, axis=0).T.astype(bf16)
    sort_out(loc_ref, dq_s, out_ref, half_rows, 0)
    k_s[...] = dk_s[...].astype(bf16)
    v_s[...] = dv_s[...].astype(bf16)
    sort_out(loc_ref, k_s, out_ref, half_rows, 1)
    sort_out(loc_ref, v_s, out_ref, half_rows, 2)


def attend_back_call(qkv, da, lse, loc):
    count, _, rows, _ = qkv.shape
    seq = count * rows
    return local_call(
        functools.partial(attend_back_kernel, 256),
        "attention_backward",
        [loc],
        [qkv, da, lse],
        [],
        shape_of(qkv.shape, bf16),
        [pltpu.VMEM((seq, LANES), bf16)] * 4
        + [pltpu.VMEM((LANES, seq), bf16), pltpu.VMEM((seq, LANES), bf16)]
        + [pltpu.VMEM((seq, LANES), f32)] * 2,
    )


def by_head(parts):
    pairs, rows, lanes = parts.shape
    return jnp.transpose(parts, (1, 0, 2)).reshape(rows, HEADS, pairs * lanes // HEADS)


def by_pair(heads):
    rows = heads.shape[0]
    return jnp.transpose(heads.reshape(rows, -1, LANES), (1, 0, 2))


def wide_scores(queries, keys, query_pos, key_pos):
    raw = jnp.einsum("qhd,khd->hqk", queries, keys, preferred_element_type=f32)
    allowed = (query_pos[:, None] >= key_pos[None, :])[None]
    return jnp.where(allowed, raw * queries.shape[-1] ** (-0.5), MASKED_SCORE)


def key_blocks(arrays, rows):
    return tuple(a.reshape((a.shape[0] // rows, rows) + a.shape[1:]) for a in arrays)


def wide_attend(qkv, query_pos, key_pos):
    queries = by_head(qkv[:, 0])
    keys = lax.all_gather(by_head(qkv[:, 1]), "ctx", axis=0, tiled=True)
    values = lax.all_gather(by_head(qkv[:, 2]), "ctx", axis=0, tiled=True)
    block = min(512, keys.shape[0])
    split = key_blocks((keys, values, key_pos), block)
    rows, _, head_size = queries.shape

    def max_step(carry, block_in):
        top, total = carry
        scores = wide_scores(queries, block_in[0], query_pos, block_in[2])
        new_top = jnp.maximum(top, jnp.max(scores, axis=-1))
        part = jnp.sum(jnp.exp(scores - new_top[..., None]), axis=-1)
        return ((new_top, total * jnp.exp(top - new_top) + part), None)

    start = (jnp.full((HEADS, rows), MASKED_SCORE, f32), jnp.zeros((HEADS, rows), f32))
    (top, total), _ = lax.scan(max_step, start, split)
    lse = top + jnp.log(total)

    def value_step(running, block_in):
        scores = wide_scores(queries, block_in[0], query_pos, block_in[2])
        probs = jnp.exp(scores - lse[..., None]).astype(bf16)
        term = jnp.einsum("hqk,khd->qhd", probs, block_in[1], preferred_element_type=f32)
        return (running + term, None)

    attended, _ = lax.scan(value_step, jnp.zeros((rows, HEADS, head_size), f32), split)
    return by_pair(attended.astype(bf16)), (queries, keys, values, lse)


def wide_attend_back(kept, da, query_pos, key_pos):
    queries, keys, values, lse = kept
    grads = by_head(da)
    block = min(512, keys.shape[0])
    split = key_blocks((keys, values, key_pos), block)
    scale = queries.shape[-1] ** (-0.5)

    def pieces(block_in):
        scores = wide_scores(queries, block_in[0], query_pos, block_in[2])
        probs = jnp.exp(scores - lse[..., None])
        dprobs = jnp.einsum("qhd,khd->hqk", grads, block_in[1], preferred_element_type=f32)
        return probs, dprobs

    def dot_step(running, block_in):
        probs, dprobs = pieces(block_in)
        return (running + jnp.sum(probs * dprobs, axis=-1), None)

    row_dot, _ = lax.scan(dot_step, jnp.zeros(lse.shape, f32), split)

    def key_step(running, block_in):
        probs, dprobs = pieces(block_in)
        ds = (scale * probs * (dprobs - row_dot[..., None])).astype(bf16)
        running = running + jnp.einsum("hqk,khd->qhd", ds, block_in[0], preferred_element_type=f32)
        dk = jnp.einsum("hqk,qhd->khd", ds, queries, preferred_element_type=f32)
        dv = jnp.einsum("hqk,qhd->khd", probs.astype(bf16), grads, preferred_element_type=f32)
        return (running, (dk.astype(bf16), dv.astype(bf16)))

    dq, (dk, dv) = lax.scan(key_step, jnp.zeros(queries.shape, f32), split)
    dk, dv = (
        lax.psum_scatter(part.reshape(keys.shape), "ctx", scatter_dimension=0, tiled=True)
        for part in (dk, dv)
    )
    return jnp.stack([by_pair(dq.astype(bf16)), by_pair(dk), by_pair(dv)], axis=1)


def lanes_of(ref):
    return jnp.concatenate([ref[i] for i in range(ref.shape[0])], axis=1)


def both_halves(w_own, w_oth, buf, sems):
    return start_all(
        [
            pltpu.make_async_copy(weight, buf.at[side], sems.at[side])
            for side, weight in enumerate((w_own, w_oth))
        ]
    )


def half_scratch(weight):
    return [pltpu.VMEM((2,) + weight.shape, bf16), pltpu.SemaphoreType.DMA((2,))]


def proj_kernel(wsh_ref, a_ref, x_ref, mlp_ref, bias_ref, p_own, p_oth, y_ref, a_own, a_oth, buf, sems):
    copies = both_halves(p_own, p_oth, buf, sems)
    half = buf.shape[1]
    first = wsh_ref[0] == 0
    a = lanes_of(a_ref)
    a_own[...] = jnp.where(first, a[:, :half], a[:, half:])
    a_oth[...] = jnp.where(first, a[:, half:], a[:, :half])
    wait_all(copies)
    attn = dot_nn(a_own[...], buf[0]) + dot_nn(a_oth[...], buf[1]) + bias_ref[...]
    y_ref[...] = (x_ref[...].astype(f32) + attn + mlp_ref[...]).astype(bf16)


def proj_call(a, x, mlp, bias, p_own, p_oth, wsh):
    rows, dim = x.shape
    half = p_own.shape[0]
    return local_call(
        proj_kernel,
        "attn_out",
        [wsh],
        [a, x, mlp, bias],
        [p_own, p_oth],
        [shape_of((rows, dim), bf16)] + [shape_of((rows, half), bf16)] * 2,
        half_scratch(p_own),
    )


def da_kernel(index, own_given, wsh_ref, given_ref, got_ref, p_own, p_oth, out_ref, dy_ref, buf, sems):
    copies = both_halves(p_own, p_oth, buf, sems)
    dy = given_ref[index]
    if not own_given:
        dy = jnp.where(wsh_ref[1] == 1, got_ref[...], dy)
    dy_ref[...] = dy
    wsh = wsh_ref[0]
    count = out_ref.shape[0] // 2
    wait_all(copies)
    for place, side in ((wsh * count, 0), ((1 - wsh) * count, 1)):
        part = dot_nt(dy, buf[side]).astype(bf16)
        for i in range(count):
            out_ref[place + i] = part[:, i * LANES : (i + 1) * LANES]


def da_call(given, index, got, p_own, p_oth, wsh):
    rows, dim = given.shape[1:]
    return local_call(
        functools.partial(da_kernel, index, got is None),
        "attn_out_backward",
        [wsh],
        [given, given if got is None else got],
        [p_own, p_oth],
        [shape_of((dim // LANES, rows, LANES), bf16), shape_of((rows, dim), bf16)],
        half_scratch(p_own),
    )


def dx_kernel(wsh_ref, dqkv_ref, tab_ref, x_ref, dy_ref, dnm_ref, vec_ref, *rest):
    w_own, w_oth, back_ref, dx_ref, sums_ref, grad_s, buf, sems = rest
    copies = both_halves(w_own, w_oth, buf, sems)
    pairs = dqkv_ref.shape[0]
    for part in range(3):
        for pair in range(pairs):
            vals = dqkv_ref[pair, part]
            if part < 2:
                vals = unrope(vals.astype(f32), tab_ref).astype(bf16)
            back_ref[pair, part] = vals
            grad_s[:, pl.ds((part * pairs + pair) * LANES, LANES)] = vals
    first = wsh_ref[0] == 0
    copies[0].wait()
    own = dot_nt(grad_s[...], buf[0])
    copies[1].wait()
    oth = dot_nt(grad_s[...], buf[1])
    dna = jnp.concatenate([jnp.where(first, own, oth), jnp.where(first, oth, own)], axis=1)
    dnm = dnm_ref[...]
    xhat, scale = normalized(x_ref[...].astype(f32))
    grad = dna * vec_ref[0:1] + dnm * vec_ref[2:3]
    inner = (
        grad
        - jnp.mean(grad, axis=-1, keepdims=True)
        - xhat * jnp.mean(grad * xhat, axis=-1, keepdims=True)
    )
    dx_ref[...] = (dy_ref[...].astype(f32) + scale * inner).astype(bf16)
    sums_ref[0:1] = jnp.sum(dna * xhat, axis=0, keepdims=True)
    sums_ref[1:2] = jnp.sum(dna, axis=0, keepdims=True)
    sums_ref[2:3] = jnp.sum(dnm * xhat, axis=0, keepdims=True)
    sums_ref[3:4] = jnp.sum(dnm, axis=0, keepdims=True)


def dx_call(dqkv, tab, x, dy, dnm, vecs, w_own, w_oth, wsh):
    rows, dim = x.shape
    return local_call(
        dx_kernel,
        "section_input_grad",
        [wsh],
        [dqkv, tab, x, dy, dnm, vecs],
        [w_own, w_oth],
        [shape_of(dqkv.shape, bf16), shape_of((rows, dim), bf16), shape_of((4, dim), f32)],
        [pltpu.VMEM((rows, 3 * dim), bf16)] + half_scratch(w_own),
    )


def stack_rows(refs, cols=slice(None)):
    return jnp.concatenate([ref[:, cols] for ref in refs], axis=0)


def down_grad_kernel(micros, *refs):
    gt_refs, dy_refs = refs[:micros], refs[micros : 2 * micros]
    out_ref, sum_ref, dy_s = refs[2 * micros :]

    @pl.when(pl.program_id(0) == 0)
    def _():
        dy = stack_rows(dy_refs)
        dy_s[...] = dy
        sum_ref[...] = jnp.sum(dy.astype(f32), axis=0, keepdims=True)

    left = jnp.concatenate([ref[...] for ref in gt_refs], axis=1)
    out_ref[...] = dot_nn(left, dy_s[...]).astype(bf16)


def down_grad_call(gt_list, dy_list):
    ff_rows, rows = gt_list[0].shape
    dim = dy_list[0].shape[1]
    micros = len(dy_list)
    tile = 512
    return pl.pallas_call(
        functools.partial(down_grad_kernel, micros),
        grid=(ff_rows // tile,),
        in_specs=[pl.BlockSpec((tile, rows), lambda j: (j, 0))] * micros
        + [whole((rows, dim))] * micros,
        out_specs=[pl.BlockSpec((tile, dim), lambda j: (j, 0)), whole((1, dim))],
        out_shape=[shape_of((ff_rows, dim), bf16), shape_of((1, dim), f32)],
        scratch_shapes=[pltpu.VMEM((micros * rows, dim), bf16)],
        name="down_grad",
        **params_of(),
    )(*gt_list, *dy_list)


def up_grad_kernel(micros, *refs):
    x_refs, du_refs = refs[:micros], refs[micros : 2 * micros]
    out_ref, sum_ref, xt_s = refs[2 * micros :]

    @pl.when(pl.program_id(0) == 0)
    def _():
        xt_s[...] = stack_rows(x_refs).T

    du = jnp.concatenate([ref[...] for ref in du_refs], axis=1)
    sum_ref[...] = dot_nt(jnp.ones((8, du.shape[1]), bf16), du)[:1]
    out_ref[...] = dot_nt(xt_s[...], du).astype(bf16)


def up_grad_call(x_list, du_list):
    rows, half = x_list[0].shape[1:]
    ff = du_list[0].shape[0]
    micros = len(x_list)
    tile = 1024
    return pl.pallas_call(
        functools.partial(up_grad_kernel, micros),
        grid=(ff // tile,),
        in_specs=[layer_of((rows, half), 1)] * micros
        + [pl.BlockSpec((tile, rows), lambda j: (j, 0))] * micros,
        out_specs=[
            pl.BlockSpec((half, tile), lambda j: (0, j)),
            pl.BlockSpec((1, tile), lambda j: (0, j)),
        ],
        out_shape=[shape_of((half, ff), bf16), shape_of((1, ff), f32)],
        scratch_shapes=[pltpu.VMEM((half, micros * rows), bf16)],
        name="up_grad",
        **params_of(),
    )(*x_list, *du_list)


def attn_grad_kernel(micros, *refs):
    x_refs, a_refs, d_refs, dy_refs = (refs[i * micros : (i + 1) * micros] for i in range(4))
    out_ref, sum_ref, xt_s = refs[4 * micros :]
    part = pl.program_id(0)

    def finish(dy):
        sum_ref[...] = jnp.sum(dy.astype(f32), axis=0, keepdims=True)
        out_ref[...] = dot_nn(xt_s[...], dy).astype(bf16)

    @pl.when(part == 0)
    def _():
        xt_s[...] = stack_rows(x_refs).T

    @pl.when(part < 3)
    def _():
        finish(jnp.concatenate([lanes_of(ref) for ref in d_refs], axis=0))

    @pl.when(part == 3)
    def _():
        xt_s[...] = stack_rows(a_refs).T
        finish(stack_rows(dy_refs))


def attn_grad_call(x_list, a_list, d_list, dy_list):
    rows, half = x_list[0].shape[1:]
    pairs = d_list[0].shape[0]
    dim = pairs * LANES
    micros = len(x_list)
    d_spec = pl.BlockSpec(
        (pairs, pl.squeezed, rows, LANES), lambda j: (0, jnp.minimum(j, 2), 0, 0)
    )
    return pl.pallas_call(
        functools.partial(attn_grad_kernel, micros),
        grid=(4,),
        in_specs=[layer_of((rows, half), 0)] * micros
        + [whole((rows, half))] * micros
        + [d_spec] * micros
        + [whole((rows, dim))] * micros,
        out_specs=[
            pl.BlockSpec((half, dim), lambda j: (0, j)),
            pl.BlockSpec((1, dim), lambda j: (0, j)),
        ],
        out_shape=[shape_of((half, 4 * dim), bf16), shape_of((1, 4 * dim), f32)],
        scratch_shapes=[pltpu.VMEM((half, micros * rows), bf16)],
        name="attn_grad",
        **params_of(),
    )(*x_list, *a_list, *d_list, *dy_list)


def ring_of(count):
    return list(range(0, count, 2)) + list(range(count - 1, 0, -2))


def ring_place(axis):
    count = lax.axis_size(axis)
    me = lax.axis_index(axis)
    return jnp.where(me % 2 == 0, me // 2, count - (me + 1) // 2)


def ring_shift(vals, axis, by):
    order = ring_of(lax.axis_size(axis))
    count = len(order)
    pairs = [(order[i], order[(i + by) % count]) for i in range(count)]
    return lax.ppermute(vals, axis, pairs)


def tied(token, *vals):
    return lax.optimization_barrier((token, vals))[1]


def fetch(idx_ref, slots, own_ref, bufs, sems):
    return start_all(
        [
            pltpu.make_async_copy(own_ref.at[idx_ref[slot]], bufs.at[i], sems.at[i])
            for i, slot in enumerate(slots)
        ]
    )


def ring_split_kernel(slots, idx_ref, own_ref, ahead_ref, behind_ref, bufs, sems):
    wait_all(fetch(idx_ref, slots, own_ref, bufs, sems))
    cut = ahead_ref.shape[1]
    ahead_ref[...] = bufs[0, :, :cut]
    behind_ref[...] = bufs[0, :, cut:]


def ring_add_kernel(slots, idx_ref, ahead_ref, behind_ref, own_ref, out_a, out_b, bufs, sems):
    def total(left, right):
        return (left.astype(f32) + right.astype(f32)).astype(bf16)

    wait_all(fetch(idx_ref, slots, own_ref, bufs, sems))
    cut = ahead_ref.shape[1]
    if cut < out_a.shape[1]:
        out_a[:, :cut] = total(bufs[0, :, :cut], ahead_ref[...])
        out_a[:, cut:] = bufs[0, :, cut:]
        out_b[:, :cut] = bufs[1, :, :cut]
        out_b[:, cut:] = total(bufs[1, :, cut:], behind_ref[...])
    else:
        out_a[...] = total(bufs[0], ahead_ref[...])
        out_b[...] = total(bufs[1], behind_ref[...])


def put_copies(chunk, cols, buf, totals, starts, sem):
    lo, hi = cols, cols + buf.shape[1]
    copies = []
    for i, (total, start) in enumerate(zip(totals, starts)):
        first, last = max(lo, start), min(hi, start + total.shape[2])
        if first < last:
            copies.append(
                pltpu.make_async_copy(
                    buf.at[:, pl.ds(first - lo, last - first)],
                    total.at[chunk, :, pl.ds(first - start, last - first)],
                    sem.at[i],
                )
            )
    return copies


def ring_own_kernel(starts, idx_ref, ahead_ref, behind_ref, own_ref, out_ref, *rest):
    totals, (bufs, sems, wide, put_sems) = rest[:-4], rest[-4:]
    wait_all(fetch(idx_ref, (0,), own_ref, bufs, sems))
    mine = (
        bufs[0].astype(f32) + ahead_ref[...].astype(f32) + behind_ref[...].astype(f32)
    ).astype(bf16)
    out_ref[...] = mine
    wide[...] = mine.astype(f32)
    wait_all(start_all(put_copies(idx_ref[0], 0, wide, totals, starts, put_sems)))


def ring_put_kernel(starts, slots, cols, idx_ref, ahead_ref, behind_ref, *rest):
    totals, bufs, sems = rest[len(starts) : 2 * len(starts)], rest[-3:-1], rest[-1]
    copies = []
    for side, ref in enumerate((ahead_ref, behind_ref)):
        bufs[side][...] = ref[...].astype(f32)
        made = put_copies(
            idx_ref[slots[side]], cols[side], bufs[side], totals, starts, sems.at[side]
        )
        for copy in made:
            copy.start()
        copies += made
    for copy in copies:
        copy.wait()


def ring_sum(own, widths, axis):
    count = lax.axis_size(axis)
    half = count // 2
    full_rows, cols = own.shape
    rows = full_rows // count
    own = own.reshape(count, rows, cols)
    cut = cols // 2
    starts = [sum(widths[:i]) for i in range(len(widths))]
    idx = (ring_place(axis) + jnp.arange(count, dtype=jnp.int32)) % count
    chunk, piece = shape_of((rows, cols), bf16), shape_of((rows, cut), bf16)
    sums = [shape_of((count, rows, width), f32) for width in widths]

    def call(kernel, name, arrays, out_specs, out_shape, scratch, aliases=None):
        return pl.pallas_call(
            kernel,
            in_specs=[SCALARS, HERE, HERE] + [ANYWHERE] * (len(arrays) - 2),
            out_specs=out_specs,
            out_shape=out_shape,
            scratch_shapes=scratch,
            input_output_aliases=aliases or {},
            name=name,
            **params_of(),
        )(idx, *arrays)

    def taken(number):
        return [pltpu.VMEM((number, rows, cols), bf16), pltpu.SemaphoreType.DMA((number,))]

    def put(totals, ahead, behind, k):
        width = ahead.shape[1]
        part_cols = (0, 0) if width == cols else (0, cut)
        return call(
            functools.partial(ring_put_kernel, starts, ((-k) % count, k % count), part_cols),
            "ring_put",
            [ahead, behind, *totals],
            [ANYWHERE] * len(sums),
            sums,
            [pltpu.VMEM((rows, width), f32)] * 2 + [pltpu.SemaphoreType.DMA((2, len(sums)))],
            {3 + i: i for i in range(len(sums))},
        )

    token = yield None
    (own,) = tied(token, own)
    ahead, behind = pl.pallas_call(
        functools.partial(ring_split_kernel, (half,)),
        in_specs=[SCALARS, ANYWHERE],
        out_specs=[HERE, HERE],
        out_shape=[piece, piece],
        scratch_shapes=taken(1),
        name="ring_split",
        **params_of(),
    )(idx, own)
    token = behind
    ahead, behind = ring_shift(ahead, axis, 1), ring_shift(behind, axis, -1)
    token = yield token
    for k in range(half - 1, 0, -1):
        ahead, behind = tied(token, ahead, behind)
        ahead, behind = call(
            functools.partial(ring_add_kernel, (k % count, (-k) % count)),
            "ring_add",
            [ahead, behind, own],
            [HERE, HERE],
            [chunk, chunk],
            taken(2),
        )
        token = behind
        ahead, behind = ring_shift(ahead, axis, 1), ring_shift(behind, axis, -1)
        token = yield token
    ahead, behind = tied(token, ahead, behind)
    mine, *totals = call(
        functools.partial(ring_own_kernel, starts),
        "ring_own",
        [ahead, behind, own],
        [HERE] + [ANYWHERE] * len(sums),
        [chunk] + sums,
        taken(1) + [pltpu.VMEM((rows, cols), f32), pltpu.SemaphoreType.DMA((len(sums),))],
    )
    token = mine
    ahead, behind = ring_shift(mine, axis, 1), ring_shift(mine, axis, -1)
    token = yield token
    for k in range(1, half):
        ahead, behind = tied(token, ahead, behind)
        last = k == half - 1
        next_ahead = ring_shift(ahead[:, :cut] if last else ahead, axis, 1)
        next_behind = ring_shift(behind[:, cut:] if last else behind, axis, -1)
        totals = put(totals, ahead, behind, k)
        token = behind
        ahead, behind = next_ahead, next_behind
        token = yield token
    ahead, behind = tied(token, ahead, behind)
    totals = put(totals, ahead, behind, half)
    yield [total.reshape(full_rows, -1) for total in totals]


def butterfly_sum(vals, axis):
    count = lax.axis_size(axis)
    if count & (count - 1):
        return lax.psum(vals, axis)
    by = 1
    while by < count:
        vals = vals + lax.ppermute(vals, axis, [(i, i ^ by) for i in range(count)])
        by *= 2
    return vals


def swap(vals):
    return lax.ppermute(vals, "wsh", [(0, 1), (1, 0)])


def pass_on(vals, by):
    pairs = [(0, 1)] if by > 0 else [(1, 0)]
    return lax.ppermute(vals, "section", pairs)


def block_places(block_pair, count):
    want = jnp.arange(2 * count, dtype=jnp.int32)
    device = jnp.arange(count, dtype=jnp.int32)
    first = (block_pair[None, :] == want[:, None]).astype(jnp.int32)
    second = ((2 * count - 1 - block_pair)[None, :] == want[:, None]).astype(jnp.int32)
    return jnp.sum(first * (2 * device) + second * (2 * device + 1), axis=1)


def row_positions(block_pair, stored, tok_dev):
    count = block_pair.shape[0]
    device = stored // tok_dev
    within = stored % tok_dev
    half_rows = tok_dev // 2
    matches = device[:, None] == jnp.arange(count, dtype=jnp.int32)[None, :]
    pair_block = jnp.sum(jnp.where(matches, block_pair[None, :], 0), axis=1)
    block_idx = jnp.where(within < half_rows, pair_block, 2 * count - 1 - pair_block)
    return block_idx * half_rows + within % half_rows


def rotary_table(positions, head_size):
    half_rot = ROT // 2
    lane = jnp.arange(LANES, dtype=jnp.int32) % head_size
    inv_freq = ROPE_BASE ** (-((lane % half_rot).astype(f32) * 2.0) / ROT)
    angles = positions.astype(f32)[:, None] * inv_freq[None, :]
    cosine, sine = jnp.cos(angles), jnp.sin(angles)
    lead, second = (lane < half_rot)[None], ((lane >= half_rot) & (lane < ROT))[None]
    return jnp.stack(
        [
            jnp.where(lead | second, cosine, 1.0),
            jnp.where(lead, -sine, 0.0),
            jnp.where(second, sine, 0.0),
        ]
    )


def body(
    inputs,
    cotangent,
    block_pair,
    qkv_weight,
    qkv_bias,
    proj_weight,
    proj_bias,
    up_weight,
    up_bias,
    down_weight,
    down_bias,
    attn_gain,
    attn_shift,
    mlp_gain,
    mlp_shift,
):
    first_section = lax.axis_index("section") == 0
    count = lax.axis_size("ctx")
    micros, _, tok_dev, dim = inputs.shape
    head_size = dim // HEADS
    half = dim // 2
    my_half = lax.axis_index("wsh")
    wsh = jnp.stack([my_half.astype(jnp.int32), first_section.astype(jnp.int32)])
    one_pair_each = count == dim // LANES

    wq, wp, wu, wd = (w[0] for w in (qkv_weight, proj_weight, up_weight, down_weight))
    small = jnp.concatenate(
        [
            v[0].reshape(-1, half)
            for v in (
                attn_gain,
                attn_shift,
                mlp_gain,
                mlp_shift,
                proj_bias,
                down_bias,
                qkv_bias,
                up_bias,
            )
        ],
        axis=0,
    )
    small_oth = swap(small)
    wq_oth = swap(wq)
    first_here = lax.optimization_barrier((wq_oth, small_oth))
    wq_oth, small_oth = first_here
    wu_oth = swap(tied(wq_oth, wu)[0])
    wd_oth = swap(tied(wq_oth, wd)[0])
    wp_oth = swap(tied(wu_oth, wp)[0])
    low_part = jnp.where(my_half == 0, small, small_oth).astype(f32)
    high_part = jnp.where(my_half == 0, small_oth, small).astype(f32)
    vecs = jnp.concatenate([low_part[:6], high_part[:6]], axis=1)
    qkv_rows = 6 + qkv_bias.shape[1] // half
    proj_b, down_b = vecs[4:5], vecs[5:6]
    qkv_b = jnp.concatenate([low_part[6:qkv_rows], high_part[6:qkv_rows]], axis=0).reshape(1, -1)
    up_b = jnp.concatenate([low_part[qkv_rows:], high_part[qkv_rows:]], axis=0).reshape(1, -1)

    local_rows = lax.axis_index("ctx") * tok_dev + jnp.arange(tok_dev, dtype=jnp.int32)
    query_pos = row_positions(block_pair, local_rows, tok_dev)
    key_pos = row_positions(block_pair, jnp.arange(count * tok_dev, dtype=jnp.int32), tok_dev)
    tab = rotary_table(query_pos, head_size)
    loc = block_places(block_pair, count)

    def exchange(vals):
        return lax.all_to_all(vals, "ctx", split_axis=0, concat_axis=0, tiled=True)

    def norm_qkv(index, got):
        return qkv_call(rows_in, index, got, vecs, qkv_b, tab, wq, wq_oth, wsh)

    def mlp(made, save):
        return mlp_call(made[2], made[3], up_b, down_b, wu, wu_oth, wd, wd_oth, wsh, save)

    def mlp_back(dy, mlp_kept):
        return mlp_back_call(dy, mlp_kept[1], wu, wu_oth, wd, wd_oth, wsh)

    def out_back(index, got):
        return da_call(cot_in, index, got, wp, wp_oth, wsh)

    def to_heads(vals):
        return exchange(vals) if one_pair_each else vals

    def to_rows(vals):
        return exchange(vals) if one_pair_each else vals

    def attend(qkv):
        if one_pair_each:
            attended, lse = attend_call(qkv, loc)
            return attended, (qkv, lse)
        return wide_attend(qkv, query_pos, key_pos)

    def attend_back(kept, da):
        if one_pair_each:
            return attend_back_call(kept[0], da, kept[1], loc)
        return wide_attend_back(kept, da, query_pos, key_pos)

    def project(attended, made, mlp_out):
        return proj_call(attended, made[1], mlp_out[0], proj_b, wp, wp_oth, wsh)

    def input_grad_of(dqkv, made, dy, dnm):
        return dx_call(dqkv, tab, made[1], dy, dnm, vecs, wq, wq_oth, wsh)

    rows_in, cot_in = inputs[:, 0], cotangent[:, 0]
    made_a = norm_qkv(0, None)
    qkv_a = to_heads(made_a[0])
    mlp_a = mlp(made_a, False)
    (qkv_a,) = tied(mlp_a[0], qkv_a)
    att_a, _ = attend(qkv_a)
    att_a = to_rows(att_a)
    da_a, dy_a = out_back(0, None)
    (att_a,) = tied(dy_a, att_a)
    y_a = project(att_a, made_a, mlp_a)[0]
    da_a = to_heads(tied(y_a, da_a)[0])

    made_b = norm_qkv(1, pass_on(y_a, 1))
    qkv_b_ = to_heads(tied(da_a, made_b[0])[0])
    norms_b = swap(made_b[3])
    mlp_b = mlp(made_b, True)
    (qkv_b_,) = tied((mlp_b[0], norms_b), qkv_b_)
    att_b, kept_b = attend(qkv_b_)
    att_b = to_rows(att_b)
    gt_b = swap(mlp_b[3])
    (da_a,) = tied((gt_b, kept_b[1]), da_a)
    dqkv_a = attend_back(kept_b, da_a)
    (att_b,) = tied(dqkv_a, att_b)
    dqkv_a = to_rows(dqkv_a)
    y_b, *a_b = project(att_b, made_b, mlp_b)

    made_c = norm_qkv(0, pass_on(y_b, 1))
    (dy_a2,) = tied(made_c[1], dy_a)
    _, dnm_a = mlp_back(dy_a2, mlp_b)
    qkv_c = to_heads(made_c[0])
    norms_c = swap(made_c[3])
    a_b_oth = swap(a_b[1])
    (dqkv_a,) = tied((dnm_a, norms_c, a_b_oth), dqkv_a)
    _, dx_a, _ = input_grad_of(dqkv_a, made_b, dy_a, dnm_a)
    got_a = pass_on(dx_a, -1)
    made_c = list(made_c[:2]) + list(tied(dx_a, made_c[2], made_c[3]))
    mlp_c = mlp(made_c, True)
    (got_a,) = tied(mlp_c[0], got_a)
    da_b, dy_b = out_back(1, got_a)
    (qkv_c,) = tied(dy_b, qkv_c)
    da_b = to_heads(tied(qkv_c, da_b)[0])
    att_c, kept_c = attend(qkv_c)
    dy_b_oth, gt_c = swap(dy_b), swap(mlp_c[3])
    (da_b,) = tied((dy_b_oth, gt_c), da_b)
    dqkv_b = attend_back(kept_c, da_b)
    (dy_b2,) = tied(dqkv_b, dy_b)
    dqkv_b = to_rows(dqkv_b)
    du_b, dnm_b = mlp_back(dy_b2, mlp_c)
    du_b_oth = swap(du_b)
    (dqkv_b,) = tied((dnm_b, du_b_oth), dqkv_b)
    back_b, dx_b, sums_b = input_grad_of(dqkv_b, made_c, dy_b, dnm_b)
    got_b = pass_on(dx_b, -1)
    back_b_oth = swap(back_b)
    (got_b,) = tied(back_b_oth, got_b)

    da_c, dy_c = out_back(0, got_b)
    dy_list = [dy_c, dy_b, swap(dy_c), dy_b_oth]
    da_c = to_heads(da_c)
    down_grad, dy_sum = down_grad_call([mlp_b[2], mlp_c[2], gt_b, gt_c], dy_list)
    down_ring = ring_sum(down_grad, (dim,), "ctx")
    next(down_ring)
    token = down_ring.send(dy_sum)
    token = down_ring.send(token)
    (dy_c2,) = tied(token, dy_c)
    du_c, dnm_c = mlp_back(dy_c2, mlp_b)
    token = down_ring.send(dnm_c)
    up_grad, du_sum = up_grad_call(
        [made_b[2], made_c[2], norms_b, norms_c], [du_c, du_b, swap(du_c), du_b_oth]
    )
    up_ring = ring_sum(up_grad, (up_grad.shape[1],), "ctx")
    next(up_ring)
    token = up_ring.send(du_sum)
    token = down_ring.send(token)
    (da_c,) = tied(token, da_c)
    dqkv_c = attend_back(kept_b, da_c)
    token = up_ring.send(dqkv_c)
    dqkv_c = to_rows(dqkv_c)
    token = down_ring.send(token)
    (dqkv_c,) = tied(token, dqkv_c)
    att_c = to_rows(tied(dqkv_c, att_c)[0])
    back_c, dx_c, sums_c = input_grad_of(dqkv_c, made_b, dy_c, dnm_c)
    back_c_oth = swap(back_c)
    token = up_ring.send(dx_c)
    (att_c,) = tied(token, att_c)
    y_c, *a_c = project(att_c, made_c, mlp_c)
    a_c_oth = swap(a_c[1])
    token = down_ring.send(y_c)
    (back_c2,) = tied(token, back_c)
    attn_grad, attn_sum = attn_grad_call(
        [made_b[2], made_c[2], norms_b, norms_c],
        [a_b[0], a_c[0], a_b_oth, a_c_oth],
        [back_c2, back_b, back_c_oth, back_b_oth],
        dy_list,
    )
    dqkv_sum = attn_sum[:, : 3 * dim]
    attn_ring = ring_sum(attn_grad, (3 * dim, dim), "ctx")
    next(attn_ring)
    token = dqkv_sum
    steps = count + 1
    left = {down_ring: steps - 6, up_ring: steps - 3, attn_ring: steps}
    late = [attn_ring, up_ring, attn_ring, down_ring]
    results = {}

    def turn(ring, token):
        left[ring] -= 1
        made = ring.send(token)
        if left[ring] == 0:
            results[ring] = made
            return token
        return made

    at = 0
    while any(left.values()):
        ring = late[at % len(late)]
        if left[ring]:
            token = turn(ring, token)
        at += 1
        if at == 6:
            middle = token
    (down_grad,) = results[down_ring]
    (up_grad,) = results[up_ring]
    qkv_grad, proj_grad = results[attn_ring]

    norm_sums = tied(middle, sums_b + sums_c)[0]
    norm_own = lax.dynamic_slice_in_dim(norm_sums, my_half * half, half, 1)
    norm_oth = swap(lax.dynamic_slice_in_dim(norm_sums, (1 - my_half) * half, half, 1))

    def own_part(vec):
        size = vec.shape[1] // 2
        return lax.dynamic_slice_in_dim(vec, my_half * size, size, 1).reshape(-1, half)

    small_sums = jnp.concatenate(
        [norm_own + norm_oth, own_part(dy_sum), own_part(dqkv_sum), own_part(du_sum)], axis=0
    )
    small_sums = butterfly_sum(tied(middle, small_sums)[0], "ctx")
    qkv_end = 5 + dqkv_sum.shape[1] // 2 // half
    dy_total = small_sums[4:5]
    pick = lambda yes, no: jnp.where(first_section, yes, no)
    layer_out = jnp.stack([pick(y_c, y_b), pick(y_b, y_c)])[None, :, None]
    input_grad = jnp.stack([pick(dx_b, dx_c), pick(dx_c, dx_b)])[None, :, None]
    return (
        layer_out,
        input_grad,
        qkv_grad[None],
        small_sums[5:qkv_end].reshape(1, -1),
        proj_grad[None],
        dy_total,
        up_grad[None],
        small_sums[qkv_end:].reshape(1, -1),
        down_grad[None],
        dy_total,
        small_sums[0:1],
        small_sums[1:2],
        small_sums[2:3],
        small_sums[3:4],
    )


def solution(mesh):
    in_specs = (
        P(None, "wsh", "ctx", None),
        P(None, "wsh", "ctx", None),
        P(),
        P("section", "wsh", None),
        P("section", "wsh"),
        P("section", "wsh", None),
        P("section", "wsh"),
        P("section", "wsh", None),
        P("section", "wsh"),
        P("section", "wsh", None),
        P("section", "wsh"),
        P("section", "wsh"),
        P("section", "wsh"),
        P("section", "wsh"),
        P("section", "wsh"),
    )
    out_specs = (
        P("section", None, "wsh", "ctx", None),
        P("section", None, "wsh", "ctx", None),
        P("section", "wsh", None),
        P("section", "wsh"),
        P("section", "wsh", None),
        P("section", "wsh"),
        P("section", "wsh", None),
        P("section", "wsh"),
        P("section", "wsh", None),
        P("section", "wsh"),
        P("section", "wsh"),
        P("section", "wsh"),
        P("section", "wsh"),
        P("section", "wsh"),
    )
    return jax.shard_map(body, mesh=mesh, in_specs=in_specs, out_specs=out_specs, check_vma=False)
```

```python
import functools

import jax
import jax.numpy as jnp
from jax import lax
from jax.experimental import pallas as pl
from jax.experimental.pallas import tpu as pltpu
from jax.sharding import PartitionSpec as P

HEADS = 16
ROT = 16
NORM_EPS = 1e-05
ROPE_BASE = 10000.0
MASKED_SCORE = -1e30
LANES = 128
VMEM_LIMIT = 60 * 1024 * 1024
INV_SQRT2 = 0.7071067811865476
INV_SQRT_2PI = 0.3989422804014327

f32 = jnp.float32
bf16 = jnp.bfloat16


def dot_nn(left, right):
    return lax.dot_general(left, right, (((1,), (0,)), ((), ())), preferred_element_type=f32)


def dot_nt(left, right):
    return lax.dot_general(left, right, (((1,), (1,)), ((), ())), preferred_element_type=f32)


def params_of(**extra):
    return dict(
        compiler_params=pltpu.CompilerParams(vmem_limit_bytes=VMEM_LIMIT),
        cost_estimate=pl.CostEstimate(flops=1, bytes_accessed=1, transcendentals=0),
        **extra,
    )


def whole(shape):
    rank = len(shape)
    return pl.BlockSpec(shape, lambda *args: (0,) * rank)


def shape_of(shape, dtype):
    return jax.ShapeDtypeStruct(shape, dtype)


def rope(vals, tab_ref):
    return (
        vals * tab_ref[0]
        + pltpu.roll(vals, LANES - ROT // 2, 1) * tab_ref[1]
        + pltpu.roll(vals, ROT // 2, 1) * tab_ref[2]
    )


def unrope(vals, tab_ref):
    return (
        vals * tab_ref[0]
        - pltpu.roll(vals, LANES - ROT // 2, 1) * tab_ref[1]
        - pltpu.roll(vals, ROT // 2, 1) * tab_ref[2]
    )


def normalized(hidden):
    row_mean = jnp.mean(hidden, axis=-1, keepdims=True)
    centered = hidden - row_mean
    spread = jnp.mean(centered * centered, axis=-1, keepdims=True)
    scale = lax.rsqrt(spread + NORM_EPS)
    return centered * scale, scale


def start_all(copies):
    for copy in copies:
        copy.start()
    return copies


def wait_all(copies):
    for copy in copies:
        copy.wait()


def qkv_kernel(own_given, wsh_ref, inputs, weights, outputs, buf, sems):
    half, dim = buf.shape[2:]
    copies = start_all(
        [
            pltpu.make_async_copy(
                weight.at[:, pl.ds(part * dim, dim)], buf.at[part, side], sems.at[part, side]
            )
            for part in range(3)
            for side, weight in enumerate(weights)
        ]
    )
    out, x_out, own, oth = outputs
    x = inputs[0].ref()[...]
    if not own_given:
        x = jnp.where(wsh_ref[1] == 1, x, inputs[4].ref()[...])
    x_out.ref[...] = x
    x_out.send()
    xhat, _ = normalized(x.astype(f32))
    vec_ref, bias_ref, tab_ref = (item.ref() for item in inputs[1:4])
    na = (xhat * vec_ref[0:1] + vec_ref[1:2]).astype(bf16)
    nm = (xhat * vec_ref[2:3] + vec_ref[3:4]).astype(bf16)
    first = wsh_ref[0] == 0
    for i, rows in enumerate((na, nm)):
        own.ref[i] = jnp.where(first, rows[:, :half], rows[:, half:])
        oth.ref[i] = jnp.where(first, rows[:, half:], rows[:, :half])
    own.send()
    oth.send()
    for part in range(3):
        wait_all(copies[2 * part : 2 * part + 2])
        for at in range(0, dim, 2 * LANES):
            cols = slice(at, at + 2 * LANES)
            res = (
                dot_nn(own.ref[0], buf[part, 0, :, cols])
                + dot_nn(oth.ref[0], buf[part, 1, :, cols])
                + bias_ref[:, part * dim + at : part * dim + at + 2 * LANES]
            )
            for i in range(2):
                vals = res[:, i * LANES : (i + 1) * LANES]
                if part < 2:
                    vals = rope(vals, tab_ref)
                out.ref[at // LANES + i, part] = vals.astype(bf16)


def layer_of(shape, index):
    return pl.BlockSpec((pl.squeezed,) + shape, lambda *args: (index, 0, 0))


HERE = pl.BlockSpec(memory_space=pltpu.VMEM)
SCALARS = pl.BlockSpec(memory_space=pltpu.SMEM)
ANYWHERE = pl.BlockSpec(memory_space=pl.ANY)


class Arriving:
    def __init__(self, copy, buf):
        self.copy, self.buf, self.here = copy, buf, False

    def ref(self):
        if not self.here:
            self.copy.wait()
            self.here = True
        return self.buf


class Leaving:
    def __init__(self, copy, buf):
        self.copy, self.ref, self.sent = copy, buf, False

    def send(self):
        if not self.sent:
            self.copy.start()
            self.sent = True


def local_kernel(body, scalars, arrays, weights, outs, *refs):
    at = 0
    groups = []
    for number in (scalars, arrays, weights, outs, arrays, outs, 1, 1):
        groups.append(refs[at : at + number])
        at += number
    scalar_refs, array_refs, weight_refs, out_refs, in_bufs, out_bufs, in_sems, out_sems = groups
    inputs = []
    for i in range(arrays):
        copy = pltpu.make_async_copy(array_refs[i], in_bufs[i], in_sems[0].at[i])
        copy.start()
        inputs.append(Arriving(copy, in_bufs[i]))
    outputs = [
        Leaving(pltpu.make_async_copy(out_bufs[i], out_refs[i], out_sems[0].at[i]), out_bufs[i])
        for i in range(outs)
    ]
    body(*scalar_refs, inputs, weight_refs, outputs, *refs[at:])
    for item in inputs:
        item.ref()
    for item in outputs:
        item.send()
    for item in outputs:
        item.copy.wait()


def local_call(body, name, scalars, arrays, weights, out_shape, scratch=()):
    multiple = isinstance(out_shape, (list, tuple))
    shapes = list(out_shape) if multiple else [out_shape]
    res = pl.pallas_call(
        functools.partial(
            local_kernel, body, len(scalars), len(arrays), len(weights), len(shapes)
        ),
        in_specs=[SCALARS] * len(scalars) + [ANYWHERE] * (len(arrays) + len(weights)),
        out_specs=[ANYWHERE] * len(shapes),
        out_shape=shapes,
        scratch_shapes=[pltpu.VMEM(a.shape, a.dtype) for a in arrays]
        + [pltpu.VMEM(o.shape, o.dtype) for o in shapes]
        + [pltpu.SemaphoreType.DMA((len(arrays) + 1,)), pltpu.SemaphoreType.DMA((len(shapes),))]
        + list(scratch),
        name=name,
        **params_of(),
    )(*scalars, *arrays, *weights)
    return res if multiple else res[0]


def qkv_call(given, got, vecs, qkv_b, tab, w_own, w_oth, wsh):
    rows, dim = given.shape
    half = w_own.shape[0]
    pairs = dim // LANES
    return local_call(
        functools.partial(qkv_kernel, got is None),
        "qkv_proj",
        [wsh],
        [given, vecs, qkv_b, tab] + ([] if got is None else [got]),
        [w_own, w_oth],
        [shape_of((pairs, 3, rows, LANES), bf16), shape_of((rows, dim), bf16)]
        + [shape_of((2, rows, half), bf16)] * 2,
        [pltpu.VMEM((3, 2, half, dim), bf16), pltpu.SemaphoreType.DMA((3, 2))],
    )


FF_TILE = 512


def ff_tiles(wsh_ref, up_own, up_oth, dn_own, dn_oth, up_buf, dn_buf, sems):
    own = dn_own.shape[0] // FF_TILE
    tiles = []
    for t in range(2 * own):
        start = pl.multiple_of(((wsh_ref[0] * own + t) % (2 * own)) * FF_TILE, FF_TILE)
        place = pl.ds(start, FF_TILE)
        down = (dn_own if t < own else dn_oth).at[pl.ds((t % own) * FF_TILE, FF_TILE)]
        copies = [
            pltpu.make_async_copy(up_own.at[:, place], up_buf.at[t, 0], sems.at[t, 0]),
            pltpu.make_async_copy(up_oth.at[:, place], up_buf.at[t, 1], sems.at[t, 1]),
            pltpu.make_async_copy(down, dn_buf.at[t], sems.at[t, 2]),
        ]
        start_all(copies)
        tiles.append((t, place, t < own, slice((t % own) * FF_TILE, (t % own + 1) * FF_TILE), copies))
    for t, place, held, rows, copies in tiles:
        wait_all(copies)
        yield t, place, held, rows


def ff_scratch(half, ff, dim):
    tiles = ff // FF_TILE
    return [
        pltpu.VMEM((tiles, 2, half, FF_TILE), bf16),
        pltpu.VMEM((tiles, FF_TILE, dim), bf16),
        pltpu.SemaphoreType.DMA((tiles, 3)),
    ]


def mlp_kernel(save, wsh_ref, inputs, weights, outputs, up_buf, dn_buf, sems):
    out_ref = outputs[0].ref
    tiles = ff_tiles(wsh_ref, *weights, up_buf, dn_buf, sems)
    for t, place, held, rows in tiles:
        own_ref, oth_ref, up_b, down_b = (item.ref() for item in inputs)
        if t == 0:
            out_ref[...] = jnp.broadcast_to(down_b[...], out_ref.shape)
        pre = dot_nn(own_ref[1], up_buf[t, 0]) + dot_nn(oth_ref[1], up_buf[t, 1]) + up_b[:, place]
        gate = 0.5 + 0.5 * lax.erf(pre * INV_SQRT2)
        act = (pre * gate).astype(bf16)
        if save:
            slope = gate + pre * (INV_SQRT_2PI * jnp.exp(-0.5 * pre * pre))
            outputs[1].ref[place] = slope.astype(bf16).T
            outputs[2 if held else 3].ref[rows] = act.T
            if not held:
                outputs[2].send()
        out_ref[...] += dot_nn(act, dn_buf[t])


def mlp_call(own, oth, up_b, down_b, up_own, up_oth, dn_own, dn_oth, wsh, save):
    rows, half = own.shape[1:]
    dim = dn_own.shape[1]
    ff = up_own.shape[1]
    out_shape = [shape_of((rows, dim), f32)]
    if save:
        out_shape += [shape_of((ff, rows), bf16)] + [shape_of((ff // 2, rows), bf16)] * 2
    return local_call(
        functools.partial(mlp_kernel, save),
        "mlp_forward",
        [wsh],
        [own, oth, up_b, down_b],
        [up_own, up_oth, dn_own, dn_oth],
        out_shape,
        ff_scratch(half, ff, dim),
    )


def mlp_back_kernel(wsh_ref, inputs, weights, outputs, acc_own, acc_oth, up_buf, dn_buf, sems):
    du, dnm = outputs
    half = acc_own.shape[0]
    acc_own[...] = jnp.zeros(acc_own.shape, f32)
    acc_oth[...] = jnp.zeros(acc_oth.shape, f32)
    for t, place, _, _ in ff_tiles(wsh_ref, *weights, up_buf, dn_buf, sems):
        dy_ref, slope_ref = (item.ref() for item in inputs)
        dact = dot_nt(dn_buf[t], dy_ref[...])
        vals = (dact * slope_ref[place].astype(f32)).astype(bf16)
        du.ref[place] = vals
        acc_own[...] += dot_nn(up_buf[t, 0], vals)
        acc_oth[...] += dot_nn(up_buf[t, 1], vals)
    du.send()
    first = wsh_ref[0] == 0
    dnm.ref[:, :half] = jnp.where(first, acc_own[...], acc_oth[...]).T
    dnm.ref[:, half:] = jnp.where(first, acc_oth[...], acc_own[...]).T


def mlp_back_call(dy, slope, up_own, up_oth, dn_own, dn_oth, wsh):
    rows, dim = dy.shape
    half, ff = up_own.shape
    return local_call(
        mlp_back_kernel,
        "mlp_backward",
        [wsh],
        [dy, slope],
        [up_own, up_oth, dn_own, dn_oth],
        [shape_of(slope.shape, bf16), shape_of((rows, dim), f32)],
        [pltpu.VMEM((half, rows), f32), pltpu.VMEM((half, rows), f32)] + ff_scratch(half, ff, dim),
    )


def sort_in(loc_ref, ref, dst, half_rows, part=None):
    for block in range(dst.shape[0] // half_rows):
        place = loc_ref[block]
        rows = pl.ds(pl.multiple_of((place % 2) * half_rows, half_rows), half_rows)
        if part is None:
            vals = ref[place // 2, rows, :]
        else:
            vals = ref[place // 2, part, rows, :]
        dst[block * half_rows : (block + 1) * half_rows] = vals


def sort_out(loc_ref, vals, ref, half_rows, part=None):
    for block in range(vals.shape[0] // half_rows):
        place = loc_ref[block]
        rows = pl.ds(pl.multiple_of((place % 2) * half_rows, half_rows), half_rows)
        piece = vals[block * half_rows : (block + 1) * half_rows]
        if part is None:
            ref[place // 2, rows, :] = piece
        else:
            ref[place // 2, part, rows, :] = piece


def head_of(vals, head):
    lane = lax.broadcasted_iota(jnp.int32, vals.shape, 1)
    return jnp.where(lane // (LANES // 2) == head, vals, jnp.zeros_like(vals))


def scores_of(keys, queries, scale, diagonal):
    scores = dot_nt(keys, queries) * scale
    if diagonal:
        key_at = lax.broadcasted_iota(jnp.int32, scores.shape, 0)
        query_at = lax.broadcasted_iota(jnp.int32, scores.shape, 1)
        scores = jnp.where(key_at <= query_at, scores, MASKED_SCORE)
    return scores


def attend_kernel(tile, loc_ref, inputs, weights, outputs, q_s, k_s, v_s, vt_s, o_s):
    qkv_ref = inputs[0].ref()
    o_ref, lse_ref = (item.ref for item in outputs)
    half_rows = qkv_ref.shape[2] // 2
    seq = q_s.shape[0]
    head_size = LANES // 2
    scale = head_size**-0.5
    sort_in(loc_ref, qkv_ref, q_s, half_rows, 0)
    sort_in(loc_ref, qkv_ref, k_s, half_rows, 1)
    sort_in(loc_ref, qkv_ref, v_s, half_rows, 2)
    vt_s[...] = v_s[...].T
    for t in range(seq // tile):
        rows = slice(t * tile, (t + 1) * tile)
        queries = q_s[rows]
        outs = []
        for head in range(2):
            picked = head_of(queries, head)
            parts = [
                scores_of(k_s[i * tile : (i + 1) * tile], picked, scale, i == t)
                for i in range(t + 1)
            ]
            top = functools.reduce(
                jnp.maximum, [jnp.max(p, axis=0, keepdims=True) for p in parts]
            )
            parts = [jnp.exp(p - top) for p in parts]
            total = sum(jnp.sum(p, axis=0, keepdims=True) for p in parts)
            lse_ref[head : head + 1, rows] = top + jnp.log(total)
            inverse = 1.0 / total
            acc = None
            for i, p in enumerate(parts):
                term = dot_nn(
                    vt_s[head * head_size : (head + 1) * head_size, i * tile : (i + 1) * tile],
                    (p * inverse).astype(bf16),
                )
                acc = term if acc is None else acc + term
            outs.append(acc)
        o_s[rows] = jnp.concatenate(outs, axis=0).T.astype(bf16)
    sort_out(loc_ref, o_s, o_ref, half_rows)


def attend_call(qkv, loc):
    count, _, rows, _ = qkv.shape
    seq = count * rows
    return local_call(
        functools.partial(attend_kernel, 256),
        "attention",
        [loc],
        [qkv],
        [],
        [shape_of((count, rows, LANES), bf16), shape_of((2, seq), f32)],
        [
            pltpu.VMEM((seq, LANES), bf16),
            pltpu.VMEM((seq, LANES), bf16),
            pltpu.VMEM((seq, LANES), bf16),
            pltpu.VMEM((LANES, seq), bf16),
            pltpu.VMEM((seq, LANES), bf16),
        ],
    )


def attend_back_kernel(
    tile, loc_ref, inputs, weights, outputs, q_s, k_s, v_s, da_s, kt_s, dq_s, dk_s, dv_s
):
    qkv_ref, da_ref, lse_ref = (item.ref() for item in inputs)
    out_ref = outputs[0].ref
    half_rows = qkv_ref.shape[2] // 2
    seq = q_s.shape[0]
    head_size = LANES // 2
    scale = head_size**-0.5
    sort_in(loc_ref, qkv_ref, q_s, half_rows, 0)
    sort_in(loc_ref, qkv_ref, k_s, half_rows, 1)
    sort_in(loc_ref, qkv_ref, v_s, half_rows, 2)
    sort_in(loc_ref, da_ref, da_s, half_rows)
    kt_s[...] = k_s[...].T
    dk_s[...] = jnp.zeros(dk_s.shape, f32)
    dv_s[...] = jnp.zeros(dv_s.shape, f32)
    for t in range(seq // tile):
        rows = slice(t * tile, (t + 1) * tile)
        outs = []
        for head in range(2):
            queries = head_of(q_s[rows], head)
            grads = head_of(da_s[rows], head)
            lse = lse_ref[head : head + 1, rows]
            probs, dprobs, row_dot = [], [], 0.0
            for i in range(t + 1):
                keys = slice(i * tile, (i + 1) * tile)
                p = jnp.exp(scores_of(k_s[keys], queries, scale, i == t) - lse)
                dp = dot_nt(v_s[keys], grads)
                row_dot = row_dot + jnp.sum(p * dp, axis=0, keepdims=True)
                dv_s[keys] += dot_nn(p.astype(bf16), grads)
                probs.append(p)
                dprobs.append(dp)
            acc = None
            for i in range(t + 1):
                keys = slice(i * tile, (i + 1) * tile)
                ds = (probs[i] * (dprobs[i] - row_dot) * scale).astype(bf16)
                dk_s[keys] += dot_nn(ds, queries)
                term = dot_nn(kt_s[head * head_size : (head + 1) * head_size, keys], ds)
                acc = term if acc is None else acc + term
            outs.append(acc)
        dq_s[rows] = jnp.concatenate(outs, axis=0).T.astype(bf16)
    sort_out(loc_ref, dq_s, out_ref, half_rows, 0)
    k_s[...] = dk_s[...].astype(bf16)
    v_s[...] = dv_s[...].astype(bf16)
    sort_out(loc_ref, k_s, out_ref, half_rows, 1)
    sort_out(loc_ref, v_s, out_ref, half_rows, 2)


def attend_back_call(qkv, da, lse, loc):
    count, _, rows, _ = qkv.shape
    seq = count * rows
    return local_call(
        functools.partial(attend_back_kernel, 256),
        "attention_backward",
        [loc],
        [qkv, da, lse],
        [],
        shape_of(qkv.shape, bf16),
        [pltpu.VMEM((seq, LANES), bf16)] * 4
        + [pltpu.VMEM((LANES, seq), bf16), pltpu.VMEM((seq, LANES), bf16)]
        + [pltpu.VMEM((seq, LANES), f32)] * 2,
    )


def by_head(parts):
    pairs, rows, lanes = parts.shape
    return jnp.transpose(parts, (1, 0, 2)).reshape(rows, HEADS, pairs * lanes // HEADS)


def by_pair(heads):
    rows = heads.shape[0]
    return jnp.transpose(heads.reshape(rows, -1, LANES), (1, 0, 2))


def wide_scores(queries, keys, query_pos, key_pos):
    raw = jnp.einsum("qhd,khd->hqk", queries, keys, preferred_element_type=f32)
    allowed = (query_pos[:, None] >= key_pos[None, :])[None]
    return jnp.where(allowed, raw * queries.shape[-1] ** (-0.5), MASKED_SCORE)


def key_blocks(arrays, rows):
    return tuple(a.reshape((a.shape[0] // rows, rows) + a.shape[1:]) for a in arrays)


def wide_attend(qkv, query_pos, key_pos):
    queries = by_head(qkv[:, 0])
    keys = lax.all_gather(by_head(qkv[:, 1]), "ctx", axis=0, tiled=True)
    values = lax.all_gather(by_head(qkv[:, 2]), "ctx", axis=0, tiled=True)
    block = min(512, keys.shape[0])
    split = key_blocks((keys, values, key_pos), block)
    rows, _, head_size = queries.shape

    def max_step(carry, block_in):
        top, total = carry
        scores = wide_scores(queries, block_in[0], query_pos, block_in[2])
        new_top = jnp.maximum(top, jnp.max(scores, axis=-1))
        part = jnp.sum(jnp.exp(scores - new_top[..., None]), axis=-1)
        return ((new_top, total * jnp.exp(top - new_top) + part), None)

    start = (jnp.full((HEADS, rows), MASKED_SCORE, f32), jnp.zeros((HEADS, rows), f32))
    (top, total), _ = lax.scan(max_step, start, split)
    lse = top + jnp.log(total)

    def value_step(running, block_in):
        scores = wide_scores(queries, block_in[0], query_pos, block_in[2])
        probs = jnp.exp(scores - lse[..., None]).astype(bf16)
        term = jnp.einsum("hqk,khd->qhd", probs, block_in[1], preferred_element_type=f32)
        return (running + term, None)

    attended, _ = lax.scan(value_step, jnp.zeros((rows, HEADS, head_size), f32), split)
    return by_pair(attended.astype(bf16)), (queries, keys, values, lse)


def wide_attend_back(kept, da, query_pos, key_pos):
    queries, keys, values, lse = kept
    grads = by_head(da)
    block = min(512, keys.shape[0])
    split = key_blocks((keys, values, key_pos), block)
    scale = queries.shape[-1] ** (-0.5)

    def pieces(block_in):
        scores = wide_scores(queries, block_in[0], query_pos, block_in[2])
        probs = jnp.exp(scores - lse[..., None])
        dprobs = jnp.einsum("qhd,khd->hqk", grads, block_in[1], preferred_element_type=f32)
        return probs, dprobs

    def dot_step(running, block_in):
        probs, dprobs = pieces(block_in)
        return (running + jnp.sum(probs * dprobs, axis=-1), None)

    row_dot, _ = lax.scan(dot_step, jnp.zeros(lse.shape, f32), split)

    def key_step(running, block_in):
        probs, dprobs = pieces(block_in)
        ds = (scale * probs * (dprobs - row_dot[..., None])).astype(bf16)
        running = running + jnp.einsum("hqk,khd->qhd", ds, block_in[0], preferred_element_type=f32)
        dk = jnp.einsum("hqk,qhd->khd", ds, queries, preferred_element_type=f32)
        dv = jnp.einsum("hqk,qhd->khd", probs.astype(bf16), grads, preferred_element_type=f32)
        return (running, (dk.astype(bf16), dv.astype(bf16)))

    dq, (dk, dv) = lax.scan(key_step, jnp.zeros(queries.shape, f32), split)
    dk, dv = (
        lax.psum_scatter(part.reshape(keys.shape), "ctx", scatter_dimension=0, tiled=True)
        for part in (dk, dv)
    )
    return jnp.stack([by_pair(dq.astype(bf16)), by_pair(dk), by_pair(dv)], axis=1)


def lanes_of(ref):
    return jnp.concatenate([ref[i] for i in range(ref.shape[0])], axis=1)


def both_halves(w_own, w_oth, buf, sems):
    return start_all(
        [
            pltpu.make_async_copy(weight, buf.at[side], sems.at[side])
            for side, weight in enumerate((w_own, w_oth))
        ]
    )


def half_scratch(weight):
    return [pltpu.VMEM((2,) + weight.shape, bf16), pltpu.SemaphoreType.DMA((2,))]


def proj_kernel(wsh_ref, inputs, weights, outputs, buf, sems):
    copies = both_halves(*weights, buf, sems)
    y, own, oth = outputs
    half = buf.shape[1]
    first = wsh_ref[0] == 0
    a = lanes_of(inputs[0].ref())
    own.ref[...] = jnp.where(first, a[:, :half], a[:, half:])
    oth.ref[...] = jnp.where(first, a[:, half:], a[:, :half])
    own.send()
    oth.send()
    x_ref, mlp_ref, bias_ref = (item.ref() for item in inputs[1:])
    wait_all(copies)
    attn = dot_nn(own.ref[...], buf[0]) + dot_nn(oth.ref[...], buf[1]) + bias_ref[...]
    y.ref[...] = (x_ref[...].astype(f32) + attn + mlp_ref[...]).astype(bf16)


def proj_call(a, x, mlp, bias, p_own, p_oth, wsh):
    rows, dim = x.shape
    half = p_own.shape[0]
    return local_call(
        proj_kernel,
        "attn_out",
        [wsh],
        [a, x, mlp, bias],
        [p_own, p_oth],
        [shape_of((rows, dim), bf16)] + [shape_of((rows, half), bf16)] * 2,
        half_scratch(p_own),
    )


def da_kernel(own_given, wsh_ref, inputs, weights, outputs, buf, sems):
    copies = both_halves(*weights, buf, sems)
    out_ref, dy_out = outputs[0].ref, outputs[1]
    dy = inputs[0].ref()[...]
    if not own_given:
        dy = jnp.where(wsh_ref[1] == 1, inputs[1].ref()[...], dy)
    dy_out.ref[...] = dy
    dy_out.send()
    wsh = wsh_ref[0]
    count = out_ref.shape[0] // 2
    for place, side in ((wsh * count, 0), ((1 - wsh) * count, 1)):
        copies[side].wait()
        part = dot_nt(dy, buf[side]).astype(bf16)
        for i in range(count):
            out_ref[place + i] = part[:, i * LANES : (i + 1) * LANES]


def da_call(given, got, p_own, p_oth, wsh):
    rows, dim = given.shape
    return local_call(
        functools.partial(da_kernel, got is None),
        "attn_out_backward",
        [wsh],
        [given] + ([] if got is None else [got]),
        [p_own, p_oth],
        [shape_of((dim // LANES, rows, LANES), bf16), shape_of((rows, dim), bf16)],
        half_scratch(p_own),
    )


def dx_kernel(wsh_ref, inputs, weights, outputs, grad_s, buf, sems):
    copies = both_halves(*weights, buf, sems)
    back, dx, sums = outputs
    dqkv_ref, tab_ref = inputs[0].ref(), inputs[1].ref()
    pairs = dqkv_ref.shape[0]
    for part in range(3):
        for pair in range(pairs):
            vals = dqkv_ref[pair, part]
            if part < 2:
                vals = unrope(vals.astype(f32), tab_ref).astype(bf16)
            back.ref[pair, part] = vals
            grad_s[:, pl.ds((part * pairs + pair) * LANES, LANES)] = vals
    back.send()
    x_ref, dy_ref, dnm_ref, vec_ref = (item.ref() for item in inputs[2:])
    first = wsh_ref[0] == 0
    copies[0].wait()
    own = dot_nt(grad_s[...], buf[0])
    copies[1].wait()
    oth = dot_nt(grad_s[...], buf[1])
    dna = jnp.concatenate([jnp.where(first, own, oth), jnp.where(first, oth, own)], axis=1)
    dnm = dnm_ref[...]
    xhat, scale = normalized(x_ref[...].astype(f32))
    grad = dna * vec_ref[0:1] + dnm * vec_ref[2:3]
    inner = (
        grad
        - jnp.mean(grad, axis=-1, keepdims=True)
        - xhat * jnp.mean(grad * xhat, axis=-1, keepdims=True)
    )
    dx.ref[...] = (dy_ref[...].astype(f32) + scale * inner).astype(bf16)
    dx.send()
    sums.ref[0:1] = jnp.sum(dna * xhat, axis=0, keepdims=True)
    sums.ref[1:2] = jnp.sum(dna, axis=0, keepdims=True)
    sums.ref[2:3] = jnp.sum(dnm * xhat, axis=0, keepdims=True)
    sums.ref[3:4] = jnp.sum(dnm, axis=0, keepdims=True)


def dx_call(dqkv, tab, x, dy, dnm, vecs, w_own, w_oth, wsh):
    rows, dim = x.shape
    return local_call(
        dx_kernel,
        "section_input_grad",
        [wsh],
        [dqkv, tab, x, dy, dnm, vecs],
        [w_own, w_oth],
        [shape_of(dqkv.shape, bf16), shape_of((rows, dim), bf16), shape_of((4, dim), f32)],
        [pltpu.VMEM((rows, 3 * dim), bf16)] + half_scratch(w_own),
    )


def stack_rows(refs, cols=slice(None)):
    return jnp.concatenate([ref[:, cols] for ref in refs], axis=0)


def down_grad_kernel(micros, *refs):
    gt_refs, dy_refs = refs[:micros], refs[micros : 2 * micros]
    out_ref, sum_ref, dy_s = refs[2 * micros :]

    @pl.when(pl.program_id(0) == 0)
    def _():
        dy = stack_rows(dy_refs)
        dy_s[...] = dy
        sum_ref[...] = jnp.sum(dy.astype(f32), axis=0, keepdims=True)

    left = jnp.concatenate([ref[...] for ref in gt_refs], axis=1)
    out_ref[...] = dot_nn(left, dy_s[...]).astype(bf16)


def down_grad_call(gt_list, dy_list):
    ff_rows, rows = gt_list[0].shape
    dim = dy_list[0].shape[1]
    micros = len(dy_list)
    tile = 512
    return pl.pallas_call(
        functools.partial(down_grad_kernel, micros),
        grid=(ff_rows // tile,),
        in_specs=[pl.BlockSpec((tile, rows), lambda j: (j, 0))] * micros
        + [whole((rows, dim))] * micros,
        out_specs=[pl.BlockSpec((tile, dim), lambda j: (j, 0)), whole((1, dim))],
        out_shape=[shape_of((ff_rows, dim), bf16), shape_of((1, dim), f32)],
        scratch_shapes=[pltpu.VMEM((micros * rows, dim), bf16)],
        name="down_grad",
        **params_of(),
    )(*gt_list, *dy_list)


def up_grad_kernel(micros, *refs):
    x_refs, du_refs = refs[:micros], refs[micros : 2 * micros]
    out_ref, sum_ref, xt_s = refs[2 * micros :]

    @pl.when(pl.program_id(0) == 0)
    def _():
        xt_s[...] = stack_rows(x_refs).T

    du = jnp.concatenate([ref[...] for ref in du_refs], axis=1)
    sum_ref[...] = dot_nt(jnp.ones((8, du.shape[1]), bf16), du)[:1]
    out_ref[...] = dot_nt(xt_s[...], du).astype(bf16)


def up_grad_call(x_list, du_list):
    rows, half = x_list[0].shape[1:]
    ff = du_list[0].shape[0]
    micros = len(x_list)
    tile = 1024
    return pl.pallas_call(
        functools.partial(up_grad_kernel, micros),
        grid=(ff // tile,),
        in_specs=[layer_of((rows, half), 1)] * micros
        + [pl.BlockSpec((tile, rows), lambda j: (j, 0))] * micros,
        out_specs=[
            pl.BlockSpec((half, tile), lambda j: (0, j)),
            pl.BlockSpec((1, tile), lambda j: (0, j)),
        ],
        out_shape=[shape_of((half, ff), bf16), shape_of((1, ff), f32)],
        scratch_shapes=[pltpu.VMEM((half, micros * rows), bf16)],
        name="up_grad",
        **params_of(),
    )(*x_list, *du_list)


def attn_grad_kernel(micros, *refs):
    x_refs, a_refs, d_refs, dy_refs = (refs[i * micros : (i + 1) * micros] for i in range(4))
    out_ref, sum_ref, xt_s = refs[4 * micros :]
    part = pl.program_id(0)

    def finish(dy):
        sum_ref[...] = jnp.sum(dy.astype(f32), axis=0, keepdims=True)
        out_ref[...] = dot_nn(xt_s[...], dy).astype(bf16)

    @pl.when(part == 0)
    def _():
        xt_s[...] = stack_rows(x_refs).T

    @pl.when(part < 3)
    def _():
        finish(jnp.concatenate([lanes_of(ref) for ref in d_refs], axis=0))

    @pl.when(part == 3)
    def _():
        xt_s[...] = stack_rows(a_refs).T
        finish(stack_rows(dy_refs))


def attn_grad_call(x_list, a_list, d_list, dy_list):
    rows, half = x_list[0].shape[1:]
    pairs = d_list[0].shape[0]
    dim = pairs * LANES
    micros = len(x_list)
    d_spec = pl.BlockSpec(
        (pairs, pl.squeezed, rows, LANES), lambda j: (0, jnp.minimum(j, 2), 0, 0)
    )
    return pl.pallas_call(
        functools.partial(attn_grad_kernel, micros),
        grid=(4,),
        in_specs=[layer_of((rows, half), 0)] * micros
        + [whole((rows, half))] * micros
        + [d_spec] * micros
        + [whole((rows, dim))] * micros,
        out_specs=[
            pl.BlockSpec((half, dim), lambda j: (0, j)),
            pl.BlockSpec((1, dim), lambda j: (0, j)),
        ],
        out_shape=[shape_of((half, 4 * dim), bf16), shape_of((1, 4 * dim), f32)],
        scratch_shapes=[pltpu.VMEM((half, micros * rows), bf16)],
        name="attn_grad",
        **params_of(),
    )(*x_list, *a_list, *d_list, *dy_list)


def ring_of(count):
    return list(range(0, count, 2)) + list(range(count - 1, 0, -2))


def ring_place(axis):
    count = lax.axis_size(axis)
    me = lax.axis_index(axis)
    return jnp.where(me % 2 == 0, me // 2, count - (me + 1) // 2)


def ring_shift(vals, axis, by):
    order = ring_of(lax.axis_size(axis))
    count = len(order)
    pairs = [(order[i], order[(i + by) % count]) for i in range(count)]
    return lax.ppermute(vals, axis, pairs)


def tied(token, *vals):
    return lax.optimization_barrier((token, vals))[1]


def fetch(idx_ref, slots, own_ref, bufs, sems):
    return start_all(
        [
            pltpu.make_async_copy(own_ref.at[idx_ref[slot]], bufs.at[i], sems.at[i])
            for i, slot in enumerate(slots)
        ]
    )


def low_total(*terms):
    total = terms[0].astype(f32)
    for term in terms[1:]:
        total = total + term.astype(f32)
    return total.astype(bf16)


def ring_split_kernel(slots, idx_ref, inputs, own_refs, outputs, bufs, sems):
    wait_all(fetch(idx_ref, slots, own_refs[0], bufs, sems))
    cut = outputs[0].ref.shape[1]
    for i, item in enumerate(outputs):
        item.ref[...] = bufs[0, :, i * cut : (i + 1) * cut]


def ring_add_kernel(slots, idx_ref, inputs, own_refs, outputs, bufs, sems):
    copies = fetch(idx_ref, slots, own_refs[0], bufs, sems)
    for i, item in enumerate(outputs):
        copies[i].wait()
        got = inputs[i].ref()
        cols, cut = item.ref.shape[1], got.shape[1]
        summed = slice(0, cut) if i == 0 else slice(cols - cut, cols)
        item.ref[:, summed] = low_total(bufs[i, :, summed], got[...])
        if cut < cols:
            rest = slice(cut, cols) if i == 0 else slice(0, cols - cut)
            item.ref[:, rest] = bufs[i, :, rest]
        item.send()


def put_copies(chunk, cols, buf, totals, starts, sem):
    lo, hi = cols, cols + buf.shape[1]
    copies = []
    for i, (total, start) in enumerate(zip(totals, starts)):
        first, last = max(lo, start), min(hi, start + total.shape[2])
        if first < last:
            copies.append(
                pltpu.make_async_copy(
                    buf.at[:, pl.ds(first - lo, last - first)],
                    total.at[chunk, :, pl.ds(first - start, last - first)],
                    sem.at[i],
                )
            )
    return copies


def ring_own_kernel(slots, idx_ref, inputs, own_refs, outputs, bufs, sems):
    wait_all(fetch(idx_ref, slots, own_refs[0], bufs, sems))
    outputs[0].ref[...] = low_total(bufs[0], inputs[0].ref()[...], inputs[1].ref()[...])


def ring_put_kernel(starts, slots, cols, fresh, idx_ref, *refs):
    number = len(slots)
    pieces = refs[:number]
    refs = refs[number + (0 if fresh else len(starts)) :]
    totals, token_ref = refs[: len(starts)], refs[len(starts)]
    narrow, wide, in_sems, out_sems = refs[len(starts) + 1 :]
    arriving = start_all(
        [pltpu.make_async_copy(pieces[i], narrow.at[i], in_sems.at[i]) for i in range(number)]
    )
    token_ref[...] = jnp.zeros(token_ref.shape, f32)
    leaving = []
    for i in range(number):
        arriving[i].wait()
        wide[i] = narrow[i].astype(f32)
        leaving += start_all(
            put_copies(idx_ref[slots[i]], cols[i], wide.at[i], totals, starts, out_sems.at[i])
        )
    wait_all(leaving)


def ring_sum(own, widths, axis):
    count = lax.axis_size(axis)
    half = count // 2
    full_rows, cols = own.shape
    rows = full_rows // count
    own = own.reshape(count, rows, cols)
    cut = cols // 2
    starts = [sum(widths[:i]) for i in range(len(widths))]
    idx = (ring_place(axis) + jnp.arange(count, dtype=jnp.int32)) % count
    chunk, piece = shape_of((rows, cols), bf16), shape_of((rows, cut), bf16)
    sums = [shape_of((count, rows, width), f32) for width in widths]

    def taken(number):
        return [pltpu.VMEM((number, rows, cols), bf16), pltpu.SemaphoreType.DMA((number,))]

    def put(totals, pieces, slots):
        number, width = len(pieces), pieces[0].shape[1]
        first_cols = (0,) * number if width == cols else (0, cut)
        fresh = totals is None
        out = pl.pallas_call(
            functools.partial(
                ring_put_kernel, starts, tuple(k % count for k in slots), first_cols, fresh
            ),
            in_specs=[SCALARS] + [ANYWHERE] * (number + (0 if fresh else len(sums))),
            out_specs=[ANYWHERE] * len(sums) + [HERE],
            out_shape=sums + [shape_of((8, LANES), f32)],
            scratch_shapes=[
                pltpu.VMEM((number, rows, width), bf16),
                pltpu.VMEM((number, rows, width), f32),
                pltpu.SemaphoreType.DMA((number,)),
                pltpu.SemaphoreType.DMA((number, len(sums))),
            ],
            input_output_aliases={} if fresh else {1 + number + i: i for i in range(len(sums))},
            name="ring_put",
            **params_of(),
        )(idx, *pieces, *([] if fresh else totals))
        return out[:-1], out[-1]

    token = yield None
    (own,) = tied(token, own)
    ahead, behind = local_call(
        functools.partial(ring_split_kernel, (half,)),
        "ring_split",
        [idx],
        [],
        [own],
        [piece, piece],
        taken(1),
    )
    token = behind
    ahead, behind = ring_shift(ahead, axis, 1), ring_shift(behind, axis, -1)
    token = yield token
    for k in range(half - 1, 0, -1):
        ahead, behind = tied(token, ahead, behind)
        ahead, behind = local_call(
            functools.partial(ring_add_kernel, (k % count, (-k) % count)),
            "ring_add",
            [idx],
            [ahead, behind],
            [own],
            [chunk, chunk],
            taken(2),
        )
        token = behind
        ahead, behind = ring_shift(ahead, axis, 1), ring_shift(behind, axis, -1)
        token = yield token
    ahead, behind = tied(token, ahead, behind)
    (mine,) = local_call(
        functools.partial(ring_own_kernel, (0,)),
        "ring_own",
        [idx],
        [ahead, behind],
        [own],
        [chunk],
        taken(1),
    )
    ahead, behind = ring_shift(mine, axis, 1), ring_shift(mine, axis, -1)
    totals, token = put(None, [mine], [0])
    token = yield token
    for k in range(1, half):
        ahead, behind = tied(token, ahead, behind)
        last = k == half - 1
        next_ahead = ring_shift(ahead[:, :cut] if last else ahead, axis, 1)
        next_behind = ring_shift(behind[:, cut:] if last else behind, axis, -1)
        totals, token = put(totals, [ahead, behind], [-k, k])
        ahead, behind = next_ahead, next_behind
        token = yield token
    ahead, behind = tied(token, ahead, behind)
    totals, token = put(totals, [ahead, behind], [-half, half])
    yield [total.reshape(full_rows, -1) for total in totals]


def butterfly_sum(vals, axis):
    count = lax.axis_size(axis)
    by = 1
    token = yield None
    if count & (count - 1):
        yield lax.psum(tied(token, vals)[0], axis)
        return
    (vals,) = tied(token, vals)
    while by < count:
        got = lax.ppermute(vals, axis, [(i, i ^ by) for i in range(count)])
        token = yield None
        (got,) = tied(token, got)
        vals = vals + got
        by *= 2
    yield vals


def swap(vals):
    return lax.ppermute(vals, "wsh", [(0, 1), (1, 0)])


def pass_on(vals, by):
    pairs = [(0, 1)] if by > 0 else [(1, 0)]
    return lax.ppermute(vals, "section", pairs)


def block_places(block_pair, count):
    want = jnp.arange(2 * count, dtype=jnp.int32)
    device = jnp.arange(count, dtype=jnp.int32)
    first = (block_pair[None, :] == want[:, None]).astype(jnp.int32)
    second = ((2 * count - 1 - block_pair)[None, :] == want[:, None]).astype(jnp.int32)
    return jnp.sum(first * (2 * device) + second * (2 * device + 1), axis=1)


def row_positions(block_pair, stored, tok_dev):
    count = block_pair.shape[0]
    device = stored // tok_dev
    within = stored % tok_dev
    half_rows = tok_dev // 2
    matches = device[:, None] == jnp.arange(count, dtype=jnp.int32)[None, :]
    pair_block = jnp.sum(jnp.where(matches, block_pair[None, :], 0), axis=1)
    block_idx = jnp.where(within < half_rows, pair_block, 2 * count - 1 - pair_block)
    return block_idx * half_rows + within % half_rows


def rotary_table(positions, head_size):
    half_rot = ROT // 2
    lane = jnp.arange(LANES, dtype=jnp.int32) % head_size
    inv_freq = ROPE_BASE ** (-((lane % half_rot).astype(f32) * 2.0) / ROT)
    angles = positions.astype(f32)[:, None] * inv_freq[None, :]
    cosine, sine = jnp.cos(angles), jnp.sin(angles)
    lead, second = (lane < half_rot)[None], ((lane >= half_rot) & (lane < ROT))[None]
    return jnp.stack(
        [
            jnp.where(lead | second, cosine, 1.0),
            jnp.where(lead, -sine, 0.0),
            jnp.where(second, sine, 0.0),
        ]
    )


def body(
    inputs,
    cotangent,
    block_pair,
    qkv_weight,
    qkv_bias,
    proj_weight,
    proj_bias,
    up_weight,
    up_bias,
    down_weight,
    down_bias,
    attn_gain,
    attn_shift,
    mlp_gain,
    mlp_shift,
):
    first_section = lax.axis_index("section") == 0
    count = lax.axis_size("ctx")
    micros, _, tok_dev, dim = inputs.shape
    head_size = dim // HEADS
    half = dim // 2
    my_half = lax.axis_index("wsh")
    wsh = jnp.stack([my_half.astype(jnp.int32), first_section.astype(jnp.int32)])
    one_pair_each = count == dim // LANES

    wq, wp, wu, wd = (w[0] for w in (qkv_weight, proj_weight, up_weight, down_weight))
    small = jnp.concatenate(
        [
            v[0].reshape(-1, half)
            for v in (
                attn_gain,
                attn_shift,
                mlp_gain,
                mlp_shift,
                proj_bias,
                down_bias,
                qkv_bias,
                up_bias,
            )
        ],
        axis=0,
    )
    small_oth = swap(small)
    wq_oth = swap(wq)
    first_here = lax.optimization_barrier((wq_oth, small_oth))
    wq_oth, small_oth = first_here
    wu_oth = swap(tied(wq_oth, wu)[0])
    wd_oth = swap(tied(wq_oth, wd)[0])
    wp_oth = swap(tied(wu_oth, wp)[0])
    low_part = jnp.where(my_half == 0, small, small_oth).astype(f32)
    high_part = jnp.where(my_half == 0, small_oth, small).astype(f32)
    vecs = jnp.concatenate([low_part[:6], high_part[:6]], axis=1)
    qkv_rows = 6 + qkv_bias.shape[1] // half
    proj_b, down_b = vecs[4:5], vecs[5:6]
    qkv_b = jnp.concatenate([low_part[6:qkv_rows], high_part[6:qkv_rows]], axis=0).reshape(1, -1)
    up_b = jnp.concatenate([low_part[qkv_rows:], high_part[qkv_rows:]], axis=0).reshape(1, -1)

    local_rows = lax.axis_index("ctx") * tok_dev + jnp.arange(tok_dev, dtype=jnp.int32)
    query_pos = row_positions(block_pair, local_rows, tok_dev)
    key_pos = row_positions(block_pair, jnp.arange(count * tok_dev, dtype=jnp.int32), tok_dev)
    tab = rotary_table(query_pos, head_size)
    loc = block_places(block_pair, count)

    def exchange(vals):
        return lax.all_to_all(vals, "ctx", split_axis=0, concat_axis=0, tiled=True)

    def norm_qkv(index, got):
        return qkv_call(rows_in[index], got, vecs, qkv_b, tab, wq, wq_oth, wsh)

    def mlp(made, save):
        return mlp_call(made[2], made[3], up_b, down_b, wu, wu_oth, wd, wd_oth, wsh, save)

    def mlp_back(dy, mlp_kept):
        return mlp_back_call(dy, mlp_kept[1], wu, wu_oth, wd, wd_oth, wsh)

    def out_back(index, got):
        return da_call(cot_in[index], got, wp, wp_oth, wsh)

    def to_heads(vals):
        return exchange(vals) if one_pair_each else vals

    def to_rows(vals):
        return exchange(vals) if one_pair_each else vals

    def attend(qkv):
        if one_pair_each:
            attended, lse = attend_call(qkv, loc)
            return attended, (qkv, lse)
        return wide_attend(qkv, query_pos, key_pos)

    def attend_back(kept, da):
        if one_pair_each:
            return attend_back_call(kept[0], da, kept[1], loc)
        return wide_attend_back(kept, da, query_pos, key_pos)

    def project(attended, made, mlp_out):
        return proj_call(attended, made[1], mlp_out[0], proj_b, wp, wp_oth, wsh)

    def input_grad_of(dqkv, made, dy, dnm):
        return dx_call(dqkv, tab, made[1], dy, dnm, vecs, wq, wq_oth, wsh)

    rows_in = [inputs[i, 0] for i in range(micros)]
    cot_in = [cotangent[i, 0] for i in range(micros)]
    made_a = norm_qkv(0, None)
    qkv_a = to_heads(made_a[0])
    mlp_a = mlp(made_a, False)
    (qkv_a,) = tied(mlp_a[0], qkv_a)
    att_a, _ = attend(qkv_a)
    att_a = to_rows(att_a)
    da_a, dy_a = out_back(0, None)
    (att_a,) = tied(dy_a, att_a)
    y_a = project(att_a, made_a, mlp_a)[0]
    da_a = to_heads(tied(y_a, da_a)[0])

    made_b = norm_qkv(1, pass_on(y_a, 1))
    qkv_b_ = to_heads(tied(da_a, made_b[0])[0])
    norms_b = swap(made_b[3])
    mlp_b = mlp(made_b, True)
    (qkv_b_,) = tied((mlp_b[0], norms_b), qkv_b_)
    att_b, kept_b = attend(qkv_b_)
    att_b = to_rows(att_b)
    gt_b = swap(mlp_b[3])
    (da_a,) = tied((gt_b, kept_b[1]), da_a)
    dqkv_a = attend_back(kept_b, da_a)
    (att_b,) = tied(dqkv_a, att_b)
    dqkv_a = to_rows(dqkv_a)
    y_b, *a_b = project(att_b, made_b, mlp_b)

    made_c = norm_qkv(0, pass_on(y_b, 1))
    (dy_a2,) = tied(made_c[1], dy_a)
    _, dnm_a = mlp_back(dy_a2, mlp_b)
    qkv_c = to_heads(made_c[0])
    norms_c = swap(made_c[3])
    a_b_oth = swap(a_b[1])
    (dqkv_a,) = tied((dnm_a, norms_c, a_b_oth), dqkv_a)
    _, dx_a, _ = input_grad_of(dqkv_a, made_b, dy_a, dnm_a)
    got_a = pass_on(dx_a, -1)
    made_c = list(made_c[:2]) + list(tied(dx_a, made_c[2], made_c[3]))
    mlp_c = mlp(made_c, True)
    (got_a,) = tied(mlp_c[0], got_a)
    da_b, dy_b = out_back(1, got_a)
    (qkv_c,) = tied(dy_b, qkv_c)
    da_b = to_heads(tied(qkv_c, da_b)[0])
    att_c, kept_c = attend(qkv_c)
    dy_b_oth, gt_c = swap(dy_b), swap(mlp_c[3])
    (da_b,) = tied((dy_b_oth, gt_c), da_b)
    dqkv_b = attend_back(kept_c, da_b)
    (dy_b2,) = tied(dqkv_b, dy_b)
    dqkv_b = to_rows(dqkv_b)
    du_b, dnm_b = mlp_back(dy_b2, mlp_c)
    du_b_oth = swap(du_b)
    (dqkv_b,) = tied((dnm_b, du_b_oth), dqkv_b)
    back_b, dx_b, sums_b = input_grad_of(dqkv_b, made_c, dy_b, dnm_b)
    got_b = pass_on(dx_b, -1)
    back_b_oth = swap(back_b)
    (got_b,) = tied(back_b_oth, got_b)

    da_c, dy_c = out_back(0, got_b)
    dy_list = [dy_c, dy_b, swap(dy_c), dy_b_oth]
    da_c = to_heads(da_c)
    down_grad, dy_sum = down_grad_call([mlp_b[2], mlp_c[2], gt_b, gt_c], dy_list)
    down_ring = ring_sum(down_grad, (dim,), "ctx")
    next(down_ring)
    token = down_ring.send(dy_sum)
    token = down_ring.send(token)
    (dy_c2,) = tied(token, dy_c)
    du_c, dnm_c = mlp_back(dy_c2, mlp_b)
    token = down_ring.send(dnm_c)
    up_grad, du_sum = up_grad_call(
        [made_b[2], made_c[2], norms_b, norms_c], [du_c, du_b, swap(du_c), du_b_oth]
    )
    up_ring = ring_sum(up_grad, (up_grad.shape[1],), "ctx")
    next(up_ring)
    steps = count + 1
    left = {down_ring: steps - 3, up_ring: steps}
    results = {}

    def turn(ring, token):
        if not left[ring]:
            return token
        left[ring] -= 1
        made = ring.send(token)
        if left[ring] == 0:
            results[ring] = made
            return token
        return made

    token = turn(up_ring, du_sum)
    token = turn(down_ring, token)
    (da_c,) = tied(token, da_c)
    dqkv_c = attend_back(kept_b, da_c)
    token = turn(up_ring, dqkv_c)
    dqkv_c = to_rows(dqkv_c)
    token = turn(down_ring, token)
    token = turn(up_ring, token)
    token = turn(down_ring, token)
    (dqkv_c,) = tied(token, dqkv_c)
    att_c = to_rows(tied(dqkv_c, att_c)[0])
    back_c, dx_c, sums_c = input_grad_of(dqkv_c, made_b, dy_c, dnm_c)
    back_c_oth = swap(back_c)
    token = turn(up_ring, dx_c)
    token = turn(down_ring, token)
    (att_c,) = tied(token, att_c)
    y_c, *a_c = project(att_c, made_c, mlp_c)
    a_c_oth = swap(a_c[1])
    token = turn(up_ring, y_c)
    (back_c2,) = tied(token, back_c)
    attn_grad, attn_sum = attn_grad_call(
        [made_b[2], made_c[2], norms_b, norms_c],
        [a_b[0], a_c[0], a_b_oth, a_c_oth],
        [back_c2, back_b, back_c_oth, back_b_oth],
        dy_list,
    )
    dqkv_sum = attn_sum[:, : 3 * dim]
    attn_ring = ring_sum(attn_grad, (3 * dim, dim), "ctx")
    next(attn_ring)
    left[attn_ring] = steps

    norm_sums = sums_b + sums_c
    norm_own = lax.dynamic_slice_in_dim(norm_sums, my_half * half, half, 1)
    norm_oth = swap(lax.dynamic_slice_in_dim(norm_sums, (1 - my_half) * half, half, 1))

    def own_part(vec):
        size = vec.shape[1] // 2
        return lax.dynamic_slice_in_dim(vec, my_half * size, size, 1).reshape(-1, half)

    token = turn(attn_ring, dqkv_sum)
    token = turn(down_ring, token)
    (norm_oth,) = tied(token, norm_oth)
    small_sums = jnp.concatenate(
        [norm_own + norm_oth, own_part(dy_sum), own_part(dqkv_sum), own_part(du_sum)], axis=0
    )
    small_ring = butterfly_sum(small_sums, "ctx")
    next(small_ring)
    at = 0
    summed = None
    while any(left.values()):
        token = turn((attn_ring, up_ring, attn_ring, down_ring)[at % 4], token)
        if at % 2 == 0 and summed is None:
            summed = small_ring.send(token)
        at += 1
    while summed is None:
        summed = small_ring.send(token)
    small_sums = summed
    (down_grad,) = results[down_ring]
    (up_grad,) = results[up_ring]
    qkv_grad, proj_grad = results[attn_ring]

    qkv_end = 5 + dqkv_sum.shape[1] // 2 // half
    dy_total = small_sums[4:5]
    pick = lambda yes, no: jnp.where(first_section, yes, no)
    layer_out = jnp.stack([pick(y_c, y_b), pick(y_b, y_c)])[None, :, None]
    input_grad = jnp.stack([pick(dx_b, dx_c), pick(dx_c, dx_b)])[None, :, None]
    return (
        layer_out,
        input_grad,
        qkv_grad[None],
        small_sums[5:qkv_end].reshape(1, -1),
        proj_grad[None],
        dy_total,
        up_grad[None],
        small_sums[qkv_end:].reshape(1, -1),
        down_grad[None],
        dy_total,
        small_sums[0:1],
        small_sums[1:2],
        small_sums[2:3],
        small_sums[3:4],
    )


def solution(mesh):
    in_specs = (
        P(None, "wsh", "ctx", None),
        P(None, "wsh", "ctx", None),
        P(),
        P("section", "wsh", None),
        P("section", "wsh"),
        P("section", "wsh", None),
        P("section", "wsh"),
        P("section", "wsh", None),
        P("section", "wsh"),
        P("section", "wsh", None),
        P("section", "wsh"),
        P("section", "wsh"),
        P("section", "wsh"),
        P("section", "wsh"),
        P("section", "wsh"),
    )
    out_specs = (
        P("section", None, "wsh", "ctx", None),
        P("section", None, "wsh", "ctx", None),
        P("section", "wsh", None),
        P("section", "wsh"),
        P("section", "wsh", None),
        P("section", "wsh"),
        P("section", "wsh", None),
        P("section", "wsh"),
        P("section", "wsh", None),
        P("section", "wsh"),
        P("section", "wsh"),
        P("section", "wsh"),
        P("section", "wsh"),
        P("section", "wsh"),
    )
    return jax.shard_map(body, mesh=mesh, in_specs=in_specs, out_specs=out_specs, check_vma=False)
```

```python
import functools

import jax
import jax.numpy as jnp
from jax import lax
from jax.experimental import pallas as pl
from jax.experimental.pallas import tpu as pltpu
from jax.sharding import PartitionSpec as P

HEADS = 16
ROT = 16
NORM_EPS = 1e-05
ROPE_BASE = 10000.0
MASKED_SCORE = -1e30
LANES = 128
VMEM_LIMIT = 50 * 1024 * 1024
INV_SQRT2 = 0.7071067811865476
INV_SQRT_2PI = 0.3989422804014327

f32 = jnp.float32
bf16 = jnp.bfloat16


def dot_nn(left, right):
    return lax.dot_general(left, right, (((1,), (0,)), ((), ())), preferred_element_type=f32)


def dot_nt(left, right):
    return lax.dot_general(left, right, (((1,), (1,)), ((), ())), preferred_element_type=f32)


def params_of(**extra):
    return dict(
        compiler_params=pltpu.CompilerParams(vmem_limit_bytes=VMEM_LIMIT),
        cost_estimate=pl.CostEstimate(flops=1, bytes_accessed=1, transcendentals=0),
        **extra,
    )


def whole(shape):
    rank = len(shape)
    return pl.BlockSpec(shape, lambda *args: (0,) * rank)


def shape_of(shape, dtype):
    return jax.ShapeDtypeStruct(shape, dtype)


def rope(vals, tab_ref):
    return (
        vals * tab_ref[0]
        + pltpu.roll(vals, LANES - ROT // 2, 1) * tab_ref[1]
        + pltpu.roll(vals, ROT // 2, 1) * tab_ref[2]
    )


def unrope(vals, tab_ref):
    return (
        vals * tab_ref[0]
        - pltpu.roll(vals, LANES - ROT // 2, 1) * tab_ref[1]
        - pltpu.roll(vals, ROT // 2, 1) * tab_ref[2]
    )


def normalized(hidden):
    row_mean = jnp.mean(hidden, axis=-1, keepdims=True)
    centered = hidden - row_mean
    spread = jnp.mean(centered * centered, axis=-1, keepdims=True)
    scale = lax.rsqrt(spread + NORM_EPS)
    return centered * scale, scale


def start_all(copies):
    for copy in copies:
        copy.start()
    return copies


def wait_all(copies):
    for copy in copies:
        copy.wait()


def qkv_kernel(index, own_given, wsh_ref, given_ref, got_ref, vec_ref, bias_ref, tab_ref, *rest):
    w_own, w_oth, out_ref, x_ref, own_ref, oth_ref, buf, sems = rest
    half, dim = buf.shape[2:]
    copies = start_all(
        [
            pltpu.make_async_copy(
                weight.at[:, pl.ds(part * dim, dim)], buf.at[part, side], sems.at[part, side]
            )
            for part in range(3)
            for side, weight in enumerate((w_own, w_oth))
        ]
    )
    x = given_ref[index]
    if not own_given:
        x = jnp.where(wsh_ref[1] == 1, x, got_ref[...])
    x_ref[...] = x
    xhat, _ = normalized(x.astype(f32))
    na = (xhat * vec_ref[0:1] + vec_ref[1:2]).astype(bf16)
    nm = (xhat * vec_ref[2:3] + vec_ref[3:4]).astype(bf16)
    first = wsh_ref[0] == 0
    for i, rows in enumerate((na, nm)):
        own_ref[i] = jnp.where(first, rows[:, :half], rows[:, half:])
        oth_ref[i] = jnp.where(first, rows[:, half:], rows[:, :half])
    for part in range(3):
        wait_all(copies[2 * part : 2 * part + 2])
        for at in range(0, dim, 2 * LANES):
            cols = slice(at, at + 2 * LANES)
            res = (
                dot_nn(own_ref[0], buf[part, 0, :, cols])
                + dot_nn(oth_ref[0], buf[part, 1, :, cols])
                + bias_ref[:, part * dim + at : part * dim + at + 2 * LANES]
            )
            for i in range(2):
                vals = res[:, i * LANES : (i + 1) * LANES]
                if part < 2:
                    vals = rope(vals, tab_ref)
                out_ref[at // LANES + i, part] = vals.astype(bf16)


def layer_of(shape, index):
    return pl.BlockSpec((pl.squeezed,) + shape, lambda *args: (index, 0, 0))


HERE = pl.BlockSpec(memory_space=pltpu.VMEM)
SCALARS = pl.BlockSpec(memory_space=pltpu.SMEM)
ANYWHERE = pl.BlockSpec(memory_space=pl.ANY)
IN_HBM = pl.BlockSpec(memory_space=pltpu.HBM)


def local_call(kernel, name, scalars, arrays, weights, out_shape, scratch=()):
    multiple = isinstance(out_shape, (list, tuple))
    return pl.pallas_call(
        kernel,
        in_specs=[SCALARS] * len(scalars) + [HERE] * len(arrays) + [IN_HBM] * len(weights),
        out_specs=[HERE] * len(out_shape) if multiple else HERE,
        out_shape=out_shape,
        scratch_shapes=scratch,
        name=name,
        **params_of(),
    )(*scalars, *arrays, *weights)


def qkv_call(given, index, got, vecs, qkv_b, tab, w_own, w_oth, wsh):
    rows, dim = given.shape[1:]
    half = w_own.shape[0]
    pairs = dim // LANES
    return local_call(
        functools.partial(qkv_kernel, index, got is None),
        "qkv_proj",
        [wsh],
        [given, given if got is None else got, vecs, qkv_b, tab],
        [w_own, w_oth],
        [shape_of((pairs, 3, rows, LANES), bf16), shape_of((rows, dim), bf16)]
        + [shape_of((2, rows, half), bf16)] * 2,
        [pltpu.VMEM((3, 2, half, dim), bf16), pltpu.SemaphoreType.DMA((3, 2))],
    )


FF_TILE = 1024
FF_PIECE = 512


def ff_tiles(wsh_ref, up_own, up_oth, dn_own, dn_oth, up_buf, dn_buf, sems):
    own = dn_own.shape[0] // FF_TILE
    tiles = []
    for t in range(2 * own):
        start = pl.multiple_of(((wsh_ref[0] * own + t) % (2 * own)) * FF_TILE, FF_TILE)
        cols = pl.ds(start, FF_TILE)
        down = (dn_own if t < own else dn_oth).at[pl.ds((t % own) * FF_TILE, FF_TILE)]
        copies = [
            pltpu.make_async_copy(up_own.at[:, cols], up_buf.at[t, 0], sems.at[t, 0]),
            pltpu.make_async_copy(up_oth.at[:, cols], up_buf.at[t, 1], sems.at[t, 1]),
            pltpu.make_async_copy(down, dn_buf.at[t], sems.at[t, 2]),
        ]
        tiles.append((t, start, start_all(copies)))
    for t, start, copies in tiles:
        wait_all(copies)
        for at in range(0, FF_TILE, FF_PIECE):
            row = (t % own) * FF_TILE + at
            place = pl.ds(pl.multiple_of(start + at, FF_PIECE), FF_PIECE)
            yield t, place, t < own, slice(row, row + FF_PIECE), slice(at, at + FF_PIECE)


def ff_scratch(half, ff, dim):
    tiles = ff // FF_TILE
    return [
        pltpu.VMEM((tiles, 2, half, FF_TILE), bf16),
        pltpu.VMEM((tiles, FF_TILE, dim), bf16),
        pltpu.SemaphoreType.DMA((tiles, 3)),
    ]


def mlp_kernel(save, wsh_ref, own_ref, oth_ref, up_b, down_b, *rest):
    weights, outs, (up_buf, dn_buf, sems) = rest[:4], rest[4:-3], rest[-3:]
    out_ref = outs[0]
    out_ref[...] = jnp.broadcast_to(down_b[...], out_ref.shape)
    for t, place, held, rows, piece in ff_tiles(wsh_ref, *weights, up_buf, dn_buf, sems):
        pre = (
            dot_nn(own_ref[1], up_buf[t, 0, :, piece])
            + dot_nn(oth_ref[1], up_buf[t, 1, :, piece])
            + up_b[:, place]
        )
        gate = 0.5 + 0.5 * lax.erf(pre * INV_SQRT2)
        act = (pre * gate).astype(bf16)
        if save:
            slope_ref, gt_own, gt_oth = outs[1:]
            slope = gate + pre * (INV_SQRT_2PI * jnp.exp(-0.5 * pre * pre))
            slope_ref[place] = slope.astype(bf16).T
            (gt_own if held else gt_oth)[rows] = act.T
        out_ref[...] += dot_nn(act, dn_buf[t, piece])


def mlp_call(own, oth, up_b, down_b, up_own, up_oth, dn_own, dn_oth, wsh, save):
    rows, half = own.shape[1:]
    dim = dn_own.shape[1]
    ff = up_own.shape[1]
    out_shape = [shape_of((rows, dim), f32)]
    if save:
        out_shape += [shape_of((ff, rows), bf16)] + [shape_of((ff // 2, rows), bf16)] * 2
    return local_call(
        functools.partial(mlp_kernel, save),
        "mlp_forward",
        [wsh],
        [own, oth, up_b, down_b],
        [up_own, up_oth, dn_own, dn_oth],
        out_shape,
        ff_scratch(half, ff, dim),
    )


def mlp_back_kernel(wsh_ref, dy_ref, slope_ref, *rest):
    weights, (du_ref, dnm_ref, acc_own, acc_oth, up_buf, dn_buf, sems) = rest[:4], rest[4:]
    half = acc_own.shape[0]
    acc_own[...] = jnp.zeros(acc_own.shape, f32)
    acc_oth[...] = jnp.zeros(acc_oth.shape, f32)
    for t, place, _, _, piece in ff_tiles(wsh_ref, *weights, up_buf, dn_buf, sems):
        dact = dot_nt(dn_buf[t, piece], dy_ref[...])
        du = (dact * slope_ref[place].astype(f32)).astype(bf16)
        du_ref[place] = du
        acc_own[...] += dot_nn(up_buf[t, 0, :, piece], du)
        acc_oth[...] += dot_nn(up_buf[t, 1, :, piece], du)
    first = wsh_ref[0] == 0
    dnm_ref[:, :half] = jnp.where(first, acc_own[...], acc_oth[...]).T
    dnm_ref[:, half:] = jnp.where(first, acc_oth[...], acc_own[...]).T


def mlp_back_call(dy, slope, up_own, up_oth, dn_own, dn_oth, wsh):
    rows, dim = dy.shape
    half, ff = up_own.shape
    return local_call(
        mlp_back_kernel,
        "mlp_backward",
        [wsh],
        [dy, slope],
        [up_own, up_oth, dn_own, dn_oth],
        [shape_of(slope.shape, bf16), shape_of((rows, dim), f32)],
        [pltpu.VMEM((half, rows), f32), pltpu.VMEM((half, rows), f32)] + ff_scratch(half, ff, dim),
    )


def sort_in(loc_ref, ref, dst, half_rows, part=None):
    for block in range(dst.shape[0] // half_rows):
        place = loc_ref[block]
        rows = pl.ds(pl.multiple_of((place % 2) * half_rows, half_rows), half_rows)
        if part is None:
            vals = ref[place // 2, rows, :]
        else:
            vals = ref[place // 2, part, rows, :]
        dst[block * half_rows : (block + 1) * half_rows] = vals


def sort_out(loc_ref, vals, ref, half_rows, part=None):
    for block in range(vals.shape[0] // half_rows):
        place = loc_ref[block]
        rows = pl.ds(pl.multiple_of((place % 2) * half_rows, half_rows), half_rows)
        piece = vals[block * half_rows : (block + 1) * half_rows]
        if part is None:
            ref[place // 2, rows, :] = piece
        else:
            ref[place // 2, part, rows, :] = piece


def head_of(vals, head):
    lane = lax.broadcasted_iota(jnp.int32, vals.shape, 1)
    return jnp.where(lane // (LANES // 2) == head, vals, jnp.zeros_like(vals))


def scores_of(keys, queries, scale, diagonal):
    scores = dot_nt(keys, queries) * scale
    if diagonal:
        key_at = lax.broadcasted_iota(jnp.int32, scores.shape, 0)
        query_at = lax.broadcasted_iota(jnp.int32, scores.shape, 1)
        scores = jnp.where(key_at <= query_at, scores, MASKED_SCORE)
    return scores


def attend_kernel(tile, loc_ref, qkv_ref, o_ref, lse_ref, q_s, k_s, v_s, vt_s, o_s):
    half_rows = qkv_ref.shape[2] // 2
    seq = q_s.shape[0]
    head_size = LANES // 2
    scale = head_size**-0.5
    sort_in(loc_ref, qkv_ref, q_s, half_rows, 0)
    sort_in(loc_ref, qkv_ref, k_s, half_rows, 1)
    sort_in(loc_ref, qkv_ref, v_s, half_rows, 2)
    vt_s[...] = v_s[...].T
    for t in range(seq // tile):
        rows = slice(t * tile, (t + 1) * tile)
        queries = q_s[rows]
        outs = []
        for head in range(2):
            picked = head_of(queries, head)
            parts = [
                scores_of(k_s[i * tile : (i + 1) * tile], picked, scale, i == t)
                for i in range(t + 1)
            ]
            top = functools.reduce(
                jnp.maximum, [jnp.max(p, axis=0, keepdims=True) for p in parts]
            )
            parts = [jnp.exp(p - top) for p in parts]
            total = sum(jnp.sum(p, axis=0, keepdims=True) for p in parts)
            lse_ref[head : head + 1, rows] = top + jnp.log(total)
            inverse = 1.0 / total
            acc = None
            for i, p in enumerate(parts):
                term = dot_nn(
                    vt_s[head * head_size : (head + 1) * head_size, i * tile : (i + 1) * tile],
                    (p * inverse).astype(bf16),
                )
                acc = term if acc is None else acc + term
            outs.append(acc)
        o_s[rows] = jnp.concatenate(outs, axis=0).T.astype(bf16)
    sort_out(loc_ref, o_s, o_ref, half_rows)


def attend_call(qkv, loc):
    count, _, rows, _ = qkv.shape
    seq = count * rows
    return local_call(
        functools.partial(attend_kernel, 256),
        "attention",
        [loc],
        [qkv],
        [],
        [shape_of((count, rows, LANES), bf16), shape_of((2, seq), f32)],
        [
            pltpu.VMEM((seq, LANES), bf16),
            pltpu.VMEM((seq, LANES), bf16),
            pltpu.VMEM((seq, LANES), bf16),
            pltpu.VMEM((LANES, seq), bf16),
            pltpu.VMEM((seq, LANES), bf16),
        ],
    )


def attend_back_kernel(
    tile, loc_ref, qkv_ref, da_ref, lse_ref, out_ref, q_s, k_s, v_s, da_s, kt_s, dq_s, dk_s, dv_s
):
    half_rows = qkv_ref.shape[2] // 2
    seq = q_s.shape[0]
    head_size = LANES // 2
    scale = head_size**-0.5
    sort_in(loc_ref, qkv_ref, q_s, half_rows, 0)
    sort_in(loc_ref, qkv_ref, k_s, half_rows, 1)
    sort_in(loc_ref, qkv_ref, v_s, half_rows, 2)
    sort_in(loc_ref, da_ref, da_s, half_rows)
    kt_s[...] = k_s[...].T
    dk_s[...] = jnp.zeros(dk_s.shape, f32)
    dv_s[...] = jnp.zeros(dv_s.shape, f32)
    for t in range(seq // tile):
        rows = slice(t * tile, (t + 1) * tile)
        outs = []
        for head in range(2):
            queries = head_of(q_s[rows], head)
            grads = head_of(da_s[rows], head)
            lse = lse_ref[head : head + 1, rows]
            probs, dprobs, row_dot = [], [], 0.0
            for i in range(t + 1):
                keys = slice(i * tile, (i + 1) * tile)
                p = jnp.exp(scores_of(k_s[keys], queries, scale, i == t) - lse)
                dp = dot_nt(v_s[keys], grads)
                row_dot = row_dot + jnp.sum(p * dp, axis=0, keepdims=True)
                dv_s[keys] += dot_nn(p.astype(bf16), grads)
                probs.append(p)
                dprobs.append(dp)
            acc = None
            for i in range(t + 1):
                keys = slice(i * tile, (i + 1) * tile)
                ds = (probs[i] * (dprobs[i] - row_dot) * scale).astype(bf16)
                dk_s[keys] += dot_nn(ds, queries)
                term = dot_nn(kt_s[head * head_size : (head + 1) * head_size, keys], ds)
                acc = term if acc is None else acc + term
            outs.append(acc)
        dq_s[rows] = jnp.concatenate(outs, axis=0).T.astype(bf16)
    sort_out(loc_ref, dq_s, out_ref, half_rows, 0)
    k_s[...] = dk_s[...].astype(bf16)
    v_s[...] = dv_s[...].astype(bf16)
    sort_out(loc_ref, k_s, out_ref, half_rows, 1)
    sort_out(loc_ref, v_s, out_ref, half_rows, 2)


def attend_back_call(qkv, da, lse, loc):
    count, _, rows, _ = qkv.shape
    seq = count * rows
    return local_call(
        functools.partial(attend_back_kernel, 256),
        "attention_backward",
        [loc],
        [qkv, da, lse],
        [],
        shape_of(qkv.shape, bf16),
        [pltpu.VMEM((seq, LANES), bf16)] * 4
        + [pltpu.VMEM((LANES, seq), bf16), pltpu.VMEM((seq, LANES), bf16)]
        + [pltpu.VMEM((seq, LANES), f32)] * 2,
    )


def by_head(parts):
    pairs, rows, lanes = parts.shape
    return jnp.transpose(parts, (1, 0, 2)).reshape(rows, HEADS, pairs * lanes // HEADS)


def by_pair(heads):
    rows = heads.shape[0]
    return jnp.transpose(heads.reshape(rows, -1, LANES), (1, 0, 2))


def wide_scores(queries, keys, query_pos, key_pos):
    raw = jnp.einsum("qhd,khd->hqk", queries, keys, preferred_element_type=f32)
    allowed = (query_pos[:, None] >= key_pos[None, :])[None]
    return jnp.where(allowed, raw * queries.shape[-1] ** (-0.5), MASKED_SCORE)


def key_blocks(arrays, rows):
    return tuple(a.reshape((a.shape[0] // rows, rows) + a.shape[1:]) for a in arrays)


def wide_attend(qkv, query_pos, key_pos):
    queries = by_head(qkv[:, 0])
    keys = lax.all_gather(by_head(qkv[:, 1]), "ctx", axis=0, tiled=True)
    values = lax.all_gather(by_head(qkv[:, 2]), "ctx", axis=0, tiled=True)
    block = min(512, keys.shape[0])
    split = key_blocks((keys, values, key_pos), block)
    rows, _, head_size = queries.shape

    def max_step(carry, block_in):
        top, total = carry
        scores = wide_scores(queries, block_in[0], query_pos, block_in[2])
        new_top = jnp.maximum(top, jnp.max(scores, axis=-1))
        part = jnp.sum(jnp.exp(scores - new_top[..., None]), axis=-1)
        return ((new_top, total * jnp.exp(top - new_top) + part), None)

    start = (jnp.full((HEADS, rows), MASKED_SCORE, f32), jnp.zeros((HEADS, rows), f32))
    (top, total), _ = lax.scan(max_step, start, split)
    lse = top + jnp.log(total)

    def value_step(running, block_in):
        scores = wide_scores(queries, block_in[0], query_pos, block_in[2])
        probs = jnp.exp(scores - lse[..., None]).astype(bf16)
        term = jnp.einsum("hqk,khd->qhd", probs, block_in[1], preferred_element_type=f32)
        return (running + term, None)

    attended, _ = lax.scan(value_step, jnp.zeros((rows, HEADS, head_size), f32), split)
    return by_pair(attended.astype(bf16)), (queries, keys, values, lse)


def wide_attend_back(kept, da, query_pos, key_pos):
    queries, keys, values, lse = kept
    grads = by_head(da)
    block = min(512, keys.shape[0])
    split = key_blocks((keys, values, key_pos), block)
    scale = queries.shape[-1] ** (-0.5)

    def pieces(block_in):
        scores = wide_scores(queries, block_in[0], query_pos, block_in[2])
        probs = jnp.exp(scores - lse[..., None])
        dprobs = jnp.einsum("qhd,khd->hqk", grads, block_in[1], preferred_element_type=f32)
        return probs, dprobs

    def dot_step(running, block_in):
        probs, dprobs = pieces(block_in)
        return (running + jnp.sum(probs * dprobs, axis=-1), None)

    row_dot, _ = lax.scan(dot_step, jnp.zeros(lse.shape, f32), split)

    def key_step(running, block_in):
        probs, dprobs = pieces(block_in)
        ds = (scale * probs * (dprobs - row_dot[..., None])).astype(bf16)
        running = running + jnp.einsum("hqk,khd->qhd", ds, block_in[0], preferred_element_type=f32)
        dk = jnp.einsum("hqk,qhd->khd", ds, queries, preferred_element_type=f32)
        dv = jnp.einsum("hqk,qhd->khd", probs.astype(bf16), grads, preferred_element_type=f32)
        return (running, (dk.astype(bf16), dv.astype(bf16)))

    dq, (dk, dv) = lax.scan(key_step, jnp.zeros(queries.shape, f32), split)
    dk, dv = (
        lax.psum_scatter(part.reshape(keys.shape), "ctx", scatter_dimension=0, tiled=True)
        for part in (dk, dv)
    )
    return jnp.stack([by_pair(dq.astype(bf16)), by_pair(dk), by_pair(dv)], axis=1)


def lanes_of(ref):
    return jnp.concatenate([ref[i] for i in range(ref.shape[0])], axis=1)


def both_halves(w_own, w_oth, buf, sems):
    return start_all(
        [
            pltpu.make_async_copy(weight, buf.at[side], sems.at[side])
            for side, weight in enumerate((w_own, w_oth))
        ]
    )


def half_scratch(weight):
    return [pltpu.VMEM((2,) + weight.shape, bf16), pltpu.SemaphoreType.DMA((2,))]


def proj_kernel(wsh_ref, a_ref, x_ref, mlp_ref, bias_ref, p_own, p_oth, y_ref, a_own, a_oth, buf, sems):
    copies = both_halves(p_own, p_oth, buf, sems)
    half = buf.shape[1]
    first = wsh_ref[0] == 0
    a = lanes_of(a_ref)
    a_own[...] = jnp.where(first, a[:, :half], a[:, half:])
    a_oth[...] = jnp.where(first, a[:, half:], a[:, :half])
    wait_all(copies)
    attn = dot_nn(a_own[...], buf[0]) + dot_nn(a_oth[...], buf[1]) + bias_ref[...]
    y_ref[...] = (x_ref[...].astype(f32) + attn + mlp_ref[...]).astype(bf16)


def proj_call(a, x, mlp, bias, p_own, p_oth, wsh):
    rows, dim = x.shape
    half = p_own.shape[0]
    return local_call(
        proj_kernel,
        "attn_out",
        [wsh],
        [a, x, mlp, bias],
        [p_own, p_oth],
        [shape_of((rows, dim), bf16)] + [shape_of((rows, half), bf16)] * 2,
        half_scratch(p_own),
    )


def da_kernel(index, own_given, wsh_ref, given_ref, got_ref, p_own, p_oth, out_ref, dy_ref, buf, sems):
    copies = both_halves(p_own, p_oth, buf, sems)
    dy = given_ref[index]
    if not own_given:
        dy = jnp.where(wsh_ref[1] == 1, got_ref[...], dy)
    dy_ref[...] = dy
    wsh = wsh_ref[0]
    count = out_ref.shape[0] // 2
    wait_all(copies)
    for place, side in ((wsh * count, 0), ((1 - wsh) * count, 1)):
        part = dot_nt(dy, buf[side]).astype(bf16)
        for i in range(count):
            out_ref[place + i] = part[:, i * LANES : (i + 1) * LANES]


def da_call(given, index, got, p_own, p_oth, wsh):
    rows, dim = given.shape[1:]
    return local_call(
        functools.partial(da_kernel, index, got is None),
        "attn_out_backward",
        [wsh],
        [given, given if got is None else got],
        [p_own, p_oth],
        [shape_of((dim // LANES, rows, LANES), bf16), shape_of((rows, dim), bf16)],
        half_scratch(p_own),
    )


def dx_kernel(wsh_ref, dqkv_ref, tab_ref, x_ref, dy_ref, dnm_ref, vec_ref, *rest):
    w_own, w_oth, back_ref, dx_ref, sums_ref, grad_s, buf, sems = rest
    copies = both_halves(w_own, w_oth, buf, sems)
    pairs = dqkv_ref.shape[0]
    for part in range(3):
        for pair in range(pairs):
            vals = dqkv_ref[pair, part]
            if part < 2:
                vals = unrope(vals.astype(f32), tab_ref).astype(bf16)
            back_ref[pair, part] = vals
            grad_s[:, pl.ds((part * pairs + pair) * LANES, LANES)] = vals
    first = wsh_ref[0] == 0
    copies[0].wait()
    own = dot_nt(grad_s[...], buf[0])
    copies[1].wait()
    oth = dot_nt(grad_s[...], buf[1])
    dna = jnp.concatenate([jnp.where(first, own, oth), jnp.where(first, oth, own)], axis=1)
    dnm = dnm_ref[...]
    xhat, scale = normalized(x_ref[...].astype(f32))
    grad = dna * vec_ref[0:1] + dnm * vec_ref[2:3]
    inner = (
        grad
        - jnp.mean(grad, axis=-1, keepdims=True)
        - xhat * jnp.mean(grad * xhat, axis=-1, keepdims=True)
    )
    dx_ref[...] = (dy_ref[...].astype(f32) + scale * inner).astype(bf16)
    sums_ref[0:1] = jnp.sum(dna * xhat, axis=0, keepdims=True)
    sums_ref[1:2] = jnp.sum(dna, axis=0, keepdims=True)
    sums_ref[2:3] = jnp.sum(dnm * xhat, axis=0, keepdims=True)
    sums_ref[3:4] = jnp.sum(dnm, axis=0, keepdims=True)


def dx_call(dqkv, tab, x, dy, dnm, vecs, w_own, w_oth, wsh):
    rows, dim = x.shape
    return local_call(
        dx_kernel,
        "section_input_grad",
        [wsh],
        [dqkv, tab, x, dy, dnm, vecs],
        [w_own, w_oth],
        [shape_of(dqkv.shape, bf16), shape_of((rows, dim), bf16), shape_of((4, dim), f32)],
        [pltpu.VMEM((rows, 3 * dim), bf16)] + half_scratch(w_own),
    )


def stack_rows(refs, cols=slice(None)):
    return jnp.concatenate([ref[:, cols] for ref in refs], axis=0)


def down_grad_kernel(micros, *refs):
    gt_refs, dy_refs = refs[:micros], refs[micros : 2 * micros]
    out_ref, sum_ref, dy_s = refs[2 * micros :]

    @pl.when(pl.program_id(0) == 0)
    def _():
        dy = stack_rows(dy_refs)
        dy_s[...] = dy
        sum_ref[...] = jnp.sum(dy.astype(f32), axis=0, keepdims=True)

    left = jnp.concatenate([ref[...] for ref in gt_refs], axis=1)
    out_ref[...] = dot_nn(left, dy_s[...]).astype(bf16)


def down_grad_call(gt_list, dy_list):
    ff_rows, rows = gt_list[0].shape
    dim = dy_list[0].shape[1]
    micros = len(dy_list)
    tile = 512
    return pl.pallas_call(
        functools.partial(down_grad_kernel, micros),
        grid=(ff_rows // tile,),
        in_specs=[pl.BlockSpec((tile, rows), lambda j: (j, 0))] * micros
        + [whole((rows, dim))] * micros,
        out_specs=[pl.BlockSpec((tile, dim), lambda j: (j, 0)), whole((1, dim))],
        out_shape=[shape_of((ff_rows, dim), bf16), shape_of((1, dim), f32)],
        scratch_shapes=[pltpu.VMEM((micros * rows, dim), bf16)],
        name="down_grad",
        **params_of(),
    )(*gt_list, *dy_list)


def up_grad_kernel(micros, *refs):
    x_refs, du_refs = refs[:micros], refs[micros : 2 * micros]
    out_ref, sum_ref, xt_s = refs[2 * micros :]

    @pl.when(pl.program_id(0) == 0)
    def _():
        xt_s[...] = stack_rows(x_refs).T

    du = jnp.concatenate([ref[...] for ref in du_refs], axis=1)
    sum_ref[...] = dot_nt(jnp.ones((8, du.shape[1]), bf16), du)[:1]
    out_ref[...] = dot_nt(xt_s[...], du).astype(bf16)


def up_grad_call(x_list, du_list):
    rows, half = x_list[0].shape[1:]
    ff = du_list[0].shape[0]
    micros = len(x_list)
    tile = 1024
    return pl.pallas_call(
        functools.partial(up_grad_kernel, micros),
        grid=(ff // tile,),
        in_specs=[layer_of((rows, half), 1)] * micros
        + [pl.BlockSpec((tile, rows), lambda j: (j, 0))] * micros,
        out_specs=[
            pl.BlockSpec((half, tile), lambda j: (0, j)),
            pl.BlockSpec((1, tile), lambda j: (0, j)),
        ],
        out_shape=[shape_of((half, ff), bf16), shape_of((1, ff), f32)],
        scratch_shapes=[pltpu.VMEM((half, micros * rows), bf16)],
        name="up_grad",
        **params_of(),
    )(*x_list, *du_list)


def attn_grad_kernel(micros, *refs):
    x_refs, a_refs, d_refs, dy_refs = (refs[i * micros : (i + 1) * micros] for i in range(4))
    out_ref, sum_ref, xt_s = refs[4 * micros :]
    part = pl.program_id(0)

    def finish(dy):
        sum_ref[...] = jnp.sum(dy.astype(f32), axis=0, keepdims=True)
        out_ref[...] = dot_nn(xt_s[...], dy).astype(bf16)

    @pl.when(part == 0)
    def _():
        xt_s[...] = stack_rows(x_refs).T

    @pl.when(part < 3)
    def _():
        finish(jnp.concatenate([lanes_of(ref) for ref in d_refs], axis=0))

    @pl.when(part == 3)
    def _():
        xt_s[...] = stack_rows(a_refs).T
        finish(stack_rows(dy_refs))


def attn_grad_call(x_list, a_list, d_list, dy_list):
    rows, half = x_list[0].shape[1:]
    pairs = d_list[0].shape[0]
    dim = pairs * LANES
    micros = len(x_list)
    d_spec = pl.BlockSpec(
        (pairs, pl.squeezed, rows, LANES), lambda j: (0, jnp.minimum(j, 2), 0, 0)
    )
    return pl.pallas_call(
        functools.partial(attn_grad_kernel, micros),
        grid=(4,),
        in_specs=[layer_of((rows, half), 0)] * micros
        + [whole((rows, half))] * micros
        + [d_spec] * micros
        + [whole((rows, dim))] * micros,
        out_specs=[
            pl.BlockSpec((half, dim), lambda j: (0, j)),
            pl.BlockSpec((1, dim), lambda j: (0, j)),
        ],
        out_shape=[shape_of((half, 4 * dim), bf16), shape_of((1, 4 * dim), f32)],
        scratch_shapes=[pltpu.VMEM((half, micros * rows), bf16)],
        name="attn_grad",
        **params_of(),
    )(*x_list, *a_list, *d_list, *dy_list)


def ring_of(count):
    return list(range(0, count, 2)) + list(range(count - 1, 0, -2))


def ring_place(axis):
    count = lax.axis_size(axis)
    me = lax.axis_index(axis)
    return jnp.where(me % 2 == 0, me // 2, count - (me + 1) // 2)


def ring_shift(vals, axis, by):
    order = ring_of(lax.axis_size(axis))
    count = len(order)
    pairs = [(order[i], order[(i + by) % count]) for i in range(count)]
    return lax.ppermute(vals, axis, pairs)


def tied(token, *vals):
    return lax.optimization_barrier((token, vals))[1]


def fetch(idx_ref, slots, own_ref, bufs, sems):
    return start_all(
        [
            pltpu.make_async_copy(own_ref.at[idx_ref[slot]], bufs.at[i], sems.at[i])
            for i, slot in enumerate(slots)
        ]
    )


def ring_split_kernel(slots, idx_ref, own_ref, ahead_ref, behind_ref, bufs, sems):
    wait_all(fetch(idx_ref, slots, own_ref, bufs, sems))
    cut = ahead_ref.shape[1]
    ahead_ref[...] = bufs[0, :, :cut]
    behind_ref[...] = bufs[0, :, cut:]


def ring_add_kernel(slots, idx_ref, ahead_ref, behind_ref, own_ref, out_a, out_b, bufs, sems):
    def total(left, right):
        return (left.astype(f32) + right.astype(f32)).astype(bf16)

    wait_all(fetch(idx_ref, slots, own_ref, bufs, sems))
    cut = ahead_ref.shape[1]
    if cut < out_a.shape[1]:
        out_a[:, :cut] = total(bufs[0, :, :cut], ahead_ref[...])
        out_a[:, cut:] = bufs[0, :, cut:]
        out_b[:, :cut] = bufs[1, :, :cut]
        out_b[:, cut:] = total(bufs[1, :, cut:], behind_ref[...])
    else:
        out_a[...] = total(bufs[0], ahead_ref[...])
        out_b[...] = total(bufs[1], behind_ref[...])


def put_copies(chunk, cols, buf, totals, starts, sem):
    lo, hi = cols, cols + buf.shape[1]
    copies = []
    for i, (total, start) in enumerate(zip(totals, starts)):
        first, last = max(lo, start), min(hi, start + total.shape[2])
        if first < last:
            copies.append(
                pltpu.make_async_copy(
                    buf.at[:, pl.ds(first - lo, last - first)],
                    total.at[chunk, :, pl.ds(first - start, last - first)],
                    sem.at[i],
                )
            )
    return copies


def ring_own_kernel(idx_ref, ahead_ref, behind_ref, own_ref, out_ref, bufs, sems):
    wait_all(fetch(idx_ref, (0,), own_ref, bufs, sems))
    out_ref[...] = (
        bufs[0].astype(f32) + ahead_ref[...].astype(f32) + behind_ref[...].astype(f32)
    ).astype(bf16)


def ring_put_kernel(starts, slots, cols, fresh, idx_ref, *refs):
    number = len(slots)
    pieces = refs[:number]
    refs = refs[number + (0 if fresh else len(starts)) :]
    totals, (token_ref, wide, sems) = refs[: len(starts)], refs[len(starts) :]
    leaving = []
    for i in range(number):
        wide[i] = pieces[i][...].astype(f32)
        leaving += start_all(
            put_copies(idx_ref[slots[i]], cols[i], wide.at[i], totals, starts, sems.at[i])
        )
    token_ref[...] = jnp.zeros(token_ref.shape, f32)
    wait_all(leaving)


def ring_sum(own, widths, axis):
    count = lax.axis_size(axis)
    half = count // 2
    full_rows, cols = own.shape
    rows = full_rows // count
    own = own.reshape(count, rows, cols)
    cut = cols // 2
    starts = [sum(widths[:i]) for i in range(len(widths))]
    idx = (ring_place(axis) + jnp.arange(count, dtype=jnp.int32)) % count
    chunk, piece = shape_of((rows, cols), bf16), shape_of((rows, cut), bf16)
    sums = [shape_of((count, rows, width), f32) for width in widths]

    def taken(number):
        return [pltpu.VMEM((number, rows, cols), bf16), pltpu.SemaphoreType.DMA((number,))]

    def put(totals, pieces, slots):
        number, width = len(pieces), pieces[0].shape[1]
        first_cols = (0,) * number if width == cols else (0, cut)
        fresh = totals is None
        out = pl.pallas_call(
            functools.partial(
                ring_put_kernel, starts, tuple(k % count for k in slots), first_cols, fresh
            ),
            in_specs=[SCALARS] + [HERE] * number + [IN_HBM] * (0 if fresh else len(sums)),
            out_specs=[IN_HBM] * len(sums) + [HERE],
            out_shape=sums + [shape_of((8, LANES), f32)],
            scratch_shapes=[
                pltpu.VMEM((number, rows, width), f32),
                pltpu.SemaphoreType.DMA((number, len(sums))),
            ],
            input_output_aliases={} if fresh else {1 + number + i: i for i in range(len(sums))},
            name="ring_put",
            **params_of(),
        )(idx, *pieces, *([] if fresh else totals))
        return out[:-1], out[-1]

    token = yield None
    (own,) = tied(token, own)
    ahead, behind = local_call(
        functools.partial(ring_split_kernel, (half,)),
        "ring_split",
        [idx],
        [],
        [own],
        [piece, piece],
        taken(1),
    )
    token = behind
    ahead, behind = ring_shift(ahead, axis, 1), ring_shift(behind, axis, -1)
    token = yield token
    for k in range(half - 1, 0, -1):
        ahead, behind = tied(token, ahead, behind)
        ahead, behind = local_call(
            functools.partial(ring_add_kernel, (k % count, (-k) % count)),
            "ring_add",
            [idx],
            [ahead, behind],
            [own],
            [chunk, chunk],
            taken(2),
        )
        token = behind
        ahead, behind = ring_shift(ahead, axis, 1), ring_shift(behind, axis, -1)
        token = yield token
    ahead, behind = tied(token, ahead, behind)
    mine = local_call(
        ring_own_kernel, "ring_own", [idx], [ahead, behind], [own], chunk, taken(1)
    )
    ahead, behind = ring_shift(mine, axis, 1), ring_shift(mine, axis, -1)
    totals, token = put(None, [mine], [0])
    token = yield token
    for k in range(1, half):
        ahead, behind = tied(token, ahead, behind)
        last = k == half - 1
        next_ahead = ring_shift(ahead[:, :cut] if last else ahead, axis, 1)
        next_behind = ring_shift(behind[:, cut:] if last else behind, axis, -1)
        totals, token = put(totals, [ahead, behind], [-k, k])
        ahead, behind = next_ahead, next_behind
        token = yield token
    ahead, behind = tied(token, ahead, behind)
    totals, token = put(totals, [ahead, behind], [-half, half])
    yield [total.reshape(full_rows, -1) for total in totals]


def butterfly_sum(vals, axis):
    count = lax.axis_size(axis)
    by = 1
    token = yield None
    if count & (count - 1):
        yield lax.psum(tied(token, vals)[0], axis)
        return
    (vals,) = tied(token, vals)
    while by < count:
        got = lax.ppermute(vals, axis, [(i, i ^ by) for i in range(count)])
        token = yield None
        (got,) = tied(token, got)
        vals = vals + got
        by *= 2
    yield vals


def swap(vals):
    return lax.ppermute(vals, "wsh", [(0, 1), (1, 0)])


def pass_on(vals, by):
    pairs = [(0, 1)] if by > 0 else [(1, 0)]
    return lax.ppermute(vals, "section", pairs)


def block_places(block_pair, count):
    want = jnp.arange(2 * count, dtype=jnp.int32)
    device = jnp.arange(count, dtype=jnp.int32)
    first = (block_pair[None, :] == want[:, None]).astype(jnp.int32)
    second = ((2 * count - 1 - block_pair)[None, :] == want[:, None]).astype(jnp.int32)
    return jnp.sum(first * (2 * device) + second * (2 * device + 1), axis=1)


def row_positions(block_pair, stored, tok_dev):
    count = block_pair.shape[0]
    device = stored // tok_dev
    within = stored % tok_dev
    half_rows = tok_dev // 2
    matches = device[:, None] == jnp.arange(count, dtype=jnp.int32)[None, :]
    pair_block = jnp.sum(jnp.where(matches, block_pair[None, :], 0), axis=1)
    block_idx = jnp.where(within < half_rows, pair_block, 2 * count - 1 - pair_block)
    return block_idx * half_rows + within % half_rows


def rotary_table(positions, head_size):
    half_rot = ROT // 2
    lane = jnp.arange(LANES, dtype=jnp.int32) % head_size
    inv_freq = ROPE_BASE ** (-((lane % half_rot).astype(f32) * 2.0) / ROT)
    angles = positions.astype(f32)[:, None] * inv_freq[None, :]
    cosine, sine = jnp.cos(angles), jnp.sin(angles)
    lead, second = (lane < half_rot)[None], ((lane >= half_rot) & (lane < ROT))[None]
    return jnp.stack(
        [
            jnp.where(lead | second, cosine, 1.0),
            jnp.where(lead, -sine, 0.0),
            jnp.where(second, sine, 0.0),
        ]
    )


def body(
    inputs,
    cotangent,
    block_pair,
    qkv_weight,
    qkv_bias,
    proj_weight,
    proj_bias,
    up_weight,
    up_bias,
    down_weight,
    down_bias,
    attn_gain,
    attn_shift,
    mlp_gain,
    mlp_shift,
):
    first_section = lax.axis_index("section") == 0
    count = lax.axis_size("ctx")
    micros, _, tok_dev, dim = inputs.shape
    head_size = dim // HEADS
    half = dim // 2
    my_half = lax.axis_index("wsh")
    wsh = jnp.stack([my_half.astype(jnp.int32), first_section.astype(jnp.int32)])
    one_pair_each = count == dim // LANES

    wq, wp, wu, wd = (w[0] for w in (qkv_weight, proj_weight, up_weight, down_weight))
    small = jnp.concatenate(
        [
            v[0].reshape(-1, half)
            for v in (
                attn_gain,
                attn_shift,
                mlp_gain,
                mlp_shift,
                proj_bias,
                down_bias,
                qkv_bias,
                up_bias,
            )
        ],
        axis=0,
    )
    small_oth = swap(small)
    wq_oth = swap(wq)
    first_here = lax.optimization_barrier((wq_oth, small_oth))
    wq_oth, small_oth = first_here
    wu_oth = swap(tied(wq_oth, wu)[0])
    wd_oth = swap(tied(wq_oth, wd)[0])
    wp_oth = swap(tied(wu_oth, wp)[0])
    low_part = jnp.where(my_half == 0, small, small_oth).astype(f32)
    high_part = jnp.where(my_half == 0, small_oth, small).astype(f32)
    vecs = jnp.concatenate([low_part[:6], high_part[:6]], axis=1)
    qkv_rows = 6 + qkv_bias.shape[1] // half
    proj_b, down_b = vecs[4:5], vecs[5:6]
    qkv_b = jnp.concatenate([low_part[6:qkv_rows], high_part[6:qkv_rows]], axis=0).reshape(1, -1)
    up_b = jnp.concatenate([low_part[qkv_rows:], high_part[qkv_rows:]], axis=0).reshape(1, -1)

    local_rows = lax.axis_index("ctx") * tok_dev + jnp.arange(tok_dev, dtype=jnp.int32)
    query_pos = row_positions(block_pair, local_rows, tok_dev)
    key_pos = row_positions(block_pair, jnp.arange(count * tok_dev, dtype=jnp.int32), tok_dev)
    tab = rotary_table(query_pos, head_size)
    loc = block_places(block_pair, count)

    def exchange(vals):
        return lax.all_to_all(vals, "ctx", split_axis=0, concat_axis=0, tiled=True)

    def norm_qkv(index, got):
        return qkv_call(rows_in, index, got, vecs, qkv_b, tab, wq, wq_oth, wsh)

    def mlp(made, save):
        return mlp_call(made[2], made[3], up_b, down_b, wu, wu_oth, wd, wd_oth, wsh, save)

    def mlp_back(dy, mlp_kept):
        return mlp_back_call(dy, mlp_kept[1], wu, wu_oth, wd, wd_oth, wsh)

    def out_back(index, got):
        return da_call(cot_in, index, got, wp, wp_oth, wsh)

    def to_heads(vals):
        return exchange(vals) if one_pair_each else vals

    def to_rows(vals):
        return exchange(vals) if one_pair_each else vals

    def attend(qkv):
        if one_pair_each:
            attended, lse = attend_call(qkv, loc)
            return attended, (qkv, lse)
        return wide_attend(qkv, query_pos, key_pos)

    def attend_back(kept, da):
        if one_pair_each:
            return attend_back_call(kept[0], da, kept[1], loc)
        return wide_attend_back(kept, da, query_pos, key_pos)

    def project(attended, made, mlp_out):
        return proj_call(attended, made[1], mlp_out[0], proj_b, wp, wp_oth, wsh)

    def input_grad_of(dqkv, made, dy, dnm):
        return dx_call(dqkv, tab, made[1], dy, dnm, vecs, wq, wq_oth, wsh)

    rows_in, cot_in = inputs[:, 0], cotangent[:, 0]
    made_a = norm_qkv(0, None)
    qkv_a = to_heads(made_a[0])
    mlp_a = mlp(made_a, False)
    (qkv_a,) = tied(mlp_a[0], qkv_a)
    att_a, _ = attend(qkv_a)
    att_a = to_rows(att_a)
    da_a, dy_a = out_back(0, None)
    (att_a,) = tied(dy_a, att_a)
    y_a = project(att_a, made_a, mlp_a)[0]
    da_a = to_heads(tied(y_a, da_a)[0])

    made_b = norm_qkv(1, pass_on(y_a, 1))
    qkv_b_ = to_heads(tied(da_a, made_b[0])[0])
    norms_b = swap(made_b[3])
    mlp_b = mlp(made_b, True)
    (qkv_b_,) = tied((mlp_b[0], norms_b), qkv_b_)
    att_b, kept_b = attend(qkv_b_)
    att_b = to_rows(att_b)
    gt_b = swap(mlp_b[3])
    (da_a,) = tied((gt_b, kept_b[1]), da_a)
    dqkv_a = attend_back(kept_b, da_a)
    (att_b,) = tied(dqkv_a, att_b)
    dqkv_a = to_rows(dqkv_a)
    y_b, *a_b = project(att_b, made_b, mlp_b)

    made_c = norm_qkv(0, pass_on(y_b, 1))
    (dy_a2,) = tied(made_c[1], dy_a)
    _, dnm_a = mlp_back(dy_a2, mlp_b)
    qkv_c = to_heads(made_c[0])
    norms_c = swap(made_c[3])
    a_b_oth = swap(a_b[1])
    (dqkv_a,) = tied((dnm_a, norms_c, a_b_oth), dqkv_a)
    _, dx_a, _ = input_grad_of(dqkv_a, made_b, dy_a, dnm_a)
    got_a = pass_on(dx_a, -1)
    made_c = list(made_c[:2]) + list(tied(dx_a, made_c[2], made_c[3]))
    mlp_c = mlp(made_c, True)
    (got_a,) = tied(mlp_c[0], got_a)
    da_b, dy_b = out_back(1, got_a)
    (qkv_c,) = tied(dy_b, qkv_c)
    da_b = to_heads(tied(qkv_c, da_b)[0])
    att_c, kept_c = attend(qkv_c)
    dy_b_oth, gt_c = swap(dy_b), swap(mlp_c[3])
    (da_b,) = tied((dy_b_oth, gt_c), da_b)
    dqkv_b = attend_back(kept_c, da_b)
    (dy_b2,) = tied(dqkv_b, dy_b)
    dqkv_b = to_rows(dqkv_b)
    du_b, dnm_b = mlp_back(dy_b2, mlp_c)
    du_b_oth = swap(du_b)
    (dqkv_b,) = tied((dnm_b, du_b_oth), dqkv_b)
    back_b, dx_b, sums_b = input_grad_of(dqkv_b, made_c, dy_b, dnm_b)
    got_b = pass_on(dx_b, -1)
    back_b_oth = swap(back_b)
    (got_b,) = tied(back_b_oth, got_b)

    da_c, dy_c = out_back(0, got_b)
    dy_list = [dy_c, dy_b, swap(dy_c), dy_b_oth]
    da_c = to_heads(da_c)
    down_grad, dy_sum = down_grad_call([mlp_b[2], mlp_c[2], gt_b, gt_c], dy_list)
    down_grad = lax.psum(down_grad, "ctx")
    (dy_c2,) = tied(dy_sum, dy_c)
    du_c, dnm_c = mlp_back(dy_c2, mlp_b)
    up_grad, du_sum = up_grad_call(
        [made_b[2], made_c[2], norms_b, norms_c], [du_c, du_b, swap(du_c), du_b_oth]
    )
    up_ring = ring_sum(up_grad, (up_grad.shape[1],), "ctx")
    next(up_ring)
    steps = count + 1
    left = {up_ring: steps}
    results = {}

    def turn(ring, token):
        if not left[ring]:
            return token
        left[ring] -= 1
        made = ring.send(token)
        if left[ring] == 0:
            results[ring] = made
            return token
        return made

    token = turn(up_ring, du_sum)
    (da_c,) = tied(token, da_c)
    dqkv_c = attend_back(kept_b, da_c)
    token = turn(up_ring, dqkv_c)
    dqkv_c = to_rows(dqkv_c)
    token = turn(up_ring, token)
    token = turn(up_ring, token)
    (dqkv_c,) = tied(token, dqkv_c)
    att_c = to_rows(tied(dqkv_c, att_c)[0])
    back_c, dx_c, sums_c = input_grad_of(dqkv_c, made_b, dy_c, dnm_c)
    back_c_oth = swap(back_c)
    token = turn(up_ring, dx_c)
    (att_c,) = tied(token, att_c)
    y_c, *a_c = project(att_c, made_c, mlp_c)
    a_c_oth = swap(a_c[1])
    token = turn(up_ring, y_c)
    (back_c2,) = tied(token, back_c)
    attn_grad, attn_sum = attn_grad_call(
        [made_b[2], made_c[2], norms_b, norms_c],
        [a_b[0], a_c[0], a_b_oth, a_c_oth],
        [back_c2, back_b, back_c_oth, back_b_oth],
        dy_list,
    )
    dqkv_sum = attn_sum[:, : 3 * dim]
    attn_ring = ring_sum(attn_grad, (3 * dim, dim), "ctx")
    next(attn_ring)
    left[attn_ring] = steps

    norm_sums = sums_b + sums_c
    norm_own = lax.dynamic_slice_in_dim(norm_sums, my_half * half, half, 1)
    norm_oth = swap(lax.dynamic_slice_in_dim(norm_sums, (1 - my_half) * half, half, 1))

    def own_part(vec):
        size = vec.shape[1] // 2
        return lax.dynamic_slice_in_dim(vec, my_half * size, size, 1).reshape(-1, half)

    token = turn(attn_ring, dqkv_sum)
    (norm_oth,) = tied(token, norm_oth)
    small_sums = jnp.concatenate(
        [norm_own + norm_oth, own_part(dy_sum), own_part(dqkv_sum), own_part(du_sum)], axis=0
    )
    small_ring = butterfly_sum(small_sums, "ctx")
    next(small_ring)
    at = 0
    summed = None
    while any(left.values()):
        token = turn((attn_ring, up_ring)[at % 2], token)
        if at % 2 == 0 and summed is None:
            summed = small_ring.send(token)
        at += 1
    while summed is None:
        summed = small_ring.send(token)
    small_sums = summed
    down_grad = tied(token, down_grad)[0].astype(f32)
    (up_grad,) = results[up_ring]
    qkv_grad, proj_grad = results[attn_ring]

    qkv_end = 5 + dqkv_sum.shape[1] // 2 // half
    dy_total = small_sums[4:5]
    pick = lambda yes, no: jnp.where(first_section, yes, no)
    layer_out = jnp.stack([pick(y_c, y_b), pick(y_b, y_c)])[None, :, None]
    input_grad = jnp.stack([pick(dx_b, dx_c), pick(dx_c, dx_b)])[None, :, None]
    return (
        layer_out,
        input_grad,
        qkv_grad[None],
        small_sums[5:qkv_end].reshape(1, -1),
        proj_grad[None],
        dy_total,
        up_grad[None],
        small_sums[qkv_end:].reshape(1, -1),
        down_grad[None],
        dy_total,
        small_sums[0:1],
        small_sums[1:2],
        small_sums[2:3],
        small_sums[3:4],
    )


def solution(mesh):
    in_specs = (
        P(None, "wsh", "ctx", None),
        P(None, "wsh", "ctx", None),
        P(),
        P("section", "wsh", None),
        P("section", "wsh"),
        P("section", "wsh", None),
        P("section", "wsh"),
        P("section", "wsh", None),
        P("section", "wsh"),
        P("section", "wsh", None),
        P("section", "wsh"),
        P("section", "wsh"),
        P("section", "wsh"),
        P("section", "wsh"),
        P("section", "wsh"),
    )
    out_specs = (
        P("section", None, "wsh", "ctx", None),
        P("section", None, "wsh", "ctx", None),
        P("section", "wsh", None),
        P("section", "wsh"),
        P("section", "wsh", None),
        P("section", "wsh"),
        P("section", "wsh", None),
        P("section", "wsh"),
        P("section", "wsh", None),
        P("section", "wsh"),
        P("section", "wsh"),
        P("section", "wsh"),
        P("section", "wsh"),
        P("section", "wsh"),
    )
    return jax.shard_map(body, mesh=mesh, in_specs=in_specs, out_specs=out_specs, check_vma=False)
```

```python
import functools

import jax
import jax.numpy as jnp
from jax import lax
from jax.experimental import pallas as pl
from jax.experimental.pallas import tpu as pltpu
from jax.sharding import PartitionSpec as P

HEADS = 16
ROT = 16
NORM_EPS = 1e-05
ROPE_BASE = 10000.0
MASKED_SCORE = -1e30
LANES = 128
VMEM_LIMIT = 50 * 1024 * 1024
INV_SQRT2 = 0.7071067811865476
INV_SQRT_2PI = 0.3989422804014327

f32 = jnp.float32
bf16 = jnp.bfloat16


def dot_nn(left, right):
    return lax.dot_general(left, right, (((1,), (0,)), ((), ())), preferred_element_type=f32)


def dot_nt(left, right):
    return lax.dot_general(left, right, (((1,), (1,)), ((), ())), preferred_element_type=f32)


def params_of(**extra):
    return dict(
        compiler_params=pltpu.CompilerParams(vmem_limit_bytes=VMEM_LIMIT),
        cost_estimate=pl.CostEstimate(flops=1, bytes_accessed=1, transcendentals=0),
        **extra,
    )


def whole(shape):
    rank = len(shape)
    return pl.BlockSpec(shape, lambda *args: (0,) * rank)


def shape_of(shape, dtype):
    return jax.ShapeDtypeStruct(shape, dtype)


def rope(vals, tab_ref):
    return (
        vals * tab_ref[0]
        + pltpu.roll(vals, LANES - ROT // 2, 1) * tab_ref[1]
        + pltpu.roll(vals, ROT // 2, 1) * tab_ref[2]
    )


def unrope(vals, tab_ref):
    return (
        vals * tab_ref[0]
        - pltpu.roll(vals, LANES - ROT // 2, 1) * tab_ref[1]
        - pltpu.roll(vals, ROT // 2, 1) * tab_ref[2]
    )


def normalized(hidden):
    row_mean = jnp.mean(hidden, axis=-1, keepdims=True)
    centered = hidden - row_mean
    spread = jnp.mean(centered * centered, axis=-1, keepdims=True)
    scale = lax.rsqrt(spread + NORM_EPS)
    return centered * scale, scale


def start_all(copies):
    for copy in copies:
        copy.start()
    return copies


def wait_all(copies):
    for copy in copies:
        copy.wait()


def qkv_kernel(own_given, wsh_ref, inputs, weights, outputs, buf, sems):
    half, dim = buf.shape[2:]
    copies = start_all(
        [
            pltpu.make_async_copy(
                weight.at[:, pl.ds(part * dim, dim)], buf.at[part, side], sems.at[part, side]
            )
            for part in range(3)
            for side, weight in enumerate(weights)
        ]
    )
    out, x_out, own, oth = outputs
    x = inputs[0].ref()[...]
    if not own_given:
        x = jnp.where(wsh_ref[1] == 1, x, inputs[4].ref()[...])
    x_out.ref[...] = x
    x_out.send()
    xhat, _ = normalized(x.astype(f32))
    vec_ref, bias_ref, tab_ref = (item.ref() for item in inputs[1:4])
    na = (xhat * vec_ref[0:1] + vec_ref[1:2]).astype(bf16)
    nm = (xhat * vec_ref[2:3] + vec_ref[3:4]).astype(bf16)
    first = wsh_ref[0] == 0
    for i, rows in enumerate((na, nm)):
        own.ref[i] = jnp.where(first, rows[:, :half], rows[:, half:])
        oth.ref[i] = jnp.where(first, rows[:, half:], rows[:, :half])
    own.send()
    oth.send()
    for part in range(3):
        wait_all(copies[2 * part : 2 * part + 2])
        for at in range(0, dim, 2 * LANES):
            cols = slice(at, at + 2 * LANES)
            res = (
                dot_nn(own.ref[0], buf[part, 0, :, cols])
                + dot_nn(oth.ref[0], buf[part, 1, :, cols])
                + bias_ref[:, part * dim + at : part * dim + at + 2 * LANES]
            )
            for i in range(2):
                vals = res[:, i * LANES : (i + 1) * LANES]
                if part < 2:
                    vals = rope(vals, tab_ref)
                out.ref[at // LANES + i, part] = vals.astype(bf16)


def layer_of(shape, index):
    return pl.BlockSpec((pl.squeezed,) + shape, lambda *args: (index, 0, 0))


HERE = pl.BlockSpec(memory_space=pltpu.VMEM)
SCALARS = pl.BlockSpec(memory_space=pltpu.SMEM)
ANYWHERE = pl.BlockSpec(memory_space=pl.ANY)
IN_HBM = pl.BlockSpec(memory_space=pltpu.HBM)


class Arriving:
    def __init__(self, buf, copy=None):
        self.buf, self.copy = buf, copy

    def ref(self):
        if self.copy is not None:
            self.copy.wait()
            self.copy = None
        return self.buf


class Leaving:
    def __init__(self, buf, copy=None):
        self.ref, self.copy, self.sent = buf, copy, copy is None

    def send(self):
        if not self.sent:
            self.copy.start()
            self.sent = True


def local_kernel(body, near_in, near_out, scalars, weights, followed, *refs):
    refs = list(refs)

    def take(number):
        taken = refs[:number]
        del refs[:number]
        return taken

    scalar_refs, array_refs = take(scalars), take(len(near_in))
    weight_refs, _, out_refs = take(weights), take(followed), take(len(near_out))
    in_sems, out_sems = take(2)
    inputs, outputs = [], []
    for i, (near, ref) in enumerate(zip(near_in, array_refs)):
        if near:
            inputs.append(Arriving(ref))
        else:
            buf = take(1)[0]
            copy = pltpu.make_async_copy(ref, buf, in_sems.at[i])
            copy.start()
            inputs.append(Arriving(buf, copy))
    for i, (near, ref) in enumerate(zip(near_out, out_refs)):
        if near:
            outputs.append(Leaving(ref))
        else:
            buf = take(1)[0]
            outputs.append(Leaving(buf, pltpu.make_async_copy(buf, ref, out_sems.at[i])))
    body(*scalar_refs, inputs, weight_refs, outputs, *refs)
    for item in inputs:
        item.ref()
    for item in outputs:
        item.send()
    for item in outputs:
        if item.copy is not None:
            item.copy.wait()


def far(array):
    return (array,)


def local_call(body, name, scalars, arrays, weights, out_shape, scratch=(), after=()):
    near_in = [not isinstance(a, tuple) for a in arrays]
    near_out = [not isinstance(o, tuple) for o in out_shape]
    arrays = [a if near else a[0] for a, near in zip(arrays, near_in)]
    shapes = [o if near else o[0] for o, near in zip(out_shape, near_out)]
    far_bufs = [
        pltpu.VMEM(a.shape, a.dtype)
        for a, near in zip(arrays + shapes, near_in + near_out)
        if not near
    ]
    return pl.pallas_call(
        functools.partial(
            local_kernel, body, near_in, near_out, len(scalars), len(weights), len(after)
        ),
        in_specs=[SCALARS] * len(scalars)
        + [HERE if near else IN_HBM for near in near_in]
        + [IN_HBM] * len(weights)
        + [ANYWHERE] * len(after),
        out_specs=[HERE if near else IN_HBM for near in near_out],
        out_shape=shapes,
        scratch_shapes=[
            pltpu.SemaphoreType.DMA((len(arrays) + 1,)),
            pltpu.SemaphoreType.DMA((len(shapes),)),
        ]
        + far_bufs
        + list(scratch),
        name=name,
        **params_of(),
    )(*scalars, *arrays, *weights, *after)


def qkv_call(given, got, vecs, qkv_b, tab, w_own, w_oth, wsh):
    rows, dim = given.shape
    half = w_own.shape[0]
    pairs = dim // LANES
    return local_call(
        functools.partial(qkv_kernel, got is None),
        "qkv_proj",
        [wsh],
        [given, vecs, qkv_b, tab] if got is None else [far(given), vecs, qkv_b, tab, got],
        [w_own, w_oth],
        [far(shape_of((pairs, 3, rows, LANES), bf16)), far(shape_of((rows, dim), bf16))]
        + [far(shape_of((2, rows, half), bf16))] * 2,
        [pltpu.VMEM((3, 2, half, dim), bf16), pltpu.SemaphoreType.DMA((3, 2))],
    )


FF_TILE = 1024
FF_PIECE = 512


def ff_tiles(wsh_ref, up_own, up_oth, dn_own, dn_oth, up_buf, dn_buf, sems):
    own = dn_own.shape[0] // FF_TILE
    tiles = []
    for t in range(2 * own):
        start = pl.multiple_of(((wsh_ref[0] * own + t) % (2 * own)) * FF_TILE, FF_TILE)
        cols = pl.ds(start, FF_TILE)
        down = (dn_own if t < own else dn_oth).at[pl.ds((t % own) * FF_TILE, FF_TILE)]
        copies = [
            pltpu.make_async_copy(up_own.at[:, cols], up_buf.at[t, 0], sems.at[t, 0]),
            pltpu.make_async_copy(up_oth.at[:, cols], up_buf.at[t, 1], sems.at[t, 1]),
            pltpu.make_async_copy(down, dn_buf.at[t], sems.at[t, 2]),
        ]
        tiles.append((t, start, start_all(copies)))
    for t, start, copies in tiles:
        wait_all(copies)
        for at in range(0, FF_TILE, FF_PIECE):
            row = (t % own) * FF_TILE + at
            place = pl.ds(pl.multiple_of(start + at, FF_PIECE), FF_PIECE)
            yield t, place, t < own, slice(row, row + FF_PIECE), slice(at, at + FF_PIECE)


def ff_scratch(half, ff, dim):
    tiles = ff // FF_TILE
    return [
        pltpu.VMEM((tiles, 2, half, FF_TILE), bf16),
        pltpu.VMEM((tiles, FF_TILE, dim), bf16),
        pltpu.SemaphoreType.DMA((tiles, 3)),
    ]


def mlp_kernel(save, wsh_ref, inputs, weights, outputs, up_buf, dn_buf, sems):
    out_ref = outputs[0].ref
    started = False
    for t, place, held, rows, piece in ff_tiles(wsh_ref, *weights, up_buf, dn_buf, sems):
        own_ref, oth_ref, up_b, down_b = (item.ref() for item in inputs)
        if not started:
            out_ref[...] = jnp.broadcast_to(down_b[...], out_ref.shape)
            started = True
        pre = (
            dot_nn(own_ref[1], up_buf[t, 0, :, piece])
            + dot_nn(oth_ref[1], up_buf[t, 1, :, piece])
            + up_b[:, place]
        )
        gate = 0.5 + 0.5 * lax.erf(pre * INV_SQRT2)
        act = (pre * gate).astype(bf16)
        if save:
            slope = gate + pre * (INV_SQRT_2PI * jnp.exp(-0.5 * pre * pre))
            outputs[1].ref[place] = slope.astype(bf16).T
            outputs[2 if held else 3].ref[rows] = act.T
            if not held:
                outputs[2].send()
        out_ref[...] += dot_nn(act, dn_buf[t, piece])


def mlp_call(own, oth, up_b, down_b, up_own, up_oth, dn_own, dn_oth, wsh, save):
    rows, half = own.shape[1:]
    dim = dn_own.shape[1]
    ff = up_own.shape[1]
    out_shape = [far(shape_of((rows, dim), f32))]
    if save:
        out_shape += [far(shape_of((ff, rows), bf16))]
        out_shape += [far(shape_of((ff // 2, rows), bf16))] * 2
    return local_call(
        functools.partial(mlp_kernel, save),
        "mlp_forward",
        [wsh],
        [far(own), far(oth), up_b, down_b],
        [up_own, up_oth, dn_own, dn_oth],
        out_shape,
        ff_scratch(half, ff, dim),
    )


def mlp_back_kernel(wsh_ref, inputs, weights, outputs, acc_own, acc_oth, up_buf, dn_buf, sems):
    du, dnm = outputs
    half = acc_own.shape[0]
    acc_own[...] = jnp.zeros(acc_own.shape, f32)
    acc_oth[...] = jnp.zeros(acc_oth.shape, f32)
    for t, place, _, _, piece in ff_tiles(wsh_ref, *weights, up_buf, dn_buf, sems):
        dy_ref, slope_ref = (item.ref() for item in inputs)
        dact = dot_nt(dn_buf[t, piece], dy_ref[...])
        vals = (dact * slope_ref[place].astype(f32)).astype(bf16)
        du.ref[place] = vals
        acc_own[...] += dot_nn(up_buf[t, 0, :, piece], vals)
        acc_oth[...] += dot_nn(up_buf[t, 1, :, piece], vals)
    du.send()
    first = wsh_ref[0] == 0
    dnm.ref[:, :half] = jnp.where(first, acc_own[...], acc_oth[...]).T
    dnm.ref[:, half:] = jnp.where(first, acc_oth[...], acc_own[...]).T


def mlp_back_call(dy, slope, up_own, up_oth, dn_own, dn_oth, wsh, after):
    rows, dim = dy.shape
    half, ff = up_own.shape
    return local_call(
        mlp_back_kernel,
        "mlp_backward",
        [wsh],
        [far(dy), far(slope)],
        [up_own, up_oth, dn_own, dn_oth],
        [far(shape_of(slope.shape, bf16)), far(shape_of((rows, dim), f32))],
        [pltpu.VMEM((half, rows), f32), pltpu.VMEM((half, rows), f32)] + ff_scratch(half, ff, dim),
        after,
    )


def sort_in(loc_ref, ref, dst, half_rows, part=None):
    for block in range(dst.shape[0] // half_rows):
        place = loc_ref[block]
        rows = pl.ds(pl.multiple_of((place % 2) * half_rows, half_rows), half_rows)
        if part is None:
            vals = ref[place // 2, rows, :]
        else:
            vals = ref[place // 2, part, rows, :]
        dst[block * half_rows : (block + 1) * half_rows] = vals


def sort_out(loc_ref, vals, ref, half_rows, part=None):
    for block in range(vals.shape[0] // half_rows):
        place = loc_ref[block]
        rows = pl.ds(pl.multiple_of((place % 2) * half_rows, half_rows), half_rows)
        piece = vals[block * half_rows : (block + 1) * half_rows]
        if part is None:
            ref[place // 2, rows, :] = piece
        else:
            ref[place // 2, part, rows, :] = piece


def head_of(vals, head):
    lane = lax.broadcasted_iota(jnp.int32, vals.shape, 1)
    return jnp.where(lane // (LANES // 2) == head, vals, jnp.zeros_like(vals))


def scores_of(keys, queries, scale, diagonal):
    scores = dot_nt(keys, queries) * scale
    if diagonal:
        key_at = lax.broadcasted_iota(jnp.int32, scores.shape, 0)
        query_at = lax.broadcasted_iota(jnp.int32, scores.shape, 1)
        scores = jnp.where(key_at <= query_at, scores, MASKED_SCORE)
    return scores


def attend_kernel(tile, loc_ref, inputs, weights, outputs, q_s, k_s, v_s, vt_s, o_s):
    qkv_ref = inputs[0].ref()
    o_ref, lse_ref = (item.ref for item in outputs)
    half_rows = qkv_ref.shape[2] // 2
    seq = q_s.shape[0]
    head_size = LANES // 2
    scale = head_size**-0.5
    sort_in(loc_ref, qkv_ref, q_s, half_rows, 0)
    sort_in(loc_ref, qkv_ref, k_s, half_rows, 1)
    sort_in(loc_ref, qkv_ref, v_s, half_rows, 2)
    vt_s[...] = v_s[...].T
    for t in range(seq // tile):
        rows = slice(t * tile, (t + 1) * tile)
        queries = q_s[rows]
        outs = []
        for head in range(2):
            picked = head_of(queries, head)
            parts = [
                scores_of(k_s[i * tile : (i + 1) * tile], picked, scale, i == t)
                for i in range(t + 1)
            ]
            top = functools.reduce(
                jnp.maximum, [jnp.max(p, axis=0, keepdims=True) for p in parts]
            )
            parts = [jnp.exp(p - top) for p in parts]
            total = sum(jnp.sum(p, axis=0, keepdims=True) for p in parts)
            lse_ref[head : head + 1, rows] = top + jnp.log(total)
            inverse = 1.0 / total
            acc = None
            for i, p in enumerate(parts):
                term = dot_nn(
                    vt_s[head * head_size : (head + 1) * head_size, i * tile : (i + 1) * tile],
                    (p * inverse).astype(bf16),
                )
                acc = term if acc is None else acc + term
            outs.append(acc)
        o_s[rows] = jnp.concatenate(outs, axis=0).T.astype(bf16)
    sort_out(loc_ref, o_s, o_ref, half_rows)


def attend_call(qkv, loc, after):
    count, _, rows, _ = qkv.shape
    seq = count * rows
    return local_call(
        functools.partial(attend_kernel, 256),
        "attention",
        [loc],
        [qkv],
        [],
        [far(shape_of((count, rows, LANES), bf16)), far(shape_of((2, seq), f32))],
        [
            pltpu.VMEM((seq, LANES), bf16),
            pltpu.VMEM((seq, LANES), bf16),
            pltpu.VMEM((seq, LANES), bf16),
            pltpu.VMEM((LANES, seq), bf16),
            pltpu.VMEM((seq, LANES), bf16),
        ],
        after,
    )


def attend_back_kernel(
    tile, part, loc_ref, inputs, weights, outputs, q_s, k_s, v_s, da_s, kt_s, dq_s, dk_s, dv_s
):
    da_ref, qkv_ref, lse_ref = (item.ref() for item in inputs)
    out_ref = outputs[0].ref
    half_rows = qkv_ref.shape[2] // 2
    seq = q_s.shape[0]
    head_size = LANES // 2
    scale = head_size**-0.5
    sort_in(loc_ref, qkv_ref, q_s, half_rows, 0)
    sort_in(loc_ref, qkv_ref, k_s, half_rows, 1)
    sort_in(loc_ref, qkv_ref, v_s, half_rows, 2)
    sort_in(loc_ref, da_ref, da_s, half_rows, part)
    kt_s[...] = k_s[...].T
    dk_s[...] = jnp.zeros(dk_s.shape, f32)
    dv_s[...] = jnp.zeros(dv_s.shape, f32)
    for t in range(seq // tile):
        rows = slice(t * tile, (t + 1) * tile)
        outs = []
        for head in range(2):
            queries = head_of(q_s[rows], head)
            grads = head_of(da_s[rows], head)
            lse = lse_ref[head : head + 1, rows]
            probs, dprobs, row_dot = [], [], 0.0
            for i in range(t + 1):
                keys = slice(i * tile, (i + 1) * tile)
                p = jnp.exp(scores_of(k_s[keys], queries, scale, i == t) - lse)
                dp = dot_nt(v_s[keys], grads)
                row_dot = row_dot + jnp.sum(p * dp, axis=0, keepdims=True)
                dv_s[keys] += dot_nn(p.astype(bf16), grads)
                probs.append(p)
                dprobs.append(dp)
            acc = None
            for i in range(t + 1):
                keys = slice(i * tile, (i + 1) * tile)
                ds = (probs[i] * (dprobs[i] - row_dot) * scale).astype(bf16)
                dk_s[keys] += dot_nn(ds, queries)
                term = dot_nn(kt_s[head * head_size : (head + 1) * head_size, keys], ds)
                acc = term if acc is None else acc + term
            outs.append(acc)
        dq_s[rows] = jnp.concatenate(outs, axis=0).T.astype(bf16)
    sort_out(loc_ref, dq_s, out_ref, half_rows, 0)
    k_s[...] = dk_s[...].astype(bf16)
    v_s[...] = dv_s[...].astype(bf16)
    sort_out(loc_ref, k_s, out_ref, half_rows, 1)
    sort_out(loc_ref, v_s, out_ref, half_rows, 2)


def attend_back_call(qkv, da, lse, loc, after):
    count, _, rows, _ = qkv.shape
    seq = count * rows
    part = 0 if da.ndim == 4 else None
    (res,) = local_call(
        functools.partial(attend_back_kernel, 256, part),
        "attention_backward",
        [loc],
        [da, far(qkv), far(lse)],
        [],
        [far(shape_of(qkv.shape, bf16))],
        [pltpu.VMEM((seq, LANES), bf16)] * 4
        + [pltpu.VMEM((LANES, seq), bf16), pltpu.VMEM((seq, LANES), bf16)]
        + [pltpu.VMEM((seq, LANES), f32)] * 2,
        after,
    )
    return res


def by_head(parts):
    pairs, rows, lanes = parts.shape
    return jnp.transpose(parts, (1, 0, 2)).reshape(rows, HEADS, pairs * lanes // HEADS)


def by_pair(heads):
    rows = heads.shape[0]
    return jnp.transpose(heads.reshape(rows, -1, LANES), (1, 0, 2))


def wide_scores(queries, keys, query_pos, key_pos):
    raw = jnp.einsum("qhd,khd->hqk", queries, keys, preferred_element_type=f32)
    allowed = (query_pos[:, None] >= key_pos[None, :])[None]
    return jnp.where(allowed, raw * queries.shape[-1] ** (-0.5), MASKED_SCORE)


def key_blocks(arrays, rows):
    return tuple(a.reshape((a.shape[0] // rows, rows) + a.shape[1:]) for a in arrays)


def wide_attend(qkv, query_pos, key_pos):
    queries = by_head(qkv[:, 0])
    keys = lax.all_gather(by_head(qkv[:, 1]), "ctx", axis=0, tiled=True)
    values = lax.all_gather(by_head(qkv[:, 2]), "ctx", axis=0, tiled=True)
    block = min(512, keys.shape[0])
    split = key_blocks((keys, values, key_pos), block)
    rows, _, head_size = queries.shape

    def max_step(carry, block_in):
        top, total = carry
        scores = wide_scores(queries, block_in[0], query_pos, block_in[2])
        new_top = jnp.maximum(top, jnp.max(scores, axis=-1))
        part = jnp.sum(jnp.exp(scores - new_top[..., None]), axis=-1)
        return ((new_top, total * jnp.exp(top - new_top) + part), None)

    start = (jnp.full((HEADS, rows), MASKED_SCORE, f32), jnp.zeros((HEADS, rows), f32))
    (top, total), _ = lax.scan(max_step, start, split)
    lse = top + jnp.log(total)

    def value_step(running, block_in):
        scores = wide_scores(queries, block_in[0], query_pos, block_in[2])
        probs = jnp.exp(scores - lse[..., None]).astype(bf16)
        term = jnp.einsum("hqk,khd->qhd", probs, block_in[1], preferred_element_type=f32)
        return (running + term, None)

    attended, _ = lax.scan(value_step, jnp.zeros((rows, HEADS, head_size), f32), split)
    return by_pair(attended.astype(bf16)), (queries, keys, values, lse)


def wide_attend_back(kept, da, query_pos, key_pos):
    queries, keys, values, lse = kept
    grads = by_head(da)
    block = min(512, keys.shape[0])
    split = key_blocks((keys, values, key_pos), block)
    scale = queries.shape[-1] ** (-0.5)

    def pieces(block_in):
        scores = wide_scores(queries, block_in[0], query_pos, block_in[2])
        probs = jnp.exp(scores - lse[..., None])
        dprobs = jnp.einsum("qhd,khd->hqk", grads, block_in[1], preferred_element_type=f32)
        return probs, dprobs

    def dot_step(running, block_in):
        probs, dprobs = pieces(block_in)
        return (running + jnp.sum(probs * dprobs, axis=-1), None)

    row_dot, _ = lax.scan(dot_step, jnp.zeros(lse.shape, f32), split)

    def key_step(running, block_in):
        probs, dprobs = pieces(block_in)
        ds = (scale * probs * (dprobs - row_dot[..., None])).astype(bf16)
        running = running + jnp.einsum("hqk,khd->qhd", ds, block_in[0], preferred_element_type=f32)
        dk = jnp.einsum("hqk,qhd->khd", ds, queries, preferred_element_type=f32)
        dv = jnp.einsum("hqk,qhd->khd", probs.astype(bf16), grads, preferred_element_type=f32)
        return (running, (dk.astype(bf16), dv.astype(bf16)))

    dq, (dk, dv) = lax.scan(key_step, jnp.zeros(queries.shape, f32), split)
    dk, dv = (
        lax.psum_scatter(part.reshape(keys.shape), "ctx", scatter_dimension=0, tiled=True)
        for part in (dk, dv)
    )
    return jnp.stack([by_pair(dq.astype(bf16)), by_pair(dk), by_pair(dv)], axis=1)


def lanes_of(ref):
    return jnp.concatenate([ref[i] for i in range(ref.shape[0])], axis=1)


def both_halves(w_own, w_oth, buf, sems):
    return start_all(
        [
            pltpu.make_async_copy(weight, buf.at[side], sems.at[side])
            for side, weight in enumerate((w_own, w_oth))
        ]
    )


def half_scratch(weight):
    return [pltpu.VMEM((2,) + weight.shape, bf16), pltpu.SemaphoreType.DMA((2,))]


def proj_kernel(part, wsh_ref, inputs, weights, outputs, buf, sems):
    copies = both_halves(*weights, buf, sems)
    y, own, oth = outputs
    half = buf.shape[1]
    first = wsh_ref[0] == 0
    a_ref = inputs[0].ref()
    a = lanes_of(a_ref if part is None else a_ref.at[:, part])
    own.ref[...] = jnp.where(first, a[:, :half], a[:, half:])
    oth.ref[...] = jnp.where(first, a[:, half:], a[:, :half])
    own.send()
    oth.send()
    bias_ref, x_ref, mlp_ref = (item.ref() for item in inputs[1:])
    wait_all(copies)
    attn = dot_nn(own.ref[...], buf[0]) + dot_nn(oth.ref[...], buf[1]) + bias_ref[...]
    y.ref[...] = (x_ref[...].astype(f32) + attn + mlp_ref[...]).astype(bf16)


def proj_call(a, x, mlp, bias, p_own, p_oth, wsh, after):
    rows, dim = x.shape
    half = p_own.shape[0]
    return local_call(
        functools.partial(proj_kernel, 1 if a.ndim == 4 else None),
        "attn_out",
        [wsh],
        [a, bias, far(x), far(mlp)],
        [p_own, p_oth],
        [far(shape_of((rows, dim), bf16))] + [far(shape_of((rows, half), bf16))] * 2,
        half_scratch(p_own),
        after,
    )


def da_kernel(own_given, wsh_ref, inputs, weights, outputs, buf, sems):
    copies = both_halves(*weights, buf, sems)
    out_ref, dy_out = outputs[0].ref, outputs[1]
    dy = inputs[0].ref()[...]
    if not own_given:
        dy = jnp.where(wsh_ref[1] == 1, inputs[1].ref()[...], dy)
    dy_out.ref[...] = dy
    dy_out.send()
    wsh = wsh_ref[0]
    joined = len(out_ref.shape) == 4
    if joined:
        out_ref[:, 1] = inputs[2].ref()[...]
    count = out_ref.shape[0] // 2
    for place, side in ((wsh * count, 0), ((1 - wsh) * count, 1)):
        copies[side].wait()
        part = dot_nt(dy, buf[side]).astype(bf16)
        for i in range(count):
            vals = part[:, i * LANES : (i + 1) * LANES]
            if joined:
                out_ref[place + i, 0] = vals
            else:
                out_ref[place + i] = vals


def da_call(given, got, p_own, p_oth, wsh, joined=None):
    rows, dim = given.shape
    pairs = dim // LANES
    arrays = [far(given)] + ([] if got is None else [got])
    arrays += [] if joined is None else [far(joined)]
    shape = (pairs, rows, LANES) if joined is None else (pairs, 2, rows, LANES)
    return local_call(
        functools.partial(da_kernel, got is None),
        "attn_out_backward",
        [wsh],
        arrays,
        [p_own, p_oth],
        [far(shape_of(shape, bf16)), far(shape_of((rows, dim), bf16))],
        half_scratch(p_own),
    )


def dx_kernel(wsh_ref, inputs, weights, outputs, grad_s, buf, sems):
    copies = both_halves(*weights, buf, sems)
    back, dx, sums = outputs
    dqkv_ref, tab_ref = inputs[0].ref(), inputs[1].ref()
    pairs = dqkv_ref.shape[0]
    for part in range(3):
        for pair in range(pairs):
            vals = dqkv_ref[pair, part]
            if part < 2:
                vals = unrope(vals.astype(f32), tab_ref).astype(bf16)
            back.ref[pair, part] = vals
            grad_s[:, pl.ds((part * pairs + pair) * LANES, LANES)] = vals
    back.send()
    vec_ref, x_ref, dy_ref, dnm_ref = (item.ref() for item in inputs[2:])
    first = wsh_ref[0] == 0
    copies[0].wait()
    own = dot_nt(grad_s[...], buf[0])
    copies[1].wait()
    oth = dot_nt(grad_s[...], buf[1])
    dna = jnp.concatenate([jnp.where(first, own, oth), jnp.where(first, oth, own)], axis=1)
    dnm = dnm_ref[...]
    xhat, scale = normalized(x_ref[...].astype(f32))
    grad = dna * vec_ref[0:1] + dnm * vec_ref[2:3]
    inner = (
        grad
        - jnp.mean(grad, axis=-1, keepdims=True)
        - xhat * jnp.mean(grad * xhat, axis=-1, keepdims=True)
    )
    dx.ref[...] = (dy_ref[...].astype(f32) + scale * inner).astype(bf16)
    dx.send()
    sums.ref[0:1] = jnp.sum(dna * xhat, axis=0, keepdims=True)
    sums.ref[1:2] = jnp.sum(dna, axis=0, keepdims=True)
    sums.ref[2:3] = jnp.sum(dnm * xhat, axis=0, keepdims=True)
    sums.ref[3:4] = jnp.sum(dnm, axis=0, keepdims=True)


def dx_call(dqkv, tab, x, dy, dnm, vecs, w_own, w_oth, wsh, after):
    rows, dim = x.shape
    return local_call(
        dx_kernel,
        "section_input_grad",
        [wsh],
        [dqkv, tab, vecs, far(x), far(dy), far(dnm)],
        [w_own, w_oth],
        [far(shape_of(o, t)) for o, t in ((dqkv.shape, bf16), ((rows, dim), bf16), ((4, dim), f32))],
        [pltpu.VMEM((rows, 3 * dim), bf16)] + half_scratch(w_own),
        after,
    )


def stack_rows(refs, cols=slice(None)):
    return jnp.concatenate([ref[:, cols] for ref in refs], axis=0)


def down_grad_kernel(micros, *refs):
    gt_refs, dy_refs = refs[:micros], refs[micros : 2 * micros]
    out_ref, sum_ref, dy_s = refs[-3:]

    @pl.when(pl.program_id(0) == 0)
    def _():
        dy = stack_rows(dy_refs)
        dy_s[...] = dy
        sum_ref[...] = jnp.sum(dy.astype(f32), axis=0, keepdims=True)

    left = jnp.concatenate([ref[...] for ref in gt_refs], axis=1)
    out_ref[...] = dot_nn(left, dy_s[...]).astype(bf16)


def down_grad_call(gt_list, dy_list):
    ff_rows, rows = gt_list[0].shape
    dim = dy_list[0].shape[1]
    micros = len(dy_list)
    tile = 512
    return pl.pallas_call(
        functools.partial(down_grad_kernel, micros),
        grid=(ff_rows // tile,),
        in_specs=[pl.BlockSpec((tile, rows), lambda j: (j, 0))] * micros
        + [whole((rows, dim))] * micros,
        out_specs=[pl.BlockSpec((tile, dim), lambda j: (j, 0)), whole((1, dim))],
        out_shape=[shape_of((ff_rows, dim), bf16), shape_of((1, dim), f32)],
        scratch_shapes=[pltpu.VMEM((micros * rows, dim), bf16)],
        name="down_grad",
        **params_of(),
    )(*gt_list, *dy_list)


def up_grad_kernel(micros, *refs):
    x_refs, du_refs = refs[:micros], refs[micros : 2 * micros]
    out_ref, sum_ref, xt_s = refs[-3:]

    @pl.when(pl.program_id(0) == 0)
    def _():
        xt_s[...] = stack_rows(x_refs).T

    du = jnp.concatenate([ref[...] for ref in du_refs], axis=1)
    sum_ref[...] = dot_nt(jnp.ones((8, du.shape[1]), bf16), du)[:1]
    out_ref[...] = dot_nt(xt_s[...], du).astype(bf16)


def up_grad_call(x_list, du_list, after):
    rows, half = x_list[0].shape[1:]
    ff = du_list[0].shape[0]
    micros = len(x_list)
    tile = 1024
    return pl.pallas_call(
        functools.partial(up_grad_kernel, micros),
        grid=(ff // tile,),
        in_specs=[layer_of((rows, half), 1)] * micros
        + [pl.BlockSpec((tile, rows), lambda j: (j, 0))] * micros
        + [ANYWHERE] * len(after),
        out_specs=[
            pl.BlockSpec((half, tile), lambda j: (0, j)),
            pl.BlockSpec((1, tile), lambda j: (0, j)),
        ],
        out_shape=[shape_of((half, ff), bf16), shape_of((1, ff), f32)],
        scratch_shapes=[pltpu.VMEM((half, micros * rows), bf16)],
        name="up_grad",
        **params_of(),
    )(*x_list, *du_list, *after)


def attn_grad_kernel(micros, *refs):
    x_refs, a_refs, d_refs, dy_refs = (refs[i * micros : (i + 1) * micros] for i in range(4))
    out_ref, sum_ref, xt_s = refs[-3:]
    part = pl.program_id(0)

    def finish(dy):
        sum_ref[...] = jnp.sum(dy.astype(f32), axis=0, keepdims=True)
        out_ref[...] = dot_nn(xt_s[...], dy).astype(bf16)

    @pl.when(part == 0)
    def _():
        xt_s[...] = stack_rows(x_refs).T

    @pl.when(part < 3)
    def _():
        finish(jnp.concatenate([lanes_of(ref) for ref in d_refs], axis=0))

    @pl.when(part == 3)
    def _():
        xt_s[...] = stack_rows(a_refs).T
        finish(stack_rows(dy_refs))


def attn_grad_call(x_list, a_list, d_list, dy_list, after):
    rows, half = x_list[0].shape[1:]
    pairs = d_list[0].shape[0]
    dim = pairs * LANES
    micros = len(x_list)
    d_spec = pl.BlockSpec(
        (pairs, pl.squeezed, rows, LANES), lambda j: (0, jnp.minimum(j, 2), 0, 0)
    )
    return pl.pallas_call(
        functools.partial(attn_grad_kernel, micros),
        grid=(4,),
        in_specs=[layer_of((rows, half), 0)] * micros
        + [whole((rows, half))] * micros
        + [d_spec] * micros
        + [whole((rows, dim))] * micros
        + [ANYWHERE] * len(after),
        out_specs=[
            pl.BlockSpec((half, dim), lambda j: (0, j)),
            pl.BlockSpec((1, dim), lambda j: (0, j)),
        ],
        out_shape=[shape_of((half, 4 * dim), bf16), shape_of((1, 4 * dim), f32)],
        scratch_shapes=[pltpu.VMEM((half, micros * rows), bf16)],
        name="attn_grad",
        **params_of(),
    )(*x_list, *a_list, *d_list, *dy_list, *after)


def ring_of(count):
    return list(range(0, count, 2)) + list(range(count - 1, 0, -2))


def ring_place(axis):
    count = lax.axis_size(axis)
    me = lax.axis_index(axis)
    return jnp.where(me % 2 == 0, me // 2, count - (me + 1) // 2)


def ring_shift(vals, axis, by):
    order = ring_of(lax.axis_size(axis))
    count = len(order)
    pairs = [(order[i], order[(i + by) % count]) for i in range(count)]
    return lax.ppermute(vals, axis, pairs)


def tied(token, *vals):
    return lax.optimization_barrier((token, vals))[1]


def fetch(idx_ref, slots, own_ref, bufs, sems):
    return start_all(
        [
            pltpu.make_async_copy(own_ref.at[idx_ref[slot]], bufs.at[i], sems.at[i])
            for i, slot in enumerate(slots)
        ]
    )


def low_total(*terms):
    total = terms[0].astype(f32)
    for term in terms[1:]:
        total = total + term.astype(f32)
    return total.astype(bf16)


def ring_split_kernel(slots, idx_ref, inputs, own_refs, outputs, bufs, sems):
    wait_all(fetch(idx_ref, slots, own_refs[0], bufs, sems))
    cut = outputs[0].ref.shape[1]
    for i, item in enumerate(outputs):
        item.ref[...] = bufs[0, :, i * cut : (i + 1) * cut]


def ring_add_kernel(slots, idx_ref, inputs, own_refs, outputs, bufs, sems):
    copies = fetch(idx_ref, slots, own_refs[0], bufs, sems)
    for i, item in enumerate(outputs):
        copies[i].wait()
        got = inputs[i].ref()
        cols, cut = item.ref.shape[1], got.shape[1]
        summed = slice(0, cut) if i == 0 else slice(cols - cut, cols)
        item.ref[:, summed] = low_total(bufs[i, :, summed], got[...])
        if cut < cols:
            rest = slice(cut, cols) if i == 0 else slice(0, cols - cut)
            item.ref[:, rest] = bufs[i, :, rest]


def put_copies(chunk, cols, buf, totals, starts, sem):
    lo, hi = cols, cols + buf.shape[1]
    copies = []
    for i, (total, start) in enumerate(zip(totals, starts)):
        first, last = max(lo, start), min(hi, start + total.shape[2])
        if first < last:
            copies.append(
                pltpu.make_async_copy(
                    buf.at[:, pl.ds(first - lo, last - first)],
                    total.at[chunk, :, pl.ds(first - start, last - first)],
                    sem.at[i],
                )
            )
    return copies


def ring_own_kernel(slots, idx_ref, inputs, own_refs, outputs, bufs, sems):
    wait_all(fetch(idx_ref, slots, own_refs[0], bufs, sems))
    outputs[0].ref[...] = low_total(bufs[0], inputs[0].ref()[...], inputs[1].ref()[...])


def ring_put_kernel(starts, slots, cols, fresh, onward, idx_ref, *refs):
    number = len(slots)
    pieces = refs[:number]
    wide, sems = refs[-2:]
    passed = refs[-2 - onward : -2]
    totals = refs[-2 - onward - len(starts) : -2 - onward]
    leaving = []
    for i in range(number):
        wide[i] = pieces[i][...].astype(f32)
        leaving += start_all(
            put_copies(idx_ref[slots[i]], cols[i], wide.at[i], totals, starts, sems.at[i])
        )
    for i, ref in enumerate(passed):
        width = ref.shape[1]
        ref[...] = pieces[i][:, :width] if i == 0 else pieces[i][:, -width:]
    wait_all(leaving)


def ring_sum(own, widths, axis):
    count = lax.axis_size(axis)
    half = count // 2
    full_rows, cols = own.shape
    rows = full_rows // count
    own = own.reshape(count, rows, cols)
    cut = cols // 2
    starts = [sum(widths[:i]) for i in range(len(widths))]
    idx = (ring_place(axis) + jnp.arange(count, dtype=jnp.int32)) % count
    chunk, piece = shape_of((rows, cols), bf16), shape_of((rows, cut), bf16)
    sums = [shape_of((count, rows, width), f32) for width in widths]

    def taken(number):
        return [pltpu.VMEM((number, rows, cols), bf16), pltpu.SemaphoreType.DMA((number,))]

    def put(totals, pieces, slots, passed, after):
        number, width = len(pieces), pieces[0].shape[1]
        first_cols = (0,) * number if width == cols else (0, cut)
        fresh = totals is None
        out = pl.pallas_call(
            functools.partial(
                ring_put_kernel,
                starts,
                tuple(k % count for k in slots),
                first_cols,
                fresh,
                len(passed),
            ),
            in_specs=[SCALARS]
            + [HERE] * number
            + [IN_HBM] * (0 if fresh else len(sums))
            + [ANYWHERE] * len(after),
            out_specs=[IN_HBM] * len(sums) + [HERE] * len(passed),
            out_shape=sums + passed,
            scratch_shapes=[
                pltpu.VMEM((number, rows, width), f32),
                pltpu.SemaphoreType.DMA((number, len(sums))),
            ],
            input_output_aliases={} if fresh else {1 + number + i: i for i in range(len(sums))},
            name="ring_put",
            **params_of(),
        )(idx, *pieces, *([] if fresh else totals), *after)
        return out[: len(sums)], out[len(sums) :]

    def both_ways(ahead, behind):
        return ring_shift(ahead, axis, 1), ring_shift(behind, axis, -1)

    token = yield None
    ahead, behind = local_call(
        functools.partial(ring_split_kernel, (half,)),
        "ring_split",
        [idx],
        [],
        [own],
        [piece, piece],
        taken(1),
        [token],
    )
    token = behind
    ahead, behind = both_ways(ahead, behind)
    token = yield token
    for k in range(half - 1, 0, -1):
        ahead, behind = local_call(
            functools.partial(ring_add_kernel, (k % count, (-k) % count)),
            "ring_add",
            [idx],
            [ahead, behind],
            [own],
            [chunk, chunk],
            taken(2),
            [token],
        )
        token = behind
        ahead, behind = both_ways(ahead, behind)
        token = yield token
    (mine,) = local_call(
        functools.partial(ring_own_kernel, (0,)),
        "ring_own",
        [idx],
        [ahead, behind],
        [own],
        [chunk],
        taken(1),
        [token],
    )
    ahead, behind = both_ways(mine, mine)
    totals, (token,) = put(None, [mine], [0], [shape_of((rows, LANES), bf16)], [])
    token = yield token
    for k in range(1, half):
        passed = [piece if k == half - 1 else chunk] * 2
        totals, passed = put(totals, [ahead, behind], [-k, k], passed, [token])
        token = passed[1]
        ahead, behind = both_ways(*passed)
        token = yield token
    totals, _ = put(totals, [ahead, behind], [-half, half], [], [token])
    yield [total.reshape(full_rows, -1) for total in totals]


def butterfly_sum(vals, axis):
    count = lax.axis_size(axis)
    by = 1
    token = yield None
    if count & (count - 1):
        yield lax.psum(tied(token, vals)[0], axis)
        return
    (vals,) = tied(token, vals)
    while by < count:
        got = lax.ppermute(vals, axis, [(i, i ^ by) for i in range(count)])
        token = yield None
        (got,) = tied(token, got)
        vals = vals + got
        by *= 2
    yield vals


def swap(vals):
    return lax.ppermute(vals, "wsh", [(0, 1), (1, 0)])


def pass_on(vals, by):
    pairs = [(0, 1)] if by > 0 else [(1, 0)]
    return lax.ppermute(vals, "section", pairs)


def block_places(block_pair, count):
    want = jnp.arange(2 * count, dtype=jnp.int32)
    device = jnp.arange(count, dtype=jnp.int32)
    first = (block_pair[None, :] == want[:, None]).astype(jnp.int32)
    second = ((2 * count - 1 - block_pair)[None, :] == want[:, None]).astype(jnp.int32)
    return jnp.sum(first * (2 * device) + second * (2 * device + 1), axis=1)


def row_positions(block_pair, stored, tok_dev):
    count = block_pair.shape[0]
    device = stored // tok_dev
    within = stored % tok_dev
    half_rows = tok_dev // 2
    matches = device[:, None] == jnp.arange(count, dtype=jnp.int32)[None, :]
    pair_block = jnp.sum(jnp.where(matches, block_pair[None, :], 0), axis=1)
    block_idx = jnp.where(within < half_rows, pair_block, 2 * count - 1 - pair_block)
    return block_idx * half_rows + within % half_rows


def rotary_table(positions, head_size):
    half_rot = ROT // 2
    lane = jnp.arange(LANES, dtype=jnp.int32) % head_size
    inv_freq = ROPE_BASE ** (-((lane % half_rot).astype(f32) * 2.0) / ROT)
    angles = positions.astype(f32)[:, None] * inv_freq[None, :]
    cosine, sine = jnp.cos(angles), jnp.sin(angles)
    lead, second = (lane < half_rot)[None], ((lane >= half_rot) & (lane < ROT))[None]
    return jnp.stack(
        [
            jnp.where(lead | second, cosine, 1.0),
            jnp.where(lead, -sine, 0.0),
            jnp.where(second, sine, 0.0),
        ]
    )


def body(
    inputs,
    cotangent,
    block_pair,
    qkv_weight,
    qkv_bias,
    proj_weight,
    proj_bias,
    up_weight,
    up_bias,
    down_weight,
    down_bias,
    attn_gain,
    attn_shift,
    mlp_gain,
    mlp_shift,
):
    first_section = lax.axis_index("section") == 0
    count = lax.axis_size("ctx")
    micros, _, tok_dev, dim = inputs.shape
    head_size = dim // HEADS
    half = dim // 2
    my_half = lax.axis_index("wsh")
    wsh = jnp.stack([my_half.astype(jnp.int32), first_section.astype(jnp.int32)])
    one_pair_each = count == dim // LANES

    wq, wp, wu, wd = (w[0] for w in (qkv_weight, proj_weight, up_weight, down_weight))
    small = jnp.concatenate(
        [
            v[0].reshape(-1, half)
            for v in (
                attn_gain,
                attn_shift,
                mlp_gain,
                mlp_shift,
                proj_bias,
                down_bias,
                qkv_bias,
                up_bias,
            )
        ],
        axis=0,
    )
    small_oth = swap(small)
    wq_oth = swap(wq)
    first_here = lax.optimization_barrier((wq_oth, small_oth))
    wq_oth, small_oth = first_here
    wu_oth = swap(tied(wq_oth, wu)[0])
    wd_oth = swap(tied(wq_oth, wd)[0])
    wp_oth = swap(tied(wu_oth, wp)[0])
    low_part = jnp.where(my_half == 0, small, small_oth).astype(f32)
    high_part = jnp.where(my_half == 0, small_oth, small).astype(f32)
    vecs = jnp.concatenate([low_part[:6], high_part[:6]], axis=1)
    qkv_rows = 6 + qkv_bias.shape[1] // half
    proj_b, down_b = vecs[4:5], vecs[5:6]
    qkv_b = jnp.concatenate([low_part[6:qkv_rows], high_part[6:qkv_rows]], axis=0).reshape(1, -1)
    up_b = jnp.concatenate([low_part[qkv_rows:], high_part[qkv_rows:]], axis=0).reshape(1, -1)

    local_rows = lax.axis_index("ctx") * tok_dev + jnp.arange(tok_dev, dtype=jnp.int32)
    query_pos = row_positions(block_pair, local_rows, tok_dev)
    key_pos = row_positions(block_pair, jnp.arange(count * tok_dev, dtype=jnp.int32), tok_dev)
    tab = rotary_table(query_pos, head_size)
    loc = block_places(block_pair, count)

    def exchange(vals):
        return lax.all_to_all(vals, "ctx", split_axis=0, concat_axis=0, tiled=True)

    rows_in = [inputs[i, 0] for i in range(micros)]
    cot_in = [cotangent[i, 0] for i in range(micros)]

    def norm_qkv(index, got):
        return qkv_call(rows_in[index], got, vecs, qkv_b, tab, wq, wq_oth, wsh)

    def mlp(made, save):
        return mlp_call(made[2], made[3], up_b, down_b, wu, wu_oth, wd, wd_oth, wsh, save)

    def mlp_back(dy, mlp_kept, after=()):
        return mlp_back_call(dy, mlp_kept[1], wu, wu_oth, wd, wd_oth, wsh, after)

    def out_back(index, got, joined=None):
        return da_call(cot_in[index], got, wp, wp_oth, wsh, joined)

    def moved(vals):
        return exchange(vals) if one_pair_each else vals

    def attend(qkv, after=()):
        if one_pair_each:
            attended, lse = attend_call(qkv, loc, after)
            return attended, (qkv, lse)
        return wide_attend(qkv, query_pos, key_pos)

    def attend_back(kept, da, after=()):
        if one_pair_each:
            return attend_back_call(kept[0], da, kept[1], loc, after)
        da = da[:, 0] if da.ndim == 4 else da
        return wide_attend_back(kept, da, query_pos, key_pos)

    def project(attended, made, mlp_out, after=()):
        return proj_call(attended, made[1], mlp_out[0], proj_b, wp, wp_oth, wsh, after)

    def input_grad_of(dqkv, made, dy, dnm, after=()):
        return dx_call(dqkv, tab, made[1], dy, dnm, vecs, wq, wq_oth, wsh, after)

    made_a = norm_qkv(0, None)
    qkv_a = moved(made_a[0])
    mlp_a = mlp(made_a, False)
    att_a, _ = attend(qkv_a, [mlp_a[0]])
    att_a = moved(att_a)
    da_a, dy_a = out_back(0, None)
    y_a = project(att_a, made_a, mlp_a, [dy_a])[0]
    da_a = moved(tied(y_a, da_a)[0])

    made_b = norm_qkv(1, pass_on(y_a, 1))
    qkv_2 = moved(tied(da_a, made_b[0])[0])
    norms_b = swap(made_b[3])
    mlp_b = mlp(made_b, True)
    att_b, kept_b = attend(qkv_2, [mlp_b[0], norms_b])
    att_b = moved(att_b)
    gt_b = swap(mlp_b[3])
    dqkv_a_ = attend_back(kept_b, da_a, [gt_b])
    dqkv_a = moved(dqkv_a_)
    y_b, *a_b = project(att_b, made_b, mlp_b, [dqkv_a_])

    made_c = norm_qkv(0, pass_on(y_b, 1))
    qkv_3 = moved(tied(dqkv_a, made_c[0])[0])
    norms_c = swap(made_c[3])
    a_b_oth = swap(a_b[1])
    _, dnm_a = mlp_back(dy_a, mlp_b, [made_c[1]])
    _, dx_a, _ = input_grad_of(dqkv_a, made_b, dy_a, dnm_a, [norms_c, a_b_oth])
    got_a = pass_on(dx_a, -1)
    mlp_c = mlp_call(
        made_c[2], tied(dx_a, made_c[3])[0], up_b, down_b, wu, wu_oth, wd, wd_oth, wsh, True
    )
    da_b, dy_b = out_back(1, tied(mlp_c[0], got_a)[0])
    da_b = moved(tied(qkv_3, da_b)[0])
    att_c, kept_c = attend(qkv_3, [dy_b])
    dy_b_oth, gt_c = swap(dy_b), swap(mlp_c[3])
    dqkv_b = attend_back(kept_c, da_b, [dy_b_oth, gt_c])
    dqkv_b_ = moved(dqkv_b)
    du_b, dnm_b = mlp_back(dy_b, mlp_c, [dqkv_b])
    du_b_oth = swap(du_b)
    back_b, dx_b, sums_b = input_grad_of(dqkv_b_, made_c, dy_b, dnm_b, [du_b_oth])
    got_b = pass_on(dx_b, -1)
    back_b_oth = swap(back_b)

    da_c, dy_c = out_back(0, tied(back_b_oth, got_b)[0], att_c if one_pair_each else None)
    dy_list = [dy_c, dy_b, swap(dy_c), dy_b_oth]
    da_c = moved(da_c)
    down_grad, dy_sum = down_grad_call([mlp_b[2], mlp_c[2], gt_b, gt_c], dy_list)
    down_ring = ring_sum(down_grad, (dim,), "ctx")
    next(down_ring)
    token = down_ring.send(dy_sum)
    du_c, dnm_c = mlp_back(dy_c, mlp_b, [token])
    dqkv_c = attend_back(kept_b, da_c, [dnm_c])
    token = down_ring.send(dqkv_c)
    dqkv_c = moved(dqkv_c)
    up_grad, du_sum = up_grad_call(
        [made_b[2], made_c[2], norms_b, norms_c], [du_c, du_b, swap(du_c), du_b_oth], [token]
    )
    up_ring = ring_sum(up_grad, (up_grad.shape[1],), "ctx")
    next(up_ring)
    steps = count + 1
    left = {down_ring: steps - 2, up_ring: steps}
    results = {}

    def turn(ring, token):
        if not left[ring]:
            return token
        left[ring] -= 1
        made = ring.send(token)
        if left[ring] == 0:
            results[ring] = made
            return token
        return made

    token = turn(up_ring, du_sum)
    token = turn(down_ring, token)
    token = turn(up_ring, token)
    back_c, dx_c, sums_c = input_grad_of(dqkv_c, made_b, dy_c, dnm_c, [token])
    back_c_oth = swap(back_c)
    token = turn(down_ring, dx_c)
    y_c, *a_c = project(da_c if one_pair_each else att_c, made_c, mlp_c, [token])
    a_c_oth = swap(a_c[1])
    token = turn(up_ring, y_c)
    token = turn(down_ring, token)
    attn_grad, attn_sum = attn_grad_call(
        [made_b[2], made_c[2], norms_b, norms_c],
        [a_b[0], a_c[0], a_b_oth, a_c_oth],
        [back_c, back_b, back_c_oth, back_b_oth],
        dy_list,
        [token],
    )
    dqkv_sum = attn_sum[:, : 3 * dim]
    attn_ring = ring_sum(attn_grad, (3 * dim, dim), "ctx")
    next(attn_ring)
    left[attn_ring] = steps

    norm_sums = sums_b + sums_c
    norm_own = lax.dynamic_slice_in_dim(norm_sums, my_half * half, half, 1)
    norm_oth = swap(lax.dynamic_slice_in_dim(norm_sums, (1 - my_half) * half, half, 1))

    def own_part(vec):
        size = vec.shape[1] // 2
        return lax.dynamic_slice_in_dim(vec, my_half * size, size, 1).reshape(-1, half)

    token = turn(attn_ring, attn_sum)
    (norm_oth,) = tied(token, norm_oth)
    small_sums = jnp.concatenate(
        [norm_own + norm_oth, own_part(dy_sum), own_part(dqkv_sum), own_part(du_sum)], axis=0
    )
    small_ring = butterfly_sum(small_sums, "ctx")
    next(small_ring)
    at = 0
    summed = None
    while any(left.values()):
        token = turn((up_ring, attn_ring, down_ring, attn_ring)[at % 4], token)
        if at % 2 == 0 and summed is None:
            summed = small_ring.send(token)
        at += 1
    while summed is None:
        summed = small_ring.send(token)
    small_sums = summed
    (down_grad,) = results[down_ring]
    (up_grad,) = results[up_ring]
    qkv_grad, proj_grad = results[attn_ring]

    qkv_end = 5 + dqkv_sum.shape[1] // 2 // half
    dy_total = small_sums[4:5]
    pick = lambda yes, no: jnp.where(first_section, yes, no)
    layer_out = jnp.stack([pick(y_c, y_b), pick(y_b, y_c)])[None, :, None]
    input_grad = jnp.stack([pick(dx_b, dx_c), pick(dx_c, dx_b)])[None, :, None]
    return (
        layer_out,
        input_grad,
        qkv_grad[None],
        small_sums[5:qkv_end].reshape(1, -1),
        proj_grad[None],
        dy_total,
        up_grad[None],
        small_sums[qkv_end:].reshape(1, -1),
        down_grad[None],
        dy_total,
        small_sums[0:1],
        small_sums[1:2],
        small_sums[2:3],
        small_sums[3:4],
    )


def solution(mesh):
    in_specs = (
        P(None, "wsh", "ctx", None),
        P(None, "wsh", "ctx", None),
        P(),
        P("section", "wsh", None),
        P("section", "wsh"),
        P("section", "wsh", None),
        P("section", "wsh"),
        P("section", "wsh", None),
        P("section", "wsh"),
        P("section", "wsh", None),
        P("section", "wsh"),
        P("section", "wsh"),
        P("section", "wsh"),
        P("section", "wsh"),
        P("section", "wsh"),
    )
    out_specs = (
        P("section", None, "wsh", "ctx", None),
        P("section", None, "wsh", "ctx", None),
        P("section", "wsh", None),
        P("section", "wsh"),
        P("section", "wsh", None),
        P("section", "wsh"),
        P("section", "wsh", None),
        P("section", "wsh"),
        P("section", "wsh", None),
        P("section", "wsh"),
        P("section", "wsh"),
        P("section", "wsh"),
        P("section", "wsh"),
        P("section", "wsh"),
    )
    return jax.shard_map(body, mesh=mesh, in_specs=in_specs, out_specs=out_specs, check_vma=False)
```

```python
import functools

import jax
import jax.numpy as jnp
from jax import lax
from jax.experimental import pallas as pl
from jax.experimental.pallas import tpu as pltpu
from jax.sharding import PartitionSpec as P

HEADS = 16
ROT = 16
NORM_EPS = 1e-05
ROPE_BASE = 10000.0
MASKED_SCORE = -1e30
LANES = 128
VMEM_LIMIT = 56 * 1024 * 1024
TAIL_LIMIT = 56 * 1024 * 1024
RING_LIMIT = 50 * 1024 * 1024
INV_SQRT2 = 0.7071067811865476
INV_SQRT_2PI = 0.3989422804014327

f32 = jnp.float32
bf16 = jnp.bfloat16


def dot_nn(left, right):
    return lax.dot_general(left, right, (((1,), (0,)), ((), ())), preferred_element_type=f32)


def dot_nt(left, right):
    return lax.dot_general(left, right, (((1,), (1,)), ((), ())), preferred_element_type=f32)


def params_of(limit):
    return dict(
        compiler_params=pltpu.CompilerParams(vmem_limit_bytes=limit),
        cost_estimate=pl.CostEstimate(flops=1, bytes_accessed=1, transcendentals=0),
    )


def whole(shape):
    rank = len(shape)
    return pl.BlockSpec(shape, lambda *args: (0,) * rank)


def shape_of(shape, dtype):
    return jax.ShapeDtypeStruct(shape, dtype)


def rope(vals, tab_ref):
    return (
        vals * tab_ref[0]
        + pltpu.roll(vals, LANES - ROT // 2, 1) * tab_ref[1]
        + pltpu.roll(vals, ROT // 2, 1) * tab_ref[2]
    )


def unrope(vals, tab_ref):
    return (
        vals * tab_ref[0]
        - pltpu.roll(vals, LANES - ROT // 2, 1) * tab_ref[1]
        - pltpu.roll(vals, ROT // 2, 1) * tab_ref[2]
    )


def normalized(hidden):
    row_mean = jnp.mean(hidden, axis=-1, keepdims=True)
    centered = hidden - row_mean
    spread = jnp.mean(centered * centered, axis=-1, keepdims=True)
    scale = lax.rsqrt(spread + NORM_EPS)
    return centered * scale, scale


def start_all(copies):
    for copy in copies:
        copy.start()
    return copies


def wait_all(copies):
    for copy in copies:
        copy.wait()


def qkv_kernel(own_given, wsh_ref, inputs, weights, outputs, buf, sems):
    half, dim = buf.shape[2:]
    copies = start_all(
        [
            pltpu.make_async_copy(
                weight.at[:, pl.ds(part * dim, dim)], buf.at[part, side], sems.at[part, side]
            )
            for part in range(3)
            for side, weight in enumerate(weights)
        ]
    )
    out, x_out, own, oth = outputs
    x = inputs[0].ref()[...]
    if not own_given:
        x = jnp.where(wsh_ref[1] == 1, x, inputs[4].ref()[...])
    x_out.ref[...] = x
    x_out.send()
    xhat, _ = normalized(x.astype(f32))
    vec_ref, bias_ref, tab_ref = (item.ref() for item in inputs[1:4])
    na = (xhat * vec_ref[0:1] + vec_ref[1:2]).astype(bf16)
    nm = (xhat * vec_ref[2:3] + vec_ref[3:4]).astype(bf16)
    first = wsh_ref[0] == 0
    for i, rows in enumerate((na, nm)):
        own.ref[i] = jnp.where(first, rows[:, :half], rows[:, half:])
        oth.ref[i] = jnp.where(first, rows[:, half:], rows[:, :half])
    own.send()
    oth.send()
    for part in range(3):
        wait_all(copies[2 * part : 2 * part + 2])
        for at in range(0, dim, 2 * LANES):
            cols = slice(at, at + 2 * LANES)
            res = (
                dot_nn(own.ref[0], buf[part, 0, :, cols])
                + dot_nn(oth.ref[0], buf[part, 1, :, cols])
                + bias_ref[:, part * dim + at : part * dim + at + 2 * LANES]
            )
            for i in range(2):
                vals = res[:, i * LANES : (i + 1) * LANES]
                if part < 2:
                    vals = rope(vals, tab_ref)
                out.ref[at // LANES + i, part] = vals.astype(bf16)


def layer_of(shape, index):
    return pl.BlockSpec((pl.squeezed,) + shape, lambda *args: (index, 0, 0))


HERE = pl.BlockSpec(memory_space=pltpu.VMEM)
SCALARS = pl.BlockSpec(memory_space=pltpu.SMEM)
ANYWHERE = pl.BlockSpec(memory_space=pl.ANY)
IN_HBM = pl.BlockSpec(memory_space=pltpu.HBM)


class Arriving:
    def __init__(self, buf, copy=None):
        self.buf, self.copy = buf, copy

    def ref(self):
        if self.copy is not None:
            self.copy.wait()
            self.copy = None
        return self.buf


class Leaving:
    def __init__(self, buf, copy=None):
        self.ref, self.copy, self.sent = buf, copy, copy is None

    def send(self):
        if not self.sent:
            self.copy.start()
            self.sent = True


def local_kernel(body, near_in, near_out, scalars, weights, followed, *refs):
    refs = list(refs)

    def take(number):
        taken = refs[:number]
        del refs[:number]
        return taken

    scalar_refs, array_refs = take(scalars), take(len(near_in))
    weight_refs, _, out_refs = take(weights), take(followed), take(len(near_out))
    in_sems, out_sems = take(2)
    inputs, outputs = [], []
    for i, (near, ref) in enumerate(zip(near_in, array_refs)):
        if near:
            inputs.append(Arriving(ref))
        else:
            buf = take(1)[0]
            copy = pltpu.make_async_copy(ref, buf, in_sems.at[i])
            copy.start()
            inputs.append(Arriving(buf, copy))
    for i, (near, ref) in enumerate(zip(near_out, out_refs)):
        if near:
            outputs.append(Leaving(ref))
        else:
            buf = take(1)[0]
            outputs.append(Leaving(buf, pltpu.make_async_copy(buf, ref, out_sems.at[i])))
    body(*scalar_refs, inputs, weight_refs, outputs, *refs)
    for item in inputs:
        item.ref()
    for item in outputs:
        item.send()
    for item in outputs:
        if item.copy is not None:
            item.copy.wait()


def far(array):
    return (array,)


def local_call(body, name, scalars, arrays, weights, out_shape, scratch=(), after=(), limit=VMEM_LIMIT):
    near_in = [not isinstance(a, tuple) for a in arrays]
    near_out = [not isinstance(o, tuple) for o in out_shape]
    raw_out = [isinstance(o, list) for o in out_shape]
    arrays = [a if near else a[0] for a, near in zip(arrays, near_in)]
    shapes = [o if near and not raw else o[0] for o, near, raw in zip(out_shape, near_out, raw_out)]
    far_bufs = [
        pltpu.VMEM(a.shape, a.dtype)
        for a, near in zip(arrays + shapes, near_in + near_out)
        if not near
    ]
    return pl.pallas_call(
        functools.partial(
            local_kernel, body, near_in, near_out, len(scalars), len(weights), len(after)
        ),
        in_specs=[SCALARS] * len(scalars)
        + [HERE if near else IN_HBM for near in near_in]
        + [IN_HBM] * len(weights)
        + [ANYWHERE] * len(after),
        out_specs=[HERE if near and not raw else IN_HBM for near, raw in zip(near_out, raw_out)],
        out_shape=shapes,
        scratch_shapes=[
            pltpu.SemaphoreType.DMA((len(arrays) + 1,)),
            pltpu.SemaphoreType.DMA((len(shapes),)),
        ]
        + far_bufs
        + list(scratch),
        name=name,
        **params_of(limit),
    )(*scalars, *arrays, *weights, *after)


def qkv_call(given, got, vecs, qkv_b, tab, w_own, w_oth, wsh):
    rows, dim = given.shape
    half = w_own.shape[0]
    pairs = dim // LANES
    return local_call(
        functools.partial(qkv_kernel, got is None),
        "qkv_proj",
        [wsh],
        [given, vecs, qkv_b, tab] if got is None else [far(given), vecs, qkv_b, tab, got],
        [w_own, w_oth],
        [far(shape_of((pairs, 3, rows, LANES), bf16)), far(shape_of((rows, dim), bf16))]
        + [far(shape_of((2, rows, half), bf16))] * 2,
        [pltpu.VMEM((3, 2, half, dim), bf16), pltpu.SemaphoreType.DMA((3, 2))],
    )


FF_TILE = 1024
FF_PIECE = 512


def ff_tiles(wsh_ref, up_own, up_oth, dn_own, dn_oth, up_buf, dn_buf, sems):
    own = dn_own.shape[0] // FF_TILE
    tiles = []
    for t in range(2 * own):
        start = pl.multiple_of(((wsh_ref[0] * own + t) % (2 * own)) * FF_TILE, FF_TILE)
        cols = pl.ds(start, FF_TILE)
        down = (dn_own if t < own else dn_oth).at[pl.ds((t % own) * FF_TILE, FF_TILE)]
        copies = [
            pltpu.make_async_copy(up_own.at[:, cols], up_buf.at[t, 0], sems.at[t, 0]),
            pltpu.make_async_copy(up_oth.at[:, cols], up_buf.at[t, 1], sems.at[t, 1]),
            pltpu.make_async_copy(down, dn_buf.at[t], sems.at[t, 2]),
        ]
        tiles.append((t, start, start_all(copies)))
    for t, start, copies in tiles:
        wait_all(copies)
        for at in range(0, FF_TILE, FF_PIECE):
            row = (t % own) * FF_TILE + at
            place = pl.ds(pl.multiple_of(start + at, FF_PIECE), FF_PIECE)
            yield t, place, t < own, slice(row, row + FF_PIECE), slice(at, at + FF_PIECE)


def ff_scratch(half, ff, dim):
    tiles = ff // FF_TILE
    return [
        pltpu.VMEM((tiles, 2, half, FF_TILE), bf16),
        pltpu.VMEM((tiles, FF_TILE, dim), bf16),
        pltpu.SemaphoreType.DMA((tiles, 3)),
    ]


def mlp_kernel(save, wsh_ref, inputs, weights, outputs, up_buf, dn_buf, sems):
    out_ref = outputs[0].ref
    started = False
    for t, place, held, rows, piece in ff_tiles(wsh_ref, *weights, up_buf, dn_buf, sems):
        own_ref, oth_ref, up_b, down_b = (item.ref() for item in inputs)
        if not started:
            out_ref[...] = jnp.broadcast_to(down_b[...], out_ref.shape)
            started = True
        pre = (
            dot_nn(own_ref[1], up_buf[t, 0, :, piece])
            + dot_nn(oth_ref[1], up_buf[t, 1, :, piece])
            + up_b[:, place]
        )
        gate = 0.5 + 0.5 * lax.erf(pre * INV_SQRT2)
        act = (pre * gate).astype(bf16)
        if save:
            slope = gate + pre * (INV_SQRT_2PI * jnp.exp(-0.5 * pre * pre))
            outputs[1].ref[place] = slope.astype(bf16).T
            outputs[2 if held else 3].ref[rows] = act.T
            if not held:
                outputs[2].send()
        out_ref[...] += dot_nn(act, dn_buf[t, piece])


def mlp_call(own, oth, up_b, down_b, up_own, up_oth, dn_own, dn_oth, wsh, save):
    rows, half = own.shape[1:]
    dim = dn_own.shape[1]
    ff = up_own.shape[1]
    out_shape = [far(shape_of((rows, dim), f32))]
    if save:
        out_shape += [far(shape_of((ff, rows), bf16))]
        out_shape += [far(shape_of((ff // 2, rows), bf16))] * 2
    return local_call(
        functools.partial(mlp_kernel, save),
        "mlp_forward",
        [wsh],
        [far(own), far(oth), up_b, down_b],
        [up_own, up_oth, dn_own, dn_oth],
        out_shape,
        ff_scratch(half, ff, dim),
    )


def mlp_back_kernel(wsh_ref, inputs, weights, outputs, acc_own, acc_oth, up_buf, dn_buf, sems):
    du, dnm = outputs
    half = acc_own.shape[0]
    acc_own[...] = jnp.zeros(acc_own.shape, f32)
    acc_oth[...] = jnp.zeros(acc_oth.shape, f32)
    for t, place, _, _, piece in ff_tiles(wsh_ref, *weights, up_buf, dn_buf, sems):
        dy_ref, slope_ref = (item.ref() for item in inputs)
        dact = dot_nt(dn_buf[t, piece], dy_ref[...])
        vals = (dact * slope_ref[place].astype(f32)).astype(bf16)
        du.ref[place] = vals
        acc_own[...] += dot_nn(up_buf[t, 0, :, piece], vals)
        acc_oth[...] += dot_nn(up_buf[t, 1, :, piece], vals)
    du.send()
    first = wsh_ref[0] == 0
    dnm.ref[:, :half] = jnp.where(first, acc_own[...], acc_oth[...]).T
    dnm.ref[:, half:] = jnp.where(first, acc_oth[...], acc_own[...]).T


def mlp_back_call(dy, slope, up_own, up_oth, dn_own, dn_oth, wsh, after, limit):
    rows, dim = dy.shape
    half, ff = up_own.shape
    return local_call(
        mlp_back_kernel,
        "mlp_backward",
        [wsh],
        [far(dy), far(slope)],
        [up_own, up_oth, dn_own, dn_oth],
        [far(shape_of(slope.shape, bf16)), far(shape_of((rows, dim), f32))],
        [pltpu.VMEM((half, rows), f32), pltpu.VMEM((half, rows), f32)] + ff_scratch(half, ff, dim),
        after,
        limit,
    )


def sort_in(loc_ref, ref, dst, half_rows, part=None):
    for block in range(dst.shape[0] // half_rows):
        place = loc_ref[block]
        rows = pl.ds(pl.multiple_of((place % 2) * half_rows, half_rows), half_rows)
        if part is None:
            vals = ref[place // 2, rows, :]
        else:
            vals = ref[place // 2, part, rows, :]
        dst[block * half_rows : (block + 1) * half_rows] = vals


def sort_out(loc_ref, vals, ref, half_rows, part=None):
    for block in range(vals.shape[0] // half_rows):
        place = loc_ref[block]
        rows = pl.ds(pl.multiple_of((place % 2) * half_rows, half_rows), half_rows)
        piece = vals[block * half_rows : (block + 1) * half_rows]
        if part is None:
            ref[place // 2, rows, :] = piece
        else:
            ref[place // 2, part, rows, :] = piece


def head_of(vals, head):
    lane = lax.broadcasted_iota(jnp.int32, vals.shape, 1)
    return jnp.where(lane // (LANES // 2) == head, vals, jnp.zeros_like(vals))


def scores_of(keys, queries, scale, diagonal):
    scores = dot_nt(keys, queries) * scale
    if diagonal:
        key_at = lax.broadcasted_iota(jnp.int32, scores.shape, 0)
        query_at = lax.broadcasted_iota(jnp.int32, scores.shape, 1)
        scores = jnp.where(key_at <= query_at, scores, MASKED_SCORE)
    return scores


def attend_kernel(tile, loc_ref, inputs, weights, outputs, q_s, k_s, v_s, vt_s, o_s):
    qkv_ref = inputs[0].ref()
    o_ref, lse_ref = (item.ref for item in outputs)
    half_rows = qkv_ref.shape[2] // 2
    seq = q_s.shape[0]
    head_size = LANES // 2
    scale = head_size**-0.5
    sort_in(loc_ref, qkv_ref, q_s, half_rows, 0)
    sort_in(loc_ref, qkv_ref, k_s, half_rows, 1)
    sort_in(loc_ref, qkv_ref, v_s, half_rows, 2)
    vt_s[...] = v_s[...].T
    for t in range(seq // tile):
        rows = slice(t * tile, (t + 1) * tile)
        queries = q_s[rows]
        outs = []
        for head in range(2):
            picked = head_of(queries, head)
            parts = [
                scores_of(k_s[i * tile : (i + 1) * tile], picked, scale, i == t)
                for i in range(t + 1)
            ]
            top = functools.reduce(
                jnp.maximum, [jnp.max(p, axis=0, keepdims=True) for p in parts]
            )
            parts = [jnp.exp(p - top) for p in parts]
            total = sum(jnp.sum(p, axis=0, keepdims=True) for p in parts)
            lse_ref[head : head + 1, rows] = top + jnp.log(total)
            inverse = 1.0 / total
            acc = None
            for i, p in enumerate(parts):
                term = dot_nn(
                    vt_s[head * head_size : (head + 1) * head_size, i * tile : (i + 1) * tile],
                    (p * inverse).astype(bf16),
                )
                acc = term if acc is None else acc + term
            outs.append(acc)
        o_s[rows] = jnp.concatenate(outs, axis=0).T.astype(bf16)
    sort_out(loc_ref, o_s, o_ref, half_rows)


def attend_call(qkv, loc, after):
    count, _, rows, _ = qkv.shape
    seq = count * rows
    return local_call(
        functools.partial(attend_kernel, 256),
        "attention",
        [loc],
        [qkv],
        [],
        [far(shape_of((count, rows, LANES), bf16)), far(shape_of((2, seq), f32))],
        [
            pltpu.VMEM((seq, LANES), bf16),
            pltpu.VMEM((seq, LANES), bf16),
            pltpu.VMEM((seq, LANES), bf16),
            pltpu.VMEM((LANES, seq), bf16),
            pltpu.VMEM((seq, LANES), bf16),
        ],
        after,
    )


def attend_back_kernel(
    tile, part, loc_ref, inputs, weights, outputs, q_s, k_s, v_s, da_s, kt_s, dq_s, dk_s, dv_s
):
    da_ref, qkv_ref, lse_ref = (item.ref() for item in inputs)
    out_ref = outputs[0].ref
    half_rows = qkv_ref.shape[2] // 2
    seq = q_s.shape[0]
    head_size = LANES // 2
    scale = head_size**-0.5
    sort_in(loc_ref, qkv_ref, q_s, half_rows, 0)
    sort_in(loc_ref, qkv_ref, k_s, half_rows, 1)
    sort_in(loc_ref, qkv_ref, v_s, half_rows, 2)
    sort_in(loc_ref, da_ref, da_s, half_rows, part)
    kt_s[...] = k_s[...].T
    dk_s[...] = jnp.zeros(dk_s.shape, f32)
    dv_s[...] = jnp.zeros(dv_s.shape, f32)
    for t in range(seq // tile):
        rows = slice(t * tile, (t + 1) * tile)
        outs = []
        for head in range(2):
            queries = head_of(q_s[rows], head)
            grads = head_of(da_s[rows], head)
            lse = lse_ref[head : head + 1, rows]
            probs, dprobs, row_dot = [], [], 0.0
            for i in range(t + 1):
                keys = slice(i * tile, (i + 1) * tile)
                p = jnp.exp(scores_of(k_s[keys], queries, scale, i == t) - lse)
                dp = dot_nt(v_s[keys], grads)
                row_dot = row_dot + jnp.sum(p * dp, axis=0, keepdims=True)
                dv_s[keys] += dot_nn(p.astype(bf16), grads)
                probs.append(p)
                dprobs.append(dp)
            acc = None
            for i in range(t + 1):
                keys = slice(i * tile, (i + 1) * tile)
                ds = (probs[i] * (dprobs[i] - row_dot) * scale).astype(bf16)
                dk_s[keys] += dot_nn(ds, queries)
                term = dot_nn(kt_s[head * head_size : (head + 1) * head_size, keys], ds)
                acc = term if acc is None else acc + term
            outs.append(acc)
        dq_s[rows] = jnp.concatenate(outs, axis=0).T.astype(bf16)
    sort_out(loc_ref, dq_s, out_ref, half_rows, 0)
    k_s[...] = dk_s[...].astype(bf16)
    v_s[...] = dv_s[...].astype(bf16)
    sort_out(loc_ref, k_s, out_ref, half_rows, 1)
    sort_out(loc_ref, v_s, out_ref, half_rows, 2)


def attend_back_call(qkv, da, lse, loc, after, limit):
    count, _, rows, _ = qkv.shape
    seq = count * rows
    part = 0 if da.ndim == 4 else None
    (res,) = local_call(
        functools.partial(attend_back_kernel, 256, part),
        "attention_backward",
        [loc],
        [da, far(qkv), far(lse)],
        [],
        [far(shape_of(qkv.shape, bf16))],
        [pltpu.VMEM((seq, LANES), bf16)] * 4
        + [pltpu.VMEM((LANES, seq), bf16), pltpu.VMEM((seq, LANES), bf16)]
        + [pltpu.VMEM((seq, LANES), f32)] * 2,
        after,
        limit,
    )
    return res


def by_head(parts):
    pairs, rows, lanes = parts.shape
    return jnp.transpose(parts, (1, 0, 2)).reshape(rows, HEADS, pairs * lanes // HEADS)


def by_pair(heads):
    rows = heads.shape[0]
    return jnp.transpose(heads.reshape(rows, -1, LANES), (1, 0, 2))


def wide_scores(queries, keys, query_pos, key_pos):
    raw = jnp.einsum("qhd,khd->hqk", queries, keys, preferred_element_type=f32)
    allowed = (query_pos[:, None] >= key_pos[None, :])[None]
    return jnp.where(allowed, raw * queries.shape[-1] ** (-0.5), MASKED_SCORE)


def key_blocks(arrays, rows):
    return tuple(a.reshape((a.shape[0] // rows, rows) + a.shape[1:]) for a in arrays)


def wide_attend(qkv, query_pos, key_pos):
    queries = by_head(qkv[:, 0])
    keys = lax.all_gather(by_head(qkv[:, 1]), "ctx", axis=0, tiled=True)
    values = lax.all_gather(by_head(qkv[:, 2]), "ctx", axis=0, tiled=True)
    block = min(512, keys.shape[0])
    split = key_blocks((keys, values, key_pos), block)
    rows, _, head_size = queries.shape

    def max_step(carry, block_in):
        top, total = carry
        scores = wide_scores(queries, block_in[0], query_pos, block_in[2])
        new_top = jnp.maximum(top, jnp.max(scores, axis=-1))
        part = jnp.sum(jnp.exp(scores - new_top[..., None]), axis=-1)
        return ((new_top, total * jnp.exp(top - new_top) + part), None)

    start = (jnp.full((HEADS, rows), MASKED_SCORE, f32), jnp.zeros((HEADS, rows), f32))
    (top, total), _ = lax.scan(max_step, start, split)
    lse = top + jnp.log(total)

    def value_step(running, block_in):
        scores = wide_scores(queries, block_in[0], query_pos, block_in[2])
        probs = jnp.exp(scores - lse[..., None]).astype(bf16)
        term = jnp.einsum("hqk,khd->qhd", probs, block_in[1], preferred_element_type=f32)
        return (running + term, None)

    attended, _ = lax.scan(value_step, jnp.zeros((rows, HEADS, head_size), f32), split)
    return by_pair(attended.astype(bf16)), (queries, keys, values, lse)


def wide_attend_back(kept, da, query_pos, key_pos):
    queries, keys, values, lse = kept
    grads = by_head(da)
    block = min(512, keys.shape[0])
    split = key_blocks((keys, values, key_pos), block)
    scale = queries.shape[-1] ** (-0.5)

    def pieces(block_in):
        scores = wide_scores(queries, block_in[0], query_pos, block_in[2])
        probs = jnp.exp(scores - lse[..., None])
        dprobs = jnp.einsum("qhd,khd->hqk", grads, block_in[1], preferred_element_type=f32)
        return probs, dprobs

    def dot_step(running, block_in):
        probs, dprobs = pieces(block_in)
        return (running + jnp.sum(probs * dprobs, axis=-1), None)

    row_dot, _ = lax.scan(dot_step, jnp.zeros(lse.shape, f32), split)

    def key_step(running, block_in):
        probs, dprobs = pieces(block_in)
        ds = (scale * probs * (dprobs - row_dot[..., None])).astype(bf16)
        running = running + jnp.einsum("hqk,khd->qhd", ds, block_in[0], preferred_element_type=f32)
        dk = jnp.einsum("hqk,qhd->khd", ds, queries, preferred_element_type=f32)
        dv = jnp.einsum("hqk,qhd->khd", probs.astype(bf16), grads, preferred_element_type=f32)
        return (running, (dk.astype(bf16), dv.astype(bf16)))

    dq, (dk, dv) = lax.scan(key_step, jnp.zeros(queries.shape, f32), split)
    dk, dv = (
        lax.psum_scatter(part.reshape(keys.shape), "ctx", scatter_dimension=0, tiled=True)
        for part in (dk, dv)
    )
    return jnp.stack([by_pair(dq.astype(bf16)), by_pair(dk), by_pair(dv)], axis=1)


def lanes_of(ref):
    return jnp.concatenate([ref[i] for i in range(ref.shape[0])], axis=1)


def both_halves(w_own, w_oth, buf, sems):
    return start_all(
        [
            pltpu.make_async_copy(weight, buf.at[side], sems.at[side])
            for side, weight in enumerate((w_own, w_oth))
        ]
    )


def half_scratch(weight):
    return [pltpu.VMEM((2,) + weight.shape, bf16), pltpu.SemaphoreType.DMA((2,))]


def proj_kernel(part, wsh_ref, inputs, weights, outputs, buf, sems):
    copies = both_halves(*weights, buf, sems)
    y, own, oth = outputs
    half = buf.shape[1]
    first = wsh_ref[0] == 0
    a_ref = inputs[0].ref()
    a = lanes_of(a_ref if part is None else a_ref.at[:, part])
    own.ref[...] = jnp.where(first, a[:, :half], a[:, half:])
    oth.ref[...] = jnp.where(first, a[:, half:], a[:, :half])
    own.send()
    oth.send()
    bias_ref, x_ref, mlp_ref = (item.ref() for item in inputs[1:])
    wait_all(copies)
    attn = dot_nn(own.ref[...], buf[0]) + dot_nn(oth.ref[...], buf[1]) + bias_ref[...]
    y.ref[...] = (x_ref[...].astype(f32) + attn + mlp_ref[...]).astype(bf16)


def proj_call(a, x, mlp, bias, p_own, p_oth, wsh, after, limit):
    rows, dim = x.shape
    half = p_own.shape[0]
    return local_call(
        functools.partial(proj_kernel, 1 if a.ndim == 4 else None),
        "attn_out",
        [wsh],
        [a, bias, far(x), far(mlp)],
        [p_own, p_oth],
        [far(shape_of((rows, dim), bf16))] + [far(shape_of((rows, half), bf16))] * 2,
        half_scratch(p_own),
        after,
        limit,
    )


def da_kernel(own_given, wsh_ref, inputs, weights, outputs, buf, sems):
    copies = both_halves(*weights, buf, sems)
    out_ref, dy_out = outputs[0].ref, outputs[1]
    dy = inputs[0].ref()[...]
    if not own_given:
        dy = jnp.where(wsh_ref[1] == 1, inputs[1].ref()[...], dy)
    dy_out.ref[...] = dy
    dy_out.send()
    wsh = wsh_ref[0]
    joined = len(out_ref.shape) == 4
    if joined:
        out_ref[:, 1] = inputs[2].ref()[...]
    count = out_ref.shape[0] // 2
    for place, side in ((wsh * count, 0), ((1 - wsh) * count, 1)):
        copies[side].wait()
        part = dot_nt(dy, buf[side]).astype(bf16)
        for i in range(count):
            vals = part[:, i * LANES : (i + 1) * LANES]
            if joined:
                out_ref[place + i, 0] = vals
            else:
                out_ref[place + i] = vals


def da_call(given, got, p_own, p_oth, wsh, joined=None):
    rows, dim = given.shape
    pairs = dim // LANES
    arrays = [far(given)] + ([] if got is None else [got])
    arrays += [] if joined is None else [far(joined)]
    shape = (pairs, rows, LANES) if joined is None else (pairs, 2, rows, LANES)
    return local_call(
        functools.partial(da_kernel, got is None),
        "attn_out_backward",
        [wsh],
        arrays,
        [p_own, p_oth],
        [far(shape_of(shape, bf16)), far(shape_of((rows, dim), bf16))],
        half_scratch(p_own),
    )


def dx_kernel(wsh_ref, inputs, weights, outputs, grad_s, buf, sems):
    copies = both_halves(*weights, buf, sems)
    back, dx, sums = outputs
    dqkv_ref, tab_ref = inputs[0].ref(), inputs[1].ref()
    pairs = dqkv_ref.shape[0]
    for part in range(3):
        for pair in range(pairs):
            vals = dqkv_ref[pair, part]
            if part < 2:
                vals = unrope(vals.astype(f32), tab_ref).astype(bf16)
            back.ref[pair, part] = vals
            grad_s[:, pl.ds((part * pairs + pair) * LANES, LANES)] = vals
    back.send()
    vec_ref, x_ref, dy_ref, dnm_ref = (item.ref() for item in inputs[2:])
    first = wsh_ref[0] == 0
    copies[0].wait()
    own = dot_nt(grad_s[...], buf[0])
    copies[1].wait()
    oth = dot_nt(grad_s[...], buf[1])
    dna = jnp.concatenate([jnp.where(first, own, oth), jnp.where(first, oth, own)], axis=1)
    dnm = dnm_ref[...]
    xhat, scale = normalized(x_ref[...].astype(f32))
    grad = dna * vec_ref[0:1] + dnm * vec_ref[2:3]
    inner = (
        grad
        - jnp.mean(grad, axis=-1, keepdims=True)
        - xhat * jnp.mean(grad * xhat, axis=-1, keepdims=True)
    )
    dx.ref[...] = (dy_ref[...].astype(f32) + scale * inner).astype(bf16)
    dx.send()
    sums.ref[0:1] = jnp.sum(dna * xhat, axis=0, keepdims=True)
    sums.ref[1:2] = jnp.sum(dna, axis=0, keepdims=True)
    sums.ref[2:3] = jnp.sum(dnm * xhat, axis=0, keepdims=True)
    sums.ref[3:4] = jnp.sum(dnm, axis=0, keepdims=True)


def dx_call(dqkv, tab, x, dy, dnm, vecs, w_own, w_oth, wsh, after, limit):
    rows, dim = x.shape
    return local_call(
        dx_kernel,
        "section_input_grad",
        [wsh],
        [dqkv, tab, vecs, far(x), far(dy), far(dnm)],
        [w_own, w_oth],
        [far(shape_of(o, t)) for o, t in ((dqkv.shape, bf16), ((rows, dim), bf16), ((4, dim), f32))],
        [pltpu.VMEM((rows, 3 * dim), bf16)] + half_scratch(w_own),
        after,
        limit,
    )


def joined_rows(items):
    return jnp.concatenate([item.ref()[...] for item in items], axis=0)


class Pieces:
    def __init__(self, out_ref, buf, sems):
        self.out_ref, self.buf, self.sems, self.copies = out_ref, buf, sems, []

    def put(self, rows, cols, vals):
        self.buf[rows, cols] = vals.astype(bf16)
        at = len(self.copies)
        self.copies.append(
            pltpu.make_async_copy(
                self.buf.at[rows, cols], self.out_ref.at[rows, cols], self.sems.at[at]
            )
        )
        self.copies[-1].start()

    def finish(self, chunk, ahead, behind):
        height, cut = ahead.ref.shape
        rows = pl.ds(pl.multiple_of(chunk * height, height), height)
        ahead.ref[...] = self.buf[rows, :cut]
        ahead.send()
        behind.ref[...] = self.buf[rows, cut:]
        behind.send()
        wait_all(self.copies)


def grad_call(body, name, idx, arrays, shape, width, count, scratch, after):
    halves = shape_of((shape[0] // count, shape[1] // 2), bf16)
    return local_call(
        functools.partial(body, len(arrays)),
        name,
        [idx],
        arrays,
        [],
        [[shape_of(shape, bf16)], far(halves), far(halves), far(shape_of((1, width), f32))],
        [pltpu.VMEM(shape, bf16), pltpu.SemaphoreType.DMA((4,))] + scratch,
        after,
        TAIL_LIMIT,
    )


def parts_of(items, number):
    size = len(items) // number
    return [items[i * size : (i + 1) * size] for i in range(number)]


def down_grad_kernel(number, idx_ref, inputs, weights, outputs, buf, sems):
    gts, dys = parts_of(inputs, 2)
    out = Pieces(outputs[0].ref, buf, sems)
    dy = joined_rows(dys)
    outputs[3].ref[...] = jnp.sum(dy.astype(f32), axis=0, keepdims=True)
    rows, dim = buf.shape
    tile = rows // 4
    for t in range(4):
        part = slice(t * tile, (t + 1) * tile)
        left = jnp.concatenate([item.ref()[part] for item in gts], axis=1)
        out.put(part, slice(0, dim), dot_nn(left, dy))
    out.finish(idx_ref[idx_ref.shape[0] // 2], outputs[1], outputs[2])


def down_grad_call(idx, gt_list, dy_list, count):
    dim = dy_list[0].shape[1]
    return grad_call(
        down_grad_kernel,
        "down_grad",
        idx,
        [far(a) for a in gt_list + dy_list],
        (gt_list[0].shape[0], dim),
        dim,
        count,
        [],
        [],
    )


def up_grad_kernel(number, idx_ref, inputs, weights, outputs, buf, sems):
    norms, dus = parts_of(inputs, 2)
    out = Pieces(outputs[0].ref, buf, sems)
    left = jnp.concatenate([item.ref()[1] for item in norms], axis=0).T
    rows, ff = buf.shape
    tile = ff // 4
    for t in range(4):
        part = slice(t * tile, (t + 1) * tile)
        du = jnp.concatenate([item.ref()[part] for item in dus], axis=1)
        outputs[3].ref[:, part] = dot_nt(jnp.ones((8, du.shape[1]), bf16), du)[:1]
        out.put(slice(0, rows), part, dot_nt(left, du))
    out.finish(idx_ref[idx_ref.shape[0] // 2], outputs[1], outputs[2])


def up_grad_call(idx, norm_list, du_list, count, after):
    half, ff = norm_list[0].shape[2], du_list[0].shape[0]
    return grad_call(
        up_grad_kernel,
        "up_grad",
        idx,
        [far(a) for a in norm_list + du_list],
        (half, ff),
        ff,
        count,
        [],
        after,
    )


def attn_grad_kernel(number, idx_ref, inputs, weights, outputs, buf, sems):
    norms, outs, dqkvs, dys = parts_of(inputs, 4)
    out = Pieces(outputs[0].ref, buf, sems)
    rows, width = buf.shape
    dim = width // 4
    left = jnp.concatenate([item.ref()[0] for item in norms], axis=0).T
    for part in range(4):
        cols = slice(part * dim, (part + 1) * dim)
        if part < 3:
            right = jnp.concatenate([lanes_of(item.ref().at[:, part]) for item in dqkvs], axis=0)
        else:
            left, right = joined_rows(outs).T, joined_rows(dys)
        outputs[3].ref[:, cols] = jnp.sum(right.astype(f32), axis=0, keepdims=True)
        out.put(slice(0, rows), cols, dot_nn(left, right))
    out.finish(idx_ref[idx_ref.shape[0] // 2], outputs[1], outputs[2])


def attn_grad_call(idx, norm_list, out_list, dqkv_list, dy_list, count, after):
    half, dim = norm_list[0].shape[2], dy_list[0].shape[1]
    return grad_call(
        attn_grad_kernel,
        "attn_grad",
        idx,
        [far(a) for a in norm_list + out_list + dqkv_list + dy_list],
        (half, 4 * dim),
        4 * dim,
        count,
        [],
        after,
    )


def ring_of(count):
    return list(range(0, count, 2)) + list(range(count - 1, 0, -2))


def ring_place(axis):
    count = lax.axis_size(axis)
    me = lax.axis_index(axis)
    return jnp.where(me % 2 == 0, me // 2, count - (me + 1) // 2)


def ring_index(axis):
    count = lax.axis_size(axis)
    return (ring_place(axis) + jnp.arange(count, dtype=jnp.int32)) % count


def ring_shift(vals, axis, by):
    order = ring_of(lax.axis_size(axis))
    count = len(order)
    pairs = [(order[i], order[(i + by) % count]) for i in range(count)]
    return lax.ppermute(vals, axis, pairs)


def tied(token, *vals):
    return lax.optimization_barrier((token, vals))[1]


def fetch(idx_ref, slots, own_ref, bufs, sems):
    return start_all(
        [
            pltpu.make_async_copy(own_ref.at[idx_ref[slot]], bufs.at[i], sems.at[i])
            for i, slot in enumerate(slots)
        ]
    )


def low_total(*terms):
    total = terms[0].astype(f32)
    for term in terms[1:]:
        total = total + term.astype(f32)
    return total.astype(bf16)


def ring_add_kernel(slots, idx_ref, inputs, own_refs, outputs, bufs, sems):
    copies = fetch(idx_ref, slots, own_refs[0], bufs, sems)
    for i, item in enumerate(outputs):
        copies[i].wait()
        got = inputs[i].ref()
        cols, cut = item.ref.shape[1], got.shape[1]
        summed = slice(0, cut) if i == 0 else slice(cols - cut, cols)
        item.ref[:, summed] = low_total(bufs[i, :, summed], got[...])
        if cut < cols:
            rest = slice(cut, cols) if i == 0 else slice(0, cols - cut)
            item.ref[:, rest] = bufs[i, :, rest]
        item.send()


def put_copies(chunk, cols, buf, totals, starts, sem):
    lo, hi = cols, cols + buf.shape[1]
    copies = []
    for i, (total, start) in enumerate(zip(totals, starts)):
        first, last = max(lo, start), min(hi, start + total.shape[2])
        if first < last:
            copies.append(
                pltpu.make_async_copy(
                    buf.at[:, pl.ds(first - lo, last - first)],
                    total.at[chunk, :, pl.ds(first - start, last - first)],
                    sem.at[i],
                )
            )
    return copies


def ring_own_kernel(slots, idx_ref, inputs, own_refs, outputs, bufs, sems):
    wait_all(fetch(idx_ref, slots, own_refs[0], bufs, sems))
    outputs[0].ref[...] = low_total(bufs[0], inputs[0].ref()[...], inputs[1].ref()[...])


def ring_put_kernel(starts, slots, cols, fresh, onward, idx_ref, *refs):
    number = len(slots)
    pieces = refs[:number]
    wide, sems, pass_buf, pass_sems = refs[-4:]
    passed = refs[-4 - onward : -4]
    totals = refs[-4 - onward - len(starts) : -4 - onward]
    leaving = []
    for i, ref in enumerate(passed):
        width = ref.shape[1]
        pass_buf[i, :, :width] = pieces[i][:, :width] if i == 0 else pieces[i][:, -width:]
        leaving += start_all(
            [pltpu.make_async_copy(pass_buf.at[i, :, pl.ds(0, width)], ref, pass_sems.at[i])]
        )
    for i in range(number):
        wide[i] = pieces[i][...].astype(f32)
        leaving += start_all(
            put_copies(idx_ref[slots[i]], cols[i], wide.at[i], totals, starts, sems.at[i])
        )
    wait_all(leaving)


def ring_sum(own, ahead, behind, widths, axis):
    count = lax.axis_size(axis)
    half = count // 2
    full_rows, cols = own.shape
    rows = full_rows // count
    own = own.reshape(count, rows, cols)
    cut = cols // 2
    starts = [sum(widths[:i]) for i in range(len(widths))]
    idx = ring_index(axis)
    chunk, piece = shape_of((rows, cols), bf16), shape_of((rows, cut), bf16)
    sums = [shape_of((count, rows, width), f32) for width in widths]

    def taken(number):
        return [pltpu.VMEM((number, rows, cols), bf16), pltpu.SemaphoreType.DMA((number,))]

    def put(totals, pieces, slots, passed, after):
        number, width = len(pieces), pieces[0].shape[1]
        first_cols = (0,) * number if width == cols else (0, cut)
        fresh = totals is None
        out = pl.pallas_call(
            functools.partial(
                ring_put_kernel,
                starts,
                tuple(k % count for k in slots),
                first_cols,
                fresh,
                len(passed),
            ),
            in_specs=[SCALARS]
            + [HERE] * number
            + [IN_HBM] * (0 if fresh else len(sums))
            + [ANYWHERE] * len(after),
            out_specs=[IN_HBM] * (len(sums) + len(passed)),
            out_shape=sums + passed,
            scratch_shapes=[
                pltpu.VMEM((number, rows, width), f32),
                pltpu.SemaphoreType.DMA((number, len(sums))),
                pltpu.VMEM((2, rows, cols), bf16),
                pltpu.SemaphoreType.DMA((2,)),
            ],
            input_output_aliases={} if fresh else {1 + number + i: i for i in range(len(sums))},
            name="ring_put",
            **params_of(RING_LIMIT),
        )(idx, *pieces, *([] if fresh else totals), *after)
        return out[: len(sums)], out[len(sums) :]

    def both_ways(ahead, behind):
        return ring_shift(ahead, axis, 1), ring_shift(behind, axis, -1)

    token = behind
    ahead, behind = both_ways(ahead, behind)
    token = yield token
    for k in range(half - 1, 0, -1):
        ahead, behind = local_call(
            functools.partial(ring_add_kernel, (k % count, (-k) % count)),
            "ring_add",
            [idx],
            [ahead, behind],
            [own],
            [far(chunk), far(chunk)],
            taken(2),
            [token],
            RING_LIMIT,
        )
        token = behind
        ahead, behind = both_ways(ahead, behind)
        token = yield token
    (mine,) = local_call(
        functools.partial(ring_own_kernel, (0,)),
        "ring_own",
        [idx],
        [ahead, behind],
        [own],
        [far(chunk)],
        taken(1),
        [token],
        RING_LIMIT,
    )
    ahead, behind = both_ways(mine, mine)
    totals, (token,) = put(None, [mine], [0], [shape_of((rows, LANES), bf16)], [])
    token = yield token
    for k in range(1, half):
        passed = [piece if k == half - 1 else chunk] * 2
        totals, passed = put(totals, [ahead, behind], [-k, k], passed, [token])
        token = passed[1]
        ahead, behind = both_ways(*passed)
        token = yield token
    totals, _ = put(totals, [ahead, behind], [-half, half], [], [token])
    yield [total.reshape(full_rows, -1) for total in totals]


def butterfly_sum(vals, axis):
    count = lax.axis_size(axis)
    by = 1
    token = yield None
    if count & (count - 1):
        yield lax.psum(tied(token, vals)[0], axis)
        return
    (vals,) = tied(token, vals)
    while by < count:
        got = lax.ppermute(vals, axis, [(i, i ^ by) for i in range(count)])
        token = yield None
        (got,) = tied(token, got)
        vals = vals + got
        by *= 2
    yield vals


def swap(vals):
    return lax.ppermute(vals, "wsh", [(0, 1), (1, 0)])


def pass_on(vals, by):
    pairs = [(0, 1)] if by > 0 else [(1, 0)]
    return lax.ppermute(vals, "section", pairs)


def block_places(block_pair, count):
    want = jnp.arange(2 * count, dtype=jnp.int32)
    device = jnp.arange(count, dtype=jnp.int32)
    first = (block_pair[None, :] == want[:, None]).astype(jnp.int32)
    second = ((2 * count - 1 - block_pair)[None, :] == want[:, None]).astype(jnp.int32)
    return jnp.sum(first * (2 * device) + second * (2 * device + 1), axis=1)


def row_positions(block_pair, stored, tok_dev):
    count = block_pair.shape[0]
    device = stored // tok_dev
    within = stored % tok_dev
    half_rows = tok_dev // 2
    matches = device[:, None] == jnp.arange(count, dtype=jnp.int32)[None, :]
    pair_block = jnp.sum(jnp.where(matches, block_pair[None, :], 0), axis=1)
    block_idx = jnp.where(within < half_rows, pair_block, 2 * count - 1 - pair_block)
    return block_idx * half_rows + within % half_rows


def rotary_table(positions, head_size):
    half_rot = ROT // 2
    lane = jnp.arange(LANES, dtype=jnp.int32) % head_size
    inv_freq = ROPE_BASE ** (-((lane % half_rot).astype(f32) * 2.0) / ROT)
    angles = positions.astype(f32)[:, None] * inv_freq[None, :]
    cosine, sine = jnp.cos(angles), jnp.sin(angles)
    lead, second = (lane < half_rot)[None], ((lane >= half_rot) & (lane < ROT))[None]
    return jnp.stack(
        [
            jnp.where(lead | second, cosine, 1.0),
            jnp.where(lead, -sine, 0.0),
            jnp.where(second, sine, 0.0),
        ]
    )


def body(
    inputs,
    cotangent,
    block_pair,
    qkv_weight,
    qkv_bias,
    proj_weight,
    proj_bias,
    up_weight,
    up_bias,
    down_weight,
    down_bias,
    attn_gain,
    attn_shift,
    mlp_gain,
    mlp_shift,
):
    first_section = lax.axis_index("section") == 0
    count = lax.axis_size("ctx")
    micros, _, tok_dev, dim = inputs.shape
    head_size = dim // HEADS
    half = dim // 2
    my_half = lax.axis_index("wsh")
    wsh = jnp.stack([my_half.astype(jnp.int32), first_section.astype(jnp.int32)])
    one_pair_each = count == dim // LANES

    wq, wp, wu, wd = (w[0] for w in (qkv_weight, proj_weight, up_weight, down_weight))
    small = jnp.concatenate(
        [
            v[0].reshape(-1, half)
            for v in (
                attn_gain,
                attn_shift,
                mlp_gain,
                mlp_shift,
                proj_bias,
                down_bias,
                qkv_bias,
                up_bias,
            )
        ],
        axis=0,
    )
    small_oth = swap(small)
    wq_oth = swap(wq)
    first_here = lax.optimization_barrier((wq_oth, small_oth))
    wq_oth, small_oth = first_here
    wu_oth = swap(tied(wq_oth, wu)[0])
    wd_oth = swap(tied(wq_oth, wd)[0])
    wp_oth = swap(tied(wu_oth, wp)[0])
    low_part = jnp.where(my_half == 0, small, small_oth).astype(f32)
    high_part = jnp.where(my_half == 0, small_oth, small).astype(f32)
    vecs = jnp.concatenate([low_part[:6], high_part[:6]], axis=1)
    qkv_rows = 6 + qkv_bias.shape[1] // half
    proj_b, down_b = vecs[4:5], vecs[5:6]
    qkv_b = jnp.concatenate([low_part[6:qkv_rows], high_part[6:qkv_rows]], axis=0).reshape(1, -1)
    up_b = jnp.concatenate([low_part[qkv_rows:], high_part[qkv_rows:]], axis=0).reshape(1, -1)

    local_rows = lax.axis_index("ctx") * tok_dev + jnp.arange(tok_dev, dtype=jnp.int32)
    query_pos = row_positions(block_pair, local_rows, tok_dev)
    key_pos = row_positions(block_pair, jnp.arange(count * tok_dev, dtype=jnp.int32), tok_dev)
    tab = rotary_table(query_pos, head_size)
    loc = block_places(block_pair, count)

    def exchange(vals):
        return lax.all_to_all(vals, "ctx", split_axis=0, concat_axis=0, tiled=True)

    rows_in = [inputs[i, 0] for i in range(micros)]
    cot_in = [cotangent[i, 0] for i in range(micros)]

    def norm_qkv(index, got):
        return qkv_call(rows_in[index], got, vecs, qkv_b, tab, wq, wq_oth, wsh)

    def mlp(made, save):
        return mlp_call(made[2], made[3], up_b, down_b, wu, wu_oth, wd, wd_oth, wsh, save)

    def mlp_back(dy, mlp_kept, after=(), limit=VMEM_LIMIT):
        return mlp_back_call(dy, mlp_kept[1], wu, wu_oth, wd, wd_oth, wsh, after, limit)

    def out_back(index, got, joined=None):
        return da_call(cot_in[index], got, wp, wp_oth, wsh, joined)

    def moved(vals):
        return exchange(vals) if one_pair_each else vals

    def attend(qkv, after=()):
        if one_pair_each:
            attended, lse = attend_call(qkv, loc, after)
            return attended, (qkv, lse)
        return wide_attend(qkv, query_pos, key_pos)

    def attend_back(kept, da, after=(), limit=VMEM_LIMIT):
        if one_pair_each:
            return attend_back_call(kept[0], da, kept[1], loc, after, limit)
        da = da[:, 0] if da.ndim == 4 else da
        return wide_attend_back(kept, da, query_pos, key_pos)

    def project(attended, made, mlp_out, after=(), limit=VMEM_LIMIT):
        return proj_call(attended, made[1], mlp_out[0], proj_b, wp, wp_oth, wsh, after, limit)

    def input_grad_of(dqkv, made, dy, dnm, after=(), limit=VMEM_LIMIT):
        return dx_call(dqkv, tab, made[1], dy, dnm, vecs, wq, wq_oth, wsh, after, limit)

    made_a = norm_qkv(0, None)
    qkv_a = moved(made_a[0])
    mlp_a = mlp(made_a, False)
    att_a, _ = attend(qkv_a, [mlp_a[0]])
    att_a = moved(att_a)
    da_a, dy_a = out_back(0, None)
    y_a = project(att_a, made_a, mlp_a, [dy_a])[0]
    da_a = moved(tied(y_a, da_a)[0])

    made_b = norm_qkv(1, pass_on(y_a, 1))
    qkv_2 = moved(tied(da_a, made_b[0])[0])
    norms_b = swap(made_b[3])
    mlp_b = mlp(made_b, True)
    att_b, kept_b = attend(qkv_2, [mlp_b[0], norms_b])
    att_b = moved(att_b)
    gt_b = swap(mlp_b[3])
    dqkv_a_ = attend_back(kept_b, da_a, [gt_b])
    dqkv_a = moved(dqkv_a_)
    y_b, *a_b = project(att_b, made_b, mlp_b, [dqkv_a_])

    made_c = norm_qkv(0, pass_on(y_b, 1))
    qkv_3 = moved(tied(dqkv_a, made_c[0])[0])
    norms_c = swap(made_c[3])
    a_b_oth = swap(a_b[1])
    _, dnm_a = mlp_back(dy_a, mlp_b, [made_c[1]])
    _, dx_a, _ = input_grad_of(dqkv_a, made_b, dy_a, dnm_a, [norms_c, a_b_oth])
    got_a = pass_on(dx_a, -1)
    mlp_c = mlp_call(
        made_c[2], tied(dx_a, made_c[3])[0], up_b, down_b, wu, wu_oth, wd, wd_oth, wsh, True
    )
    da_b, dy_b = out_back(1, tied(mlp_c[0], got_a)[0])
    da_b = moved(tied(qkv_3, da_b)[0])
    att_c, kept_c = attend(qkv_3, [dy_b])
    dy_b_oth, gt_c = swap(dy_b), swap(mlp_c[3])
    dqkv_b = attend_back(kept_c, da_b, [dy_b_oth, gt_c])
    dqkv_b_ = moved(dqkv_b)
    du_b, dnm_b = mlp_back(dy_b, mlp_c, [dqkv_b])
    du_b_oth = swap(du_b)
    back_b, dx_b, sums_b = input_grad_of(dqkv_b_, made_c, dy_b, dnm_b, [du_b_oth])
    got_b = pass_on(dx_b, -1)
    back_b_oth = swap(back_b)

    da_c, dy_c = out_back(0, tied(back_b_oth, got_b)[0], att_c if one_pair_each else None)
    dy_list = [dy_c, dy_b, swap(dy_c), dy_b_oth]
    da_c = moved(da_c)
    idx = ring_index("ctx")
    *down_made, dy_sum = down_grad_call(idx, [mlp_b[2], mlp_c[2], gt_b, gt_c], dy_list, count)
    down_ring = ring_sum(*down_made, (dim,), "ctx")
    token = next(down_ring)
    token = down_ring.send(token)
    du_c, dnm_c = mlp_back(dy_c, mlp_b, [token], TAIL_LIMIT)
    dqkv_c = attend_back(kept_b, da_c, [dnm_c], TAIL_LIMIT)
    token = down_ring.send(dqkv_c)
    dqkv_c = moved(dqkv_c)
    *up_made, du_sum = up_grad_call(
        idx,
        [made_b[2], made_c[2], norms_b, norms_c],
        [du_c, du_b, swap(du_c), du_b_oth],
        count,
        [token],
    )
    up_ring = ring_sum(*up_made, (up_made[0].shape[1],), "ctx")
    token = next(up_ring)
    steps = count + 1
    left = {down_ring: steps - 3, up_ring: steps - 1}
    results = {}

    def turn(ring, token):
        if not left[ring]:
            return token
        left[ring] -= 1
        made = ring.send(token)
        if left[ring] == 0:
            results[ring] = made
            return token
        return made

    token = turn(down_ring, token)
    token = turn(up_ring, token)
    back_c, dx_c, sums_c = input_grad_of(dqkv_c, made_b, dy_c, dnm_c, [token], TAIL_LIMIT)
    back_c_oth = swap(back_c)
    token = turn(down_ring, dx_c)
    y_c, *a_c = project(da_c if one_pair_each else att_c, made_c, mlp_c, [token], TAIL_LIMIT)
    a_c_oth = swap(a_c[1])
    token = turn(up_ring, y_c)
    token = turn(down_ring, token)
    *attn_made, attn_sum = attn_grad_call(
        idx,
        [made_b[2], made_c[2], norms_b, norms_c],
        [a_b[0], a_c[0], a_b_oth, a_c_oth],
        [back_c, back_b, back_c_oth, back_b_oth],
        dy_list,
        count,
        [token],
    )
    dqkv_sum = attn_sum[:, : 3 * dim]
    attn_ring = ring_sum(*attn_made, (3 * dim, dim), "ctx")
    token = next(attn_ring)
    left[attn_ring] = steps - 1

    norm_sums = sums_b + sums_c
    norm_own = lax.dynamic_slice_in_dim(norm_sums, my_half * half, half, 1)
    norm_oth = swap(lax.dynamic_slice_in_dim(norm_sums, (1 - my_half) * half, half, 1))

    def own_part(vec):
        size = vec.shape[1] // 2
        return lax.dynamic_slice_in_dim(vec, my_half * size, size, 1).reshape(-1, half)

    (norm_oth,) = tied(token, norm_oth)
    small_sums = jnp.concatenate(
        [norm_own + norm_oth, own_part(dy_sum), own_part(dqkv_sum), own_part(du_sum)], axis=0
    )
    small_ring = butterfly_sum(small_sums, "ctx")
    next(small_ring)
    at = 0
    summed = None
    while any(left.values()):
        token = turn((up_ring, attn_ring, down_ring, attn_ring)[at % 4], token)
        if at % 2 == 0 and summed is None:
            summed = small_ring.send(token)
        at += 1
    while summed is None:
        summed = small_ring.send(token)
    small_sums = summed
    (down_grad,) = results[down_ring]
    (up_grad,) = results[up_ring]
    qkv_grad, proj_grad = results[attn_ring]

    qkv_end = 5 + dqkv_sum.shape[1] // 2 // half
    dy_total = small_sums[4:5]
    pick = lambda yes, no: jnp.where(first_section, yes, no)
    layer_out = jnp.stack([pick(y_c, y_b), pick(y_b, y_c)])[None, :, None]
    input_grad = jnp.stack([pick(dx_b, dx_c), pick(dx_c, dx_b)])[None, :, None]
    return (
        layer_out,
        input_grad,
        qkv_grad[None],
        small_sums[5:qkv_end].reshape(1, -1),
        proj_grad[None],
        dy_total,
        up_grad[None],
        small_sums[qkv_end:].reshape(1, -1),
        down_grad[None],
        dy_total,
        small_sums[0:1],
        small_sums[1:2],
        small_sums[2:3],
        small_sums[3:4],
    )


def solution(mesh):
    in_specs = (
        P(None, "wsh", "ctx", None),
        P(None, "wsh", "ctx", None),
        P(),
        P("section", "wsh", None),
        P("section", "wsh"),
        P("section", "wsh", None),
        P("section", "wsh"),
        P("section", "wsh", None),
        P("section", "wsh"),
        P("section", "wsh", None),
        P("section", "wsh"),
        P("section", "wsh"),
        P("section", "wsh"),
        P("section", "wsh"),
        P("section", "wsh"),
    )
    out_specs = (
        P("section", None, "wsh", "ctx", None),
        P("section", None, "wsh", "ctx", None),
        P("section", "wsh", None),
        P("section", "wsh"),
        P("section", "wsh", None),
        P("section", "wsh"),
        P("section", "wsh", None),
        P("section", "wsh"),
        P("section", "wsh", None),
        P("section", "wsh"),
        P("section", "wsh"),
        P("section", "wsh"),
        P("section", "wsh"),
        P("section", "wsh"),
    )
    return jax.shard_map(body, mesh=mesh, in_specs=in_specs, out_specs=out_specs, check_vma=False)
```

```python
import functools

import jax
import jax.numpy as jnp
from jax import lax
from jax.experimental import pallas as pl
from jax.experimental.pallas import tpu as pltpu
from jax.sharding import PartitionSpec as P

HEADS = 16
ROT = 16
NORM_EPS = 1e-05
ROPE_BASE = 10000.0
MASKED_SCORE = -1e30
LANES = 128
VMEM_LIMIT = 50 * 1024 * 1024
TAIL_LIMIT = VMEM_LIMIT
RING_LIMIT = VMEM_LIMIT
INV_SQRT2 = 0.7071067811865476
INV_SQRT_2PI = 0.3989422804014327

f32 = jnp.float32
bf16 = jnp.bfloat16


def dot_nn(left, right):
    return lax.dot_general(left, right, (((1,), (0,)), ((), ())), preferred_element_type=f32)


def dot_nt(left, right):
    return lax.dot_general(left, right, (((1,), (1,)), ((), ())), preferred_element_type=f32)


def params_of(limit):
    return dict(
        compiler_params=pltpu.CompilerParams(vmem_limit_bytes=limit),
        cost_estimate=pl.CostEstimate(flops=1, bytes_accessed=1, transcendentals=0),
    )


def whole(shape):
    rank = len(shape)
    return pl.BlockSpec(shape, lambda *args: (0,) * rank)


def shape_of(shape, dtype):
    return jax.ShapeDtypeStruct(shape, dtype)


def rope(vals, tab_ref):
    return (
        vals * tab_ref[0]
        + pltpu.roll(vals, LANES - ROT // 2, 1) * tab_ref[1]
        + pltpu.roll(vals, ROT // 2, 1) * tab_ref[2]
    )


def unrope(vals, tab_ref):
    return (
        vals * tab_ref[0]
        - pltpu.roll(vals, LANES - ROT // 2, 1) * tab_ref[1]
        - pltpu.roll(vals, ROT // 2, 1) * tab_ref[2]
    )


def normalized(hidden):
    row_mean = jnp.mean(hidden, axis=-1, keepdims=True)
    centered = hidden - row_mean
    spread = jnp.mean(centered * centered, axis=-1, keepdims=True)
    scale = lax.rsqrt(spread + NORM_EPS)
    return centered * scale, scale


def start_all(copies):
    for copy in copies:
        copy.start()
    return copies


def wait_all(copies):
    for copy in copies:
        copy.wait()


def qkv_kernel(own_given, wsh_ref, inputs, weights, outputs, buf, sems):
    half, dim = buf.shape[2:]
    copies = start_all(
        [
            pltpu.make_async_copy(
                weight.at[:, pl.ds(part * dim, dim)], buf.at[part, side], sems.at[part, side]
            )
            for part in range(3)
            for side, weight in enumerate(weights)
        ]
    )
    out, x_out, own, oth = outputs
    x = inputs[0].ref()[...]
    if not own_given:
        x = jnp.where(wsh_ref[1] == 1, x, inputs[4].ref()[...])
    x_out.ref[...] = x
    x_out.send()
    xhat, _ = normalized(x.astype(f32))
    vec_ref, bias_ref, tab_ref = (item.ref() for item in inputs[1:4])
    na = (xhat * vec_ref[0:1] + vec_ref[1:2]).astype(bf16)
    nm = (xhat * vec_ref[2:3] + vec_ref[3:4]).astype(bf16)
    first = wsh_ref[0] == 0
    for i, rows in enumerate((na, nm)):
        own.ref[i] = jnp.where(first, rows[:, :half], rows[:, half:])
        oth.ref[i] = jnp.where(first, rows[:, half:], rows[:, :half])
    own.send()
    oth.send()
    for part in range(3):
        wait_all(copies[2 * part : 2 * part + 2])
        for at in range(0, dim, 2 * LANES):
            cols = slice(at, at + 2 * LANES)
            res = (
                dot_nn(own.ref[0], buf[part, 0, :, cols])
                + dot_nn(oth.ref[0], buf[part, 1, :, cols])
                + bias_ref[:, part * dim + at : part * dim + at + 2 * LANES]
            )
            for i in range(2):
                vals = res[:, i * LANES : (i + 1) * LANES]
                if part < 2:
                    vals = rope(vals, tab_ref)
                out.ref[at // LANES + i, part] = vals.astype(bf16)


def layer_of(shape, index):
    return pl.BlockSpec((pl.squeezed,) + shape, lambda *args: (index, 0, 0))


HERE = pl.BlockSpec(memory_space=pltpu.VMEM)
SCALARS = pl.BlockSpec(memory_space=pltpu.SMEM)
ANYWHERE = pl.BlockSpec(memory_space=pl.ANY)
IN_HBM = pl.BlockSpec(memory_space=pltpu.HBM)


class Arriving:
    def __init__(self, buf, copy=None):
        self.buf, self.copy = buf, copy

    def ref(self):
        if self.copy is not None:
            self.copy.wait()
            self.copy = None
        return self.buf


class Leaving:
    def __init__(self, buf, copy=None):
        self.ref, self.copy, self.sent = buf, copy, copy is None

    def send(self):
        if not self.sent:
            self.copy.start()
            self.sent = True


def local_kernel(body, near_in, near_out, scalars, weights, followed, *refs):
    refs = list(refs)

    def take(number):
        taken = refs[:number]
        del refs[:number]
        return taken

    scalar_refs, array_refs = take(scalars), take(len(near_in))
    weight_refs, _, out_refs = take(weights), take(followed), take(len(near_out))
    in_sems, out_sems = take(2)
    inputs, outputs = [], []
    for i, (near, ref) in enumerate(zip(near_in, array_refs)):
        if near:
            inputs.append(Arriving(ref))
        else:
            buf = take(1)[0]
            copy = pltpu.make_async_copy(ref, buf, in_sems.at[i])
            copy.start()
            inputs.append(Arriving(buf, copy))
    for i, (near, ref) in enumerate(zip(near_out, out_refs)):
        if near:
            outputs.append(Leaving(ref))
        else:
            buf = take(1)[0]
            outputs.append(Leaving(buf, pltpu.make_async_copy(buf, ref, out_sems.at[i])))
    body(*scalar_refs, inputs, weight_refs, outputs, *refs)
    for item in inputs:
        item.ref()
    for item in outputs:
        item.send()
    for item in outputs:
        if item.copy is not None:
            item.copy.wait()


def far(array):
    return (array,)


def local_call(body, name, scalars, arrays, weights, out_shape, scratch=(), after=(), limit=VMEM_LIMIT):
    near_in = [not isinstance(a, tuple) for a in arrays]
    near_out = [not isinstance(o, tuple) for o in out_shape]
    raw_out = [isinstance(o, list) for o in out_shape]
    arrays = [a if near else a[0] for a, near in zip(arrays, near_in)]
    shapes = [o if near and not raw else o[0] for o, near, raw in zip(out_shape, near_out, raw_out)]
    far_bufs = [
        pltpu.VMEM(a.shape, a.dtype)
        for a, near in zip(arrays + shapes, near_in + near_out)
        if not near
    ]
    return pl.pallas_call(
        functools.partial(
            local_kernel, body, near_in, near_out, len(scalars), len(weights), len(after)
        ),
        in_specs=[SCALARS] * len(scalars)
        + [HERE if near else IN_HBM for near in near_in]
        + [IN_HBM] * len(weights)
        + [ANYWHERE] * len(after),
        out_specs=[HERE if near and not raw else IN_HBM for near, raw in zip(near_out, raw_out)],
        out_shape=shapes,
        scratch_shapes=[
            pltpu.SemaphoreType.DMA((len(arrays) + 1,)),
            pltpu.SemaphoreType.DMA((len(shapes),)),
        ]
        + far_bufs
        + list(scratch),
        name=name,
        **params_of(limit),
    )(*scalars, *arrays, *weights, *after)


def qkv_call(given, got, vecs, qkv_b, tab, w_own, w_oth, wsh):
    rows, dim = given.shape
    half = w_own.shape[0]
    pairs = dim // LANES
    return local_call(
        functools.partial(qkv_kernel, got is None),
        "qkv_proj",
        [wsh],
        [given, vecs, qkv_b, tab] if got is None else [given, vecs, qkv_b, tab, got],
        [w_own, w_oth],
        [shape_of((pairs, 3, rows, LANES), bf16), shape_of((rows, dim), bf16)]
        + [shape_of((2, rows, half), bf16)] * 2,
        [pltpu.VMEM((3, 2, half, dim), bf16), pltpu.SemaphoreType.DMA((3, 2))],
    )


FF_TILE = 1024
FF_PIECE = 512


def ff_tiles(wsh_ref, up_own, up_oth, dn_own, dn_oth, up_buf, dn_buf, sems):
    own = dn_own.shape[0] // FF_TILE
    tiles = []
    for t in range(2 * own):
        start = pl.multiple_of(((wsh_ref[0] * own + t) % (2 * own)) * FF_TILE, FF_TILE)
        cols = pl.ds(start, FF_TILE)
        down = (dn_own if t < own else dn_oth).at[pl.ds((t % own) * FF_TILE, FF_TILE)]
        copies = [
            pltpu.make_async_copy(up_own.at[:, cols], up_buf.at[t, 0], sems.at[t, 0]),
            pltpu.make_async_copy(up_oth.at[:, cols], up_buf.at[t, 1], sems.at[t, 1]),
            pltpu.make_async_copy(down, dn_buf.at[t], sems.at[t, 2]),
        ]
        tiles.append((t, start, start_all(copies)))
    for t, start, copies in tiles:
        wait_all(copies)
        for at in range(0, FF_TILE, FF_PIECE):
            row = (t % own) * FF_TILE + at
            place = pl.ds(pl.multiple_of(start + at, FF_PIECE), FF_PIECE)
            yield t, place, t < own, slice(row, row + FF_PIECE), slice(at, at + FF_PIECE)


def ff_scratch(half, ff, dim):
    tiles = ff // FF_TILE
    return [
        pltpu.VMEM((tiles, 2, half, FF_TILE), bf16),
        pltpu.VMEM((tiles, FF_TILE, dim), bf16),
        pltpu.SemaphoreType.DMA((tiles, 3)),
    ]


def mlp_kernel(save, wsh_ref, inputs, weights, outputs, up_buf, dn_buf, sems):
    out_ref = outputs[0].ref
    started = False
    for t, place, held, rows, piece in ff_tiles(wsh_ref, *weights, up_buf, dn_buf, sems):
        own_ref, oth_ref, up_b, down_b = (item.ref() for item in inputs)
        if not started:
            out_ref[...] = jnp.broadcast_to(down_b[...], out_ref.shape)
            started = True
        pre = (
            dot_nn(own_ref[1], up_buf[t, 0, :, piece])
            + dot_nn(oth_ref[1], up_buf[t, 1, :, piece])
            + up_b[:, place]
        )
        gate = 0.5 + 0.5 * lax.erf(pre * INV_SQRT2)
        act = (pre * gate).astype(bf16)
        if save:
            slope = gate + pre * (INV_SQRT_2PI * jnp.exp(-0.5 * pre * pre))
            outputs[1].ref[place] = slope.astype(bf16).T
            outputs[2 if held else 3].ref[rows] = act.T
            if not held:
                outputs[2].send()
        out_ref[...] += dot_nn(act, dn_buf[t, piece])


def mlp_call(own, oth, up_b, down_b, up_own, up_oth, dn_own, dn_oth, wsh, save):
    rows, half = own.shape[1:]
    dim = dn_own.shape[1]
    ff = up_own.shape[1]
    out_shape = [shape_of((rows, dim), f32)]
    if save:
        out_shape += [shape_of((ff, rows), bf16)]
        out_shape += [shape_of((ff // 2, rows), bf16)] * 2
    return local_call(
        functools.partial(mlp_kernel, save),
        "mlp_forward",
        [wsh],
        [own, oth, up_b, down_b],
        [up_own, up_oth, dn_own, dn_oth],
        out_shape,
        ff_scratch(half, ff, dim),
    )


def mlp_back_kernel(wsh_ref, inputs, weights, outputs, acc_own, acc_oth, up_buf, dn_buf, sems):
    du, dnm = outputs
    half = acc_own.shape[0]
    acc_own[...] = jnp.zeros(acc_own.shape, f32)
    acc_oth[...] = jnp.zeros(acc_oth.shape, f32)
    for t, place, _, _, piece in ff_tiles(wsh_ref, *weights, up_buf, dn_buf, sems):
        dy_ref, slope_ref = (item.ref() for item in inputs)
        dact = dot_nt(dn_buf[t, piece], dy_ref[...])
        vals = (dact * slope_ref[place].astype(f32)).astype(bf16)
        du.ref[place] = vals
        acc_own[...] += dot_nn(up_buf[t, 0, :, piece], vals)
        acc_oth[...] += dot_nn(up_buf[t, 1, :, piece], vals)
    du.send()
    first = wsh_ref[0] == 0
    dnm.ref[:, :half] = jnp.where(first, acc_own[...], acc_oth[...]).T
    dnm.ref[:, half:] = jnp.where(first, acc_oth[...], acc_own[...]).T


def mlp_back_call(dy, slope, up_own, up_oth, dn_own, dn_oth, wsh, after, limit):
    rows, dim = dy.shape
    half, ff = up_own.shape
    return local_call(
        mlp_back_kernel,
        "mlp_backward",
        [wsh],
        [dy, slope],
        [up_own, up_oth, dn_own, dn_oth],
        [shape_of(slope.shape, bf16), shape_of((rows, dim), f32)],
        [pltpu.VMEM((half, rows), f32), pltpu.VMEM((half, rows), f32)] + ff_scratch(half, ff, dim),
        after,
        limit,
    )


def sort_in(loc_ref, ref, dst, half_rows, part=None):
    for block in range(dst.shape[0] // half_rows):
        place = loc_ref[block]
        rows = pl.ds(pl.multiple_of((place % 2) * half_rows, half_rows), half_rows)
        if part is None:
            vals = ref[place // 2, rows, :]
        else:
            vals = ref[place // 2, part, rows, :]
        dst[block * half_rows : (block + 1) * half_rows] = vals


def sort_out(loc_ref, vals, ref, half_rows, part=None):
    for block in range(vals.shape[0] // half_rows):
        place = loc_ref[block]
        rows = pl.ds(pl.multiple_of((place % 2) * half_rows, half_rows), half_rows)
        piece = vals[block * half_rows : (block + 1) * half_rows]
        if part is None:
            ref[place // 2, rows, :] = piece
        else:
            ref[place // 2, part, rows, :] = piece


def head_of(vals, head):
    lane = lax.broadcasted_iota(jnp.int32, vals.shape, 1)
    return jnp.where(lane // (LANES // 2) == head, vals, jnp.zeros_like(vals))


def scores_of(keys, queries, scale, diagonal):
    scores = dot_nt(keys, queries) * scale
    if diagonal:
        key_at = lax.broadcasted_iota(jnp.int32, scores.shape, 0)
        query_at = lax.broadcasted_iota(jnp.int32, scores.shape, 1)
        scores = jnp.where(key_at <= query_at, scores, MASKED_SCORE)
    return scores


def attend_kernel(tile, loc_ref, inputs, weights, outputs, q_s, k_s, v_s, vt_s, o_s):
    qkv_ref = inputs[0].ref()
    o_ref, lse_ref = (item.ref for item in outputs)
    half_rows = qkv_ref.shape[2] // 2
    seq = q_s.shape[0]
    head_size = LANES // 2
    scale = head_size**-0.5
    sort_in(loc_ref, qkv_ref, q_s, half_rows, 0)
    sort_in(loc_ref, qkv_ref, k_s, half_rows, 1)
    sort_in(loc_ref, qkv_ref, v_s, half_rows, 2)
    vt_s[...] = v_s[...].T
    for t in range(seq // tile):
        rows = slice(t * tile, (t + 1) * tile)
        queries = q_s[rows]
        outs = []
        for head in range(2):
            picked = head_of(queries, head)
            parts = [
                scores_of(k_s[i * tile : (i + 1) * tile], picked, scale, i == t)
                for i in range(t + 1)
            ]
            top = functools.reduce(
                jnp.maximum, [jnp.max(p, axis=0, keepdims=True) for p in parts]
            )
            parts = [jnp.exp(p - top) for p in parts]
            total = sum(jnp.sum(p, axis=0, keepdims=True) for p in parts)
            lse_ref[head : head + 1, rows] = top + jnp.log(total)
            inverse = 1.0 / total
            acc = None
            for i, p in enumerate(parts):
                term = dot_nn(
                    vt_s[head * head_size : (head + 1) * head_size, i * tile : (i + 1) * tile],
                    (p * inverse).astype(bf16),
                )
                acc = term if acc is None else acc + term
            outs.append(acc)
        o_s[rows] = jnp.concatenate(outs, axis=0).T.astype(bf16)
    sort_out(loc_ref, o_s, o_ref, half_rows)


def attend_call(qkv, loc, after):
    count, _, rows, _ = qkv.shape
    seq = count * rows
    return local_call(
        functools.partial(attend_kernel, 256),
        "attention",
        [loc],
        [qkv],
        [],
        [shape_of((count, rows, LANES), bf16), shape_of((2, seq), f32)],
        [
            pltpu.VMEM((seq, LANES), bf16),
            pltpu.VMEM((seq, LANES), bf16),
            pltpu.VMEM((seq, LANES), bf16),
            pltpu.VMEM((LANES, seq), bf16),
            pltpu.VMEM((seq, LANES), bf16),
        ],
        after,
    )


def attend_back_kernel(
    tile, part, loc_ref, inputs, weights, outputs, q_s, k_s, v_s, da_s, kt_s, dq_s, dk_s, dv_s
):
    da_ref, qkv_ref, lse_ref = (item.ref() for item in inputs)
    out_ref = outputs[0].ref
    half_rows = qkv_ref.shape[2] // 2
    seq = q_s.shape[0]
    head_size = LANES // 2
    scale = head_size**-0.5
    sort_in(loc_ref, qkv_ref, q_s, half_rows, 0)
    sort_in(loc_ref, qkv_ref, k_s, half_rows, 1)
    sort_in(loc_ref, qkv_ref, v_s, half_rows, 2)
    sort_in(loc_ref, da_ref, da_s, half_rows, part)
    kt_s[...] = k_s[...].T
    dk_s[...] = jnp.zeros(dk_s.shape, f32)
    dv_s[...] = jnp.zeros(dv_s.shape, f32)
    for t in range(seq // tile):
        rows = slice(t * tile, (t + 1) * tile)
        outs = []
        for head in range(2):
            queries = head_of(q_s[rows], head)
            grads = head_of(da_s[rows], head)
            lse = lse_ref[head : head + 1, rows]
            probs, dprobs, row_dot = [], [], 0.0
            for i in range(t + 1):
                keys = slice(i * tile, (i + 1) * tile)
                p = jnp.exp(scores_of(k_s[keys], queries, scale, i == t) - lse)
                dp = dot_nt(v_s[keys], grads)
                row_dot = row_dot + jnp.sum(p * dp, axis=0, keepdims=True)
                dv_s[keys] += dot_nn(p.astype(bf16), grads)
                probs.append(p)
                dprobs.append(dp)
            acc = None
            for i in range(t + 1):
                keys = slice(i * tile, (i + 1) * tile)
                ds = (probs[i] * (dprobs[i] - row_dot) * scale).astype(bf16)
                dk_s[keys] += dot_nn(ds, queries)
                term = dot_nn(kt_s[head * head_size : (head + 1) * head_size, keys], ds)
                acc = term if acc is None else acc + term
            outs.append(acc)
        dq_s[rows] = jnp.concatenate(outs, axis=0).T.astype(bf16)
    sort_out(loc_ref, dq_s, out_ref, half_rows, 0)
    k_s[...] = dk_s[...].astype(bf16)
    v_s[...] = dv_s[...].astype(bf16)
    sort_out(loc_ref, k_s, out_ref, half_rows, 1)
    sort_out(loc_ref, v_s, out_ref, half_rows, 2)


def attend_back_call(qkv, da, lse, loc, after, limit):
    count, _, rows, _ = qkv.shape
    seq = count * rows
    part = 0 if da.ndim == 4 else None
    (res,) = local_call(
        functools.partial(attend_back_kernel, 256, part),
        "attention_backward",
        [loc],
        [da, qkv, lse],
        [],
        [shape_of(qkv.shape, bf16)],
        [pltpu.VMEM((seq, LANES), bf16)] * 4
        + [pltpu.VMEM((LANES, seq), bf16), pltpu.VMEM((seq, LANES), bf16)]
        + [pltpu.VMEM((seq, LANES), f32)] * 2,
        after,
        limit,
    )
    return res


def by_head(parts):
    pairs, rows, lanes = parts.shape
    return jnp.transpose(parts, (1, 0, 2)).reshape(rows, HEADS, pairs * lanes // HEADS)


def by_pair(heads):
    rows = heads.shape[0]
    return jnp.transpose(heads.reshape(rows, -1, LANES), (1, 0, 2))


def wide_scores(queries, keys, query_pos, key_pos):
    raw = jnp.einsum("qhd,khd->hqk", queries, keys, preferred_element_type=f32)
    allowed = (query_pos[:, None] >= key_pos[None, :])[None]
    return jnp.where(allowed, raw * queries.shape[-1] ** (-0.5), MASKED_SCORE)


def key_blocks(arrays, rows):
    return tuple(a.reshape((a.shape[0] // rows, rows) + a.shape[1:]) for a in arrays)


def wide_attend(qkv, query_pos, key_pos):
    queries = by_head(qkv[:, 0])
    keys = lax.all_gather(by_head(qkv[:, 1]), "ctx", axis=0, tiled=True)
    values = lax.all_gather(by_head(qkv[:, 2]), "ctx", axis=0, tiled=True)
    block = min(512, keys.shape[0])
    split = key_blocks((keys, values, key_pos), block)
    rows, _, head_size = queries.shape

    def max_step(carry, block_in):
        top, total = carry
        scores = wide_scores(queries, block_in[0], query_pos, block_in[2])
        new_top = jnp.maximum(top, jnp.max(scores, axis=-1))
        part = jnp.sum(jnp.exp(scores - new_top[..., None]), axis=-1)
        return ((new_top, total * jnp.exp(top - new_top) + part), None)

    start = (jnp.full((HEADS, rows), MASKED_SCORE, f32), jnp.zeros((HEADS, rows), f32))
    (top, total), _ = lax.scan(max_step, start, split)
    lse = top + jnp.log(total)

    def value_step(running, block_in):
        scores = wide_scores(queries, block_in[0], query_pos, block_in[2])
        probs = jnp.exp(scores - lse[..., None]).astype(bf16)
        term = jnp.einsum("hqk,khd->qhd", probs, block_in[1], preferred_element_type=f32)
        return (running + term, None)

    attended, _ = lax.scan(value_step, jnp.zeros((rows, HEADS, head_size), f32), split)
    return by_pair(attended.astype(bf16)), (queries, keys, values, lse)


def wide_attend_back(kept, da, query_pos, key_pos):
    queries, keys, values, lse = kept
    grads = by_head(da)
    block = min(512, keys.shape[0])
    split = key_blocks((keys, values, key_pos), block)
    scale = queries.shape[-1] ** (-0.5)

    def pieces(block_in):
        scores = wide_scores(queries, block_in[0], query_pos, block_in[2])
        probs = jnp.exp(scores - lse[..., None])
        dprobs = jnp.einsum("qhd,khd->hqk", grads, block_in[1], preferred_element_type=f32)
        return probs, dprobs

    def dot_step(running, block_in):
        probs, dprobs = pieces(block_in)
        return (running + jnp.sum(probs * dprobs, axis=-1), None)

    row_dot, _ = lax.scan(dot_step, jnp.zeros(lse.shape, f32), split)

    def key_step(running, block_in):
        probs, dprobs = pieces(block_in)
        ds = (scale * probs * (dprobs - row_dot[..., None])).astype(bf16)
        running = running + jnp.einsum("hqk,khd->qhd", ds, block_in[0], preferred_element_type=f32)
        dk = jnp.einsum("hqk,qhd->khd", ds, queries, preferred_element_type=f32)
        dv = jnp.einsum("hqk,qhd->khd", probs.astype(bf16), grads, preferred_element_type=f32)
        return (running, (dk.astype(bf16), dv.astype(bf16)))

    dq, (dk, dv) = lax.scan(key_step, jnp.zeros(queries.shape, f32), split)
    dk, dv = (
        lax.psum_scatter(part.reshape(keys.shape), "ctx", scatter_dimension=0, tiled=True)
        for part in (dk, dv)
    )
    return jnp.stack([by_pair(dq.astype(bf16)), by_pair(dk), by_pair(dv)], axis=1)


def lanes_of(ref):
    return jnp.concatenate([ref[i] for i in range(ref.shape[0])], axis=1)


def both_halves(w_own, w_oth, buf, sems):
    return start_all(
        [
            pltpu.make_async_copy(weight, buf.at[side], sems.at[side])
            for side, weight in enumerate((w_own, w_oth))
        ]
    )


def half_scratch(weight):
    return [pltpu.VMEM((2,) + weight.shape, bf16), pltpu.SemaphoreType.DMA((2,))]


def proj_kernel(part, wsh_ref, inputs, weights, outputs, buf, sems):
    copies = both_halves(*weights, buf, sems)
    y, own, oth = outputs
    half = buf.shape[1]
    first = wsh_ref[0] == 0
    a_ref = inputs[0].ref()
    a = lanes_of(a_ref if part is None else a_ref.at[:, part])
    own.ref[...] = jnp.where(first, a[:, :half], a[:, half:])
    oth.ref[...] = jnp.where(first, a[:, half:], a[:, :half])
    own.send()
    oth.send()
    bias_ref, x_ref, mlp_ref = (item.ref() for item in inputs[1:])
    wait_all(copies)
    attn = dot_nn(own.ref[...], buf[0]) + dot_nn(oth.ref[...], buf[1]) + bias_ref[...]
    y.ref[...] = (x_ref[...].astype(f32) + attn + mlp_ref[...]).astype(bf16)


def proj_call(a, x, mlp, bias, p_own, p_oth, wsh, after, limit):
    rows, dim = x.shape
    half = p_own.shape[0]
    return local_call(
        functools.partial(proj_kernel, 1 if a.ndim == 4 else None),
        "attn_out",
        [wsh],
        [a, bias, x, mlp],
        [p_own, p_oth],
        [shape_of((rows, dim), bf16)] + [shape_of((rows, half), bf16)] * 2,
        half_scratch(p_own),
        after,
        limit,
    )


def da_kernel(own_given, wsh_ref, inputs, weights, outputs, buf, sems):
    copies = both_halves(*weights, buf, sems)
    out_ref, dy_out = outputs[0].ref, outputs[1]
    dy = inputs[0].ref()[...]
    if not own_given:
        dy = jnp.where(wsh_ref[1] == 1, inputs[1].ref()[...], dy)
    dy_out.ref[...] = dy
    dy_out.send()
    wsh = wsh_ref[0]
    joined = len(out_ref.shape) == 4
    if joined:
        out_ref[:, 1] = inputs[2].ref()[...]
    count = out_ref.shape[0] // 2
    for place, side in ((wsh * count, 0), ((1 - wsh) * count, 1)):
        copies[side].wait()
        part = dot_nt(dy, buf[side]).astype(bf16)
        for i in range(count):
            vals = part[:, i * LANES : (i + 1) * LANES]
            if joined:
                out_ref[place + i, 0] = vals
            else:
                out_ref[place + i] = vals


def da_call(given, got, p_own, p_oth, wsh, joined=None):
    rows, dim = given.shape
    pairs = dim // LANES
    arrays = [given] + ([] if got is None else [got])
    arrays += [] if joined is None else [joined]
    shape = (pairs, rows, LANES) if joined is None else (pairs, 2, rows, LANES)
    return local_call(
        functools.partial(da_kernel, got is None),
        "attn_out_backward",
        [wsh],
        arrays,
        [p_own, p_oth],
        [shape_of(shape, bf16), shape_of((rows, dim), bf16)],
        half_scratch(p_own),
    )


def dx_kernel(wsh_ref, inputs, weights, outputs, grad_s, buf, sems):
    copies = both_halves(*weights, buf, sems)
    back, dx, sums = outputs
    dqkv_ref, tab_ref = inputs[0].ref(), inputs[1].ref()
    pairs = dqkv_ref.shape[0]
    for part in range(3):
        for pair in range(pairs):
            vals = dqkv_ref[pair, part]
            if part < 2:
                vals = unrope(vals.astype(f32), tab_ref).astype(bf16)
            back.ref[pair, part] = vals
            grad_s[:, pl.ds((part * pairs + pair) * LANES, LANES)] = vals
    back.send()
    vec_ref, x_ref, dy_ref, dnm_ref = (item.ref() for item in inputs[2:])
    first = wsh_ref[0] == 0
    copies[0].wait()
    own = dot_nt(grad_s[...], buf[0])
    copies[1].wait()
    oth = dot_nt(grad_s[...], buf[1])
    dna = jnp.concatenate([jnp.where(first, own, oth), jnp.where(first, oth, own)], axis=1)
    dnm = dnm_ref[...]
    xhat, scale = normalized(x_ref[...].astype(f32))
    grad = dna * vec_ref[0:1] + dnm * vec_ref[2:3]
    inner = (
        grad
        - jnp.mean(grad, axis=-1, keepdims=True)
        - xhat * jnp.mean(grad * xhat, axis=-1, keepdims=True)
    )
    dx.ref[...] = (dy_ref[...].astype(f32) + scale * inner).astype(bf16)
    dx.send()
    sums.ref[0:1] = jnp.sum(dna * xhat, axis=0, keepdims=True)
    sums.ref[1:2] = jnp.sum(dna, axis=0, keepdims=True)
    sums.ref[2:3] = jnp.sum(dnm * xhat, axis=0, keepdims=True)
    sums.ref[3:4] = jnp.sum(dnm, axis=0, keepdims=True)


def dx_call(dqkv, tab, x, dy, dnm, vecs, w_own, w_oth, wsh, after, limit):
    rows, dim = x.shape
    return local_call(
        dx_kernel,
        "section_input_grad",
        [wsh],
        [dqkv, tab, vecs, x, dy, dnm],
        [w_own, w_oth],
        [shape_of(o, t) for o, t in ((dqkv.shape, bf16), ((rows, dim), bf16), ((4, dim), f32))],
        [pltpu.VMEM((rows, 3 * dim), bf16)] + half_scratch(w_own),
        after,
        limit,
    )


def joined_rows(items):
    return jnp.concatenate([item.ref()[...] for item in items], axis=0)


class Pieces:
    def __init__(self, out_ref, buf, sems):
        self.out_ref, self.buf, self.sems, self.copies = out_ref, buf, sems, []

    def put(self, rows, cols, vals):
        self.buf[rows, cols] = vals.astype(bf16)
        at = len(self.copies)
        self.copies.append(
            pltpu.make_async_copy(
                self.buf.at[rows, cols], self.out_ref.at[rows, cols], self.sems.at[at]
            )
        )
        self.copies[-1].start()

    def finish(self, chunk, ahead, behind):
        height, cut = ahead.ref.shape
        rows = pl.ds(pl.multiple_of(chunk * height, height), height)
        ahead.ref[...] = self.buf[rows, :cut]
        ahead.send()
        behind.ref[...] = self.buf[rows, cut:]
        behind.send()
        wait_all(self.copies)


def grad_call(body, name, idx, arrays, shape, width, count, scratch, after):
    halves = shape_of((shape[0] // count, shape[1] // 2), bf16)
    return local_call(
        functools.partial(body, len(arrays)),
        name,
        [idx],
        arrays,
        [],
        [[shape_of(shape, bf16)], far(halves), far(halves), far(shape_of((1, width), f32))],
        [pltpu.VMEM(shape, bf16), pltpu.SemaphoreType.DMA((4,))] + scratch,
        after,
        TAIL_LIMIT,
    )


def parts_of(items, number):
    size = len(items) // number
    return [items[i * size : (i + 1) * size] for i in range(number)]


def down_grad_kernel(number, idx_ref, inputs, weights, outputs, buf, sems):
    gts, dys = parts_of(inputs, 2)
    out = Pieces(outputs[0].ref, buf, sems)
    dy = joined_rows(dys)
    outputs[3].ref[...] = jnp.sum(dy.astype(f32), axis=0, keepdims=True)
    rows, dim = buf.shape
    tile = rows // 4
    for t in range(4):
        part = slice(t * tile, (t + 1) * tile)
        left = jnp.concatenate([item.ref()[part] for item in gts], axis=1)
        out.put(part, slice(0, dim), dot_nn(left, dy))
    out.finish(idx_ref[idx_ref.shape[0] // 2], outputs[1], outputs[2])


def down_grad_call(idx, gt_list, dy_list, count):
    dim = dy_list[0].shape[1]
    return grad_call(
        down_grad_kernel,
        "down_grad",
        idx,
        [far(a) for a in gt_list + dy_list],
        (gt_list[0].shape[0], dim),
        dim,
        count,
        [],
        [],
    )


def up_grad_kernel(number, idx_ref, inputs, weights, outputs, buf, sems):
    norms, dus = parts_of(inputs, 2)
    out = Pieces(outputs[0].ref, buf, sems)
    left = jnp.concatenate([item.ref()[1] for item in norms], axis=0).T
    rows, ff = buf.shape
    tile = ff // 4
    for t in range(4):
        part = slice(t * tile, (t + 1) * tile)
        du = jnp.concatenate([item.ref()[part] for item in dus], axis=1)
        outputs[3].ref[:, part] = dot_nt(jnp.ones((8, du.shape[1]), bf16), du)[:1]
        out.put(slice(0, rows), part, dot_nt(left, du))
    out.finish(idx_ref[idx_ref.shape[0] // 2], outputs[1], outputs[2])


def up_grad_call(idx, norm_list, du_list, count, after):
    half, ff = norm_list[0].shape[2], du_list[0].shape[0]
    return grad_call(
        up_grad_kernel,
        "up_grad",
        idx,
        [far(a) for a in norm_list + du_list],
        (half, ff),
        ff,
        count,
        [],
        after,
    )


def attn_grad_kernel(number, idx_ref, inputs, weights, outputs, buf, sems):
    norms, outs, dqkvs, dys = parts_of(inputs, 4)
    out = Pieces(outputs[0].ref, buf, sems)
    rows, width = buf.shape
    dim = width // 4
    left = jnp.concatenate([item.ref()[0] for item in norms], axis=0).T
    for part in range(4):
        cols = slice(part * dim, (part + 1) * dim)
        if part < 3:
            right = jnp.concatenate([lanes_of(item.ref().at[:, part]) for item in dqkvs], axis=0)
        else:
            left, right = joined_rows(outs).T, joined_rows(dys)
        outputs[3].ref[:, cols] = jnp.sum(right.astype(f32), axis=0, keepdims=True)
        out.put(slice(0, rows), cols, dot_nn(left, right))
    out.finish(idx_ref[idx_ref.shape[0] // 2], outputs[1], outputs[2])


def attn_grad_call(idx, norm_list, out_list, dqkv_list, dy_list, count, after):
    half, dim = norm_list[0].shape[2], dy_list[0].shape[1]
    return grad_call(
        attn_grad_kernel,
        "attn_grad",
        idx,
        [far(a) for a in norm_list + out_list + dqkv_list + dy_list],
        (half, 4 * dim),
        4 * dim,
        count,
        [],
        after,
    )


def ring_of(count):
    return list(range(0, count, 2)) + list(range(count - 1, 0, -2))


def ring_place(axis):
    count = lax.axis_size(axis)
    me = lax.axis_index(axis)
    return jnp.where(me % 2 == 0, me // 2, count - (me + 1) // 2)


def ring_index(axis):
    count = lax.axis_size(axis)
    return (ring_place(axis) + jnp.arange(count, dtype=jnp.int32)) % count


def ring_shift(vals, axis, by):
    order = ring_of(lax.axis_size(axis))
    count = len(order)
    pairs = [(order[i], order[(i + by) % count]) for i in range(count)]
    return lax.ppermute(vals, axis, pairs)


def tied(token, *vals):
    return lax.optimization_barrier((token, vals))[1]


def fetch(idx_ref, slots, own_ref, bufs, sems):
    return start_all(
        [
            pltpu.make_async_copy(own_ref.at[idx_ref[slot]], bufs.at[i], sems.at[i])
            for i, slot in enumerate(slots)
        ]
    )


def low_total(*terms):
    total = terms[0].astype(f32)
    for term in terms[1:]:
        total = total + term.astype(f32)
    return total.astype(bf16)


def ring_add_kernel(slots, idx_ref, inputs, own_refs, outputs, bufs, sems):
    copies = fetch(idx_ref, slots, own_refs[0], bufs, sems)
    for i, item in enumerate(outputs):
        copies[i].wait()
        got = inputs[i].ref()
        cols, cut = item.ref.shape[1], got.shape[1]
        summed = slice(0, cut) if i == 0 else slice(cols - cut, cols)
        item.ref[:, summed] = low_total(bufs[i, :, summed], got[...])
        if cut < cols:
            rest = slice(cut, cols) if i == 0 else slice(0, cols - cut)
            item.ref[:, rest] = bufs[i, :, rest]
        item.send()


def put_copies(chunk, cols, buf, totals, starts, sem):
    lo, hi = cols, cols + buf.shape[1]
    copies = []
    for i, (total, start) in enumerate(zip(totals, starts)):
        first, last = max(lo, start), min(hi, start + total.shape[2])
        if first < last:
            copies.append(
                pltpu.make_async_copy(
                    buf.at[:, pl.ds(first - lo, last - first)],
                    total.at[chunk, :, pl.ds(first - start, last - first)],
                    sem.at[i],
                )
            )
    return copies


def ring_own_kernel(slots, idx_ref, inputs, own_refs, outputs, bufs, sems):
    wait_all(fetch(idx_ref, slots, own_refs[0], bufs, sems))
    outputs[0].ref[...] = low_total(bufs[0], inputs[0].ref()[...], inputs[1].ref()[...])


def ring_put_kernel(starts, slots, cols, fresh, onward, idx_ref, *refs):
    number = len(slots)
    pieces = refs[:number]
    wide, sems, pass_buf, pass_sems = refs[-4:]
    passed = refs[-4 - onward : -4]
    totals = refs[-4 - onward - len(starts) : -4 - onward]
    leaving = []
    for i, ref in enumerate(passed):
        width = ref.shape[1]
        pass_buf[i, :, :width] = pieces[i][:, :width] if i == 0 else pieces[i][:, -width:]
        leaving += start_all(
            [pltpu.make_async_copy(pass_buf.at[i, :, pl.ds(0, width)], ref, pass_sems.at[i])]
        )
    for i in range(number):
        wide[i] = pieces[i][...].astype(f32)
        leaving += start_all(
            put_copies(idx_ref[slots[i]], cols[i], wide.at[i], totals, starts, sems.at[i])
        )
    wait_all(leaving)


def ring_sum(own, ahead, behind, widths, axis):
    count = lax.axis_size(axis)
    half = count // 2
    full_rows, cols = own.shape
    rows = full_rows // count
    own = own.reshape(count, rows, cols)
    cut = cols // 2
    starts = [sum(widths[:i]) for i in range(len(widths))]
    idx = ring_index(axis)
    chunk, piece = shape_of((rows, cols), bf16), shape_of((rows, cut), bf16)
    sums = [shape_of((count, rows, width), f32) for width in widths]

    def taken(number):
        return [pltpu.VMEM((number, rows, cols), bf16), pltpu.SemaphoreType.DMA((number,))]

    def put(totals, pieces, slots, passed, after):
        number, width = len(pieces), pieces[0].shape[1]
        first_cols = (0,) * number if width == cols else (0, cut)
        fresh = totals is None
        out = pl.pallas_call(
            functools.partial(
                ring_put_kernel,
                starts,
                tuple(k % count for k in slots),
                first_cols,
                fresh,
                len(passed),
            ),
            in_specs=[SCALARS]
            + [HERE] * number
            + [IN_HBM] * (0 if fresh else len(sums))
            + [ANYWHERE] * len(after),
            out_specs=[IN_HBM] * (len(sums) + len(passed)),
            out_shape=sums + passed,
            scratch_shapes=[
                pltpu.VMEM((number, rows, width), f32),
                pltpu.SemaphoreType.DMA((number, len(sums))),
                pltpu.VMEM((2, rows, cols), bf16),
                pltpu.SemaphoreType.DMA((2,)),
            ],
            input_output_aliases={} if fresh else {1 + number + i: i for i in range(len(sums))},
            name="ring_put",
            **params_of(RING_LIMIT),
        )(idx, *pieces, *([] if fresh else totals), *after)
        return out[: len(sums)], out[len(sums) :]

    def both_ways(ahead, behind):
        return ring_shift(ahead, axis, 1), ring_shift(behind, axis, -1)

    token = behind
    ahead, behind = both_ways(ahead, behind)
    token = yield token
    for k in range(half - 1, 0, -1):
        ahead, behind = local_call(
            functools.partial(ring_add_kernel, (k % count, (-k) % count)),
            "ring_add",
            [idx],
            [ahead, behind],
            [own],
            [chunk, chunk],
            taken(2),
            [token],
            RING_LIMIT,
        )
        token = behind
        ahead, behind = both_ways(ahead, behind)
        token = yield token
    (mine,) = local_call(
        functools.partial(ring_own_kernel, (0,)),
        "ring_own",
        [idx],
        [ahead, behind],
        [own],
        [chunk],
        taken(1),
        [token],
        RING_LIMIT,
    )
    ahead, behind = both_ways(mine, mine)
    totals, (token,) = put(None, [mine], [0], [shape_of((rows, LANES), bf16)], [])
    token = yield token
    for k in range(1, half):
        passed = [piece if k == half - 1 else chunk] * 2
        totals, passed = put(totals, [ahead, behind], [-k, k], passed, [token])
        token = passed[1]
        ahead, behind = both_ways(*passed)
        token = yield token
    totals, _ = put(totals, [ahead, behind], [-half, half], [], [token])
    yield [total.reshape(full_rows, -1) for total in totals]


def add_kernel(inputs, weights, outputs):
    outputs[0].ref[...] = inputs[0].ref()[...] + inputs[1].ref()[...]


def butterfly_sum(vals, axis):
    count = lax.axis_size(axis)
    by = 1
    token = yield None
    if count & (count - 1):
        yield lax.psum(vals, axis)
        return
    while by < count:
        got = lax.ppermute(vals, axis, [(i, i ^ by) for i in range(count)])
        token = yield None
        (vals,) = local_call(
            add_kernel, "small_add", [], [vals, got], [], [shape_of(vals.shape, f32)], [], [token]
        )
        by *= 2
    yield vals


def swap(vals):
    return lax.ppermute(vals, "wsh", [(0, 1), (1, 0)])


def pass_on(vals, by):
    pairs = [(0, 1)] if by > 0 else [(1, 0)]
    return lax.ppermute(vals, "section", pairs)


def block_places(block_pair, count):
    want = jnp.arange(2 * count, dtype=jnp.int32)
    device = jnp.arange(count, dtype=jnp.int32)
    first = (block_pair[None, :] == want[:, None]).astype(jnp.int32)
    second = ((2 * count - 1 - block_pair)[None, :] == want[:, None]).astype(jnp.int32)
    return jnp.sum(first * (2 * device) + second * (2 * device + 1), axis=1)


def row_positions(block_pair, stored, tok_dev):
    count = block_pair.shape[0]
    device = stored // tok_dev
    within = stored % tok_dev
    half_rows = tok_dev // 2
    matches = device[:, None] == jnp.arange(count, dtype=jnp.int32)[None, :]
    pair_block = jnp.sum(jnp.where(matches, block_pair[None, :], 0), axis=1)
    block_idx = jnp.where(within < half_rows, pair_block, 2 * count - 1 - pair_block)
    return block_idx * half_rows + within % half_rows


def rotary_table(positions, head_size):
    half_rot = ROT // 2
    lane = jnp.arange(LANES, dtype=jnp.int32) % head_size
    inv_freq = ROPE_BASE ** (-((lane % half_rot).astype(f32) * 2.0) / ROT)
    angles = positions.astype(f32)[:, None] * inv_freq[None, :]
    cosine, sine = jnp.cos(angles), jnp.sin(angles)
    lead, second = (lane < half_rot)[None], ((lane >= half_rot) & (lane < ROT))[None]
    return jnp.stack(
        [
            jnp.where(lead | second, cosine, 1.0),
            jnp.where(lead, -sine, 0.0),
            jnp.where(second, sine, 0.0),
        ]
    )


def body(
    inputs,
    cotangent,
    block_pair,
    qkv_weight,
    qkv_bias,
    proj_weight,
    proj_bias,
    up_weight,
    up_bias,
    down_weight,
    down_bias,
    attn_gain,
    attn_shift,
    mlp_gain,
    mlp_shift,
):
    first_section = lax.axis_index("section") == 0
    count = lax.axis_size("ctx")
    micros, _, tok_dev, dim = inputs.shape
    head_size = dim // HEADS
    half = dim // 2
    my_half = lax.axis_index("wsh")
    wsh = jnp.stack([my_half.astype(jnp.int32), first_section.astype(jnp.int32)])
    one_pair_each = count == dim // LANES

    wq, wp, wu, wd = (w[0] for w in (qkv_weight, proj_weight, up_weight, down_weight))
    small = jnp.concatenate(
        [
            v[0].reshape(-1, half)
            for v in (
                attn_gain,
                attn_shift,
                mlp_gain,
                mlp_shift,
                proj_bias,
                down_bias,
                qkv_bias,
                up_bias,
            )
        ],
        axis=0,
    )
    small_oth = swap(small)
    wq_oth = swap(wq)
    first_here = lax.optimization_barrier((wq_oth, small_oth))
    wq_oth, small_oth = first_here
    wu_oth = swap(tied(wq_oth, wu)[0])
    wd_oth = swap(tied(wq_oth, wd)[0])
    wp_oth = swap(tied(wu_oth, wp)[0])
    low_part = jnp.where(my_half == 0, small, small_oth).astype(f32)
    high_part = jnp.where(my_half == 0, small_oth, small).astype(f32)
    vecs = jnp.concatenate([low_part[:6], high_part[:6]], axis=1)
    qkv_rows = 6 + qkv_bias.shape[1] // half
    proj_b, down_b = vecs[4:5], vecs[5:6]
    qkv_b = jnp.concatenate([low_part[6:qkv_rows], high_part[6:qkv_rows]], axis=0).reshape(1, -1)
    up_b = jnp.concatenate([low_part[qkv_rows:], high_part[qkv_rows:]], axis=0).reshape(1, -1)

    local_rows = lax.axis_index("ctx") * tok_dev + jnp.arange(tok_dev, dtype=jnp.int32)
    query_pos = row_positions(block_pair, local_rows, tok_dev)
    key_pos = row_positions(block_pair, jnp.arange(count * tok_dev, dtype=jnp.int32), tok_dev)
    tab = rotary_table(query_pos, head_size)
    loc = block_places(block_pair, count)

    def exchange(vals):
        return lax.all_to_all(vals, "ctx", split_axis=0, concat_axis=0, tiled=True)

    rows_in = [inputs[i, 0] for i in range(micros)]
    cot_in = [cotangent[i, 0] for i in range(micros)]

    def norm_qkv(index, got):
        return qkv_call(rows_in[index], got, vecs, qkv_b, tab, wq, wq_oth, wsh)

    def mlp(made, save):
        return mlp_call(made[2], made[3], up_b, down_b, wu, wu_oth, wd, wd_oth, wsh, save)

    def mlp_back(dy, mlp_kept, after=(), limit=VMEM_LIMIT):
        return mlp_back_call(dy, mlp_kept[1], wu, wu_oth, wd, wd_oth, wsh, after, limit)

    def out_back(index, got, joined=None):
        return da_call(cot_in[index], got, wp, wp_oth, wsh, joined)

    def moved(vals):
        return exchange(vals) if one_pair_each else vals

    def attend(qkv, after=()):
        if one_pair_each:
            attended, lse = attend_call(qkv, loc, after)
            return attended, (qkv, lse)
        return wide_attend(qkv, query_pos, key_pos)

    def attend_back(kept, da, after=(), limit=VMEM_LIMIT):
        if one_pair_each:
            return attend_back_call(kept[0], da, kept[1], loc, after, limit)
        da = da[:, 0] if da.ndim == 4 else da
        return wide_attend_back(kept, da, query_pos, key_pos)

    def project(attended, made, mlp_out, after=(), limit=VMEM_LIMIT):
        return proj_call(attended, made[1], mlp_out[0], proj_b, wp, wp_oth, wsh, after, limit)

    def input_grad_of(dqkv, made, dy, dnm, after=(), limit=VMEM_LIMIT):
        return dx_call(dqkv, tab, made[1], dy, dnm, vecs, wq, wq_oth, wsh, after, limit)

    made_a = norm_qkv(0, None)
    qkv_a = moved(made_a[0])
    mlp_a = mlp(made_a, False)
    att_a, _ = attend(qkv_a, [mlp_a[0]])
    att_a = moved(att_a)
    da_a, dy_a = out_back(0, None)
    y_a = project(att_a, made_a, mlp_a, [dy_a])[0]
    da_a = moved(tied(y_a, da_a)[0])

    made_b = norm_qkv(1, pass_on(y_a, 1))
    qkv_2 = moved(tied(da_a, made_b[0])[0])
    norms_b = swap(made_b[3])
    mlp_b = mlp(made_b, True)
    _, dnm_a = mlp_back(dy_a, mlp_b)
    att_b, kept_b = attend(qkv_2, [dnm_a, norms_b])
    att_b = moved(att_b)
    gt_b = swap(mlp_b[3])
    dqkv_a_ = attend_back(kept_b, da_a, [gt_b])
    dqkv_a = moved(dqkv_a_)
    y_b, *a_b = project(att_b, made_b, mlp_b, [dqkv_a_])

    made_c = norm_qkv(0, pass_on(y_b, 1))
    qkv_3 = moved(tied(dqkv_a, made_c[0])[0])
    norms_c = swap(made_c[3])
    a_b_oth = swap(a_b[1])
    _, dx_a, _ = input_grad_of(dqkv_a, made_b, dy_a, dnm_a, [norms_c, a_b_oth])
    got_a = pass_on(dx_a, -1)
    mlp_c = mlp_call(
        made_c[2], tied(dx_a, made_c[3])[0], up_b, down_b, wu, wu_oth, wd, wd_oth, wsh, True
    )
    da_b, dy_b = out_back(1, tied(mlp_c[0], got_a)[0])
    da_b = moved(tied(qkv_3, da_b)[0])
    att_c, kept_c = attend(qkv_3, [dy_b])
    dy_b_oth, gt_c = swap(dy_b), swap(mlp_c[3])
    dqkv_b = attend_back(kept_c, da_b, [dy_b_oth, gt_c])
    dqkv_b_ = moved(dqkv_b)
    du_b, dnm_b = mlp_back(dy_b, mlp_c, [dqkv_b])
    du_b_oth = swap(du_b)
    back_b, dx_b, sums_b = input_grad_of(dqkv_b_, made_c, dy_b, dnm_b, [du_b_oth])
    got_b = pass_on(dx_b, -1)
    back_b_oth = swap(back_b)

    da_c, dy_c = out_back(0, tied(back_b_oth, got_b)[0], att_c if one_pair_each else None)
    dy_list = [dy_c, dy_b, swap(dy_c), dy_b_oth]
    da_c = moved(da_c)
    idx = ring_index("ctx")
    *down_made, dy_sum = down_grad_call(idx, [mlp_b[2], mlp_c[2], gt_b, gt_c], dy_list, count)
    down_ring = ring_sum(*down_made, (dim,), "ctx")
    token = next(down_ring)
    token = down_ring.send(token)
    du_c, dnm_c = mlp_back(dy_c, mlp_b, [token], TAIL_LIMIT)
    dqkv_c = attend_back(kept_b, da_c, [dnm_c], TAIL_LIMIT)
    token = down_ring.send(dqkv_c)
    dqkv_c = moved(dqkv_c)
    *up_made, du_sum = up_grad_call(
        idx,
        [made_b[2], made_c[2], norms_b, norms_c],
        [du_c, du_b, swap(du_c), du_b_oth],
        count,
        [token],
    )
    up_ring = ring_sum(*up_made, (up_made[0].shape[1],), "ctx")
    token = next(up_ring)
    steps = count + 1
    left = {down_ring: steps - 3, up_ring: steps - 1}
    results = {}

    def turn(ring, token):
        if not left[ring]:
            return token
        left[ring] -= 1
        made = ring.send(token)
        if left[ring] == 0:
            results[ring] = made
            return token
        return made

    token = turn(down_ring, token)
    token = turn(up_ring, token)
    back_c, dx_c, sums_c = input_grad_of(dqkv_c, made_b, dy_c, dnm_c, [token], TAIL_LIMIT)
    back_c_oth = swap(back_c)
    token = turn(down_ring, dx_c)
    y_c, *a_c = project(da_c if one_pair_each else att_c, made_c, mlp_c, [token], TAIL_LIMIT)
    a_c_oth = swap(a_c[1])
    token = turn(up_ring, y_c)
    token = turn(down_ring, token)
    *attn_made, attn_sum = attn_grad_call(
        idx,
        [made_b[2], made_c[2], norms_b, norms_c],
        [a_b[0], a_c[0], a_b_oth, a_c_oth],
        [back_c, back_b, back_c_oth, back_b_oth],
        dy_list,
        count,
        [token],
    )
    dqkv_sum = attn_sum[:, : 3 * dim]
    attn_ring = ring_sum(*attn_made, (3 * dim, dim), "ctx")
    token = next(attn_ring)
    left[attn_ring] = steps - 1

    norm_sums = sums_b + sums_c
    norm_own = lax.dynamic_slice_in_dim(norm_sums, my_half * half, half, 1)
    norm_oth = swap(lax.dynamic_slice_in_dim(norm_sums, (1 - my_half) * half, half, 1))

    def own_part(vec):
        size = vec.shape[1] // 2
        return lax.dynamic_slice_in_dim(vec, my_half * size, size, 1).reshape(-1, half)

    (norm_oth,) = tied(token, norm_oth)
    small_sums = jnp.concatenate(
        [norm_own + norm_oth, own_part(dy_sum), own_part(dqkv_sum), own_part(du_sum)], axis=0
    )
    small_ring = butterfly_sum(small_sums, "ctx")
    next(small_ring)
    at = 0
    summed = None
    while any(left.values()):
        token = turn((up_ring, attn_ring, down_ring, attn_ring)[at % 4], token)
        if at % 4 == 0 and summed is None:
            summed = small_ring.send(token)
        at += 1
    while summed is None:
        summed = small_ring.send(token)
    small_sums = summed
    (down_grad,) = results[down_ring]
    (up_grad,) = results[up_ring]
    qkv_grad, proj_grad = results[attn_ring]

    qkv_end = 5 + dqkv_sum.shape[1] // 2 // half
    dy_total = small_sums[4:5]
    pick = lambda yes, no: jnp.where(first_section, yes, no)
    layer_out = jnp.stack([pick(y_c, y_b), pick(y_b, y_c)])[None, :, None]
    input_grad = jnp.stack([pick(dx_b, dx_c), pick(dx_c, dx_b)])[None, :, None]
    return (
        layer_out,
        input_grad,
        qkv_grad[None],
        small_sums[5:qkv_end].reshape(1, -1),
        proj_grad[None],
        dy_total,
        up_grad[None],
        small_sums[qkv_end:].reshape(1, -1),
        down_grad[None],
        dy_total,
        small_sums[0:1],
        small_sums[1:2],
        small_sums[2:3],
        small_sums[3:4],
    )


def solution(mesh):
    in_specs = (
        P(None, "wsh", "ctx", None),
        P(None, "wsh", "ctx", None),
        P(),
        P("section", "wsh", None),
        P("section", "wsh"),
        P("section", "wsh", None),
        P("section", "wsh"),
        P("section", "wsh", None),
        P("section", "wsh"),
        P("section", "wsh", None),
        P("section", "wsh"),
        P("section", "wsh"),
        P("section", "wsh"),
        P("section", "wsh"),
        P("section", "wsh"),
    )
    out_specs = (
        P("section", None, "wsh", "ctx", None),
        P("section", None, "wsh", "ctx", None),
        P("section", "wsh", None),
        P("section", "wsh"),
        P("section", "wsh", None),
        P("section", "wsh"),
        P("section", "wsh", None),
        P("section", "wsh"),
        P("section", "wsh", None),
        P("section", "wsh"),
        P("section", "wsh"),
        P("section", "wsh"),
        P("section", "wsh"),
        P("section", "wsh"),
    )
    return jax.shard_map(body, mesh=mesh, in_specs=in_specs, out_specs=out_specs, check_vma=False)
```

```python
import functools

import jax
import jax.numpy as jnp
from jax import lax
from jax.experimental import pallas as pl
from jax.experimental.pallas import tpu as pltpu
from jax.sharding import PartitionSpec as P

HEADS = 16
ROT = 16
NORM_EPS = 1e-05
ROPE_BASE = 10000.0
MASKED_SCORE = -1e30
LANES = 128
VMEM_LIMIT = 50 * 1024 * 1024
TAIL_LIMIT = VMEM_LIMIT
RING_LIMIT = VMEM_LIMIT
INV_SQRT2 = 0.7071067811865476
INV_SQRT_2PI = 0.3989422804014327

f32 = jnp.float32
bf16 = jnp.bfloat16


def dot_nn(left, right):
    return lax.dot_general(left, right, (((1,), (0,)), ((), ())), preferred_element_type=f32)


def dot_nt(left, right):
    return lax.dot_general(left, right, (((1,), (1,)), ((), ())), preferred_element_type=f32)


def params_of(limit):
    return dict(
        compiler_params=pltpu.CompilerParams(vmem_limit_bytes=limit),
        cost_estimate=pl.CostEstimate(flops=1, bytes_accessed=1, transcendentals=0),
    )


def whole(shape):
    rank = len(shape)
    return pl.BlockSpec(shape, lambda *args: (0,) * rank)


def shape_of(shape, dtype):
    return jax.ShapeDtypeStruct(shape, dtype)


def rope(vals, tab_ref):
    return (
        vals * tab_ref[0]
        + pltpu.roll(vals, LANES - ROT // 2, 1) * tab_ref[1]
        + pltpu.roll(vals, ROT // 2, 1) * tab_ref[2]
    )


def unrope(vals, tab_ref):
    return (
        vals * tab_ref[0]
        - pltpu.roll(vals, LANES - ROT // 2, 1) * tab_ref[1]
        - pltpu.roll(vals, ROT // 2, 1) * tab_ref[2]
    )


def normalized(hidden):
    row_mean = jnp.mean(hidden, axis=-1, keepdims=True)
    centered = hidden - row_mean
    spread = jnp.mean(centered * centered, axis=-1, keepdims=True)
    scale = lax.rsqrt(spread + NORM_EPS)
    return centered * scale, scale


def start_all(copies):
    for copy in copies:
        copy.start()
    return copies


def wait_all(copies):
    for copy in copies:
        copy.wait()


def qkv_kernel(own_given, wsh_ref, inputs, weights, outputs, buf, sems):
    half, dim = buf.shape[2:]
    copies = start_all(
        [
            pltpu.make_async_copy(
                weight.at[:, pl.ds(part * dim, dim)], buf.at[part, side], sems.at[part, side]
            )
            for part in range(3)
            for side, weight in enumerate(weights)
        ]
    )
    out, x_out, own, oth = outputs
    x = inputs[0].ref()[...]
    if not own_given:
        x = jnp.where(wsh_ref[1] == 1, x, inputs[4].ref()[...])
    x_out.ref[...] = x
    x_out.send()
    xhat, _ = normalized(x.astype(f32))
    vec_ref, bias_ref, tab_ref = (item.ref() for item in inputs[1:4])
    na = (xhat * vec_ref[0:1] + vec_ref[1:2]).astype(bf16)
    nm = (xhat * vec_ref[2:3] + vec_ref[3:4]).astype(bf16)
    first = wsh_ref[0] == 0
    for i, rows in enumerate((na, nm)):
        own.ref[i] = jnp.where(first, rows[:, :half], rows[:, half:])
        oth.ref[i] = jnp.where(first, rows[:, half:], rows[:, :half])
    own.send()
    oth.send()
    for part in range(3):
        wait_all(copies[2 * part : 2 * part + 2])
        for at in range(0, dim, 2 * LANES):
            cols = slice(at, at + 2 * LANES)
            res = (
                dot_nn(own.ref[0], buf[part, 0, :, cols])
                + dot_nn(oth.ref[0], buf[part, 1, :, cols])
                + bias_ref[:, part * dim + at : part * dim + at + 2 * LANES]
            )
            for i in range(2):
                vals = res[:, i * LANES : (i + 1) * LANES]
                if part < 2:
                    vals = rope(vals, tab_ref)
                out.ref[at // LANES + i, part] = vals.astype(bf16)


def layer_of(shape, index):
    return pl.BlockSpec((pl.squeezed,) + shape, lambda *args: (index, 0, 0))


HERE = pl.BlockSpec(memory_space=pltpu.VMEM)
SCALARS = pl.BlockSpec(memory_space=pltpu.SMEM)
ANYWHERE = pl.BlockSpec(memory_space=pl.ANY)
IN_HBM = pl.BlockSpec(memory_space=pltpu.HBM)


class Arriving:
    def __init__(self, buf, copy=None):
        self.buf, self.copy = buf, copy

    def ref(self):
        if self.copy is not None:
            self.copy.wait()
            self.copy = None
        return self.buf


class Leaving:
    def __init__(self, buf, copy=None):
        self.ref, self.copy, self.sent = buf, copy, copy is None

    def send(self):
        if not self.sent:
            self.copy.start()
            self.sent = True


def local_kernel(body, near_in, near_out, scalars, weights, followed, *refs):
    refs = list(refs)

    def take(number):
        taken = refs[:number]
        del refs[:number]
        return taken

    scalar_refs, array_refs = take(scalars), take(len(near_in))
    weight_refs, _, out_refs = take(weights), take(followed), take(len(near_out))
    in_sems, out_sems = take(2)
    inputs, outputs = [], []
    for i, (near, ref) in enumerate(zip(near_in, array_refs)):
        if near:
            inputs.append(Arriving(ref))
        else:
            buf = take(1)[0]
            copy = pltpu.make_async_copy(ref, buf, in_sems.at[i])
            copy.start()
            inputs.append(Arriving(buf, copy))
    for i, (near, ref) in enumerate(zip(near_out, out_refs)):
        if near:
            outputs.append(Leaving(ref))
        else:
            buf = take(1)[0]
            outputs.append(Leaving(buf, pltpu.make_async_copy(buf, ref, out_sems.at[i])))
    body(*scalar_refs, inputs, weight_refs, outputs, *refs)
    for item in inputs:
        item.ref()
    for item in outputs:
        item.send()
    for item in outputs:
        if item.copy is not None:
            item.copy.wait()


def far(array):
    return (array,)


def local_call(body, name, scalars, arrays, weights, out_shape, scratch=(), after=(), limit=VMEM_LIMIT):
    near_in = [not isinstance(a, tuple) for a in arrays]
    near_out = [not isinstance(o, tuple) for o in out_shape]
    raw_out = [isinstance(o, list) for o in out_shape]
    arrays = [a if near else a[0] for a, near in zip(arrays, near_in)]
    shapes = [o if near and not raw else o[0] for o, near, raw in zip(out_shape, near_out, raw_out)]
    far_bufs = [
        pltpu.VMEM(a.shape, a.dtype)
        for a, near in zip(arrays + shapes, near_in + near_out)
        if not near
    ]
    return pl.pallas_call(
        functools.partial(
            local_kernel, body, near_in, near_out, len(scalars), len(weights), len(after)
        ),
        in_specs=[SCALARS] * len(scalars)
        + [HERE if near else IN_HBM for near in near_in]
        + [IN_HBM] * len(weights)
        + [ANYWHERE] * len(after),
        out_specs=[HERE if near and not raw else IN_HBM for near, raw in zip(near_out, raw_out)],
        out_shape=shapes,
        scratch_shapes=[
            pltpu.SemaphoreType.DMA((len(arrays) + 1,)),
            pltpu.SemaphoreType.DMA((len(shapes),)),
        ]
        + far_bufs
        + list(scratch),
        name=name,
        **params_of(limit),
    )(*scalars, *arrays, *weights, *after)


def qkv_call(given, got, vecs, qkv_b, tab, w_own, w_oth, wsh):
    rows, dim = given.shape
    half = w_own.shape[0]
    pairs = dim // LANES
    return local_call(
        functools.partial(qkv_kernel, got is None),
        "qkv_proj",
        [wsh],
        [given, vecs, qkv_b, tab] if got is None else [given, vecs, qkv_b, tab, got],
        [w_own, w_oth],
        [shape_of((pairs, 3, rows, LANES), bf16), shape_of((rows, dim), bf16)]
        + [shape_of((2, rows, half), bf16)] * 2,
        [pltpu.VMEM((3, 2, half, dim), bf16), pltpu.SemaphoreType.DMA((3, 2))],
    )


FF_TILE = 1024
FF_PIECE = 512


def ff_tiles(wsh_ref, up_own, up_oth, dn_own, dn_oth, up_buf, dn_buf, sems):
    own = dn_own.shape[0] // FF_TILE
    tiles = []
    for t in range(2 * own):
        start = pl.multiple_of(((wsh_ref[0] * own + t) % (2 * own)) * FF_TILE, FF_TILE)
        cols = pl.ds(start, FF_TILE)
        down = (dn_own if t < own else dn_oth).at[pl.ds((t % own) * FF_TILE, FF_TILE)]
        copies = [
            pltpu.make_async_copy(up_own.at[:, cols], up_buf.at[t, 0], sems.at[t, 0]),
            pltpu.make_async_copy(up_oth.at[:, cols], up_buf.at[t, 1], sems.at[t, 1]),
            pltpu.make_async_copy(down, dn_buf.at[t], sems.at[t, 2]),
        ]
        tiles.append((t, start, start_all(copies)))
    for t, start, copies in tiles:
        wait_all(copies)
        for at in range(0, FF_TILE, FF_PIECE):
            row = (t % own) * FF_TILE + at
            place = pl.ds(pl.multiple_of(start + at, FF_PIECE), FF_PIECE)
            yield t, place, t < own, slice(row, row + FF_PIECE), slice(at, at + FF_PIECE)


def ff_scratch(half, ff, dim):
    tiles = ff // FF_TILE
    return [
        pltpu.VMEM((tiles, 2, half, FF_TILE), bf16),
        pltpu.VMEM((tiles, FF_TILE, dim), bf16),
        pltpu.SemaphoreType.DMA((tiles, 3)),
    ]


def mlp_kernel(save, wsh_ref, inputs, weights, outputs, up_buf, dn_buf, sems):
    out_ref = outputs[0].ref
    started = False
    for t, place, held, rows, piece in ff_tiles(wsh_ref, *weights, up_buf, dn_buf, sems):
        own_ref, oth_ref, up_b, down_b = (item.ref() for item in inputs)
        if not started:
            out_ref[...] = jnp.broadcast_to(down_b[...], out_ref.shape)
            started = True
        pre = (
            dot_nn(own_ref[1], up_buf[t, 0, :, piece])
            + dot_nn(oth_ref[1], up_buf[t, 1, :, piece])
            + up_b[:, place]
        )
        gate = 0.5 + 0.5 * lax.erf(pre * INV_SQRT2)
        act = (pre * gate).astype(bf16)
        if save:
            slope = gate + pre * (INV_SQRT_2PI * jnp.exp(-0.5 * pre * pre))
            outputs[1].ref[place] = slope.astype(bf16).T
            outputs[2 if held else 3].ref[rows] = act.T
            if not held:
                outputs[2].send()
        out_ref[...] += dot_nn(act, dn_buf[t, piece])


def mlp_call(own, oth, up_b, down_b, up_own, up_oth, dn_own, dn_oth, wsh, save):
    rows, half = own.shape[1:]
    dim = dn_own.shape[1]
    ff = up_own.shape[1]
    out_shape = [shape_of((rows, dim), f32)]
    if save:
        out_shape += [shape_of((ff, rows), bf16)]
        out_shape += [shape_of((ff // 2, rows), bf16)] * 2
    return local_call(
        functools.partial(mlp_kernel, save),
        "mlp_forward",
        [wsh],
        [own, oth, up_b, down_b],
        [up_own, up_oth, dn_own, dn_oth],
        out_shape,
        ff_scratch(half, ff, dim),
    )


def mlp_back_kernel(wsh_ref, inputs, weights, outputs, acc_own, acc_oth, up_buf, dn_buf, sems):
    du, dnm = outputs
    half = acc_own.shape[0]
    acc_own[...] = jnp.zeros(acc_own.shape, f32)
    acc_oth[...] = jnp.zeros(acc_oth.shape, f32)
    for t, place, _, _, piece in ff_tiles(wsh_ref, *weights, up_buf, dn_buf, sems):
        dy_ref, slope_ref = (item.ref() for item in inputs)
        dact = dot_nt(dn_buf[t, piece], dy_ref[...])
        vals = (dact * slope_ref[place].astype(f32)).astype(bf16)
        du.ref[place] = vals
        acc_own[...] += dot_nn(up_buf[t, 0, :, piece], vals)
        acc_oth[...] += dot_nn(up_buf[t, 1, :, piece], vals)
    du.send()
    first = wsh_ref[0] == 0
    dnm.ref[:, :half] = jnp.where(first, acc_own[...], acc_oth[...]).T
    dnm.ref[:, half:] = jnp.where(first, acc_oth[...], acc_own[...]).T


def mlp_back_call(dy, slope, up_own, up_oth, dn_own, dn_oth, wsh, after, limit):
    rows, dim = dy.shape
    half, ff = up_own.shape
    return local_call(
        mlp_back_kernel,
        "mlp_backward",
        [wsh],
        [dy, slope],
        [up_own, up_oth, dn_own, dn_oth],
        [shape_of(slope.shape, bf16), shape_of((rows, dim), f32)],
        [pltpu.VMEM((half, rows), f32), pltpu.VMEM((half, rows), f32)] + ff_scratch(half, ff, dim),
        after,
        limit,
    )


def sort_in(loc_ref, ref, dst, half_rows, part=None):
    for block in range(dst.shape[0] // half_rows):
        place = loc_ref[block]
        rows = pl.ds(pl.multiple_of((place % 2) * half_rows, half_rows), half_rows)
        if part is None:
            vals = ref[place // 2, rows, :]
        else:
            vals = ref[place // 2, part, rows, :]
        dst[block * half_rows : (block + 1) * half_rows] = vals


def sort_out(loc_ref, vals, ref, half_rows, part=None):
    for block in range(vals.shape[0] // half_rows):
        place = loc_ref[block]
        rows = pl.ds(pl.multiple_of((place % 2) * half_rows, half_rows), half_rows)
        piece = vals[block * half_rows : (block + 1) * half_rows]
        if part is None:
            ref[place // 2, rows, :] = piece
        else:
            ref[place // 2, part, rows, :] = piece


def head_of(vals, head):
    lane = lax.broadcasted_iota(jnp.int32, vals.shape, 1)
    return jnp.where(lane // (LANES // 2) == head, vals, jnp.zeros_like(vals))


def scores_of(keys, queries, scale, diagonal):
    scores = dot_nt(keys, queries) * scale
    if diagonal:
        key_at = lax.broadcasted_iota(jnp.int32, scores.shape, 0)
        query_at = lax.broadcasted_iota(jnp.int32, scores.shape, 1)
        scores = jnp.where(key_at <= query_at, scores, MASKED_SCORE)
    return scores


def attend_kernel(tile, loc_ref, inputs, weights, outputs, q_s, k_s, v_s, vt_s, o_s):
    qkv_ref = inputs[0].ref()
    o_ref, lse_ref = (item.ref for item in outputs)
    half_rows = qkv_ref.shape[2] // 2
    seq = q_s.shape[0]
    head_size = LANES // 2
    scale = head_size**-0.5
    sort_in(loc_ref, qkv_ref, q_s, half_rows, 0)
    sort_in(loc_ref, qkv_ref, k_s, half_rows, 1)
    sort_in(loc_ref, qkv_ref, v_s, half_rows, 2)
    vt_s[...] = v_s[...].T
    for t in range(seq // tile):
        rows = slice(t * tile, (t + 1) * tile)
        queries = q_s[rows]
        outs = []
        for head in range(2):
            picked = head_of(queries, head)
            parts = [
                scores_of(k_s[i * tile : (i + 1) * tile], picked, scale, i == t)
                for i in range(t + 1)
            ]
            top = functools.reduce(
                jnp.maximum, [jnp.max(p, axis=0, keepdims=True) for p in parts]
            )
            parts = [jnp.exp(p - top) for p in parts]
            total = sum(jnp.sum(p, axis=0, keepdims=True) for p in parts)
            lse_ref[head : head + 1, rows] = top + jnp.log(total)
            inverse = 1.0 / total
            acc = None
            for i, p in enumerate(parts):
                term = dot_nn(
                    vt_s[head * head_size : (head + 1) * head_size, i * tile : (i + 1) * tile],
                    (p * inverse).astype(bf16),
                )
                acc = term if acc is None else acc + term
            outs.append(acc)
        o_s[rows] = jnp.concatenate(outs, axis=0).T.astype(bf16)
    sort_out(loc_ref, o_s, o_ref, half_rows)


def attend_call(qkv, loc, after):
    count, _, rows, _ = qkv.shape
    seq = count * rows
    return local_call(
        functools.partial(attend_kernel, 256),
        "attention",
        [loc],
        [qkv],
        [],
        [shape_of((count, rows, LANES), bf16), shape_of((2, seq), f32)],
        [
            pltpu.VMEM((seq, LANES), bf16),
            pltpu.VMEM((seq, LANES), bf16),
            pltpu.VMEM((seq, LANES), bf16),
            pltpu.VMEM((LANES, seq), bf16),
            pltpu.VMEM((seq, LANES), bf16),
        ],
        after,
    )


def attend_back_kernel(
    tile, part, loc_ref, inputs, weights, outputs, q_s, k_s, v_s, da_s, kt_s, dq_s, dk_s, dv_s
):
    da_ref, qkv_ref, lse_ref = (item.ref() for item in inputs)
    out_ref = outputs[0].ref
    half_rows = qkv_ref.shape[2] // 2
    seq = q_s.shape[0]
    head_size = LANES // 2
    scale = head_size**-0.5
    sort_in(loc_ref, qkv_ref, q_s, half_rows, 0)
    sort_in(loc_ref, qkv_ref, k_s, half_rows, 1)
    sort_in(loc_ref, qkv_ref, v_s, half_rows, 2)
    sort_in(loc_ref, da_ref, da_s, half_rows, part)
    kt_s[...] = k_s[...].T
    dk_s[...] = jnp.zeros(dk_s.shape, f32)
    dv_s[...] = jnp.zeros(dv_s.shape, f32)
    for t in range(seq // tile):
        rows = slice(t * tile, (t + 1) * tile)
        outs = []
        for head in range(2):
            queries = head_of(q_s[rows], head)
            grads = head_of(da_s[rows], head)
            lse = lse_ref[head : head + 1, rows]
            probs, dprobs, row_dot = [], [], 0.0
            for i in range(t + 1):
                keys = slice(i * tile, (i + 1) * tile)
                p = jnp.exp(scores_of(k_s[keys], queries, scale, i == t) - lse)
                dp = dot_nt(v_s[keys], grads)
                row_dot = row_dot + jnp.sum(p * dp, axis=0, keepdims=True)
                dv_s[keys] += dot_nn(p.astype(bf16), grads)
                probs.append(p)
                dprobs.append(dp)
            acc = None
            for i in range(t + 1):
                keys = slice(i * tile, (i + 1) * tile)
                ds = (probs[i] * (dprobs[i] - row_dot) * scale).astype(bf16)
                dk_s[keys] += dot_nn(ds, queries)
                term = dot_nn(kt_s[head * head_size : (head + 1) * head_size, keys], ds)
                acc = term if acc is None else acc + term
            outs.append(acc)
        dq_s[rows] = jnp.concatenate(outs, axis=0).T.astype(bf16)
    sort_out(loc_ref, dq_s, out_ref, half_rows, 0)
    k_s[...] = dk_s[...].astype(bf16)
    v_s[...] = dv_s[...].astype(bf16)
    sort_out(loc_ref, k_s, out_ref, half_rows, 1)
    sort_out(loc_ref, v_s, out_ref, half_rows, 2)


def attend_back_call(qkv, da, lse, loc, after, limit):
    count, _, rows, _ = qkv.shape
    seq = count * rows
    part = 0 if da.ndim == 4 else None
    (res,) = local_call(
        functools.partial(attend_back_kernel, 256, part),
        "attention_backward",
        [loc],
        [da, qkv, lse],
        [],
        [shape_of(qkv.shape, bf16)],
        [pltpu.VMEM((seq, LANES), bf16)] * 4
        + [pltpu.VMEM((LANES, seq), bf16), pltpu.VMEM((seq, LANES), bf16)]
        + [pltpu.VMEM((seq, LANES), f32)] * 2,
        after,
        limit,
    )
    return res


def by_head(parts):
    pairs, rows, lanes = parts.shape
    return jnp.transpose(parts, (1, 0, 2)).reshape(rows, HEADS, pairs * lanes // HEADS)


def by_pair(heads):
    rows = heads.shape[0]
    return jnp.transpose(heads.reshape(rows, -1, LANES), (1, 0, 2))


def wide_scores(queries, keys, query_pos, key_pos):
    raw = jnp.einsum("qhd,khd->hqk", queries, keys, preferred_element_type=f32)
    allowed = (query_pos[:, None] >= key_pos[None, :])[None]
    return jnp.where(allowed, raw * queries.shape[-1] ** (-0.5), MASKED_SCORE)


def key_blocks(arrays, rows):
    return tuple(a.reshape((a.shape[0] // rows, rows) + a.shape[1:]) for a in arrays)


def wide_attend(qkv, query_pos, key_pos):
    queries = by_head(qkv[:, 0])
    keys = lax.all_gather(by_head(qkv[:, 1]), "ctx", axis=0, tiled=True)
    values = lax.all_gather(by_head(qkv[:, 2]), "ctx", axis=0, tiled=True)
    block = min(512, keys.shape[0])
    split = key_blocks((keys, values, key_pos), block)
    rows, _, head_size = queries.shape

    def max_step(carry, block_in):
        top, total = carry
        scores = wide_scores(queries, block_in[0], query_pos, block_in[2])
        new_top = jnp.maximum(top, jnp.max(scores, axis=-1))
        part = jnp.sum(jnp.exp(scores - new_top[..., None]), axis=-1)
        return ((new_top, total * jnp.exp(top - new_top) + part), None)

    start = (jnp.full((HEADS, rows), MASKED_SCORE, f32), jnp.zeros((HEADS, rows), f32))
    (top, total), _ = lax.scan(max_step, start, split)
    lse = top + jnp.log(total)

    def value_step(running, block_in):
        scores = wide_scores(queries, block_in[0], query_pos, block_in[2])
        probs = jnp.exp(scores - lse[..., None]).astype(bf16)
        term = jnp.einsum("hqk,khd->qhd", probs, block_in[1], preferred_element_type=f32)
        return (running + term, None)

    attended, _ = lax.scan(value_step, jnp.zeros((rows, HEADS, head_size), f32), split)
    return by_pair(attended.astype(bf16)), (queries, keys, values, lse)


def wide_attend_back(kept, da, query_pos, key_pos):
    queries, keys, values, lse = kept
    grads = by_head(da)
    block = min(512, keys.shape[0])
    split = key_blocks((keys, values, key_pos), block)
    scale = queries.shape[-1] ** (-0.5)

    def pieces(block_in):
        scores = wide_scores(queries, block_in[0], query_pos, block_in[2])
        probs = jnp.exp(scores - lse[..., None])
        dprobs = jnp.einsum("qhd,khd->hqk", grads, block_in[1], preferred_element_type=f32)
        return probs, dprobs

    def dot_step(running, block_in):
        probs, dprobs = pieces(block_in)
        return (running + jnp.sum(probs * dprobs, axis=-1), None)

    row_dot, _ = lax.scan(dot_step, jnp.zeros(lse.shape, f32), split)

    def key_step(running, block_in):
        probs, dprobs = pieces(block_in)
        ds = (scale * probs * (dprobs - row_dot[..., None])).astype(bf16)
        running = running + jnp.einsum("hqk,khd->qhd", ds, block_in[0], preferred_element_type=f32)
        dk = jnp.einsum("hqk,qhd->khd", ds, queries, preferred_element_type=f32)
        dv = jnp.einsum("hqk,qhd->khd", probs.astype(bf16), grads, preferred_element_type=f32)
        return (running, (dk.astype(bf16), dv.astype(bf16)))

    dq, (dk, dv) = lax.scan(key_step, jnp.zeros(queries.shape, f32), split)
    dk, dv = (
        lax.psum_scatter(part.reshape(keys.shape), "ctx", scatter_dimension=0, tiled=True)
        for part in (dk, dv)
    )
    return jnp.stack([by_pair(dq.astype(bf16)), by_pair(dk), by_pair(dv)], axis=1)


def lanes_of(ref):
    return jnp.concatenate([ref[i] for i in range(ref.shape[0])], axis=1)


def both_halves(w_own, w_oth, buf, sems):
    return start_all(
        [
            pltpu.make_async_copy(weight, buf.at[side], sems.at[side])
            for side, weight in enumerate((w_own, w_oth))
        ]
    )


def half_scratch(weight):
    return [pltpu.VMEM((2,) + weight.shape, bf16), pltpu.SemaphoreType.DMA((2,))]


def proj_kernel(part, wsh_ref, inputs, weights, outputs, buf, sems):
    copies = both_halves(*weights, buf, sems)
    y, own, oth = outputs
    half = buf.shape[1]
    first = wsh_ref[0] == 0
    a_ref = inputs[0].ref()
    a = lanes_of(a_ref if part is None else a_ref.at[:, part])
    own.ref[...] = jnp.where(first, a[:, :half], a[:, half:])
    oth.ref[...] = jnp.where(first, a[:, half:], a[:, :half])
    own.send()
    oth.send()
    bias_ref, x_ref, mlp_ref = (item.ref() for item in inputs[1:])
    wait_all(copies)
    attn = dot_nn(own.ref[...], buf[0]) + dot_nn(oth.ref[...], buf[1]) + bias_ref[...]
    y.ref[...] = (x_ref[...].astype(f32) + attn + mlp_ref[...]).astype(bf16)


def proj_call(a, x, mlp, bias, p_own, p_oth, wsh, after, limit):
    rows, dim = x.shape
    half = p_own.shape[0]
    return local_call(
        functools.partial(proj_kernel, 1 if a.ndim == 4 else None),
        "attn_out",
        [wsh],
        [a, bias, x, mlp],
        [p_own, p_oth],
        [shape_of((rows, dim), bf16)] + [shape_of((rows, half), bf16)] * 2,
        half_scratch(p_own),
        after,
        limit,
    )


def da_kernel(own_given, wsh_ref, inputs, weights, outputs, buf, sems):
    copies = both_halves(*weights, buf, sems)
    out_ref, dy_out = outputs[0].ref, outputs[1]
    dy = inputs[0].ref()[...]
    if not own_given:
        dy = jnp.where(wsh_ref[1] == 1, inputs[1].ref()[...], dy)
    dy_out.ref[...] = dy
    dy_out.send()
    wsh = wsh_ref[0]
    joined = len(out_ref.shape) == 4
    if joined:
        out_ref[:, 1] = inputs[2].ref()[...]
    count = out_ref.shape[0] // 2
    for place, side in ((wsh * count, 0), ((1 - wsh) * count, 1)):
        copies[side].wait()
        part = dot_nt(dy, buf[side]).astype(bf16)
        for i in range(count):
            vals = part[:, i * LANES : (i + 1) * LANES]
            if joined:
                out_ref[place + i, 0] = vals
            else:
                out_ref[place + i] = vals


def da_call(given, got, p_own, p_oth, wsh, joined=None):
    rows, dim = given.shape
    pairs = dim // LANES
    arrays = [given] + ([] if got is None else [got])
    arrays += [] if joined is None else [joined]
    shape = (pairs, rows, LANES) if joined is None else (pairs, 2, rows, LANES)
    return local_call(
        functools.partial(da_kernel, got is None),
        "attn_out_backward",
        [wsh],
        arrays,
        [p_own, p_oth],
        [shape_of(shape, bf16), shape_of((rows, dim), bf16)],
        half_scratch(p_own),
    )


def dx_kernel(wsh_ref, inputs, weights, outputs, grad_s, buf, sems):
    copies = both_halves(*weights, buf, sems)
    back, dx, sums = outputs
    dqkv_ref, tab_ref = inputs[0].ref(), inputs[1].ref()
    pairs = dqkv_ref.shape[0]
    for part in range(3):
        for pair in range(pairs):
            vals = dqkv_ref[pair, part]
            if part < 2:
                vals = unrope(vals.astype(f32), tab_ref).astype(bf16)
            back.ref[pair, part] = vals
            grad_s[:, pl.ds((part * pairs + pair) * LANES, LANES)] = vals
    back.send()
    vec_ref, x_ref, dy_ref, dnm_ref = (item.ref() for item in inputs[2:])
    first = wsh_ref[0] == 0
    copies[0].wait()
    own = dot_nt(grad_s[...], buf[0])
    copies[1].wait()
    oth = dot_nt(grad_s[...], buf[1])
    dna = jnp.concatenate([jnp.where(first, own, oth), jnp.where(first, oth, own)], axis=1)
    dnm = dnm_ref[...]
    xhat, scale = normalized(x_ref[...].astype(f32))
    grad = dna * vec_ref[0:1] + dnm * vec_ref[2:3]
    inner = (
        grad
        - jnp.mean(grad, axis=-1, keepdims=True)
        - xhat * jnp.mean(grad * xhat, axis=-1, keepdims=True)
    )
    dx.ref[...] = (dy_ref[...].astype(f32) + scale * inner).astype(bf16)
    dx.send()
    sums.ref[0:1] = jnp.sum(dna * xhat, axis=0, keepdims=True)
    sums.ref[1:2] = jnp.sum(dna, axis=0, keepdims=True)
    sums.ref[2:3] = jnp.sum(dnm * xhat, axis=0, keepdims=True)
    sums.ref[3:4] = jnp.sum(dnm, axis=0, keepdims=True)


def dx_call(dqkv, tab, x, dy, dnm, vecs, w_own, w_oth, wsh, after, limit):
    rows, dim = x.shape
    return local_call(
        dx_kernel,
        "section_input_grad",
        [wsh],
        [dqkv, tab, vecs, x, dy, dnm],
        [w_own, w_oth],
        [shape_of(o, t) for o, t in ((dqkv.shape, bf16), ((rows, dim), bf16), ((4, dim), f32))],
        [pltpu.VMEM((rows, 3 * dim), bf16)] + half_scratch(w_own),
        after,
        limit,
    )


def joined_rows(items):
    return jnp.concatenate([item.ref()[...] for item in items], axis=0)


class Pieces:
    def __init__(self, out_ref, buf, sems):
        self.out_ref, self.buf, self.sems, self.copies = out_ref, buf, sems, []

    def put(self, rows, cols, vals):
        self.buf[rows, cols] = vals.astype(bf16)
        at = len(self.copies)
        self.copies.append(
            pltpu.make_async_copy(
                self.buf.at[rows, cols], self.out_ref.at[rows, cols], self.sems.at[at]
            )
        )
        self.copies[-1].start()

    def finish(self, chunk, ahead, behind):
        height, cut = ahead.ref.shape
        rows = pl.ds(pl.multiple_of(chunk * height, height), height)
        ahead.ref[...] = self.buf[rows, :cut]
        ahead.send()
        behind.ref[...] = self.buf[rows, cut:]
        behind.send()
        wait_all(self.copies)


def first_half(cols):
    return cols // 2 // LANES * LANES


def grad_call(body, name, scalars, arrays, shape, width, count, scratch, after):
    cut = first_half(shape[1])
    halves = [far(shape_of((shape[0] // count, c), bf16)) for c in (cut, shape[1] - cut)]
    return local_call(
        functools.partial(body, len(arrays)),
        name,
        scalars,
        arrays,
        [],
        [[shape_of(shape, bf16)]] + halves + [far(shape_of((1, width), f32))],
        [pltpu.VMEM(shape, bf16), pltpu.SemaphoreType.DMA((5,))] + scratch,
        after,
        TAIL_LIMIT,
    )


def parts_of(items, number):
    size = len(items) // number
    return [items[i * size : (i + 1) * size] for i in range(number)]


def down_grad_kernel(number, idx_ref, inputs, weights, outputs, buf, sems):
    gts, dys = parts_of(inputs, 2)
    out = Pieces(outputs[0].ref, buf, sems)
    dy = joined_rows(dys)
    outputs[3].ref[...] = jnp.sum(dy.astype(f32), axis=0, keepdims=True)
    rows, dim = buf.shape
    tile = rows // 4
    for t in range(4):
        part = slice(t * tile, (t + 1) * tile)
        left = jnp.concatenate([item.ref()[part] for item in gts], axis=1)
        out.put(part, slice(0, dim), dot_nn(left, dy))
    out.finish(idx_ref[idx_ref.shape[0] // 2], outputs[1], outputs[2])


def down_grad_call(idx, gt_list, dy_list, count):
    dim = dy_list[0].shape[1]
    return grad_call(
        down_grad_kernel,
        "down_grad",
        [idx],
        [far(a) for a in gt_list + dy_list],
        (gt_list[0].shape[0], dim),
        dim,
        count,
        [],
        [],
    )


def up_grad_kernel(number, idx_ref, inputs, weights, outputs, buf, sems):
    norms, dus = parts_of(inputs, 2)
    out = Pieces(outputs[0].ref, buf, sems)
    left = jnp.concatenate([item.ref()[1] for item in norms], axis=0).T
    rows, ff = buf.shape
    tile = ff // 4
    for t in range(4):
        part = slice(t * tile, (t + 1) * tile)
        du = jnp.concatenate([item.ref()[part] for item in dus], axis=1)
        outputs[3].ref[:, part] = dot_nt(jnp.ones((8, du.shape[1]), bf16), du)[:1]
        out.put(slice(0, rows), part, dot_nt(left, du))
    out.finish(idx_ref[idx_ref.shape[0] // 2], outputs[1], outputs[2])


def up_grad_call(idx, norm_list, du_list, count, after):
    half, ff = norm_list[0].shape[2], du_list[0].shape[0]
    return grad_call(
        up_grad_kernel,
        "up_grad",
        [idx],
        [far(a) for a in norm_list + du_list],
        (half, ff),
        ff,
        count,
        [],
        after,
    )


def attn_grad_kernel(number, idx_ref, wsh_ref, inputs, weights, outputs, buf, sems, small_s):
    norms, outs, dqkvs, dys = parts_of(inputs[:-1], 4)
    out = Pieces(outputs[0].ref, buf, sems)
    sums = outputs[3].ref
    rows, dim = buf.shape[0], sums.shape[1] // 4
    left = jnp.concatenate([item.ref()[0] for item in norms], axis=0).T
    for part in range(4):
        cols = slice(part * dim, (part + 1) * dim)
        if part < 3:
            right = jnp.concatenate([lanes_of(item.ref().at[:, part]) for item in dqkvs], axis=0)
        else:
            left, right = joined_rows(outs).T, joined_rows(dys)
        sums[:, cols] = jnp.sum(right.astype(f32), axis=0, keepdims=True)
        out.put(slice(0, rows), cols, dot_nn(left, right))
    given = inputs[-1].ref()
    at = given.shape[0]
    small_s[:at] = given[...]
    base = wsh_ref[0] * (3 * dim // 2)
    for i in range(3 * dim // 2 // LANES):
        place = pl.ds(pl.multiple_of(base + i * LANES, LANES), LANES)
        small_s[at + i : at + i + 1] = sums[:, place]
    small = small_s[...]
    empty = jnp.zeros((rows - small.shape[0], LANES), f32)
    out.put(slice(0, rows), slice(4 * dim, 4 * dim + LANES), jnp.concatenate([small, empty], axis=0))
    out.finish(idx_ref[idx_ref.shape[0] // 2], outputs[1], outputs[2])


def attn_grad_call(idx, wsh, norm_list, out_list, dqkv_list, dy_list, small, count, after):
    half, dim = norm_list[0].shape[2], dy_list[0].shape[1]
    return grad_call(
        attn_grad_kernel,
        "attn_grad",
        [idx, wsh],
        [far(a) for a in norm_list + out_list + dqkv_list + dy_list] + [small],
        (half, 4 * dim + LANES),
        4 * dim,
        count,
        [pltpu.VMEM((small.shape[0] + 3 * dim // 2 // LANES, LANES), f32)],
        after,
    )


def ring_of(count):
    return list(range(0, count, 2)) + list(range(count - 1, 0, -2))


def ring_place(axis):
    count = lax.axis_size(axis)
    me = lax.axis_index(axis)
    return jnp.where(me % 2 == 0, me // 2, count - (me + 1) // 2)


def ring_index(axis):
    count = lax.axis_size(axis)
    return (ring_place(axis) + jnp.arange(count, dtype=jnp.int32)) % count


def ring_shift(vals, axis, by):
    order = ring_of(lax.axis_size(axis))
    count = len(order)
    pairs = [(order[i], order[(i + by) % count]) for i in range(count)]
    return lax.ppermute(vals, axis, pairs)


def tied(token, *vals):
    return lax.optimization_barrier((token, vals))[1]


def fetch(idx_ref, slots, own_ref, bufs, sems):
    return start_all(
        [
            pltpu.make_async_copy(own_ref.at[idx_ref[slot]], bufs.at[i], sems.at[i])
            for i, slot in enumerate(slots)
        ]
    )


def low_total(*terms):
    total = terms[0].astype(f32)
    for term in terms[1:]:
        total = total + term.astype(f32)
    return total.astype(bf16)


def ring_add_kernel(slots, idx_ref, inputs, own_refs, outputs, bufs, sems):
    copies = fetch(idx_ref, slots, own_refs[0], bufs, sems)
    for i, item in enumerate(outputs):
        copies[i].wait()
        got = inputs[i].ref()
        cols, cut = item.ref.shape[1], got.shape[1]
        summed = slice(0, cut) if i == 0 else slice(cols - cut, cols)
        item.ref[:, summed] = low_total(bufs[i, :, summed], got[...])
        if cut < cols:
            rest = slice(cut, cols) if i == 0 else slice(0, cols - cut)
            item.ref[:, rest] = bufs[i, :, rest]
        item.send()


def put_copies(chunk, cols, buf, totals, starts, sem):
    lo, hi = cols, cols + buf.shape[1]
    copies = []
    for i, (total, start) in enumerate(zip(totals, starts)):
        first, last = max(lo, start), min(hi, start + total.shape[2])
        if first < last:
            copies.append(
                pltpu.make_async_copy(
                    buf.at[:, pl.ds(first - lo, last - first)],
                    total.at[chunk, :, pl.ds(first - start, last - first)],
                    sem.at[i],
                )
            )
    return copies


def ring_own_kernel(slots, idx_ref, inputs, own_refs, outputs, bufs, sems):
    wait_all(fetch(idx_ref, slots, own_refs[0], bufs, sems))
    outputs[0].ref[...] = low_total(bufs[0], inputs[0].ref()[...], inputs[1].ref()[...])


def ring_put_kernel(starts, slots, cols, fresh, onward, idx_ref, *refs):
    number = len(slots)
    pieces = refs[:number]
    wide, sems, pass_buf, pass_sems = refs[-4:]
    passed = refs[-4 - onward : -4]
    totals = refs[-4 - onward - len(starts) : -4 - onward]
    leaving = []
    for i, ref in enumerate(passed):
        width = ref.shape[1]
        pass_buf[i, :, :width] = pieces[i][:, :width] if i == 0 else pieces[i][:, -width:]
        leaving += start_all(
            [pltpu.make_async_copy(pass_buf.at[i, :, pl.ds(0, width)], ref, pass_sems.at[i])]
        )
    for i in range(number):
        part = pl.ds(0, pieces[i].shape[1])
        wide[i, :, part] = pieces[i][...].astype(f32)
        leaving += start_all(
            put_copies(
                idx_ref[slots[i]], cols[i], wide.at[i, :, part], totals, starts, sems.at[i]
            )
        )
    wait_all(leaving)


def ring_sum(own, ahead, behind, widths, axis):
    count = lax.axis_size(axis)
    half = count // 2
    full_rows, cols = own.shape
    rows = full_rows // count
    own = own.reshape(count, rows, cols)
    cut = ahead.shape[1]
    starts = [sum(widths[:i]) for i in range(len(widths))]
    idx = ring_index(axis)
    chunk = shape_of((rows, cols), bf16)
    halves = [shape_of((rows, cut), bf16), shape_of((rows, cols - cut), bf16)]
    sums = [shape_of((count, rows, width), f32) for width in widths]

    def taken(number):
        return [pltpu.VMEM((number, rows, cols), bf16), pltpu.SemaphoreType.DMA((number,))]

    def put(totals, pieces, slots, passed, after):
        number = len(pieces)
        first_cols = (0,) * number if pieces[0].shape[1] == cols else (0, cut)
        fresh = totals is None
        out = pl.pallas_call(
            functools.partial(
                ring_put_kernel,
                starts,
                tuple(k % count for k in slots),
                first_cols,
                fresh,
                len(passed),
            ),
            in_specs=[SCALARS]
            + [HERE] * number
            + [IN_HBM] * (0 if fresh else len(sums))
            + [ANYWHERE] * len(after),
            out_specs=[IN_HBM] * (len(sums) + len(passed)),
            out_shape=sums + passed,
            scratch_shapes=[
                pltpu.VMEM((number, rows, cols), f32),
                pltpu.SemaphoreType.DMA((number, len(sums))),
                pltpu.VMEM((2, rows, cols), bf16),
                pltpu.SemaphoreType.DMA((2,)),
            ],
            input_output_aliases={} if fresh else {1 + number + i: i for i in range(len(sums))},
            name="ring_put",
            **params_of(RING_LIMIT),
        )(idx, *pieces, *([] if fresh else totals), *after)
        return out[: len(sums)], out[len(sums) :]

    def both_ways(ahead, behind):
        return ring_shift(ahead, axis, 1), ring_shift(behind, axis, -1)

    token = behind
    ahead, behind = both_ways(ahead, behind)
    token = yield token
    for k in range(half - 1, 0, -1):
        ahead, behind = local_call(
            functools.partial(ring_add_kernel, (k % count, (-k) % count)),
            "ring_add",
            [idx],
            [ahead, behind],
            [own],
            [chunk, chunk],
            taken(2),
            [token],
            RING_LIMIT,
        )
        token = behind
        ahead, behind = both_ways(ahead, behind)
        token = yield token
    (mine,) = local_call(
        functools.partial(ring_own_kernel, (0,)),
        "ring_own",
        [idx],
        [ahead, behind],
        [own],
        [chunk],
        taken(1),
        [token],
        RING_LIMIT,
    )
    ahead, behind = both_ways(mine, mine)
    totals, (token,) = put(None, [mine], [0], [shape_of((rows, LANES), bf16)], [])
    token = yield token
    for k in range(1, half):
        passed = halves if k == half - 1 else [chunk, chunk]
        totals, passed = put(totals, [ahead, behind], [-k, k], passed, [token])
        token = passed[1]
        ahead, behind = both_ways(*passed)
        token = yield token
    totals, _ = put(totals, [ahead, behind], [-half, half], [], [token])
    yield [total.reshape(full_rows, -1) for total in totals]


def swap(vals):
    return lax.ppermute(vals, "wsh", [(0, 1), (1, 0)])


def pass_on(vals, by):
    pairs = [(0, 1)] if by > 0 else [(1, 0)]
    return lax.ppermute(vals, "section", pairs)


def block_places(block_pair, count):
    want = jnp.arange(2 * count, dtype=jnp.int32)
    device = jnp.arange(count, dtype=jnp.int32)
    first = (block_pair[None, :] == want[:, None]).astype(jnp.int32)
    second = ((2 * count - 1 - block_pair)[None, :] == want[:, None]).astype(jnp.int32)
    return jnp.sum(first * (2 * device) + second * (2 * device + 1), axis=1)


def row_positions(block_pair, stored, tok_dev):
    count = block_pair.shape[0]
    device = stored // tok_dev
    within = stored % tok_dev
    half_rows = tok_dev // 2
    matches = device[:, None] == jnp.arange(count, dtype=jnp.int32)[None, :]
    pair_block = jnp.sum(jnp.where(matches, block_pair[None, :], 0), axis=1)
    block_idx = jnp.where(within < half_rows, pair_block, 2 * count - 1 - pair_block)
    return block_idx * half_rows + within % half_rows


def rotary_table(positions, head_size):
    half_rot = ROT // 2
    lane = jnp.arange(LANES, dtype=jnp.int32) % head_size
    inv_freq = ROPE_BASE ** (-((lane % half_rot).astype(f32) * 2.0) / ROT)
    angles = positions.astype(f32)[:, None] * inv_freq[None, :]
    cosine, sine = jnp.cos(angles), jnp.sin(angles)
    lead, second = (lane < half_rot)[None], ((lane >= half_rot) & (lane < ROT))[None]
    return jnp.stack(
        [
            jnp.where(lead | second, cosine, 1.0),
            jnp.where(lead, -sine, 0.0),
            jnp.where(second, sine, 0.0),
        ]
    )


def body(
    inputs,
    cotangent,
    block_pair,
    qkv_weight,
    qkv_bias,
    proj_weight,
    proj_bias,
    up_weight,
    up_bias,
    down_weight,
    down_bias,
    attn_gain,
    attn_shift,
    mlp_gain,
    mlp_shift,
):
    first_section = lax.axis_index("section") == 0
    count = lax.axis_size("ctx")
    micros, _, tok_dev, dim = inputs.shape
    head_size = dim // HEADS
    half = dim // 2
    my_half = lax.axis_index("wsh")
    wsh = jnp.stack([my_half.astype(jnp.int32), first_section.astype(jnp.int32)])
    one_pair_each = count == dim // LANES

    wq, wp, wu, wd = (w[0] for w in (qkv_weight, proj_weight, up_weight, down_weight))
    small = jnp.concatenate(
        [
            v[0].reshape(-1, half)
            for v in (
                attn_gain,
                attn_shift,
                mlp_gain,
                mlp_shift,
                proj_bias,
                down_bias,
                qkv_bias,
                up_bias,
            )
        ],
        axis=0,
    )
    small_oth = swap(small)
    wq_oth = swap(wq)
    first_here = lax.optimization_barrier((wq_oth, small_oth))
    wq_oth, small_oth = first_here
    wu_oth = swap(tied(wq_oth, wu)[0])
    wd_oth = swap(tied(wq_oth, wd)[0])
    wp_oth = swap(tied(wu_oth, wp)[0])
    low_part = jnp.where(my_half == 0, small, small_oth).astype(f32)
    high_part = jnp.where(my_half == 0, small_oth, small).astype(f32)
    vecs = jnp.concatenate([low_part[:6], high_part[:6]], axis=1)
    qkv_rows = 6 + qkv_bias.shape[1] // half
    proj_b, down_b = vecs[4:5], vecs[5:6]
    qkv_b = jnp.concatenate([low_part[6:qkv_rows], high_part[6:qkv_rows]], axis=0).reshape(1, -1)
    up_b = jnp.concatenate([low_part[qkv_rows:], high_part[qkv_rows:]], axis=0).reshape(1, -1)

    local_rows = lax.axis_index("ctx") * tok_dev + jnp.arange(tok_dev, dtype=jnp.int32)
    query_pos = row_positions(block_pair, local_rows, tok_dev)
    key_pos = row_positions(block_pair, jnp.arange(count * tok_dev, dtype=jnp.int32), tok_dev)
    tab = rotary_table(query_pos, head_size)
    loc = block_places(block_pair, count)

    def exchange(vals):
        return lax.all_to_all(vals, "ctx", split_axis=0, concat_axis=0, tiled=True)

    rows_in = [inputs[i, 0] for i in range(micros)]
    cot_in = [cotangent[i, 0] for i in range(micros)]

    def norm_qkv(index, got):
        return qkv_call(rows_in[index], got, vecs, qkv_b, tab, wq, wq_oth, wsh)

    def mlp(made, save):
        return mlp_call(made[2], made[3], up_b, down_b, wu, wu_oth, wd, wd_oth, wsh, save)

    def mlp_back(dy, mlp_kept, after=(), limit=VMEM_LIMIT):
        return mlp_back_call(dy, mlp_kept[1], wu, wu_oth, wd, wd_oth, wsh, after, limit)

    def out_back(index, got, joined=None):
        return da_call(cot_in[index], got, wp, wp_oth, wsh, joined)

    def moved(vals):
        return exchange(vals) if one_pair_each else vals

    def attend(qkv, after=()):
        if one_pair_each:
            attended, lse = attend_call(qkv, loc, after)
            return attended, (qkv, lse)
        return wide_attend(qkv, query_pos, key_pos)

    def attend_back(kept, da, after=(), limit=VMEM_LIMIT):
        if one_pair_each:
            return attend_back_call(kept[0], da, kept[1], loc, after, limit)
        da = da[:, 0] if da.ndim == 4 else da
        return wide_attend_back(kept, da, query_pos, key_pos)

    def project(attended, made, mlp_out, after=(), limit=VMEM_LIMIT):
        return proj_call(attended, made[1], mlp_out[0], proj_b, wp, wp_oth, wsh, after, limit)

    def input_grad_of(dqkv, made, dy, dnm, after=(), limit=VMEM_LIMIT):
        return dx_call(dqkv, tab, made[1], dy, dnm, vecs, wq, wq_oth, wsh, after, limit)

    made_a = norm_qkv(0, None)
    qkv_a = moved(made_a[0])
    mlp_a = mlp(made_a, False)
    att_a, _ = attend(qkv_a, [mlp_a[0]])
    att_a = moved(att_a)
    da_a, dy_a = out_back(0, None)
    y_a = project(att_a, made_a, mlp_a, [dy_a])[0]
    da_a = moved(tied(y_a, da_a)[0])

    made_b = norm_qkv(1, pass_on(y_a, 1))
    qkv_2 = moved(tied(da_a, made_b[0])[0])
    norms_b = swap(made_b[3])
    mlp_b = mlp(made_b, True)
    _, dnm_a = mlp_back(dy_a, mlp_b)
    att_b, kept_b = attend(qkv_2, [dnm_a, norms_b])
    att_b = moved(att_b)
    gt_b = swap(mlp_b[3])
    dqkv_a_ = attend_back(kept_b, da_a, [gt_b])
    dqkv_a = moved(dqkv_a_)
    y_b, *a_b = project(att_b, made_b, mlp_b, [dqkv_a_])

    made_c = norm_qkv(0, pass_on(y_b, 1))
    qkv_3 = moved(tied(dqkv_a, made_c[0])[0])
    norms_c = swap(made_c[3])
    a_b_oth = swap(a_b[1])
    _, dx_a, _ = input_grad_of(dqkv_a, made_b, dy_a, dnm_a, [norms_c, a_b_oth])
    got_a = pass_on(dx_a, -1)
    mlp_c = mlp_call(
        made_c[2], tied(dx_a, made_c[3])[0], up_b, down_b, wu, wu_oth, wd, wd_oth, wsh, True
    )
    da_b, dy_b = out_back(1, tied(mlp_c[0], got_a)[0])
    da_b = moved(tied(qkv_3, da_b)[0])
    att_c, kept_c = attend(qkv_3, [dy_b])
    dy_b_oth, gt_c = swap(dy_b), swap(mlp_c[3])
    dqkv_b = attend_back(kept_c, da_b, [dy_b_oth, gt_c])
    dqkv_b_ = moved(dqkv_b)
    du_b, dnm_b = mlp_back(dy_b, mlp_c, [dqkv_b])
    du_b_oth = swap(du_b)
    back_b, dx_b, sums_b = input_grad_of(dqkv_b_, made_c, dy_b, dnm_b, [du_b_oth])
    got_b = pass_on(dx_b, -1)
    back_b_oth = swap(back_b)

    da_c, dy_c = out_back(0, tied(back_b_oth, got_b)[0], att_c if one_pair_each else None)
    dy_list = [dy_c, dy_b, swap(dy_c), dy_b_oth]
    da_c = moved(da_c)
    idx = ring_index("ctx")
    *down_made, dy_sum = down_grad_call(idx, [mlp_b[2], mlp_c[2], gt_b, gt_c], dy_list, count)
    down_ring = ring_sum(*down_made, (dim,), "ctx")
    token = next(down_ring)
    token = down_ring.send(token)
    du_c, dnm_c = mlp_back(dy_c, mlp_b, [token], TAIL_LIMIT)
    dqkv_c = attend_back(kept_b, da_c, [dnm_c], TAIL_LIMIT)
    token = down_ring.send(dqkv_c)
    dqkv_c = moved(dqkv_c)
    *up_made, du_sum = up_grad_call(
        idx,
        [made_b[2], made_c[2], norms_b, norms_c],
        [du_c, du_b, swap(du_c), du_b_oth],
        count,
        [token],
    )
    up_ring = ring_sum(*up_made, (up_made[0].shape[1],), "ctx")
    token = next(up_ring)
    steps = count + 1
    left = {down_ring: steps - 3, up_ring: steps - 1}
    results = {}

    def turn(ring, token):
        if not left[ring]:
            return token
        left[ring] -= 1
        made = ring.send(token)
        if left[ring] == 0:
            results[ring] = made
            return token
        return made

    token = turn(down_ring, token)
    token = turn(up_ring, token)
    back_c, dx_c, sums_c = input_grad_of(dqkv_c, made_b, dy_c, dnm_c, [token], TAIL_LIMIT)
    back_c_oth = swap(back_c)
    token = turn(down_ring, dx_c)
    y_c, *a_c = project(da_c if one_pair_each else att_c, made_c, mlp_c, [token], TAIL_LIMIT)
    a_c_oth = swap(a_c[1])
    token = turn(up_ring, y_c)
    token = turn(down_ring, token)
    norm_sums = sums_b + sums_c
    norm_own = lax.dynamic_slice_in_dim(norm_sums, my_half * half, half, 1)
    norm_oth = swap(lax.dynamic_slice_in_dim(norm_sums, (1 - my_half) * half, half, 1))

    def own_part(vec):
        size = vec.shape[1] // 2
        return lax.dynamic_slice_in_dim(vec, my_half * size, size, 1).reshape(-1, LANES)

    small = [(norm_own + norm_oth).reshape(-1, LANES), own_part(dy_sum), own_part(du_sum)]
    *attn_made, attn_sum = attn_grad_call(
        idx,
        wsh,
        [made_b[2], made_c[2], norms_b, norms_c],
        [a_b[0], a_c[0], a_b_oth, a_c_oth],
        [back_c, back_b, back_c_oth, back_b_oth],
        dy_list,
        jnp.concatenate(small, axis=0),
        count,
        [token],
    )
    attn_ring = ring_sum(*attn_made, (3 * dim, dim, LANES), "ctx")
    token = next(attn_ring)
    left[attn_ring] = steps - 1
    token = turn(down_ring, token)
    at = 0
    while any(left.values()):
        token = turn((up_ring, attn_ring, down_ring, attn_ring)[at % 4], token)
        at += 1
    (down_grad,) = results[down_ring]
    (up_grad,) = results[up_ring]
    qkv_grad, proj_grad, summed = results[attn_ring]

    sizes = [v.shape[0] for v in small] + [3 * dim // 2 // LANES]
    ends = [sum(sizes[: i + 1]) for i in range(4)]
    norm_grads, dy_total, up_b_grad, qkv_b_grad = (
        summed[end - size : end] for end, size in zip(ends, sizes)
    )
    norm_grads, dy_total = norm_grads.reshape(4, 1, half), dy_total.reshape(1, half)
    pick = lambda yes, no: jnp.where(first_section, yes, no)
    layer_out = jnp.stack([pick(y_c, y_b), pick(y_b, y_c)])[None, :, None]
    input_grad = jnp.stack([pick(dx_b, dx_c), pick(dx_c, dx_b)])[None, :, None]
    return (
        layer_out,
        input_grad,
        qkv_grad[None],
        qkv_b_grad.reshape(1, -1),
        proj_grad[None],
        dy_total,
        up_grad[None],
        up_b_grad.reshape(1, -1),
        down_grad[None],
        dy_total,
        norm_grads[0],
        norm_grads[1],
        norm_grads[2],
        norm_grads[3],
    )


def solution(mesh):
    in_specs = (
        P(None, "wsh", "ctx", None),
        P(None, "wsh", "ctx", None),
        P(),
        P("section", "wsh", None),
        P("section", "wsh"),
        P("section", "wsh", None),
        P("section", "wsh"),
        P("section", "wsh", None),
        P("section", "wsh"),
        P("section", "wsh", None),
        P("section", "wsh"),
        P("section", "wsh"),
        P("section", "wsh"),
        P("section", "wsh"),
        P("section", "wsh"),
    )
    out_specs = (
        P("section", None, "wsh", "ctx", None),
        P("section", None, "wsh", "ctx", None),
        P("section", "wsh", None),
        P("section", "wsh"),
        P("section", "wsh", None),
        P("section", "wsh"),
        P("section", "wsh", None),
        P("section", "wsh"),
        P("section", "wsh", None),
        P("section", "wsh"),
        P("section", "wsh"),
        P("section", "wsh"),
        P("section", "wsh"),
        P("section", "wsh"),
    )
    return jax.shard_map(body, mesh=mesh, in_specs=in_specs, out_specs=out_specs, check_vma=False)
```

```python
import functools

import jax
import jax.numpy as jnp
from jax import lax
from jax.experimental import pallas as pl
from jax.experimental.pallas import tpu as pltpu
from jax.sharding import PartitionSpec as P

HEADS = 16
ROT = 16
NORM_EPS = 1e-05
ROPE_BASE = 10000.0
MASKED_SCORE = -1e30
LANES = 128
VMEM_LIMIT = 50 * 1024 * 1024
TAIL_LIMIT = VMEM_LIMIT
RING_LIMIT = VMEM_LIMIT
INV_SQRT2 = 0.7071067811865476
INV_SQRT_2PI = 0.3989422804014327

f32 = jnp.float32
bf16 = jnp.bfloat16


def dot_nn(left, right):
    return lax.dot_general(left, right, (((1,), (0,)), ((), ())), preferred_element_type=f32)


def dot_nt(left, right):
    return lax.dot_general(left, right, (((1,), (1,)), ((), ())), preferred_element_type=f32)


def params_of(limit):
    return dict(
        compiler_params=pltpu.CompilerParams(vmem_limit_bytes=limit),
        cost_estimate=pl.CostEstimate(flops=1, bytes_accessed=1, transcendentals=0),
    )


def whole(shape):
    rank = len(shape)
    return pl.BlockSpec(shape, lambda *args: (0,) * rank)


def shape_of(shape, dtype):
    return jax.ShapeDtypeStruct(shape, dtype)


def rope(vals, tab_ref):
    return (
        vals * tab_ref[0]
        + pltpu.roll(vals, LANES - ROT // 2, 1) * tab_ref[1]
        + pltpu.roll(vals, ROT // 2, 1) * tab_ref[2]
    )


def unrope(vals, tab_ref):
    return (
        vals * tab_ref[0]
        - pltpu.roll(vals, LANES - ROT // 2, 1) * tab_ref[1]
        - pltpu.roll(vals, ROT // 2, 1) * tab_ref[2]
    )


def normalized(hidden):
    row_mean = jnp.mean(hidden, axis=-1, keepdims=True)
    centered = hidden - row_mean
    spread = jnp.mean(centered * centered, axis=-1, keepdims=True)
    scale = lax.rsqrt(spread + NORM_EPS)
    return centered * scale, scale


def start_all(copies):
    for copy in copies:
        copy.start()
    return copies


def wait_all(copies):
    for copy in copies:
        copy.wait()


def qkv_kernel(own_given, wsh_ref, inputs, weights, outputs, buf, sems):
    half, dim = buf.shape[2:]
    copies = start_all(
        [
            pltpu.make_async_copy(
                weight.at[:, pl.ds(part * dim, dim)], buf.at[part, side], sems.at[part, side]
            )
            for part in range(3)
            for side, weight in enumerate(weights)
        ]
    )
    out, x_out, own, oth = outputs
    x = inputs[0].ref()[...]
    if not own_given:
        x = jnp.where(wsh_ref[1] == 1, x, inputs[4].ref()[...])
    x_out.ref[...] = x
    x_out.send()
    xhat, _ = normalized(x.astype(f32))
    vec_ref, bias_ref, tab_ref = (item.ref() for item in inputs[1:4])
    na = (xhat * vec_ref[0:1] + vec_ref[1:2]).astype(bf16)
    nm = (xhat * vec_ref[2:3] + vec_ref[3:4]).astype(bf16)
    first = wsh_ref[0] == 0
    for i, rows in enumerate((na, nm)):
        own.ref[i] = jnp.where(first, rows[:, :half], rows[:, half:])
        oth.ref[i] = jnp.where(first, rows[:, half:], rows[:, :half])
    own.send()
    oth.send()
    for part in range(3):
        wait_all(copies[2 * part : 2 * part + 2])
        for at in range(0, dim, 2 * LANES):
            cols = slice(at, at + 2 * LANES)
            res = (
                dot_nn(own.ref[0], buf[part, 0, :, cols])
                + dot_nn(oth.ref[0], buf[part, 1, :, cols])
                + bias_ref[:, part * dim + at : part * dim + at + 2 * LANES]
            )
            for i in range(2):
                vals = res[:, i * LANES : (i + 1) * LANES]
                if part < 2:
                    vals = rope(vals, tab_ref)
                out.ref[at // LANES + i, part] = vals.astype(bf16)


def layer_of(shape, index):
    return pl.BlockSpec((pl.squeezed,) + shape, lambda *args: (index, 0, 0))


HERE = pl.BlockSpec(memory_space=pltpu.VMEM)
SCALARS = pl.BlockSpec(memory_space=pltpu.SMEM)
ANYWHERE = pl.BlockSpec(memory_space=pl.ANY)
IN_HBM = pl.BlockSpec(memory_space=pltpu.HBM)


class Arriving:
    def __init__(self, buf, copy=None):
        self.buf, self.copy = buf, copy

    def ref(self):
        if self.copy is not None:
            self.copy.wait()
            self.copy = None
        return self.buf


class Leaving:
    def __init__(self, buf, copy=None):
        self.ref, self.copy, self.sent = buf, copy, copy is None

    def send(self):
        if not self.sent:
            self.copy.start()
            self.sent = True


def local_kernel(body, near_in, near_out, scalars, weights, followed, *refs):
    refs = list(refs)

    def take(number):
        taken = refs[:number]
        del refs[:number]
        return taken

    scalar_refs, array_refs = take(scalars), take(len(near_in))
    weight_refs, _, out_refs = take(weights), take(followed), take(len(near_out))
    in_sems, out_sems = take(2)
    inputs, outputs = [], []
    for i, (near, ref) in enumerate(zip(near_in, array_refs)):
        if near:
            inputs.append(Arriving(ref))
        else:
            buf = take(1)[0]
            copy = pltpu.make_async_copy(ref, buf, in_sems.at[i])
            copy.start()
            inputs.append(Arriving(buf, copy))
    for i, (near, ref) in enumerate(zip(near_out, out_refs)):
        if near:
            outputs.append(Leaving(ref))
        else:
            buf = take(1)[0]
            outputs.append(Leaving(buf, pltpu.make_async_copy(buf, ref, out_sems.at[i])))
    body(*scalar_refs, inputs, weight_refs, outputs, *refs)
    for item in inputs:
        item.ref()
    for item in outputs:
        item.send()
    for item in outputs:
        if item.copy is not None:
            item.copy.wait()


def far(array):
    return (array,)


def local_call(body, name, scalars, arrays, weights, out_shape, scratch=(), after=(), limit=VMEM_LIMIT):
    near_in = [not isinstance(a, tuple) for a in arrays]
    near_out = [not isinstance(o, tuple) for o in out_shape]
    raw_out = [isinstance(o, list) for o in out_shape]
    arrays = [a if near else a[0] for a, near in zip(arrays, near_in)]
    shapes = [o if near and not raw else o[0] for o, near, raw in zip(out_shape, near_out, raw_out)]
    far_bufs = [
        pltpu.VMEM(a.shape, a.dtype)
        for a, near in zip(arrays + shapes, near_in + near_out)
        if not near
    ]
    return pl.pallas_call(
        functools.partial(
            local_kernel, body, near_in, near_out, len(scalars), len(weights), len(after)
        ),
        in_specs=[SCALARS] * len(scalars)
        + [HERE if near else IN_HBM for near in near_in]
        + [IN_HBM] * len(weights)
        + [ANYWHERE] * len(after),
        out_specs=[HERE if near and not raw else IN_HBM for near, raw in zip(near_out, raw_out)],
        out_shape=shapes,
        scratch_shapes=[
            pltpu.SemaphoreType.DMA((len(arrays) + 1,)),
            pltpu.SemaphoreType.DMA((len(shapes),)),
        ]
        + far_bufs
        + list(scratch),
        name=name,
        **params_of(limit),
    )(*scalars, *arrays, *weights, *after)


def qkv_call(given, got, vecs, qkv_b, tab, w_own, w_oth, wsh):
    rows, dim = given.shape
    half = w_own.shape[0]
    pairs = dim // LANES
    return local_call(
        functools.partial(qkv_kernel, got is None),
        "qkv_proj",
        [wsh],
        [given, vecs, qkv_b, tab] if got is None else [given, vecs, qkv_b, tab, got],
        [w_own, w_oth],
        [shape_of((pairs, 3, rows, LANES), bf16), shape_of((rows, dim), bf16)]
        + [shape_of((2, rows, half), bf16)] * 2,
        [pltpu.VMEM((3, 2, half, dim), bf16), pltpu.SemaphoreType.DMA((3, 2))],
    )


FF_TILE = 1024
FF_PIECE = 512


def ff_tiles(wsh_ref, up_own, up_oth, dn_own, dn_oth, up_buf, dn_buf, sems):
    own = dn_own.shape[0] // FF_TILE
    tiles = []
    for t in range(2 * own):
        start = pl.multiple_of(((wsh_ref[0] * own + t) % (2 * own)) * FF_TILE, FF_TILE)
        cols = pl.ds(start, FF_TILE)
        down = (dn_own if t < own else dn_oth).at[pl.ds((t % own) * FF_TILE, FF_TILE)]
        copies = [
            pltpu.make_async_copy(up_own.at[:, cols], up_buf.at[t, 0], sems.at[t, 0]),
            pltpu.make_async_copy(up_oth.at[:, cols], up_buf.at[t, 1], sems.at[t, 1]),
            pltpu.make_async_copy(down, dn_buf.at[t], sems.at[t, 2]),
        ]
        tiles.append((t, start, start_all(copies)))
    for t, start, copies in tiles:
        wait_all(copies)
        for at in range(0, FF_TILE, FF_PIECE):
            row = (t % own) * FF_TILE + at
            place = pl.ds(pl.multiple_of(start + at, FF_PIECE), FF_PIECE)
            yield t, place, t < own, slice(row, row + FF_PIECE), slice(at, at + FF_PIECE)


def ff_scratch(half, ff, dim):
    tiles = ff // FF_TILE
    return [
        pltpu.VMEM((tiles, 2, half, FF_TILE), bf16),
        pltpu.VMEM((tiles, FF_TILE, dim), bf16),
        pltpu.SemaphoreType.DMA((tiles, 3)),
    ]


def mlp_kernel(save, wsh_ref, inputs, weights, outputs, up_buf, dn_buf, sems):
    out_ref = outputs[0].ref
    started = False
    for t, place, held, rows, piece in ff_tiles(wsh_ref, *weights, up_buf, dn_buf, sems):
        own_ref, oth_ref, up_b, down_b = (item.ref() for item in inputs)
        if not started:
            out_ref[...] = jnp.broadcast_to(down_b[...], out_ref.shape)
            started = True
        pre = (
            dot_nn(own_ref[1], up_buf[t, 0, :, piece])
            + dot_nn(oth_ref[1], up_buf[t, 1, :, piece])
            + up_b[:, place]
        )
        gate = 0.5 + 0.5 * lax.erf(pre * INV_SQRT2)
        act = (pre * gate).astype(bf16)
        if save:
            slope = gate + pre * (INV_SQRT_2PI * jnp.exp(-0.5 * pre * pre))
            outputs[1].ref[place] = slope.astype(bf16).T
            outputs[2 if held else 3].ref[rows] = act.T
            if not held:
                outputs[2].send()
        out_ref[...] += dot_nn(act, dn_buf[t, piece])


def mlp_call(own, oth, up_b, down_b, up_own, up_oth, dn_own, dn_oth, wsh, save):
    rows, half = own.shape[1:]
    dim = dn_own.shape[1]
    ff = up_own.shape[1]
    out_shape = [shape_of((rows, dim), f32)]
    if save:
        out_shape += [shape_of((ff, rows), bf16)]
        out_shape += [shape_of((ff // 2, rows), bf16)] * 2
    return local_call(
        functools.partial(mlp_kernel, save),
        "mlp_forward",
        [wsh],
        [own, oth, up_b, down_b],
        [up_own, up_oth, dn_own, dn_oth],
        out_shape,
        ff_scratch(half, ff, dim),
    )


def mlp_back_kernel(wsh_ref, inputs, weights, outputs, acc_own, acc_oth, up_buf, dn_buf, sems):
    du, dnm = outputs
    half = acc_own.shape[0]
    acc_own[...] = jnp.zeros(acc_own.shape, f32)
    acc_oth[...] = jnp.zeros(acc_oth.shape, f32)
    for t, place, _, _, piece in ff_tiles(wsh_ref, *weights, up_buf, dn_buf, sems):
        dy_ref, slope_ref = (item.ref() for item in inputs)
        dact = dot_nt(dn_buf[t, piece], dy_ref[...])
        vals = (dact * slope_ref[place].astype(f32)).astype(bf16)
        du.ref[place] = vals
        acc_own[...] += dot_nn(up_buf[t, 0, :, piece], vals)
        acc_oth[...] += dot_nn(up_buf[t, 1, :, piece], vals)
    du.send()
    first = wsh_ref[0] == 0
    dnm.ref[:, :half] = jnp.where(first, acc_own[...], acc_oth[...]).T
    dnm.ref[:, half:] = jnp.where(first, acc_oth[...], acc_own[...]).T


def mlp_back_call(dy, slope, up_own, up_oth, dn_own, dn_oth, wsh, after, limit):
    rows, dim = dy.shape
    half, ff = up_own.shape
    return local_call(
        mlp_back_kernel,
        "mlp_backward",
        [wsh],
        [dy, slope],
        [up_own, up_oth, dn_own, dn_oth],
        [shape_of(slope.shape, bf16), shape_of((rows, dim), f32)],
        [pltpu.VMEM((half, rows), f32), pltpu.VMEM((half, rows), f32)] + ff_scratch(half, ff, dim),
        after,
        limit,
    )


def sort_in(loc_ref, ref, dst, half_rows, part=None):
    for block in range(dst.shape[0] // half_rows):
        place = loc_ref[block]
        rows = pl.ds(pl.multiple_of((place % 2) * half_rows, half_rows), half_rows)
        if part is None:
            vals = ref[place // 2, rows, :]
        else:
            vals = ref[place // 2, part, rows, :]
        dst[block * half_rows : (block + 1) * half_rows] = vals


def sort_out(loc_ref, vals, ref, half_rows, part=None):
    for block in range(vals.shape[0] // half_rows):
        place = loc_ref[block]
        rows = pl.ds(pl.multiple_of((place % 2) * half_rows, half_rows), half_rows)
        piece = vals[block * half_rows : (block + 1) * half_rows]
        if part is None:
            ref[place // 2, rows, :] = piece
        else:
            ref[place // 2, part, rows, :] = piece


def head_of(vals, head):
    lane = lax.broadcasted_iota(jnp.int32, vals.shape, 1)
    return jnp.where(lane // (LANES // 2) == head, vals, jnp.zeros_like(vals))


def scores_of(keys, queries, scale, diagonal):
    scores = dot_nt(keys, queries) * scale
    if diagonal:
        key_at = lax.broadcasted_iota(jnp.int32, scores.shape, 0)
        query_at = lax.broadcasted_iota(jnp.int32, scores.shape, 1)
        scores = jnp.where(key_at <= query_at, scores, MASKED_SCORE)
    return scores


def attend_kernel(tile, loc_ref, inputs, weights, outputs, q_s, k_s, v_s, vt_s, o_s):
    qkv_ref = inputs[0].ref()
    o_ref, lse_ref = (item.ref for item in outputs)
    half_rows = qkv_ref.shape[2] // 2
    seq = q_s.shape[0]
    head_size = LANES // 2
    scale = head_size**-0.5
    sort_in(loc_ref, qkv_ref, q_s, half_rows, 0)
    sort_in(loc_ref, qkv_ref, k_s, half_rows, 1)
    sort_in(loc_ref, qkv_ref, v_s, half_rows, 2)
    vt_s[...] = v_s[...].T
    for t in range(seq // tile):
        rows = slice(t * tile, (t + 1) * tile)
        queries = q_s[rows]
        outs = []
        for head in range(2):
            picked = head_of(queries, head)
            parts = [
                scores_of(k_s[i * tile : (i + 1) * tile], picked, scale, i == t)
                for i in range(t + 1)
            ]
            top = functools.reduce(
                jnp.maximum, [jnp.max(p, axis=0, keepdims=True) for p in parts]
            )
            parts = [jnp.exp(p - top) for p in parts]
            total = sum(jnp.sum(p, axis=0, keepdims=True) for p in parts)
            lse_ref[head : head + 1, rows] = top + jnp.log(total)
            inverse = 1.0 / total
            acc = None
            for i, p in enumerate(parts):
                term = dot_nn(
                    vt_s[head * head_size : (head + 1) * head_size, i * tile : (i + 1) * tile],
                    (p * inverse).astype(bf16),
                )
                acc = term if acc is None else acc + term
            outs.append(acc)
        o_s[rows] = jnp.concatenate(outs, axis=0).T.astype(bf16)
    sort_out(loc_ref, o_s, o_ref, half_rows)


def attend_call(qkv, loc, after):
    count, _, rows, _ = qkv.shape
    seq = count * rows
    return local_call(
        functools.partial(attend_kernel, 256),
        "attention",
        [loc],
        [qkv],
        [],
        [shape_of((count, rows, LANES), bf16), shape_of((2, seq), f32)],
        [
            pltpu.VMEM((seq, LANES), bf16),
            pltpu.VMEM((seq, LANES), bf16),
            pltpu.VMEM((seq, LANES), bf16),
            pltpu.VMEM((LANES, seq), bf16),
            pltpu.VMEM((seq, LANES), bf16),
        ],
        after,
    )


def attend_back_kernel(
    tile, part, loc_ref, inputs, weights, outputs, q_s, k_s, v_s, da_s, kt_s, dq_s, dk_s, dv_s
):
    da_ref, qkv_ref, lse_ref = (item.ref() for item in inputs)
    out_ref = outputs[0].ref
    half_rows = qkv_ref.shape[2] // 2
    seq = q_s.shape[0]
    head_size = LANES // 2
    scale = head_size**-0.5
    sort_in(loc_ref, qkv_ref, q_s, half_rows, 0)
    sort_in(loc_ref, qkv_ref, k_s, half_rows, 1)
    sort_in(loc_ref, qkv_ref, v_s, half_rows, 2)
    sort_in(loc_ref, da_ref, da_s, half_rows, part)
    kt_s[...] = k_s[...].T
    dk_s[...] = jnp.zeros(dk_s.shape, f32)
    dv_s[...] = jnp.zeros(dv_s.shape, f32)
    for t in range(seq // tile):
        rows = slice(t * tile, (t + 1) * tile)
        outs = []
        for head in range(2):
            queries = head_of(q_s[rows], head)
            grads = head_of(da_s[rows], head)
            lse = lse_ref[head : head + 1, rows]
            probs, dprobs, row_dot = [], [], 0.0
            for i in range(t + 1):
                keys = slice(i * tile, (i + 1) * tile)
                p = jnp.exp(scores_of(k_s[keys], queries, scale, i == t) - lse)
                dp = dot_nt(v_s[keys], grads)
                row_dot = row_dot + jnp.sum(p * dp, axis=0, keepdims=True)
                dv_s[keys] += dot_nn(p.astype(bf16), grads)
                probs.append(p)
                dprobs.append(dp)
            acc = None
            for i in range(t + 1):
                keys = slice(i * tile, (i + 1) * tile)
                ds = (probs[i] * (dprobs[i] - row_dot) * scale).astype(bf16)
                dk_s[keys] += dot_nn(ds, queries)
                term = dot_nn(kt_s[head * head_size : (head + 1) * head_size, keys], ds)
                acc = term if acc is None else acc + term
            outs.append(acc)
        dq_s[rows] = jnp.concatenate(outs, axis=0).T.astype(bf16)
    sort_out(loc_ref, dq_s, out_ref, half_rows, 0)
    k_s[...] = dk_s[...].astype(bf16)
    v_s[...] = dv_s[...].astype(bf16)
    sort_out(loc_ref, k_s, out_ref, half_rows, 1)
    sort_out(loc_ref, v_s, out_ref, half_rows, 2)


def attend_back_call(qkv, da, lse, loc, after, limit):
    count, _, rows, _ = qkv.shape
    seq = count * rows
    part = 0 if da.ndim == 4 else None
    (res,) = local_call(
        functools.partial(attend_back_kernel, 256, part),
        "attention_backward",
        [loc],
        [da, qkv, lse],
        [],
        [shape_of(qkv.shape, bf16)],
        [pltpu.VMEM((seq, LANES), bf16)] * 4
        + [pltpu.VMEM((LANES, seq), bf16), pltpu.VMEM((seq, LANES), bf16)]
        + [pltpu.VMEM((seq, LANES), f32)] * 2,
        after,
        limit,
    )
    return res


def by_head(parts):
    pairs, rows, lanes = parts.shape
    return jnp.transpose(parts, (1, 0, 2)).reshape(rows, HEADS, pairs * lanes // HEADS)


def by_pair(heads):
    rows = heads.shape[0]
    return jnp.transpose(heads.reshape(rows, -1, LANES), (1, 0, 2))


def wide_scores(queries, keys, query_pos, key_pos):
    raw = jnp.einsum("qhd,khd->hqk", queries, keys, preferred_element_type=f32)
    allowed = (query_pos[:, None] >= key_pos[None, :])[None]
    return jnp.where(allowed, raw * queries.shape[-1] ** (-0.5), MASKED_SCORE)


def key_blocks(arrays, rows):
    return tuple(a.reshape((a.shape[0] // rows, rows) + a.shape[1:]) for a in arrays)


def wide_attend(qkv, query_pos, key_pos):
    queries = by_head(qkv[:, 0])
    keys = lax.all_gather(by_head(qkv[:, 1]), "ctx", axis=0, tiled=True)
    values = lax.all_gather(by_head(qkv[:, 2]), "ctx", axis=0, tiled=True)
    block = min(512, keys.shape[0])
    split = key_blocks((keys, values, key_pos), block)
    rows, _, head_size = queries.shape

    def max_step(carry, block_in):
        top, total = carry
        scores = wide_scores(queries, block_in[0], query_pos, block_in[2])
        new_top = jnp.maximum(top, jnp.max(scores, axis=-1))
        part = jnp.sum(jnp.exp(scores - new_top[..., None]), axis=-1)
        return ((new_top, total * jnp.exp(top - new_top) + part), None)

    start = (jnp.full((HEADS, rows), MASKED_SCORE, f32), jnp.zeros((HEADS, rows), f32))
    (top, total), _ = lax.scan(max_step, start, split)
    lse = top + jnp.log(total)

    def value_step(running, block_in):
        scores = wide_scores(queries, block_in[0], query_pos, block_in[2])
        probs = jnp.exp(scores - lse[..., None]).astype(bf16)
        term = jnp.einsum("hqk,khd->qhd", probs, block_in[1], preferred_element_type=f32)
        return (running + term, None)

    attended, _ = lax.scan(value_step, jnp.zeros((rows, HEADS, head_size), f32), split)
    return by_pair(attended.astype(bf16)), (queries, keys, values, lse)


def wide_attend_back(kept, da, query_pos, key_pos):
    queries, keys, values, lse = kept
    grads = by_head(da)
    block = min(512, keys.shape[0])
    split = key_blocks((keys, values, key_pos), block)
    scale = queries.shape[-1] ** (-0.5)

    def pieces(block_in):
        scores = wide_scores(queries, block_in[0], query_pos, block_in[2])
        probs = jnp.exp(scores - lse[..., None])
        dprobs = jnp.einsum("qhd,khd->hqk", grads, block_in[1], preferred_element_type=f32)
        return probs, dprobs

    def dot_step(running, block_in):
        probs, dprobs = pieces(block_in)
        return (running + jnp.sum(probs * dprobs, axis=-1), None)

    row_dot, _ = lax.scan(dot_step, jnp.zeros(lse.shape, f32), split)

    def key_step(running, block_in):
        probs, dprobs = pieces(block_in)
        ds = (scale * probs * (dprobs - row_dot[..., None])).astype(bf16)
        running = running + jnp.einsum("hqk,khd->qhd", ds, block_in[0], preferred_element_type=f32)
        dk = jnp.einsum("hqk,qhd->khd", ds, queries, preferred_element_type=f32)
        dv = jnp.einsum("hqk,qhd->khd", probs.astype(bf16), grads, preferred_element_type=f32)
        return (running, (dk.astype(bf16), dv.astype(bf16)))

    dq, (dk, dv) = lax.scan(key_step, jnp.zeros(queries.shape, f32), split)
    dk, dv = (
        lax.psum_scatter(part.reshape(keys.shape), "ctx", scatter_dimension=0, tiled=True)
        for part in (dk, dv)
    )
    return jnp.stack([by_pair(dq.astype(bf16)), by_pair(dk), by_pair(dv)], axis=1)


def lanes_of(ref):
    return jnp.concatenate([ref[i] for i in range(ref.shape[0])], axis=1)


def both_halves(w_own, w_oth, buf, sems):
    return start_all(
        [
            pltpu.make_async_copy(weight, buf.at[side], sems.at[side])
            for side, weight in enumerate((w_own, w_oth))
        ]
    )


def half_scratch(weight):
    return [pltpu.VMEM((2,) + weight.shape, bf16), pltpu.SemaphoreType.DMA((2,))]


def proj_kernel(part, wsh_ref, inputs, weights, outputs, buf, sems):
    copies = both_halves(*weights, buf, sems)
    y, own, oth = outputs
    half = buf.shape[1]
    first = wsh_ref[0] == 0
    a_ref = inputs[0].ref()
    a = lanes_of(a_ref if part is None else a_ref.at[:, part])
    own.ref[...] = jnp.where(first, a[:, :half], a[:, half:])
    oth.ref[...] = jnp.where(first, a[:, half:], a[:, :half])
    own.send()
    oth.send()
    bias_ref, x_ref, mlp_ref = (item.ref() for item in inputs[1:])
    wait_all(copies)
    attn = dot_nn(own.ref[...], buf[0]) + dot_nn(oth.ref[...], buf[1]) + bias_ref[...]
    y.ref[...] = (x_ref[...].astype(f32) + attn + mlp_ref[...]).astype(bf16)


def proj_call(a, x, mlp, bias, p_own, p_oth, wsh, after, limit):
    rows, dim = x.shape
    half = p_own.shape[0]
    return local_call(
        functools.partial(proj_kernel, 1 if a.ndim == 4 else None),
        "attn_out",
        [wsh],
        [a, bias, x, mlp],
        [p_own, p_oth],
        [shape_of((rows, dim), bf16)] + [shape_of((rows, half), bf16)] * 2,
        half_scratch(p_own),
        after,
        limit,
    )


def da_kernel(own_given, wsh_ref, inputs, weights, outputs, buf, sems):
    copies = both_halves(*weights, buf, sems)
    out_ref, dy_out = outputs[0].ref, outputs[1]
    dy = inputs[0].ref()[...]
    if not own_given:
        dy = jnp.where(wsh_ref[1] == 1, inputs[1].ref()[...], dy)
    dy_out.ref[...] = dy
    dy_out.send()
    wsh = wsh_ref[0]
    joined = len(out_ref.shape) == 4
    if joined:
        out_ref[:, 1] = inputs[2].ref()[...]
    count = out_ref.shape[0] // 2
    for place, side in ((wsh * count, 0), ((1 - wsh) * count, 1)):
        copies[side].wait()
        part = dot_nt(dy, buf[side]).astype(bf16)
        for i in range(count):
            vals = part[:, i * LANES : (i + 1) * LANES]
            if joined:
                out_ref[place + i, 0] = vals
            else:
                out_ref[place + i] = vals


def da_call(given, got, p_own, p_oth, wsh, joined=None):
    rows, dim = given.shape
    pairs = dim // LANES
    arrays = [given] + ([] if got is None else [got])
    arrays += [] if joined is None else [joined]
    shape = (pairs, rows, LANES) if joined is None else (pairs, 2, rows, LANES)
    return local_call(
        functools.partial(da_kernel, got is None),
        "attn_out_backward",
        [wsh],
        arrays,
        [p_own, p_oth],
        [shape_of(shape, bf16), shape_of((rows, dim), bf16)],
        half_scratch(p_own),
    )


def dx_kernel(wsh_ref, inputs, weights, outputs, grad_s, buf, sems):
    copies = both_halves(*weights, buf, sems)
    back, dx, sums = outputs
    dqkv_ref, tab_ref = inputs[0].ref(), inputs[1].ref()
    pairs = dqkv_ref.shape[0]
    for part in range(3):
        for pair in range(pairs):
            vals = dqkv_ref[pair, part]
            if part < 2:
                vals = unrope(vals.astype(f32), tab_ref).astype(bf16)
            back.ref[pair, part] = vals
            grad_s[:, pl.ds((part * pairs + pair) * LANES, LANES)] = vals
    back.send()
    vec_ref, x_ref, dy_ref, dnm_ref = (item.ref() for item in inputs[2:])
    first = wsh_ref[0] == 0
    copies[0].wait()
    own = dot_nt(grad_s[...], buf[0])
    copies[1].wait()
    oth = dot_nt(grad_s[...], buf[1])
    dna = jnp.concatenate([jnp.where(first, own, oth), jnp.where(first, oth, own)], axis=1)
    dnm = dnm_ref[...]
    xhat, scale = normalized(x_ref[...].astype(f32))
    grad = dna * vec_ref[0:1] + dnm * vec_ref[2:3]
    inner = (
        grad
        - jnp.mean(grad, axis=-1, keepdims=True)
        - xhat * jnp.mean(grad * xhat, axis=-1, keepdims=True)
    )
    dx.ref[...] = (dy_ref[...].astype(f32) + scale * inner).astype(bf16)
    dx.send()
    sums.ref[0:1] = jnp.sum(dna * xhat, axis=0, keepdims=True)
    sums.ref[1:2] = jnp.sum(dna, axis=0, keepdims=True)
    sums.ref[2:3] = jnp.sum(dnm * xhat, axis=0, keepdims=True)
    sums.ref[3:4] = jnp.sum(dnm, axis=0, keepdims=True)


def dx_call(dqkv, tab, x, dy, dnm, vecs, w_own, w_oth, wsh, after, limit):
    rows, dim = x.shape
    return local_call(
        dx_kernel,
        "section_input_grad",
        [wsh],
        [dqkv, tab, vecs, x, dy, dnm],
        [w_own, w_oth],
        [shape_of(o, t) for o, t in ((dqkv.shape, bf16), ((rows, dim), bf16), ((4, dim), f32))],
        [pltpu.VMEM((rows, 3 * dim), bf16)] + half_scratch(w_own),
        after,
        limit,
    )


def joined_rows(items):
    return jnp.concatenate([item.ref()[...] for item in items], axis=0)


class Pieces:
    def __init__(self, out_ref, buf, sems):
        self.out_ref, self.buf, self.sems, self.copies = out_ref, buf, sems, []

    def put(self, rows, cols, vals):
        self.buf[rows, cols] = vals.astype(bf16)
        at = len(self.copies)
        self.copies.append(
            pltpu.make_async_copy(
                self.buf.at[rows, cols], self.out_ref.at[rows, cols], self.sems.at[at]
            )
        )
        self.copies[-1].start()

    def finish(self, chunk, ahead, behind):
        height, cut = ahead.ref.shape
        rows = pl.ds(pl.multiple_of(chunk * height, height), height)
        ahead.ref[...] = self.buf[rows, :cut]
        ahead.send()
        behind.ref[...] = self.buf[rows, cut:]
        behind.send()
        wait_all(self.copies)


def first_half(cols):
    return cols // 2 // LANES * LANES


def grad_call(body, name, scalars, arrays, shape, width, count, scratch, after):
    cut = first_half(shape[1])
    halves = [far(shape_of((shape[0] // count, c), bf16)) for c in (cut, shape[1] - cut)]
    return local_call(
        functools.partial(body, len(arrays)),
        name,
        scalars,
        arrays,
        [],
        [[shape_of(shape, bf16)]] + halves + [far(shape_of((1, width), f32))],
        [pltpu.VMEM(shape, bf16), pltpu.SemaphoreType.DMA((5,))] + scratch,
        after,
        TAIL_LIMIT,
    )


def parts_of(items, number):
    size = len(items) // number
    return [items[i * size : (i + 1) * size] for i in range(number)]


def down_grad_kernel(number, idx_ref, inputs, weights, outputs, buf, sems):
    gts, dys = parts_of(inputs, 2)
    out = Pieces(outputs[0].ref, buf, sems)
    dy = joined_rows(dys)
    outputs[3].ref[...] = jnp.sum(dy.astype(f32), axis=0, keepdims=True)
    rows, dim = buf.shape
    tile = rows // 4
    for t in range(4):
        part = slice(t * tile, (t + 1) * tile)
        left = jnp.concatenate([item.ref()[part] for item in gts], axis=1)
        out.put(part, slice(0, dim), dot_nn(left, dy))
    out.finish(idx_ref[idx_ref.shape[0] // 2], outputs[1], outputs[2])


def down_grad_call(idx, gt_list, dy_list, count):
    dim = dy_list[0].shape[1]
    return grad_call(
        down_grad_kernel,
        "down_grad",
        [idx],
        [far(a) for a in gt_list + dy_list],
        (gt_list[0].shape[0], dim),
        dim,
        count,
        [],
        [],
    )


def up_grad_kernel(number, idx_ref, inputs, weights, outputs, buf, sems):
    norms, dus = parts_of(inputs, 2)
    out = Pieces(outputs[0].ref, buf, sems)
    left = jnp.concatenate([item.ref()[1] for item in norms], axis=0).T
    rows, ff = buf.shape
    tile = ff // 4
    for t in range(4):
        part = slice(t * tile, (t + 1) * tile)
        du = jnp.concatenate([item.ref()[part] for item in dus], axis=1)
        outputs[3].ref[:, part] = dot_nt(jnp.ones((8, du.shape[1]), bf16), du)[:1]
        out.put(slice(0, rows), part, dot_nt(left, du))
    out.finish(idx_ref[idx_ref.shape[0] // 2], outputs[1], outputs[2])


def up_grad_call(idx, norm_list, du_list, count, after):
    half, ff = norm_list[0].shape[2], du_list[0].shape[0]
    return grad_call(
        up_grad_kernel,
        "up_grad",
        [idx],
        [far(a) for a in norm_list + du_list],
        (half, ff),
        ff,
        count,
        [],
        after,
    )


def attn_grad_kernel(number, idx_ref, wsh_ref, inputs, weights, outputs, buf, sems, small_s):
    norms, outs, dqkvs, dys = parts_of(inputs[:-1], 4)
    out = Pieces(outputs[0].ref, buf, sems)
    sums = outputs[3].ref
    rows, dim = buf.shape[0], sums.shape[1] // 4
    left = jnp.concatenate([item.ref()[0] for item in norms], axis=0).T
    for part in range(4):
        cols = slice(part * dim, (part + 1) * dim)
        if part < 3:
            right = jnp.concatenate([lanes_of(item.ref().at[:, part]) for item in dqkvs], axis=0)
        else:
            left, right = joined_rows(outs).T, joined_rows(dys)
        sums[:, cols] = jnp.sum(right.astype(f32), axis=0, keepdims=True)
        out.put(slice(0, rows), cols, dot_nn(left, right))
    given = inputs[-1].ref()
    at = given.shape[0]
    small_s[:at] = given[...]
    base = wsh_ref[0] * (3 * dim // 2)
    for i in range(3 * dim // 2 // LANES):
        place = pl.ds(pl.multiple_of(base + i * LANES, LANES), LANES)
        small_s[at + i : at + i + 1] = sums[:, place]
    small = small_s[...]
    empty = jnp.zeros((rows - small.shape[0], LANES), f32)
    out.put(slice(0, rows), slice(4 * dim, 4 * dim + LANES), jnp.concatenate([small, empty], axis=0))
    out.finish(idx_ref[idx_ref.shape[0] // 2], outputs[1], outputs[2])


def attn_grad_call(idx, wsh, norm_list, out_list, dqkv_list, dy_list, small, count, after):
    half, dim = norm_list[0].shape[2], dy_list[0].shape[1]
    return grad_call(
        attn_grad_kernel,
        "attn_grad",
        [idx, wsh],
        [far(a) for a in norm_list + out_list + dqkv_list + dy_list] + [small],
        (half, 4 * dim + LANES),
        4 * dim,
        count,
        [pltpu.VMEM((small.shape[0] + 3 * dim // 2 // LANES, LANES), f32)],
        after,
    )


def ring_of(count):
    return list(range(0, count, 2)) + list(range(count - 1, 0, -2))


def ring_place(axis):
    count = lax.axis_size(axis)
    me = lax.axis_index(axis)
    return jnp.where(me % 2 == 0, me // 2, count - (me + 1) // 2)


def ring_index(axis):
    count = lax.axis_size(axis)
    return (ring_place(axis) + jnp.arange(count, dtype=jnp.int32)) % count


def ring_shift(vals, axis, by):
    order = ring_of(lax.axis_size(axis))
    count = len(order)
    pairs = [(order[i], order[(i + by) % count]) for i in range(count)]
    return lax.ppermute(vals, axis, pairs)


def tied(token, *vals):
    return lax.optimization_barrier((token, vals))[1]


def fetch(idx_ref, slots, own_ref, bufs, sems):
    return start_all(
        [
            pltpu.make_async_copy(own_ref.at[idx_ref[slot]], bufs.at[i], sems.at[i])
            for i, slot in enumerate(slots)
        ]
    )


def low_total(*terms):
    total = terms[0].astype(f32)
    for term in terms[1:]:
        total = total + term.astype(f32)
    return total.astype(bf16)


def ring_add_kernel(slots, idx_ref, inputs, own_refs, outputs, bufs, sems):
    copies = fetch(idx_ref, slots, own_refs[0], bufs, sems)
    for i, item in enumerate(outputs):
        copies[i].wait()
        got = inputs[i].ref()
        cols, cut = item.ref.shape[1], got.shape[1]
        summed = slice(0, cut) if i == 0 else slice(cols - cut, cols)
        item.ref[:, summed] = low_total(bufs[i, :, summed], got[...])
        if cut < cols:
            rest = slice(cut, cols) if i == 0 else slice(0, cols - cut)
            item.ref[:, rest] = bufs[i, :, rest]
        item.send()


def put_copies(chunk, cols, buf, totals, starts, sem):
    lo, hi = cols, cols + buf.shape[1]
    copies = []
    for i, (total, start) in enumerate(zip(totals, starts)):
        first, last = max(lo, start), min(hi, start + total.shape[2])
        if first < last:
            copies.append(
                pltpu.make_async_copy(
                    buf.at[:, pl.ds(first - lo, last - first)],
                    total.at[chunk, :, pl.ds(first - start, last - first)],
                    sem.at[i],
                )
            )
    return copies


def ring_own_kernel(slots, idx_ref, inputs, own_refs, outputs, bufs, sems):
    wait_all(fetch(idx_ref, slots, own_refs[0], bufs, sems))
    outputs[0].ref[...] = low_total(bufs[0], inputs[0].ref()[...], inputs[1].ref()[...])


def ring_put_kernel(starts, slots, cols, fresh, onward, idx_ref, *refs):
    number = len(slots)
    pieces = refs[:number]
    wide, sems, pass_buf, pass_sems = refs[-4:]
    passed = refs[-4 - onward : -4]
    totals = refs[-4 - onward - len(starts) : -4 - onward]
    leaving = []
    for i, ref in enumerate(passed):
        width = ref.shape[1]
        pass_buf[i, :, :width] = pieces[i][:, :width] if i == 0 else pieces[i][:, -width:]
        leaving += start_all(
            [pltpu.make_async_copy(pass_buf.at[i, :, pl.ds(0, width)], ref, pass_sems.at[i])]
        )
    for i in range(number):
        part = pl.ds(0, pieces[i].shape[1])
        wide[i, :, part] = pieces[i][...].astype(f32)
        leaving += start_all(
            put_copies(
                idx_ref[slots[i]], cols[i], wide.at[i, :, part], totals, starts, sems.at[i]
            )
        )
    wait_all(leaving)


def ring_sum(own, ahead, behind, widths, axis):
    count = lax.axis_size(axis)
    half = count // 2
    full_rows, cols = own.shape
    rows = full_rows // count
    own = own.reshape(count, rows, cols)
    cut = ahead.shape[1]
    starts = [sum(widths[:i]) for i in range(len(widths))]
    idx = ring_index(axis)
    chunk = shape_of((rows, cols), bf16)
    halves = [shape_of((rows, cut), bf16), shape_of((rows, cols - cut), bf16)]
    sums = [shape_of((count, rows, width), f32) for width in widths]

    def taken(number):
        return [pltpu.VMEM((number, rows, cols), bf16), pltpu.SemaphoreType.DMA((number,))]

    def put(totals, pieces, slots, passed, after):
        number = len(pieces)
        first_cols = (0,) * number if pieces[0].shape[1] == cols else (0, cut)
        fresh = totals is None
        out = pl.pallas_call(
            functools.partial(
                ring_put_kernel,
                starts,
                tuple(k % count for k in slots),
                first_cols,
                fresh,
                len(passed),
            ),
            in_specs=[SCALARS]
            + [HERE] * number
            + [IN_HBM] * (0 if fresh else len(sums))
            + [ANYWHERE] * len(after),
            out_specs=[IN_HBM] * (len(sums) + len(passed)),
            out_shape=sums + passed,
            scratch_shapes=[
                pltpu.VMEM((number, rows, cols), f32),
                pltpu.SemaphoreType.DMA((number, len(sums))),
                pltpu.VMEM((2, rows, cols), bf16),
                pltpu.SemaphoreType.DMA((2,)),
            ],
            input_output_aliases={} if fresh else {1 + number + i: i for i in range(len(sums))},
            name="ring_put",
            **params_of(RING_LIMIT),
        )(idx, *pieces, *([] if fresh else totals), *after)
        return out[: len(sums)], out[len(sums) :]

    def both_ways(ahead, behind):
        return ring_shift(ahead, axis, 1), ring_shift(behind, axis, -1)

    token = behind
    ahead, behind = both_ways(ahead, behind)
    token = yield token
    for k in range(half - 1, 0, -1):
        ahead, behind = local_call(
            functools.partial(ring_add_kernel, (k % count, (-k) % count)),
            "ring_add",
            [idx],
            [ahead, behind],
            [own],
            [chunk, chunk],
            taken(2),
            [token],
            RING_LIMIT,
        )
        token = behind
        ahead, behind = both_ways(ahead, behind)
        token = yield token
    (mine,) = local_call(
        functools.partial(ring_own_kernel, (0,)),
        "ring_own",
        [idx],
        [ahead, behind],
        [own],
        [chunk],
        taken(1),
        [token],
        RING_LIMIT,
    )
    ahead, behind = both_ways(mine, mine)
    totals, (token,) = put(None, [mine], [0], [shape_of((rows, LANES), bf16)], [])
    token = yield token
    for k in range(1, half):
        passed = halves if k == half - 1 else [chunk, chunk]
        totals, passed = put(totals, [ahead, behind], [-k, k], passed, [token])
        token = passed[1]
        ahead, behind = both_ways(*passed)
        token = yield token
    totals, _ = put(totals, [ahead, behind], [-half, half], [], [token])
    yield [total.reshape(full_rows, -1) for total in totals]


def swap(vals):
    return lax.ppermute(vals, "wsh", [(0, 1), (1, 0)])


def pass_on(vals, by):
    pairs = [(0, 1)] if by > 0 else [(1, 0)]
    return lax.ppermute(vals, "section", pairs)


def block_places(block_pair, count):
    want = jnp.arange(2 * count, dtype=jnp.int32)
    device = jnp.arange(count, dtype=jnp.int32)
    first = (block_pair[None, :] == want[:, None]).astype(jnp.int32)
    second = ((2 * count - 1 - block_pair)[None, :] == want[:, None]).astype(jnp.int32)
    return jnp.sum(first * (2 * device) + second * (2 * device + 1), axis=1)


def row_positions(block_pair, stored, tok_dev):
    count = block_pair.shape[0]
    device = stored // tok_dev
    within = stored % tok_dev
    half_rows = tok_dev // 2
    matches = device[:, None] == jnp.arange(count, dtype=jnp.int32)[None, :]
    pair_block = jnp.sum(jnp.where(matches, block_pair[None, :], 0), axis=1)
    block_idx = jnp.where(within < half_rows, pair_block, 2 * count - 1 - pair_block)
    return block_idx * half_rows + within % half_rows


def rotary_table(positions, head_size):
    half_rot = ROT // 2
    lane = jnp.arange(LANES, dtype=jnp.int32) % head_size
    inv_freq = ROPE_BASE ** (-((lane % half_rot).astype(f32) * 2.0) / ROT)
    angles = positions.astype(f32)[:, None] * inv_freq[None, :]
    cosine, sine = jnp.cos(angles), jnp.sin(angles)
    lead, second = (lane < half_rot)[None], ((lane >= half_rot) & (lane < ROT))[None]
    return jnp.stack(
        [
            jnp.where(lead | second, cosine, 1.0),
            jnp.where(lead, -sine, 0.0),
            jnp.where(second, sine, 0.0),
        ]
    )


def body(
    inputs,
    cotangent,
    block_pair,
    qkv_weight,
    qkv_bias,
    proj_weight,
    proj_bias,
    up_weight,
    up_bias,
    down_weight,
    down_bias,
    attn_gain,
    attn_shift,
    mlp_gain,
    mlp_shift,
):
    first_section = lax.axis_index("section") == 0
    count = lax.axis_size("ctx")
    micros, _, tok_dev, dim = inputs.shape
    head_size = dim // HEADS
    half = dim // 2
    my_half = lax.axis_index("wsh")
    wsh = jnp.stack([my_half.astype(jnp.int32), first_section.astype(jnp.int32)])
    one_pair_each = count == dim // LANES

    wq, wp, wu, wd = (w[0] for w in (qkv_weight, proj_weight, up_weight, down_weight))
    small = jnp.concatenate(
        [
            v[0].reshape(-1, half)
            for v in (
                attn_gain,
                attn_shift,
                mlp_gain,
                mlp_shift,
                proj_bias,
                down_bias,
                qkv_bias,
                up_bias,
            )
        ],
        axis=0,
    )
    small_oth = swap(small)
    wq_oth = swap(wq)
    first_here = lax.optimization_barrier((wq_oth, small_oth))
    wq_oth, small_oth = first_here
    wu_oth = swap(tied(wq_oth, wu)[0])
    wd_oth = swap(tied(wq_oth, wd)[0])
    wp_oth = swap(tied(wu_oth, wp)[0])
    low_part = jnp.where(my_half == 0, small, small_oth).astype(f32)
    high_part = jnp.where(my_half == 0, small_oth, small).astype(f32)
    vecs = jnp.concatenate([low_part[:6], high_part[:6]], axis=1)
    qkv_rows = 6 + qkv_bias.shape[1] // half
    proj_b, down_b = vecs[4:5], vecs[5:6]
    qkv_b = jnp.concatenate([low_part[6:qkv_rows], high_part[6:qkv_rows]], axis=0).reshape(1, -1)
    up_b = jnp.concatenate([low_part[qkv_rows:], high_part[qkv_rows:]], axis=0).reshape(1, -1)

    local_rows = lax.axis_index("ctx") * tok_dev + jnp.arange(tok_dev, dtype=jnp.int32)
    query_pos = row_positions(block_pair, local_rows, tok_dev)
    key_pos = row_positions(block_pair, jnp.arange(count * tok_dev, dtype=jnp.int32), tok_dev)
    tab = rotary_table(query_pos, head_size)
    loc = block_places(block_pair, count)

    def exchange(vals):
        return lax.all_to_all(vals, "ctx", split_axis=0, concat_axis=0, tiled=True)

    rows_in = [inputs[i, 0] for i in range(micros)]
    cot_in = [cotangent[i, 0] for i in range(micros)]

    def norm_qkv(index, got):
        return qkv_call(rows_in[index], got, vecs, qkv_b, tab, wq, wq_oth, wsh)

    def mlp(made, save):
        return mlp_call(made[2], made[3], up_b, down_b, wu, wu_oth, wd, wd_oth, wsh, save)

    def mlp_back(dy, mlp_kept, after=(), limit=VMEM_LIMIT):
        return mlp_back_call(dy, mlp_kept[1], wu, wu_oth, wd, wd_oth, wsh, after, limit)

    def out_back(index, got, joined=None):
        return da_call(cot_in[index], got, wp, wp_oth, wsh, joined)

    def moved(vals):
        return exchange(vals) if one_pair_each else vals

    def attend(qkv, after=()):
        if one_pair_each:
            attended, lse = attend_call(qkv, loc, after)
            return attended, (qkv, lse)
        return wide_attend(qkv, query_pos, key_pos)

    def attend_back(kept, da, after=(), limit=VMEM_LIMIT):
        if one_pair_each:
            return attend_back_call(kept[0], da, kept[1], loc, after, limit)
        da = da[:, 0] if da.ndim == 4 else da
        return wide_attend_back(kept, da, query_pos, key_pos)

    def project(attended, made, mlp_out, after=(), limit=VMEM_LIMIT):
        return proj_call(attended, made[1], mlp_out[0], proj_b, wp, wp_oth, wsh, after, limit)

    def input_grad_of(dqkv, made, dy, dnm, after=(), limit=VMEM_LIMIT):
        return dx_call(dqkv, tab, made[1], dy, dnm, vecs, wq, wq_oth, wsh, after, limit)

    made_a = norm_qkv(0, None)
    qkv_a = moved(made_a[0])
    mlp_a = mlp(made_a, False)
    att_a, _ = attend(qkv_a, [mlp_a[0]])
    att_a = moved(att_a)
    da_a, dy_a = out_back(0, None)
    y_a = project(att_a, made_a, mlp_a, [dy_a])[0]
    da_a = moved(tied(y_a, da_a)[0])

    made_b = norm_qkv(1, pass_on(y_a, 1))
    qkv_2 = moved(tied(da_a, made_b[0])[0])
    norms_b = swap(made_b[3])
    mlp_b = mlp(made_b, True)
    att_b, kept_b = attend(qkv_2, [mlp_b[0], norms_b])
    att_b = moved(att_b)
    gt_b = swap(mlp_b[3])
    dqkv_a_ = attend_back(kept_b, da_a, [gt_b])
    dqkv_a = moved(dqkv_a_)
    y_b, *a_b = project(att_b, made_b, mlp_b, [dqkv_a_])

    made_c = norm_qkv(0, pass_on(y_b, 1))
    qkv_3 = moved(tied(dqkv_a, made_c[0])[0])
    norms_c = swap(made_c[3])
    a_b_oth = swap(a_b[1])
    _, dnm_a = mlp_back(dy_a, mlp_b, [made_c[1]])
    _, dx_a, _ = input_grad_of(dqkv_a, made_b, dy_a, dnm_a, [norms_c, a_b_oth])
    got_a = pass_on(dx_a, -1)
    mlp_c = mlp_call(
        made_c[2], tied(dx_a, made_c[3])[0], up_b, down_b, wu, wu_oth, wd, wd_oth, wsh, True
    )
    da_b, dy_b = out_back(1, tied(mlp_c[0], got_a)[0])
    da_b = moved(tied(qkv_3, da_b)[0])
    att_c, kept_c = attend(qkv_3, [dy_b])
    dy_b_oth, gt_c = swap(dy_b), swap(mlp_c[3])
    dqkv_b = attend_back(kept_c, da_b, [dy_b_oth, gt_c])
    dqkv_b_ = moved(dqkv_b)
    du_b, dnm_b = mlp_back(dy_b, mlp_c, [dqkv_b])
    du_b_oth = swap(du_b)
    back_b, dx_b, sums_b = input_grad_of(dqkv_b_, made_c, dy_b, dnm_b, [du_b_oth])
    got_b = pass_on(dx_b, -1)
    back_b_oth = swap(back_b)

    da_c, dy_c = out_back(0, tied(back_b_oth, got_b)[0], att_c if one_pair_each else None)
    dy_list = [dy_c, dy_b, swap(dy_c), dy_b_oth]
    da_c = moved(da_c)
    idx = ring_index("ctx")
    *down_made, dy_sum = down_grad_call(idx, [mlp_b[2], mlp_c[2], gt_b, gt_c], dy_list, count)
    down_ring = ring_sum(*down_made, (dim,), "ctx")
    token = next(down_ring)
    du_c, dnm_c = mlp_back(dy_c, mlp_b, [token], TAIL_LIMIT)
    token = down_ring.send(dnm_c)
    *up_made, du_sum = up_grad_call(
        idx,
        [made_b[2], made_c[2], norms_b, norms_c],
        [du_c, du_b, swap(du_c), du_b_oth],
        count,
        [token],
    )
    up_ring = ring_sum(*up_made, (up_made[0].shape[1],), "ctx")
    token = next(up_ring)
    steps = count + 1
    left = {down_ring: steps - 2, up_ring: steps - 1}
    results = {}

    def turn(ring, token):
        if not left[ring]:
            return token
        left[ring] -= 1
        made = ring.send(token)
        if left[ring] == 0:
            results[ring] = made
            return token
        return made

    for ring in (down_ring, up_ring, down_ring):
        token = turn(ring, token)
    dqkv_c = attend_back(kept_b, da_c, [token], TAIL_LIMIT)
    token = turn(up_ring, dqkv_c)
    dqkv_c = moved(dqkv_c)
    for ring in (down_ring, up_ring):
        token = turn(ring, token)
    back_c, dx_c, sums_c = input_grad_of(dqkv_c, made_b, dy_c, dnm_c, [token], TAIL_LIMIT)
    back_c_oth = swap(back_c)
    token = turn(down_ring, dx_c)
    y_c, *a_c = project(da_c if one_pair_each else att_c, made_c, mlp_c, [token], TAIL_LIMIT)
    a_c_oth = swap(a_c[1])
    token = turn(up_ring, y_c)
    norm_sums = sums_b + sums_c
    norm_own = lax.dynamic_slice_in_dim(norm_sums, my_half * half, half, 1)
    norm_oth = swap(lax.dynamic_slice_in_dim(norm_sums, (1 - my_half) * half, half, 1))

    def own_part(vec):
        size = vec.shape[1] // 2
        return lax.dynamic_slice_in_dim(vec, my_half * size, size, 1).reshape(-1, LANES)

    small = [(norm_own + norm_oth).reshape(-1, LANES), own_part(dy_sum), own_part(du_sum)]
    *attn_made, attn_sum = attn_grad_call(
        idx,
        wsh,
        [made_b[2], made_c[2], norms_b, norms_c],
        [a_b[0], a_c[0], a_b_oth, a_c_oth],
        [back_c, back_b, back_c_oth, back_b_oth],
        dy_list,
        jnp.concatenate(small, axis=0),
        count,
        [token],
    )
    attn_ring = ring_sum(*attn_made, (3 * dim, dim, LANES), "ctx")
    token = next(attn_ring)
    left[attn_ring] = steps - 1
    token = turn(down_ring, token)
    at = 0
    while any(left.values()):
        token = turn((up_ring, attn_ring, down_ring, attn_ring)[at % 4], token)
        at += 1
    (down_grad,) = results[down_ring]
    (up_grad,) = results[up_ring]
    qkv_grad, proj_grad, summed = results[attn_ring]

    sizes = [v.shape[0] for v in small] + [3 * dim // 2 // LANES]
    ends = [sum(sizes[: i + 1]) for i in range(4)]
    norm_grads, dy_total, up_b_grad, qkv_b_grad = (
        summed[end - size : end] for end, size in zip(ends, sizes)
    )
    norm_grads, dy_total = norm_grads.reshape(4, 1, half), dy_total.reshape(1, half)
    pick = lambda yes, no: jnp.where(first_section, yes, no)
    layer_out = jnp.stack([pick(y_c, y_b), pick(y_b, y_c)])[None, :, None]
    input_grad = jnp.stack([pick(dx_b, dx_c), pick(dx_c, dx_b)])[None, :, None]
    return (
        layer_out,
        input_grad,
        qkv_grad[None],
        qkv_b_grad.reshape(1, -1),
        proj_grad[None],
        dy_total,
        up_grad[None],
        up_b_grad.reshape(1, -1),
        down_grad[None],
        dy_total,
        norm_grads[0],
        norm_grads[1],
        norm_grads[2],
        norm_grads[3],
    )


def solution(mesh):
    in_specs = (
        P(None, "wsh", "ctx", None),
        P(None, "wsh", "ctx", None),
        P(),
        P("section", "wsh", None),
        P("section", "wsh"),
        P("section", "wsh", None),
        P("section", "wsh"),
        P("section", "wsh", None),
        P("section", "wsh"),
        P("section", "wsh", None),
        P("section", "wsh"),
        P("section", "wsh"),
        P("section", "wsh"),
        P("section", "wsh"),
        P("section", "wsh"),
    )
    out_specs = (
        P("section", None, "wsh", "ctx", None),
        P("section", None, "wsh", "ctx", None),
        P("section", "wsh", None),
        P("section", "wsh"),
        P("section", "wsh", None),
        P("section", "wsh"),
        P("section", "wsh", None),
        P("section", "wsh"),
        P("section", "wsh", None),
        P("section", "wsh"),
        P("section", "wsh"),
        P("section", "wsh"),
        P("section", "wsh"),
        P("section", "wsh"),
    )
    return jax.shard_map(body, mesh=mesh, in_specs=in_specs, out_specs=out_specs, check_vma=False)
```

```python
import functools

import jax
import jax.numpy as jnp
from jax import lax
from jax.experimental import pallas as pl
from jax.experimental.pallas import tpu as pltpu
from jax.sharding import PartitionSpec as P

HEADS = 16
ROT = 16
NORM_EPS = 1e-05
ROPE_BASE = 10000.0
MASKED_SCORE = -1e30
LANES = 128
VMEM_LIMIT = 50 * 1024 * 1024
TAIL_LIMIT = VMEM_LIMIT
RING_LIMIT = VMEM_LIMIT
INV_SQRT2 = 0.7071067811865476
INV_SQRT_2PI = 0.3989422804014327

f32 = jnp.float32
bf16 = jnp.bfloat16


def dot_nn(left, right):
    return lax.dot_general(left, right, (((1,), (0,)), ((), ())), preferred_element_type=f32)


def dot_nt(left, right):
    return lax.dot_general(left, right, (((1,), (1,)), ((), ())), preferred_element_type=f32)


def params_of(limit):
    return dict(
        compiler_params=pltpu.CompilerParams(vmem_limit_bytes=limit),
        cost_estimate=pl.CostEstimate(flops=1, bytes_accessed=1, transcendentals=0),
    )


def whole(shape):
    rank = len(shape)
    return pl.BlockSpec(shape, lambda *args: (0,) * rank)


def shape_of(shape, dtype):
    return jax.ShapeDtypeStruct(shape, dtype)


def rope(vals, tab_ref):
    return (
        vals * tab_ref[0]
        + pltpu.roll(vals, LANES - ROT // 2, 1) * tab_ref[1]
        + pltpu.roll(vals, ROT // 2, 1) * tab_ref[2]
    )


def unrope(vals, tab_ref):
    return (
        vals * tab_ref[0]
        - pltpu.roll(vals, LANES - ROT // 2, 1) * tab_ref[1]
        - pltpu.roll(vals, ROT // 2, 1) * tab_ref[2]
    )


def normalized(hidden):
    row_mean = jnp.mean(hidden, axis=-1, keepdims=True)
    centered = hidden - row_mean
    spread = jnp.mean(centered * centered, axis=-1, keepdims=True)
    scale = lax.rsqrt(spread + NORM_EPS)
    return centered * scale, scale


def start_all(copies):
    for copy in copies:
        copy.start()
    return copies


def wait_all(copies):
    for copy in copies:
        copy.wait()


def qkv_kernel(own_given, wsh_ref, inputs, weights, outputs, buf, sems):
    half, dim = buf.shape[2:]
    copies = start_all(
        [
            pltpu.make_async_copy(
                weight.at[:, pl.ds(part * dim, dim)], buf.at[part, side], sems.at[part, side]
            )
            for part in range(3)
            for side, weight in enumerate(weights)
        ]
    )
    out, x_out, own, oth = outputs
    x = inputs[0].ref()[...]
    if not own_given:
        x = jnp.where(wsh_ref[1] == 1, x, inputs[4].ref()[...])
    x_out.ref[...] = x
    x_out.send()
    xhat, _ = normalized(x.astype(f32))
    vec_ref, bias_ref, tab_ref = (item.ref() for item in inputs[1:4])
    na = (xhat * vec_ref[0:1] + vec_ref[1:2]).astype(bf16)
    nm = (xhat * vec_ref[2:3] + vec_ref[3:4]).astype(bf16)
    first = wsh_ref[0] == 0
    for i, rows in enumerate((na, nm)):
        own.ref[i] = jnp.where(first, rows[:, :half], rows[:, half:])
        oth.ref[i] = jnp.where(first, rows[:, half:], rows[:, :half])
    own.send()
    oth.send()
    for part in range(3):
        wait_all(copies[2 * part : 2 * part + 2])
        for at in range(0, dim, 2 * LANES):
            cols = slice(at, at + 2 * LANES)
            res = (
                dot_nn(own.ref[0], buf[part, 0, :, cols])
                + dot_nn(oth.ref[0], buf[part, 1, :, cols])
                + bias_ref[:, part * dim + at : part * dim + at + 2 * LANES]
            )
            for i in range(2):
                vals = res[:, i * LANES : (i + 1) * LANES]
                if part < 2:
                    vals = rope(vals, tab_ref)
                out.ref[at // LANES + i, part] = vals.astype(bf16)


def layer_of(shape, index):
    return pl.BlockSpec((pl.squeezed,) + shape, lambda *args: (index, 0, 0))


HERE = pl.BlockSpec(memory_space=pltpu.VMEM)
SCALARS = pl.BlockSpec(memory_space=pltpu.SMEM)
ANYWHERE = pl.BlockSpec(memory_space=pl.ANY)
IN_HBM = pl.BlockSpec(memory_space=pltpu.HBM)


class Arriving:
    def __init__(self, buf, copy=None):
        self.buf, self.copy = buf, copy

    def ref(self):
        if self.copy is not None:
            self.copy.wait()
            self.copy = None
        return self.buf


class Leaving:
    def __init__(self, buf, copy=None):
        self.ref, self.copy, self.sent = buf, copy, copy is None

    def send(self):
        if not self.sent:
            self.copy.start()
            self.sent = True


def local_kernel(body, near_in, near_out, scalars, weights, followed, *refs):
    refs = list(refs)

    def take(number):
        taken = refs[:number]
        del refs[:number]
        return taken

    scalar_refs, array_refs = take(scalars), take(len(near_in))
    weight_refs, _, out_refs = take(weights), take(followed), take(len(near_out))
    in_sems, out_sems = take(2)
    inputs, outputs = [], []
    for i, (near, ref) in enumerate(zip(near_in, array_refs)):
        if near:
            inputs.append(Arriving(ref))
        else:
            buf = take(1)[0]
            copy = pltpu.make_async_copy(ref, buf, in_sems.at[i])
            copy.start()
            inputs.append(Arriving(buf, copy))
    for i, (near, ref) in enumerate(zip(near_out, out_refs)):
        if near:
            outputs.append(Leaving(ref))
        else:
            buf = take(1)[0]
            outputs.append(Leaving(buf, pltpu.make_async_copy(buf, ref, out_sems.at[i])))
    body(*scalar_refs, inputs, weight_refs, outputs, *refs)
    for item in inputs:
        item.ref()
    for item in outputs:
        item.send()
    for item in outputs:
        if item.copy is not None:
            item.copy.wait()


def far(array):
    return (array,)


def local_call(body, name, scalars, arrays, weights, out_shape, scratch=(), after=(), limit=VMEM_LIMIT):
    near_in = [not isinstance(a, tuple) for a in arrays]
    near_out = [not isinstance(o, tuple) for o in out_shape]
    raw_out = [isinstance(o, list) for o in out_shape]
    arrays = [a if near else a[0] for a, near in zip(arrays, near_in)]
    shapes = [o if near and not raw else o[0] for o, near, raw in zip(out_shape, near_out, raw_out)]
    far_bufs = [
        pltpu.VMEM(a.shape, a.dtype)
        for a, near in zip(arrays + shapes, near_in + near_out)
        if not near
    ]
    return pl.pallas_call(
        functools.partial(
            local_kernel, body, near_in, near_out, len(scalars), len(weights), len(after)
        ),
        in_specs=[SCALARS] * len(scalars)
        + [HERE if near else IN_HBM for near in near_in]
        + [IN_HBM] * len(weights)
        + [ANYWHERE] * len(after),
        out_specs=[HERE if near and not raw else IN_HBM for near, raw in zip(near_out, raw_out)],
        out_shape=shapes,
        scratch_shapes=[
            pltpu.SemaphoreType.DMA((len(arrays) + 1,)),
            pltpu.SemaphoreType.DMA((len(shapes),)),
        ]
        + far_bufs
        + list(scratch),
        name=name,
        **params_of(limit),
    )(*scalars, *arrays, *weights, *after)


def qkv_call(given, got, vecs, qkv_b, tab, w_own, w_oth, wsh):
    rows, dim = given.shape
    half = w_own.shape[0]
    pairs = dim // LANES
    return local_call(
        functools.partial(qkv_kernel, got is None),
        "qkv_proj",
        [wsh],
        [given, vecs, qkv_b, tab] if got is None else [given, vecs, qkv_b, tab, got],
        [w_own, w_oth],
        [shape_of((pairs, 3, rows, LANES), bf16), shape_of((rows, dim), bf16)]
        + [shape_of((2, rows, half), bf16)] * 2,
        [pltpu.VMEM((3, 2, half, dim), bf16), pltpu.SemaphoreType.DMA((3, 2))],
    )


FF_TILE = 1024
FF_PIECE = 512


def ff_tiles(wsh_ref, up_own, up_oth, dn_own, dn_oth, up_buf, dn_buf, sems):
    own = dn_own.shape[0] // FF_TILE
    tiles = []
    for t in range(2 * own):
        start = pl.multiple_of(((wsh_ref[0] * own + t) % (2 * own)) * FF_TILE, FF_TILE)
        cols = pl.ds(start, FF_TILE)
        down = (dn_own if t < own else dn_oth).at[pl.ds((t % own) * FF_TILE, FF_TILE)]
        copies = [
            pltpu.make_async_copy(up_own.at[:, cols], up_buf.at[t, 0], sems.at[t, 0]),
            pltpu.make_async_copy(up_oth.at[:, cols], up_buf.at[t, 1], sems.at[t, 1]),
            pltpu.make_async_copy(down, dn_buf.at[t], sems.at[t, 2]),
        ]
        tiles.append((t, start, start_all(copies)))
    for t, start, copies in tiles:
        wait_all(copies)
        for at in range(0, FF_TILE, FF_PIECE):
            row = (t % own) * FF_TILE + at
            place = pl.ds(pl.multiple_of(start + at, FF_PIECE), FF_PIECE)
            yield t, place, t < own, slice(row, row + FF_PIECE), slice(at, at + FF_PIECE)


def ff_scratch(half, ff, dim):
    tiles = ff // FF_TILE
    return [
        pltpu.VMEM((tiles, 2, half, FF_TILE), bf16),
        pltpu.VMEM((tiles, FF_TILE, dim), bf16),
        pltpu.SemaphoreType.DMA((tiles, 3)),
    ]


def mlp_kernel(save, wsh_ref, inputs, weights, outputs, up_buf, dn_buf, sems):
    out_ref = outputs[0].ref
    started = False
    for t, place, held, rows, piece in ff_tiles(wsh_ref, *weights, up_buf, dn_buf, sems):
        own_ref, oth_ref, up_b, down_b = (item.ref() for item in inputs)
        if not started:
            out_ref[...] = jnp.broadcast_to(down_b[...], out_ref.shape)
            started = True
        pre = (
            dot_nn(own_ref[1], up_buf[t, 0, :, piece])
            + dot_nn(oth_ref[1], up_buf[t, 1, :, piece])
            + up_b[:, place]
        )
        gate = 0.5 + 0.5 * lax.erf(pre * INV_SQRT2)
        act = (pre * gate).astype(bf16)
        if save:
            slope = gate + pre * (INV_SQRT_2PI * jnp.exp(-0.5 * pre * pre))
            outputs[1].ref[place] = slope.astype(bf16).T
            outputs[2 if held else 3].ref[rows] = act.T
            if not held:
                outputs[2].send()
        out_ref[...] += dot_nn(act, dn_buf[t, piece])


def mlp_call(own, oth, up_b, down_b, up_own, up_oth, dn_own, dn_oth, wsh, save):
    rows, half = own.shape[1:]
    dim = dn_own.shape[1]
    ff = up_own.shape[1]
    out_shape = [shape_of((rows, dim), f32)]
    if save:
        out_shape += [shape_of((ff, rows), bf16)]
        out_shape += [shape_of((ff // 2, rows), bf16)] * 2
    return local_call(
        functools.partial(mlp_kernel, save),
        "mlp_forward",
        [wsh],
        [own, oth, up_b, down_b],
        [up_own, up_oth, dn_own, dn_oth],
        out_shape,
        ff_scratch(half, ff, dim),
    )


def mlp_back_kernel(wsh_ref, inputs, weights, outputs, acc_own, acc_oth, up_buf, dn_buf, sems):
    du, dnm = outputs
    half = acc_own.shape[0]
    acc_own[...] = jnp.zeros(acc_own.shape, f32)
    acc_oth[...] = jnp.zeros(acc_oth.shape, f32)
    for t, place, _, _, piece in ff_tiles(wsh_ref, *weights, up_buf, dn_buf, sems):
        dy_ref, slope_ref = (item.ref() for item in inputs)
        dact = dot_nt(dn_buf[t, piece], dy_ref[...])
        vals = (dact * slope_ref[place].astype(f32)).astype(bf16)
        du.ref[place] = vals
        acc_own[...] += dot_nn(up_buf[t, 0, :, piece], vals)
        acc_oth[...] += dot_nn(up_buf[t, 1, :, piece], vals)
    du.send()
    first = wsh_ref[0] == 0
    dnm.ref[:, :half] = jnp.where(first, acc_own[...], acc_oth[...]).T
    dnm.ref[:, half:] = jnp.where(first, acc_oth[...], acc_own[...]).T


def mlp_back_call(dy, slope, up_own, up_oth, dn_own, dn_oth, wsh, after, limit):
    rows, dim = dy.shape
    half, ff = up_own.shape
    return local_call(
        mlp_back_kernel,
        "mlp_backward",
        [wsh],
        [dy, slope],
        [up_own, up_oth, dn_own, dn_oth],
        [shape_of(slope.shape, bf16), shape_of((rows, dim), f32)],
        [pltpu.VMEM((half, rows), f32), pltpu.VMEM((half, rows), f32)] + ff_scratch(half, ff, dim),
        after,
        limit,
    )


def sort_in(loc_ref, ref, dst, half_rows, part=None):
    for block in range(dst.shape[0] // half_rows):
        place = loc_ref[block]
        rows = pl.ds(pl.multiple_of((place % 2) * half_rows, half_rows), half_rows)
        if part is None:
            vals = ref[place // 2, rows, :]
        else:
            vals = ref[place // 2, part, rows, :]
        dst[block * half_rows : (block + 1) * half_rows] = vals


def sort_out(loc_ref, vals, ref, half_rows, part=None):
    for block in range(vals.shape[0] // half_rows):
        place = loc_ref[block]
        rows = pl.ds(pl.multiple_of((place % 2) * half_rows, half_rows), half_rows)
        piece = vals[block * half_rows : (block + 1) * half_rows]
        if part is None:
            ref[place // 2, rows, :] = piece
        else:
            ref[place // 2, part, rows, :] = piece


def head_of(vals, head):
    lane = lax.broadcasted_iota(jnp.int32, vals.shape, 1)
    return jnp.where(lane // (LANES // 2) == head, vals, jnp.zeros_like(vals))


def scores_of(keys, queries, scale, diagonal):
    scores = dot_nt(keys, queries) * scale
    if diagonal:
        key_at = lax.broadcasted_iota(jnp.int32, scores.shape, 0)
        query_at = lax.broadcasted_iota(jnp.int32, scores.shape, 1)
        scores = jnp.where(key_at <= query_at, scores, MASKED_SCORE)
    return scores


def attend_kernel(tile, loc_ref, inputs, weights, outputs, q_s, k_s, v_s, vt_s, o_s):
    qkv_ref = inputs[0].ref()
    o_ref, lse_ref = (item.ref for item in outputs)
    half_rows = qkv_ref.shape[2] // 2
    seq = q_s.shape[0]
    head_size = LANES // 2
    scale = head_size**-0.5
    sort_in(loc_ref, qkv_ref, q_s, half_rows, 0)
    sort_in(loc_ref, qkv_ref, k_s, half_rows, 1)
    sort_in(loc_ref, qkv_ref, v_s, half_rows, 2)
    vt_s[...] = v_s[...].T
    for t in range(seq // tile):
        rows = slice(t * tile, (t + 1) * tile)
        queries = q_s[rows]
        outs = []
        for head in range(2):
            picked = head_of(queries, head)
            parts = [
                scores_of(k_s[i * tile : (i + 1) * tile], picked, scale, i == t)
                for i in range(t + 1)
            ]
            top = functools.reduce(
                jnp.maximum, [jnp.max(p, axis=0, keepdims=True) for p in parts]
            )
            parts = [jnp.exp(p - top) for p in parts]
            total = sum(jnp.sum(p, axis=0, keepdims=True) for p in parts)
            lse_ref[head : head + 1, rows] = top + jnp.log(total)
            inverse = 1.0 / total
            acc = None
            for i, p in enumerate(parts):
                term = dot_nn(
                    vt_s[head * head_size : (head + 1) * head_size, i * tile : (i + 1) * tile],
                    (p * inverse).astype(bf16),
                )
                acc = term if acc is None else acc + term
            outs.append(acc)
        o_s[rows] = jnp.concatenate(outs, axis=0).T.astype(bf16)
    sort_out(loc_ref, o_s, o_ref, half_rows)


def attend_call(qkv, loc, after):
    count, _, rows, _ = qkv.shape
    seq = count * rows
    return local_call(
        functools.partial(attend_kernel, 256),
        "attention",
        [loc],
        [qkv],
        [],
        [shape_of((count, rows, LANES), bf16), shape_of((2, seq), f32)],
        [
            pltpu.VMEM((seq, LANES), bf16),
            pltpu.VMEM((seq, LANES), bf16),
            pltpu.VMEM((seq, LANES), bf16),
            pltpu.VMEM((LANES, seq), bf16),
            pltpu.VMEM((seq, LANES), bf16),
        ],
        after,
    )


def attend_back_kernel(
    tile, part, loc_ref, inputs, weights, outputs, q_s, k_s, v_s, da_s, kt_s, dq_s, dk_s, dv_s
):
    da_ref, qkv_ref, lse_ref = (item.ref() for item in inputs)
    out_ref = outputs[0].ref
    half_rows = qkv_ref.shape[2] // 2
    seq = q_s.shape[0]
    head_size = LANES // 2
    scale = head_size**-0.5
    sort_in(loc_ref, qkv_ref, q_s, half_rows, 0)
    sort_in(loc_ref, qkv_ref, k_s, half_rows, 1)
    sort_in(loc_ref, qkv_ref, v_s, half_rows, 2)
    sort_in(loc_ref, da_ref, da_s, half_rows, part)
    kt_s[...] = k_s[...].T
    dk_s[...] = jnp.zeros(dk_s.shape, f32)
    dv_s[...] = jnp.zeros(dv_s.shape, f32)
    for t in range(seq // tile):
        rows = slice(t * tile, (t + 1) * tile)
        outs = []
        for head in range(2):
            queries = head_of(q_s[rows], head)
            grads = head_of(da_s[rows], head)
            lse = lse_ref[head : head + 1, rows]
            probs, dprobs, row_dot = [], [], 0.0
            for i in range(t + 1):
                keys = slice(i * tile, (i + 1) * tile)
                p = jnp.exp(scores_of(k_s[keys], queries, scale, i == t) - lse)
                dp = dot_nt(v_s[keys], grads)
                row_dot = row_dot + jnp.sum(p * dp, axis=0, keepdims=True)
                dv_s[keys] += dot_nn(p.astype(bf16), grads)
                probs.append(p)
                dprobs.append(dp)
            acc = None
            for i in range(t + 1):
                keys = slice(i * tile, (i + 1) * tile)
                ds = (probs[i] * (dprobs[i] - row_dot) * scale).astype(bf16)
                dk_s[keys] += dot_nn(ds, queries)
                term = dot_nn(kt_s[head * head_size : (head + 1) * head_size, keys], ds)
                acc = term if acc is None else acc + term
            outs.append(acc)
        dq_s[rows] = jnp.concatenate(outs, axis=0).T.astype(bf16)
    sort_out(loc_ref, dq_s, out_ref, half_rows, 0)
    k_s[...] = dk_s[...].astype(bf16)
    v_s[...] = dv_s[...].astype(bf16)
    sort_out(loc_ref, k_s, out_ref, half_rows, 1)
    sort_out(loc_ref, v_s, out_ref, half_rows, 2)


def attend_back_call(qkv, da, lse, loc, after, limit):
    count, _, rows, _ = qkv.shape
    seq = count * rows
    part = 0 if da.ndim == 4 else None
    (res,) = local_call(
        functools.partial(attend_back_kernel, 256, part),
        "attention_backward",
        [loc],
        [da, qkv, lse],
        [],
        [shape_of(qkv.shape, bf16)],
        [pltpu.VMEM((seq, LANES), bf16)] * 4
        + [pltpu.VMEM((LANES, seq), bf16), pltpu.VMEM((seq, LANES), bf16)]
        + [pltpu.VMEM((seq, LANES), f32)] * 2,
        after,
        limit,
    )
    return res


def by_head(parts):
    pairs, rows, lanes = parts.shape
    return jnp.transpose(parts, (1, 0, 2)).reshape(rows, HEADS, pairs * lanes // HEADS)


def by_pair(heads):
    rows = heads.shape[0]
    return jnp.transpose(heads.reshape(rows, -1, LANES), (1, 0, 2))


def wide_scores(queries, keys, query_pos, key_pos):
    raw = jnp.einsum("qhd,khd->hqk", queries, keys, preferred_element_type=f32)
    allowed = (query_pos[:, None] >= key_pos[None, :])[None]
    return jnp.where(allowed, raw * queries.shape[-1] ** (-0.5), MASKED_SCORE)


def key_blocks(arrays, rows):
    return tuple(a.reshape((a.shape[0] // rows, rows) + a.shape[1:]) for a in arrays)


def wide_attend(qkv, query_pos, key_pos):
    queries = by_head(qkv[:, 0])
    keys = lax.all_gather(by_head(qkv[:, 1]), "ctx", axis=0, tiled=True)
    values = lax.all_gather(by_head(qkv[:, 2]), "ctx", axis=0, tiled=True)
    block = min(512, keys.shape[0])
    split = key_blocks((keys, values, key_pos), block)
    rows, _, head_size = queries.shape

    def max_step(carry, block_in):
        top, total = carry
        scores = wide_scores(queries, block_in[0], query_pos, block_in[2])
        new_top = jnp.maximum(top, jnp.max(scores, axis=-1))
        part = jnp.sum(jnp.exp(scores - new_top[..., None]), axis=-1)
        return ((new_top, total * jnp.exp(top - new_top) + part), None)

    start = (jnp.full((HEADS, rows), MASKED_SCORE, f32), jnp.zeros((HEADS, rows), f32))
    (top, total), _ = lax.scan(max_step, start, split)
    lse = top + jnp.log(total)

    def value_step(running, block_in):
        scores = wide_scores(queries, block_in[0], query_pos, block_in[2])
        probs = jnp.exp(scores - lse[..., None]).astype(bf16)
        term = jnp.einsum("hqk,khd->qhd", probs, block_in[1], preferred_element_type=f32)
        return (running + term, None)

    attended, _ = lax.scan(value_step, jnp.zeros((rows, HEADS, head_size), f32), split)
    return by_pair(attended.astype(bf16)), (queries, keys, values, lse)


def wide_attend_back(kept, da, query_pos, key_pos):
    queries, keys, values, lse = kept
    grads = by_head(da)
    block = min(512, keys.shape[0])
    split = key_blocks((keys, values, key_pos), block)
    scale = queries.shape[-1] ** (-0.5)

    def pieces(block_in):
        scores = wide_scores(queries, block_in[0], query_pos, block_in[2])
        probs = jnp.exp(scores - lse[..., None])
        dprobs = jnp.einsum("qhd,khd->hqk", grads, block_in[1], preferred_element_type=f32)
        return probs, dprobs

    def dot_step(running, block_in):
        probs, dprobs = pieces(block_in)
        return (running + jnp.sum(probs * dprobs, axis=-1), None)

    row_dot, _ = lax.scan(dot_step, jnp.zeros(lse.shape, f32), split)

    def key_step(running, block_in):
        probs, dprobs = pieces(block_in)
        ds = (scale * probs * (dprobs - row_dot[..., None])).astype(bf16)
        running = running + jnp.einsum("hqk,khd->qhd", ds, block_in[0], preferred_element_type=f32)
        dk = jnp.einsum("hqk,qhd->khd", ds, queries, preferred_element_type=f32)
        dv = jnp.einsum("hqk,qhd->khd", probs.astype(bf16), grads, preferred_element_type=f32)
        return (running, (dk.astype(bf16), dv.astype(bf16)))

    dq, (dk, dv) = lax.scan(key_step, jnp.zeros(queries.shape, f32), split)
    dk, dv = (
        lax.psum_scatter(part.reshape(keys.shape), "ctx", scatter_dimension=0, tiled=True)
        for part in (dk, dv)
    )
    return jnp.stack([by_pair(dq.astype(bf16)), by_pair(dk), by_pair(dv)], axis=1)


def lanes_of(ref):
    return jnp.concatenate([ref[i] for i in range(ref.shape[0])], axis=1)


def both_halves(w_own, w_oth, buf, sems):
    return start_all(
        [
            pltpu.make_async_copy(weight, buf.at[side], sems.at[side])
            for side, weight in enumerate((w_own, w_oth))
        ]
    )


def half_scratch(weight):
    return [pltpu.VMEM((2,) + weight.shape, bf16), pltpu.SemaphoreType.DMA((2,))]


def proj_kernel(part, wsh_ref, inputs, weights, outputs, buf, sems):
    copies = both_halves(*weights, buf, sems)
    y, own, oth = outputs
    half = buf.shape[1]
    first = wsh_ref[0] == 0
    a_ref = inputs[0].ref()
    a = lanes_of(a_ref if part is None else a_ref.at[:, part])
    own.ref[...] = jnp.where(first, a[:, :half], a[:, half:])
    oth.ref[...] = jnp.where(first, a[:, half:], a[:, :half])
    own.send()
    oth.send()
    bias_ref, x_ref, mlp_ref = (item.ref() for item in inputs[1:])
    wait_all(copies)
    attn = dot_nn(own.ref[...], buf[0]) + dot_nn(oth.ref[...], buf[1]) + bias_ref[...]
    y.ref[...] = (x_ref[...].astype(f32) + attn + mlp_ref[...]).astype(bf16)


def proj_call(a, x, mlp, bias, p_own, p_oth, wsh, after, limit):
    rows, dim = x.shape
    half = p_own.shape[0]
    return local_call(
        functools.partial(proj_kernel, 1 if a.ndim == 4 else None),
        "attn_out",
        [wsh],
        [a, bias, x, mlp],
        [p_own, p_oth],
        [shape_of((rows, dim), bf16)] + [shape_of((rows, half), bf16)] * 2,
        half_scratch(p_own),
        after,
        limit,
    )


def da_kernel(own_given, wsh_ref, inputs, weights, outputs, buf, sems):
    copies = both_halves(*weights, buf, sems)
    out_ref, dy_out = outputs[0].ref, outputs[1]
    dy = inputs[0].ref()[...]
    if not own_given:
        dy = jnp.where(wsh_ref[1] == 1, inputs[1].ref()[...], dy)
    dy_out.ref[...] = dy
    dy_out.send()
    wsh = wsh_ref[0]
    joined = len(out_ref.shape) == 4
    if joined:
        out_ref[:, 1] = inputs[2].ref()[...]
    count = out_ref.shape[0] // 2
    for place, side in ((wsh * count, 0), ((1 - wsh) * count, 1)):
        copies[side].wait()
        part = dot_nt(dy, buf[side]).astype(bf16)
        for i in range(count):
            vals = part[:, i * LANES : (i + 1) * LANES]
            if joined:
                out_ref[place + i, 0] = vals
            else:
                out_ref[place + i] = vals


def da_call(given, got, p_own, p_oth, wsh, joined=None):
    rows, dim = given.shape
    pairs = dim // LANES
    arrays = [given] + ([] if got is None else [got])
    arrays += [] if joined is None else [joined]
    shape = (pairs, rows, LANES) if joined is None else (pairs, 2, rows, LANES)
    return local_call(
        functools.partial(da_kernel, got is None),
        "attn_out_backward",
        [wsh],
        arrays,
        [p_own, p_oth],
        [shape_of(shape, bf16), shape_of((rows, dim), bf16)],
        half_scratch(p_own),
    )


def dx_kernel(wsh_ref, inputs, weights, outputs, grad_s, buf, sems):
    copies = both_halves(*weights, buf, sems)
    back, dx, sums = outputs
    dqkv_ref, tab_ref = inputs[0].ref(), inputs[1].ref()
    pairs = dqkv_ref.shape[0]
    for part in range(3):
        for pair in range(pairs):
            vals = dqkv_ref[pair, part]
            if part < 2:
                vals = unrope(vals.astype(f32), tab_ref).astype(bf16)
            back.ref[pair, part] = vals
            grad_s[:, pl.ds((part * pairs + pair) * LANES, LANES)] = vals
    back.send()
    vec_ref, x_ref, dy_ref, dnm_ref = (item.ref() for item in inputs[2:])
    first = wsh_ref[0] == 0
    copies[0].wait()
    own = dot_nt(grad_s[...], buf[0])
    copies[1].wait()
    oth = dot_nt(grad_s[...], buf[1])
    dna = jnp.concatenate([jnp.where(first, own, oth), jnp.where(first, oth, own)], axis=1)
    dnm = dnm_ref[...]
    xhat, scale = normalized(x_ref[...].astype(f32))
    grad = dna * vec_ref[0:1] + dnm * vec_ref[2:3]
    inner = (
        grad
        - jnp.mean(grad, axis=-1, keepdims=True)
        - xhat * jnp.mean(grad * xhat, axis=-1, keepdims=True)
    )
    dx.ref[...] = (dy_ref[...].astype(f32) + scale * inner).astype(bf16)
    dx.send()
    sums.ref[0:1] = jnp.sum(dna * xhat, axis=0, keepdims=True)
    sums.ref[1:2] = jnp.sum(dna, axis=0, keepdims=True)
    sums.ref[2:3] = jnp.sum(dnm * xhat, axis=0, keepdims=True)
    sums.ref[3:4] = jnp.sum(dnm, axis=0, keepdims=True)


def dx_call(dqkv, tab, x, dy, dnm, vecs, w_own, w_oth, wsh, after, limit):
    rows, dim = x.shape
    return local_call(
        dx_kernel,
        "section_input_grad",
        [wsh],
        [dqkv, tab, vecs, x, dy, dnm],
        [w_own, w_oth],
        [shape_of(o, t) for o, t in ((dqkv.shape, bf16), ((rows, dim), bf16), ((4, dim), f32))],
        [pltpu.VMEM((rows, 3 * dim), bf16)] + half_scratch(w_own),
        after,
        limit,
    )


def joined_rows(items):
    return jnp.concatenate([item.ref()[...] for item in items], axis=0)


class Pieces:
    def __init__(self, out_ref, buf, sems):
        self.out_ref, self.buf, self.sems, self.copies = out_ref, buf, sems, []

    def put(self, rows, cols, vals):
        self.buf[rows, cols] = vals.astype(bf16)
        at = len(self.copies)
        self.copies.append(
            pltpu.make_async_copy(
                self.buf.at[rows, cols], self.out_ref.at[rows, cols], self.sems.at[at]
            )
        )
        self.copies[-1].start()

    def finish(self, chunk, ahead, behind):
        height, cut = ahead.ref.shape
        rows = pl.ds(pl.multiple_of(chunk * height, height), height)
        ahead.ref[...] = self.buf[rows, :cut]
        ahead.send()
        behind.ref[...] = self.buf[rows, cut:]
        behind.send()
        wait_all(self.copies)


def first_half(cols):
    return cols // 2 // LANES * LANES


def grad_call(body, name, scalars, arrays, shape, width, count, scratch, after):
    cut = first_half(shape[1])
    halves = [far(shape_of((shape[0] // count, c), bf16)) for c in (cut, shape[1] - cut)]
    return local_call(
        functools.partial(body, len(arrays)),
        name,
        scalars,
        arrays,
        [],
        [[shape_of(shape, bf16)]] + halves + [far(shape_of((1, width), f32))],
        [pltpu.VMEM(shape, bf16), pltpu.SemaphoreType.DMA((5,))] + scratch,
        after,
        TAIL_LIMIT,
    )


def parts_of(items, number):
    size = len(items) // number
    return [items[i * size : (i + 1) * size] for i in range(number)]


def down_grad_kernel(number, idx_ref, inputs, weights, outputs, buf, sems):
    gts, dys = parts_of(inputs, 2)
    out = Pieces(outputs[0].ref, buf, sems)
    dy = joined_rows(dys)
    outputs[3].ref[...] = jnp.sum(dy.astype(f32), axis=0, keepdims=True)
    rows, dim = buf.shape
    tile = rows // 4
    for t in range(4):
        part = slice(t * tile, (t + 1) * tile)
        left = jnp.concatenate([item.ref()[part] for item in gts], axis=1)
        out.put(part, slice(0, dim), dot_nn(left, dy))
    out.finish(idx_ref[idx_ref.shape[0] // 2], outputs[1], outputs[2])


def down_grad_call(idx, gt_list, dy_list, count):
    dim = dy_list[0].shape[1]
    return grad_call(
        down_grad_kernel,
        "down_grad",
        [idx],
        [far(a) for a in gt_list + dy_list],
        (gt_list[0].shape[0], dim),
        dim,
        count,
        [],
        [],
    )


def up_grad_kernel(number, idx_ref, inputs, weights, outputs, buf, sems):
    norms, dus = parts_of(inputs, 2)
    out = Pieces(outputs[0].ref, buf, sems)
    left = jnp.concatenate([item.ref()[1] for item in norms], axis=0).T
    rows, ff = buf.shape
    tile = ff // 4
    for t in range(4):
        part = slice(t * tile, (t + 1) * tile)
        du = jnp.concatenate([item.ref()[part] for item in dus], axis=1)
        outputs[3].ref[:, part] = dot_nt(jnp.ones((8, du.shape[1]), bf16), du)[:1]
        out.put(slice(0, rows), part, dot_nt(left, du))
    out.finish(idx_ref[idx_ref.shape[0] // 2], outputs[1], outputs[2])


def up_grad_call(idx, norm_list, du_list, count, after):
    half, ff = norm_list[0].shape[2], du_list[0].shape[0]
    return grad_call(
        up_grad_kernel,
        "up_grad",
        [idx],
        [far(a) for a in norm_list + du_list],
        (half, ff),
        ff,
        count,
        [],
        after,
    )


def attn_grad_kernel(number, idx_ref, wsh_ref, inputs, weights, outputs, buf, sems, small_s):
    norms, outs, dqkvs, dys = parts_of(inputs[:-1], 4)
    out = Pieces(outputs[0].ref, buf, sems)
    sums = outputs[3].ref
    rows, dim = buf.shape[0], sums.shape[1] // 4
    left = jnp.concatenate([item.ref()[0] for item in norms], axis=0).T
    for part in range(4):
        cols = slice(part * dim, (part + 1) * dim)
        if part < 3:
            right = jnp.concatenate([lanes_of(item.ref().at[:, part]) for item in dqkvs], axis=0)
        else:
            left, right = joined_rows(outs).T, joined_rows(dys)
        sums[:, cols] = jnp.sum(right.astype(f32), axis=0, keepdims=True)
        out.put(slice(0, rows), cols, dot_nn(left, right))
    given = inputs[-1].ref()
    at = given.shape[0]
    small_s[:at] = given[...]
    base = wsh_ref[0] * (3 * dim // 2)
    for i in range(3 * dim // 2 // LANES):
        place = pl.ds(pl.multiple_of(base + i * LANES, LANES), LANES)
        small_s[at + i : at + i + 1] = sums[:, place]
    small = small_s[...]
    empty = jnp.zeros((rows - small.shape[0], LANES), f32)
    out.put(slice(0, rows), slice(4 * dim, 4 * dim + LANES), jnp.concatenate([small, empty], axis=0))
    out.finish(idx_ref[idx_ref.shape[0] // 2], outputs[1], outputs[2])


def attn_grad_call(idx, wsh, norm_list, out_list, dqkv_list, dy_list, small, count, after):
    half, dim = norm_list[0].shape[2], dy_list[0].shape[1]
    return grad_call(
        attn_grad_kernel,
        "attn_grad",
        [idx, wsh],
        [far(a) for a in norm_list + out_list + dqkv_list + dy_list] + [small],
        (half, 4 * dim + LANES),
        4 * dim,
        count,
        [pltpu.VMEM((small.shape[0] + 3 * dim // 2 // LANES, LANES), f32)],
        after,
    )


def ring_of(count):
    return list(range(0, count, 2)) + list(range(count - 1, 0, -2))


def ring_place(axis):
    count = lax.axis_size(axis)
    me = lax.axis_index(axis)
    return jnp.where(me % 2 == 0, me // 2, count - (me + 1) // 2)


def ring_index(axis):
    count = lax.axis_size(axis)
    return (ring_place(axis) + jnp.arange(count, dtype=jnp.int32)) % count


def ring_shift(vals, axis, by):
    order = ring_of(lax.axis_size(axis))
    count = len(order)
    pairs = [(order[i], order[(i + by) % count]) for i in range(count)]
    return lax.ppermute(vals, axis, pairs)


def tied(token, *vals):
    return lax.optimization_barrier((token, vals))[1]


def fetch(idx_ref, slots, own_ref, bufs, sems):
    return start_all(
        [
            pltpu.make_async_copy(own_ref.at[idx_ref[slot]], bufs.at[i], sems.at[i])
            for i, slot in enumerate(slots)
        ]
    )


def low_total(*terms):
    total = terms[0].astype(f32)
    for term in terms[1:]:
        total = total + term.astype(f32)
    return total.astype(bf16)


def ring_add_kernel(slots, idx_ref, inputs, own_refs, outputs, bufs, sems):
    copies = fetch(idx_ref, slots, own_refs[0], bufs, sems)
    for i, item in enumerate(outputs):
        copies[i].wait()
        got = inputs[i].ref()
        cols, cut = item.ref.shape[1], got.shape[1]
        summed = slice(0, cut) if i == 0 else slice(cols - cut, cols)
        item.ref[:, summed] = low_total(bufs[i, :, summed], got[...])
        if cut < cols:
            rest = slice(cut, cols) if i == 0 else slice(0, cols - cut)
            item.ref[:, rest] = bufs[i, :, rest]
        item.send()


def put_copies(chunk, cols, buf, totals, starts, sem):
    lo, hi = cols, cols + buf.shape[1]
    copies = []
    for i, (total, start) in enumerate(zip(totals, starts)):
        first, last = max(lo, start), min(hi, start + total.shape[2])
        if first < last:
            copies.append(
                pltpu.make_async_copy(
                    buf.at[:, pl.ds(first - lo, last - first)],
                    total.at[chunk, :, pl.ds(first - start, last - first)],
                    sem.at[i],
                )
            )
    return copies


def ring_own_kernel(slots, idx_ref, inputs, own_refs, outputs, bufs, sems):
    wait_all(fetch(idx_ref, slots, own_refs[0], bufs, sems))
    outputs[0].ref[...] = low_total(bufs[0], inputs[0].ref()[...], inputs[1].ref()[...])


def ring_put_kernel(starts, slots, cols, fresh, onward, idx_ref, *refs):
    number = len(slots)
    pieces = refs[:number]
    wide, sems, pass_buf, pass_sems = refs[-4:]
    passed = refs[-4 - onward : -4]
    totals = refs[-4 - onward - len(starts) : -4 - onward]
    leaving = []
    for i, ref in enumerate(passed):
        width = ref.shape[1]
        pass_buf[i, :, :width] = pieces[i][:, :width] if i == 0 else pieces[i][:, -width:]
        leaving += start_all(
            [pltpu.make_async_copy(pass_buf.at[i, :, pl.ds(0, width)], ref, pass_sems.at[i])]
        )
    for i in range(number):
        part = pl.ds(0, pieces[i].shape[1])
        wide[i, :, part] = pieces[i][...].astype(f32)
        leaving += start_all(
            put_copies(
                idx_ref[slots[i]], cols[i], wide.at[i, :, part], totals, starts, sems.at[i]
            )
        )
    wait_all(leaving)


def ring_sum(own, ahead, behind, widths, axis):
    count = lax.axis_size(axis)
    half = count // 2
    full_rows, cols = own.shape
    rows = full_rows // count
    own = own.reshape(count, rows, cols)
    cut = ahead.shape[1]
    starts = [sum(widths[:i]) for i in range(len(widths))]
    idx = ring_index(axis)
    chunk = shape_of((rows, cols), bf16)
    halves = [shape_of((rows, cut), bf16), shape_of((rows, cols - cut), bf16)]
    sums = [shape_of((count, rows, width), f32) for width in widths]

    def taken(number):
        return [pltpu.VMEM((number, rows, cols), bf16), pltpu.SemaphoreType.DMA((number,))]

    def put(totals, pieces, slots, passed, after):
        number = len(pieces)
        first_cols = (0,) * number if pieces[0].shape[1] == cols else (0, cut)
        fresh = totals is None
        out = pl.pallas_call(
            functools.partial(
                ring_put_kernel,
                starts,
                tuple(k % count for k in slots),
                first_cols,
                fresh,
                len(passed),
            ),
            in_specs=[SCALARS]
            + [HERE] * number
            + [IN_HBM] * (0 if fresh else len(sums))
            + [ANYWHERE] * len(after),
            out_specs=[IN_HBM] * (len(sums) + len(passed)),
            out_shape=sums + passed,
            scratch_shapes=[
                pltpu.VMEM((number, rows, cols), f32),
                pltpu.SemaphoreType.DMA((number, len(sums))),
                pltpu.VMEM((2, rows, cols), bf16),
                pltpu.SemaphoreType.DMA((2,)),
            ],
            input_output_aliases={} if fresh else {1 + number + i: i for i in range(len(sums))},
            name="ring_put",
            **params_of(RING_LIMIT),
        )(idx, *pieces, *([] if fresh else totals), *after)
        return out[: len(sums)], out[len(sums) :]

    def both_ways(ahead, behind):
        return ring_shift(ahead, axis, 1), ring_shift(behind, axis, -1)

    token = behind
    ahead, behind = both_ways(ahead, behind)
    token = yield token
    for k in range(half - 1, 0, -1):
        ahead, behind = local_call(
            functools.partial(ring_add_kernel, (k % count, (-k) % count)),
            "ring_add",
            [idx],
            [ahead, behind],
            [own],
            [chunk, chunk],
            taken(2),
            [token],
            RING_LIMIT,
        )
        token = behind
        ahead, behind = both_ways(ahead, behind)
        token = yield token
    (mine,) = local_call(
        functools.partial(ring_own_kernel, (0,)),
        "ring_own",
        [idx],
        [ahead, behind],
        [own],
        [chunk],
        taken(1),
        [token],
        RING_LIMIT,
    )
    ahead, behind = both_ways(mine, mine)
    totals, (token,) = put(None, [mine], [0], [shape_of((rows, LANES), bf16)], [])
    token = yield token
    for k in range(1, half):
        passed = halves if k == half - 1 else [chunk, chunk]
        totals, passed = put(totals, [ahead, behind], [-k, k], passed, [token])
        token = passed[1]
        ahead, behind = both_ways(*passed)
        token = yield token
    totals, _ = put(totals, [ahead, behind], [-half, half], [], [token])
    yield [total.reshape(full_rows, -1) for total in totals]


def swap(vals):
    return lax.ppermute(vals, "wsh", [(0, 1), (1, 0)])


def pass_on(vals, by):
    pairs = [(0, 1)] if by > 0 else [(1, 0)]
    return lax.ppermute(vals, "section", pairs)


def block_places(block_pair, count):
    want = jnp.arange(2 * count, dtype=jnp.int32)
    device = jnp.arange(count, dtype=jnp.int32)
    first = (block_pair[None, :] == want[:, None]).astype(jnp.int32)
    second = ((2 * count - 1 - block_pair)[None, :] == want[:, None]).astype(jnp.int32)
    return jnp.sum(first * (2 * device) + second * (2 * device + 1), axis=1)


def row_positions(block_pair, stored, tok_dev):
    count = block_pair.shape[0]
    device = stored // tok_dev
    within = stored % tok_dev
    half_rows = tok_dev // 2
    matches = device[:, None] == jnp.arange(count, dtype=jnp.int32)[None, :]
    pair_block = jnp.sum(jnp.where(matches, block_pair[None, :], 0), axis=1)
    block_idx = jnp.where(within < half_rows, pair_block, 2 * count - 1 - pair_block)
    return block_idx * half_rows + within % half_rows


def rotary_table(positions, head_size):
    half_rot = ROT // 2
    lane = jnp.arange(LANES, dtype=jnp.int32) % head_size
    inv_freq = ROPE_BASE ** (-((lane % half_rot).astype(f32) * 2.0) / ROT)
    angles = positions.astype(f32)[:, None] * inv_freq[None, :]
    cosine, sine = jnp.cos(angles), jnp.sin(angles)
    lead, second = (lane < half_rot)[None], ((lane >= half_rot) & (lane < ROT))[None]
    return jnp.stack(
        [
            jnp.where(lead | second, cosine, 1.0),
            jnp.where(lead, -sine, 0.0),
            jnp.where(second, sine, 0.0),
        ]
    )


def body(
    inputs,
    cotangent,
    block_pair,
    qkv_weight,
    qkv_bias,
    proj_weight,
    proj_bias,
    up_weight,
    up_bias,
    down_weight,
    down_bias,
    attn_gain,
    attn_shift,
    mlp_gain,
    mlp_shift,
):
    first_section = lax.axis_index("section") == 0
    count = lax.axis_size("ctx")
    micros, _, tok_dev, dim = inputs.shape
    head_size = dim // HEADS
    half = dim // 2
    my_half = lax.axis_index("wsh")
    wsh = jnp.stack([my_half.astype(jnp.int32), first_section.astype(jnp.int32)])
    one_pair_each = count == dim // LANES

    wq, wp, wu, wd = (w[0] for w in (qkv_weight, proj_weight, up_weight, down_weight))
    small = jnp.concatenate(
        [
            v[0].reshape(-1, half)
            for v in (
                attn_gain,
                attn_shift,
                mlp_gain,
                mlp_shift,
                proj_bias,
                down_bias,
                qkv_bias,
                up_bias,
            )
        ],
        axis=0,
    )
    small_oth = swap(small)
    wq_oth = swap(wq)
    first_here = lax.optimization_barrier((wq_oth, small_oth))
    wq_oth, small_oth = first_here
    wu_oth = swap(tied(wq_oth, wu)[0])
    wd_oth = swap(tied(wq_oth, wd)[0])
    wp_oth = swap(tied(wu_oth, wp)[0])
    low_part = jnp.where(my_half == 0, small, small_oth).astype(f32)
    high_part = jnp.where(my_half == 0, small_oth, small).astype(f32)
    vecs = jnp.concatenate([low_part[:6], high_part[:6]], axis=1)
    qkv_rows = 6 + qkv_bias.shape[1] // half
    proj_b, down_b = vecs[4:5], vecs[5:6]
    qkv_b = jnp.concatenate([low_part[6:qkv_rows], high_part[6:qkv_rows]], axis=0).reshape(1, -1)
    up_b = jnp.concatenate([low_part[qkv_rows:], high_part[qkv_rows:]], axis=0).reshape(1, -1)

    local_rows = lax.axis_index("ctx") * tok_dev + jnp.arange(tok_dev, dtype=jnp.int32)
    query_pos = row_positions(block_pair, local_rows, tok_dev)
    key_pos = row_positions(block_pair, jnp.arange(count * tok_dev, dtype=jnp.int32), tok_dev)
    tab = rotary_table(query_pos, head_size)
    loc = block_places(block_pair, count)

    def exchange(vals):
        return lax.all_to_all(vals, "ctx", split_axis=0, concat_axis=0, tiled=True)

    rows_in = [inputs[i, 0] for i in range(micros)]
    cot_in = [cotangent[i, 0] for i in range(micros)]

    def norm_qkv(index, got):
        return qkv_call(rows_in[index], got, vecs, qkv_b, tab, wq, wq_oth, wsh)

    def mlp(made, save):
        return mlp_call(made[2], made[3], up_b, down_b, wu, wu_oth, wd, wd_oth, wsh, save)

    def mlp_back(dy, mlp_kept, after=(), limit=VMEM_LIMIT):
        return mlp_back_call(dy, mlp_kept[1], wu, wu_oth, wd, wd_oth, wsh, after, limit)

    def out_back(index, got, joined=None):
        return da_call(cot_in[index], got, wp, wp_oth, wsh, joined)

    def moved(vals):
        return exchange(vals) if one_pair_each else vals

    def attend(qkv, after=()):
        if one_pair_each:
            attended, lse = attend_call(qkv, loc, after)
            return attended, (qkv, lse)
        return wide_attend(qkv, query_pos, key_pos)

    def attend_back(kept, da, after=(), limit=VMEM_LIMIT):
        if one_pair_each:
            return attend_back_call(kept[0], da, kept[1], loc, after, limit)
        da = da[:, 0] if da.ndim == 4 else da
        return wide_attend_back(kept, da, query_pos, key_pos)

    def project(attended, made, mlp_out, after=(), limit=VMEM_LIMIT):
        return proj_call(attended, made[1], mlp_out[0], proj_b, wp, wp_oth, wsh, after, limit)

    def input_grad_of(dqkv, made, dy, dnm, after=(), limit=VMEM_LIMIT):
        return dx_call(dqkv, tab, made[1], dy, dnm, vecs, wq, wq_oth, wsh, after, limit)

    made_a = norm_qkv(0, None)
    qkv_a = moved(made_a[0])
    mlp_a = mlp(made_a, False)
    att_a, _ = attend(qkv_a, [mlp_a[0]])
    att_a = moved(att_a)
    da_a, dy_a = out_back(0, None)
    y_a = project(att_a, made_a, mlp_a, [dy_a])[0]
    da_a = moved(tied(y_a, da_a)[0])

    made_b = norm_qkv(1, pass_on(y_a, 1))
    qkv_2 = moved(tied(da_a, made_b[0])[0])
    norms_b = swap(made_b[3])
    mlp_b = mlp(made_b, True)
    att_b, kept_b = attend(qkv_2, [mlp_b[0], norms_b])
    att_b = moved(att_b)
    gt_b = swap(mlp_b[3])
    dqkv_a_ = attend_back(kept_b, da_a, [gt_b])
    dqkv_a = moved(dqkv_a_)
    y_b, *a_b = project(att_b, made_b, mlp_b, [dqkv_a_])

    made_c = norm_qkv(0, pass_on(y_b, 1))
    qkv_3 = moved(tied(dqkv_a, made_c[0])[0])
    norms_c = swap(made_c[3])
    a_b_oth = swap(a_b[1])
    _, dnm_a = mlp_back(dy_a, mlp_b, [made_c[1]])
    _, dx_a, _ = input_grad_of(dqkv_a, made_b, dy_a, dnm_a, [norms_c, a_b_oth])
    got_a = pass_on(dx_a, -1)
    mlp_c = mlp_call(
        made_c[2], tied(dx_a, made_c[3])[0], up_b, down_b, wu, wu_oth, wd, wd_oth, wsh, True
    )
    da_b, dy_b = out_back(1, tied(mlp_c[0], got_a)[0])
    da_b = moved(tied(qkv_3, da_b)[0])
    att_c, kept_c = attend(qkv_3, [dy_b])
    dy_b_oth, gt_c = swap(dy_b), swap(mlp_c[3])
    dqkv_b = attend_back(kept_c, da_b, [dy_b_oth, gt_c])
    dqkv_b_ = moved(dqkv_b)
    du_b, dnm_b = mlp_back(dy_b, mlp_c, [dqkv_b])
    du_b_oth = swap(du_b)
    back_b, dx_b, sums_b = input_grad_of(dqkv_b_, made_c, dy_b, dnm_b, [du_b_oth])
    got_b = pass_on(dx_b, -1)
    back_b_oth = swap(back_b)

    da_c, dy_c = out_back(0, tied(back_b_oth, got_b)[0], att_c if one_pair_each else None)
    dy_list = [dy_c, dy_b, swap(dy_c), dy_b_oth]
    da_c = moved(da_c)
    idx = ring_index("ctx")
    *down_made, dy_sum = down_grad_call(idx, [mlp_b[2], mlp_c[2], gt_b, gt_c], dy_list, count)
    down_ring = ring_sum(*down_made, (dim,), "ctx")
    dqkv_c_ = attend_back(kept_b, da_c, [dy_sum], TAIL_LIMIT)
    dqkv_c = moved(dqkv_c_)
    next(down_ring)
    token = down_ring.send(dqkv_c_)
    du_c, dnm_c = mlp_back(dy_c, mlp_b, [token], TAIL_LIMIT)
    token = down_ring.send(dnm_c)
    *up_made, du_sum = up_grad_call(
        idx,
        [made_b[2], made_c[2], norms_b, norms_c],
        [du_c, du_b, swap(du_c), du_b_oth],
        count,
        [token],
    )
    up_ring = ring_sum(*up_made, (up_made[0].shape[1],), "ctx")
    token = next(up_ring)
    steps = count + 1
    left = {down_ring: steps - 3, up_ring: steps - 1}
    results = {}

    def turn(ring, token):
        if not left[ring]:
            return token
        left[ring] -= 1
        made = ring.send(token)
        if left[ring] == 0:
            results[ring] = made
            return token
        return made

    for ring in (down_ring, up_ring):
        token = turn(ring, token)
    back_c, dx_c, sums_c = input_grad_of(dqkv_c, made_b, dy_c, dnm_c, [token], TAIL_LIMIT)
    back_c_oth = swap(back_c)
    token = turn(down_ring, dx_c)
    y_c, *a_c = project(da_c if one_pair_each else att_c, made_c, mlp_c, [token], TAIL_LIMIT)
    a_c_oth = swap(a_c[1])
    token = turn(up_ring, y_c)
    norm_sums = sums_b + sums_c
    norm_own = lax.dynamic_slice_in_dim(norm_sums, my_half * half, half, 1)
    norm_oth = swap(lax.dynamic_slice_in_dim(norm_sums, (1 - my_half) * half, half, 1))

    def own_part(vec):
        size = vec.shape[1] // 2
        return lax.dynamic_slice_in_dim(vec, my_half * size, size, 1).reshape(-1, LANES)

    small = [(norm_own + norm_oth).reshape(-1, LANES), own_part(dy_sum), own_part(du_sum)]
    *attn_made, attn_sum = attn_grad_call(
        idx,
        wsh,
        [made_b[2], made_c[2], norms_b, norms_c],
        [a_b[0], a_c[0], a_b_oth, a_c_oth],
        [back_c, back_b, back_c_oth, back_b_oth],
        dy_list,
        jnp.concatenate(small, axis=0),
        count,
        [token],
    )
    attn_ring = ring_sum(*attn_made, (3 * dim, dim, LANES), "ctx")
    token = next(attn_ring)
    left[attn_ring] = steps - 1
    at = 0
    while any(left.values()):
        token = turn((up_ring, attn_ring, down_ring, attn_ring)[at % 4], token)
        at += 1
    (down_grad,) = results[down_ring]
    (up_grad,) = results[up_ring]
    qkv_grad, proj_grad, summed = results[attn_ring]

    sizes = [v.shape[0] for v in small] + [3 * dim // 2 // LANES]
    ends = [sum(sizes[: i + 1]) for i in range(4)]
    norm_grads, dy_total, up_b_grad, qkv_b_grad = (
        summed[end - size : end] for end, size in zip(ends, sizes)
    )
    norm_grads, dy_total = norm_grads.reshape(4, 1, half), dy_total.reshape(1, half)
    pick = lambda yes, no: jnp.where(first_section, yes, no)
    layer_out = jnp.stack([pick(y_c, y_b), pick(y_b, y_c)])[None, :, None]
    input_grad = jnp.stack([pick(dx_b, dx_c), pick(dx_c, dx_b)])[None, :, None]
    return (
        layer_out,
        input_grad,
        qkv_grad[None],
        qkv_b_grad.reshape(1, -1),
        proj_grad[None],
        dy_total,
        up_grad[None],
        up_b_grad.reshape(1, -1),
        down_grad[None],
        dy_total,
        norm_grads[0],
        norm_grads[1],
        norm_grads[2],
        norm_grads[3],
    )


def solution(mesh):
    in_specs = (
        P(None, "wsh", "ctx", None),
        P(None, "wsh", "ctx", None),
        P(),
        P("section", "wsh", None),
        P("section", "wsh"),
        P("section", "wsh", None),
        P("section", "wsh"),
        P("section", "wsh", None),
        P("section", "wsh"),
        P("section", "wsh", None),
        P("section", "wsh"),
        P("section", "wsh"),
        P("section", "wsh"),
        P("section", "wsh"),
        P("section", "wsh"),
    )
    out_specs = (
        P("section", None, "wsh", "ctx", None),
        P("section", None, "wsh", "ctx", None),
        P("section", "wsh", None),
        P("section", "wsh"),
        P("section", "wsh", None),
        P("section", "wsh"),
        P("section", "wsh", None),
        P("section", "wsh"),
        P("section", "wsh", None),
        P("section", "wsh"),
        P("section", "wsh"),
        P("section", "wsh"),
        P("section", "wsh"),
        P("section", "wsh"),
    )
    return jax.shard_map(body, mesh=mesh, in_specs=in_specs, out_specs=out_specs, check_vma=False)
```

```python
import functools

import jax
import jax.numpy as jnp
from jax import lax
from jax.experimental import pallas as pl
from jax.experimental.pallas import tpu as pltpu
from jax.sharding import PartitionSpec as P

HEADS = 16
ROT = 16
NORM_EPS = 1e-05
ROPE_BASE = 10000.0
MASKED_SCORE = -1e30
LANES = 128
VMEM_LIMIT = 50 * 1024 * 1024
TAIL_LIMIT = VMEM_LIMIT
RING_LIMIT = VMEM_LIMIT
INV_SQRT2 = 0.7071067811865476
INV_SQRT_2PI = 0.3989422804014327

f32 = jnp.float32
bf16 = jnp.bfloat16


def dot_nn(left, right):
    return lax.dot_general(left, right, (((1,), (0,)), ((), ())), preferred_element_type=f32)


def dot_nt(left, right):
    return lax.dot_general(left, right, (((1,), (1,)), ((), ())), preferred_element_type=f32)


def params_of(limit):
    return dict(
        compiler_params=pltpu.CompilerParams(vmem_limit_bytes=limit),
        cost_estimate=pl.CostEstimate(flops=1, bytes_accessed=1, transcendentals=0),
    )


def whole(shape):
    rank = len(shape)
    return pl.BlockSpec(shape, lambda *args: (0,) * rank)


def shape_of(shape, dtype):
    return jax.ShapeDtypeStruct(shape, dtype)


def rope(vals, tab_ref):
    return (
        vals * tab_ref[0]
        + pltpu.roll(vals, LANES - ROT // 2, 1) * tab_ref[1]
        + pltpu.roll(vals, ROT // 2, 1) * tab_ref[2]
    )


def unrope(vals, tab_ref):
    return (
        vals * tab_ref[0]
        - pltpu.roll(vals, LANES - ROT // 2, 1) * tab_ref[1]
        - pltpu.roll(vals, ROT // 2, 1) * tab_ref[2]
    )


def normalized(hidden):
    row_mean = jnp.mean(hidden, axis=-1, keepdims=True)
    centered = hidden - row_mean
    spread = jnp.mean(centered * centered, axis=-1, keepdims=True)
    scale = lax.rsqrt(spread + NORM_EPS)
    return centered * scale, scale


def start_all(copies):
    for copy in copies:
        copy.start()
    return copies


def wait_all(copies):
    for copy in copies:
        copy.wait()


def qkv_kernel(own_given, wsh_ref, inputs, weights, outputs, buf, sems):
    half, dim = buf.shape[2:]
    copies = start_all(
        [
            pltpu.make_async_copy(
                weight.at[:, pl.ds(part * dim, dim)], buf.at[part, side], sems.at[part, side]
            )
            for part in range(3)
            for side, weight in enumerate(weights)
        ]
    )
    out, x_out, own, oth = outputs
    x = inputs[0].ref()[...]
    if not own_given:
        x = jnp.where(wsh_ref[1] == 1, x, inputs[4].ref()[...])
    x_out.ref[...] = x
    x_out.send()
    xhat, _ = normalized(x.astype(f32))
    vec_ref, bias_ref, tab_ref = (item.ref() for item in inputs[1:4])
    na = (xhat * vec_ref[0:1] + vec_ref[1:2]).astype(bf16)
    nm = (xhat * vec_ref[2:3] + vec_ref[3:4]).astype(bf16)
    first = wsh_ref[0] == 0
    for i, rows in enumerate((na, nm)):
        own.ref[i] = jnp.where(first, rows[:, :half], rows[:, half:])
        oth.ref[i] = jnp.where(first, rows[:, half:], rows[:, :half])
    own.send()
    oth.send()
    for part in range(3):
        wait_all(copies[2 * part : 2 * part + 2])
        for at in range(0, dim, 2 * LANES):
            cols = slice(at, at + 2 * LANES)
            res = (
                dot_nn(own.ref[0], buf[part, 0, :, cols])
                + dot_nn(oth.ref[0], buf[part, 1, :, cols])
                + bias_ref[:, part * dim + at : part * dim + at + 2 * LANES]
            )
            for i in range(2):
                vals = res[:, i * LANES : (i + 1) * LANES]
                if part < 2:
                    vals = rope(vals, tab_ref)
                out.ref[at // LANES + i, part] = vals.astype(bf16)


def layer_of(shape, index):
    return pl.BlockSpec((pl.squeezed,) + shape, lambda *args: (index, 0, 0))


HERE = pl.BlockSpec(memory_space=pltpu.VMEM)
SCALARS = pl.BlockSpec(memory_space=pltpu.SMEM)
ANYWHERE = pl.BlockSpec(memory_space=pl.ANY)
IN_HBM = pl.BlockSpec(memory_space=pltpu.HBM)


class Arriving:
    def __init__(self, buf, copy=None):
        self.buf, self.copy = buf, copy

    def ref(self):
        if self.copy is not None:
            self.copy.wait()
            self.copy = None
        return self.buf


class Leaving:
    def __init__(self, buf, copy=None):
        self.ref, self.copy, self.sent = buf, copy, copy is None

    def send(self):
        if not self.sent:
            self.copy.start()
            self.sent = True


def local_kernel(body, near_in, near_out, scalars, weights, followed, *refs):
    refs = list(refs)

    def take(number):
        taken = refs[:number]
        del refs[:number]
        return taken

    scalar_refs, array_refs = take(scalars), take(len(near_in))
    weight_refs, _, out_refs = take(weights), take(followed), take(len(near_out))
    in_sems, out_sems = take(2)
    inputs, outputs = [], []
    for i, (near, ref) in enumerate(zip(near_in, array_refs)):
        if near:
            inputs.append(Arriving(ref))
        else:
            buf = take(1)[0]
            copy = pltpu.make_async_copy(ref, buf, in_sems.at[i])
            copy.start()
            inputs.append(Arriving(buf, copy))
    for i, (near, ref) in enumerate(zip(near_out, out_refs)):
        if near:
            outputs.append(Leaving(ref))
        else:
            buf = take(1)[0]
            outputs.append(Leaving(buf, pltpu.make_async_copy(buf, ref, out_sems.at[i])))
    body(*scalar_refs, inputs, weight_refs, outputs, *refs)
    for item in inputs:
        item.ref()
    for item in outputs:
        item.send()
    for item in outputs:
        if item.copy is not None:
            item.copy.wait()


def far(array):
    return (array,)


def local_call(body, name, scalars, arrays, weights, out_shape, scratch=(), after=(), limit=VMEM_LIMIT):
    near_in = [not isinstance(a, tuple) for a in arrays]
    near_out = [not isinstance(o, tuple) for o in out_shape]
    raw_out = [isinstance(o, list) for o in out_shape]
    arrays = [a if near else a[0] for a, near in zip(arrays, near_in)]
    shapes = [o if near and not raw else o[0] for o, near, raw in zip(out_shape, near_out, raw_out)]
    far_bufs = [
        pltpu.VMEM(a.shape, a.dtype)
        for a, near in zip(arrays + shapes, near_in + near_out)
        if not near
    ]
    return pl.pallas_call(
        functools.partial(
            local_kernel, body, near_in, near_out, len(scalars), len(weights), len(after)
        ),
        in_specs=[SCALARS] * len(scalars)
        + [HERE if near else IN_HBM for near in near_in]
        + [IN_HBM] * len(weights)
        + [ANYWHERE] * len(after),
        out_specs=[HERE if near and not raw else IN_HBM for near, raw in zip(near_out, raw_out)],
        out_shape=shapes,
        scratch_shapes=[
            pltpu.SemaphoreType.DMA((len(arrays) + 1,)),
            pltpu.SemaphoreType.DMA((len(shapes),)),
        ]
        + far_bufs
        + list(scratch),
        name=name,
        **params_of(limit),
    )(*scalars, *arrays, *weights, *after)


def qkv_call(given, got, vecs, qkv_b, tab, w_own, w_oth, wsh):
    rows, dim = given.shape
    half = w_own.shape[0]
    pairs = dim // LANES
    return local_call(
        functools.partial(qkv_kernel, got is None),
        "qkv_proj",
        [wsh],
        [given, vecs, qkv_b, tab] if got is None else [given, vecs, qkv_b, tab, got],
        [w_own, w_oth],
        [shape_of((pairs, 3, rows, LANES), bf16), shape_of((rows, dim), bf16)]
        + [shape_of((2, rows, half), bf16)] * 2,
        [pltpu.VMEM((3, 2, half, dim), bf16), pltpu.SemaphoreType.DMA((3, 2))],
    )


FF_TILE = 1024
FF_PIECE = 512


def ff_tiles(wsh_ref, up_own, up_oth, dn_own, dn_oth, up_buf, dn_buf, sems):
    own = dn_own.shape[0] // FF_TILE
    tiles = []
    for t in range(2 * own):
        start = pl.multiple_of(((wsh_ref[0] * own + t) % (2 * own)) * FF_TILE, FF_TILE)
        cols = pl.ds(start, FF_TILE)
        down = (dn_own if t < own else dn_oth).at[pl.ds((t % own) * FF_TILE, FF_TILE)]
        copies = [
            pltpu.make_async_copy(up_own.at[:, cols], up_buf.at[t, 0], sems.at[t, 0]),
            pltpu.make_async_copy(up_oth.at[:, cols], up_buf.at[t, 1], sems.at[t, 1]),
            pltpu.make_async_copy(down, dn_buf.at[t], sems.at[t, 2]),
        ]
        tiles.append((t, start, start_all(copies)))
    for t, start, copies in tiles:
        wait_all(copies)
        for at in range(0, FF_TILE, FF_PIECE):
            row = (t % own) * FF_TILE + at
            place = pl.ds(pl.multiple_of(start + at, FF_PIECE), FF_PIECE)
            yield t, place, t < own, slice(row, row + FF_PIECE), slice(at, at + FF_PIECE)


def ff_scratch(half, ff, dim):
    tiles = ff // FF_TILE
    return [
        pltpu.VMEM((tiles, 2, half, FF_TILE), bf16),
        pltpu.VMEM((tiles, FF_TILE, dim), bf16),
        pltpu.SemaphoreType.DMA((tiles, 3)),
    ]


def mlp_kernel(save, wsh_ref, inputs, weights, outputs, up_buf, dn_buf, sems):
    out_ref = outputs[0].ref
    started = False
    for t, place, held, rows, piece in ff_tiles(wsh_ref, *weights, up_buf, dn_buf, sems):
        own_ref, oth_ref, up_b, down_b = (item.ref() for item in inputs)
        if not started:
            out_ref[...] = jnp.broadcast_to(down_b[...], out_ref.shape)
            started = True
        pre = (
            dot_nn(own_ref[1], up_buf[t, 0, :, piece])
            + dot_nn(oth_ref[1], up_buf[t, 1, :, piece])
            + up_b[:, place]
        )
        gate = 0.5 + 0.5 * lax.erf(pre * INV_SQRT2)
        act = (pre * gate).astype(bf16)
        if save:
            slope = gate + pre * (INV_SQRT_2PI * jnp.exp(-0.5 * pre * pre))
            outputs[1].ref[place] = slope.astype(bf16).T
            outputs[2 if held else 3].ref[rows] = act.T
            if not held:
                outputs[2].send()
        out_ref[...] += dot_nn(act, dn_buf[t, piece])


def mlp_call(own, oth, up_b, down_b, up_own, up_oth, dn_own, dn_oth, wsh, save):
    rows, half = own.shape[1:]
    dim = dn_own.shape[1]
    ff = up_own.shape[1]
    out_shape = [shape_of((rows, dim), f32)]
    if save:
        out_shape += [shape_of((ff, rows), bf16)]
        out_shape += [shape_of((ff // 2, rows), bf16)] * 2
    return local_call(
        functools.partial(mlp_kernel, save),
        "mlp_forward",
        [wsh],
        [own, oth, up_b, down_b],
        [up_own, up_oth, dn_own, dn_oth],
        out_shape,
        ff_scratch(half, ff, dim),
    )


def mlp_back_kernel(wsh_ref, inputs, weights, outputs, acc_own, acc_oth, up_buf, dn_buf, sems):
    du, dnm = outputs
    half = acc_own.shape[0]
    acc_own[...] = jnp.zeros(acc_own.shape, f32)
    acc_oth[...] = jnp.zeros(acc_oth.shape, f32)
    for t, place, _, _, piece in ff_tiles(wsh_ref, *weights, up_buf, dn_buf, sems):
        dy_ref, slope_ref = (item.ref() for item in inputs)
        dact = dot_nt(dn_buf[t, piece], dy_ref[...])
        vals = (dact * slope_ref[place].astype(f32)).astype(bf16)
        du.ref[place] = vals
        acc_own[...] += dot_nn(up_buf[t, 0, :, piece], vals)
        acc_oth[...] += dot_nn(up_buf[t, 1, :, piece], vals)
    du.send()
    first = wsh_ref[0] == 0
    dnm.ref[:, :half] = jnp.where(first, acc_own[...], acc_oth[...]).T
    dnm.ref[:, half:] = jnp.where(first, acc_oth[...], acc_own[...]).T


def mlp_back_call(dy, slope, up_own, up_oth, dn_own, dn_oth, wsh, after, limit):
    rows, dim = dy.shape
    half, ff = up_own.shape
    return local_call(
        mlp_back_kernel,
        "mlp_backward",
        [wsh],
        [dy, slope],
        [up_own, up_oth, dn_own, dn_oth],
        [shape_of(slope.shape, bf16), shape_of((rows, dim), f32)],
        [pltpu.VMEM((half, rows), f32), pltpu.VMEM((half, rows), f32)] + ff_scratch(half, ff, dim),
        after,
        limit,
    )


def sort_in(loc_ref, ref, dst, half_rows, part=None):
    for block in range(dst.shape[0] // half_rows):
        place = loc_ref[block]
        rows = pl.ds(pl.multiple_of((place % 2) * half_rows, half_rows), half_rows)
        if part is None:
            vals = ref[place // 2, rows, :]
        else:
            vals = ref[place // 2, part, rows, :]
        dst[block * half_rows : (block + 1) * half_rows] = vals


def sort_out(loc_ref, vals, ref, half_rows, part=None):
    for block in range(vals.shape[0] // half_rows):
        place = loc_ref[block]
        rows = pl.ds(pl.multiple_of((place % 2) * half_rows, half_rows), half_rows)
        piece = vals[block * half_rows : (block + 1) * half_rows]
        if part is None:
            ref[place // 2, rows, :] = piece
        else:
            ref[place // 2, part, rows, :] = piece


def head_of(vals, head):
    lane = lax.broadcasted_iota(jnp.int32, vals.shape, 1)
    return jnp.where(lane // (LANES // 2) == head, vals, jnp.zeros_like(vals))


def scores_of(keys, queries, scale, diagonal):
    scores = dot_nt(keys, queries) * scale
    if diagonal:
        key_at = lax.broadcasted_iota(jnp.int32, scores.shape, 0)
        query_at = lax.broadcasted_iota(jnp.int32, scores.shape, 1)
        scores = jnp.where(key_at <= query_at, scores, MASKED_SCORE)
    return scores


def attend_kernel(tile, loc_ref, inputs, weights, outputs, q_s, k_s, v_s, vt_s, o_s):
    qkv_ref = inputs[0].ref()
    o_ref, lse_ref = (item.ref for item in outputs)
    half_rows = qkv_ref.shape[2] // 2
    seq = q_s.shape[0]
    head_size = LANES // 2
    scale = head_size**-0.5
    sort_in(loc_ref, qkv_ref, q_s, half_rows, 0)
    sort_in(loc_ref, qkv_ref, k_s, half_rows, 1)
    sort_in(loc_ref, qkv_ref, v_s, half_rows, 2)
    vt_s[...] = v_s[...].T
    for t in range(seq // tile):
        rows = slice(t * tile, (t + 1) * tile)
        queries = q_s[rows]
        outs = []
        for head in range(2):
            picked = head_of(queries, head)
            parts = [
                scores_of(k_s[i * tile : (i + 1) * tile], picked, scale, i == t)
                for i in range(t + 1)
            ]
            top = functools.reduce(
                jnp.maximum, [jnp.max(p, axis=0, keepdims=True) for p in parts]
            )
            parts = [jnp.exp(p - top) for p in parts]
            total = sum(jnp.sum(p, axis=0, keepdims=True) for p in parts)
            lse_ref[head : head + 1, rows] = top + jnp.log(total)
            inverse = 1.0 / total
            acc = None
            for i, p in enumerate(parts):
                term = dot_nn(
                    vt_s[head * head_size : (head + 1) * head_size, i * tile : (i + 1) * tile],
                    (p * inverse).astype(bf16),
                )
                acc = term if acc is None else acc + term
            outs.append(acc)
        o_s[rows] = jnp.concatenate(outs, axis=0).T.astype(bf16)
    sort_out(loc_ref, o_s, o_ref, half_rows)


def attend_call(qkv, loc, after):
    count, _, rows, _ = qkv.shape
    seq = count * rows
    return local_call(
        functools.partial(attend_kernel, 256),
        "attention",
        [loc],
        [qkv],
        [],
        [shape_of((count, rows, LANES), bf16), shape_of((2, seq), f32)],
        [
            pltpu.VMEM((seq, LANES), bf16),
            pltpu.VMEM((seq, LANES), bf16),
            pltpu.VMEM((seq, LANES), bf16),
            pltpu.VMEM((LANES, seq), bf16),
            pltpu.VMEM((seq, LANES), bf16),
        ],
        after,
    )


def attend_back_kernel(
    tile, part, loc_ref, inputs, weights, outputs, q_s, k_s, v_s, da_s, kt_s, dq_s, dk_s, dv_s
):
    da_ref, qkv_ref, lse_ref = (item.ref() for item in inputs)
    out_ref = outputs[0].ref
    half_rows = qkv_ref.shape[2] // 2
    seq = q_s.shape[0]
    head_size = LANES // 2
    scale = head_size**-0.5
    sort_in(loc_ref, qkv_ref, q_s, half_rows, 0)
    sort_in(loc_ref, qkv_ref, k_s, half_rows, 1)
    sort_in(loc_ref, qkv_ref, v_s, half_rows, 2)
    sort_in(loc_ref, da_ref, da_s, half_rows, part)
    kt_s[...] = k_s[...].T
    dk_s[...] = jnp.zeros(dk_s.shape, f32)
    dv_s[...] = jnp.zeros(dv_s.shape, f32)
    for t in range(seq // tile):
        rows = slice(t * tile, (t + 1) * tile)
        outs = []
        for head in range(2):
            queries = head_of(q_s[rows], head)
            grads = head_of(da_s[rows], head)
            lse = lse_ref[head : head + 1, rows]
            probs, dprobs, row_dot = [], [], 0.0
            for i in range(t + 1):
                keys = slice(i * tile, (i + 1) * tile)
                p = jnp.exp(scores_of(k_s[keys], queries, scale, i == t) - lse)
                dp = dot_nt(v_s[keys], grads)
                row_dot = row_dot + jnp.sum(p * dp, axis=0, keepdims=True)
                dv_s[keys] += dot_nn(p.astype(bf16), grads)
                probs.append(p)
                dprobs.append(dp)
            acc = None
            for i in range(t + 1):
                keys = slice(i * tile, (i + 1) * tile)
                ds = (probs[i] * (dprobs[i] - row_dot) * scale).astype(bf16)
                dk_s[keys] += dot_nn(ds, queries)
                term = dot_nn(kt_s[head * head_size : (head + 1) * head_size, keys], ds)
                acc = term if acc is None else acc + term
            outs.append(acc)
        dq_s[rows] = jnp.concatenate(outs, axis=0).T.astype(bf16)
    sort_out(loc_ref, dq_s, out_ref, half_rows, 0)
    k_s[...] = dk_s[...].astype(bf16)
    v_s[...] = dv_s[...].astype(bf16)
    sort_out(loc_ref, k_s, out_ref, half_rows, 1)
    sort_out(loc_ref, v_s, out_ref, half_rows, 2)


def attend_back_call(qkv, da, lse, loc, after, limit):
    count, _, rows, _ = qkv.shape
    seq = count * rows
    part = 0 if da.ndim == 4 else None
    (res,) = local_call(
        functools.partial(attend_back_kernel, 256, part),
        "attention_backward",
        [loc],
        [da, qkv, lse],
        [],
        [shape_of(qkv.shape, bf16)],
        [pltpu.VMEM((seq, LANES), bf16)] * 4
        + [pltpu.VMEM((LANES, seq), bf16), pltpu.VMEM((seq, LANES), bf16)]
        + [pltpu.VMEM((seq, LANES), f32)] * 2,
        after,
        limit,
    )
    return res


def by_head(parts):
    pairs, rows, lanes = parts.shape
    return jnp.transpose(parts, (1, 0, 2)).reshape(rows, HEADS, pairs * lanes // HEADS)


def by_pair(heads):
    rows = heads.shape[0]
    return jnp.transpose(heads.reshape(rows, -1, LANES), (1, 0, 2))


def wide_scores(queries, keys, query_pos, key_pos):
    raw = jnp.einsum("qhd,khd->hqk", queries, keys, preferred_element_type=f32)
    allowed = (query_pos[:, None] >= key_pos[None, :])[None]
    return jnp.where(allowed, raw * queries.shape[-1] ** (-0.5), MASKED_SCORE)


def key_blocks(arrays, rows):
    return tuple(a.reshape((a.shape[0] // rows, rows) + a.shape[1:]) for a in arrays)


def wide_attend(qkv, query_pos, key_pos):
    queries = by_head(qkv[:, 0])
    keys = lax.all_gather(by_head(qkv[:, 1]), "ctx", axis=0, tiled=True)
    values = lax.all_gather(by_head(qkv[:, 2]), "ctx", axis=0, tiled=True)
    block = min(512, keys.shape[0])
    split = key_blocks((keys, values, key_pos), block)
    rows, _, head_size = queries.shape

    def max_step(carry, block_in):
        top, total = carry
        scores = wide_scores(queries, block_in[0], query_pos, block_in[2])
        new_top = jnp.maximum(top, jnp.max(scores, axis=-1))
        part = jnp.sum(jnp.exp(scores - new_top[..., None]), axis=-1)
        return ((new_top, total * jnp.exp(top - new_top) + part), None)

    start = (jnp.full((HEADS, rows), MASKED_SCORE, f32), jnp.zeros((HEADS, rows), f32))
    (top, total), _ = lax.scan(max_step, start, split)
    lse = top + jnp.log(total)

    def value_step(running, block_in):
        scores = wide_scores(queries, block_in[0], query_pos, block_in[2])
        probs = jnp.exp(scores - lse[..., None]).astype(bf16)
        term = jnp.einsum("hqk,khd->qhd", probs, block_in[1], preferred_element_type=f32)
        return (running + term, None)

    attended, _ = lax.scan(value_step, jnp.zeros((rows, HEADS, head_size), f32), split)
    return by_pair(attended.astype(bf16)), (queries, keys, values, lse)


def wide_attend_back(kept, da, query_pos, key_pos):
    queries, keys, values, lse = kept
    grads = by_head(da)
    block = min(512, keys.shape[0])
    split = key_blocks((keys, values, key_pos), block)
    scale = queries.shape[-1] ** (-0.5)

    def pieces(block_in):
        scores = wide_scores(queries, block_in[0], query_pos, block_in[2])
        probs = jnp.exp(scores - lse[..., None])
        dprobs = jnp.einsum("qhd,khd->hqk", grads, block_in[1], preferred_element_type=f32)
        return probs, dprobs

    def dot_step(running, block_in):
        probs, dprobs = pieces(block_in)
        return (running + jnp.sum(probs * dprobs, axis=-1), None)

    row_dot, _ = lax.scan(dot_step, jnp.zeros(lse.shape, f32), split)

    def key_step(running, block_in):
        probs, dprobs = pieces(block_in)
        ds = (scale * probs * (dprobs - row_dot[..., None])).astype(bf16)
        running = running + jnp.einsum("hqk,khd->qhd", ds, block_in[0], preferred_element_type=f32)
        dk = jnp.einsum("hqk,qhd->khd", ds, queries, preferred_element_type=f32)
        dv = jnp.einsum("hqk,qhd->khd", probs.astype(bf16), grads, preferred_element_type=f32)
        return (running, (dk.astype(bf16), dv.astype(bf16)))

    dq, (dk, dv) = lax.scan(key_step, jnp.zeros(queries.shape, f32), split)
    dk, dv = (
        lax.psum_scatter(part.reshape(keys.shape), "ctx", scatter_dimension=0, tiled=True)
        for part in (dk, dv)
    )
    return jnp.stack([by_pair(dq.astype(bf16)), by_pair(dk), by_pair(dv)], axis=1)


def lanes_of(ref):
    return jnp.concatenate([ref[i] for i in range(ref.shape[0])], axis=1)


def both_halves(w_own, w_oth, buf, sems):
    return start_all(
        [
            pltpu.make_async_copy(weight, buf.at[side], sems.at[side])
            for side, weight in enumerate((w_own, w_oth))
        ]
    )


def half_scratch(weight):
    return [pltpu.VMEM((2,) + weight.shape, bf16), pltpu.SemaphoreType.DMA((2,))]


def proj_kernel(part, wsh_ref, inputs, weights, outputs, buf, sems):
    copies = both_halves(*weights, buf, sems)
    y, own, oth = outputs
    half = buf.shape[1]
    first = wsh_ref[0] == 0
    a_ref = inputs[0].ref()
    a = lanes_of(a_ref if part is None else a_ref.at[:, part])
    own.ref[...] = jnp.where(first, a[:, :half], a[:, half:])
    oth.ref[...] = jnp.where(first, a[:, half:], a[:, :half])
    own.send()
    oth.send()
    bias_ref, x_ref, mlp_ref = (item.ref() for item in inputs[1:])
    wait_all(copies)
    attn = dot_nn(own.ref[...], buf[0]) + dot_nn(oth.ref[...], buf[1]) + bias_ref[...]
    y.ref[...] = (x_ref[...].astype(f32) + attn + mlp_ref[...]).astype(bf16)


def proj_call(a, x, mlp, bias, p_own, p_oth, wsh, after, limit):
    rows, dim = x.shape
    half = p_own.shape[0]
    return local_call(
        functools.partial(proj_kernel, 1 if a.ndim == 4 else None),
        "attn_out",
        [wsh],
        [a, bias, x, mlp],
        [p_own, p_oth],
        [shape_of((rows, dim), bf16)] + [shape_of((rows, half), bf16)] * 2,
        half_scratch(p_own),
        after,
        limit,
    )


def da_kernel(own_given, wsh_ref, inputs, weights, outputs, buf, sems):
    copies = both_halves(*weights, buf, sems)
    out_ref, dy_out = outputs[0].ref, outputs[1]
    dy = inputs[0].ref()[...]
    if not own_given:
        dy = jnp.where(wsh_ref[1] == 1, inputs[1].ref()[...], dy)
    dy_out.ref[...] = dy
    dy_out.send()
    wsh = wsh_ref[0]
    joined = len(out_ref.shape) == 4
    if joined:
        out_ref[:, 1] = inputs[2].ref()[...]
    count = out_ref.shape[0] // 2
    for place, side in ((wsh * count, 0), ((1 - wsh) * count, 1)):
        copies[side].wait()
        part = dot_nt(dy, buf[side]).astype(bf16)
        for i in range(count):
            vals = part[:, i * LANES : (i + 1) * LANES]
            if joined:
                out_ref[place + i, 0] = vals
            else:
                out_ref[place + i] = vals


def da_call(given, got, p_own, p_oth, wsh, joined=None):
    rows, dim = given.shape
    pairs = dim // LANES
    arrays = [given] + ([] if got is None else [got])
    arrays += [] if joined is None else [joined]
    shape = (pairs, rows, LANES) if joined is None else (pairs, 2, rows, LANES)
    return local_call(
        functools.partial(da_kernel, got is None),
        "attn_out_backward",
        [wsh],
        arrays,
        [p_own, p_oth],
        [shape_of(shape, bf16), shape_of((rows, dim), bf16)],
        half_scratch(p_own),
    )


def dx_kernel(wsh_ref, inputs, weights, outputs, grad_s, buf, sems):
    copies = both_halves(*weights, buf, sems)
    back, dx, sums = outputs
    dqkv_ref, tab_ref = inputs[0].ref(), inputs[1].ref()
    pairs = dqkv_ref.shape[0]
    for part in range(3):
        for pair in range(pairs):
            vals = dqkv_ref[pair, part]
            if part < 2:
                vals = unrope(vals.astype(f32), tab_ref).astype(bf16)
            back.ref[pair, part] = vals
            grad_s[:, pl.ds((part * pairs + pair) * LANES, LANES)] = vals
    back.send()
    vec_ref, x_ref, dy_ref, dnm_ref = (item.ref() for item in inputs[2:])
    first = wsh_ref[0] == 0
    copies[0].wait()
    own = dot_nt(grad_s[...], buf[0])
    copies[1].wait()
    oth = dot_nt(grad_s[...], buf[1])
    dna = jnp.concatenate([jnp.where(first, own, oth), jnp.where(first, oth, own)], axis=1)
    dnm = dnm_ref[...]
    xhat, scale = normalized(x_ref[...].astype(f32))
    grad = dna * vec_ref[0:1] + dnm * vec_ref[2:3]
    inner = (
        grad
        - jnp.mean(grad, axis=-1, keepdims=True)
        - xhat * jnp.mean(grad * xhat, axis=-1, keepdims=True)
    )
    dx.ref[...] = (dy_ref[...].astype(f32) + scale * inner).astype(bf16)
    dx.send()
    sums.ref[0:1] = jnp.sum(dna * xhat, axis=0, keepdims=True)
    sums.ref[1:2] = jnp.sum(dna, axis=0, keepdims=True)
    sums.ref[2:3] = jnp.sum(dnm * xhat, axis=0, keepdims=True)
    sums.ref[3:4] = jnp.sum(dnm, axis=0, keepdims=True)


def dx_call(dqkv, tab, x, dy, dnm, vecs, w_own, w_oth, wsh, after, limit):
    rows, dim = x.shape
    return local_call(
        dx_kernel,
        "section_input_grad",
        [wsh],
        [dqkv, tab, vecs, x, dy, dnm],
        [w_own, w_oth],
        [shape_of(o, t) for o, t in ((dqkv.shape, bf16), ((rows, dim), bf16), ((4, dim), f32))],
        [pltpu.VMEM((rows, 3 * dim), bf16)] + half_scratch(w_own),
        after,
        limit,
    )


def joined_rows(items):
    return jnp.concatenate([item.ref()[...] for item in items], axis=0)


class Pieces:
    def __init__(self, out_ref, buf, sems):
        self.out_ref, self.buf, self.sems, self.copies = out_ref, buf, sems, []

    def put(self, rows, cols, vals):
        self.buf[rows, cols] = vals.astype(bf16)
        at = len(self.copies)
        self.copies.append(
            pltpu.make_async_copy(
                self.buf.at[rows, cols], self.out_ref.at[rows, cols], self.sems.at[at]
            )
        )
        self.copies[-1].start()

    def finish(self, chunk, ahead, behind):
        height, cut = ahead.ref.shape
        rows = pl.ds(pl.multiple_of(chunk * height, height), height)
        ahead.ref[...] = self.buf[rows, :cut]
        ahead.send()
        behind.ref[...] = self.buf[rows, cut:]
        behind.send()
        wait_all(self.copies)


def first_half(cols):
    return cols // 2 // LANES * LANES


def grad_call(body, name, scalars, arrays, shape, width, count, scratch, after):
    cut = first_half(shape[1])
    halves = [far(shape_of((shape[0] // count, c), bf16)) for c in (cut, shape[1] - cut)]
    return local_call(
        functools.partial(body, len(arrays)),
        name,
        scalars,
        arrays,
        [],
        [[shape_of(shape, bf16)]] + halves + [far(shape_of((1, width), f32))],
        [pltpu.VMEM(shape, bf16), pltpu.SemaphoreType.DMA((5,))] + scratch,
        after,
        TAIL_LIMIT,
    )


def parts_of(items, number):
    size = len(items) // number
    return [items[i * size : (i + 1) * size] for i in range(number)]


def down_grad_kernel(number, idx_ref, inputs, weights, outputs, buf, sems):
    gts, dys = parts_of(inputs, 2)
    out = Pieces(outputs[0].ref, buf, sems)
    dy = joined_rows(dys)
    outputs[3].ref[...] = jnp.sum(dy.astype(f32), axis=0, keepdims=True)
    rows, dim = buf.shape
    tile = rows // 4
    for t in range(4):
        part = slice(t * tile, (t + 1) * tile)
        left = jnp.concatenate([item.ref()[part] for item in gts], axis=1)
        out.put(part, slice(0, dim), dot_nn(left, dy))
    out.finish(idx_ref[idx_ref.shape[0] // 2], outputs[1], outputs[2])


def down_grad_call(idx, gt_list, dy_list, count):
    dim = dy_list[0].shape[1]
    return grad_call(
        down_grad_kernel,
        "down_grad",
        [idx],
        [far(a) for a in gt_list + dy_list],
        (gt_list[0].shape[0], dim),
        dim,
        count,
        [],
        [],
    )


def up_grad_kernel(number, idx_ref, inputs, weights, outputs, buf, sems):
    norms, dus = parts_of(inputs, 2)
    out = Pieces(outputs[0].ref, buf, sems)
    left = jnp.concatenate([item.ref()[1] for item in norms], axis=0).T
    rows, ff = buf.shape
    tile = ff // 4
    for t in range(4):
        part = slice(t * tile, (t + 1) * tile)
        du = jnp.concatenate([item.ref()[part] for item in dus], axis=1)
        outputs[3].ref[:, part] = dot_nt(jnp.ones((8, du.shape[1]), bf16), du)[:1]
        out.put(slice(0, rows), part, dot_nt(left, du))
    out.finish(idx_ref[idx_ref.shape[0] // 2], outputs[1], outputs[2])


def up_grad_call(idx, norm_list, du_list, count, after):
    half, ff = norm_list[0].shape[2], du_list[0].shape[0]
    return grad_call(
        up_grad_kernel,
        "up_grad",
        [idx],
        [far(a) for a in norm_list + du_list],
        (half, ff),
        ff,
        count,
        [],
        after,
    )


def attn_grad_kernel(number, idx_ref, wsh_ref, inputs, weights, outputs, buf, sems, small_s):
    norms, outs, dqkvs, dys = parts_of(inputs[:-1], 4)
    out = Pieces(outputs[0].ref, buf, sems)
    sums = outputs[3].ref
    rows, dim = buf.shape[0], sums.shape[1] // 4
    left = jnp.concatenate([item.ref()[0] for item in norms], axis=0).T
    for part in range(4):
        cols = slice(part * dim, (part + 1) * dim)
        if part < 3:
            right = jnp.concatenate([lanes_of(item.ref().at[:, part]) for item in dqkvs], axis=0)
        else:
            left, right = joined_rows(outs).T, joined_rows(dys)
        sums[:, cols] = jnp.sum(right.astype(f32), axis=0, keepdims=True)
        out.put(slice(0, rows), cols, dot_nn(left, right))
    given = inputs[-1].ref()
    at = given.shape[0]
    small_s[:at] = given[...]
    base = wsh_ref[0] * (3 * dim // 2)
    for i in range(3 * dim // 2 // LANES):
        place = pl.ds(pl.multiple_of(base + i * LANES, LANES), LANES)
        small_s[at + i : at + i + 1] = sums[:, place]
    small = small_s[...]
    empty = jnp.zeros((rows - small.shape[0], LANES), f32)
    out.put(slice(0, rows), slice(4 * dim, 4 * dim + LANES), jnp.concatenate([small, empty], axis=0))
    out.finish(idx_ref[idx_ref.shape[0] // 2], outputs[1], outputs[2])


def attn_grad_call(idx, wsh, norm_list, out_list, dqkv_list, dy_list, small, count, after):
    half, dim = norm_list[0].shape[2], dy_list[0].shape[1]
    return grad_call(
        attn_grad_kernel,
        "attn_grad",
        [idx, wsh],
        [far(a) for a in norm_list + out_list + dqkv_list + dy_list] + [small],
        (half, 4 * dim + LANES),
        4 * dim,
        count,
        [pltpu.VMEM((small.shape[0] + 3 * dim // 2 // LANES, LANES), f32)],
        after,
    )


def ring_of(count):
    return list(range(0, count, 2)) + list(range(count - 1, 0, -2))


def ring_place(axis):
    count = lax.axis_size(axis)
    me = lax.axis_index(axis)
    return jnp.where(me % 2 == 0, me // 2, count - (me + 1) // 2)


def ring_index(axis):
    count = lax.axis_size(axis)
    return (ring_place(axis) + jnp.arange(count, dtype=jnp.int32)) % count


def ring_shift(vals, axis, by):
    order = ring_of(lax.axis_size(axis))
    count = len(order)
    pairs = [(order[i], order[(i + by) % count]) for i in range(count)]
    return lax.ppermute(vals, axis, pairs)


def tied(token, *vals):
    return lax.optimization_barrier((token, vals))[1]


def fetch(idx_ref, slots, own_ref, bufs, sems):
    return start_all(
        [
            pltpu.make_async_copy(own_ref.at[idx_ref[slot]], bufs.at[i], sems.at[i])
            for i, slot in enumerate(slots)
        ]
    )


def low_total(*terms):
    total = terms[0].astype(f32)
    for term in terms[1:]:
        total = total + term.astype(f32)
    return total.astype(bf16)


def ring_add_kernel(slot, side, idx_ref, inputs, own_refs, outputs, bufs, sems):
    wait_all(fetch(idx_ref, (slot,), own_refs[0], bufs, sems))
    out, got = outputs[0].ref, inputs[0].ref()
    cols, cut = out.shape[1], got.shape[1]
    summed = slice(0, cut) if side == 0 else slice(cols - cut, cols)
    out[:, summed] = low_total(bufs[0, :, summed], got[...])
    if cut < cols:
        rest = slice(cut, cols) if side == 0 else slice(0, cols - cut)
        out[:, rest] = bufs[0, :, rest]


def put_copies(chunk, cols, buf, totals, starts, sem):
    lo, hi = cols, cols + buf.shape[1]
    copies = []
    for i, (total, start) in enumerate(zip(totals, starts)):
        first, last = max(lo, start), min(hi, start + total.shape[2])
        if first < last:
            copies.append(
                pltpu.make_async_copy(
                    buf.at[:, pl.ds(first - lo, last - first)],
                    total.at[chunk, :, pl.ds(first - start, last - first)],
                    sem.at[i],
                )
            )
    return copies


def ring_own_kernel(slots, idx_ref, inputs, own_refs, outputs, bufs, sems):
    wait_all(fetch(idx_ref, slots, own_refs[0], bufs, sems))
    outputs[0].ref[...] = low_total(bufs[0], inputs[0].ref()[...], inputs[1].ref()[...])


def ring_put_kernel(starts, slots, cols, fresh, onward, side, idx_ref, *refs):
    number = len(slots)
    pieces = refs[:number]
    wide, sems, pass_buf, pass_sems = refs[-4:]
    passed = refs[-4 - onward : -4]
    totals = refs[-4 - onward - len(starts) : -4 - onward]
    leaving = []
    for i, ref in enumerate(passed):
        width = ref.shape[1]
        pass_buf[i, :, :width] = pieces[i][:, :width] if side == 0 else pieces[i][:, -width:]
        leaving += start_all(
            [pltpu.make_async_copy(pass_buf.at[i, :, pl.ds(0, width)], ref, pass_sems.at[i])]
        )
    for i in range(number):
        part = pl.ds(0, pieces[i].shape[1])
        wide[i, :, part] = pieces[i][...].astype(f32)
        leaving += start_all(
            put_copies(
                idx_ref[slots[i]], cols[i], wide.at[i, :, part], totals, starts, sems.at[i]
            )
        )
    wait_all(leaving)


def ring_sum(own, ahead, behind, widths, axis):
    count = lax.axis_size(axis)
    half = count // 2
    full_rows, cols = own.shape
    rows = full_rows // count
    own = own.reshape(count, rows, cols)
    cut = ahead.shape[1]
    starts = [sum(widths[:i]) for i in range(len(widths))]
    idx = ring_index(axis)
    chunk = shape_of((rows, cols), bf16)
    halves = [shape_of((rows, cut), bf16), shape_of((rows, cols - cut), bf16)]
    sums = [shape_of((count, rows, width), f32) for width in widths]

    def taken(number):
        return [pltpu.VMEM((number, rows, cols), bf16), pltpu.SemaphoreType.DMA((number,))]

    def put(totals, pieces, slots, passed, after, side=0):
        number = len(pieces)
        first_cols = (0,) * number if pieces[0].shape[1] == cols else (0, cut)
        fresh = totals is None
        out = pl.pallas_call(
            functools.partial(
                ring_put_kernel,
                starts,
                tuple(k % count for k in slots),
                first_cols,
                fresh,
                len(passed),
                side,
            ),
            in_specs=[SCALARS]
            + [HERE] * number
            + [IN_HBM] * (0 if fresh else len(sums))
            + [ANYWHERE] * len(after),
            out_specs=[IN_HBM] * (len(sums) + len(passed)),
            out_shape=sums + passed,
            scratch_shapes=[
                pltpu.VMEM((number, rows, cols), f32),
                pltpu.SemaphoreType.DMA((number, len(sums))),
                pltpu.VMEM((1, rows, cols), bf16),
                pltpu.SemaphoreType.DMA((1,)),
            ],
            input_output_aliases={} if fresh else {1 + number + i: i for i in range(len(sums))},
            name="ring_put",
            **params_of(RING_LIMIT),
        )(idx, *pieces, *([] if fresh else totals), *after)
        return out[: len(sums)], out[len(sums) :]

    def both_ways(ahead, behind):
        return ring_shift(ahead, axis, 1), ring_shift(behind, axis, -1)

    token = behind
    moving = list(both_ways(ahead, behind))
    token = yield token
    for k in range(half - 1, 0, -1):
        for side, slot in enumerate((k % count, (-k) % count)):
            (summed,) = local_call(
                functools.partial(ring_add_kernel, slot, side),
                "ring_add",
                [idx],
                [moving[side]],
                [own],
                [chunk],
                taken(1),
                [token],
                RING_LIMIT,
            )
            moving[side] = ring_shift(summed, axis, 1 - 2 * side)
            token = yield summed
    (mine,) = local_call(
        functools.partial(ring_own_kernel, (0,)),
        "ring_own",
        [idx],
        moving,
        [own],
        [chunk],
        taken(1),
        [token],
        RING_LIMIT,
    )
    moving = list(both_ways(mine, mine))
    totals, (token,) = put(None, [mine], [0], [shape_of((rows, LANES), bf16)], [])
    token = yield token
    for k in range(1, half):
        for side, slot in enumerate((-k, k)):
            passed = [halves[side] if k == half - 1 else chunk]
            totals, (passed,) = put(totals, [moving[side]], [slot], passed, [token], side)
            moving[side] = ring_shift(passed, axis, 1 - 2 * side)
            token = yield passed
    totals, _ = put(totals, moving, [-half, half], [], [token])
    yield [total.reshape(full_rows, -1) for total in totals]


def swap(vals):
    return lax.ppermute(vals, "wsh", [(0, 1), (1, 0)])


def pass_on(vals, by):
    pairs = [(0, 1)] if by > 0 else [(1, 0)]
    return lax.ppermute(vals, "section", pairs)


def block_places(block_pair, count):
    want = jnp.arange(2 * count, dtype=jnp.int32)
    device = jnp.arange(count, dtype=jnp.int32)
    first = (block_pair[None, :] == want[:, None]).astype(jnp.int32)
    second = ((2 * count - 1 - block_pair)[None, :] == want[:, None]).astype(jnp.int32)
    return jnp.sum(first * (2 * device) + second * (2 * device + 1), axis=1)


def row_positions(block_pair, stored, tok_dev):
    count = block_pair.shape[0]
    device = stored // tok_dev
    within = stored % tok_dev
    half_rows = tok_dev // 2
    matches = device[:, None] == jnp.arange(count, dtype=jnp.int32)[None, :]
    pair_block = jnp.sum(jnp.where(matches, block_pair[None, :], 0), axis=1)
    block_idx = jnp.where(within < half_rows, pair_block, 2 * count - 1 - pair_block)
    return block_idx * half_rows + within % half_rows


def rotary_table(positions, head_size):
    half_rot = ROT // 2
    lane = jnp.arange(LANES, dtype=jnp.int32) % head_size
    inv_freq = ROPE_BASE ** (-((lane % half_rot).astype(f32) * 2.0) / ROT)
    angles = positions.astype(f32)[:, None] * inv_freq[None, :]
    cosine, sine = jnp.cos(angles), jnp.sin(angles)
    lead, second = (lane < half_rot)[None], ((lane >= half_rot) & (lane < ROT))[None]
    return jnp.stack(
        [
            jnp.where(lead | second, cosine, 1.0),
            jnp.where(lead, -sine, 0.0),
            jnp.where(second, sine, 0.0),
        ]
    )


def body(
    inputs,
    cotangent,
    block_pair,
    qkv_weight,
    qkv_bias,
    proj_weight,
    proj_bias,
    up_weight,
    up_bias,
    down_weight,
    down_bias,
    attn_gain,
    attn_shift,
    mlp_gain,
    mlp_shift,
):
    first_section = lax.axis_index("section") == 0
    count = lax.axis_size("ctx")
    micros, _, tok_dev, dim = inputs.shape
    head_size = dim // HEADS
    half = dim // 2
    my_half = lax.axis_index("wsh")
    wsh = jnp.stack([my_half.astype(jnp.int32), first_section.astype(jnp.int32)])
    one_pair_each = count == dim // LANES

    wq, wp, wu, wd = (w[0] for w in (qkv_weight, proj_weight, up_weight, down_weight))
    small = jnp.concatenate(
        [
            v[0].reshape(-1, half)
            for v in (
                attn_gain,
                attn_shift,
                mlp_gain,
                mlp_shift,
                proj_bias,
                down_bias,
                qkv_bias,
                up_bias,
            )
        ],
        axis=0,
    )
    small_oth = swap(small)
    wq_oth = swap(wq)
    first_here = lax.optimization_barrier((wq_oth, small_oth))
    wq_oth, small_oth = first_here
    wu_oth = swap(tied(wq_oth, wu)[0])
    wd_oth = swap(tied(wq_oth, wd)[0])
    wp_oth = swap(tied(wu_oth, wp)[0])
    low_part = jnp.where(my_half == 0, small, small_oth).astype(f32)
    high_part = jnp.where(my_half == 0, small_oth, small).astype(f32)
    vecs = jnp.concatenate([low_part[:6], high_part[:6]], axis=1)
    qkv_rows = 6 + qkv_bias.shape[1] // half
    proj_b, down_b = vecs[4:5], vecs[5:6]
    qkv_b = jnp.concatenate([low_part[6:qkv_rows], high_part[6:qkv_rows]], axis=0).reshape(1, -1)
    up_b = jnp.concatenate([low_part[qkv_rows:], high_part[qkv_rows:]], axis=0).reshape(1, -1)

    local_rows = lax.axis_index("ctx") * tok_dev + jnp.arange(tok_dev, dtype=jnp.int32)
    query_pos = row_positions(block_pair, local_rows, tok_dev)
    key_pos = row_positions(block_pair, jnp.arange(count * tok_dev, dtype=jnp.int32), tok_dev)
    tab = rotary_table(query_pos, head_size)
    loc = block_places(block_pair, count)

    def exchange(vals):
        return lax.all_to_all(vals, "ctx", split_axis=0, concat_axis=0, tiled=True)

    rows_in = [inputs[i, 0] for i in range(micros)]
    cot_in = [cotangent[i, 0] for i in range(micros)]

    def norm_qkv(index, got):
        return qkv_call(rows_in[index], got, vecs, qkv_b, tab, wq, wq_oth, wsh)

    def mlp(made, save):
        return mlp_call(made[2], made[3], up_b, down_b, wu, wu_oth, wd, wd_oth, wsh, save)

    def mlp_back(dy, mlp_kept, after=(), limit=VMEM_LIMIT):
        return mlp_back_call(dy, mlp_kept[1], wu, wu_oth, wd, wd_oth, wsh, after, limit)

    def out_back(index, got, joined=None):
        return da_call(cot_in[index], got, wp, wp_oth, wsh, joined)

    def moved(vals):
        return exchange(vals) if one_pair_each else vals

    def attend(qkv, after=()):
        if one_pair_each:
            attended, lse = attend_call(qkv, loc, after)
            return attended, (qkv, lse)
        return wide_attend(qkv, query_pos, key_pos)

    def attend_back(kept, da, after=(), limit=VMEM_LIMIT):
        if one_pair_each:
            return attend_back_call(kept[0], da, kept[1], loc, after, limit)
        da = da[:, 0] if da.ndim == 4 else da
        return wide_attend_back(kept, da, query_pos, key_pos)

    def project(attended, made, mlp_out, after=(), limit=VMEM_LIMIT):
        return proj_call(attended, made[1], mlp_out[0], proj_b, wp, wp_oth, wsh, after, limit)

    def input_grad_of(dqkv, made, dy, dnm, after=(), limit=VMEM_LIMIT):
        return dx_call(dqkv, tab, made[1], dy, dnm, vecs, wq, wq_oth, wsh, after, limit)

    made_a = norm_qkv(0, None)
    qkv_a = moved(made_a[0])
    mlp_a = mlp(made_a, False)
    att_a, _ = attend(qkv_a, [mlp_a[0]])
    att_a = moved(att_a)
    da_a, dy_a = out_back(0, None)
    y_a = project(att_a, made_a, mlp_a, [dy_a])[0]
    da_a = moved(tied(y_a, da_a)[0])

    made_b = norm_qkv(1, pass_on(y_a, 1))
    qkv_2 = moved(tied(da_a, made_b[0])[0])
    norms_b = swap(made_b[3])
    mlp_b = mlp(made_b, True)
    att_b, kept_b = attend(qkv_2, [mlp_b[0], norms_b])
    att_b = moved(att_b)
    gt_b = swap(mlp_b[3])
    dqkv_a_ = attend_back(kept_b, da_a, [gt_b])
    dqkv_a = moved(dqkv_a_)
    y_b, *a_b = project(att_b, made_b, mlp_b, [dqkv_a_])

    made_c = norm_qkv(0, pass_on(y_b, 1))
    qkv_3 = moved(tied(dqkv_a, made_c[0])[0])
    norms_c = swap(made_c[3])
    a_b_oth = swap(a_b[1])
    _, dnm_a = mlp_back(dy_a, mlp_b, [made_c[1]])
    _, dx_a, _ = input_grad_of(dqkv_a, made_b, dy_a, dnm_a, [norms_c, a_b_oth])
    got_a = pass_on(dx_a, -1)
    mlp_c = mlp_call(
        made_c[2], tied(dx_a, made_c[3])[0], up_b, down_b, wu, wu_oth, wd, wd_oth, wsh, True
    )
    da_b, dy_b = out_back(1, tied(mlp_c[0], got_a)[0])
    da_b = moved(tied(qkv_3, da_b)[0])
    att_c, kept_c = attend(qkv_3, [dy_b])
    dy_b_oth, gt_c = swap(dy_b), swap(mlp_c[3])
    dqkv_b = attend_back(kept_c, da_b, [dy_b_oth, gt_c])
    dqkv_b_ = moved(dqkv_b)
    du_b, dnm_b = mlp_back(dy_b, mlp_c, [dqkv_b])
    du_b_oth = swap(du_b)
    back_b, dx_b, sums_b = input_grad_of(dqkv_b_, made_c, dy_b, dnm_b, [du_b_oth])
    got_b = pass_on(dx_b, -1)
    back_b_oth = swap(back_b)

    da_c, dy_c = out_back(0, tied(back_b_oth, got_b)[0], att_c if one_pair_each else None)
    dy_list = [dy_c, dy_b, swap(dy_c), dy_b_oth]
    da_c = moved(da_c)
    idx = ring_index("ctx")
    *down_made, dy_sum = down_grad_call(idx, [mlp_b[2], mlp_c[2], gt_b, gt_c], dy_list, count)
    down_ring = ring_sum(*down_made, (dim,), "ctx")
    left, results = {}, {}

    def start(ring):
        left[ring] = 2 * count - 2
        return next(ring)

    def turns(token, *rings):
        for ring in rings:
            if left[ring]:
                left[ring] -= 1
                made = ring.send(token)
                if left[ring]:
                    token = made
                else:
                    results[ring] = made
        return token

    dqkv_c_ = attend_back(kept_b, da_c, [dy_sum], TAIL_LIMIT)
    dqkv_c = moved(dqkv_c_)
    start(down_ring)
    token = turns(dqkv_c_, down_ring, down_ring)
    du_c, dnm_c = mlp_back(dy_c, mlp_b, [token], TAIL_LIMIT)
    token = turns(dnm_c, down_ring, down_ring)
    *up_made, du_sum = up_grad_call(
        idx,
        [made_b[2], made_c[2], norms_b, norms_c],
        [du_c, du_b, swap(du_c), du_b_oth],
        count,
        [token],
    )
    up_ring = ring_sum(*up_made, (up_made[0].shape[1],), "ctx")
    token = turns(start(up_ring), down_ring, down_ring, up_ring, up_ring)
    back_c, dx_c, sums_c = input_grad_of(dqkv_c, made_b, dy_c, dnm_c, [token], TAIL_LIMIT)
    back_c_oth = swap(back_c)
    token = turns(dx_c, down_ring, up_ring)
    y_c, *a_c = project(da_c if one_pair_each else att_c, made_c, mlp_c, [token], TAIL_LIMIT)
    a_c_oth = swap(a_c[1])
    token = turns(y_c, up_ring)
    norm_sums = sums_b + sums_c
    norm_own = lax.dynamic_slice_in_dim(norm_sums, my_half * half, half, 1)
    norm_oth = swap(lax.dynamic_slice_in_dim(norm_sums, (1 - my_half) * half, half, 1))

    def own_part(vec):
        size = vec.shape[1] // 2
        return lax.dynamic_slice_in_dim(vec, my_half * size, size, 1).reshape(-1, LANES)

    small = [(norm_own + norm_oth).reshape(-1, LANES), own_part(dy_sum), own_part(du_sum)]
    *attn_made, attn_sum = attn_grad_call(
        idx,
        wsh,
        [made_b[2], made_c[2], norms_b, norms_c],
        [a_b[0], a_c[0], a_b_oth, a_c_oth],
        [back_c, back_b, back_c_oth, back_b_oth],
        dy_list,
        jnp.concatenate(small, axis=0),
        count,
        [token],
    )
    attn_ring = ring_sum(*attn_made, (3 * dim, dim, LANES), "ctx")
    token = start(attn_ring)
    while any(left.values()):
        token = turns(token, attn_ring, up_ring, down_ring)
    (down_grad,) = results[down_ring]
    (up_grad,) = results[up_ring]
    qkv_grad, proj_grad, summed = results[attn_ring]

    sizes = [v.shape[0] for v in small] + [3 * dim // 2 // LANES]
    ends = [sum(sizes[: i + 1]) for i in range(4)]
    norm_grads, dy_total, up_b_grad, qkv_b_grad = (
        summed[end - size : end] for end, size in zip(ends, sizes)
    )
    norm_grads, dy_total = norm_grads.reshape(4, 1, half), dy_total.reshape(1, half)
    pick = lambda yes, no: jnp.where(first_section, yes, no)
    layer_out = jnp.stack([pick(y_c, y_b), pick(y_b, y_c)])[None, :, None]
    input_grad = jnp.stack([pick(dx_b, dx_c), pick(dx_c, dx_b)])[None, :, None]
    return (
        layer_out,
        input_grad,
        qkv_grad[None],
        qkv_b_grad.reshape(1, -1),
        proj_grad[None],
        dy_total,
        up_grad[None],
        up_b_grad.reshape(1, -1),
        down_grad[None],
        dy_total,
        norm_grads[0],
        norm_grads[1],
        norm_grads[2],
        norm_grads[3],
    )


def solution(mesh):
    in_specs = (
        P(None, "wsh", "ctx", None),
        P(None, "wsh", "ctx", None),
        P(),
        P("section", "wsh", None),
        P("section", "wsh"),
        P("section", "wsh", None),
        P("section", "wsh"),
        P("section", "wsh", None),
        P("section", "wsh"),
        P("section", "wsh", None),
        P("section", "wsh"),
        P("section", "wsh"),
        P("section", "wsh"),
        P("section", "wsh"),
        P("section", "wsh"),
    )
    out_specs = (
        P("section", None, "wsh", "ctx", None),
        P("section", None, "wsh", "ctx", None),
        P("section", "wsh", None),
        P("section", "wsh"),
        P("section", "wsh", None),
        P("section", "wsh"),
        P("section", "wsh", None),
        P("section", "wsh"),
        P("section", "wsh", None),
        P("section", "wsh"),
        P("section", "wsh"),
        P("section", "wsh"),
        P("section", "wsh"),
        P("section", "wsh"),
    )
    return jax.shard_map(body, mesh=mesh, in_specs=in_specs, out_specs=out_specs, check_vma=False)
```

```python
import functools

import jax
import jax.numpy as jnp
from jax import lax
from jax.experimental import pallas as pl
from jax.experimental.pallas import tpu as pltpu
from jax.sharding import PartitionSpec as P

HEADS = 16
ROT = 16
NORM_EPS = 1e-05
ROPE_BASE = 10000.0
MASKED_SCORE = -1e30
LANES = 128
VMEM_LIMIT = 50 * 1024 * 1024
TAIL_LIMIT = VMEM_LIMIT
RING_LIMIT = VMEM_LIMIT
INV_SQRT2 = 0.7071067811865476
INV_SQRT_2PI = 0.3989422804014327

f32 = jnp.float32
bf16 = jnp.bfloat16


def dot_nn(left, right):
    return lax.dot_general(left, right, (((1,), (0,)), ((), ())), preferred_element_type=f32)


def dot_nt(left, right):
    return lax.dot_general(left, right, (((1,), (1,)), ((), ())), preferred_element_type=f32)


def params_of(limit):
    return dict(
        compiler_params=pltpu.CompilerParams(vmem_limit_bytes=limit),
        cost_estimate=pl.CostEstimate(flops=1, bytes_accessed=1, transcendentals=0),
    )


def whole(shape):
    rank = len(shape)
    return pl.BlockSpec(shape, lambda *args: (0,) * rank)


def shape_of(shape, dtype):
    return jax.ShapeDtypeStruct(shape, dtype)


def rope(vals, tab_ref):
    return (
        vals * tab_ref[0]
        + pltpu.roll(vals, LANES - ROT // 2, 1) * tab_ref[1]
        + pltpu.roll(vals, ROT // 2, 1) * tab_ref[2]
    )


def unrope(vals, tab_ref):
    return (
        vals * tab_ref[0]
        - pltpu.roll(vals, LANES - ROT // 2, 1) * tab_ref[1]
        - pltpu.roll(vals, ROT // 2, 1) * tab_ref[2]
    )


def normalized(hidden):
    row_mean = jnp.mean(hidden, axis=-1, keepdims=True)
    centered = hidden - row_mean
    spread = jnp.mean(centered * centered, axis=-1, keepdims=True)
    scale = lax.rsqrt(spread + NORM_EPS)
    return centered * scale, scale


def start_all(copies):
    for copy in copies:
        copy.start()
    return copies


def wait_all(copies):
    for copy in copies:
        copy.wait()


def qkv_kernel(own_given, wsh_ref, inputs, weights, outputs, buf, sems):
    half, dim = buf.shape[2:]
    copies = start_all(
        [
            pltpu.make_async_copy(
                weight.at[:, pl.ds(part * dim, dim)], buf.at[part, side], sems.at[part, side]
            )
            for part in range(3)
            for side, weight in enumerate(weights)
        ]
    )
    out, x_out, own, oth = outputs
    x = inputs[0].ref()[...]
    if not own_given:
        x = jnp.where(wsh_ref[1] == 1, x, inputs[4].ref()[...])
    x_out.ref[...] = x
    x_out.send()
    xhat, _ = normalized(x.astype(f32))
    vec_ref, bias_ref, tab_ref = (item.ref() for item in inputs[1:4])
    na = (xhat * vec_ref[0:1] + vec_ref[1:2]).astype(bf16)
    nm = (xhat * vec_ref[2:3] + vec_ref[3:4]).astype(bf16)
    first = wsh_ref[0] == 0
    for i, rows in enumerate((na, nm)):
        own.ref[i] = jnp.where(first, rows[:, :half], rows[:, half:])
        oth.ref[i] = jnp.where(first, rows[:, half:], rows[:, :half])
    own.send()
    oth.send()
    for part in range(3):
        wait_all(copies[2 * part : 2 * part + 2])
        for at in range(0, dim, 2 * LANES):
            cols = slice(at, at + 2 * LANES)
            res = (
                dot_nn(own.ref[0], buf[part, 0, :, cols])
                + dot_nn(oth.ref[0], buf[part, 1, :, cols])
                + bias_ref[:, part * dim + at : part * dim + at + 2 * LANES]
            )
            for i in range(2):
                vals = res[:, i * LANES : (i + 1) * LANES]
                if part < 2:
                    vals = rope(vals, tab_ref)
                out.ref[at // LANES + i, part] = vals.astype(bf16)


def layer_of(shape, index):
    return pl.BlockSpec((pl.squeezed,) + shape, lambda *args: (index, 0, 0))


HERE = pl.BlockSpec(memory_space=pltpu.VMEM)
SCALARS = pl.BlockSpec(memory_space=pltpu.SMEM)
ANYWHERE = pl.BlockSpec(memory_space=pl.ANY)
IN_HBM = pl.BlockSpec(memory_space=pltpu.HBM)


class Arriving:
    def __init__(self, buf, copy=None):
        self.buf, self.copy = buf, copy

    def ref(self):
        if self.copy is not None:
            self.copy.wait()
            self.copy = None
        return self.buf


class Leaving:
    def __init__(self, buf, copy=None):
        self.ref, self.copy, self.sent = buf, copy, copy is None

    def send(self):
        if not self.sent:
            self.copy.start()
            self.sent = True


def local_kernel(body, near_in, near_out, scalars, weights, followed, *refs):
    refs = list(refs)

    def take(number):
        taken = refs[:number]
        del refs[:number]
        return taken

    scalar_refs, array_refs = take(scalars), take(len(near_in))
    weight_refs, _, out_refs = take(weights), take(followed), take(len(near_out))
    in_sems, out_sems = take(2)
    inputs, outputs = [], []
    for i, (near, ref) in enumerate(zip(near_in, array_refs)):
        if near:
            inputs.append(Arriving(ref))
        else:
            buf = take(1)[0]
            copy = pltpu.make_async_copy(ref, buf, in_sems.at[i])
            copy.start()
            inputs.append(Arriving(buf, copy))
    for i, (near, ref) in enumerate(zip(near_out, out_refs)):
        if near:
            outputs.append(Leaving(ref))
        else:
            buf = take(1)[0]
            outputs.append(Leaving(buf, pltpu.make_async_copy(buf, ref, out_sems.at[i])))
    body(*scalar_refs, inputs, weight_refs, outputs, *refs)
    for item in inputs:
        item.ref()
    for item in outputs:
        item.send()
    for item in outputs:
        if item.copy is not None:
            item.copy.wait()


def far(array):
    return (array,)


def local_call(body, name, scalars, arrays, weights, out_shape, scratch=(), after=(), limit=VMEM_LIMIT):
    near_in = [not isinstance(a, tuple) for a in arrays]
    near_out = [not isinstance(o, tuple) for o in out_shape]
    raw_out = [isinstance(o, list) for o in out_shape]
    arrays = [a if near else a[0] for a, near in zip(arrays, near_in)]
    shapes = [o if near and not raw else o[0] for o, near, raw in zip(out_shape, near_out, raw_out)]
    far_bufs = [
        pltpu.VMEM(a.shape, a.dtype)
        for a, near in zip(arrays + shapes, near_in + near_out)
        if not near
    ]
    return pl.pallas_call(
        functools.partial(
            local_kernel, body, near_in, near_out, len(scalars), len(weights), len(after)
        ),
        in_specs=[SCALARS] * len(scalars)
        + [HERE if near else IN_HBM for near in near_in]
        + [IN_HBM] * len(weights)
        + [ANYWHERE] * len(after),
        out_specs=[HERE if near and not raw else IN_HBM for near, raw in zip(near_out, raw_out)],
        out_shape=shapes,
        scratch_shapes=[
            pltpu.SemaphoreType.DMA((len(arrays) + 1,)),
            pltpu.SemaphoreType.DMA((len(shapes),)),
        ]
        + far_bufs
        + list(scratch),
        name=name,
        **params_of(limit),
    )(*scalars, *arrays, *weights, *after)


def qkv_call(given, got, vecs, qkv_b, tab, w_own, w_oth, wsh):
    rows, dim = given.shape
    half = w_own.shape[0]
    pairs = dim // LANES
    return local_call(
        functools.partial(qkv_kernel, got is None),
        "qkv_proj",
        [wsh],
        [given, vecs, qkv_b, tab] if got is None else [given, vecs, qkv_b, tab, got],
        [w_own, w_oth],
        [shape_of((pairs, 3, rows, LANES), bf16), shape_of((rows, dim), bf16)]
        + [shape_of((2, rows, half), bf16)] * 2,
        [pltpu.VMEM((3, 2, half, dim), bf16), pltpu.SemaphoreType.DMA((3, 2))],
    )


FF_TILE = 1024
FF_PIECE = 512


def ff_tiles(wsh_ref, up_own, up_oth, dn_own, dn_oth, up_buf, dn_buf, sems):
    own = dn_own.shape[0] // FF_TILE
    tiles = []
    for t in range(2 * own):
        start = pl.multiple_of(((wsh_ref[0] * own + t) % (2 * own)) * FF_TILE, FF_TILE)
        cols = pl.ds(start, FF_TILE)
        down = (dn_own if t < own else dn_oth).at[pl.ds((t % own) * FF_TILE, FF_TILE)]
        copies = [
            pltpu.make_async_copy(up_own.at[:, cols], up_buf.at[t, 0], sems.at[t, 0]),
            pltpu.make_async_copy(up_oth.at[:, cols], up_buf.at[t, 1], sems.at[t, 1]),
            pltpu.make_async_copy(down, dn_buf.at[t], sems.at[t, 2]),
        ]
        tiles.append((t, start, start_all(copies)))
    for t, start, copies in tiles:
        wait_all(copies)
        for at in range(0, FF_TILE, FF_PIECE):
            row = (t % own) * FF_TILE + at
            place = pl.ds(pl.multiple_of(start + at, FF_PIECE), FF_PIECE)
            yield t, place, t < own, slice(row, row + FF_PIECE), slice(at, at + FF_PIECE)


def ff_scratch(half, ff, dim):
    tiles = ff // FF_TILE
    return [
        pltpu.VMEM((tiles, 2, half, FF_TILE), bf16),
        pltpu.VMEM((tiles, FF_TILE, dim), bf16),
        pltpu.SemaphoreType.DMA((tiles, 3)),
    ]


def mlp_kernel(save, wsh_ref, inputs, weights, outputs, up_buf, dn_buf, sems):
    out_ref = outputs[0].ref
    started = False
    for t, place, held, rows, piece in ff_tiles(wsh_ref, *weights, up_buf, dn_buf, sems):
        own_ref, oth_ref, up_b, down_b = (item.ref() for item in inputs)
        if not started:
            out_ref[...] = jnp.broadcast_to(down_b[...], out_ref.shape)
            started = True
        pre = (
            dot_nn(own_ref[1], up_buf[t, 0, :, piece])
            + dot_nn(oth_ref[1], up_buf[t, 1, :, piece])
            + up_b[:, place]
        )
        gate = 0.5 + 0.5 * lax.erf(pre * INV_SQRT2)
        act = (pre * gate).astype(bf16)
        if save:
            slope = gate + pre * (INV_SQRT_2PI * jnp.exp(-0.5 * pre * pre))
            outputs[1].ref[place] = slope.astype(bf16).T
            outputs[2 if held else 3].ref[rows] = act.T
            if not held:
                outputs[2].send()
        out_ref[...] += dot_nn(act, dn_buf[t, piece])


def mlp_call(own, oth, up_b, down_b, up_own, up_oth, dn_own, dn_oth, wsh, save):
    rows, half = own.shape[1:]
    dim = dn_own.shape[1]
    ff = up_own.shape[1]
    out_shape = [shape_of((rows, dim), f32)]
    if save:
        out_shape += [shape_of((ff, rows), bf16)]
        out_shape += [shape_of((ff // 2, rows), bf16)] * 2
    return local_call(
        functools.partial(mlp_kernel, save),
        "mlp_forward",
        [wsh],
        [own, oth, up_b, down_b],
        [up_own, up_oth, dn_own, dn_oth],
        out_shape,
        ff_scratch(half, ff, dim),
    )


def mlp_back_kernel(wsh_ref, inputs, weights, outputs, acc_own, acc_oth, up_buf, dn_buf, sems):
    du, dnm = outputs
    half = acc_own.shape[0]
    acc_own[...] = jnp.zeros(acc_own.shape, f32)
    acc_oth[...] = jnp.zeros(acc_oth.shape, f32)
    for t, place, _, _, piece in ff_tiles(wsh_ref, *weights, up_buf, dn_buf, sems):
        dy_ref, slope_ref = (item.ref() for item in inputs)
        dact = dot_nt(dn_buf[t, piece], dy_ref[...])
        vals = (dact * slope_ref[place].astype(f32)).astype(bf16)
        du.ref[place] = vals
        acc_own[...] += dot_nn(up_buf[t, 0, :, piece], vals)
        acc_oth[...] += dot_nn(up_buf[t, 1, :, piece], vals)
    du.send()
    first = wsh_ref[0] == 0
    dnm.ref[:, :half] = jnp.where(first, acc_own[...], acc_oth[...]).T
    dnm.ref[:, half:] = jnp.where(first, acc_oth[...], acc_own[...]).T


def mlp_back_call(dy, slope, up_own, up_oth, dn_own, dn_oth, wsh, after, limit):
    rows, dim = dy.shape
    half, ff = up_own.shape
    return local_call(
        mlp_back_kernel,
        "mlp_backward",
        [wsh],
        [dy, slope],
        [up_own, up_oth, dn_own, dn_oth],
        [shape_of(slope.shape, bf16), shape_of((rows, dim), f32)],
        [pltpu.VMEM((half, rows), f32), pltpu.VMEM((half, rows), f32)] + ff_scratch(half, ff, dim),
        after,
        limit,
    )


def sort_in(loc_ref, ref, dst, half_rows, part=None):
    for block in range(dst.shape[0] // half_rows):
        place = loc_ref[block]
        rows = pl.ds(pl.multiple_of((place % 2) * half_rows, half_rows), half_rows)
        if part is None:
            vals = ref[place // 2, rows, :]
        else:
            vals = ref[place // 2, part, rows, :]
        dst[block * half_rows : (block + 1) * half_rows] = vals


def sort_out(loc_ref, vals, ref, half_rows, part=None):
    for block in range(vals.shape[0] // half_rows):
        place = loc_ref[block]
        rows = pl.ds(pl.multiple_of((place % 2) * half_rows, half_rows), half_rows)
        piece = vals[block * half_rows : (block + 1) * half_rows]
        if part is None:
            ref[place // 2, rows, :] = piece
        else:
            ref[place // 2, part, rows, :] = piece


def head_of(vals, head):
    lane = lax.broadcasted_iota(jnp.int32, vals.shape, 1)
    return jnp.where(lane // (LANES // 2) == head, vals, jnp.zeros_like(vals))


def scores_of(keys, queries, diagonal):
    scores = dot_nt(keys, queries)
    if diagonal:
        key_at = lax.broadcasted_iota(jnp.int32, scores.shape, 0)
        query_at = lax.broadcasted_iota(jnp.int32, scores.shape, 1)
        scores = jnp.where(key_at <= query_at, scores, MASKED_SCORE)
    return scores


def attend_kernel(tile, loc_ref, inputs, weights, outputs, q_s, k_s, v_s, vt_s, o_s):
    qkv_ref = inputs[0].ref()
    o_ref, lse_ref = (item.ref for item in outputs)
    half_rows = qkv_ref.shape[2] // 2
    seq = q_s.shape[0]
    head_size = LANES // 2
    scale = head_size**-0.5
    sort_in(loc_ref, qkv_ref, q_s, half_rows, 0)
    sort_in(loc_ref, qkv_ref, k_s, half_rows, 1)
    sort_in(loc_ref, qkv_ref, v_s, half_rows, 2)
    vt_s[...] = v_s[...].T
    for t in range(seq // tile):
        rows = slice(t * tile, (t + 1) * tile)
        queries = q_s[rows]
        outs = []
        for head in range(2):
            picked = head_of(queries, head) * scale
            parts = [
                scores_of(k_s[i * tile : (i + 1) * tile], picked, i == t)
                for i in range(t + 1)
            ]
            top = functools.reduce(
                jnp.maximum, [jnp.max(p, axis=0, keepdims=True) for p in parts]
            )
            parts = [jnp.exp(p - top) for p in parts]
            total = sum(jnp.sum(p, axis=0, keepdims=True) for p in parts)
            lse_ref[head : head + 1, rows] = top + jnp.log(total)
            inverse = 1.0 / total
            acc = None
            for i, p in enumerate(parts):
                term = dot_nn(
                    vt_s[head * head_size : (head + 1) * head_size, i * tile : (i + 1) * tile],
                    p.astype(bf16),
                )
                acc = term if acc is None else acc + term
            outs.append(acc * inverse)
        o_s[rows] = jnp.concatenate(outs, axis=0).T.astype(bf16)
    sort_out(loc_ref, o_s, o_ref, half_rows)


def attend_call(qkv, loc, after):
    count, _, rows, _ = qkv.shape
    seq = count * rows
    return local_call(
        functools.partial(attend_kernel, 256),
        "attention",
        [loc],
        [qkv],
        [],
        [shape_of((count, rows, LANES), bf16), shape_of((2, seq), f32)],
        [
            pltpu.VMEM((seq, LANES), bf16),
            pltpu.VMEM((seq, LANES), bf16),
            pltpu.VMEM((seq, LANES), bf16),
            pltpu.VMEM((LANES, seq), bf16),
            pltpu.VMEM((seq, LANES), bf16),
        ],
        after,
    )


def attend_back_kernel(
    tile, part, loc_ref, inputs, weights, outputs, q_s, k_s, v_s, da_s, kt_s, dq_s, dk_s, dv_s
):
    da_ref, qkv_ref, lse_ref = (item.ref() for item in inputs)
    out_ref = outputs[0].ref
    half_rows = qkv_ref.shape[2] // 2
    seq = q_s.shape[0]
    head_size = LANES // 2
    scale = head_size**-0.5
    sort_in(loc_ref, qkv_ref, q_s, half_rows, 0)
    sort_in(loc_ref, qkv_ref, k_s, half_rows, 1)
    sort_in(loc_ref, qkv_ref, v_s, half_rows, 2)
    sort_in(loc_ref, da_ref, da_s, half_rows, part)
    kt_s[...] = k_s[...].T
    dk_s[...] = jnp.zeros(dk_s.shape, f32)
    dv_s[...] = jnp.zeros(dv_s.shape, f32)
    for t in range(seq // tile):
        rows = slice(t * tile, (t + 1) * tile)
        outs = []
        for head in range(2):
            queries = head_of(q_s[rows], head) * scale
            grads = head_of(da_s[rows], head)
            lse = lse_ref[head : head + 1, rows]
            probs, dprobs, row_dot = [], [], 0.0
            for i in range(t + 1):
                keys = slice(i * tile, (i + 1) * tile)
                p = jnp.exp(scores_of(k_s[keys], queries, i == t) - lse)
                dp = dot_nt(v_s[keys], grads)
                row_dot = row_dot + jnp.sum(p * dp, axis=0, keepdims=True)
                dv_s[keys] += dot_nn(p.astype(bf16), grads)
                probs.append(p)
                dprobs.append(dp)
            acc = None
            for i in range(t + 1):
                keys = slice(i * tile, (i + 1) * tile)
                ds = (probs[i] * (dprobs[i] - row_dot)).astype(bf16)
                dk_s[keys] += dot_nn(ds, queries)
                term = dot_nn(kt_s[head * head_size : (head + 1) * head_size, keys], ds)
                acc = term if acc is None else acc + term
            outs.append(acc * scale)
        dq_s[rows] = jnp.concatenate(outs, axis=0).T.astype(bf16)
    sort_out(loc_ref, dq_s, out_ref, half_rows, 0)
    k_s[...] = dk_s[...].astype(bf16)
    v_s[...] = dv_s[...].astype(bf16)
    sort_out(loc_ref, k_s, out_ref, half_rows, 1)
    sort_out(loc_ref, v_s, out_ref, half_rows, 2)


def attend_back_call(qkv, da, lse, loc, after, limit):
    count, _, rows, _ = qkv.shape
    seq = count * rows
    part = 0 if da.ndim == 4 else None
    (res,) = local_call(
        functools.partial(attend_back_kernel, 256, part),
        "attention_backward",
        [loc],
        [da, qkv, lse],
        [],
        [shape_of(qkv.shape, bf16)],
        [pltpu.VMEM((seq, LANES), bf16)] * 4
        + [pltpu.VMEM((LANES, seq), bf16), pltpu.VMEM((seq, LANES), bf16)]
        + [pltpu.VMEM((seq, LANES), f32)] * 2,
        after,
        limit,
    )
    return res


def by_head(parts):
    pairs, rows, lanes = parts.shape
    return jnp.transpose(parts, (1, 0, 2)).reshape(rows, HEADS, pairs * lanes // HEADS)


def by_pair(heads):
    rows = heads.shape[0]
    return jnp.transpose(heads.reshape(rows, -1, LANES), (1, 0, 2))


def wide_scores(queries, keys, query_pos, key_pos):
    raw = jnp.einsum("qhd,khd->hqk", queries, keys, preferred_element_type=f32)
    allowed = (query_pos[:, None] >= key_pos[None, :])[None]
    return jnp.where(allowed, raw * queries.shape[-1] ** (-0.5), MASKED_SCORE)


def key_blocks(arrays, rows):
    return tuple(a.reshape((a.shape[0] // rows, rows) + a.shape[1:]) for a in arrays)


def wide_attend(qkv, query_pos, key_pos):
    queries = by_head(qkv[:, 0])
    keys = lax.all_gather(by_head(qkv[:, 1]), "ctx", axis=0, tiled=True)
    values = lax.all_gather(by_head(qkv[:, 2]), "ctx", axis=0, tiled=True)
    block = min(512, keys.shape[0])
    split = key_blocks((keys, values, key_pos), block)
    rows, _, head_size = queries.shape

    def max_step(carry, block_in):
        top, total = carry
        scores = wide_scores(queries, block_in[0], query_pos, block_in[2])
        new_top = jnp.maximum(top, jnp.max(scores, axis=-1))
        part = jnp.sum(jnp.exp(scores - new_top[..., None]), axis=-1)
        return ((new_top, total * jnp.exp(top - new_top) + part), None)

    start = (jnp.full((HEADS, rows), MASKED_SCORE, f32), jnp.zeros((HEADS, rows), f32))
    (top, total), _ = lax.scan(max_step, start, split)
    lse = top + jnp.log(total)

    def value_step(running, block_in):
        scores = wide_scores(queries, block_in[0], query_pos, block_in[2])
        probs = jnp.exp(scores - lse[..., None]).astype(bf16)
        term = jnp.einsum("hqk,khd->qhd", probs, block_in[1], preferred_element_type=f32)
        return (running + term, None)

    attended, _ = lax.scan(value_step, jnp.zeros((rows, HEADS, head_size), f32), split)
    return by_pair(attended.astype(bf16)), (queries, keys, values, lse)


def wide_attend_back(kept, da, query_pos, key_pos):
    queries, keys, values, lse = kept
    grads = by_head(da)
    block = min(512, keys.shape[0])
    split = key_blocks((keys, values, key_pos), block)
    scale = queries.shape[-1] ** (-0.5)

    def pieces(block_in):
        scores = wide_scores(queries, block_in[0], query_pos, block_in[2])
        probs = jnp.exp(scores - lse[..., None])
        dprobs = jnp.einsum("qhd,khd->hqk", grads, block_in[1], preferred_element_type=f32)
        return probs, dprobs

    def dot_step(running, block_in):
        probs, dprobs = pieces(block_in)
        return (running + jnp.sum(probs * dprobs, axis=-1), None)

    row_dot, _ = lax.scan(dot_step, jnp.zeros(lse.shape, f32), split)

    def key_step(running, block_in):
        probs, dprobs = pieces(block_in)
        ds = (scale * probs * (dprobs - row_dot[..., None])).astype(bf16)
        running = running + jnp.einsum("hqk,khd->qhd", ds, block_in[0], preferred_element_type=f32)
        dk = jnp.einsum("hqk,qhd->khd", ds, queries, preferred_element_type=f32)
        dv = jnp.einsum("hqk,qhd->khd", probs.astype(bf16), grads, preferred_element_type=f32)
        return (running, (dk.astype(bf16), dv.astype(bf16)))

    dq, (dk, dv) = lax.scan(key_step, jnp.zeros(queries.shape, f32), split)
    dk, dv = (
        lax.psum_scatter(part.reshape(keys.shape), "ctx", scatter_dimension=0, tiled=True)
        for part in (dk, dv)
    )
    return jnp.stack([by_pair(dq.astype(bf16)), by_pair(dk), by_pair(dv)], axis=1)


def lanes_of(ref):
    return jnp.concatenate([ref[i] for i in range(ref.shape[0])], axis=1)


def both_halves(w_own, w_oth, buf, sems):
    return start_all(
        [
            pltpu.make_async_copy(weight, buf.at[side], sems.at[side])
            for side, weight in enumerate((w_own, w_oth))
        ]
    )


def half_scratch(weight):
    return [pltpu.VMEM((2,) + weight.shape, bf16), pltpu.SemaphoreType.DMA((2,))]


def proj_kernel(part, wsh_ref, inputs, weights, outputs, buf, sems):
    copies = both_halves(*weights, buf, sems)
    y, own, oth = outputs
    half = buf.shape[1]
    first = wsh_ref[0] == 0
    a_ref = inputs[0].ref()
    a = lanes_of(a_ref if part is None else a_ref.at[:, part])
    own.ref[...] = jnp.where(first, a[:, :half], a[:, half:])
    oth.ref[...] = jnp.where(first, a[:, half:], a[:, :half])
    own.send()
    oth.send()
    bias_ref, x_ref, mlp_ref = (item.ref() for item in inputs[1:])
    wait_all(copies)
    attn = dot_nn(own.ref[...], buf[0]) + dot_nn(oth.ref[...], buf[1]) + bias_ref[...]
    y.ref[...] = (x_ref[...].astype(f32) + attn + mlp_ref[...]).astype(bf16)


def proj_call(a, x, mlp, bias, p_own, p_oth, wsh, after, limit):
    rows, dim = x.shape
    half = p_own.shape[0]
    return local_call(
        functools.partial(proj_kernel, 1 if a.ndim == 4 else None),
        "attn_out",
        [wsh],
        [a, bias, x, mlp],
        [p_own, p_oth],
        [shape_of((rows, dim), bf16)] + [shape_of((rows, half), bf16)] * 2,
        half_scratch(p_own),
        after,
        limit,
    )


def da_kernel(own_given, wsh_ref, inputs, weights, outputs, buf, sems):
    copies = both_halves(*weights, buf, sems)
    out_ref, dy_out = outputs[0].ref, outputs[1]
    dy = inputs[0].ref()[...]
    if not own_given:
        dy = jnp.where(wsh_ref[1] == 1, inputs[1].ref()[...], dy)
    dy_out.ref[...] = dy
    dy_out.send()
    wsh = wsh_ref[0]
    joined = len(out_ref.shape) == 4
    if joined:
        out_ref[:, 1] = inputs[2].ref()[...]
    count = out_ref.shape[0] // 2
    for place, side in ((wsh * count, 0), ((1 - wsh) * count, 1)):
        copies[side].wait()
        part = dot_nt(dy, buf[side]).astype(bf16)
        for i in range(count):
            vals = part[:, i * LANES : (i + 1) * LANES]
            if joined:
                out_ref[place + i, 0] = vals
            else:
                out_ref[place + i] = vals


def da_call(given, got, p_own, p_oth, wsh, joined=None):
    rows, dim = given.shape
    pairs = dim // LANES
    arrays = [given] + ([] if got is None else [got])
    arrays += [] if joined is None else [joined]
    shape = (pairs, rows, LANES) if joined is None else (pairs, 2, rows, LANES)
    return local_call(
        functools.partial(da_kernel, got is None),
        "attn_out_backward",
        [wsh],
        arrays,
        [p_own, p_oth],
        [shape_of(shape, bf16), shape_of((rows, dim), bf16)],
        half_scratch(p_own),
    )


def dx_kernel(wsh_ref, inputs, weights, outputs, grad_s, buf, sems):
    copies = both_halves(*weights, buf, sems)
    back, dx, sums = outputs
    dqkv_ref, tab_ref = inputs[0].ref(), inputs[1].ref()
    pairs = dqkv_ref.shape[0]
    for part in range(3):
        for pair in range(pairs):
            vals = dqkv_ref[pair, part]
            if part < 2:
                vals = unrope(vals.astype(f32), tab_ref).astype(bf16)
            back.ref[pair, part] = vals
            grad_s[:, pl.ds((part * pairs + pair) * LANES, LANES)] = vals
    back.send()
    vec_ref, x_ref, dy_ref, dnm_ref = (item.ref() for item in inputs[2:])
    first = wsh_ref[0] == 0
    copies[0].wait()
    own = dot_nt(grad_s[...], buf[0])
    copies[1].wait()
    oth = dot_nt(grad_s[...], buf[1])
    dna = jnp.concatenate([jnp.where(first, own, oth), jnp.where(first, oth, own)], axis=1)
    dnm = dnm_ref[...]
    xhat, scale = normalized(x_ref[...].astype(f32))
    grad = dna * vec_ref[0:1] + dnm * vec_ref[2:3]
    inner = (
        grad
        - jnp.mean(grad, axis=-1, keepdims=True)
        - xhat * jnp.mean(grad * xhat, axis=-1, keepdims=True)
    )
    dx.ref[...] = (dy_ref[...].astype(f32) + scale * inner).astype(bf16)
    dx.send()
    sums.ref[0:1] = jnp.sum(dna * xhat, axis=0, keepdims=True)
    sums.ref[1:2] = jnp.sum(dna, axis=0, keepdims=True)
    sums.ref[2:3] = jnp.sum(dnm * xhat, axis=0, keepdims=True)
    sums.ref[3:4] = jnp.sum(dnm, axis=0, keepdims=True)


def dx_call(dqkv, tab, x, dy, dnm, vecs, w_own, w_oth, wsh, after, limit):
    rows, dim = x.shape
    return local_call(
        dx_kernel,
        "section_input_grad",
        [wsh],
        [dqkv, tab, vecs, x, dy, dnm],
        [w_own, w_oth],
        [shape_of(o, t) for o, t in ((dqkv.shape, bf16), ((rows, dim), bf16), ((4, dim), f32))],
        [pltpu.VMEM((rows, 3 * dim), bf16)] + half_scratch(w_own),
        after,
        limit,
    )


def joined_rows(items):
    return jnp.concatenate([item.ref()[...] for item in items], axis=0)


class Pieces:
    def __init__(self, out_ref, buf, sems):
        self.out_ref, self.buf, self.sems, self.copies = out_ref, buf, sems, []

    def put(self, rows, cols, vals):
        self.buf[rows, cols] = vals.astype(bf16)
        at = len(self.copies)
        self.copies.append(
            pltpu.make_async_copy(
                self.buf.at[rows, cols], self.out_ref.at[rows, cols], self.sems.at[at]
            )
        )
        self.copies[-1].start()

    def finish(self, chunk, ahead, behind):
        height, cut = ahead.ref.shape
        rows = pl.ds(pl.multiple_of(chunk * height, height), height)
        ahead.ref[...] = self.buf[rows, :cut]
        ahead.send()
        behind.ref[...] = self.buf[rows, cut:]
        behind.send()
        wait_all(self.copies)


def grad_call(body, name, idx, arrays, shape, width, count, scratch, after):
    halves = shape_of((shape[0] // count, shape[1] // 2), bf16)
    return local_call(
        functools.partial(body, len(arrays)),
        name,
        [idx],
        arrays,
        [],
        [[shape_of(shape, bf16)], far(halves), far(halves), far(shape_of((1, width), f32))],
        [pltpu.VMEM(shape, bf16), pltpu.SemaphoreType.DMA((4,))] + scratch,
        after,
        TAIL_LIMIT,
    )


def parts_of(items, number):
    size = len(items) // number
    return [items[i * size : (i + 1) * size] for i in range(number)]


def down_grad_kernel(number, idx_ref, inputs, weights, outputs, buf, sems):
    gts, dys = parts_of(inputs, 2)
    out = Pieces(outputs[0].ref, buf, sems)
    dy = joined_rows(dys)
    outputs[3].ref[...] = jnp.sum(dy.astype(f32), axis=0, keepdims=True)
    rows, dim = buf.shape
    tile = rows // 4
    for t in range(4):
        part = slice(t * tile, (t + 1) * tile)
        left = jnp.concatenate([item.ref()[part] for item in gts], axis=1)
        out.put(part, slice(0, dim), dot_nn(left, dy))
    out.finish(idx_ref[idx_ref.shape[0] // 2], outputs[1], outputs[2])


def down_grad_call(idx, gt_list, dy_list, count):
    dim = dy_list[0].shape[1]
    return grad_call(
        down_grad_kernel,
        "down_grad",
        idx,
        [far(a) for a in gt_list + dy_list],
        (gt_list[0].shape[0], dim),
        dim,
        count,
        [],
        [],
    )


def up_grad_kernel(number, idx_ref, inputs, weights, outputs, buf, sems):
    norms, dus = parts_of(inputs, 2)
    out = Pieces(outputs[0].ref, buf, sems)
    left = jnp.concatenate([item.ref()[1] for item in norms], axis=0).T
    rows, ff = buf.shape
    tile = ff // 4
    for t in range(4):
        part = slice(t * tile, (t + 1) * tile)
        du = jnp.concatenate([item.ref()[part] for item in dus], axis=1)
        outputs[3].ref[:, part] = dot_nt(jnp.ones((8, du.shape[1]), bf16), du)[:1]
        out.put(slice(0, rows), part, dot_nt(left, du))
    out.finish(idx_ref[idx_ref.shape[0] // 2], outputs[1], outputs[2])


def up_grad_call(idx, norm_list, du_list, count, after):
    half, ff = norm_list[0].shape[2], du_list[0].shape[0]
    return grad_call(
        up_grad_kernel,
        "up_grad",
        idx,
        [far(a) for a in norm_list + du_list],
        (half, ff),
        ff,
        count,
        [],
        after,
    )


def attn_grad_kernel(number, idx_ref, inputs, weights, outputs, buf, sems):
    norms, outs, dqkvs, dys = parts_of(inputs, 4)
    out = Pieces(outputs[0].ref, buf, sems)
    rows, width = buf.shape
    dim = width // 4
    left = jnp.concatenate([item.ref()[0] for item in norms], axis=0).T
    for part in range(4):
        cols = slice(part * dim, (part + 1) * dim)
        if part < 3:
            right = jnp.concatenate([lanes_of(item.ref().at[:, part]) for item in dqkvs], axis=0)
        else:
            left, right = joined_rows(outs).T, joined_rows(dys)
        outputs[3].ref[:, cols] = jnp.sum(right.astype(f32), axis=0, keepdims=True)
        out.put(slice(0, rows), cols, dot_nn(left, right))
    out.finish(idx_ref[idx_ref.shape[0] // 2], outputs[1], outputs[2])


def attn_grad_call(idx, norm_list, out_list, dqkv_list, dy_list, count, after):
    half, dim = norm_list[0].shape[2], dy_list[0].shape[1]
    return grad_call(
        attn_grad_kernel,
        "attn_grad",
        idx,
        [far(a) for a in norm_list + out_list + dqkv_list + dy_list],
        (half, 4 * dim),
        4 * dim,
        count,
        [],
        after,
    )


def ring_of(count):
    return list(range(0, count, 2)) + list(range(count - 1, 0, -2))


def ring_place(axis):
    count = lax.axis_size(axis)
    me = lax.axis_index(axis)
    return jnp.where(me % 2 == 0, me // 2, count - (me + 1) // 2)


def ring_index(axis):
    count = lax.axis_size(axis)
    return (ring_place(axis) + jnp.arange(count, dtype=jnp.int32)) % count


def ring_shift(vals, axis, by):
    order = ring_of(lax.axis_size(axis))
    count = len(order)
    pairs = [(order[i], order[(i + by) % count]) for i in range(count)]
    return lax.ppermute(vals, axis, pairs)


def tied(token, *vals):
    return lax.optimization_barrier((token, vals))[1]


def fetch(idx_ref, slots, own_ref, bufs, sems):
    return start_all(
        [
            pltpu.make_async_copy(own_ref.at[idx_ref[slot]], bufs.at[i], sems.at[i])
            for i, slot in enumerate(slots)
        ]
    )


def low_total(*terms):
    total = terms[0].astype(f32)
    for term in terms[1:]:
        total = total + term.astype(f32)
    return total.astype(bf16)


def ring_add_kernel(slots, idx_ref, inputs, own_refs, outputs, bufs, sems):
    copies = fetch(idx_ref, slots, own_refs[0], bufs, sems)
    for i, item in enumerate(outputs):
        copies[i].wait()
        got = inputs[i].ref()
        cols, cut = item.ref.shape[1], got.shape[1]
        summed = slice(0, cut) if i == 0 else slice(cols - cut, cols)
        item.ref[:, summed] = low_total(bufs[i, :, summed], got[...])
        if cut < cols:
            rest = slice(cut, cols) if i == 0 else slice(0, cols - cut)
            item.ref[:, rest] = bufs[i, :, rest]
        item.send()


def put_copies(chunk, cols, buf, totals, starts, sem):
    lo, hi = cols, cols + buf.shape[1]
    copies = []
    for i, (total, start) in enumerate(zip(totals, starts)):
        first, last = max(lo, start), min(hi, start + total.shape[2])
        if first < last:
            copies.append(
                pltpu.make_async_copy(
                    buf.at[:, pl.ds(first - lo, last - first)],
                    total.at[chunk, :, pl.ds(first - start, last - first)],
                    sem.at[i],
                )
            )
    return copies


def ring_own_kernel(slots, idx_ref, inputs, own_refs, outputs, bufs, sems):
    wait_all(fetch(idx_ref, slots, own_refs[0], bufs, sems))
    outputs[0].ref[...] = low_total(bufs[0], inputs[0].ref()[...], inputs[1].ref()[...])


def ring_put_kernel(starts, slots, cols, fresh, onward, idx_ref, *refs):
    number = len(slots)
    pieces = refs[:number]
    wide, sems, pass_buf, pass_sems = refs[-4:]
    passed = refs[-4 - onward : -4]
    totals = refs[-4 - onward - len(starts) : -4 - onward]
    leaving = []
    for i, ref in enumerate(passed):
        width = ref.shape[1]
        pass_buf[i, :, :width] = pieces[i][:, :width] if i == 0 else pieces[i][:, -width:]
        leaving += start_all(
            [pltpu.make_async_copy(pass_buf.at[i, :, pl.ds(0, width)], ref, pass_sems.at[i])]
        )
    for i in range(number):
        wide[i] = pieces[i][...].astype(f32)
        leaving += start_all(
            put_copies(idx_ref[slots[i]], cols[i], wide.at[i], totals, starts, sems.at[i])
        )
    wait_all(leaving)


def ring_sum(own, ahead, behind, widths, axis):
    count = lax.axis_size(axis)
    half = count // 2
    full_rows, cols = own.shape
    rows = full_rows // count
    own = own.reshape(count, rows, cols)
    cut = cols // 2
    starts = [sum(widths[:i]) for i in range(len(widths))]
    idx = ring_index(axis)
    chunk, piece = shape_of((rows, cols), bf16), shape_of((rows, cut), bf16)
    sums = [shape_of((count, rows, width), f32) for width in widths]

    def taken(number):
        return [pltpu.VMEM((number, rows, cols), bf16), pltpu.SemaphoreType.DMA((number,))]

    def put(totals, pieces, slots, passed, after):
        number, width = len(pieces), pieces[0].shape[1]
        first_cols = (0,) * number if width == cols else (0, cut)
        fresh = totals is None
        out = pl.pallas_call(
            functools.partial(
                ring_put_kernel,
                starts,
                tuple(k % count for k in slots),
                first_cols,
                fresh,
                len(passed),
            ),
            in_specs=[SCALARS]
            + [HERE] * number
            + [IN_HBM] * (0 if fresh else len(sums))
            + [ANYWHERE] * len(after),
            out_specs=[IN_HBM] * (len(sums) + len(passed)),
            out_shape=sums + passed,
            scratch_shapes=[
                pltpu.VMEM((number, rows, width), f32),
                pltpu.SemaphoreType.DMA((number, len(sums))),
                pltpu.VMEM((2, rows, cols), bf16),
                pltpu.SemaphoreType.DMA((2,)),
            ],
            input_output_aliases={} if fresh else {1 + number + i: i for i in range(len(sums))},
            name="ring_put",
            **params_of(RING_LIMIT),
        )(idx, *pieces, *([] if fresh else totals), *after)
        return out[: len(sums)], out[len(sums) :]

    def both_ways(ahead, behind):
        return ring_shift(ahead, axis, 1), ring_shift(behind, axis, -1)

    token = behind
    ahead, behind = both_ways(ahead, behind)
    token = yield token
    for k in range(half - 1, 0, -1):
        ahead, behind = local_call(
            functools.partial(ring_add_kernel, (k % count, (-k) % count)),
            "ring_add",
            [idx],
            [ahead, behind],
            [own],
            [chunk, chunk],
            taken(2),
            [token],
            RING_LIMIT,
        )
        token = behind
        ahead, behind = both_ways(ahead, behind)
        token = yield token
    (mine,) = local_call(
        functools.partial(ring_own_kernel, (0,)),
        "ring_own",
        [idx],
        [ahead, behind],
        [own],
        [chunk],
        taken(1),
        [token],
        RING_LIMIT,
    )
    ahead, behind = both_ways(mine, mine)
    totals, (token,) = put(None, [mine], [0], [shape_of((rows, LANES), bf16)], [])
    token = yield token
    for k in range(1, half):
        passed = [piece if k == half - 1 else chunk] * 2
        totals, passed = put(totals, [ahead, behind], [-k, k], passed, [token])
        token = passed[1]
        ahead, behind = both_ways(*passed)
        token = yield token
    totals, _ = put(totals, [ahead, behind], [-half, half], [], [token])
    yield [total.reshape(full_rows, -1) for total in totals]


def add_kernel(inputs, weights, outputs):
    outputs[0].ref[...] = inputs[0].ref()[...] + inputs[1].ref()[...]


def butterfly_sum(vals, axis):
    count = lax.axis_size(axis)
    by = 1
    token = yield None
    if count & (count - 1):
        yield lax.psum(vals, axis)
        return
    while by < count:
        got = lax.ppermute(vals, axis, [(i, i ^ by) for i in range(count)])
        token = yield None
        (vals,) = local_call(
            add_kernel, "small_add", [], [vals, got], [], [shape_of(vals.shape, f32)], [], [token]
        )
        by *= 2
    yield vals


def swap(vals):
    return lax.ppermute(vals, "wsh", [(0, 1), (1, 0)])


def pass_on(vals, by):
    pairs = [(0, 1)] if by > 0 else [(1, 0)]
    return lax.ppermute(vals, "section", pairs)


def block_places(block_pair, count):
    want = jnp.arange(2 * count, dtype=jnp.int32)
    device = jnp.arange(count, dtype=jnp.int32)
    first = (block_pair[None, :] == want[:, None]).astype(jnp.int32)
    second = ((2 * count - 1 - block_pair)[None, :] == want[:, None]).astype(jnp.int32)
    return jnp.sum(first * (2 * device) + second * (2 * device + 1), axis=1)


def row_positions(block_pair, stored, tok_dev):
    count = block_pair.shape[0]
    device = stored // tok_dev
    within = stored % tok_dev
    half_rows = tok_dev // 2
    matches = device[:, None] == jnp.arange(count, dtype=jnp.int32)[None, :]
    pair_block = jnp.sum(jnp.where(matches, block_pair[None, :], 0), axis=1)
    block_idx = jnp.where(within < half_rows, pair_block, 2 * count - 1 - pair_block)
    return block_idx * half_rows + within % half_rows


def rotary_table(positions, head_size):
    half_rot = ROT // 2
    lane = jnp.arange(LANES, dtype=jnp.int32) % head_size
    inv_freq = ROPE_BASE ** (-((lane % half_rot).astype(f32) * 2.0) / ROT)
    angles = positions.astype(f32)[:, None] * inv_freq[None, :]
    cosine, sine = jnp.cos(angles), jnp.sin(angles)
    lead, second = (lane < half_rot)[None], ((lane >= half_rot) & (lane < ROT))[None]
    return jnp.stack(
        [
            jnp.where(lead | second, cosine, 1.0),
            jnp.where(lead, -sine, 0.0),
            jnp.where(second, sine, 0.0),
        ]
    )


def body(
    inputs,
    cotangent,
    block_pair,
    qkv_weight,
    qkv_bias,
    proj_weight,
    proj_bias,
    up_weight,
    up_bias,
    down_weight,
    down_bias,
    attn_gain,
    attn_shift,
    mlp_gain,
    mlp_shift,
):
    first_section = lax.axis_index("section") == 0
    count = lax.axis_size("ctx")
    micros, _, tok_dev, dim = inputs.shape
    head_size = dim // HEADS
    half = dim // 2
    my_half = lax.axis_index("wsh")
    wsh = jnp.stack([my_half.astype(jnp.int32), first_section.astype(jnp.int32)])
    one_pair_each = count == dim // LANES

    wq, wp, wu, wd = (w[0] for w in (qkv_weight, proj_weight, up_weight, down_weight))
    small = jnp.concatenate(
        [
            v[0].reshape(-1, half)
            for v in (
                attn_gain,
                attn_shift,
                mlp_gain,
                mlp_shift,
                proj_bias,
                down_bias,
                qkv_bias,
                up_bias,
            )
        ],
        axis=0,
    )
    small_oth = swap(small)
    wq_oth = swap(wq)
    first_here = lax.optimization_barrier((wq_oth, small_oth))
    wq_oth, small_oth = first_here
    wu_oth = swap(tied(wq_oth, wu)[0])
    wd_oth = swap(tied(wq_oth, wd)[0])
    wp_oth = swap(tied(wu_oth, wp)[0])
    low_part = jnp.where(my_half == 0, small, small_oth).astype(f32)
    high_part = jnp.where(my_half == 0, small_oth, small).astype(f32)
    vecs = jnp.concatenate([low_part[:6], high_part[:6]], axis=1)
    qkv_rows = 6 + qkv_bias.shape[1] // half
    proj_b, down_b = vecs[4:5], vecs[5:6]
    qkv_b = jnp.concatenate([low_part[6:qkv_rows], high_part[6:qkv_rows]], axis=0).reshape(1, -1)
    up_b = jnp.concatenate([low_part[qkv_rows:], high_part[qkv_rows:]], axis=0).reshape(1, -1)

    local_rows = lax.axis_index("ctx") * tok_dev + jnp.arange(tok_dev, dtype=jnp.int32)
    query_pos = row_positions(block_pair, local_rows, tok_dev)
    key_pos = row_positions(block_pair, jnp.arange(count * tok_dev, dtype=jnp.int32), tok_dev)
    tab = rotary_table(query_pos, head_size)
    loc = block_places(block_pair, count)

    def exchange(vals):
        return lax.all_to_all(vals, "ctx", split_axis=0, concat_axis=0, tiled=True)

    rows_in = [inputs[i, 0] for i in range(micros)]
    cot_in = [cotangent[i, 0] for i in range(micros)]

    def norm_qkv(index, got):
        return qkv_call(rows_in[index], got, vecs, qkv_b, tab, wq, wq_oth, wsh)

    def mlp(made, save):
        return mlp_call(made[2], made[3], up_b, down_b, wu, wu_oth, wd, wd_oth, wsh, save)

    def mlp_back(dy, mlp_kept, after=(), limit=VMEM_LIMIT):
        return mlp_back_call(dy, mlp_kept[1], wu, wu_oth, wd, wd_oth, wsh, after, limit)

    def out_back(index, got, joined=None):
        return da_call(cot_in[index], got, wp, wp_oth, wsh, joined)

    def moved(vals):
        return exchange(vals) if one_pair_each else vals

    def attend(qkv, after=()):
        if one_pair_each:
            attended, lse = attend_call(qkv, loc, after)
            return attended, (qkv, lse)
        return wide_attend(qkv, query_pos, key_pos)

    def attend_back(kept, da, after=(), limit=VMEM_LIMIT):
        if one_pair_each:
            return attend_back_call(kept[0], da, kept[1], loc, after, limit)
        da = da[:, 0] if da.ndim == 4 else da
        return wide_attend_back(kept, da, query_pos, key_pos)

    def project(attended, made, mlp_out, after=(), limit=VMEM_LIMIT):
        return proj_call(attended, made[1], mlp_out[0], proj_b, wp, wp_oth, wsh, after, limit)

    def input_grad_of(dqkv, made, dy, dnm, after=(), limit=VMEM_LIMIT):
        return dx_call(dqkv, tab, made[1], dy, dnm, vecs, wq, wq_oth, wsh, after, limit)

    made_a = norm_qkv(0, None)
    qkv_a = moved(made_a[0])
    mlp_a = mlp(made_a, False)
    att_a, _ = attend(qkv_a, [mlp_a[0]])
    att_a = moved(att_a)
    da_a, dy_a = out_back(0, None)
    y_a = project(att_a, made_a, mlp_a, [dy_a])[0]
    da_a = moved(tied(y_a, da_a)[0])

    made_b = norm_qkv(1, pass_on(y_a, 1))
    qkv_2 = moved(tied(da_a, made_b[0])[0])
    norms_b = swap(made_b[3])
    mlp_b = mlp(made_b, True)
    _, dnm_a = mlp_back(dy_a, mlp_b)
    att_b, kept_b = attend(qkv_2, [dnm_a, norms_b])
    att_b = moved(att_b)
    gt_b = swap(mlp_b[3])
    dqkv_a_ = attend_back(kept_b, da_a, [gt_b])
    dqkv_a = moved(dqkv_a_)
    y_b, *a_b = project(att_b, made_b, mlp_b, [dqkv_a_])

    made_c = norm_qkv(0, pass_on(y_b, 1))
    qkv_3 = moved(tied(dqkv_a, made_c[0])[0])
    norms_c = swap(made_c[3])
    a_b_oth = swap(a_b[1])
    _, dx_a, _ = input_grad_of(dqkv_a, made_b, dy_a, dnm_a, [norms_c, a_b_oth])
    got_a = pass_on(dx_a, -1)
    mlp_c = mlp_call(
        made_c[2], tied(dx_a, made_c[3])[0], up_b, down_b, wu, wu_oth, wd, wd_oth, wsh, True
    )
    da_b, dy_b = out_back(1, tied(mlp_c[0], got_a)[0])
    da_b = moved(tied(qkv_3, da_b)[0])
    att_c, kept_c = attend(qkv_3, [dy_b])
    dy_b_oth, gt_c = swap(dy_b), swap(mlp_c[3])
    dqkv_b = attend_back(kept_c, da_b, [dy_b_oth, gt_c])
    dqkv_b_ = moved(dqkv_b)
    du_b, dnm_b = mlp_back(dy_b, mlp_c, [dqkv_b])
    du_b_oth = swap(du_b)
    back_b, dx_b, sums_b = input_grad_of(dqkv_b_, made_c, dy_b, dnm_b, [du_b_oth])
    got_b = pass_on(dx_b, -1)
    back_b_oth = swap(back_b)

    da_c, dy_c = out_back(0, tied(back_b_oth, got_b)[0], att_c if one_pair_each else None)
    dy_list = [dy_c, dy_b, swap(dy_c), dy_b_oth]
    da_c = moved(da_c)
    idx = ring_index("ctx")
    *down_made, dy_sum = down_grad_call(idx, [mlp_b[2], mlp_c[2], gt_b, gt_c], dy_list, count)
    down_ring = ring_sum(*down_made, (dim,), "ctx")
    token = next(down_ring)
    token = down_ring.send(token)
    du_c, dnm_c = mlp_back(dy_c, mlp_b, [token], TAIL_LIMIT)
    dqkv_c = attend_back(kept_b, da_c, [dnm_c], TAIL_LIMIT)
    token = down_ring.send(dqkv_c)
    dqkv_c = moved(dqkv_c)
    *up_made, du_sum = up_grad_call(
        idx,
        [made_b[2], made_c[2], norms_b, norms_c],
        [du_c, du_b, swap(du_c), du_b_oth],
        count,
        [token],
    )
    up_ring = ring_sum(*up_made, (up_made[0].shape[1],), "ctx")
    token = next(up_ring)
    steps = count + 1
    left = {down_ring: steps - 3, up_ring: steps - 1}
    results = {}

    def turn(ring, token):
        if not left[ring]:
            return token
        left[ring] -= 1
        made = ring.send(token)
        if left[ring] == 0:
            results[ring] = made
            return token
        return made

    token = turn(down_ring, token)
    token = turn(up_ring, token)
    back_c, dx_c, sums_c = input_grad_of(dqkv_c, made_b, dy_c, dnm_c, [token], TAIL_LIMIT)
    back_c_oth = swap(back_c)
    token = turn(down_ring, dx_c)
    y_c, *a_c = project(da_c if one_pair_each else att_c, made_c, mlp_c, [token], TAIL_LIMIT)
    a_c_oth = swap(a_c[1])
    token = turn(up_ring, y_c)
    token = turn(down_ring, token)
    *attn_made, attn_sum = attn_grad_call(
        idx,
        [made_b[2], made_c[2], norms_b, norms_c],
        [a_b[0], a_c[0], a_b_oth, a_c_oth],
        [back_c, back_b, back_c_oth, back_b_oth],
        dy_list,
        count,
        [token],
    )
    dqkv_sum = attn_sum[:, : 3 * dim]
    attn_ring = ring_sum(*attn_made, (3 * dim, dim), "ctx")
    token = next(attn_ring)
    left[attn_ring] = steps - 1

    norm_sums = sums_b + sums_c
    norm_own = lax.dynamic_slice_in_dim(norm_sums, my_half * half, half, 1)
    norm_oth = swap(lax.dynamic_slice_in_dim(norm_sums, (1 - my_half) * half, half, 1))

    def own_part(vec):
        size = vec.shape[1] // 2
        return lax.dynamic_slice_in_dim(vec, my_half * size, size, 1).reshape(-1, half)

    (norm_oth,) = tied(token, norm_oth)
    small_sums = jnp.concatenate(
        [norm_own + norm_oth, own_part(dy_sum), own_part(dqkv_sum), own_part(du_sum)], axis=0
    )
    small_ring = butterfly_sum(small_sums, "ctx")
    next(small_ring)
    at = 0
    summed = None
    while any(left.values()):
        token = turn((up_ring, attn_ring, down_ring, attn_ring)[at % 4], token)
        if at % 4 == 0 and summed is None:
            summed = small_ring.send(token)
        at += 1
    while summed is None:
        summed = small_ring.send(token)
    small_sums = summed
    (down_grad,) = results[down_ring]
    (up_grad,) = results[up_ring]
    qkv_grad, proj_grad = results[attn_ring]

    qkv_end = 5 + dqkv_sum.shape[1] // 2 // half
    dy_total = small_sums[4:5]
    pick = lambda yes, no: jnp.where(first_section, yes, no)
    layer_out = jnp.stack([pick(y_c, y_b), pick(y_b, y_c)])[None, :, None]
    input_grad = jnp.stack([pick(dx_b, dx_c), pick(dx_c, dx_b)])[None, :, None]
    return (
        layer_out,
        input_grad,
        qkv_grad[None],
        small_sums[5:qkv_end].reshape(1, -1),
        proj_grad[None],
        dy_total,
        up_grad[None],
        small_sums[qkv_end:].reshape(1, -1),
        down_grad[None],
        dy_total,
        small_sums[0:1],
        small_sums[1:2],
        small_sums[2:3],
        small_sums[3:4],
    )


def solution(mesh):
    in_specs = (
        P(None, "wsh", "ctx", None),
        P(None, "wsh", "ctx", None),
        P(),
        P("section", "wsh", None),
        P("section", "wsh"),
        P("section", "wsh", None),
        P("section", "wsh"),
        P("section", "wsh", None),
        P("section", "wsh"),
        P("section", "wsh", None),
        P("section", "wsh"),
        P("section", "wsh"),
        P("section", "wsh"),
        P("section", "wsh"),
        P("section", "wsh"),
    )
    out_specs = (
        P("section", None, "wsh", "ctx", None),
        P("section", None, "wsh", "ctx", None),
        P("section", "wsh", None),
        P("section", "wsh"),
        P("section", "wsh", None),
        P("section", "wsh"),
        P("section", "wsh", None),
        P("section", "wsh"),
        P("section", "wsh", None),
        P("section", "wsh"),
        P("section", "wsh"),
        P("section", "wsh"),
        P("section", "wsh"),
        P("section", "wsh"),
    )
    return jax.shard_map(body, mesh=mesh, in_specs=in_specs, out_specs=out_specs, check_vma=False)
```
